32 devices in a mesh: dp: 4 (over y, x), fsdp: 8 (over z, core).
Axes of the slice: x: 2, y: 2, z: 4, core: 2. Of those that a mesh axis runs over, the one named last changes fastest.
Arguments:
- patches: bfloat16 [16384, 768], P(('dp', 'fsdp')), may hold values from -6 to 6
- lead_index: int32 [32], P(('dp', 'fsdp')), may hold values from 0 to 15
- window_lengths: int32 [32, 8], P(('dp', 'fsdp')), may hold values from 1 to 128, 512 in all within a row
- pad_mask: int32 [16384], P(('dp', 'fsdp')), may hold values 0 or 1
- lead_table: bfloat16 [16, 768], P(None, ('dp', 'fsdp')), may hold values from -3 to 3
- attn_gain: bfloat16 [768], P(('dp', 'fsdp')), may hold values from 0.25 to 1.75
- attn_shift: bfloat16 [768], P(('dp', 'fsdp')), may hold values from -1.75 to 1.75
- qkv_weight: bfloat16 [768, 2304], P(('dp', 'fsdp')), may hold values from -0.21875 to 0.21875
- out_weight: bfloat16 [768, 768], P(('dp', 'fsdp')), may hold values from -0.875 to 0.875
- out_bias: bfloat16 [768], P(('dp', 'fsdp')), may hold values from -1.75 to 1.75
- mlp_gain: bfloat16 [768], P(('dp', 'fsdp')), may hold values from 0.25 to 1.75
- mlp_shift: bfloat16 [768], P(('dp', 'fsdp')), may hold values from -1.75 to 1.75
- up_weight: bfloat16 [768, 3072], P(('dp', 'fsdp')), may hold values from -0.21875 to 0.21875
- up_bias: bfloat16 [3072], P(('dp', 'fsdp')), may hold values from -1.75 to 1.75
- down_weight: bfloat16 [3072, 768], P(('dp', 'fsdp')), may hold values from -0.109375 to 0.109375
- down_bias: bfloat16 [768], P(('dp', 'fsdp')), may hold values from -1.75 to 1.75
- head_weight: bfloat16 [768, 4608], P(('dp', 'fsdp')), may hold values from -0.109375 to 0.109375
- head_bias: bfloat16 [4608], P(('dp', 'fsdp')), may hold values from -0.625 to 0.625
- act_cotangent: bfloat16 [16384, 768], P(('dp', 'fsdp')), may hold values from -6 to 6
- head_cotangent: bfloat16 [16384, 4608], P(('dp', 'fsdp')), may hold values from -6 to 6
Outputs:
- activations: bfloat16 [16384, 768], P(('dp', 'fsdp'))
- head_out: float32 [16384, 4608], P(('dp', 'fsdp'))
- patches_grad: float32 [16384, 768], P(('dp', 'fsdp'))
- lead_table_grad: float32 [16, 768], P(None, ('dp', 'fsdp'))
- attn_gain_grad: float32 [768], P(('dp', 'fsdp'))
- attn_shift_grad: float32 [768], P(('dp', 'fsdp'))
- qkv_weight_grad: float32 [768, 2304], P(('dp', 'fsdp'))
- out_weight_grad: float32 [768, 768], P(('dp', 'fsdp'))
- out_bias_grad: float32 [768], P(('dp', 'fsdp'))
- mlp_gain_grad: float32 [768], P(('dp', 'fsdp'))
- mlp_shift_grad: float32 [768], P(('dp', 'fsdp'))
- up_weight_grad: float32 [768, 3072], P(('dp', 'fsdp'))
- up_bias_grad: float32 [3072], P(('dp', 'fsdp'))
- down_weight_grad: float32 [3072, 768], P(('dp', 'fsdp'))
- down_bias_grad: float32 [768], P(('dp', 'fsdp'))
- head_weight_grad: float32 [768, 4608], P(('dp', 'fsdp'))
- head_bias_grad: float32 [4608], P(('dp', 'fsdp'))
The draws below stay inside these ranges and needn't reach their ends.
Inputs may be any that keep to these rules, and one draw needn't show every extreme that they name: `window_lengths`: the 8 window lengths of a pack sum to 512; in every pack the longest is exactly 128.
All inputs are finite; a program needn't handle non-finite values. No bound on the sum of `pad_mask` on one device may be relied on, other than what follows from the above.
Results may differ from the reference program's by a relative error of at most 0.014.
Values may be sent and summed in bfloat16 or wider, within the bound.
No kernel may reach another device: no remote copies, remote signals or barrier semaphores. Data moves between devices by JAX's collectives and lax.ppermute only.
A program may use at most 192 MiB of HBM per device.

```python
import math
import jax
import jax.numpy as jnp
import numpy as np
from jax import lax

D = 768
HEADS = 12
HD = 64
FF = 3072
PIX = 64
EXPERTS = 3
LEADS = 16
NWIN = 8
HOUT = 4608
SEQ = 512
WMAX = 128
PACKS = 32
TOKENS = 16384


def set_ends(entries, stream_key, least, high):
    index_at = [jax.random.randint(jax.random.fold_in(stream_key, axis), (), 0, length) for axis, length in enumerate(entries.shape)]
    longest = entries.shape.index(max(entries.shape))
    neighbour = index_at[:longest] + [(index_at[longest] + 1) % entries.shape[longest]] + index_at[longest + 1:]
    return entries.at[tuple(index_at)].set(least).at[tuple(neighbour)].set(high)


def strengthened(result, key, source, target, blocks, factor):
    owner, partner = [(jnp.arange(result.shape[position]) // (result.shape[position] // blocks)).reshape([-1 if axis == position else 1 for axis in range(result.ndim)]) for position in (source, target)]
    chosen = jax.random.permutation(key, blocks)[partner]
    strong = (owner == chosen) | (owner == (partner + blocks // 2) % blocks)
    return jnp.where(strong, factor * result, result)


def levels(key, dims, cuts, smallest, high):
    gain, own = 1.0, jax.random.fold_in(key, 6)
    for axis_at, blocks in cuts:
        steps = jnp.exp(jax.random.uniform(jax.random.fold_in(own, axis_at), (blocks,), jnp.float32, smallest / len(cuts), high / len(cuts)))
        gain = gain * jnp.repeat(steps, dims[axis_at] // blocks).reshape([-1 if axis == axis_at else 1 for axis in range(len(dims))])
    return gain


def profile(number_of, total, limit, lean):
    portions = [(1 << 20) // math.isqrt(rank ** lean) + 1 for rank in range(2, number_of + 1)]
    surplus, given = total - limit - (number_of - 1), [1] * (number_of - 1)
    while surplus > 0:
        candidates = [i for i in range(number_of - 1) if given[i] < limit]
        mass, left = sum([portions[i] for i in candidates]), surplus
        for i in candidates:
            more = min(limit - given[i], max(1, left * portions[i] // mass), surplus)
            given[i] = given[i] + more
            surplus = surplus - more
    return np.array([limit] + given)


def uneven_parts(stream_key, count, total, limit, slope):
    if count == 2:
        one = jax.random.randint(stream_key, (), max(1, total - limit), min(limit, total - 1) + 1)
        return jnp.stack([one, total - one])
    lengths = jnp.asarray(profile(count, total, limit, slope), jnp.int32)
    pairs = (count - 1) // 2
    giver, sink = lengths[1:1 + 2 * pairs:2], lengths[2:2 + 2 * pairs:2]
    margin = jnp.minimum(giver - 1, limit - sink)
    shifted = jax.random.randint(jax.random.fold_in(stream_key, 1), (pairs,), 0, 1 << 20) % (margin + 1)
    lengths = lengths.at[1:1 + 2 * pairs:2].set(giver - shifted).at[2:2 + 2 * pairs:2].set(sink + shifted)
    return lengths[jax.random.permutation(jax.random.fold_in(stream_key, 2), count)]


def bell_draw(rng, dims, spread, limit, pieces=(), kind=jnp.bfloat16):
    entries = jax.random.normal(rng, dims, jnp.float32) * spread
    if len(pieces) > 0:
        entries = levels(rng, dims, pieces, -0.22, 0.18) * entries
    return jnp.clip(entries, min=-limit, max=limit).astype(kind)


def noise_with(stream_key, extent, scale, most, pieces, heavy, kind=jnp.bfloat16):
    result = scale * jax.random.normal(stream_key, extent, jnp.float32)
    if pieces:
        result = result * levels(stream_key, extent, pieces, -0.22, 0.18)
    return jnp.clip(strengthened(result, jax.random.fold_in(stream_key, 3), *heavy), -most, most).astype(kind)


def setup_inputs(seed: int = 0) -> dict:
    splits = jax.random.split(jax.random.key(seed), 21)
    return {
        "patches": noise_with(splits[0], (TOKENS, D), 1.0, 6.0, ((0, 32),), (0, 1, 32, 2.75)),
        "lead_index": set_ends(jax.random.randint(splits[1], (PACKS,), 0, LEADS), jax.random.fold_in(splits[1], 1), 0, LEADS - 1).astype(jnp.int32),
        "window_lengths": jax.vmap(lambda own: uneven_parts(own, NWIN, SEQ, WMAX, 1))(jax.random.split(splits[2], PACKS)).reshape((PACKS, NWIN)).astype(jnp.int32),
        "pad_mask": set_ends((jax.random.randint(splits[3], (TOKENS,), 0, 8) < 7).astype(jnp.int32), jax.random.fold_in(splits[3], 1), 0, 1),
        "lead_table": bell_draw(splits[4], (LEADS, D), 0.5, 3.0, ((1, 32),)),
        "attn_gain": jnp.clip(1.0 + 0.15 * jax.random.normal(splits[5], (D,), jnp.float32), 0.25, 1.75).astype(jnp.bfloat16),
        "attn_shift": bell_draw(splits[6], (D,), 0.3, 1.75, ((0, 32),)),
        "qkv_weight": bell_draw(splits[7], (D, 3 * D), D ** -0.5, 0.21875, ((0, 32),)),
        "out_weight": bell_draw(splits[8], (D, D), (D // 16) ** -0.5, 0.875, ((0, 32),)),
        "out_bias": bell_draw(splits[9], (D,), 0.3, 1.75, ((0, 32),)),
        "mlp_gain": jnp.clip(1.0 + 0.15 * jax.random.normal(splits[10], (D,), jnp.float32), 0.25, 1.75).astype(jnp.bfloat16),
        "mlp_shift": bell_draw(splits[11], (D,), 0.3, 1.75, ((0, 32),)),
        "up_weight": bell_draw(splits[12], (D, FF), D ** -0.5, 0.21875, ((0, 32),)),
        "up_bias": bell_draw(splits[13], (FF,), 0.3, 1.75, ((0, 32),)),
        "down_weight": bell_draw(splits[14], (FF, D), FF ** -0.5, 0.109375, ((0, 32),)),
        "down_bias": bell_draw(splits[15], (D,), 0.3, 1.75, ((0, 32),)),
        "head_weight": bell_draw(splits[16], (D, HOUT), (4 * D) ** -0.5, 0.109375, ((0, 32),)),
        "head_bias": bell_draw(splits[17], (HOUT,), 0.1, 0.625, ((0, 32),)),
        "act_cotangent": bell_draw(splits[18], (TOKENS, D), 1.0, 6.0, ((0, 32),)),
        "head_cotangent": bell_draw(splits[19], (TOKENS, HOUT), 1.0, 6.0, ((0, 32),)),
    }


@jax.custom_vjp
def low(v):
    return lax.optimization_barrier(v.astype(jnp.bfloat16)).astype(jnp.float32)

@jax.custom_vjp
def low_back(v):
    return v

def low_keep(v):
    return (low(v), None)

def low_pass(kept, grad):
    return (grad,)

def back_keep(v):
    return (v, None)

def back_low(kept, grad):
    return (low(grad),)
low.defvjp(low_keep, low_pass)
low_back.defvjp(back_keep, back_low)
norm_epsilon = 1e-05
score_scale = 0.125

def matmul(left, right):
    return jnp.dot(left, right, precision=lax.Precision.HIGHEST, preferred_element_type=jnp.float32)

def layer_norm(hidden, norm_gain, norm_shift):
    average = lax.optimization_barrier(jnp.mean(hidden, axis=-1, keepdims=True))
    centered = hidden - average
    variance = lax.optimization_barrier(jnp.mean(centered * centered, axis=-1, keepdims=True))
    return centered * lax.rsqrt(variance + norm_epsilon) * norm_gain + norm_shift

def gelu_exact(values):
    return 0.5 * values * (1.0 + lax.erf(values * 0.7071067811865476))

def expert_softmax(logits, experts, pixels):
    gate_part = logits[:, :experts * pixels].reshape(logits.shape[0], experts, pixels)
    largest = lax.optimization_barrier(jnp.max(gate_part, axis=1, keepdims=True))
    raised = jnp.exp(gate_part - largest)
    shares = raised / lax.optimization_barrier(jnp.sum(raised, axis=1, keepdims=True))
    return jnp.concatenate([shares.reshape(logits.shape[0], experts * pixels), logits[:, experts * pixels:]], axis=1)

def attend_pack(inputs):
    queries, keys, values, window, valid = inputs
    seq_rows = queries.shape[0]
    query_heads = queries.reshape(seq_rows, HEADS, HD)
    key_heads = keys.reshape(seq_rows, HEADS, HD)
    value_heads = values.reshape(seq_rows, HEADS, HD)
    scores = low_back(jnp.einsum('qhd,khd->hqk', query_heads, key_heads, precision=lax.Precision.HIGHEST, preferred_element_type=jnp.float32) * score_scale)
    place = jnp.arange(seq_rows, dtype=jnp.int32)
    allowed = (window[:, None] == window[None, :]) & ((valid[None, :] > 0) | (place[:, None] == place[None, :]))
    masked = jnp.where(allowed[None], scores, -1e+30)
    largest = lax.optimization_barrier(jnp.max(masked, axis=-1, keepdims=True))
    raised = jnp.exp(masked - largest)
    probs = low(raised / lax.optimization_barrier(jnp.sum(raised, axis=-1, keepdims=True)))
    mixed = jnp.einsum('hqk,khd->qhd', probs, value_heads, precision=lax.Precision.HIGHEST, preferred_element_type=jnp.float32)
    return mixed.reshape(seq_rows, HEADS * HD)

def forward_group(patch_rows, lead_rows, window, valid, weights):
    lead_table, attn_gain, attn_shift, qkv_weight, out_weight, out_bias, mlp_gain, mlp_shift, up_weight, up_bias, down_weight, down_bias, head_weight, head_bias = weights
    group_rows = patch_rows.shape[0]
    pack_count = group_rows // SEQ
    start_state = patch_rows + matmul(lead_rows, lead_table)
    attn_input = low(layer_norm(start_state, attn_gain, attn_shift))
    qkv_rows = low_back(low(matmul(attn_input, qkv_weight)))
    queries = qkv_rows[:, :D].reshape(pack_count, SEQ, D)
    keys = qkv_rows[:, D:2 * D].reshape(pack_count, SEQ, D)
    values = qkv_rows[:, 2 * D:].reshape(pack_count, SEQ, D)
    mixed = lax.map(jax.checkpoint(attend_pack), (queries, keys, values, window, valid))
    attended = low_back(low(mixed.reshape(group_rows, D)))
    mid_state = start_state + low_back(matmul(attended, out_weight) + out_bias)
    mlp_input = low(layer_norm(mid_state, mlp_gain, mlp_shift))
    pre_act = low_back(matmul(mlp_input, up_weight) + up_bias)
    act_rows = low(gelu_exact(pre_act))
    end_state = mid_state + low_back(matmul(act_rows, down_weight) + down_bias)
    outputs = low(end_state)
    logits = low_back(matmul(outputs, head_weight) + head_bias)
    return (outputs, expert_softmax(logits, EXPERTS, PIX))

def reference(patches, lead_index, window_lengths, pad_mask, lead_table, attn_gain, attn_shift, qkv_weight, out_weight, out_bias, mlp_gain, mlp_shift, up_weight, up_bias, down_weight, down_bias, head_weight, head_bias, act_cotangent, head_cotangent):
    weights = tuple((item.astype(jnp.float32) for item in (lead_table, attn_gain, attn_shift, qkv_weight, out_weight, out_bias, mlp_gain, mlp_shift, up_weight, up_bias, down_weight, down_bias, head_weight, head_bias)))
    ends = jnp.cumsum(window_lengths, axis=1).astype(jnp.int32)
    positions = jnp.arange(SEQ, dtype=jnp.int32)
    window = lax.optimization_barrier(jnp.sum((positions[None, :, None] >= ends[:, None, :]).astype(jnp.int32), axis=2)).astype(jnp.int32)
    lead_hot = (lead_index[:, None] == jnp.arange(LEADS, dtype=jnp.int32)[None, :]).astype(jnp.float32)
    valid = pad_mask.reshape(PACKS, SEQ)
    group_packs = math.gcd(PACKS, max(1, 4096 // SEQ))
    group_count = PACKS // group_packs
    group_rows = group_packs * SEQ

    def group_step(totals, inputs):
        patch_group, hot_group, window_group, valid_group, act_cot, head_cot = inputs
        hot_rows = jnp.repeat(hot_group, SEQ, axis=0)

        def apply(patch_values, weight_values):
            return forward_group(patch_values, hot_rows, window_group, valid_group, weight_values)
        results, pull = jax.vjp(apply, patch_group.astype(jnp.float32), weights)
        patch_grad, weight_grads = pull((act_cot.astype(jnp.float32), head_cot.astype(jnp.float32)))
        totals = jax.tree.map(jnp.add, totals, weight_grads)
        return (totals, (results[0].astype(jnp.bfloat16), results[1], patch_grad))
    zeros = jax.tree.map(jnp.zeros_like, weights)
    inputs = (patches.reshape(group_count, group_rows, D), lead_hot.reshape(group_count, group_packs, LEADS), window.reshape(group_count, group_packs, SEQ), valid.reshape(group_count, group_packs, SEQ), act_cotangent.reshape(group_count, group_rows, D), head_cotangent.reshape(group_count, group_rows, HOUT))
    totals, (outputs, head_out, patch_grad) = lax.scan(group_step, zeros, inputs)
    return (outputs.reshape(TOKENS, D), head_out.reshape(TOKENS, HOUT), patch_grad.reshape(TOKENS, D), totals[0], totals[1], totals[2], totals[3], totals[4], totals[5], totals[6], totals[7], totals[8], totals[9], totals[10], totals[11], totals[12], totals[13])
```

```python
from functools import partial

import jax
import jax.numpy as jnp
from jax import lax
from jax.experimental import pallas as pl
from jax.experimental.pallas import tpu as pltpu
from jax.sharding import PartitionSpec as P

HEADS = 12
PIX = 64
EXPERTS = 3
LEADS = 16


norm_epsilon = 1e-05
score_scale = 0.125


def layer_norm(hidden, norm_gain, norm_shift):
    average = jnp.mean(hidden, axis=-1, keepdims=True)
    centered = hidden - average
    variance = jnp.mean(centered * centered, axis=-1, keepdims=True)
    return centered * lax.rsqrt(variance + norm_epsilon) * norm_gain + norm_shift


def gelu_exact(values):
    return 0.5 * values * (1.0 + lax.erf(values * 0.7071067811865476))


def expert_softmax(logits, experts, pixels):
    gate_part = logits[:, : experts * pixels].reshape(logits.shape[0], experts, pixels)
    largest = jnp.max(gate_part, axis=1, keepdims=True)
    raised = jnp.exp(gate_part - largest)
    shares = raised / jnp.sum(raised, axis=1, keepdims=True)
    return jnp.concatenate(
        [shares.reshape(logits.shape[0], experts * pixels), logits[:, experts * pixels :]], axis=1
    )


def allowed_keys(query_window, key_window, key_valid, query_start):
    query_place = query_start + jnp.arange(query_window.shape[0], dtype=jnp.int32)
    key_place = jnp.arange(key_window.shape[0], dtype=jnp.int32)
    same_window = query_window[:, None] == key_window[None, :]
    usable = (key_valid[None, :] > 0) | (query_place[:, None] == key_place[None, :])
    return same_window & usable

AXES = ("dp", "fsdp")
STEPS = ((4, 4), (8, 16), (2, 2), (16, 8))


def chip_masks(lane):
    masks = []
    for place in range(16):
        mask = 0
        for step in range(4):
            if place >> step & 1:
                mask ^= STEPS[step][lane]
        masks.append(mask >> 1)
    return masks


def exchange(array, masks):
    return lax.ppermute(array, AXES, [(d, d ^ masks[d & 1]) for d in range(32)])


def whereabouts():
    device = lax.axis_index("dp") * 8 + lax.axis_index("fsdp")
    core, chip = device % 2, device // 2
    tables = jnp.array([chip_masks(0), chip_masks(1)], jnp.int32) ^ chip
    mine = jnp.where(core == 0, tables[0], tables[1])
    theirs = jnp.where(core == 0, tables[1], tables[0])
    return core, jnp.concatenate([core[None].astype(jnp.int32), mine, theirs])


def doubled(block):
    held = block[None]
    for masks in STEPS[:3]:
        held = jnp.concatenate([held, exchange(held, masks)], axis=0)
    return held, exchange(held, STEPS[3])


def halves(array, core):
    half = array.shape[1] // 2
    left, right = array[:, :half], array[:, half:]
    return jnp.where(core == 0, left, right), jnp.where(core == 0, right, left)


def in_core_order(core, mine, theirs, axis):
    return jnp.where(
        core == 0,
        jnp.concatenate([mine, theirs], axis=axis),
        jnp.concatenate([theirs, mine], axis=axis),
    )


def lane_block(shard, core):
    mine, theirs = halves(shard, core)
    return in_core_order(core, mine, exchange(theirs, (1, 1)), 0)


def place_kernel(widths, where_ref, *refs):
    sources, outs, sems = refs[:4], refs[4:-1], refs[-1]
    rows = sources[0].shape[1]
    core = where_ref[0]
    copies = []
    for side in range(2):
        lane = core if side == 0 else 1 - core
        for place in range(16):
            source = sources[2 * side + place // 8]
            row = pl.multiple_of(where_ref[1 + 16 * side + place] * rows, rows)
            start = 0
            for out, width in zip(outs, widths):
                column = pl.multiple_of(lane * width, 128)
                copies.append(
                    pltpu.make_async_copy(
                        source.at[place % 8, :, pl.ds(start, width)],
                        out.at[pl.ds(row, rows), pl.ds(column, width)],
                        sems.at[len(copies)],
                    )
                )
                start += width
    for copy in copies:
        copy.start()
    for copy in copies:
        copy.wait()


def placed(where, arrays, widths):
    rows = arrays[0].shape[1]
    return pl.pallas_call(
        partial(place_kernel, widths),
        out_shape=[jax.ShapeDtypeStruct((16 * rows, 2 * width), jnp.bfloat16) for width in widths],
        in_specs=[pl.BlockSpec(memory_space=pltpu.SMEM)] + [pl.BlockSpec(memory_space=pl.ANY)] * 4,
        out_specs=[pl.BlockSpec(memory_space=pl.ANY)] * len(widths),
        scratch_shapes=[pltpu.SemaphoreType.DMA((32 * len(widths),))],
    )(where, *arrays)


def gathered(block, where, widths):
    first, second = doubled(block)
    arrays = (first, second, exchange(first, (1, 1)), exchange(second, (1, 1)))
    return placed(where, arrays, widths)


def spread_kernel(widths, where_ref, *refs):
    sources, outs, sems = refs[: len(widths)], refs[len(widths) : -1], refs[-1]
    rows = outs[0].shape[1]
    core = where_ref[0]
    copies = []
    for side in range(2):
        lane = core if side == 0 else 1 - core
        for place in range(16):
            out = outs[place // 8 if side == 0 else 2]
            slot = place % 8 if side == 0 else place
            row = pl.multiple_of(where_ref[1 + 16 * side + place] * rows, rows)
            start = 0
            for source, width in zip(sources, widths):
                column = pl.multiple_of(lane * width, 128)
                copies.append(
                    pltpu.make_async_copy(
                        source.at[pl.ds(row, rows), pl.ds(column, width)],
                        out.at[slot, :, pl.ds(start, width)],
                        sems.at[len(copies)],
                    )
                )
                start += width
    for copy in copies:
        copy.start()
    for copy in copies:
        copy.wait()


def spread(where, arrays):
    rows = arrays[0].shape[0] // 16
    widths = [array.shape[1] // 2 for array in arrays]
    return pl.pallas_call(
        partial(spread_kernel, widths),
        out_shape=[
            jax.ShapeDtypeStruct((count, rows, sum(widths)), jnp.bfloat16) for count in (8, 8, 16)
        ],
        in_specs=[pl.BlockSpec(memory_space=pltpu.SMEM)]
        + [pl.BlockSpec(memory_space=pl.ANY)] * len(arrays),
        out_specs=[pl.BlockSpec(memory_space=pl.ANY)] * 3,
        scratch_shapes=[pltpu.SemaphoreType.DMA((32 * len(widths),))],
    )(where, *arrays)


def total(first, second):
    return first.astype(jnp.float32) + second.astype(jnp.float32)


def scattered(arrays, where, core):
    keep, send, theirs = spread(where, arrays)
    got = exchange(theirs, (1, 1))
    send = total(send, got[8:]).astype(jnp.bfloat16)
    keep = total(keep, got[:8]).astype(jnp.bfloat16)
    for masks in STEPS[:0:-1]:
        got = exchange(send, masks)
        half = keep.shape[0] // 2
        send = total(keep[half:], got[half:]).astype(jnp.bfloat16)
        keep = total(keep[:half], got[:half]).astype(jnp.bfloat16)
    block = total(keep, exchange(send, STEPS[0]))[0]
    rows = block.shape[0] // 2
    upper, lower = block[:rows], block[rows:]
    mine = jnp.where(core == 0, upper, lower)
    theirs = jnp.where(core == 0, lower, upper).astype(jnp.bfloat16)
    other = exchange(theirs, (1, 1)).astype(jnp.float32)
    pieces, start = [], 0
    for array in arrays:
        width = array.shape[1] // 2
        pieces.append(
            in_core_order(
                core, mine[:, start : start + width], other[:, start : start + width], 1
            )
        )
        start += width
    return pieces


def shards(
    patches,
    lead_index,
    window_lengths,
    pad_mask,
    lead_table,
    attn_gain,
    attn_shift,
    qkv_weight,
    out_weight,
    out_bias,
    mlp_gain,
    mlp_shift,
    up_weight,
    up_bias,
    down_weight,
    down_bias,
    head_weight,
    head_bias,
    act_cotangent,
    head_cotangent,
):
    core, where = whereabouts()
    small = jnp.concatenate(
        [
            attn_gain[:, None],
            attn_shift[:, None],
            out_bias[:, None],
            mlp_gain[:, None],
            mlp_shift[:, None],
            down_bias[:, None],
            up_bias.reshape(24, 4),
            head_bias.reshape(24, 6),
            lead_table.T,
            jnp.zeros((24, 96), jnp.bfloat16),
        ],
        axis=1,
    )
    small = jnp.concatenate([small, exchange(small, (1, 1))], axis=0)
    small = jnp.where(core == 0, small, jnp.concatenate([small[24:], small[:24]], axis=0))
    front = jnp.concatenate([lane_block(qkv_weight, core), lane_block(out_weight, core), small], axis=1)
    qkv_full, out_full, small_full = gathered(front, where, (1152, 384, 128))
    (up_full,) = gathered(lane_block(up_weight, core), where, (1536,))
    (down_full,) = gathered(lane_block(down_weight, core), where, (384,))
    (head_full,) = gathered(lane_block(head_weight, core), where, (2304,))
    small_full = small_full[:, :32]
    gain_one, shift_one, out_bias_full, gain_two, shift_two, down_bias_full = [
        small_full[:, i] for i in range(6)
    ]
    up_bias_full = small_full[:, 6:10].reshape(3072)
    head_bias_full = small_full[:, 10:16].reshape(4608)
    table_full = small_full[:, 16:32].T
    token_rows, width = patches.shape
    head_dim = width // HEADS
    block_rows = min(512, token_rows)
    block_count = token_rows // block_rows
    ends = jnp.cumsum(window_lengths[0])
    positions = jnp.arange(token_rows, dtype=jnp.int32)
    window = jnp.sum((positions[:, None] >= ends[None, :]).astype(jnp.int32), axis=1)
    lead_hot = (jnp.arange(LEADS, dtype=jnp.int32) == lead_index[0]).astype(jnp.float32)
    lead_row = jnp.sum(lead_hot[:, None] * table_full.astype(jnp.float32), axis=0)
    start_state = patches.astype(jnp.float32) + lead_row[None, :]
    normed_one, pull_one = jax.vjp(
        layer_norm, start_state, gain_one.astype(jnp.float32), shift_one.astype(jnp.float32)
    )
    attn_input = normed_one.astype(jnp.bfloat16)
    qkv_rows = jnp.dot(attn_input, qkv_full, preferred_element_type=jnp.float32).astype(
        jnp.bfloat16
    )
    queries = qkv_rows[:, :width].reshape(block_count, block_rows, HEADS, head_dim)
    keys = qkv_rows[:, width : 2 * width].reshape(token_rows, HEADS, head_dim)
    values = qkv_rows[:, 2 * width :].reshape(token_rows, HEADS, head_dim)
    query_windows = window.reshape(block_count, block_rows)
    block_starts = jnp.arange(block_count, dtype=jnp.int32) * block_rows

    def block_scores(query_block, window_block, block_start):
        scores = (
            jnp.einsum("qhd,khd->hqk", query_block, keys, preferred_element_type=jnp.float32)
            * score_scale
        )
        allowed = allowed_keys(window_block, window, pad_mask, block_start)
        return jnp.where(allowed[None], scores, -1e30)

    def forward_block(inputs):
        query_block, window_block, block_start = inputs
        masked = block_scores(query_block, window_block, block_start)
        largest = jnp.max(masked, axis=-1, keepdims=True)
        raised = jnp.exp(masked - largest)
        total = jnp.sum(raised, axis=-1, keepdims=True)
        probs = (raised / total).astype(jnp.bfloat16)
        mixed = jnp.einsum("hqk,khd->qhd", probs, values, preferred_element_type=jnp.float32)
        return (
            mixed.reshape(block_rows, width).astype(jnp.bfloat16),
            (largest + jnp.log(total))[:, :, 0],
        )

    mixed_blocks, log_totals = lax.map(forward_block, (queries, query_windows, block_starts))
    attended = mixed_blocks.reshape(token_rows, width)
    mid_state = (
        start_state
        + jnp.dot(attended, out_full, preferred_element_type=jnp.float32)
        + out_bias_full.astype(jnp.float32)
    )
    normed_two, pull_two = jax.vjp(
        layer_norm, mid_state, gain_two.astype(jnp.float32), shift_two.astype(jnp.float32)
    )
    mlp_input = normed_two.astype(jnp.bfloat16)
    pre_act = jnp.dot(mlp_input, up_full, preferred_element_type=jnp.float32) + up_bias_full.astype(
        jnp.float32
    )
    activated, pull_act = jax.vjp(gelu_exact, pre_act)
    act_rows = activated.astype(jnp.bfloat16)
    end_state = (
        mid_state
        + jnp.dot(act_rows, down_full, preferred_element_type=jnp.float32)
        + down_bias_full.astype(jnp.float32)
    )
    outputs = end_state.astype(jnp.bfloat16)
    logits = jnp.dot(
        outputs, head_full, preferred_element_type=jnp.float32
    ) + head_bias_full.astype(jnp.float32)
    head_out, pull_head = jax.vjp(partial(expert_softmax, experts=EXPERTS, pixels=PIX), logits)
    up_back, down_back, head_back = up_full, down_full, head_full
    qkv_back, out_back = qkv_full, out_full
    logit_grad = pull_head(head_cotangent.astype(jnp.float32))[0].astype(jnp.bfloat16)
    head_bias_term = jnp.sum(logit_grad.astype(jnp.float32), axis=0)
    head_term = jnp.einsum("td,tn->dn", outputs, logit_grad, preferred_element_type=jnp.float32)
    end_grad = act_cotangent.astype(jnp.float32) + jnp.einsum(
        "tn,dn->td", logit_grad, head_back, preferred_element_type=jnp.float32
    )
    branch_grad = end_grad.astype(jnp.bfloat16)
    down_bias_term = jnp.sum(branch_grad.astype(jnp.float32), axis=0)
    down_term = jnp.einsum("tf,td->fd", act_rows, branch_grad, preferred_element_type=jnp.float32)
    act_grad = jnp.einsum("td,fd->tf", branch_grad, down_back, preferred_element_type=jnp.float32)
    pre_grad = pull_act(act_grad)[0].astype(jnp.bfloat16)
    up_bias_term = jnp.sum(pre_grad.astype(jnp.float32), axis=0)
    up_term = jnp.einsum("td,tf->df", mlp_input, pre_grad, preferred_element_type=jnp.float32)
    normed_two_grad = jnp.einsum("tf,df->td", pre_grad, up_back, preferred_element_type=jnp.float32)
    state_grad_two, gain_two_term, shift_two_term = pull_two(normed_two_grad)
    mid_grad = end_grad + state_grad_two
    out_grad = mid_grad.astype(jnp.bfloat16)
    out_bias_term = jnp.sum(out_grad.astype(jnp.float32), axis=0)
    out_term = jnp.einsum("td,te->de", attended, out_grad, preferred_element_type=jnp.float32)
    mixed_grad = jnp.einsum(
        "te,de->td", out_grad, out_back, preferred_element_type=jnp.float32
    ).astype(jnp.bfloat16)
    grad_blocks = mixed_grad.reshape(block_count, block_rows, HEADS, head_dim)

    def backward_block(carry, inputs):
        key_sum, value_sum = carry
        query_block, grad_block, window_block, total_block, block_start = inputs
        masked = block_scores(query_block, window_block, block_start)
        probs = jnp.exp(masked - total_block[:, :, None])
        prob_grad = jnp.einsum(
            "qhd,khd->hqk", grad_block, values, preferred_element_type=jnp.float32
        )
        inner = jnp.sum(probs * prob_grad, axis=-1, keepdims=True)
        score_grad = (probs * (prob_grad - inner)).astype(jnp.bfloat16)
        query_grad = (
            jnp.einsum("hqk,khd->qhd", score_grad, keys, preferred_element_type=jnp.float32)
            * score_scale
        )
        key_sum = (
            key_sum
            + jnp.einsum(
                "hqk,qhd->khd", score_grad, query_block, preferred_element_type=jnp.float32
            )
            * score_scale
        )
        value_sum = value_sum + jnp.einsum(
            "hqk,qhd->khd",
            probs.astype(jnp.bfloat16),
            grad_block,
            preferred_element_type=jnp.float32,
        )
        return ((key_sum, value_sum), query_grad.reshape(block_rows, width))

    zero_keys = jnp.zeros((token_rows, HEADS, head_dim), jnp.float32)
    (key_grad, value_grad), query_grads = lax.scan(
        backward_block,
        (zero_keys, zero_keys),
        (queries, grad_blocks, query_windows, log_totals, block_starts),
    )
    qkv_grad = jnp.concatenate(
        [
            query_grads.reshape(token_rows, width),
            key_grad.reshape(token_rows, width),
            value_grad.reshape(token_rows, width),
        ],
        axis=1,
    ).astype(jnp.bfloat16)
    qkv_term = jnp.einsum("td,te->de", attn_input, qkv_grad, preferred_element_type=jnp.float32)
    normed_one_grad = jnp.einsum(
        "te,de->td", qkv_grad, qkv_back, preferred_element_type=jnp.float32
    )
    state_grad_one, gain_one_term, shift_one_term = pull_one(normed_one_grad)
    patch_grad = mid_grad + state_grad_one
    lead_term = lead_hot[:, None] * jnp.sum(patch_grad, axis=0)[None, :]
    (head_grad,) = scattered([head_term.astype(jnp.bfloat16)], where, core)
    (down_grad,) = scattered([down_term.astype(jnp.bfloat16)], where, core)
    (up_grad,) = scattered([up_term.astype(jnp.bfloat16)], where, core)
    small_term = jnp.concatenate(
        [
            gain_one_term[:, None],
            shift_one_term[:, None],
            out_bias_term[:, None],
            gain_two_term[:, None],
            shift_two_term[:, None],
            down_bias_term[:, None],
            up_bias_term.reshape(768, 4),
            head_bias_term.reshape(768, 6),
            lead_term.T,
            jnp.zeros((768, 224), jnp.float32),
        ],
        axis=1,
    )
    qkv_grad_sum, out_grad_sum, small_grad = scattered(
        [
            qkv_term.astype(jnp.bfloat16),
            out_term.astype(jnp.bfloat16),
            small_term.astype(jnp.bfloat16),
        ],
        where,
        core,
    )
    front_grads = (
        small_grad[:, 16:32].T,
        small_grad[:, 0],
        small_grad[:, 1],
        qkv_grad_sum,
        out_grad_sum,
        small_grad[:, 2],
    )
    rear_grads = (
        small_grad[:, 3],
        small_grad[:, 4],
        up_grad,
        small_grad[:, 6:10].reshape(96),
        down_grad,
        small_grad[:, 5],
        head_grad,
        small_grad[:, 10:16].reshape(144),
    )
    return (
        outputs,
        head_out,
        patch_grad,
        front_grads[0],
        front_grads[1],
        front_grads[2],
        front_grads[3],
        front_grads[4],
        front_grads[5],
        rear_grads[0],
        rear_grads[1],
        rear_grads[2],
        rear_grads[3],
        rear_grads[4],
        rear_grads[5],
        rear_grads[6],
        rear_grads[7],
    )


def plain_shards(
    patches,
    lead_index,
    window_lengths,
    pad_mask,
    lead_table,
    attn_gain,
    attn_shift,
    qkv_weight,
    out_weight,
    out_bias,
    mlp_gain,
    mlp_shift,
    up_weight,
    up_bias,
    down_weight,
    down_bias,
    head_weight,
    head_bias,
    act_cotangent,
    head_cotangent,
):
    front = (
        lax.all_gather(lead_table, ("dp", "fsdp"), axis=1, tiled=True),
        lax.all_gather(attn_gain, ("dp", "fsdp"), axis=0, tiled=True),
        lax.all_gather(attn_shift, ("dp", "fsdp"), axis=0, tiled=True),
        lax.all_gather(qkv_weight, ("dp", "fsdp"), axis=0, tiled=True),
        lax.all_gather(out_weight, ("dp", "fsdp"), axis=0, tiled=True),
        lax.all_gather(out_bias, ("dp", "fsdp"), axis=0, tiled=True),
    )
    rear = (
        lax.all_gather(mlp_gain, ("dp", "fsdp"), axis=0, tiled=True),
        lax.all_gather(mlp_shift, ("dp", "fsdp"), axis=0, tiled=True),
        lax.all_gather(up_weight, ("dp", "fsdp"), axis=0, tiled=True),
        lax.all_gather(up_bias, ("dp", "fsdp"), axis=0, tiled=True),
        lax.all_gather(down_weight, ("dp", "fsdp"), axis=0, tiled=True),
        lax.all_gather(down_bias, ("dp", "fsdp"), axis=0, tiled=True),
        lax.all_gather(head_weight, ("dp", "fsdp"), axis=0, tiled=True),
        lax.all_gather(head_bias, ("dp", "fsdp"), axis=0, tiled=True),
    )
    table_full, gain_one, shift_one, qkv_full, out_full, out_bias_full = front
    (
        gain_two,
        shift_two,
        up_full,
        up_bias_full,
        down_full,
        down_bias_full,
        head_full,
        head_bias_full,
    ) = rear
    token_rows, width = patches.shape
    head_dim = width // HEADS
    block_rows = min(512, token_rows)
    block_count = token_rows // block_rows
    ends = jnp.cumsum(window_lengths[0])
    positions = jnp.arange(token_rows, dtype=jnp.int32)
    window = jnp.sum((positions[:, None] >= ends[None, :]).astype(jnp.int32), axis=1)
    lead_hot = (jnp.arange(LEADS, dtype=jnp.int32) == lead_index[0]).astype(jnp.float32)
    lead_row = jnp.sum(lead_hot[:, None] * table_full.astype(jnp.float32), axis=0)
    start_state = patches.astype(jnp.float32) + lead_row[None, :]
    normed_one, pull_one = jax.vjp(
        layer_norm, start_state, gain_one.astype(jnp.float32), shift_one.astype(jnp.float32)
    )
    attn_input = normed_one.astype(jnp.bfloat16)
    qkv_rows = jnp.dot(attn_input, qkv_full, preferred_element_type=jnp.float32).astype(
        jnp.bfloat16
    )
    queries = qkv_rows[:, :width].reshape(block_count, block_rows, HEADS, head_dim)
    keys = qkv_rows[:, width : 2 * width].reshape(token_rows, HEADS, head_dim)
    values = qkv_rows[:, 2 * width :].reshape(token_rows, HEADS, head_dim)
    query_windows = window.reshape(block_count, block_rows)
    block_starts = jnp.arange(block_count, dtype=jnp.int32) * block_rows

    def block_scores(query_block, window_block, block_start):
        scores = (
            jnp.einsum("qhd,khd->hqk", query_block, keys, preferred_element_type=jnp.float32)
            * score_scale
        )
        allowed = allowed_keys(window_block, window, pad_mask, block_start)
        return jnp.where(allowed[None], scores, -1e30)

    def forward_block(inputs):
        query_block, window_block, block_start = inputs
        masked = block_scores(query_block, window_block, block_start)
        largest = jnp.max(masked, axis=-1, keepdims=True)
        raised = jnp.exp(masked - largest)
        total = jnp.sum(raised, axis=-1, keepdims=True)
        probs = (raised / total).astype(jnp.bfloat16)
        mixed = jnp.einsum("hqk,khd->qhd", probs, values, preferred_element_type=jnp.float32)
        return (
            mixed.reshape(block_rows, width).astype(jnp.bfloat16),
            (largest + jnp.log(total))[:, :, 0],
        )

    mixed_blocks, log_totals = lax.map(forward_block, (queries, query_windows, block_starts))
    attended = mixed_blocks.reshape(token_rows, width)
    mid_state = (
        start_state
        + jnp.dot(attended, out_full, preferred_element_type=jnp.float32)
        + out_bias_full.astype(jnp.float32)
    )
    normed_two, pull_two = jax.vjp(
        layer_norm, mid_state, gain_two.astype(jnp.float32), shift_two.astype(jnp.float32)
    )
    mlp_input = normed_two.astype(jnp.bfloat16)
    pre_act = jnp.dot(mlp_input, up_full, preferred_element_type=jnp.float32) + up_bias_full.astype(
        jnp.float32
    )
    activated, pull_act = jax.vjp(gelu_exact, pre_act)
    act_rows = activated.astype(jnp.bfloat16)
    end_state = (
        mid_state
        + jnp.dot(act_rows, down_full, preferred_element_type=jnp.float32)
        + down_bias_full.astype(jnp.float32)
    )
    outputs = end_state.astype(jnp.bfloat16)
    logits = jnp.dot(
        outputs, head_full, preferred_element_type=jnp.float32
    ) + head_bias_full.astype(jnp.float32)
    head_out, pull_head = jax.vjp(partial(expert_softmax, experts=EXPERTS, pixels=PIX), logits)
    up_back, down_back, head_back = (
        lax.all_gather(up_weight, ("dp", "fsdp"), axis=0, tiled=True),
        lax.all_gather(down_weight, ("dp", "fsdp"), axis=0, tiled=True),
        lax.all_gather(head_weight, ("dp", "fsdp"), axis=0, tiled=True),
    )
    qkv_back, out_back = (
        lax.all_gather(qkv_weight, ("dp", "fsdp"), axis=0, tiled=True),
        lax.all_gather(out_weight, ("dp", "fsdp"), axis=0, tiled=True),
    )
    logit_grad = pull_head(head_cotangent.astype(jnp.float32))[0].astype(jnp.bfloat16)
    head_bias_term = jnp.sum(logit_grad.astype(jnp.float32), axis=0)
    head_term = jnp.einsum("td,tn->dn", outputs, logit_grad, preferred_element_type=jnp.float32)
    end_grad = act_cotangent.astype(jnp.float32) + jnp.einsum(
        "tn,dn->td", logit_grad, head_back, preferred_element_type=jnp.float32
    )
    branch_grad = end_grad.astype(jnp.bfloat16)
    down_bias_term = jnp.sum(branch_grad.astype(jnp.float32), axis=0)
    down_term = jnp.einsum("tf,td->fd", act_rows, branch_grad, preferred_element_type=jnp.float32)
    act_grad = jnp.einsum("td,fd->tf", branch_grad, down_back, preferred_element_type=jnp.float32)
    pre_grad = pull_act(act_grad)[0].astype(jnp.bfloat16)
    up_bias_term = jnp.sum(pre_grad.astype(jnp.float32), axis=0)
    up_term = jnp.einsum("td,tf->df", mlp_input, pre_grad, preferred_element_type=jnp.float32)
    normed_two_grad = jnp.einsum("tf,df->td", pre_grad, up_back, preferred_element_type=jnp.float32)
    state_grad_two, gain_two_term, shift_two_term = pull_two(normed_two_grad)
    (
        gain_part,
        shift_part,
        up_part,
        up_bias_part,
        down_part,
        down_bias_part,
        head_part,
        head_bias_part,
    ) = (
        lax.psum_scatter(
            gain_two_term.astype(jnp.bfloat16), "dp", scatter_dimension=0, tiled=True
        ).astype(jnp.float32),
        lax.psum_scatter(
            shift_two_term.astype(jnp.bfloat16), "dp", scatter_dimension=0, tiled=True
        ).astype(jnp.float32),
        lax.psum_scatter(
            up_term.astype(jnp.bfloat16), "dp", scatter_dimension=0, tiled=True
        ).astype(jnp.float32),
        lax.psum_scatter(
            up_bias_term.astype(jnp.bfloat16), "dp", scatter_dimension=0, tiled=True
        ).astype(jnp.float32),
        lax.psum_scatter(
            down_term.astype(jnp.bfloat16), "dp", scatter_dimension=0, tiled=True
        ).astype(jnp.float32),
        lax.psum_scatter(
            down_bias_term.astype(jnp.bfloat16), "dp", scatter_dimension=0, tiled=True
        ).astype(jnp.float32),
        lax.psum_scatter(
            head_term.astype(jnp.bfloat16), "dp", scatter_dimension=0, tiled=True
        ).astype(jnp.float32),
        lax.psum_scatter(
            head_bias_term.astype(jnp.bfloat16), "dp", scatter_dimension=0, tiled=True
        ).astype(jnp.float32),
    )
    rear_grads = (
        lax.psum_scatter(gain_part, "fsdp", scatter_dimension=0, tiled=True),
        lax.psum_scatter(shift_part, "fsdp", scatter_dimension=0, tiled=True),
        lax.psum_scatter(up_part, "fsdp", scatter_dimension=0, tiled=True),
        lax.psum_scatter(up_bias_part, "fsdp", scatter_dimension=0, tiled=True),
        lax.psum_scatter(down_part, "fsdp", scatter_dimension=0, tiled=True),
        lax.psum_scatter(down_bias_part, "fsdp", scatter_dimension=0, tiled=True),
        lax.psum_scatter(head_part, "fsdp", scatter_dimension=0, tiled=True),
        lax.psum_scatter(head_bias_part, "fsdp", scatter_dimension=0, tiled=True),
    )
    mid_grad = end_grad + state_grad_two
    out_grad = mid_grad.astype(jnp.bfloat16)
    out_bias_term = jnp.sum(out_grad.astype(jnp.float32), axis=0)
    out_term = jnp.einsum("td,te->de", attended, out_grad, preferred_element_type=jnp.float32)
    mixed_grad = jnp.einsum(
        "te,de->td", out_grad, out_back, preferred_element_type=jnp.float32
    ).astype(jnp.bfloat16)
    grad_blocks = mixed_grad.reshape(block_count, block_rows, HEADS, head_dim)

    def backward_block(carry, inputs):
        key_sum, value_sum = carry
        query_block, grad_block, window_block, total_block, block_start = inputs
        masked = block_scores(query_block, window_block, block_start)
        probs = jnp.exp(masked - total_block[:, :, None])
        prob_grad = jnp.einsum(
            "qhd,khd->hqk", grad_block, values, preferred_element_type=jnp.float32
        )
        inner = jnp.sum(probs * prob_grad, axis=-1, keepdims=True)
        score_grad = (probs * (prob_grad - inner)).astype(jnp.bfloat16)
        query_grad = (
            jnp.einsum("hqk,khd->qhd", score_grad, keys, preferred_element_type=jnp.float32)
            * score_scale
        )
        key_sum = (
            key_sum
            + jnp.einsum(
                "hqk,qhd->khd", score_grad, query_block, preferred_element_type=jnp.float32
            )
            * score_scale
        )
        value_sum = value_sum + jnp.einsum(
            "hqk,qhd->khd",
            probs.astype(jnp.bfloat16),
            grad_block,
            preferred_element_type=jnp.float32,
        )
        return ((key_sum, value_sum), query_grad.reshape(block_rows, width))

    zero_keys = jnp.zeros((token_rows, HEADS, head_dim), jnp.float32)
    (key_grad, value_grad), query_grads = lax.scan(
        backward_block,
        (zero_keys, zero_keys),
        (queries, grad_blocks, query_windows, log_totals, block_starts),
    )
    qkv_grad = jnp.concatenate(
        [
            query_grads.reshape(token_rows, width),
            key_grad.reshape(token_rows, width),
            value_grad.reshape(token_rows, width),
        ],
        axis=1,
    ).astype(jnp.bfloat16)
    qkv_term = jnp.einsum("td,te->de", attn_input, qkv_grad, preferred_element_type=jnp.float32)
    normed_one_grad = jnp.einsum(
        "te,de->td", qkv_grad, qkv_back, preferred_element_type=jnp.float32
    )
    state_grad_one, gain_one_term, shift_one_term = pull_one(normed_one_grad)
    patch_grad = mid_grad + state_grad_one
    lead_term = lead_hot[:, None] * jnp.sum(patch_grad, axis=0)[None, :]
    lead_part, gain_one_part, shift_one_part, qkv_part, out_part, out_bias_part = (
        lax.psum_scatter(
            lead_term.astype(jnp.bfloat16), "dp", scatter_dimension=1, tiled=True
        ).astype(jnp.float32),
        lax.psum_scatter(
            gain_one_term.astype(jnp.bfloat16), "dp", scatter_dimension=0, tiled=True
        ).astype(jnp.float32),
        lax.psum_scatter(
            shift_one_term.astype(jnp.bfloat16), "dp", scatter_dimension=0, tiled=True
        ).astype(jnp.float32),
        lax.psum_scatter(
            qkv_term.astype(jnp.bfloat16), "dp", scatter_dimension=0, tiled=True
        ).astype(jnp.float32),
        lax.psum_scatter(
            out_term.astype(jnp.bfloat16), "dp", scatter_dimension=0, tiled=True
        ).astype(jnp.float32),
        lax.psum_scatter(
            out_bias_term.astype(jnp.bfloat16), "dp", scatter_dimension=0, tiled=True
        ).astype(jnp.float32),
    )
    front_grads = (
        lax.psum_scatter(lead_part, "fsdp", scatter_dimension=1, tiled=True),
        lax.psum_scatter(gain_one_part, "fsdp", scatter_dimension=0, tiled=True),
        lax.psum_scatter(shift_one_part, "fsdp", scatter_dimension=0, tiled=True),
        lax.psum_scatter(qkv_part, "fsdp", scatter_dimension=0, tiled=True),
        lax.psum_scatter(out_part, "fsdp", scatter_dimension=0, tiled=True),
        lax.psum_scatter(out_bias_part, "fsdp", scatter_dimension=0, tiled=True),
    )
    return (
        outputs,
        head_out,
        patch_grad,
        front_grads[0],
        front_grads[1],
        front_grads[2],
        front_grads[3],
        front_grads[4],
        front_grads[5],
        rear_grads[0],
        rear_grads[1],
        rear_grads[2],
        rear_grads[3],
        rear_grads[4],
        rear_grads[5],
        rear_grads[6],
        rear_grads[7],
    )


def solution(mesh):
    in_specs = (
        P(("dp", "fsdp"), None),
        P(("dp", "fsdp")),
        P(("dp", "fsdp"), None),
        P(("dp", "fsdp")),
        P(None, ("dp", "fsdp")),
        P(("dp", "fsdp")),
        P(("dp", "fsdp")),
        P(("dp", "fsdp"), None),
        P(("dp", "fsdp"), None),
        P(("dp", "fsdp")),
        P(("dp", "fsdp")),
        P(("dp", "fsdp")),
        P(("dp", "fsdp"), None),
        P(("dp", "fsdp")),
        P(("dp", "fsdp"), None),
        P(("dp", "fsdp")),
        P(("dp", "fsdp"), None),
        P(("dp", "fsdp")),
        P(("dp", "fsdp"), None),
        P(("dp", "fsdp"), None),
    )
    out_specs = (
        P(("dp", "fsdp"), None),
        P(("dp", "fsdp"), None),
        P(("dp", "fsdp"), None),
        P(None, ("dp", "fsdp")),
        P(("dp", "fsdp")),
        P(("dp", "fsdp")),
        P(("dp", "fsdp"), None),
        P(("dp", "fsdp"), None),
        P(("dp", "fsdp")),
        P(("dp", "fsdp")),
        P(("dp", "fsdp")),
        P(("dp", "fsdp"), None),
        P(("dp", "fsdp")),
        P(("dp", "fsdp"), None),
        P(("dp", "fsdp")),
        P(("dp", "fsdp"), None),
        P(("dp", "fsdp")),
    )
    body = shards if dict(mesh.shape) == {"dp": 4, "fsdp": 8} else plain_shards
    return jax.shard_map(body, mesh=mesh, in_specs=in_specs, out_specs=out_specs, check_vma=False)
```

```python
import math
from functools import partial

import jax
import jax.numpy as jnp
from jax import lax
from jax.experimental import pallas as pl
from jax.experimental.pallas import tpu as pltpu
from jax.sharding import PartitionSpec as P

HEADS = 12
PIX = 64
EXPERTS = 3
LEADS = 16


norm_epsilon = 1e-05
score_scale = 0.125


def layer_norm(hidden, norm_gain, norm_shift):
    average = jnp.mean(hidden, axis=-1, keepdims=True)
    centered = hidden - average
    variance = jnp.mean(centered * centered, axis=-1, keepdims=True)
    return centered * lax.rsqrt(variance + norm_epsilon) * norm_gain + norm_shift


def gelu_exact(values):
    return 0.5 * values * (1.0 + lax.erf(values * 0.7071067811865476))


def expert_softmax(logits, experts, pixels):
    gate_part = logits[:, : experts * pixels].reshape(logits.shape[0], experts, pixels)
    largest = jnp.max(gate_part, axis=1, keepdims=True)
    raised = jnp.exp(gate_part - largest)
    shares = raised / jnp.sum(raised, axis=1, keepdims=True)
    return jnp.concatenate(
        [shares.reshape(logits.shape[0], experts * pixels), logits[:, experts * pixels :]], axis=1
    )


def allowed_keys(query_window, key_window, key_valid, query_start):
    query_place = query_start + jnp.arange(query_window.shape[0], dtype=jnp.int32)
    key_place = jnp.arange(key_window.shape[0], dtype=jnp.int32)
    same_window = query_window[:, None] == key_window[None, :]
    usable = (key_valid[None, :] > 0) | (query_place[:, None] == key_place[None, :])
    return same_window & usable


AXES = ("dp", "fsdp")
STEPS = ((4, 4), (8, 16), (2, 2), (16, 8))
SIBLING = (1, 1)
WIDTH = 768
TOKENS = 512
GATE = 512
F32 = jnp.float32
BF16 = jnp.bfloat16
VMEM = pl.BlockSpec(memory_space=pltpu.VMEM)
ANY = pl.BlockSpec(memory_space=pl.ANY)
QKV_PART, OUT_PART, GATE_PART, SMALL_PART = (0, 1152), (1152, 384), (1536, 256), (1792, 128)


def chip_masks(lane):
    masks = []
    for place in range(16):
        mask = 0
        for step in range(4):
            if place >> step & 1:
                mask ^= STEPS[step][lane]
        masks.append(mask >> 1)
    return masks


def exchange(array, masks):
    return lax.ppermute(array, AXES, [(d, d ^ masks[d & 1]) for d in range(32)])


def whereabouts():
    device = lax.axis_index("dp") * 8 + lax.axis_index("fsdp")
    core, chip = device % 2, device // 2
    tables = jnp.array([chip_masks(0), chip_masks(1)], jnp.int32) ^ chip
    mine = jnp.where(core == 0, tables[0], tables[1])
    theirs = jnp.where(core == 0, tables[1], tables[0])
    return core, jnp.concatenate([core[None].astype(jnp.int32), mine, theirs])


def halves(array, core):
    half = array.shape[1] // 2
    left, right = array[:, :half], array[:, half:]
    return jnp.where(core == 0, left, right), jnp.where(core == 0, right, left)


def in_core_order(core, mine, theirs, axis):
    return jnp.where(
        core == 0,
        jnp.concatenate([mine, theirs], axis=axis),
        jnp.concatenate([theirs, mine], axis=axis),
    )


def gathered(parts, small, core):
    pairs = [halves(part, core) for part in parts]
    mine = jnp.concatenate([pair[0] for pair in pairs] + small, axis=1)
    theirs = jnp.concatenate([pair[1] for pair in pairs] + small, axis=1)
    held = in_core_order(core, mine, exchange(theirs, SIBLING), 0)[None]
    for masks in STEPS[:3]:
        held = jnp.concatenate([held, exchange(held, masks)], axis=0)
    other = exchange(held, STEPS[3])
    return held, other, exchange(held, SIBLING), exchange(other, SIBLING)


def total(first, second):
    return first.astype(F32) + second.astype(F32)


def scattered(keep, send, core, widths):
    for masks in STEPS[:0:-1]:
        got = exchange(send, masks)
        half = keep.shape[0] // 2
        send = total(keep[half:], got[half:]).astype(BF16)
        keep = total(keep[:half], got[:half]).astype(BF16)
    block = total(keep, exchange(send, STEPS[0]))[0]
    rows = block.shape[0] // 2
    upper, lower = block[:rows], block[rows:]
    mine = jnp.where(core == 0, upper, lower)
    theirs = jnp.where(core == 0, lower, upper).astype(BF16)
    other = exchange(theirs, SIBLING).astype(F32)
    pieces, start = [], 0
    for width in widths:
        span = slice(start, start + width)
        pieces.append(in_core_order(core, mine[:, span], other[:, span], 1))
        start += width
    return pieces


def across(first, second):
    return lax.dot_general(first, second, (((1,), (1,)), ((), ())), preferred_element_type=F32)


def down_rows(first, second):
    return lax.dot_general(first, second, (((0,), (0,)), ((), ())), preferred_element_type=F32)


def times(first, second):
    return jnp.dot(first, second, preferred_element_type=F32)


def block_copies(where, sources, part, target, sems, side):
    start, width = part
    rows = sources[0].shape[1]
    copies = []
    for place in range(16):
        row = pl.multiple_of(where[1 + 16 * side + place] * rows, rows)
        copies.append(
            pltpu.make_async_copy(
                sources[2 * side + place // 8].at[place % 8, :, pl.ds(start, width)],
                target.at[side, pl.ds(row, rows), :],
                sems.at[side, place],
            )
        )
    return copies


def start_blocks(*args):
    for side in range(2):
        for copy in block_copies(*args, side):
            copy.start()


def wait_blocks(side, *args):
    for copy in block_copies(*args, side):
        copy.wait()


def lane_columns(where, side, width):
    return pl.ds(pl.multiple_of((where[0] ^ side) * width, 128), width)


def tile_columns(tile, width):
    return pl.ds(pl.multiple_of(tile * width, 128), width)


def mean_and_scale(hidden):
    average = jnp.mean(hidden, axis=1, keepdims=True)
    centered = hidden - average
    variance = jnp.mean(centered * centered, axis=1, keepdims=True)
    return centered, lax.rsqrt(variance + norm_epsilon)


def norm_backward(hidden, gain, upstream):
    centered, scale = mean_and_scale(hidden)
    normed = centered * scale
    gain_grad = jnp.sum(upstream * normed, axis=0, keepdims=True)
    shift_grad = jnp.sum(upstream, axis=0, keepdims=True)
    scaled = upstream * gain
    first = jnp.mean(scaled, axis=1, keepdims=True)
    second = jnp.mean(scaled * normed, axis=1, keepdims=True)
    return scale * (scaled - first - normed * second), gain_grad, shift_grad


def call(kernel, grid, operands, in_specs, outs, scratch, flops):
    shapes = [jax.ShapeDtypeStruct(shape, kind) for shape, kind, _ in outs]
    size = sum(math.prod(shape.shape) * shape.dtype.itemsize for shape in shapes)
    size += sum(math.prod(item.shape) * item.dtype.itemsize for item in operands)
    return pl.pallas_call(
        kernel,
        out_shape=shapes,
        grid_spec=pltpu.PrefetchScalarGridSpec(
            num_scalar_prefetch=1,
            grid=(grid,),
            in_specs=in_specs,
            out_specs=[spec for _, _, spec in outs],
            scratch_shapes=scratch,
        ),
        compiler_params=pltpu.CompilerParams(vmem_limit_bytes=48 * 1024 * 1024),
        cost_estimate=pl.CostEstimate(flops=flops, bytes_accessed=size, transcendentals=0),
    )(*operands)


def whole(shape):
    return pl.BlockSpec(shape, lambda step, where: (0,) * len(shape))


def side_tile(rows, width, tiles, first=0, lead=0):
    def place(step, where):
        after = jnp.maximum(step - lead, 0)
        side = after // tiles
        column = first + (where[0] ^ side) * tiles + after % tiles
        return 0, jnp.where(step < lead, 0, column)

    return pl.BlockSpec((rows, width), place)


def weight_scratch(rows, width):
    return [pltpu.VMEM((2, rows, width), BF16), pltpu.SemaphoreType.DMA((2, 16))]


def front_kernel(
    where, lead, patches, w0, w1, w2, w3, out, turned, qkv, small, weight, sems, smalls, small_sems
):
    step = pl.program_id(0)
    loads = (where, (w0, w1, w2, w3), QKV_PART, weight, sems)
    small_loads = (where, (w0, w1, w2, w3), SMALL_PART, smalls, small_sems)

    @pl.when(step == 0)
    def _():
        for copy in block_copies(*small_loads, 0):
            copy.start()
        start_blocks(*loads)
        wait_blocks(0, *small_loads)
        rows = smalls[0].astype(F32).T
        places = lax.broadcasted_iota(jnp.int32, (LEADS, WIDTH), 0)
        lead_row = jnp.sum(
            jnp.where(places == lead[0], rows[16 : 16 + LEADS], 0.0), axis=0, keepdims=True
        )
        small[...] = rows[:32]
        small[16:17, :] = lead_row
        centered, scale = mean_and_scale(patches[...].astype(F32) + lead_row)
        normed = (centered * scale * rows[0:1] + rows[1:2]).astype(BF16)
        out[...] = normed
        turned[...] = normed.T
        wait_blocks(0, *loads)

    @pl.when(step == 3)
    def _():
        wait_blocks(1, *loads)

    qkv[...] = times(out[...], weight[step // 3, :, tile_columns(step % 3, 384)]).astype(BF16)


def front_forward(where, lead_index, patches, arrays):
    return call(
        front_kernel,
        6,
        (where, lead_index, patches, *arrays),
        [pl.BlockSpec(memory_space=pltpu.SMEM), whole((TOKENS, WIDTH))] + [ANY] * 4,
        [
            ((TOKENS, WIDTH), BF16, whole((TOKENS, WIDTH))),
            ((WIDTH, TOKENS), BF16, whole((WIDTH, TOKENS))),
            ((TOKENS, 3 * WIDTH), BF16, side_tile(TOKENS, 384, 3)),
            ((32, WIDTH), F32, whole((32, WIDTH))),
        ],
        weight_scratch(WIDTH, 1152)
        + [pltpu.VMEM((1, WIDTH, 128), BF16), pltpu.SemaphoreType.DMA((1, 16))],
        2 * TOKENS * WIDTH * 3 * WIDTH,
    )


KEY_SPANS = ((0, 256), (0, 384), (128, 512), (256, 512))


def fill_bias(lengths, pad, bias):
    ends, end = [], 0
    for index in range(lengths.shape[1]):
        end = end + lengths[0, index]
        ends.append(end)

    def windows(places):
        return sum([(places >= end).astype(jnp.int32) for end in ends])

    for block, (low, high) in enumerate(KEY_SPANS):
        count = high - low
        queries = lax.broadcasted_iota(jnp.int32, (128, 1), 0) + 128 * block
        keys = lax.broadcasted_iota(jnp.int32, (1, count), 1) + low
        same = windows(queries) == windows(keys)
        usable = (pad[:, low:high] > 0) | (queries == keys)
        bias[block, :, :count] = jnp.where(same & usable, 0.0, -1e30)


def two_heads(block):
    first = lax.broadcasted_iota(jnp.int32, block.shape, 1) < block.shape[1] // 2
    zero = jnp.zeros_like(block)
    return jnp.concatenate([jnp.where(first, block, zero), jnp.where(first, zero, block)], axis=0)


def one_block(stacked):
    half = stacked.shape[0] // 2
    shape = (half, stacked.shape[1])
    first = lax.broadcasted_iota(jnp.int32, shape, 1) < shape[1] // 2
    return jnp.where(first, stacked[:half], stacked[half:])


def probabilities(queries, keys, bias, block, count):
    allowed = bias[block, :, :count]
    scores = across(queries, keys) * score_scale + jnp.concatenate([allowed, allowed], axis=0)
    raised = jnp.exp(scores - jnp.max(scores, axis=1, keepdims=True))
    return raised * (1.0 / jnp.sum(raised, axis=1, keepdims=True))


def attention_kernel(
    where, lengths, pad, patches, small, qkv, w0, w1, w2, w3,
    attended, attended_turned, mid, mlp_input, mlp_turned, weight, sems, bias,
):
    loads = (where, (w0, w1, w2, w3), OUT_PART, weight, sems)
    start_blocks(*loads)
    fill_bias(lengths, pad, bias)

    def pair(index, carry):
        columns = tile_columns(index, 128)
        keys_at, values_at = tile_columns(index + 6, 128), tile_columns(index + 12, 128)
        for block, (low, high) in enumerate(KEY_SPANS):
            rows = slice(128 * block, 128 * block + 128)
            queries = two_heads(qkv[rows, columns])
            probs = probabilities(queries, qkv[low:high, keys_at], bias, block, high - low)
            mixed = times(probs.astype(BF16), qkv[low:high, values_at])
            attended[rows, columns] = one_block(mixed).astype(BF16)
        return carry

    lax.fori_loop(0, 6, pair, 0)
    attended_turned[...] = attended[...].T
    for side in range(2):
        wait_blocks(side, *loads)
        columns = lane_columns(where, side, 384)
        mid[:, columns] = (
            patches[:, columns].astype(F32)
            + small[16:17, columns]
            + times(attended[...], weight[side])
            + small[2:3, columns]
        )
    centered, scale = mean_and_scale(mid[...])
    normed = (centered * scale * small[3:4, :] + small[4:5, :]).astype(BF16)
    mlp_input[...] = normed
    mlp_turned[...] = normed.T


def attention_forward(where, lengths, pad, patches, small, qkv, arrays):
    rows, columns = (TOKENS, WIDTH), (WIDTH, TOKENS)
    return call(
        attention_kernel,
        1,
        (where, lengths, pad, patches, small, qkv, *arrays),
        [
            pl.BlockSpec(memory_space=pltpu.SMEM),
            whole((1, TOKENS)),
            whole(rows),
            whole((32, WIDTH)),
            whole((TOKENS, 3 * WIDTH)),
        ]
        + [ANY] * 4,
        [
            (rows, BF16, whole(rows)),
            (columns, BF16, whole(columns)),
            (rows, F32, whole(rows)),
            (rows, BF16, whole(rows)),
            (columns, BF16, whole(columns)),
        ],
        weight_scratch(WIDTH, 384) + [pltpu.VMEM((4, 128, 384), F32)],
        2 * TOKENS * WIDTH * (WIDTH + 4 * TOKENS),
    )


def up_kernel(where, rows, bias, w0, w1, w2, w3, act, act_turned, slope, weight, sems):
    step = pl.program_id(0)
    loads = (where, (w0, w1, w2, w3), (0, 1536), weight, sems)

    @pl.when(step == 0)
    def _():
        start_blocks(*loads)
        wait_blocks(0, *loads)

    @pl.when(step == 3)
    def _():
        wait_blocks(1, *loads)

    values = times(rows[...], weight[step // 3, :, tile_columns(step % 3, 512)]) + bias[...]
    share = 0.5 * (1.0 + lax.erf(values * 0.7071067811865476))
    density = jnp.exp(-0.5 * values * values) * 0.3989422804014327
    activated = (values * share).astype(BF16)
    act[...] = activated
    act_turned[...] = activated.T
    slope[...] = (share + values * density).astype(BF16)


def up_forward(where, rows, bias, arrays):
    hidden = 4 * WIDTH

    def turned(step, where):
        return (where[0] ^ (step // 3)) * 3 + step % 3, 0

    return call(
        up_kernel,
        6,
        (where, rows, bias, *arrays),
        [whole((TOKENS, WIDTH)), side_tile(1, 512, 3)] + [ANY] * 4,
        [
            ((TOKENS, hidden), BF16, side_tile(TOKENS, 512, 3)),
            ((hidden, TOKENS), BF16, pl.BlockSpec((512, TOKENS), turned)),
            ((TOKENS, hidden), BF16, side_tile(TOKENS, 512, 3)),
        ],
        weight_scratch(WIDTH, 1536),
        2 * TOKENS * WIDTH * hidden,
    )


def down_kernel(
    where, act, mid, small, cotangent, bias, w0, w1, w2, w3, g0, g1, g2, g3,
    outputs, turned, shares, gate_grad, gate_bias, weight, sems, gate, gate_sems, logits,
):
    loads = (where, (w0, w1, w2, w3), (0, 384), weight, sems)
    gate_loads = (where, (g0, g1, g2, g3), GATE_PART, gate, gate_sems)
    start_blocks(*loads)
    start_blocks(*gate_loads)
    for side in range(2):
        wait_blocks(side, *loads)
        columns = lane_columns(where, side, 384)
        outputs[:, columns] = (
            mid[:, columns] + times(act[...], weight[side]) + small[5:6, columns]
        ).astype(BF16)
    turned[...] = outputs[...].T
    for side in range(2):
        wait_blocks(side, *gate_loads)
        logits[:, lane_columns(where, side, 256)] = times(outputs[...], gate[side])
    logits[...] = logits[...] + bias[...]
    shares[:, 256:] = logits[:, 256:]
    gate_grad[:, 256:] = cotangent[:, 256:]
    first, rest = logits[:, :128], logits[:, 128:256]
    left = lax.broadcasted_iota(jnp.int32, first.shape, 1) < PIX
    third = jnp.where(left, rest, pltpu.roll(rest, PIX, 1))
    largest = jnp.maximum(jnp.maximum(first, pltpu.roll(first, PIX, 1)), third)
    raised, raised_third = jnp.exp(first - largest), jnp.exp(third - largest)
    scale = 1.0 / (raised + pltpu.roll(raised, PIX, 1) + raised_third)
    share, share_third = raised * scale, raised_third * scale
    shares[:, :128] = share
    shares[:, 128:256] = jnp.where(left, share_third, rest)
    pull, other = cotangent[:, :128].astype(F32), cotangent[:, 128:256].astype(F32)
    pull_third = jnp.where(left, other, pltpu.roll(other, PIX, 1))
    weighed = share * pull
    inner = weighed + pltpu.roll(weighed, PIX, 1) + share_third * pull_third
    gate_grad[:, :128] = (share * (pull - inner)).astype(BF16)
    gate_grad[:, 128:256] = jnp.where(left, share_third * (pull_third - inner), other).astype(BF16)
    gate_bias[...] = jnp.sum(gate_grad[...].astype(F32), axis=0, keepdims=True)


def down_forward(where, act, mid, small, cotangent, bias, arrays, gate_arrays):
    rows, hidden = (TOKENS, WIDTH), 4 * WIDTH
    return call(
        down_kernel,
        1,
        (where, act, mid, small, cotangent, bias, *arrays, *gate_arrays),
        [
            whole((TOKENS, hidden)),
            whole(rows),
            whole((32, WIDTH)),
            whole((TOKENS, GATE)),
            whole((1, GATE)),
        ]
        + [ANY] * 8,
        [
            (rows, BF16, whole(rows)),
            ((WIDTH, TOKENS), BF16, whole((WIDTH, TOKENS))),
            ((TOKENS, GATE), F32, whole((TOKENS, GATE))),
            ((TOKENS, GATE), BF16, whole((TOKENS, GATE))),
            ((1, GATE), F32, whole((1, GATE))),
        ],
        weight_scratch(hidden, 384)
        + weight_scratch(WIDTH, 256)
        + [pltpu.VMEM((TOKENS, GATE), F32)],
        2 * TOKENS * WIDTH * (hidden + GATE),
    )


def head_kernel(where, rows, gate_out, bias, w0, w1, w2, w3, out, weight, sems):
    step = pl.program_id(0)
    loads = (where, (w0, w1, w2, w3), (0, 2048), weight, sems)

    @pl.when(step == 0)
    def _():
        start_blocks(*loads)
        out[...] = gate_out[...]

    @pl.when(step == 1)
    def _():
        wait_blocks(0, *loads)

    @pl.when(step == 5)
    def _():
        wait_blocks(1, *loads)

    @pl.when(step > 0)
    def _():
        tile = step - 1
        out[...] = times(rows[...], weight[tile // 4, :, tile_columns(tile % 4, 512)]) + bias[...]


def head_forward(where, rows, gate_out, bias, arrays):
    return call(
        head_kernel,
        9,
        (where, rows, gate_out, bias, *arrays),
        [whole((TOKENS, WIDTH)), whole((TOKENS, GATE)), side_tile(1, 512, 4, 1, 1)] + [ANY] * 4,
        [((TOKENS, 6 * WIDTH), F32, side_tile(TOKENS, 512, 4, 1, 1))],
        weight_scratch(WIDTH, 2048),
        2 * TOKENS * WIDTH * 4096,
    )[0]


def head_back_kernel(
    where, act_cotangent, gate_grad, cotangent, g0, g1, g2, g3, w0, w1, w2, w3,
    end_grad, branch, bias_grad, gate, gate_sems, weight, sems,
):
    step = pl.program_id(0)
    gate_loads = (where, (g0, g1, g2, g3), GATE_PART, gate, gate_sems)
    loads = (where, (w0, w1, w2, w3), (0, 2048), weight, sems)

    @pl.when(step == 0)
    def _():
        start_blocks(*gate_loads)
        start_blocks(*loads)
        end_grad[...] = act_cotangent[...].astype(F32)
        for side in range(2):
            wait_blocks(side, *gate_loads)
            end_grad[...] += across(gate_grad[:, lane_columns(where, side, 256)], gate[side])

    @pl.when(step == 1)
    def _():
        wait_blocks(0, *loads)

    @pl.when(step == 5)
    def _():
        wait_blocks(1, *loads)

    @pl.when(step > 0)
    def _():
        tile = step - 1
        end_grad[...] += across(cotangent[...], weight[tile // 4, :, tile_columns(tile % 4, 512)])

    @pl.when(step == 8)
    def _():
        rounded = end_grad[...].astype(BF16)
        branch[...] = rounded
        bias_grad[...] = jnp.sum(rounded.astype(F32), axis=0, keepdims=True)


def head_backward(where, act_cotangent, gate_grad, cotangent, gate_arrays, arrays):
    rows = (TOKENS, WIDTH)
    return call(
        head_back_kernel,
        9,
        (where, act_cotangent, gate_grad, cotangent, *gate_arrays, *arrays),
        [whole(rows), whole((TOKENS, GATE)), side_tile(TOKENS, 512, 4, 1, 1)] + [ANY] * 8,
        [(rows, F32, whole(rows)), (rows, BF16, whole(rows)), ((1, WIDTH), F32, whole((1, WIDTH)))],
        weight_scratch(WIDTH, 256) + weight_scratch(WIDTH, 2048),
        2 * TOKENS * WIDTH * 6 * WIDTH,
    )


def down_back_kernel(
    where, branch, slope, w0, w1, w2, w3, pre_grad, bias_grad, weight, sems
):
    step = pl.program_id(0)
    loads = (where, (w0, w1, w2, w3), (0, 384), weight, sems)

    @pl.when(step == 0)
    def _():
        start_blocks(*loads)
        for side in range(2):
            wait_blocks(side, *loads)

    rows = pl.ds(pl.multiple_of(step * 512, 512), 512)
    grad = across(branch[:, lane_columns(where, 0, 384)], weight[0, rows, :])
    grad += across(branch[:, lane_columns(where, 1, 384)], weight[1, rows, :])
    rounded = (slope[...].astype(F32) * grad).astype(BF16)
    pre_grad[...] = rounded
    bias_grad[...] = jnp.sum(rounded.astype(F32), axis=0, keepdims=True)


def down_backward(where, branch, slope, arrays):
    hidden = 4 * WIDTH
    tile = pl.BlockSpec((TOKENS, 512), lambda step, where: (0, step))
    row = pl.BlockSpec((1, 512), lambda step, where: (0, step))
    return call(
        down_back_kernel,
        6,
        (where, branch, slope, *arrays),
        [whole((TOKENS, WIDTH)), tile] + [ANY] * 4,
        [((TOKENS, hidden), BF16, tile), ((1, hidden), F32, row)],
        weight_scratch(hidden, 384),
        2 * TOKENS * WIDTH * hidden,
    )


def up_back_kernel(
    where, pre_grad, mid, end_grad, small, w0, w1, w2, w3,
    mid_grad, out_grad, terms, weight, sems, total_grad,
):
    step = pl.program_id(0)
    loads = (where, (w0, w1, w2, w3), (0, 1536), weight, sems)

    @pl.when(step == 0)
    def _():
        start_blocks(*loads)
        wait_blocks(0, *loads)
        total_grad[...] = jnp.zeros_like(total_grad)

    @pl.when(step == 3)
    def _():
        wait_blocks(1, *loads)

    total_grad[...] += across(pre_grad[...], weight[step // 3, :, tile_columns(step % 3, 512)])

    @pl.when(step == 5)
    def _():
        pulled, gain_grad, shift_grad = norm_backward(mid[...], small[3:4, :], total_grad[...])
        pulled = pulled + end_grad[...]
        rounded = pulled.astype(BF16)
        mid_grad[...] = pulled
        out_grad[...] = rounded
        terms[...] = jnp.zeros_like(terms)
        terms[0:1, :] = jnp.sum(rounded.astype(F32), axis=0, keepdims=True)
        terms[1:2, :] = gain_grad
        terms[2:3, :] = shift_grad


def up_backward(where, pre_grad, mid, end_grad, small, arrays):
    rows = (TOKENS, WIDTH)
    return call(
        up_back_kernel,
        6,
        (where, pre_grad, mid, end_grad, small, *arrays),
        [side_tile(TOKENS, 512, 3), whole(rows), whole(rows), whole((32, WIDTH))] + [ANY] * 4,
        [(rows, F32, whole(rows)), (rows, BF16, whole(rows)), ((8, WIDTH), F32, whole((8, WIDTH)))],
        weight_scratch(WIDTH, 1536) + [pltpu.VMEM(rows, F32)],
        2 * TOKENS * WIDTH * 4 * WIDTH,
    )


def attention_back_kernel(
    where, lengths, pad, out_grad, qkv, w0, w1, w2, w3,
    qkv_grad, weight, sems, bias, mixed, key_sum, value_sum,
):
    loads = (where, (w0, w1, w2, w3), OUT_PART, weight, sems)
    start_blocks(*loads)
    fill_bias(lengths, pad, bias)
    for side in range(2):
        wait_blocks(side, *loads)
    mixed[...] = (
        across(out_grad[:, lane_columns(where, 0, 384)], weight[0])
        + across(out_grad[:, lane_columns(where, 1, 384)], weight[1])
    ).astype(BF16)

    def pair(index, carry):
        columns = tile_columns(index, 128)
        keys_at, values_at = tile_columns(index + 6, 128), tile_columns(index + 12, 128)
        key_sum[...] = jnp.zeros_like(key_sum)
        value_sum[...] = jnp.zeros_like(value_sum)
        for block, (low, high) in enumerate(KEY_SPANS):
            rows = slice(128 * block, 128 * block + 128)
            queries = two_heads(qkv[rows, columns])
            keys, values = qkv[low:high, keys_at], qkv[low:high, values_at]
            grads = two_heads(mixed[rows, columns])
            probs = probabilities(queries, keys, bias, block, high - low)
            prob_grad = across(grads, values)
            inner = jnp.sum(probs * prob_grad, axis=1, keepdims=True)
            score_grad = (probs * (prob_grad - inner)).astype(BF16)
            query_grad = one_block(times(score_grad, keys)) * score_scale
            qkv_grad[rows, columns] = query_grad.astype(BF16)
            key_sum[low:high, :] += down_rows(score_grad, queries)
            value_sum[low:high, :] += down_rows(probs.astype(BF16), grads)
        qkv_grad[:, keys_at] = (key_sum[...] * score_scale).astype(BF16)
        qkv_grad[:, values_at] = value_sum[...].astype(BF16)
        return carry

    lax.fori_loop(0, 6, pair, 0)


def attention_backward(where, lengths, pad, out_grad, qkv, arrays):
    rows, wide = (TOKENS, WIDTH), (TOKENS, 3 * WIDTH)
    return call(
        attention_back_kernel,
        1,
        (where, lengths, pad, out_grad, qkv, *arrays),
        [pl.BlockSpec(memory_space=pltpu.SMEM), whole((1, TOKENS)), whole(rows), whole(wide)]
        + [ANY] * 4,
        [(wide, BF16, whole(wide))],
        weight_scratch(WIDTH, 384)
        + [
            pltpu.VMEM((4, 128, 384), F32),
            pltpu.VMEM(rows, BF16),
            pltpu.VMEM((TOKENS, 128), F32),
            pltpu.VMEM((TOKENS, 128), F32),
        ],
        2 * TOKENS * WIDTH * (WIDTH + 10 * TOKENS),
    )[0]


def front_back_kernel(
    where, lead, qkv_grad, patches, mid_grad, small, terms, down_row, up_rows, head_rows,
    w0, w1, w2, w3, patch_grad, small_grad, weight, sems, total_grad,
):
    step = pl.program_id(0)
    loads = (where, (w0, w1, w2, w3), QKV_PART, weight, sems)

    @pl.when(step == 0)
    def _():
        start_blocks(*loads)
        wait_blocks(0, *loads)
        total_grad[...] = jnp.zeros_like(total_grad)

    @pl.when(step == 3)
    def _():
        wait_blocks(1, *loads)

    total_grad[...] += across(qkv_grad[...], weight[step // 3, :, tile_columns(step % 3, 384)])

    @pl.when(step == 5)
    def _():
        state = patches[...].astype(F32) + small[16:17, :]
        pulled, gain_grad, shift_grad = norm_backward(state, small[0:1, :], total_grad[...])
        pulled = pulled + mid_grad[...]
        patch_grad[...] = pulled
        lead_grad = jnp.sum(pulled, axis=0, keepdims=True)
        small_grad[0:1, :] = gain_grad
        small_grad[1:2, :] = shift_grad
        small_grad[2:5, :] = terms[0:3, :]
        small_grad[5:6, :] = down_row[...]
        small_grad[6:10, :] = up_rows[...]
        small_grad[10:16, :] = head_rows[...]
        places = lax.broadcasted_iota(jnp.int32, (LEADS, WIDTH), 0)
        small_grad[16:32, :] = jnp.where(places == lead[0], lead_grad, 0.0)


def front_backward(
    where, lead, qkv_grad, patches, mid_grad, small, terms, down_row, up_rows, head_rows, arrays
):
    rows = (TOKENS, WIDTH)
    return call(
        front_back_kernel,
        6,
        (
            where, lead, qkv_grad, patches, mid_grad, small, terms, down_row, up_rows, head_rows,
            *arrays,
        ),
        [
            pl.BlockSpec(memory_space=pltpu.SMEM),
            side_tile(TOKENS, 384, 3),
            whole(rows),
            whole(rows),
            whole((32, WIDTH)),
            whole((8, WIDTH)),
            whole((1, WIDTH)),
            whole((4, WIDTH)),
            whole((6, WIDTH)),
        ]
        + [ANY] * 4,
        [(rows, F32, whole(rows)), ((32, WIDTH), F32, whole((32, WIDTH)))],
        weight_scratch(WIDTH, 1152) + [pltpu.VMEM(rows, F32)],
        2 * TOKENS * WIDTH * 3 * WIDTH,
    )


def store_blocks(where, side, product, got, outs, columns):
    rows = outs[0].shape[1]
    for place in range(16):
        row = pl.multiple_of(where[1 + 16 * side + place] * rows, rows)
        block = product[pl.ds(row, rows), :]
        if side == 0:
            block = block + got[place, :, columns].astype(F32)
        outs[place // 8 if side == 0 else 0][place % 8 if side == 0 else place, :, columns] = (
            block.astype(BF16)
        )


def term_call(kernel, side, grid, where, operands, in_specs, got, rows, width, tile, scratch, flops):
    def blocks(count):
        return pl.BlockSpec((count, rows, tile), lambda step, where: (0, 0, step))

    outs = [(8, rows, width)] * 2 if side == 0 else [(16, rows, width)]
    if side == 0:
        operands, in_specs = (*operands, got), [*in_specs, blocks(16)]
    result = call(
        partial(kernel, side),
        grid,
        (where, *operands),
        in_specs,
        [(shape, BF16, blocks(shape[0])) for shape in outs],
        scratch,
        flops,
    )
    return result if side == 0 else result[0]


def both_sides(make):
    got = exchange(make(1, None), SIBLING)
    return make(0, got)


def head_term_kernel(side, where, turned, gate_grad, cotangent, *refs):
    got, outs, product = refs[0] if side == 0 else None, refs[1 - side : -1], refs[-1]
    logit_grad = jnp.where(pl.program_id(0) == 0, gate_grad[...], cotangent[...])
    product[...] = times(turned[...], logit_grad)
    store_blocks(where, side, product, got, outs, slice(None))


def head_terms(where, turned, gate_grad, cotangent):
    def make(side, got):
        gate_spec = pl.BlockSpec((TOKENS, 256), lambda step, where: (0, where[0] ^ side))
        spec = pl.BlockSpec(
            (TOKENS, 256),
            lambda step, where: (0, 2 + (where[0] ^ side) * 8 + jnp.maximum(step - 1, 0)),
        )
        return term_call(
            head_term_kernel, side, 9, where, (turned, gate_grad, cotangent),
            [whole((WIDTH, TOKENS)), gate_spec, spec], got, 48, 2304, 256,
            [pltpu.VMEM((WIDTH, 256), F32)], TOKENS * WIDTH * 6 * WIDTH,
        )

    return both_sides(make)


def down_term_kernel(side, where, turned, branch, *refs):
    got, outs, product = refs[0] if side == 0 else None, refs[1 - side : -1], refs[-1]
    for part in range(4):
        rows = slice(part * WIDTH, (part + 1) * WIDTH)
        product[rows, :] = times(turned[rows, :], branch[...])
    store_blocks(where, side, product, got, outs, slice(None))


def down_terms(where, turned, branch):
    hidden = 4 * WIDTH

    def make(side, got):
        spec = pl.BlockSpec((TOKENS, 384), lambda step, where: (0, where[0] ^ side))
        return term_call(
            down_term_kernel, side, 1, where, (turned, branch),
            [whole((hidden, TOKENS)), spec], got, 192, 384, 384,
            [pltpu.VMEM((hidden, 384), F32)], TOKENS * WIDTH * hidden,
        )

    return both_sides(make)


def up_term_kernel(side, where, turned, pre_grad, *refs):
    got, outs, product = refs[0] if side == 0 else None, refs[1 - side : -1], refs[-1]
    product[...] = times(turned[...], pre_grad[...])
    store_blocks(where, side, product, got, outs, slice(None))


def up_terms(where, turned, pre_grad):
    def make(side, got):
        spec = pl.BlockSpec((TOKENS, 512), lambda step, where: (0, (where[0] ^ side) * 3 + step))
        return term_call(
            up_term_kernel, side, 3, where, (turned, pre_grad),
            [whole((WIDTH, TOKENS)), spec], got, 48, 1536, 512,
            [pltpu.VMEM((WIDTH, 512), F32)], TOKENS * WIDTH * 4 * WIDTH,
        )

    return both_sides(make)


def front_term_kernel(
    side, where, input_turned, qkv_grad, attended_turned, out_grad, small_grad, *refs
):
    got, outs, product = refs[0] if side == 0 else None, refs[1 - side : -1], refs[-1]
    product[:, 0:1152] = times(input_turned[...], qkv_grad[...])
    product[:, 1152:1536] = times(attended_turned[...], out_grad[...])
    rows = small_grad[pl.ds(pl.multiple_of((where[0] ^ side) * 16, 16), 16), :]
    product[:, 1536:1664] = jnp.concatenate([rows, jnp.zeros((112, WIDTH), F32)], axis=0).T
    store_blocks(where, side, product, got, outs, slice(None))


def front_terms(where, input_turned, qkv_grad, attended_turned, out_grad, small_grad):
    def make(side, got):
        def lane(width):
            return pl.BlockSpec((TOKENS, width), lambda step, where: (0, where[0] ^ side))

        return term_call(
            front_term_kernel, side, 1, where,
            (input_turned, qkv_grad, attended_turned, out_grad, small_grad),
            [
                whole((WIDTH, TOKENS)), lane(1152), whole((WIDTH, TOKENS)), lane(384),
                whole((32, WIDTH)),
            ],
            got, 48, 1664, 1664, [pltpu.VMEM((WIDTH, 1664), F32)], TOKENS * WIDTH * 4 * WIDTH,
        )

    return both_sides(make)


def rows_of(vector, count):
    return vector.reshape(32, count, 24).transpose(1, 0, 2).reshape(count, WIDTH)


def vector_of(rows):
    count = rows.shape[0]
    return rows.reshape(count, 32, 24).transpose(1, 0, 2).reshape(1, count * WIDTH)


def shards(
    patches,
    lead_index,
    window_lengths,
    pad_mask,
    lead_table,
    attn_gain,
    attn_shift,
    qkv_weight,
    out_weight,
    out_bias,
    mlp_gain,
    mlp_shift,
    up_weight,
    up_bias,
    down_weight,
    down_bias,
    head_weight,
    head_bias,
    act_cotangent,
    head_cotangent,
):
    core, where = whereabouts()
    vectors = [attn_gain, attn_shift, out_bias, mlp_gain, mlp_shift, down_bias]
    small = jnp.concatenate(
        [vector[None] for vector in vectors]
        + [up_bias.reshape(4, 24), head_bias.reshape(6, 24), lead_table, jnp.zeros((96, 24), BF16)],
        axis=0,
    ).T
    front = gathered([qkv_weight, out_weight, head_weight[:, :GATE]], [small], core)
    up = gathered([up_weight], [], core)
    down = gathered([down_weight], [], core)
    head = gathered([head_weight[:, GATE:]], [], core)
    pad = pad_mask[None]
    cotangent_sum = jnp.sum(head_cotangent[:, GATE:].astype(F32), axis=0, keepdims=True)

    attn_input, attn_turned, qkv, small_rows = front_forward(where, lead_index, patches, front)
    attended, attended_turned, mid_state, mlp_input, mlp_turned = attention_forward(
        where, window_lengths, pad, patches, small_rows, qkv, front
    )
    act_rows, act_turned, slope = up_forward(where, mlp_input, vector_of(small_rows[6:10]), up)
    head_bias_row = vector_of(small_rows[10:16])
    outputs, outputs_turned, gate_out, gate_grad, gate_bias_sum = down_forward(
        where, act_rows, mid_state, small_rows, head_cotangent, head_bias_row, down, front
    )
    head_keep, head_send = head_terms(where, outputs_turned, gate_grad, head_cotangent)
    end_grad, branch_grad, down_bias_sum = head_backward(
        where, act_cotangent, gate_grad, head_cotangent, front, head
    )
    pre_grad, up_bias_sum = down_backward(where, branch_grad, slope, down)
    down_keep, down_send = down_terms(where, act_turned, branch_grad)
    mid_grad, out_grad, terms = up_backward(where, pre_grad, mid_state, end_grad, small_rows, up)
    up_keep, up_send = up_terms(where, mlp_turned, pre_grad)
    qkv_grad = attention_backward(where, window_lengths, pad, out_grad, qkv, front)
    head_rows = rows_of(jnp.concatenate([gate_bias_sum, cotangent_sum], axis=1), 6)
    patch_grad, small_grad = front_backward(
        where,
        lead_index,
        qkv_grad,
        patches,
        mid_grad,
        small_rows,
        terms,
        down_bias_sum,
        rows_of(up_bias_sum, 4),
        head_rows,
        front,
    )
    front_keep, front_send = front_terms(
        where, attn_turned, qkv_grad, attended_turned, out_grad, small_grad
    )
    head_out = head_forward(where, outputs, gate_out, head_bias_row, head)

    gate_sum, rest_sum = scattered(head_keep, head_send, core, (256, 2048))
    (down_sum,) = scattered(down_keep, down_send, core, (384,))
    (up_sum,) = scattered(up_keep, up_send, core, (1536,))
    qkv_sum, out_sum, small_sum = scattered(front_keep, front_send, core, (1152, 384, 128))
    small_sum = small_sum.T
    return (
        outputs,
        head_out,
        patch_grad,
        small_sum[128:144],
        small_sum[0],
        small_sum[1],
        qkv_sum,
        out_sum,
        small_sum[2],
        small_sum[3],
        small_sum[4],
        up_sum,
        small_sum[6:10].reshape(96),
        down_sum,
        small_sum[5],
        jnp.concatenate([gate_sum, rest_sum], axis=1),
        small_sum[10:16].reshape(144),
    )


def plain_shards(
    patches,
    lead_index,
    window_lengths,
    pad_mask,
    lead_table,
    attn_gain,
    attn_shift,
    qkv_weight,
    out_weight,
    out_bias,
    mlp_gain,
    mlp_shift,
    up_weight,
    up_bias,
    down_weight,
    down_bias,
    head_weight,
    head_bias,
    act_cotangent,
    head_cotangent,
):
    front = (
        lax.all_gather(lead_table, ("dp", "fsdp"), axis=1, tiled=True),
        lax.all_gather(attn_gain, ("dp", "fsdp"), axis=0, tiled=True),
        lax.all_gather(attn_shift, ("dp", "fsdp"), axis=0, tiled=True),
        lax.all_gather(qkv_weight, ("dp", "fsdp"), axis=0, tiled=True),
        lax.all_gather(out_weight, ("dp", "fsdp"), axis=0, tiled=True),
        lax.all_gather(out_bias, ("dp", "fsdp"), axis=0, tiled=True),
    )
    rear = (
        lax.all_gather(mlp_gain, ("dp", "fsdp"), axis=0, tiled=True),
        lax.all_gather(mlp_shift, ("dp", "fsdp"), axis=0, tiled=True),
        lax.all_gather(up_weight, ("dp", "fsdp"), axis=0, tiled=True),
        lax.all_gather(up_bias, ("dp", "fsdp"), axis=0, tiled=True),
        lax.all_gather(down_weight, ("dp", "fsdp"), axis=0, tiled=True),
        lax.all_gather(down_bias, ("dp", "fsdp"), axis=0, tiled=True),
        lax.all_gather(head_weight, ("dp", "fsdp"), axis=0, tiled=True),
        lax.all_gather(head_bias, ("dp", "fsdp"), axis=0, tiled=True),
    )
    table_full, gain_one, shift_one, qkv_full, out_full, out_bias_full = front
    (
        gain_two,
        shift_two,
        up_full,
        up_bias_full,
        down_full,
        down_bias_full,
        head_full,
        head_bias_full,
    ) = rear
    token_rows, width = patches.shape
    head_dim = width // HEADS
    block_rows = min(512, token_rows)
    block_count = token_rows // block_rows
    ends = jnp.cumsum(window_lengths[0])
    positions = jnp.arange(token_rows, dtype=jnp.int32)
    window = jnp.sum((positions[:, None] >= ends[None, :]).astype(jnp.int32), axis=1)
    lead_hot = (jnp.arange(LEADS, dtype=jnp.int32) == lead_index[0]).astype(jnp.float32)
    lead_row = jnp.sum(lead_hot[:, None] * table_full.astype(jnp.float32), axis=0)
    start_state = patches.astype(jnp.float32) + lead_row[None, :]
    normed_one, pull_one = jax.vjp(
        layer_norm, start_state, gain_one.astype(jnp.float32), shift_one.astype(jnp.float32)
    )
    attn_input = normed_one.astype(jnp.bfloat16)
    qkv_rows = jnp.dot(attn_input, qkv_full, preferred_element_type=jnp.float32).astype(
        jnp.bfloat16
    )
    queries = qkv_rows[:, :width].reshape(block_count, block_rows, HEADS, head_dim)
    keys = qkv_rows[:, width : 2 * width].reshape(token_rows, HEADS, head_dim)
    values = qkv_rows[:, 2 * width :].reshape(token_rows, HEADS, head_dim)
    query_windows = window.reshape(block_count, block_rows)
    block_starts = jnp.arange(block_count, dtype=jnp.int32) * block_rows

    def block_scores(query_block, window_block, block_start):
        scores = (
            jnp.einsum("qhd,khd->hqk", query_block, keys, preferred_element_type=jnp.float32)
            * score_scale
        )
        allowed = allowed_keys(window_block, window, pad_mask, block_start)
        return jnp.where(allowed[None], scores, -1e30)

    def forward_block(inputs):
        query_block, window_block, block_start = inputs
        masked = block_scores(query_block, window_block, block_start)
        largest = jnp.max(masked, axis=-1, keepdims=True)
        raised = jnp.exp(masked - largest)
        total = jnp.sum(raised, axis=-1, keepdims=True)
        probs = (raised / total).astype(jnp.bfloat16)
        mixed = jnp.einsum("hqk,khd->qhd", probs, values, preferred_element_type=jnp.float32)
        return (
            mixed.reshape(block_rows, width).astype(jnp.bfloat16),
            (largest + jnp.log(total))[:, :, 0],
        )

    mixed_blocks, log_totals = lax.map(forward_block, (queries, query_windows, block_starts))
    attended = mixed_blocks.reshape(token_rows, width)
    mid_state = (
        start_state
        + jnp.dot(attended, out_full, preferred_element_type=jnp.float32)
        + out_bias_full.astype(jnp.float32)
    )
    normed_two, pull_two = jax.vjp(
        layer_norm, mid_state, gain_two.astype(jnp.float32), shift_two.astype(jnp.float32)
    )
    mlp_input = normed_two.astype(jnp.bfloat16)
    pre_act = jnp.dot(mlp_input, up_full, preferred_element_type=jnp.float32) + up_bias_full.astype(
        jnp.float32
    )
    activated, pull_act = jax.vjp(gelu_exact, pre_act)
    act_rows = activated.astype(jnp.bfloat16)
    end_state = (
        mid_state
        + jnp.dot(act_rows, down_full, preferred_element_type=jnp.float32)
        + down_bias_full.astype(jnp.float32)
    )
    outputs = end_state.astype(jnp.bfloat16)
    logits = jnp.dot(
        outputs, head_full, preferred_element_type=jnp.float32
    ) + head_bias_full.astype(jnp.float32)
    head_out, pull_head = jax.vjp(partial(expert_softmax, experts=EXPERTS, pixels=PIX), logits)
    up_back, down_back, head_back = (
        lax.all_gather(up_weight, ("dp", "fsdp"), axis=0, tiled=True),
        lax.all_gather(down_weight, ("dp", "fsdp"), axis=0, tiled=True),
        lax.all_gather(head_weight, ("dp", "fsdp"), axis=0, tiled=True),
    )
    qkv_back, out_back = (
        lax.all_gather(qkv_weight, ("dp", "fsdp"), axis=0, tiled=True),
        lax.all_gather(out_weight, ("dp", "fsdp"), axis=0, tiled=True),
    )
    logit_grad = pull_head(head_cotangent.astype(jnp.float32))[0].astype(jnp.bfloat16)
    head_bias_term = jnp.sum(logit_grad.astype(jnp.float32), axis=0)
    head_term = jnp.einsum("td,tn->dn", outputs, logit_grad, preferred_element_type=jnp.float32)
    end_grad = act_cotangent.astype(jnp.float32) + jnp.einsum(
        "tn,dn->td", logit_grad, head_back, preferred_element_type=jnp.float32
    )
    branch_grad = end_grad.astype(jnp.bfloat16)
    down_bias_term = jnp.sum(branch_grad.astype(jnp.float32), axis=0)
    down_term = jnp.einsum("tf,td->fd", act_rows, branch_grad, preferred_element_type=jnp.float32)
    act_grad = jnp.einsum("td,fd->tf", branch_grad, down_back, preferred_element_type=jnp.float32)
    pre_grad = pull_act(act_grad)[0].astype(jnp.bfloat16)
    up_bias_term = jnp.sum(pre_grad.astype(jnp.float32), axis=0)
    up_term = jnp.einsum("td,tf->df", mlp_input, pre_grad, preferred_element_type=jnp.float32)
    normed_two_grad = jnp.einsum("tf,df->td", pre_grad, up_back, preferred_element_type=jnp.float32)
    state_grad_two, gain_two_term, shift_two_term = pull_two(normed_two_grad)
    (
        gain_part,
        shift_part,
        up_part,
        up_bias_part,
        down_part,
        down_bias_part,
        head_part,
        head_bias_part,
    ) = (
        lax.psum_scatter(
            gain_two_term.astype(jnp.bfloat16), "dp", scatter_dimension=0, tiled=True
        ).astype(jnp.float32),
        lax.psum_scatter(
            shift_two_term.astype(jnp.bfloat16), "dp", scatter_dimension=0, tiled=True
        ).astype(jnp.float32),
        lax.psum_scatter(
            up_term.astype(jnp.bfloat16), "dp", scatter_dimension=0, tiled=True
        ).astype(jnp.float32),
        lax.psum_scatter(
            up_bias_term.astype(jnp.bfloat16), "dp", scatter_dimension=0, tiled=True
        ).astype(jnp.float32),
        lax.psum_scatter(
            down_term.astype(jnp.bfloat16), "dp", scatter_dimension=0, tiled=True
        ).astype(jnp.float32),
        lax.psum_scatter(
            down_bias_term.astype(jnp.bfloat16), "dp", scatter_dimension=0, tiled=True
        ).astype(jnp.float32),
        lax.psum_scatter(
            head_term.astype(jnp.bfloat16), "dp", scatter_dimension=0, tiled=True
        ).astype(jnp.float32),
        lax.psum_scatter(
            head_bias_term.astype(jnp.bfloat16), "dp", scatter_dimension=0, tiled=True
        ).astype(jnp.float32),
    )
    rear_grads = (
        lax.psum_scatter(gain_part, "fsdp", scatter_dimension=0, tiled=True),
        lax.psum_scatter(shift_part, "fsdp", scatter_dimension=0, tiled=True),
        lax.psum_scatter(up_part, "fsdp", scatter_dimension=0, tiled=True),
        lax.psum_scatter(up_bias_part, "fsdp", scatter_dimension=0, tiled=True),
        lax.psum_scatter(down_part, "fsdp", scatter_dimension=0, tiled=True),
        lax.psum_scatter(down_bias_part, "fsdp", scatter_dimension=0, tiled=True),
        lax.psum_scatter(head_part, "fsdp", scatter_dimension=0, tiled=True),
        lax.psum_scatter(head_bias_part, "fsdp", scatter_dimension=0, tiled=True),
    )
    mid_grad = end_grad + state_grad_two
    out_grad = mid_grad.astype(jnp.bfloat16)
    out_bias_term = jnp.sum(out_grad.astype(jnp.float32), axis=0)
    out_term = jnp.einsum("td,te->de", attended, out_grad, preferred_element_type=jnp.float32)
    mixed_grad = jnp.einsum(
        "te,de->td", out_grad, out_back, preferred_element_type=jnp.float32
    ).astype(jnp.bfloat16)
    grad_blocks = mixed_grad.reshape(block_count, block_rows, HEADS, head_dim)

    def backward_block(carry, inputs):
        key_sum, value_sum = carry
        query_block, grad_block, window_block, total_block, block_start = inputs
        masked = block_scores(query_block, window_block, block_start)
        probs = jnp.exp(masked - total_block[:, :, None])
        prob_grad = jnp.einsum(
            "qhd,khd->hqk", grad_block, values, preferred_element_type=jnp.float32
        )
        inner = jnp.sum(probs * prob_grad, axis=-1, keepdims=True)
        score_grad = (probs * (prob_grad - inner)).astype(jnp.bfloat16)
        query_grad = (
            jnp.einsum("hqk,khd->qhd", score_grad, keys, preferred_element_type=jnp.float32)
            * score_scale
        )
        key_sum = (
            key_sum
            + jnp.einsum(
                "hqk,qhd->khd", score_grad, query_block, preferred_element_type=jnp.float32
            )
            * score_scale
        )
        value_sum = value_sum + jnp.einsum(
            "hqk,qhd->khd",
            probs.astype(jnp.bfloat16),
            grad_block,
            preferred_element_type=jnp.float32,
        )
        return ((key_sum, value_sum), query_grad.reshape(block_rows, width))

    zero_keys = jnp.zeros((token_rows, HEADS, head_dim), jnp.float32)
    (key_grad, value_grad), query_grads = lax.scan(
        backward_block,
        (zero_keys, zero_keys),
        (queries, grad_blocks, query_windows, log_totals, block_starts),
    )
    qkv_grad = jnp.concatenate(
        [
            query_grads.reshape(token_rows, width),
            key_grad.reshape(token_rows, width),
            value_grad.reshape(token_rows, width),
        ],
        axis=1,
    ).astype(jnp.bfloat16)
    qkv_term = jnp.einsum("td,te->de", attn_input, qkv_grad, preferred_element_type=jnp.float32)
    normed_one_grad = jnp.einsum(
        "te,de->td", qkv_grad, qkv_back, preferred_element_type=jnp.float32
    )
    state_grad_one, gain_one_term, shift_one_term = pull_one(normed_one_grad)
    patch_grad = mid_grad + state_grad_one
    lead_term = lead_hot[:, None] * jnp.sum(patch_grad, axis=0)[None, :]
    lead_part, gain_one_part, shift_one_part, qkv_part, out_part, out_bias_part = (
        lax.psum_scatter(
            lead_term.astype(jnp.bfloat16), "dp", scatter_dimension=1, tiled=True
        ).astype(jnp.float32),
        lax.psum_scatter(
            gain_one_term.astype(jnp.bfloat16), "dp", scatter_dimension=0, tiled=True
        ).astype(jnp.float32),
        lax.psum_scatter(
            shift_one_term.astype(jnp.bfloat16), "dp", scatter_dimension=0, tiled=True
        ).astype(jnp.float32),
        lax.psum_scatter(
            qkv_term.astype(jnp.bfloat16), "dp", scatter_dimension=0, tiled=True
        ).astype(jnp.float32),
        lax.psum_scatter(
            out_term.astype(jnp.bfloat16), "dp", scatter_dimension=0, tiled=True
        ).astype(jnp.float32),
        lax.psum_scatter(
            out_bias_term.astype(jnp.bfloat16), "dp", scatter_dimension=0, tiled=True
        ).astype(jnp.float32),
    )
    front_grads = (
        lax.psum_scatter(lead_part, "fsdp", scatter_dimension=1, tiled=True),
        lax.psum_scatter(gain_one_part, "fsdp", scatter_dimension=0, tiled=True),
        lax.psum_scatter(shift_one_part, "fsdp", scatter_dimension=0, tiled=True),
        lax.psum_scatter(qkv_part, "fsdp", scatter_dimension=0, tiled=True),
        lax.psum_scatter(out_part, "fsdp", scatter_dimension=0, tiled=True),
        lax.psum_scatter(out_bias_part, "fsdp", scatter_dimension=0, tiled=True),
    )
    return (
        outputs,
        head_out,
        patch_grad,
        front_grads[0],
        front_grads[1],
        front_grads[2],
        front_grads[3],
        front_grads[4],
        front_grads[5],
        rear_grads[0],
        rear_grads[1],
        rear_grads[2],
        rear_grads[3],
        rear_grads[4],
        rear_grads[5],
        rear_grads[6],
        rear_grads[7],
    )


def solution(mesh):
    in_specs = (
        P(("dp", "fsdp"), None),
        P(("dp", "fsdp")),
        P(("dp", "fsdp"), None),
        P(("dp", "fsdp")),
        P(None, ("dp", "fsdp")),
        P(("dp", "fsdp")),
        P(("dp", "fsdp")),
        P(("dp", "fsdp"), None),
        P(("dp", "fsdp"), None),
        P(("dp", "fsdp")),
        P(("dp", "fsdp")),
        P(("dp", "fsdp")),
        P(("dp", "fsdp"), None),
        P(("dp", "fsdp")),
        P(("dp", "fsdp"), None),
        P(("dp", "fsdp")),
        P(("dp", "fsdp"), None),
        P(("dp", "fsdp")),
        P(("dp", "fsdp"), None),
        P(("dp", "fsdp"), None),
    )
    out_specs = (
        P(("dp", "fsdp"), None),
        P(("dp", "fsdp"), None),
        P(("dp", "fsdp"), None),
        P(None, ("dp", "fsdp")),
        P(("dp", "fsdp")),
        P(("dp", "fsdp")),
        P(("dp", "fsdp"), None),
        P(("dp", "fsdp"), None),
        P(("dp", "fsdp")),
        P(("dp", "fsdp")),
        P(("dp", "fsdp")),
        P(("dp", "fsdp"), None),
        P(("dp", "fsdp")),
        P(("dp", "fsdp"), None),
        P(("dp", "fsdp")),
        P(("dp", "fsdp"), None),
        P(("dp", "fsdp")),
    )
    body = shards if dict(mesh.shape) == {"dp": 4, "fsdp": 8} else plain_shards
    return jax.shard_map(body, mesh=mesh, in_specs=in_specs, out_specs=out_specs, check_vma=False)
```

```python
import math
from functools import partial

import jax
import jax.numpy as jnp
from jax import lax
from jax.experimental import pallas as pl
from jax.experimental.pallas import tpu as pltpu
from jax.sharding import PartitionSpec as P

HEADS = 12
PIX = 64
EXPERTS = 3
LEADS = 16


norm_epsilon = 1e-05
score_scale = 0.125


def layer_norm(hidden, norm_gain, norm_shift):
    average = jnp.mean(hidden, axis=-1, keepdims=True)
    centered = hidden - average
    variance = jnp.mean(centered * centered, axis=-1, keepdims=True)
    return centered * lax.rsqrt(variance + norm_epsilon) * norm_gain + norm_shift


def gelu_exact(values):
    return 0.5 * values * (1.0 + lax.erf(values * 0.7071067811865476))


def expert_softmax(logits, experts, pixels):
    gate_part = logits[:, : experts * pixels].reshape(logits.shape[0], experts, pixels)
    largest = jnp.max(gate_part, axis=1, keepdims=True)
    raised = jnp.exp(gate_part - largest)
    shares = raised / jnp.sum(raised, axis=1, keepdims=True)
    return jnp.concatenate(
        [shares.reshape(logits.shape[0], experts * pixels), logits[:, experts * pixels :]], axis=1
    )


def allowed_keys(query_window, key_window, key_valid, query_start):
    query_place = query_start + jnp.arange(query_window.shape[0], dtype=jnp.int32)
    key_place = jnp.arange(key_window.shape[0], dtype=jnp.int32)
    same_window = query_window[:, None] == key_window[None, :]
    usable = (key_valid[None, :] > 0) | (query_place[:, None] == key_place[None, :])
    return same_window & usable


AXES = ("dp", "fsdp")
STEPS = ((4, 4), (8, 16), (2, 2), (16, 8))
SIBLING = (1, 1)
WIDTH = 768
TOKENS = 512
GATE = 512
F32 = jnp.float32
BF16 = jnp.bfloat16
VMEM = pl.BlockSpec(memory_space=pltpu.VMEM)
ANY = pl.BlockSpec(memory_space=pl.ANY)
QKV_PART, SMALL_PART = (0, 1152), (1152, 128)
UP_PART, OUT_PART, GATE_PART = (0, 1536), (1536, 384), (1920, 256)


def chip_masks(lane):
    masks = []
    for place in range(16):
        mask = 0
        for step in range(4):
            if place >> step & 1:
                mask ^= STEPS[step][lane]
        masks.append(mask >> 1)
    return masks


def exchange(array, masks):
    return lax.ppermute(array, AXES, [(d, d ^ masks[d & 1]) for d in range(32)])


def whereabouts():
    device = lax.axis_index("dp") * 8 + lax.axis_index("fsdp")
    core, chip = device % 2, device // 2
    tables = jnp.array([chip_masks(0), chip_masks(1)], jnp.int32) ^ chip
    mine = jnp.where(core == 0, tables[0], tables[1])
    theirs = jnp.where(core == 0, tables[1], tables[0])
    return core, jnp.concatenate([core[None].astype(jnp.int32), mine, theirs])


def halves(array, core):
    half = array.shape[1] // 2
    left, right = array[:, :half], array[:, half:]
    return jnp.where(core == 0, left, right), jnp.where(core == 0, right, left)


def in_core_order(core, mine, theirs, axis):
    return jnp.where(
        core == 0,
        jnp.concatenate([mine, theirs], axis=axis),
        jnp.concatenate([theirs, mine], axis=axis),
    )


def after(value, *marks):
    return lax.optimization_barrier((value, marks))[0]


def lane_chunk(parts, small, core):
    pairs = [halves(part, core) for part in parts]
    mine = jnp.concatenate([pair[0] for pair in pairs] + small, axis=1)
    theirs = jnp.concatenate([pair[1] for pair in pairs] + small, axis=1)
    return in_core_order(core, mine, exchange(theirs, SIBLING), 0)[None]


def first_pair(chunk):
    return jnp.concatenate([chunk, exchange(chunk, STEPS[0])], axis=0)


def first_four(pair):
    other = exchange(pair, STEPS[1])
    return jnp.concatenate([pair, other], axis=0), other


def second_four(pair, other):
    return jnp.concatenate([exchange(pair, STEPS[2]), exchange(other, STEPS[2])], axis=0)


def both_lanes(quarters):
    return tuple(quarters) + tuple(exchange(quarter, SIBLING) for quarter in quarters)


def total(first, second):
    return first.astype(F32) + second.astype(F32)


def folded(keep, got):
    half = keep.shape[0] // 2
    send = total(keep[half:], got[half:]).astype(BF16)
    return total(keep[:half], got[:half]).astype(BF16), send


def finished(keep, got, core, widths):
    block = total(keep, got)[0]
    rows = block.shape[0] // 2
    upper, lower = block[:rows], block[rows:]
    mine = jnp.where(core == 0, upper, lower)
    theirs = jnp.where(core == 0, lower, upper).astype(BF16)
    other = exchange(theirs, SIBLING).astype(F32)
    pieces, start = [], 0
    for width in widths:
        span = slice(start, start + width)
        pieces.append(in_core_order(core, mine[:, span], other[:, span], 1))
        start += width
    return pieces


def across(first, second):
    return lax.dot_general(first, second, (((1,), (1,)), ((), ())), preferred_element_type=F32)


def down_rows(first, second):
    return lax.dot_general(first, second, (((0,), (0,)), ((), ())), preferred_element_type=F32)


def times(first, second):
    return jnp.dot(first, second, preferred_element_type=F32)


def block_copies(where, sources, part, target, sems, side):
    start, width = part
    rows = sources[0].shape[1]
    copies = []
    for place in range(16):
        row = pl.multiple_of(where[1 + 16 * side + place] * rows, rows)
        copies.append(
            pltpu.make_async_copy(
                sources[4 * side + place // 4].at[place % 4, :, pl.ds(start, width)],
                target.at[side, pl.ds(row, rows), :],
                sems.at[side, place],
            )
        )
    return copies


def start_blocks(*args):
    for side in range(2):
        for copy in block_copies(*args, side):
            copy.start()


def wait_blocks(side, *args):
    for copy in block_copies(*args, side):
        copy.wait()


def lane_columns(where, side, width):
    return pl.ds(pl.multiple_of((where[0] ^ side) * width, 128), width)


def tile_columns(tile, width):
    return pl.ds(pl.multiple_of(tile * width, 128), width)


def mean_and_scale(hidden):
    average = jnp.mean(hidden, axis=1, keepdims=True)
    centered = hidden - average
    variance = jnp.mean(centered * centered, axis=1, keepdims=True)
    return centered, lax.rsqrt(variance + norm_epsilon)


def norm_backward(hidden, gain, upstream):
    centered, scale = mean_and_scale(hidden)
    normed = centered * scale
    gain_grad = jnp.sum(upstream * normed, axis=0, keepdims=True)
    shift_grad = jnp.sum(upstream, axis=0, keepdims=True)
    scaled = upstream * gain
    first = jnp.mean(scaled, axis=1, keepdims=True)
    second = jnp.mean(scaled * normed, axis=1, keepdims=True)
    return scale * (scaled - first - normed * second), gain_grad, shift_grad


def call(kernel, grid, operands, in_specs, outs, scratch, flops):
    shapes = [jax.ShapeDtypeStruct(shape, kind) for shape, kind, _ in outs]
    size = sum(math.prod(shape.shape) * shape.dtype.itemsize for shape in shapes)
    size += sum(math.prod(item.shape) * item.dtype.itemsize for item in operands)
    return pl.pallas_call(
        kernel,
        out_shape=shapes,
        grid_spec=pltpu.PrefetchScalarGridSpec(
            num_scalar_prefetch=1,
            grid=(grid,),
            in_specs=in_specs,
            out_specs=[spec for _, _, spec in outs],
            scratch_shapes=scratch,
        ),
        compiler_params=pltpu.CompilerParams(vmem_limit_bytes=48 * 1024 * 1024),
        cost_estimate=pl.CostEstimate(flops=flops // 1000, bytes_accessed=size // 1000, transcendentals=0),
    )(*operands)


def whole(shape):
    return pl.BlockSpec(shape, lambda step, where: (0,) * len(shape))


def side_tile(rows, width, tiles, first=0, lead=0):
    def place(step, where):
        after = jnp.maximum(step - lead, 0)
        side = after // tiles
        column = first + (where[0] ^ side) * tiles + after % tiles
        return 0, jnp.where(step < lead, 0, column)

    return pl.BlockSpec((rows, width), place)


def weight_scratch(rows, width):
    return [pltpu.VMEM((2, rows, width), BF16), pltpu.SemaphoreType.DMA((2, 16))]


def front_kernel(
    where, lead, patches, *refs
):
    sources, (out, turned, qkv, small, weight, sems, smalls, small_sems) = refs[:8], refs[8:]
    step = pl.program_id(0)
    loads = (where, sources, QKV_PART, weight, sems)
    small_loads = (where, sources, SMALL_PART, smalls, small_sems)

    @pl.when(step == 0)
    def _():
        for copy in block_copies(*small_loads, 0):
            copy.start()
        start_blocks(*loads)
        wait_blocks(0, *small_loads)
        rows = smalls[0].astype(F32).T
        places = lax.broadcasted_iota(jnp.int32, (LEADS, WIDTH), 0)
        lead_row = jnp.sum(
            jnp.where(places == lead[0], rows[16 : 16 + LEADS], 0.0), axis=0, keepdims=True
        )
        small[...] = rows[:32]
        small[16:17, :] = lead_row
        centered, scale = mean_and_scale(patches[...].astype(F32) + lead_row)
        normed = (centered * scale * rows[0:1] + rows[1:2]).astype(BF16)
        out[...] = normed
        turned[...] = normed.T
        wait_blocks(0, *loads)

    @pl.when(step == 3)
    def _():
        wait_blocks(1, *loads)

    qkv[...] = times(out[...], weight[step // 3, :, tile_columns(step % 3, 384)]).astype(BF16)


def front_forward(where, lead_index, patches, arrays):
    return call(
        front_kernel,
        6,
        (where, lead_index, patches, *arrays),
        [pl.BlockSpec(memory_space=pltpu.SMEM), whole((TOKENS, WIDTH))] + [ANY] * 8,
        [
            ((TOKENS, WIDTH), BF16, whole((TOKENS, WIDTH))),
            ((WIDTH, TOKENS), BF16, whole((WIDTH, TOKENS))),
            ((TOKENS, 3 * WIDTH), BF16, side_tile(TOKENS, 384, 3)),
            ((32, WIDTH), F32, whole((32, WIDTH))),
        ],
        weight_scratch(WIDTH, 1152)
        + [pltpu.VMEM((1, WIDTH, 128), BF16), pltpu.SemaphoreType.DMA((1, 16))],
        2 * TOKENS * WIDTH * 3 * WIDTH,
    )


KEY_SPANS = ((0, 256), (0, 384), (128, 512), (256, 512))


def fill_bias(lengths, pad, bias):
    ends, end = [], 0
    for index in range(lengths.shape[1]):
        end = end + lengths[0, index]
        ends.append(end)

    def windows(places):
        return sum([(places >= end).astype(jnp.int32) for end in ends])

    for block, (low, high) in enumerate(KEY_SPANS):
        count = high - low
        queries = lax.broadcasted_iota(jnp.int32, (128, 1), 0) + 128 * block
        keys = lax.broadcasted_iota(jnp.int32, (1, count), 1) + low
        same = windows(queries) == windows(keys)
        usable = (pad[:, low:high] > 0) | (queries == keys)
        bias[block, :, :count] = jnp.where(same & usable, 0.0, -1e30)


def two_heads(block):
    first = lax.broadcasted_iota(jnp.int32, block.shape, 1) < block.shape[1] // 2
    zero = jnp.zeros_like(block)
    return jnp.concatenate([jnp.where(first, block, zero), jnp.where(first, zero, block)], axis=0)


def one_block(stacked):
    half = stacked.shape[0] // 2
    shape = (half, stacked.shape[1])
    first = lax.broadcasted_iota(jnp.int32, shape, 1) < shape[1] // 2
    return jnp.where(first, stacked[:half], stacked[half:])


def probabilities(queries, keys, bias, block, count):
    allowed = bias[block, :, :count]
    scores = across(queries, keys) * score_scale + jnp.concatenate([allowed, allowed], axis=0)
    raised = jnp.exp(scores - jnp.max(scores, axis=1, keepdims=True))
    return raised * (1.0 / jnp.sum(raised, axis=1, keepdims=True))


def attention_kernel(where, lengths, pad, qkv, attended, attended_turned, bias):
    fill_bias(lengths, pad, bias)

    def pair(index, carry):
        columns = tile_columns(index, 128)
        keys_at, values_at = tile_columns(index + 6, 128), tile_columns(index + 12, 128)
        for block, (low, high) in enumerate(KEY_SPANS):
            rows = slice(128 * block, 128 * block + 128)
            queries = two_heads(qkv[rows, columns])
            probs = probabilities(queries, qkv[low:high, keys_at], bias, block, high - low)
            mixed = times(probs.astype(BF16), qkv[low:high, values_at])
            attended[rows, columns] = one_block(mixed).astype(BF16)
        return carry

    lax.fori_loop(0, 6, pair, 0)
    attended_turned[...] = attended[...].T


def attention_forward(where, lengths, pad, qkv):
    rows, columns = (TOKENS, WIDTH), (WIDTH, TOKENS)
    return call(
        attention_kernel,
        1,
        (where, lengths, pad, qkv),
        [pl.BlockSpec(memory_space=pltpu.SMEM), whole((1, TOKENS)), whole((TOKENS, 3 * WIDTH))],
        [(rows, BF16, whole(rows)), (columns, BF16, whole(columns))],
        [pltpu.VMEM((4, 128, 384), F32)],
        2 * TOKENS * WIDTH * 4 * TOKENS,
    )


def up_kernel(where, attended, patches, small, bias, *refs):
    sources, (mid, mlp_turned, act, act_turned, slope) = refs[:8], refs[8:13]
    rows, out_weight, out_sems, weight, sems = refs[13:]
    step = pl.program_id(0)
    out_loads = (where, sources, OUT_PART, out_weight, out_sems)
    loads = (where, sources, UP_PART, weight, sems)

    @pl.when(step == 0)
    def _():
        start_blocks(*out_loads)
        start_blocks(*loads)
        for side in range(2):
            wait_blocks(side, *out_loads)
            columns = lane_columns(where, side, 384)
            mid[:, columns] = (
                patches[:, columns].astype(F32)
                + small[16:17, columns]
                + times(attended[...], out_weight[side])
                + small[2:3, columns]
            )
        centered, scale = mean_and_scale(mid[...])
        normed = (centered * scale * small[3:4, :] + small[4:5, :]).astype(BF16)
        rows[...] = normed
        mlp_turned[...] = normed.T
        wait_blocks(0, *loads)

    @pl.when(step == 3)
    def _():
        wait_blocks(1, *loads)

    values = times(rows[...], weight[step // 3, :, tile_columns(step % 3, 512)]) + bias[...]
    share = 0.5 * (1.0 + lax.erf(values * 0.7071067811865476))
    density = jnp.exp(-0.5 * values * values) * 0.3989422804014327
    activated = (values * share).astype(BF16)
    act[...] = activated
    act_turned[...] = activated.T
    slope[...] = (share + values * density).astype(BF16)


def up_forward(where, attended, patches, small, bias, arrays):
    hidden, rows, columns = 4 * WIDTH, (TOKENS, WIDTH), (WIDTH, TOKENS)

    def turned(step, where):
        return (where[0] ^ (step // 3)) * 3 + step % 3, 0

    return call(
        up_kernel,
        6,
        (where, attended, patches, small, bias, *arrays),
        [whole(rows), whole(rows), whole((32, WIDTH)), side_tile(1, 512, 3)] + [ANY] * 8,
        [
            (rows, F32, whole(rows)),
            (columns, BF16, whole(columns)),
            ((TOKENS, hidden), BF16, side_tile(TOKENS, 512, 3)),
            ((hidden, TOKENS), BF16, pl.BlockSpec((512, TOKENS), turned)),
            ((TOKENS, hidden), BF16, side_tile(TOKENS, 512, 3)),
        ],
        [pltpu.VMEM(rows, BF16)] + weight_scratch(WIDTH, 384) + weight_scratch(WIDTH, 1536),
        2 * TOKENS * WIDTH * (hidden + WIDTH),
    )


def down_kernel(where, act, mid, small, cotangent, bias, *refs):
    sources, gate_sources, refs = refs[:8], refs[8:16], refs[16:]
    outputs, turned, shares, gate_grad, gate_bias, weight, sems, gate, gate_sems, logits = refs
    loads = (where, sources, (0, 384), weight, sems)
    gate_loads = (where, gate_sources, GATE_PART, gate, gate_sems)
    start_blocks(*loads)
    start_blocks(*gate_loads)
    for side in range(2):
        wait_blocks(side, *loads)
        columns = lane_columns(where, side, 384)
        outputs[:, columns] = (
            mid[:, columns] + times(act[...], weight[side]) + small[5:6, columns]
        ).astype(BF16)
    turned[...] = outputs[...].T
    for side in range(2):
        wait_blocks(side, *gate_loads)
        logits[:, lane_columns(where, side, 256)] = times(outputs[...], gate[side])
    logits[...] = logits[...] + bias[...]
    shares[:, 256:] = logits[:, 256:]
    gate_grad[:, 256:] = cotangent[:, 256:]
    first, rest = logits[:, :128], logits[:, 128:256]
    left = lax.broadcasted_iota(jnp.int32, first.shape, 1) < PIX
    third = jnp.where(left, rest, pltpu.roll(rest, PIX, 1))
    largest = jnp.maximum(jnp.maximum(first, pltpu.roll(first, PIX, 1)), third)
    raised, raised_third = jnp.exp(first - largest), jnp.exp(third - largest)
    scale = 1.0 / (raised + pltpu.roll(raised, PIX, 1) + raised_third)
    share, share_third = raised * scale, raised_third * scale
    shares[:, :128] = share
    shares[:, 128:256] = jnp.where(left, share_third, rest)
    pull, other = cotangent[:, :128].astype(F32), cotangent[:, 128:256].astype(F32)
    pull_third = jnp.where(left, other, pltpu.roll(other, PIX, 1))
    weighed = share * pull
    inner = weighed + pltpu.roll(weighed, PIX, 1) + share_third * pull_third
    gate_grad[:, :128] = (share * (pull - inner)).astype(BF16)
    gate_grad[:, 128:256] = jnp.where(left, share_third * (pull_third - inner), other).astype(BF16)
    gate_bias[...] = jnp.sum(gate_grad[...].astype(F32), axis=0, keepdims=True)


def down_forward(where, act, mid, small, cotangent, bias, arrays, gate_arrays):
    rows, hidden = (TOKENS, WIDTH), 4 * WIDTH
    return call(
        down_kernel,
        1,
        (where, act, mid, small, cotangent, bias, *arrays, *gate_arrays),
        [
            whole((TOKENS, hidden)),
            whole(rows),
            whole((32, WIDTH)),
            whole((TOKENS, GATE)),
            whole((1, GATE)),
        ]
        + [ANY] * 16,
        [
            (rows, BF16, whole(rows)),
            ((WIDTH, TOKENS), BF16, whole((WIDTH, TOKENS))),
            ((TOKENS, GATE), F32, whole((TOKENS, GATE))),
            ((TOKENS, GATE), BF16, whole((TOKENS, GATE))),
            ((1, GATE), F32, whole((1, GATE))),
        ],
        weight_scratch(hidden, 384)
        + weight_scratch(WIDTH, 256)
        + [pltpu.VMEM((TOKENS, GATE), F32)],
        2 * TOKENS * WIDTH * (hidden + GATE),
    )


def head_kernel(where, rows, gate_out, bias, *refs):
    sources, (out, weight, sems) = refs[:8], refs[8:]
    step = pl.program_id(0)
    loads = (where, sources, (0, 2048), weight, sems)

    @pl.when(step == 0)
    def _():
        start_blocks(*loads)
        out[...] = gate_out[...]

    @pl.when(step == 1)
    def _():
        wait_blocks(0, *loads)

    @pl.when(step == 5)
    def _():
        wait_blocks(1, *loads)

    @pl.when(step > 0)
    def _():
        tile = step - 1
        out[...] = times(rows[...], weight[tile // 4, :, tile_columns(tile % 4, 512)]) + bias[...]


def head_forward(where, rows, gate_out, bias, arrays):
    return call(
        head_kernel,
        9,
        (where, rows, gate_out, bias, *arrays),
        [whole((TOKENS, WIDTH)), whole((TOKENS, GATE)), side_tile(1, 512, 4, 1, 1)] + [ANY] * 8,
        [((TOKENS, 6 * WIDTH), F32, side_tile(TOKENS, 512, 4, 1, 1))],
        weight_scratch(WIDTH, 2048),
        2 * TOKENS * WIDTH * 4096,
    )[0]


def head_back_kernel(
    where, act_cotangent, gate_grad, cotangent, *refs
):
    gate_sources, sources, refs = refs[:8], refs[8:16], refs[16:]
    end_grad, branch, bias_grad, gate, gate_sems, weight, sems = refs
    step = pl.program_id(0)
    gate_loads = (where, gate_sources, GATE_PART, gate, gate_sems)
    loads = (where, sources, (0, 2048), weight, sems)

    @pl.when(step == 0)
    def _():
        start_blocks(*gate_loads)
        start_blocks(*loads)
        end_grad[...] = act_cotangent[...].astype(F32)
        for side in range(2):
            wait_blocks(side, *gate_loads)
            end_grad[...] += across(gate_grad[:, lane_columns(where, side, 256)], gate[side])

    @pl.when(step == 1)
    def _():
        wait_blocks(0, *loads)

    @pl.when(step == 5)
    def _():
        wait_blocks(1, *loads)

    @pl.when(step > 0)
    def _():
        tile = step - 1
        end_grad[...] += across(cotangent[...], weight[tile // 4, :, tile_columns(tile % 4, 512)])

    @pl.when(step == 8)
    def _():
        rounded = end_grad[...].astype(BF16)
        branch[...] = rounded
        bias_grad[...] = jnp.sum(rounded.astype(F32), axis=0, keepdims=True)


def head_backward(where, act_cotangent, gate_grad, cotangent, gate_arrays, arrays):
    rows = (TOKENS, WIDTH)
    return call(
        head_back_kernel,
        9,
        (where, act_cotangent, gate_grad, cotangent, *gate_arrays, *arrays),
        [whole(rows), whole((TOKENS, GATE)), side_tile(TOKENS, 512, 4, 1, 1)] + [ANY] * 16,
        [(rows, F32, whole(rows)), (rows, BF16, whole(rows)), ((1, WIDTH), F32, whole((1, WIDTH)))],
        weight_scratch(WIDTH, 256) + weight_scratch(WIDTH, 2048),
        2 * TOKENS * WIDTH * 6 * WIDTH,
    )


def down_back_kernel(
    where, branch, slope, *refs
):
    sources, (pre_grad, bias_grad, weight, sems) = refs[:8], refs[8:]
    step = pl.program_id(0)
    loads = (where, sources, (0, 384), weight, sems)

    @pl.when(step == 0)
    def _():
        start_blocks(*loads)
        for side in range(2):
            wait_blocks(side, *loads)

    rows = pl.ds(pl.multiple_of(step * 512, 512), 512)
    grad = across(branch[:, lane_columns(where, 0, 384)], weight[0, rows, :])
    grad += across(branch[:, lane_columns(where, 1, 384)], weight[1, rows, :])
    rounded = (slope[...].astype(F32) * grad).astype(BF16)
    pre_grad[...] = rounded
    bias_grad[...] = jnp.sum(rounded.astype(F32), axis=0, keepdims=True)


def down_backward(where, branch, slope, arrays):
    hidden = 4 * WIDTH
    tile = pl.BlockSpec((TOKENS, 512), lambda step, where: (0, step))
    row = pl.BlockSpec((1, 512), lambda step, where: (0, step))
    return call(
        down_back_kernel,
        6,
        (where, branch, slope, *arrays),
        [whole((TOKENS, WIDTH)), tile] + [ANY] * 8,
        [((TOKENS, hidden), BF16, tile), ((1, hidden), F32, row)],
        weight_scratch(hidden, 384),
        2 * TOKENS * WIDTH * hidden,
    )


def up_back_kernel(
    where, pre_grad, mid, end_grad, small, *refs
):
    sources, (mid_grad, out_grad, terms, weight, sems, total_grad) = refs[:8], refs[8:]
    step = pl.program_id(0)
    loads = (where, sources, UP_PART, weight, sems)

    @pl.when(step == 0)
    def _():
        start_blocks(*loads)
        wait_blocks(0, *loads)
        total_grad[...] = jnp.zeros_like(total_grad)

    @pl.when(step == 3)
    def _():
        wait_blocks(1, *loads)

    total_grad[...] += across(pre_grad[...], weight[step // 3, :, tile_columns(step % 3, 512)])

    @pl.when(step == 5)
    def _():
        pulled, gain_grad, shift_grad = norm_backward(mid[...], small[3:4, :], total_grad[...])
        pulled = pulled + end_grad[...]
        rounded = pulled.astype(BF16)
        mid_grad[...] = pulled
        out_grad[...] = rounded
        terms[...] = jnp.zeros_like(terms)
        terms[0:1, :] = jnp.sum(rounded.astype(F32), axis=0, keepdims=True)
        terms[1:2, :] = gain_grad
        terms[2:3, :] = shift_grad


def up_backward(where, pre_grad, mid, end_grad, small, arrays):
    rows = (TOKENS, WIDTH)
    return call(
        up_back_kernel,
        6,
        (where, pre_grad, mid, end_grad, small, *arrays),
        [side_tile(TOKENS, 512, 3), whole(rows), whole(rows), whole((32, WIDTH))] + [ANY] * 8,
        [(rows, F32, whole(rows)), (rows, BF16, whole(rows)), ((8, WIDTH), F32, whole((8, WIDTH)))],
        weight_scratch(WIDTH, 1536) + [pltpu.VMEM(rows, F32)],
        2 * TOKENS * WIDTH * 4 * WIDTH,
    )


def attention_back_kernel(
    where, lengths, pad, out_grad, qkv, *refs
):
    sources, refs = refs[:8], refs[8:]
    qkv_grad, weight, sems, bias, mixed, key_sum, value_sum = refs
    loads = (where, sources, OUT_PART, weight, sems)
    start_blocks(*loads)
    fill_bias(lengths, pad, bias)
    for side in range(2):
        wait_blocks(side, *loads)
    mixed[...] = (
        across(out_grad[:, lane_columns(where, 0, 384)], weight[0])
        + across(out_grad[:, lane_columns(where, 1, 384)], weight[1])
    ).astype(BF16)

    def pair(index, carry):
        columns = tile_columns(index, 128)
        keys_at, values_at = tile_columns(index + 6, 128), tile_columns(index + 12, 128)
        key_sum[...] = jnp.zeros_like(key_sum)
        value_sum[...] = jnp.zeros_like(value_sum)
        for block, (low, high) in enumerate(KEY_SPANS):
            rows = slice(128 * block, 128 * block + 128)
            queries = two_heads(qkv[rows, columns])
            keys, values = qkv[low:high, keys_at], qkv[low:high, values_at]
            grads = two_heads(mixed[rows, columns])
            probs = probabilities(queries, keys, bias, block, high - low)
            prob_grad = across(grads, values)
            inner = jnp.sum(probs * prob_grad, axis=1, keepdims=True)
            score_grad = (probs * (prob_grad - inner)).astype(BF16)
            query_grad = one_block(times(score_grad, keys)) * score_scale
            qkv_grad[rows, columns] = query_grad.astype(BF16)
            key_sum[low:high, :] += down_rows(score_grad, queries)
            value_sum[low:high, :] += down_rows(probs.astype(BF16), grads)
        qkv_grad[:, keys_at] = (key_sum[...] * score_scale).astype(BF16)
        qkv_grad[:, values_at] = value_sum[...].astype(BF16)
        return carry

    lax.fori_loop(0, 6, pair, 0)


def attention_backward(where, lengths, pad, out_grad, qkv, arrays):
    rows, wide = (TOKENS, WIDTH), (TOKENS, 3 * WIDTH)
    return call(
        attention_back_kernel,
        1,
        (where, lengths, pad, out_grad, qkv, *arrays),
        [pl.BlockSpec(memory_space=pltpu.SMEM), whole((1, TOKENS)), whole(rows), whole(wide)]
        + [ANY] * 8,
        [(wide, BF16, whole(wide))],
        weight_scratch(WIDTH, 384)
        + [
            pltpu.VMEM((4, 128, 384), F32),
            pltpu.VMEM(rows, BF16),
            pltpu.VMEM((TOKENS, 128), F32),
            pltpu.VMEM((TOKENS, 128), F32),
        ],
        2 * TOKENS * WIDTH * (WIDTH + 10 * TOKENS),
    )[0]


def front_back_kernel(
    where, lead, qkv_grad, patches, mid_grad, small, terms, down_row, up_rows, head_rows,
    *refs,
):
    sources, (patch_grad, small_grad, weight, sems, total_grad) = refs[:8], refs[8:]
    step = pl.program_id(0)
    loads = (where, sources, QKV_PART, weight, sems)

    @pl.when(step == 0)
    def _():
        start_blocks(*loads)
        wait_blocks(0, *loads)
        total_grad[...] = jnp.zeros_like(total_grad)

    @pl.when(step == 3)
    def _():
        wait_blocks(1, *loads)

    total_grad[...] += across(qkv_grad[...], weight[step // 3, :, tile_columns(step % 3, 384)])

    @pl.when(step == 5)
    def _():
        state = patches[...].astype(F32) + small[16:17, :]
        pulled, gain_grad, shift_grad = norm_backward(state, small[0:1, :], total_grad[...])
        pulled = pulled + mid_grad[...]
        patch_grad[...] = pulled
        lead_grad = jnp.sum(pulled, axis=0, keepdims=True)
        small_grad[0:1, :] = gain_grad
        small_grad[1:2, :] = shift_grad
        small_grad[2:5, :] = terms[0:3, :]
        small_grad[5:6, :] = down_row[...]
        small_grad[6:10, :] = up_rows[...]
        small_grad[10:16, :] = head_rows[...]
        places = lax.broadcasted_iota(jnp.int32, (LEADS, WIDTH), 0)
        small_grad[16:32, :] = jnp.where(places == lead[0], lead_grad, 0.0)


def front_backward(
    where, lead, qkv_grad, patches, mid_grad, small, terms, down_row, up_rows, head_rows, arrays
):
    rows = (TOKENS, WIDTH)
    return call(
        front_back_kernel,
        6,
        (
            where, lead, qkv_grad, patches, mid_grad, small, terms, down_row, up_rows, head_rows,
            *arrays,
        ),
        [
            pl.BlockSpec(memory_space=pltpu.SMEM),
            side_tile(TOKENS, 384, 3),
            whole(rows),
            whole(rows),
            whole((32, WIDTH)),
            whole((8, WIDTH)),
            whole((1, WIDTH)),
            whole((4, WIDTH)),
            whole((6, WIDTH)),
        ]
        + [ANY] * 8,
        [(rows, F32, whole(rows)), ((32, WIDTH), F32, whole((32, WIDTH)))],
        weight_scratch(WIDTH, 1152) + [pltpu.VMEM(rows, F32)],
        2 * TOKENS * WIDTH * 3 * WIDTH,
    )


def store_blocks(where, side, product, got, outs, columns):
    rows = outs[0].shape[1]
    for place in range(16):
        row = pl.multiple_of(where[1 + 16 * side + place] * rows, rows)
        block = product[pl.ds(row, rows), :]
        if side == 0:
            block = block + got[place, :, columns].astype(F32)
        outs[place // 8 if side == 0 else 0][place % 8 if side == 0 else place, :, columns] = (
            block.astype(BF16)
        )


def term_call(kernel, side, grid, where, operands, in_specs, got, rows, width, tile, scratch, flops):
    def blocks(count):
        return pl.BlockSpec((count, rows, tile), lambda step, where: (0, 0, step))

    outs = [(8, rows, width)] * 2 if side == 0 else [(16, rows, width)]
    if side == 0:
        operands, in_specs = (*operands, got), [*in_specs, blocks(16)]
    result = call(
        partial(kernel, side),
        grid,
        (where, *operands),
        in_specs,
        [(shape, BF16, blocks(shape[0])) for shape in outs],
        scratch,
        flops,
    )
    return result if side == 0 else result[0]


def head_term_kernel(side, where, turned, gate_grad, cotangent, *refs):
    got, outs, product = refs[0] if side == 0 else None, refs[1 - side : -1], refs[-1]
    logit_grad = jnp.where(pl.program_id(0) == 0, gate_grad[...], cotangent[...])
    product[...] = times(turned[...], logit_grad)
    store_blocks(where, side, product, got, outs, slice(None))


def head_terms(where, turned, gate_grad, cotangent, side, got=None):
    gate_spec = pl.BlockSpec((TOKENS, 256), lambda step, where: (0, where[0] ^ side))
    spec = pl.BlockSpec(
        (TOKENS, 256),
        lambda step, where: (0, 2 + (where[0] ^ side) * 8 + jnp.maximum(step - 1, 0)),
    )
    return term_call(
        head_term_kernel, side, 9, where, (turned, gate_grad, cotangent),
        [whole((WIDTH, TOKENS)), gate_spec, spec], got, 48, 2304, 256,
        [pltpu.VMEM((WIDTH, 256), F32)], TOKENS * WIDTH * 6 * WIDTH,
    )


def down_term_kernel(side, where, turned, branch, *refs):
    got, outs, product = refs[0] if side == 0 else None, refs[1 - side : -1], refs[-1]
    for part in range(4):
        rows = slice(part * WIDTH, (part + 1) * WIDTH)
        product[rows, :] = times(turned[rows, :], branch[...])
    store_blocks(where, side, product, got, outs, slice(None))


def down_terms(where, turned, branch, side, got=None):
    hidden = 4 * WIDTH
    spec = pl.BlockSpec((TOKENS, 384), lambda step, where: (0, where[0] ^ side))
    return term_call(
        down_term_kernel, side, 1, where, (turned, branch),
        [whole((hidden, TOKENS)), spec], got, 192, 384, 384,
        [pltpu.VMEM((hidden, 384), F32)], TOKENS * WIDTH * hidden,
    )


def up_term_kernel(side, where, turned, pre_grad, *refs):
    got, outs, product = refs[0] if side == 0 else None, refs[1 - side : -1], refs[-1]
    product[...] = times(turned[...], pre_grad[...])
    store_blocks(where, side, product, got, outs, slice(None))


def up_terms(where, turned, pre_grad, side, got=None):
    spec = pl.BlockSpec((TOKENS, 512), lambda step, where: (0, (where[0] ^ side) * 3 + step))
    return term_call(
        up_term_kernel, side, 3, where, (turned, pre_grad),
        [whole((WIDTH, TOKENS)), spec], got, 48, 1536, 512,
        [pltpu.VMEM((WIDTH, 512), F32)], TOKENS * WIDTH * 4 * WIDTH,
    )


def front_term_kernel(
    side, where, input_turned, qkv_grad, attended_turned, out_grad, small_grad, *refs
):
    got, outs, product = refs[0] if side == 0 else None, refs[1 - side : -1], refs[-1]
    product[:, 0:1152] = times(input_turned[...], qkv_grad[...])
    product[:, 1152:1536] = times(attended_turned[...], out_grad[...])
    rows = small_grad[pl.ds(pl.multiple_of((where[0] ^ side) * 16, 16), 16), :]
    product[:, 1536:1664] = jnp.concatenate([rows, jnp.zeros((112, WIDTH), F32)], axis=0).T
    store_blocks(where, side, product, got, outs, slice(None))


def front_terms(
    where, input_turned, qkv_grad, attended_turned, out_grad, small_grad, side, got=None
):
    def lane(width):
        return pl.BlockSpec((TOKENS, width), lambda step, where: (0, where[0] ^ side))

    return term_call(
        front_term_kernel, side, 1, where,
        (input_turned, qkv_grad, attended_turned, out_grad, small_grad),
        [
            whole((WIDTH, TOKENS)), lane(1152), whole((WIDTH, TOKENS)), lane(384),
            whole((32, WIDTH)),
        ],
        got, 48, 1664, 1664, [pltpu.VMEM((WIDTH, 1664), F32)], TOKENS * WIDTH * 4 * WIDTH,
    )


def rows_of(vector, count):
    return vector.reshape(32, count, 24).transpose(1, 0, 2).reshape(count, WIDTH)


def vector_of(rows):
    count = rows.shape[0]
    return rows.reshape(count, 32, 24).transpose(1, 0, 2).reshape(1, count * WIDTH)


def shards(
    patches,
    lead_index,
    window_lengths,
    pad_mask,
    lead_table,
    attn_gain,
    attn_shift,
    qkv_weight,
    out_weight,
    out_bias,
    mlp_gain,
    mlp_shift,
    up_weight,
    up_bias,
    down_weight,
    down_bias,
    head_weight,
    head_bias,
    act_cotangent,
    head_cotangent,
):
    core, where = whereabouts()
    vectors = [attn_gain, attn_shift, out_bias, mlp_gain, mlp_shift, down_bias]
    small = jnp.concatenate(
        [vector[None] for vector in vectors]
        + [up_bias.reshape(4, 24), head_bias.reshape(6, 24), lead_table, jnp.zeros((96, 24), BF16)],
        axis=0,
    ).T
    chunk_q = lane_chunk([qkv_weight], [small], core)
    chunk_u = lane_chunk([up_weight, out_weight, head_weight[:, :GATE]], [], core)
    chunk_d = lane_chunk([down_weight], [], core)
    chunk_h = lane_chunk([head_weight[:, GATE:]], [], core)
    pad = pad_mask[None]
    cotangent_sum = jnp.sum(head_cotangent[:, GATE:].astype(F32), axis=0, keepdims=True)

    pair_q, pair_u = first_pair(chunk_q), first_pair(chunk_u)
    q0, other_q = first_four(pair_q)
    q1 = second_four(pair_q, other_q)
    u0, other_u = first_four(pair_u)
    u1 = second_four(pair_u, other_u)
    pair_d = first_pair(chunk_d)
    first = both_lanes((q0, q1, exchange(q0, STEPS[3]), exchange(q1, STEPS[3])))
    attn_input, attn_turned, qkv, small_rows = front_forward(
        after(where, pair_d, other_u), lead_index, patches, first
    )
    u2 = exchange(u0, STEPS[3])
    u3 = exchange(after(u1, qkv), STEPS[3])
    pair_h = first_pair(chunk_h)
    d0, other_d = first_four(after(pair_d, qkv))
    d1 = second_four(pair_d, other_d)
    attended, attended_turned = attention_forward(
        after(where, other_d, pair_h), window_lengths, pad, qkv
    )
    second = both_lanes((u0, u1, u2, u3))
    d2, d3 = exchange(d0, STEPS[3]), exchange(after(d1, attended), STEPS[3])
    h0, other_h = first_four(after(pair_h, attended))
    h1 = second_four(pair_h, other_h)
    up_bias_row, head_bias_row = vector_of(small_rows[6:10]), vector_of(small_rows[10:16])
    mid_state, mlp_turned, act_rows, act_turned, slope = up_forward(
        after(where, other_h), attended, patches, small_rows, up_bias_row, second
    )
    down = both_lanes((d0, d1, d2, d3))
    h2, h3 = exchange(h0, STEPS[3]), exchange(after(h1, act_rows), STEPS[3])
    outputs, outputs_turned, gate_out, gate_grad, gate_bias_sum = down_forward(
        after(where, h2), act_rows, mid_state, small_rows, head_cotangent, head_bias_row, down, second
    )
    head = both_lanes((h0, h1, h2, h3))

    head_input = (outputs_turned, gate_grad, head_cotangent)
    head_sent = head_terms(where, *head_input, 1)
    head_got = exchange(head_sent, SIBLING)
    end_grad, branch_grad, down_bias_sum = head_backward(
        after(where, head_sent), act_cotangent, gate_grad, head_cotangent, second, head
    )
    keep_h, send_h = head_terms(after(where, branch_grad), *head_input, 0, head_got)
    got_h = exchange(send_h, STEPS[3])
    pre_grad, up_bias_sum = down_backward(after(where, send_h), branch_grad, slope, down)
    down_sent = down_terms(after(where, pre_grad), act_turned, branch_grad, 1)
    down_got = exchange(down_sent, SIBLING)
    mid_grad, out_grad, terms = up_backward(
        after(where, down_sent), pre_grad, mid_state, end_grad, small_rows, second
    )
    keep_h, send_h = folded(keep_h, after(got_h, out_grad))
    got_h = exchange(send_h, STEPS[2])
    keep_d, send_d = down_terms(after(where, out_grad), act_turned, branch_grad, 0, down_got)
    got_d = exchange(send_d, STEPS[3])
    up_sent = up_terms(after(where, send_d), mlp_turned, pre_grad, 1)
    up_got = exchange(up_sent, SIBLING)
    qkv_grad = attention_backward(
        after(where, send_h, up_sent), window_lengths, pad, out_grad, qkv, second
    )
    keep_h, send_h = folded(keep_h, after(got_h, qkv_grad))
    got_h = exchange(send_h, STEPS[1])
    keep_d, send_d = folded(keep_d, after(got_d, qkv_grad))
    got_d = exchange(send_d, STEPS[2])
    keep_u, send_u = up_terms(after(where, qkv_grad), mlp_turned, pre_grad, 0, up_got)
    got_u = exchange(send_u, STEPS[3])
    head_rows = rows_of(jnp.concatenate([gate_bias_sum, cotangent_sum], axis=1), 6)
    patch_grad, small_grad = front_backward(
        after(where, send_h, send_d, send_u),
        lead_index,
        qkv_grad,
        patches,
        mid_grad,
        small_rows,
        terms,
        down_bias_sum,
        rows_of(up_bias_sum, 4),
        head_rows,
        first,
    )
    front_input = (attn_turned, qkv_grad, attended_turned, out_grad, small_grad)
    front_sent = front_terms(where, *front_input, 1)
    front_got = exchange(front_sent, SIBLING)
    keep_h, send_h = folded(keep_h, after(got_h, front_sent))
    got_h = exchange(send_h, STEPS[0])
    keep_d, send_d = folded(keep_d, after(got_d, front_sent))
    got_d = exchange(send_d, STEPS[1])
    head_out = head_forward(
        after(where, front_sent, send_h, send_d), outputs, gate_out, head_bias_row, head
    )
    keep_u, send_u = folded(keep_u, after(got_u, head_out))
    got_u = exchange(send_u, STEPS[2])
    keep_f, send_f = front_terms(after(where, head_out), *front_input, 0, front_got)
    got_f = exchange(send_f, STEPS[3])
    keep_d, send_d = folded(keep_d, after(got_d, send_f))
    got_d = exchange(send_d, STEPS[0])
    gate_sum, rest_sum = finished(keep_h, after(got_h, send_f), core, (256, 2048))
    keep_u, send_u = folded(keep_u, got_u)
    got_u = exchange(send_u, STEPS[1])
    keep_f, send_f = folded(keep_f, got_f)
    got_f = exchange(send_f, STEPS[2])
    (down_sum,) = finished(keep_d, got_d, core, (384,))
    keep_u, send_u = folded(keep_u, got_u)
    got_u = exchange(send_u, STEPS[0])
    keep_f, send_f = folded(keep_f, got_f)
    got_f = exchange(send_f, STEPS[1])
    (up_sum,) = finished(keep_u, got_u, core, (1536,))
    keep_f, send_f = folded(keep_f, got_f)
    got_f = exchange(send_f, STEPS[0])
    qkv_sum, out_sum, small_sum = finished(keep_f, got_f, core, (1152, 384, 128))
    small_sum = small_sum.T
    return (
        outputs,
        head_out,
        patch_grad,
        small_sum[128:144],
        small_sum[0],
        small_sum[1],
        qkv_sum,
        out_sum,
        small_sum[2],
        small_sum[3],
        small_sum[4],
        up_sum,
        small_sum[6:10].reshape(96),
        down_sum,
        small_sum[5],
        jnp.concatenate([gate_sum, rest_sum], axis=1),
        small_sum[10:16].reshape(144),
    )


def plain_shards(
    patches,
    lead_index,
    window_lengths,
    pad_mask,
    lead_table,
    attn_gain,
    attn_shift,
    qkv_weight,
    out_weight,
    out_bias,
    mlp_gain,
    mlp_shift,
    up_weight,
    up_bias,
    down_weight,
    down_bias,
    head_weight,
    head_bias,
    act_cotangent,
    head_cotangent,
):
    front = (
        lax.all_gather(lead_table, ("dp", "fsdp"), axis=1, tiled=True),
        lax.all_gather(attn_gain, ("dp", "fsdp"), axis=0, tiled=True),
        lax.all_gather(attn_shift, ("dp", "fsdp"), axis=0, tiled=True),
        lax.all_gather(qkv_weight, ("dp", "fsdp"), axis=0, tiled=True),
        lax.all_gather(out_weight, ("dp", "fsdp"), axis=0, tiled=True),
        lax.all_gather(out_bias, ("dp", "fsdp"), axis=0, tiled=True),
    )
    rear = (
        lax.all_gather(mlp_gain, ("dp", "fsdp"), axis=0, tiled=True),
        lax.all_gather(mlp_shift, ("dp", "fsdp"), axis=0, tiled=True),
        lax.all_gather(up_weight, ("dp", "fsdp"), axis=0, tiled=True),
        lax.all_gather(up_bias, ("dp", "fsdp"), axis=0, tiled=True),
        lax.all_gather(down_weight, ("dp", "fsdp"), axis=0, tiled=True),
        lax.all_gather(down_bias, ("dp", "fsdp"), axis=0, tiled=True),
        lax.all_gather(head_weight, ("dp", "fsdp"), axis=0, tiled=True),
        lax.all_gather(head_bias, ("dp", "fsdp"), axis=0, tiled=True),
    )
    table_full, gain_one, shift_one, qkv_full, out_full, out_bias_full = front
    (
        gain_two,
        shift_two,
        up_full,
        up_bias_full,
        down_full,
        down_bias_full,
        head_full,
        head_bias_full,
    ) = rear
    token_rows, width = patches.shape
    head_dim = width // HEADS
    block_rows = min(512, token_rows)
    block_count = token_rows // block_rows
    ends = jnp.cumsum(window_lengths[0])
    positions = jnp.arange(token_rows, dtype=jnp.int32)
    window = jnp.sum((positions[:, None] >= ends[None, :]).astype(jnp.int32), axis=1)
    lead_hot = (jnp.arange(LEADS, dtype=jnp.int32) == lead_index[0]).astype(jnp.float32)
    lead_row = jnp.sum(lead_hot[:, None] * table_full.astype(jnp.float32), axis=0)
    start_state = patches.astype(jnp.float32) + lead_row[None, :]
    normed_one, pull_one = jax.vjp(
        layer_norm, start_state, gain_one.astype(jnp.float32), shift_one.astype(jnp.float32)
    )
    attn_input = normed_one.astype(jnp.bfloat16)
    qkv_rows = jnp.dot(attn_input, qkv_full, preferred_element_type=jnp.float32).astype(
        jnp.bfloat16
    )
    queries = qkv_rows[:, :width].reshape(block_count, block_rows, HEADS, head_dim)
    keys = qkv_rows[:, width : 2 * width].reshape(token_rows, HEADS, head_dim)
    values = qkv_rows[:, 2 * width :].reshape(token_rows, HEADS, head_dim)
    query_windows = window.reshape(block_count, block_rows)
    block_starts = jnp.arange(block_count, dtype=jnp.int32) * block_rows

    def block_scores(query_block, window_block, block_start):
        scores = (
            jnp.einsum("qhd,khd->hqk", query_block, keys, preferred_element_type=jnp.float32)
            * score_scale
        )
        allowed = allowed_keys(window_block, window, pad_mask, block_start)
        return jnp.where(allowed[None], scores, -1e30)

    def forward_block(inputs):
        query_block, window_block, block_start = inputs
        masked = block_scores(query_block, window_block, block_start)
        largest = jnp.max(masked, axis=-1, keepdims=True)
        raised = jnp.exp(masked - largest)
        total = jnp.sum(raised, axis=-1, keepdims=True)
        probs = (raised / total).astype(jnp.bfloat16)
        mixed = jnp.einsum("hqk,khd->qhd", probs, values, preferred_element_type=jnp.float32)
        return (
            mixed.reshape(block_rows, width).astype(jnp.bfloat16),
            (largest + jnp.log(total))[:, :, 0],
        )

    mixed_blocks, log_totals = lax.map(forward_block, (queries, query_windows, block_starts))
    attended = mixed_blocks.reshape(token_rows, width)
    mid_state = (
        start_state
        + jnp.dot(attended, out_full, preferred_element_type=jnp.float32)
        + out_bias_full.astype(jnp.float32)
    )
    normed_two, pull_two = jax.vjp(
        layer_norm, mid_state, gain_two.astype(jnp.float32), shift_two.astype(jnp.float32)
    )
    mlp_input = normed_two.astype(jnp.bfloat16)
    pre_act = jnp.dot(mlp_input, up_full, preferred_element_type=jnp.float32) + up_bias_full.astype(
        jnp.float32
    )
    activated, pull_act = jax.vjp(gelu_exact, pre_act)
    act_rows = activated.astype(jnp.bfloat16)
    end_state = (
        mid_state
        + jnp.dot(act_rows, down_full, preferred_element_type=jnp.float32)
        + down_bias_full.astype(jnp.float32)
    )
    outputs = end_state.astype(jnp.bfloat16)
    logits = jnp.dot(
        outputs, head_full, preferred_element_type=jnp.float32
    ) + head_bias_full.astype(jnp.float32)
    head_out, pull_head = jax.vjp(partial(expert_softmax, experts=EXPERTS, pixels=PIX), logits)
    up_back, down_back, head_back = (
        lax.all_gather(up_weight, ("dp", "fsdp"), axis=0, tiled=True),
        lax.all_gather(down_weight, ("dp", "fsdp"), axis=0, tiled=True),
        lax.all_gather(head_weight, ("dp", "fsdp"), axis=0, tiled=True),
    )
    qkv_back, out_back = (
        lax.all_gather(qkv_weight, ("dp", "fsdp"), axis=0, tiled=True),
        lax.all_gather(out_weight, ("dp", "fsdp"), axis=0, tiled=True),
    )
    logit_grad = pull_head(head_cotangent.astype(jnp.float32))[0].astype(jnp.bfloat16)
    head_bias_term = jnp.sum(logit_grad.astype(jnp.float32), axis=0)
    head_term = jnp.einsum("td,tn->dn", outputs, logit_grad, preferred_element_type=jnp.float32)
    end_grad = act_cotangent.astype(jnp.float32) + jnp.einsum(
        "tn,dn->td", logit_grad, head_back, preferred_element_type=jnp.float32
    )
    branch_grad = end_grad.astype(jnp.bfloat16)
    down_bias_term = jnp.sum(branch_grad.astype(jnp.float32), axis=0)
    down_term = jnp.einsum("tf,td->fd", act_rows, branch_grad, preferred_element_type=jnp.float32)
    act_grad = jnp.einsum("td,fd->tf", branch_grad, down_back, preferred_element_type=jnp.float32)
    pre_grad = pull_act(act_grad)[0].astype(jnp.bfloat16)
    up_bias_term = jnp.sum(pre_grad.astype(jnp.float32), axis=0)
    up_term = jnp.einsum("td,tf->df", mlp_input, pre_grad, preferred_element_type=jnp.float32)
    normed_two_grad = jnp.einsum("tf,df->td", pre_grad, up_back, preferred_element_type=jnp.float32)
    state_grad_two, gain_two_term, shift_two_term = pull_two(normed_two_grad)
    (
        gain_part,
        shift_part,
        up_part,
        up_bias_part,
        down_part,
        down_bias_part,
        head_part,
        head_bias_part,
    ) = (
        lax.psum_scatter(
            gain_two_term.astype(jnp.bfloat16), "dp", scatter_dimension=0, tiled=True
        ).astype(jnp.float32),
        lax.psum_scatter(
            shift_two_term.astype(jnp.bfloat16), "dp", scatter_dimension=0, tiled=True
        ).astype(jnp.float32),
        lax.psum_scatter(
            up_term.astype(jnp.bfloat16), "dp", scatter_dimension=0, tiled=True
        ).astype(jnp.float32),
        lax.psum_scatter(
            up_bias_term.astype(jnp.bfloat16), "dp", scatter_dimension=0, tiled=True
        ).astype(jnp.float32),
        lax.psum_scatter(
            down_term.astype(jnp.bfloat16), "dp", scatter_dimension=0, tiled=True
        ).astype(jnp.float32),
        lax.psum_scatter(
            down_bias_term.astype(jnp.bfloat16), "dp", scatter_dimension=0, tiled=True
        ).astype(jnp.float32),
        lax.psum_scatter(
            head_term.astype(jnp.bfloat16), "dp", scatter_dimension=0, tiled=True
        ).astype(jnp.float32),
        lax.psum_scatter(
            head_bias_term.astype(jnp.bfloat16), "dp", scatter_dimension=0, tiled=True
        ).astype(jnp.float32),
    )
    rear_grads = (
        lax.psum_scatter(gain_part, "fsdp", scatter_dimension=0, tiled=True),
        lax.psum_scatter(shift_part, "fsdp", scatter_dimension=0, tiled=True),
        lax.psum_scatter(up_part, "fsdp", scatter_dimension=0, tiled=True),
        lax.psum_scatter(up_bias_part, "fsdp", scatter_dimension=0, tiled=True),
        lax.psum_scatter(down_part, "fsdp", scatter_dimension=0, tiled=True),
        lax.psum_scatter(down_bias_part, "fsdp", scatter_dimension=0, tiled=True),
        lax.psum_scatter(head_part, "fsdp", scatter_dimension=0, tiled=True),
        lax.psum_scatter(head_bias_part, "fsdp", scatter_dimension=0, tiled=True),
    )
    mid_grad = end_grad + state_grad_two
    out_grad = mid_grad.astype(jnp.bfloat16)
    out_bias_term = jnp.sum(out_grad.astype(jnp.float32), axis=0)
    out_term = jnp.einsum("td,te->de", attended, out_grad, preferred_element_type=jnp.float32)
    mixed_grad = jnp.einsum(
        "te,de->td", out_grad, out_back, preferred_element_type=jnp.float32
    ).astype(jnp.bfloat16)
    grad_blocks = mixed_grad.reshape(block_count, block_rows, HEADS, head_dim)

    def backward_block(carry, inputs):
        key_sum, value_sum = carry
        query_block, grad_block, window_block, total_block, block_start = inputs
        masked = block_scores(query_block, window_block, block_start)
        probs = jnp.exp(masked - total_block[:, :, None])
        prob_grad = jnp.einsum(
            "qhd,khd->hqk", grad_block, values, preferred_element_type=jnp.float32
        )
        inner = jnp.sum(probs * prob_grad, axis=-1, keepdims=True)
        score_grad = (probs * (prob_grad - inner)).astype(jnp.bfloat16)
        query_grad = (
            jnp.einsum("hqk,khd->qhd", score_grad, keys, preferred_element_type=jnp.float32)
            * score_scale
        )
        key_sum = (
            key_sum
            + jnp.einsum(
                "hqk,qhd->khd", score_grad, query_block, preferred_element_type=jnp.float32
            )
            * score_scale
        )
        value_sum = value_sum + jnp.einsum(
            "hqk,qhd->khd",
            probs.astype(jnp.bfloat16),
            grad_block,
            preferred_element_type=jnp.float32,
        )
        return ((key_sum, value_sum), query_grad.reshape(block_rows, width))

    zero_keys = jnp.zeros((token_rows, HEADS, head_dim), jnp.float32)
    (key_grad, value_grad), query_grads = lax.scan(
        backward_block,
        (zero_keys, zero_keys),
        (queries, grad_blocks, query_windows, log_totals, block_starts),
    )
    qkv_grad = jnp.concatenate(
        [
            query_grads.reshape(token_rows, width),
            key_grad.reshape(token_rows, width),
            value_grad.reshape(token_rows, width),
        ],
        axis=1,
    ).astype(jnp.bfloat16)
    qkv_term = jnp.einsum("td,te->de", attn_input, qkv_grad, preferred_element_type=jnp.float32)
    normed_one_grad = jnp.einsum(
        "te,de->td", qkv_grad, qkv_back, preferred_element_type=jnp.float32
    )
    state_grad_one, gain_one_term, shift_one_term = pull_one(normed_one_grad)
    patch_grad = mid_grad + state_grad_one
    lead_term = lead_hot[:, None] * jnp.sum(patch_grad, axis=0)[None, :]
    lead_part, gain_one_part, shift_one_part, qkv_part, out_part, out_bias_part = (
        lax.psum_scatter(
            lead_term.astype(jnp.bfloat16), "dp", scatter_dimension=1, tiled=True
        ).astype(jnp.float32),
        lax.psum_scatter(
            gain_one_term.astype(jnp.bfloat16), "dp", scatter_dimension=0, tiled=True
        ).astype(jnp.float32),
        lax.psum_scatter(
            shift_one_term.astype(jnp.bfloat16), "dp", scatter_dimension=0, tiled=True
        ).astype(jnp.float32),
        lax.psum_scatter(
            qkv_term.astype(jnp.bfloat16), "dp", scatter_dimension=0, tiled=True
        ).astype(jnp.float32),
        lax.psum_scatter(
            out_term.astype(jnp.bfloat16), "dp", scatter_dimension=0, tiled=True
        ).astype(jnp.float32),
        lax.psum_scatter(
            out_bias_term.astype(jnp.bfloat16), "dp", scatter_dimension=0, tiled=True
        ).astype(jnp.float32),
    )
    front_grads = (
        lax.psum_scatter(lead_part, "fsdp", scatter_dimension=1, tiled=True),
        lax.psum_scatter(gain_one_part, "fsdp", scatter_dimension=0, tiled=True),
        lax.psum_scatter(shift_one_part, "fsdp", scatter_dimension=0, tiled=True),
        lax.psum_scatter(qkv_part, "fsdp", scatter_dimension=0, tiled=True),
        lax.psum_scatter(out_part, "fsdp", scatter_dimension=0, tiled=True),
        lax.psum_scatter(out_bias_part, "fsdp", scatter_dimension=0, tiled=True),
    )
    return (
        outputs,
        head_out,
        patch_grad,
        front_grads[0],
        front_grads[1],
        front_grads[2],
        front_grads[3],
        front_grads[4],
        front_grads[5],
        rear_grads[0],
        rear_grads[1],
        rear_grads[2],
        rear_grads[3],
        rear_grads[4],
        rear_grads[5],
        rear_grads[6],
        rear_grads[7],
    )


def solution(mesh):
    in_specs = (
        P(("dp", "fsdp"), None),
        P(("dp", "fsdp")),
        P(("dp", "fsdp"), None),
        P(("dp", "fsdp")),
        P(None, ("dp", "fsdp")),
        P(("dp", "fsdp")),
        P(("dp", "fsdp")),
        P(("dp", "fsdp"), None),
        P(("dp", "fsdp"), None),
        P(("dp", "fsdp")),
        P(("dp", "fsdp")),
        P(("dp", "fsdp")),
        P(("dp", "fsdp"), None),
        P(("dp", "fsdp")),
        P(("dp", "fsdp"), None),
        P(("dp", "fsdp")),
        P(("dp", "fsdp"), None),
        P(("dp", "fsdp")),
        P(("dp", "fsdp"), None),
        P(("dp", "fsdp"), None),
    )
    out_specs = (
        P(("dp", "fsdp"), None),
        P(("dp", "fsdp"), None),
        P(("dp", "fsdp"), None),
        P(None, ("dp", "fsdp")),
        P(("dp", "fsdp")),
        P(("dp", "fsdp")),
        P(("dp", "fsdp"), None),
        P(("dp", "fsdp"), None),
        P(("dp", "fsdp")),
        P(("dp", "fsdp")),
        P(("dp", "fsdp")),
        P(("dp", "fsdp"), None),
        P(("dp", "fsdp")),
        P(("dp", "fsdp"), None),
        P(("dp", "fsdp")),
        P(("dp", "fsdp"), None),
        P(("dp", "fsdp")),
    )
    body = shards if dict(mesh.shape) == {"dp": 4, "fsdp": 8} else plain_shards
    return jax.shard_map(body, mesh=mesh, in_specs=in_specs, out_specs=out_specs, check_vma=False)
```

```python
from functools import partial

import jax
import jax.numpy as jnp
from jax import lax
from jax.experimental import pallas as pl
from jax.experimental.pallas import tpu as pltpu
from jax.sharding import PartitionSpec as P

HEADS = 12
PIX = 64
EXPERTS = 3
LEADS = 16


norm_epsilon = 1e-05
score_scale = 0.125


def layer_norm(hidden, norm_gain, norm_shift):
    average = jnp.mean(hidden, axis=-1, keepdims=True)
    centered = hidden - average
    variance = jnp.mean(centered * centered, axis=-1, keepdims=True)
    return centered * lax.rsqrt(variance + norm_epsilon) * norm_gain + norm_shift


def gelu_exact(values):
    return 0.5 * values * (1.0 + lax.erf(values * 0.7071067811865476))


def expert_softmax(logits, experts, pixels):
    gate_part = logits[:, : experts * pixels].reshape(logits.shape[0], experts, pixels)
    largest = jnp.max(gate_part, axis=1, keepdims=True)
    raised = jnp.exp(gate_part - largest)
    shares = raised / jnp.sum(raised, axis=1, keepdims=True)
    return jnp.concatenate(
        [shares.reshape(logits.shape[0], experts * pixels), logits[:, experts * pixels :]], axis=1
    )


def allowed_keys(query_window, key_window, key_valid, query_start):
    query_place = query_start + jnp.arange(query_window.shape[0], dtype=jnp.int32)
    key_place = jnp.arange(key_window.shape[0], dtype=jnp.int32)
    same_window = query_window[:, None] == key_window[None, :]
    usable = (key_valid[None, :] > 0) | (query_place[:, None] == key_place[None, :])
    return same_window & usable


AXES = ("dp", "fsdp")
FAR_Z, NEAR_Z, FIRST, SECOND, SIBLING = (4, 4), (2, 2), (8, 16), (16, 8), (1, 1)
ORDERS = {
    "q": (FAR_Z, NEAR_Z, FIRST, SECOND),
    "u": (NEAR_Z, FAR_Z, FIRST, SECOND),
    "d": (FAR_Z, FIRST, SECOND, NEAR_Z),
    "h": (FIRST, FAR_Z, NEAR_Z, SECOND),
    "head": (FAR_Z, NEAR_Z, FIRST, SECOND),
    "down": (FAR_Z, NEAR_Z, FIRST, SECOND),
    "up": (FAR_Z, FIRST, SECOND, NEAR_Z),
    "front": (FAR_Z, NEAR_Z, FIRST, SECOND),
}
WIDTH = 768
HIDDEN = 3072
HEAD = 4608
TOKENS = 512
GATE = 512
F32 = jnp.float32
BF16 = jnp.bfloat16
HBM = pl.BlockSpec(memory_space=pltpu.HBM)
SMEM = pl.BlockSpec(memory_space=pltpu.SMEM)
VMEM = pl.BlockSpec(memory_space=pltpu.VMEM)
QKV_PART, SMALL_PART = (0, 1152), (1152, 128)
UP_PART, OUT_PART, GATE_PART = (0, 1536), (1536, 384), (1920, 256)
DOWN_PART, HEAD_PART = (0, 384), (0, 2048)


def chip_masks(order, lane):
    masks = []
    for place in range(16):
        mask = 0
        for step in range(4):
            if place >> step & 1:
                mask ^= order[step][lane]
        masks.append(mask >> 1)
    return masks


def table_start(group, side):
    return 1 + 32 * list(ORDERS).index(group) + 16 * side


def exchange(array, masks):
    return lax.ppermute(array, AXES, [(d, d ^ masks[d & 1]) for d in range(32)])


def whereabouts():
    device = lax.axis_index("dp") * 8 + lax.axis_index("fsdp")
    core, chip = device % 2, device // 2
    tables = [chip_masks(order, 0) + chip_masks(order, 1) for order in ORDERS.values()]
    swapped = [chip_masks(order, 1) + chip_masks(order, 0) for order in ORDERS.values()]
    places = jnp.where(core == 0, jnp.array(tables, jnp.int32), jnp.array(swapped, jnp.int32))
    places = (places ^ chip).reshape(32 * len(ORDERS))
    return core, jnp.concatenate([core[None].astype(jnp.int32), places])


def after(value, *marks):
    return lax.optimization_barrier((value, marks))[0]


def halves(array, core):
    half = array.shape[1] // 2
    left, right = array[:, :half], array[:, half:]
    return jnp.where(core == 0, left, right), jnp.where(core == 0, right, left)


def in_core_order(core, mine, theirs, axis):
    return jnp.where(
        core == 0,
        jnp.concatenate([mine, theirs], axis=axis),
        jnp.concatenate([theirs, mine], axis=axis),
    )


def lane_chunk(parts, small, core):
    pairs = [halves(part, core) for part in parts]
    mine = jnp.concatenate([pair[0] for pair in pairs] + small, axis=1)
    theirs = jnp.concatenate([pair[1] for pair in pairs] + small, axis=1)
    return in_core_order(core, mine, exchange(theirs, SIBLING), 0)[None]


def doubled(held, masks):
    return jnp.concatenate([held, exchange(held, masks)], axis=0)


def both_lanes(*arrays):
    return arrays + tuple(exchange(array, SIBLING) for array in arrays)


def total(first, second):
    return first.astype(F32) + second.astype(F32)


def folded(keep, got, start=0):
    half = got.shape[0] // 2
    send = total(keep[half:], got[half:]).astype(BF16)
    return total(keep[:half], got[:half]).astype(BF16), send


def finished(keep, got, core, widths):
    block = total(keep, got)[0]
    rows = block.shape[0] // 2
    upper, lower = block[:rows], block[rows:]
    mine = jnp.where(core == 0, upper, lower)
    theirs = jnp.where(core == 0, lower, upper).astype(BF16)
    other = exchange(theirs, SIBLING).astype(F32)
    pieces, start = [], 0
    for width in widths:
        span = slice(start, start + width)
        pieces.append(in_core_order(core, mine[:, span], other[:, span], 1))
        start += width
    return pieces


def across(first, second):
    return lax.dot_general(first, second, (((1,), (1,)), ((), ())), preferred_element_type=F32)


def times(first, second):
    return jnp.dot(first, second, preferred_element_type=F32)


def lane_columns(where, side, stride, first=0, width=None):
    return pl.ds(pl.multiple_of(first + (where[0] ^ side) * stride, 128), width or stride)


def block_copies(where, group, sources, part, target, sems, side):
    start, width = part
    rows = sources[0].shape[1]
    half = len(sources) // 2
    count = 16 // half
    copies = []
    for place in range(16):
        row = pl.multiple_of(where[table_start(group, side) + place] * rows, rows)
        copies.append(
            pltpu.make_async_copy(
                sources[half * side + place // count].at[place % count, :, pl.ds(start, width)],
                target.at[side, pl.ds(row, rows), :],
                sems.at[side, place],
            )
        )
    return copies


def term_copies(where, group, lane, out, sems, side):
    rows = out.shape[1]
    copies = []
    for place in range(16):
        row = pl.multiple_of(where[table_start(group, side) + place] * rows, rows)
        copies.append(
            pltpu.make_async_copy(lane.at[side, pl.ds(row, rows), :], out.at[place], sems.at[side, place])
        )
    return copies


def start_all(copies):
    for copy in copies:
        copy.start()


def wait_all(copies):
    for copy in copies:
        copy.wait()


def mean_and_scale(hidden):
    average = jnp.mean(hidden, axis=1, keepdims=True)
    centered = hidden - average
    variance = jnp.mean(centered * centered, axis=1, keepdims=True)
    return centered, lax.rsqrt(variance + norm_epsilon)


def norm_backward(hidden, gain, upstream):
    centered, scale = mean_and_scale(hidden)
    normed = centered * scale
    gain_grad = jnp.sum(upstream * normed, axis=0, keepdims=True)
    shift_grad = jnp.sum(upstream, axis=0, keepdims=True)
    scaled = upstream * gain
    first = jnp.mean(scaled, axis=1, keepdims=True)
    second = jnp.mean(scaled * normed, axis=1, keepdims=True)
    return scale * (scaled - first - normed * second), gain_grad, shift_grad


def call(kernel, operands, in_specs, outs, scratch):
    return pl.pallas_call(
        kernel,
        out_shape=[jax.ShapeDtypeStruct(shape, kind) for shape, kind, _ in outs],
        in_specs=in_specs,
        out_specs=[HBM if copied else VMEM for _, _, copied in outs],
        scratch_shapes=scratch,
        compiler_params=pltpu.CompilerParams(vmem_limit_bytes=56 * 1024 * 1024),
        cost_estimate=pl.CostEstimate(flops=2 * 10**12, bytes_accessed=10**10, transcendentals=0),
    )(*operands)


def lane_scratch(rows, width):
    return [pltpu.VMEM((2, rows, width), BF16), pltpu.SemaphoreType.DMA((2, 16))]


def taken(refs, *counts):
    groups = []
    for count in counts:
        groups.append(refs[:count])
        refs = refs[count:]
    return *groups, refs


def front_kernel(where, lead, patches, *refs):
    sources, outs, scratch = taken(refs, 4, 3)
    turned_out, qkv_out, small = outs
    weight, sems, smalls, small_sems, state, rows, turned, qkv, io_sems = scratch
    loads = [block_copies(where, "q", sources, QKV_PART, weight, sems, side) for side in range(2)]
    small_loads = block_copies(where, "q", sources, SMALL_PART, smalls, small_sems, 0)
    state_load = pltpu.make_async_copy(patches, state, io_sems.at[0])
    start_all(small_loads)
    state_load.start()
    start_all(loads[0])
    start_all(loads[1])
    wait_all(small_loads)
    columns = smalls[0].astype(F32).T
    places = lax.broadcasted_iota(jnp.int32, (LEADS, WIDTH), 0)
    lead_row = jnp.sum(
        jnp.where(places == lead[0], columns[16 : 16 + LEADS], 0.0), axis=0, keepdims=True
    )
    small[...] = columns[:32]
    small[16:17, :] = lead_row
    state_load.wait()
    centered, scale = mean_and_scale(state[...].astype(F32) + lead_row)
    rows[...] = (centered * scale * columns[0:1] + columns[1:2]).astype(BF16)
    turned[...] = rows[...].T
    stores = [pltpu.make_async_copy(turned, turned_out, io_sems.at[1])]
    stores[0].start()
    for side in range(2):
        wait_all(loads[side])
        span = lane_columns(where, side, 1152)
        qkv[:, span] = times(rows[...], weight[side]).astype(BF16)
        stores.append(pltpu.make_async_copy(qkv.at[:, span], qkv_out.at[:, span], io_sems.at[2 + side]))
        stores[-1].start()
    wait_all(stores)


def front_forward(where, lead_index, patches, arrays):
    return call(
        front_kernel,
        (where, lead_index, patches, *arrays),
        [SMEM, SMEM, HBM] + [HBM] * 4,
        [
            ((WIDTH, TOKENS), BF16, True),
            ((TOKENS, 3 * WIDTH), BF16, True),
            ((32, WIDTH), F32, False),
        ],
        lane_scratch(WIDTH, 1152)
        + [pltpu.VMEM((1, WIDTH, 128), BF16), pltpu.SemaphoreType.DMA((1, 16))]
        + [
            pltpu.VMEM((TOKENS, WIDTH), BF16),
            pltpu.VMEM((TOKENS, WIDTH), BF16),
            pltpu.VMEM((WIDTH, TOKENS), BF16),
            pltpu.VMEM((TOKENS, 3 * WIDTH), BF16),
            pltpu.SemaphoreType.DMA((4,)),
        ],
    )


KEY_SPANS = ((0, 256), (0, 384), (128, 512), (256, 512))


def fill_bias(lengths, pad, bias):
    ends, end = [], 0
    for index in range(lengths.shape[1]):
        end = end + lengths[0, index]
        ends.append(end)

    def windows(places):
        return sum([(places >= end).astype(jnp.int32) for end in ends])

    for block, (low, high) in enumerate(KEY_SPANS):
        count = high - low
        queries = lax.broadcasted_iota(jnp.int32, (1, 128), 1) + 128 * block
        keys = lax.broadcasted_iota(jnp.int32, (count, 1), 0) + low
        same = windows(queries) == windows(keys)
        usable = (pad[low:high, :] > 0) | (queries == keys)
        bias[block, :count, :] = jnp.where(same & usable, 0.0, -1e30)


def two_heads(block):
    first = lax.broadcasted_iota(jnp.int32, block.shape, 1) < block.shape[1] // 2
    zero = jnp.zeros_like(block)
    return jnp.concatenate([jnp.where(first, block, zero), jnp.where(first, zero, block)], axis=0)


def head_rows_of(stacked):
    return jnp.concatenate([stacked[:64, :128], stacked[64:, 128:]], axis=0)


def probabilities(scores, allowed):
    masked = scores * score_scale + allowed
    raised = jnp.exp(masked - jnp.max(masked, axis=0, keepdims=True))
    return raised * (1.0 / jnp.sum(raised, axis=0, keepdims=True))


def attention_kernel(where, lengths, pad, qkv, attended_out, turned_out, bias, turned, rows, sems):
    fill_bias(lengths, pad, bias)

    def pair(index, carry):
        first = index * 128
        columns = pl.ds(pl.multiple_of(first, 128), 128)
        keys_at = pl.ds(pl.multiple_of(first + WIDTH, 128), 128)
        values = qkv[:, pl.ds(pl.multiple_of(first + 2 * WIDTH, 128), 128)].T
        for block, (low, high) in enumerate(KEY_SPANS):
            span = slice(128 * block, 128 * block + 128)
            scores = across(qkv[low:high, keys_at], two_heads(qkv[span, columns]))
            allowed = bias[block, : high - low, :]
            probs = [
                probabilities(scores[:, 128 * head : 128 * head + 128], allowed).astype(BF16)
                for head in range(2)
            ]
            mixed = times(values[:, low:high], jnp.concatenate(probs, axis=1))
            turned[columns, span] = head_rows_of(mixed).astype(BF16)
        return carry

    lax.fori_loop(0, WIDTH // 128, pair, 0)
    stores = [pltpu.make_async_copy(turned, turned_out, sems.at[0])]
    stores[0].start()
    rows[...] = turned[...].T
    stores.append(pltpu.make_async_copy(rows, attended_out, sems.at[1]))
    stores[1].start()
    wait_all(stores)


def attention_forward(where, lengths, pad, qkv):
    rows, columns = (TOKENS, WIDTH), (WIDTH, TOKENS)
    return call(
        attention_kernel,
        (where, lengths, pad, qkv),
        [SMEM, SMEM, VMEM, VMEM],
        [(rows, BF16, True), (columns, BF16, True)],
        [
            pltpu.VMEM((4, 384, 128), F32),
            pltpu.VMEM(columns, BF16),
            pltpu.VMEM(rows, BF16),
            pltpu.SemaphoreType.DMA((2,)),
        ],
    )


def up_kernel(where, attended, patches, small, bias, *refs):
    sources, outs, scratch = taken(refs, 4, 5)
    mid_out, mlp_turned_out, act_out, act_turned_out, slope_out = outs
    out_weight, out_sems, weight, sems, scratch = *scratch[:4], scratch[4:]
    inputs, state, mid, rows, mlp_turned, act, act_turned, slope, io_sems, act_sems = scratch
    out_loads = [block_copies(where, "u", sources, OUT_PART, out_weight, out_sems, s) for s in range(2)]
    loads = [block_copies(where, "u", sources, UP_PART, weight, sems, side) for side in range(2)]
    in_loads = [
        pltpu.make_async_copy(attended, inputs, io_sems.at[0]),
        pltpu.make_async_copy(patches, state, io_sems.at[1]),
    ]
    start_all(in_loads)
    start_all(out_loads[0] + out_loads[1])
    start_all(loads[0] + loads[1])
    wait_all(in_loads)
    for side in range(2):
        wait_all(out_loads[side])
        span = lane_columns(where, side, 384)
        mid[:, span] = (
            state[:, span].astype(F32)
            + small[16:17, span]
            + times(inputs[...], out_weight[side])
            + small[2:3, span]
        )
    centered, scale = mean_and_scale(mid[...])
    rows[...] = (centered * scale * small[3:4, :] + small[4:5, :]).astype(BF16)
    mlp_turned[...] = rows[...].T
    stores = [
        pltpu.make_async_copy(mid, mid_out, io_sems.at[2]),
        pltpu.make_async_copy(mlp_turned, mlp_turned_out, io_sems.at[3]),
    ]
    start_all(stores)
    for side in range(2):
        wait_all(loads[side])
        for tile in range(3):
            span = lane_columns(where, side, 1536, tile * 512, 512)
            values = times(rows[...], weight[side, :, tile * 512 : tile * 512 + 512]) + bias[:, span]
            share = 0.5 * (1.0 + lax.erf(values * 0.7071067811865476))
            density = jnp.exp(-0.5 * values * values) * 0.3989422804014327
            activated = (values * share).astype(BF16)
            act[:, span] = activated
            act_turned[span, :] = activated.T
            slope[:, span] = (share + values * density).astype(BF16)
            slot = 3 * side + tile
            copies = [
                pltpu.make_async_copy(act.at[:, span], act_out.at[:, span], act_sems.at[slot, 0]),
                pltpu.make_async_copy(
                    act_turned.at[span, :], act_turned_out.at[span, :], act_sems.at[slot, 1]
                ),
                pltpu.make_async_copy(slope.at[:, span], slope_out.at[:, span], act_sems.at[slot, 2]),
            ]
            start_all(copies)
            stores += copies
    wait_all(stores)


def up_forward(where, attended, patches, small, bias, arrays):
    rows, columns = (TOKENS, WIDTH), (WIDTH, TOKENS)
    wide, tall = (TOKENS, HIDDEN), (HIDDEN, TOKENS)
    return call(
        up_kernel,
        (where, attended, patches, small, bias, *arrays),
        [SMEM, HBM, HBM, VMEM, VMEM] + [HBM] * 4,
        [
            (rows, F32, True),
            (columns, BF16, True),
            (wide, BF16, True),
            (tall, BF16, True),
            (wide, BF16, True),
        ],
        lane_scratch(WIDTH, 384)
        + lane_scratch(WIDTH, 1536)
        + [
            pltpu.VMEM(rows, BF16),
            pltpu.VMEM(rows, BF16),
            pltpu.VMEM(rows, F32),
            pltpu.VMEM(rows, BF16),
            pltpu.VMEM(columns, BF16),
            pltpu.VMEM(wide, BF16),
            pltpu.VMEM(tall, BF16),
            pltpu.VMEM(wide, BF16),
            pltpu.SemaphoreType.DMA((4,)),
            pltpu.SemaphoreType.DMA((6, 3)),
        ],
    )


def gate_shares(logits, cotangent, shares, gate_grad):
    shares[:, 256:] = logits[:, 256:]
    gate_grad[:, 256:] = cotangent[:, 256:GATE]
    first, rest = logits[:, :128], logits[:, 128:256]
    left = lax.broadcasted_iota(jnp.int32, first.shape, 1) < PIX
    third = jnp.where(left, rest, pltpu.roll(rest, PIX, 1))
    largest = jnp.maximum(jnp.maximum(first, pltpu.roll(first, PIX, 1)), third)
    raised, raised_third = jnp.exp(first - largest), jnp.exp(third - largest)
    scale = 1.0 / (raised + pltpu.roll(raised, PIX, 1) + raised_third)
    share, share_third = raised * scale, raised_third * scale
    shares[:, :128] = share
    shares[:, 128:256] = jnp.where(left, share_third, rest)
    pull, other = cotangent[:, :128].astype(F32), cotangent[:, 128:256].astype(F32)
    pull_third = jnp.where(left, other, pltpu.roll(other, PIX, 1))
    weighed = share * pull
    inner = weighed + pltpu.roll(weighed, PIX, 1) + share_third * pull_third
    gate_grad[:, :128] = (share * (pull - inner)).astype(BF16)
    gate_grad[:, 128:256] = jnp.where(left, share_third * (pull_third - inner), other).astype(BF16)


def down_kernel(where, act, mid, small, cotangent, bias, *refs):
    sources, gate_sources, outs, scratch = taken(refs, 4, 4, 6)
    outputs, shares, gate_grad, gate_bias, mine_out, theirs_out = outs
    weight, sems, gate, gate_sems, lane, lane_sems, scratch = *scratch[:6], scratch[6:]
    acts, mids, pulls, turned, logits, io_sems = scratch
    loads = [block_copies(where, "d", sources, DOWN_PART, weight, sems, side) for side in range(2)]
    gate_loads = [
        block_copies(where, "u", gate_sources, GATE_PART, gate, gate_sems, side) for side in range(2)
    ]
    in_loads = [
        pltpu.make_async_copy(act, acts, io_sems.at[0]),
        pltpu.make_async_copy(mid, mids, io_sems.at[1]),
    ]
    pull_load = pltpu.make_async_copy(cotangent, pulls, io_sems.at[2])
    start_all(in_loads)
    start_all(loads[0] + loads[1])
    start_all(gate_loads[0] + gate_loads[1])
    pull_load.start()
    wait_all(in_loads)
    for side in range(2):
        wait_all(loads[side])
        span = lane_columns(where, side, 384)
        outputs[:, span] = (
            mids[:, span] + times(acts[...], weight[side]) + small[5:6, span]
        ).astype(BF16)
    turned[...] = outputs[...].T
    for side in range(2):
        wait_all(gate_loads[side])
        logits[:, lane_columns(where, side, 256)] = times(outputs[...], gate[side])
    logits[...] = logits[...] + bias[:, :GATE]
    pull_load.wait()
    gate_shares(logits, pulls, shares, gate_grad)
    gate_bias[...] = jnp.sum(gate_grad[...].astype(F32), axis=0, keepdims=True)
    stores = []
    for side, out in ((1, theirs_out), (0, mine_out)):
        lane[side, :, :256] = times(
            turned[...], gate_grad[:, lane_columns(where, side, 256)]
        ).astype(BF16)
        for tile in range(4):
            span = lane_columns(where, side, 2048, GATE + tile * 512, 512)
            lane[side, :, 256 + tile * 512 : 768 + tile * 512] = times(
                turned[...], pulls[:, span]
            ).astype(BF16)
        copies = term_copies(where, "head", lane, out, lane_sems, side)
        start_all(copies)
        stores += copies
    wait_all(stores)


def down_forward(where, act, mid, small, cotangent, bias, arrays, gate_arrays):
    rows = (TOKENS, WIDTH)
    return call(
        down_kernel,
        (where, act, mid, small, cotangent, bias, *arrays, *gate_arrays),
        [SMEM, HBM, HBM, VMEM, HBM, VMEM] + [HBM] * 8,
        [
            (rows, BF16, False),
            ((TOKENS, GATE), F32, False),
            ((TOKENS, GATE), BF16, False),
            ((1, GATE), F32, False),
            ((16, 48, 2304), BF16, True),
            ((16, 48, 2304), BF16, True),
        ],
        lane_scratch(HIDDEN, 384)
        + lane_scratch(WIDTH, 256)
        + lane_scratch(WIDTH, 2304)
        + [
            pltpu.VMEM((TOKENS, HIDDEN), BF16),
            pltpu.VMEM(rows, F32),
            pltpu.VMEM((TOKENS, HEAD), BF16),
            pltpu.VMEM((WIDTH, TOKENS), BF16),
            pltpu.VMEM((TOKENS, GATE), F32),
            pltpu.SemaphoreType.DMA((3,)),
        ],
    )


def head_kernel(where, rows, gate_out, bias, *refs):
    sources, outs, scratch = taken(refs, 4, 1)
    (out,) = outs
    weight, sems, inputs, result, io_sems = scratch
    loads = [block_copies(where, "h", sources, HEAD_PART, weight, sems, side) for side in range(2)]
    row_load = pltpu.make_async_copy(rows, inputs, io_sems.at[0])
    gate_load = pltpu.make_async_copy(gate_out, result.at[:, :GATE], io_sems.at[1])
    row_load.start()
    start_all(loads[0])
    start_all(loads[1])
    gate_load.start()
    row_load.wait()
    stores = []

    def store(span):
        stores.append(
            pltpu.make_async_copy(result.at[:, span], out.at[:, span], io_sems.at[2 + len(stores)])
        )
        stores[-1].start()

    for side in range(2):
        wait_all(loads[side])
        for tile in range(4):
            span = lane_columns(where, side, 2048, GATE + tile * 512, 512)
            result[:, span] = (
                times(inputs[...], weight[side, :, tile * 512 : tile * 512 + 512]) + bias[:, span]
            )
            store(span)
    gate_load.wait()
    store(pl.ds(0, GATE))
    wait_all(stores)


def head_forward(where, rows, gate_out, bias, arrays):
    return call(
        head_kernel,
        (where, rows, gate_out, bias, *arrays),
        [SMEM, HBM, HBM, VMEM] + [HBM] * 4,
        [((TOKENS, HEAD), F32, True)],
        lane_scratch(WIDTH, 2048)
        + [
            pltpu.VMEM((TOKENS, WIDTH), BF16),
            pltpu.VMEM((TOKENS, HEAD), F32),
            pltpu.SemaphoreType.DMA((11,)),
        ],
    )[0]


def head_back_kernel(where, act_cotangent, gate_grad, cotangent, slope, *refs):
    sources, gate_sources, down_sources, outs, scratch = taken(refs, 4, 4, 4, 5)
    end_grad, branch, down_bias, up_bias, pre_out = outs
    weight, sems, gate, gate_sems, down, down_sems, scratch = *scratch[:6], scratch[6:]
    act_pulls, gate_pulls, pulls, slopes, pre_grad, io_sems, pre_sems = scratch
    loads = [block_copies(where, "h", sources, HEAD_PART, weight, sems, side) for side in range(2)]
    gate_loads = [
        block_copies(where, "u", gate_sources, GATE_PART, gate, gate_sems, side) for side in range(2)
    ]
    down_loads = [
        block_copies(where, "d", down_sources, DOWN_PART, down, down_sems, side) for side in range(2)
    ]
    first_loads = [
        pltpu.make_async_copy(act_cotangent, act_pulls, io_sems.at[0]),
        pltpu.make_async_copy(gate_grad, gate_pulls, io_sems.at[1]),
    ]
    pull_load = pltpu.make_async_copy(cotangent, pulls, io_sems.at[2])
    slope_load = pltpu.make_async_copy(slope, slopes, io_sems.at[3])
    start_all(first_loads + gate_loads[0] + gate_loads[1])
    pull_load.start()
    start_all(loads[0])
    start_all(loads[1])
    start_all(down_loads[0] + down_loads[1])
    slope_load.start()
    wait_all(first_loads)
    grad = act_pulls[...].astype(F32)
    for side in range(2):
        wait_all(gate_loads[side])
        grad += across(gate_pulls[:, lane_columns(where, side, 256)], gate[side])
    end_grad[...] = grad
    pull_load.wait()
    for side in range(2):
        wait_all(loads[side])
        end_grad[...] += across(pulls[:, lane_columns(where, side, 2048, GATE)], weight[side])
    branch[...] = end_grad[...].astype(BF16)
    down_bias[...] = jnp.sum(branch[...].astype(F32), axis=0, keepdims=True)
    wait_all(down_loads[0] + down_loads[1])
    slope_load.wait()
    stores = []
    for tile in range(6):
        span = slice(tile * 512, tile * 512 + 512)
        grad = across(branch[:, lane_columns(where, 0, 384)], down[0, span, :])
        grad += across(branch[:, lane_columns(where, 1, 384)], down[1, span, :])
        rounded = (slopes[:, span].astype(F32) * grad).astype(BF16)
        pre_grad[:, span] = rounded
        up_bias[:, span] = jnp.sum(rounded.astype(F32), axis=0, keepdims=True)
        stores.append(
            pltpu.make_async_copy(pre_grad.at[:, span], pre_out.at[:, span], pre_sems.at[tile])
        )
        stores[-1].start()
    wait_all(stores)


def head_backward(where, act_cotangent, gate_grad, cotangent, slope, arrays, gate_arrays, down_arrays):
    rows, wide = (TOKENS, WIDTH), (TOKENS, HIDDEN)
    return call(
        head_back_kernel,
        (where, act_cotangent, gate_grad, cotangent, slope, *arrays, *gate_arrays, *down_arrays),
        [SMEM, HBM, HBM, HBM, HBM] + [HBM] * 12,
        [
            (rows, F32, False),
            (rows, BF16, False),
            ((1, WIDTH), F32, False),
            ((1, HIDDEN), F32, False),
            (wide, BF16, True),
        ],
        lane_scratch(WIDTH, 2048)
        + lane_scratch(WIDTH, 256)
        + lane_scratch(HIDDEN, 384)
        + [
            pltpu.VMEM(rows, BF16),
            pltpu.VMEM((TOKENS, GATE), BF16),
            pltpu.VMEM((TOKENS, HEAD), BF16),
            pltpu.VMEM(wide, BF16),
            pltpu.VMEM(wide, BF16),
            pltpu.SemaphoreType.DMA((4,)),
            pltpu.SemaphoreType.DMA((6,)),
        ],
    )


def up_back_kernel(
    where, small, pre_grad, branch, act_turned, mlp_turned, mid, end_grad, *refs
):
    sources, outs, scratch = taken(refs, 4, 7)
    mid_grad, out_grad, terms, down_mine, down_theirs, up_mine, up_theirs = outs
    weight, sems, down_lane, down_sems, up_lane, up_sems, scratch = *scratch[:6], scratch[6:]
    pres, branches, acts, mlps, mids, ends, io_sems = scratch
    loads = [block_copies(where, "u", sources, UP_PART, weight, sems, side) for side in range(2)]
    pre_load = pltpu.make_async_copy(pre_grad, pres, io_sems.at[0])
    branch_load = pltpu.make_async_copy(branch, branches, io_sems.at[1])
    act_load = pltpu.make_async_copy(act_turned, acts, io_sems.at[2])
    mlp_load = pltpu.make_async_copy(mlp_turned, mlps, io_sems.at[3])
    norm_loads = [
        pltpu.make_async_copy(mid, mids, io_sems.at[4]),
        pltpu.make_async_copy(end_grad, ends, io_sems.at[5]),
    ]
    branch_load.start()
    act_load.start()
    pre_load.start()
    mlp_load.start()
    start_all(loads[0] + loads[1])
    start_all(norm_loads)
    branch_load.wait()
    act_load.wait()
    stores = []
    for side, out in ((1, down_theirs), (0, down_mine)):
        span = lane_columns(where, side, 384)
        for part in range(4):
            rows = slice(part * WIDTH, part * WIDTH + WIDTH)
            down_lane[side, rows, :] = times(acts[rows, :], branches[:, span]).astype(BF16)
        copies = term_copies(where, "down", down_lane, out, down_sems, side)
        start_all(copies)
        stores += copies
    pre_load.wait()
    mlp_load.wait()
    for side, out in ((1, up_theirs), (0, up_mine)):
        for tile in range(3):
            span = lane_columns(where, side, 1536, tile * 512, 512)
            up_lane[side, :, tile * 512 : tile * 512 + 512] = times(mlps[...], pres[:, span]).astype(
                BF16
            )
        copies = term_copies(where, "up", up_lane, out, up_sems, side)
        start_all(copies)
        stores += copies
    wait_all(loads[0] + loads[1])
    grad = across(pres[:, lane_columns(where, 0, 1536)], weight[0])
    grad += across(pres[:, lane_columns(where, 1, 1536)], weight[1])
    wait_all(norm_loads)
    pulled, gain_grad, shift_grad = norm_backward(mids[...], small[3:4, :], grad)
    pulled = pulled + ends[...]
    rounded = pulled.astype(BF16)
    mid_grad[...] = pulled
    out_grad[...] = rounded
    terms[...] = jnp.zeros_like(terms)
    terms[0:1, :] = jnp.sum(rounded.astype(F32), axis=0, keepdims=True)
    terms[1:2, :] = gain_grad
    terms[2:3, :] = shift_grad
    wait_all(stores)


def up_backward(
    where, small, pre_grad, branch, act_turned, mlp_turned, mid, end_grad, arrays
):
    rows = (TOKENS, WIDTH)
    return call(
        up_back_kernel,
        (where, small, pre_grad, branch, act_turned, mlp_turned, mid, end_grad, *arrays),
        [SMEM, VMEM] + [HBM] * 10,
        [
            (rows, F32, False),
            (rows, BF16, False),
            ((8, WIDTH), F32, False),
            ((16, 192, 384), BF16, True),
            ((16, 192, 384), BF16, True),
            ((16, 48, 1536), BF16, True),
            ((16, 48, 1536), BF16, True),
        ],
        lane_scratch(WIDTH, 1536)
        + lane_scratch(HIDDEN, 384)
        + lane_scratch(WIDTH, 1536)
        + [
            pltpu.VMEM((TOKENS, HIDDEN), BF16),
            pltpu.VMEM(rows, BF16),
            pltpu.VMEM((HIDDEN, TOKENS), BF16),
            pltpu.VMEM((WIDTH, TOKENS), BF16),
            pltpu.VMEM(rows, F32),
            pltpu.VMEM(rows, F32),
            pltpu.SemaphoreType.DMA((6,)),
        ],
    )


def attention_back_kernel(where, lengths, pad, out_grad, qkv, *refs):
    sources, outs, scratch = taken(refs, 4, 1)
    (qkv_grad,) = outs
    weight, sems, bias, mixed, turned, key_sum, value_sum = scratch
    loads = [block_copies(where, "u", sources, OUT_PART, weight, sems, side) for side in range(2)]
    start_all(loads[0] + loads[1])
    fill_bias(lengths, pad, bias)
    wait_all(loads[0] + loads[1])
    mixed[...] = (
        across(out_grad[:, lane_columns(where, 0, 384)], weight[0])
        + across(out_grad[:, lane_columns(where, 1, 384)], weight[1])
    ).astype(BF16)

    def pair(index, carry):
        first = index * 128
        columns = pl.ds(pl.multiple_of(first, 128), 128)
        keys_at = pl.ds(pl.multiple_of(first + WIDTH, 128), 128)
        values_at = pl.ds(pl.multiple_of(first + 2 * WIDTH, 128), 128)
        keys_turned = qkv[:, keys_at].T
        key_sum[...] = jnp.zeros_like(key_sum)
        value_sum[...] = jnp.zeros_like(value_sum)
        for block, (low, high) in enumerate(KEY_SPANS):
            span = slice(128 * block, 128 * block + 128)
            queries, grads = two_heads(qkv[span, columns]), two_heads(mixed[span, columns])
            scores = across(qkv[low:high, keys_at], queries)
            prob_grads = across(qkv[low:high, values_at], grads)
            allowed = bias[block, : high - low, :]
            probs, score_grads = [], []
            for head in range(2):
                part = slice(128 * head, 128 * head + 128)
                prob = probabilities(scores[:, part], allowed)
                pulled = prob * prob_grads[:, part]
                inner = jnp.sum(pulled, axis=0, keepdims=True)
                probs.append(prob.astype(BF16))
                score_grads.append((pulled - prob * inner).astype(BF16))
            score_grad = jnp.concatenate(score_grads, axis=1)
            key_sum[low:high, :] += times(score_grad, queries)
            value_sum[low:high, :] += times(jnp.concatenate(probs, axis=1), grads)
            turned[:, span] = head_rows_of(times(keys_turned[:, low:high], score_grad)) * score_scale
        qkv_grad[:, columns] = turned[...].T.astype(BF16)
        qkv_grad[:, keys_at] = (key_sum[...] * score_scale).astype(BF16)
        qkv_grad[:, values_at] = value_sum[...].astype(BF16)
        return carry

    lax.fori_loop(0, WIDTH // 128, pair, 0)


def attention_backward(where, lengths, pad, out_grad, qkv, arrays):
    return call(
        attention_back_kernel,
        (where, lengths, pad, out_grad, qkv, *arrays),
        [SMEM, SMEM, VMEM, VMEM, VMEM] + [HBM] * 4,
        [((TOKENS, 3 * WIDTH), BF16, False)],
        lane_scratch(WIDTH, 384)
        + [
            pltpu.VMEM((4, 384, 128), F32),
            pltpu.VMEM((TOKENS, WIDTH), BF16),
            pltpu.VMEM((128, TOKENS), F32),
            pltpu.VMEM((TOKENS, 128), F32),
            pltpu.VMEM((TOKENS, 128), F32),
        ],
    )[0]


def front_back_kernel(
    where, lead, small, terms, down_row, up_rows, head_rows,
    qkv_grad, patches, mid_grad, input_turned, attended_turned, out_grad, *refs
):
    sources, outs, scratch = taken(refs, 4, 3)
    patch_out, mine_out, theirs_out = outs
    weight, sems, lane, lane_sems, scratch = *scratch[:4], scratch[4:]
    pulls, state, mids, inputs, mixes, out_pulls, patch_grad, small_grad, io_sems = scratch
    loads = [block_copies(where, "q", sources, QKV_PART, weight, sems, side) for side in range(2)]
    pairs = (
        (qkv_grad, pulls), (patches, state), (mid_grad, mids),
        (input_turned, inputs), (attended_turned, mixes), (out_grad, out_pulls),
    )
    in_loads = [pltpu.make_async_copy(*pair, io_sems.at[at]) for at, pair in enumerate(pairs)]
    in_loads[0].start()
    start_all(loads[0] + loads[1])
    start_all(in_loads[1:])
    in_loads[0].wait()
    wait_all(loads[0] + loads[1])
    grad = across(pulls[:, lane_columns(where, 0, 1152)], weight[0])
    grad += across(pulls[:, lane_columns(where, 1, 1152)], weight[1])
    wait_all(in_loads[1:])
    pulled, gain_grad, shift_grad = norm_backward(
        state[...].astype(F32) + small[16:17, :], small[0:1, :], grad
    )
    pulled = pulled + mids[...]
    patch_grad[...] = pulled
    stores = [pltpu.make_async_copy(patch_grad, patch_out, io_sems.at[6])]
    stores[0].start()
    small_grad[0:1, :] = gain_grad
    small_grad[1:2, :] = shift_grad
    small_grad[2:5, :] = terms[0:3, :]
    small_grad[5:6, :] = down_row[...]
    small_grad[6:10, :] = up_rows[...]
    small_grad[10:16, :] = head_rows[...]
    places = lax.broadcasted_iota(jnp.int32, (LEADS, WIDTH), 0)
    lead_grad = jnp.sum(pulled, axis=0, keepdims=True)
    small_grad[16:32, :] = jnp.where(places == lead[0], lead_grad, 0.0)
    for side, out in ((1, theirs_out), (0, mine_out)):
        for tile in range(3):
            span = lane_columns(where, side, 1152, tile * 384, 384)
            lane[side, :, tile * 384 : tile * 384 + 384] = times(inputs[...], pulls[:, span]).astype(
                BF16
            )
        span = lane_columns(where, side, 384)
        lane[side, :, 1152:1536] = times(mixes[...], out_pulls[:, span]).astype(BF16)
        rows = small_grad[pl.ds(pl.multiple_of((where[0] ^ side) * 16, 16), 16), :]
        rows = jnp.concatenate([rows, jnp.zeros((112, WIDTH), F32)], axis=0)
        lane[side, :, 1536:1664] = rows.T.astype(BF16)
        copies = term_copies(where, "front", lane, out, lane_sems, side)
        start_all(copies)
        stores += copies
    wait_all(stores)


def front_backward(
    where, lead, small, terms, down_row, up_rows, head_rows,
    qkv_grad, patches, mid_grad, input_turned, attended_turned, out_grad, arrays,
):
    rows, columns = (TOKENS, WIDTH), (WIDTH, TOKENS)
    return call(
        front_back_kernel,
        (
            where, lead, small, terms, down_row, up_rows, head_rows,
            qkv_grad, patches, mid_grad, input_turned, attended_turned, out_grad, *arrays,
        ),
        [SMEM, SMEM] + [VMEM] * 5 + [HBM] * 10,
        [(rows, F32, True), ((16, 48, 1664), BF16, True), ((16, 48, 1664), BF16, True)],
        lane_scratch(WIDTH, 1152)
        + lane_scratch(WIDTH, 1664)
        + [
            pltpu.VMEM((TOKENS, 3 * WIDTH), BF16),
            pltpu.VMEM(rows, BF16),
            pltpu.VMEM(rows, F32),
            pltpu.VMEM(columns, BF16),
            pltpu.VMEM(columns, BF16),
            pltpu.VMEM(rows, BF16),
            pltpu.VMEM(rows, F32),
            pltpu.VMEM((32, WIDTH), F32),
            pltpu.SemaphoreType.DMA((7,)),
        ],
    )


def rows_of(vector, count):
    return vector.reshape(32, count, 24).transpose(1, 0, 2).reshape(count, WIDTH)


def vector_of(rows):
    count = rows.shape[0]
    return rows.reshape(count, 32, 24).transpose(1, 0, 2).reshape(1, count * WIDTH)


def shards(
    patches,
    lead_index,
    window_lengths,
    pad_mask,
    lead_table,
    attn_gain,
    attn_shift,
    qkv_weight,
    out_weight,
    out_bias,
    mlp_gain,
    mlp_shift,
    up_weight,
    up_bias,
    down_weight,
    down_bias,
    head_weight,
    head_bias,
    act_cotangent,
    head_cotangent,
):
    core, where = whereabouts()
    vectors = [attn_gain, attn_shift, out_bias, mlp_gain, mlp_shift, down_bias]
    small = jnp.concatenate(
        [vector[None] for vector in vectors]
        + [up_bias.reshape(4, 24), head_bias.reshape(6, 24), lead_table, jnp.zeros((96, 24), BF16)],
        axis=0,
    ).T
    pad = pad_mask[:, None]
    cotangent_sum = jnp.sum(head_cotangent[:, GATE:].astype(F32), axis=0, keepdims=True)

    q = lane_chunk([qkv_weight], [small], core)
    u = lane_chunk([up_weight, out_weight, head_weight[:, :GATE]], [], core)
    d = lane_chunk([down_weight], [], core)
    h = lane_chunk([head_weight[:, GATE:]], [], core)
    orders = ORDERS

    q, u, d = [doubled(held, orders[name][0]) for name, held in (("q", q), ("u", u), ("d", d))]
    h = doubled(h, orders["h"][0])
    q = doubled(q, orders["q"][1])
    u = doubled(u, orders["u"][1])
    d = doubled(d, orders["d"][1])
    h = doubled(h, orders["h"][1])
    d = doubled(d, orders["d"][2])
    q = doubled(q, orders["q"][2])
    first = both_lanes(q, exchange(q, orders["q"][3]))
    input_turned, qkv, small_rows = front_forward(
        after(where, d, h, u), lead_index, patches, first
    )
    u = doubled(after(u, qkv), orders["u"][2])
    d_rest = exchange(d, orders["d"][3])
    h = doubled(h, orders["h"][2])
    attended, attended_turned = attention_forward(
        after(where, u), window_lengths, pad, qkv
    )
    second = both_lanes(u, exchange(u, orders["u"][3]))
    up_bias_row, head_bias_row = vector_of(small_rows[6:10]), vector_of(small_rows[10:16])
    mid_state, mlp_turned, act_rows, act_turned, slope = up_forward(
        after(where, h), attended, patches, small_rows, up_bias_row, second
    )
    down = both_lanes(d, d_rest)
    head = both_lanes(h, exchange(h, orders["h"][3]))
    outputs, gate_out, gate_grad, gate_bias_sum, mine_h, theirs_h = down_forward(
        where, act_rows, mid_state, small_rows, head_cotangent, head_bias_row, down, second
    )
    got_h = exchange(theirs_h, SIBLING)
    end_grad, branch_grad, down_bias_sum, up_bias_sum, pre_grad = head_backward(
        after(where, theirs_h), act_cotangent, gate_grad, head_cotangent, slope, head, second, down
    )
    keep_h, send_h = folded(mine_h, after(got_h, pre_grad))
    got_h = exchange(send_h, orders["head"][3])
    mid_grad, out_grad, terms, mine_d, theirs_d, mine_u, theirs_u = up_backward(
        after(where, send_h), small_rows, pre_grad, branch_grad, act_turned, mlp_turned,
        mid_state, end_grad, second,
    )
    got_d, got_u = exchange(theirs_d, SIBLING), exchange(theirs_u, SIBLING)
    keep_d, send_d = folded(mine_d, got_d)
    got_d = exchange(send_d, orders["down"][3])
    keep_u, send_u = folded(mine_u, got_u)
    got_u = exchange(send_u, orders["up"][3])
    keep_h, send_h = folded(keep_h, after(got_h, out_grad))
    got_h = exchange(send_h, orders["head"][2])
    qkv_grad = attention_backward(
        after(where, send_h, send_d, send_u), window_lengths, pad, out_grad, qkv, second
    )
    keep_h, send_h = folded(keep_h, after(got_h, qkv_grad))
    got_h = exchange(send_h, orders["head"][1])
    keep_d, send_d = folded(keep_d, after(got_d, qkv_grad))
    got_d = exchange(send_d, orders["down"][2])
    head_rows = rows_of(jnp.concatenate([gate_bias_sum, cotangent_sum], axis=1), 6)
    patch_grad, mine_f, theirs_f = front_backward(
        after(where, send_h, send_d), lead_index, small_rows, terms, down_bias_sum,
        rows_of(up_bias_sum, 4), head_rows, qkv_grad, patches, mid_grad, input_turned,
        attended_turned, out_grad, first,
    )
    got_f = exchange(theirs_f, SIBLING)
    keep_f, send_f = folded(mine_f, got_f)
    got_f = exchange(send_f, orders["front"][3])
    keep_u, send_u = folded(keep_u, after(got_u, patch_grad))
    got_u = exchange(send_u, orders["up"][2])
    keep_h, send_h = folded(keep_h, after(got_h, patch_grad))
    got_h = exchange(send_h, orders["head"][0])
    keep_d, send_d = folded(keep_d, after(got_d, patch_grad))
    got_d = exchange(send_d, orders["down"][1])
    head_out = head_forward(
        after(where, send_f, send_u, send_d), outputs, gate_out, head_bias_row, head
    )
    keep_f, send_f = folded(keep_f, after(got_f, head_out))
    got_f = exchange(send_f, orders["front"][2])
    keep_u, send_u = folded(keep_u, after(got_u, head_out))
    got_u = exchange(send_u, orders["up"][1])
    keep_d, send_d = folded(keep_d, after(got_d, head_out))
    got_d = exchange(send_d, orders["down"][0])
    gate_sum, rest_sum = finished(keep_h, after(got_h, head_out), core, (256, 2048))
    keep_f, send_f = folded(keep_f, got_f)
    got_f = exchange(send_f, orders["front"][1])
    keep_u, send_u = folded(keep_u, got_u)
    got_u = exchange(send_u, orders["up"][0])
    (down_sum,) = finished(keep_d, got_d, core, (384,))
    keep_f, send_f = folded(keep_f, got_f)
    got_f = exchange(send_f, orders["front"][0])
    (up_sum,) = finished(keep_u, got_u, core, (1536,))
    qkv_sum, out_sum, small_sum = finished(keep_f, got_f, core, (1152, 384, 128))
    small_sum = small_sum.T
    return (
        outputs,
        head_out,
        patch_grad,
        small_sum[128:144],
        small_sum[0],
        small_sum[1],
        qkv_sum,
        out_sum,
        small_sum[2],
        small_sum[3],
        small_sum[4],
        up_sum,
        small_sum[6:10].reshape(96),
        down_sum,
        small_sum[5],
        jnp.concatenate([gate_sum, rest_sum], axis=1),
        small_sum[10:16].reshape(144),
    )


def plain_shards(
    patches,
    lead_index,
    window_lengths,
    pad_mask,
    lead_table,
    attn_gain,
    attn_shift,
    qkv_weight,
    out_weight,
    out_bias,
    mlp_gain,
    mlp_shift,
    up_weight,
    up_bias,
    down_weight,
    down_bias,
    head_weight,
    head_bias,
    act_cotangent,
    head_cotangent,
):
    front = (
        lax.all_gather(lead_table, ("dp", "fsdp"), axis=1, tiled=True),
        lax.all_gather(attn_gain, ("dp", "fsdp"), axis=0, tiled=True),
        lax.all_gather(attn_shift, ("dp", "fsdp"), axis=0, tiled=True),
        lax.all_gather(qkv_weight, ("dp", "fsdp"), axis=0, tiled=True),
        lax.all_gather(out_weight, ("dp", "fsdp"), axis=0, tiled=True),
        lax.all_gather(out_bias, ("dp", "fsdp"), axis=0, tiled=True),
    )
    rear = (
        lax.all_gather(mlp_gain, ("dp", "fsdp"), axis=0, tiled=True),
        lax.all_gather(mlp_shift, ("dp", "fsdp"), axis=0, tiled=True),
        lax.all_gather(up_weight, ("dp", "fsdp"), axis=0, tiled=True),
        lax.all_gather(up_bias, ("dp", "fsdp"), axis=0, tiled=True),
        lax.all_gather(down_weight, ("dp", "fsdp"), axis=0, tiled=True),
        lax.all_gather(down_bias, ("dp", "fsdp"), axis=0, tiled=True),
        lax.all_gather(head_weight, ("dp", "fsdp"), axis=0, tiled=True),
        lax.all_gather(head_bias, ("dp", "fsdp"), axis=0, tiled=True),
    )
    table_full, gain_one, shift_one, qkv_full, out_full, out_bias_full = front
    (
        gain_two,
        shift_two,
        up_full,
        up_bias_full,
        down_full,
        down_bias_full,
        head_full,
        head_bias_full,
    ) = rear
    token_rows, width = patches.shape
    head_dim = width // HEADS
    block_rows = min(512, token_rows)
    block_count = token_rows // block_rows
    ends = jnp.cumsum(window_lengths[0])
    positions = jnp.arange(token_rows, dtype=jnp.int32)
    window = jnp.sum((positions[:, None] >= ends[None, :]).astype(jnp.int32), axis=1)
    lead_hot = (jnp.arange(LEADS, dtype=jnp.int32) == lead_index[0]).astype(jnp.float32)
    lead_row = jnp.sum(lead_hot[:, None] * table_full.astype(jnp.float32), axis=0)
    start_state = patches.astype(jnp.float32) + lead_row[None, :]
    normed_one, pull_one = jax.vjp(
        layer_norm, start_state, gain_one.astype(jnp.float32), shift_one.astype(jnp.float32)
    )
    attn_input = normed_one.astype(jnp.bfloat16)
    qkv_rows = jnp.dot(attn_input, qkv_full, preferred_element_type=jnp.float32).astype(
        jnp.bfloat16
    )
    queries = qkv_rows[:, :width].reshape(block_count, block_rows, HEADS, head_dim)
    keys = qkv_rows[:, width : 2 * width].reshape(token_rows, HEADS, head_dim)
    values = qkv_rows[:, 2 * width :].reshape(token_rows, HEADS, head_dim)
    query_windows = window.reshape(block_count, block_rows)
    block_starts = jnp.arange(block_count, dtype=jnp.int32) * block_rows

    def block_scores(query_block, window_block, block_start):
        scores = (
            jnp.einsum("qhd,khd->hqk", query_block, keys, preferred_element_type=jnp.float32)
            * score_scale
        )
        allowed = allowed_keys(window_block, window, pad_mask, block_start)
        return jnp.where(allowed[None], scores, -1e30)

    def forward_block(inputs):
        query_block, window_block, block_start = inputs
        masked = block_scores(query_block, window_block, block_start)
        largest = jnp.max(masked, axis=-1, keepdims=True)
        raised = jnp.exp(masked - largest)
        total = jnp.sum(raised, axis=-1, keepdims=True)
        probs = (raised / total).astype(jnp.bfloat16)
        mixed = jnp.einsum("hqk,khd->qhd", probs, values, preferred_element_type=jnp.float32)
        return (
            mixed.reshape(block_rows, width).astype(jnp.bfloat16),
            (largest + jnp.log(total))[:, :, 0],
        )

    mixed_blocks, log_totals = lax.map(forward_block, (queries, query_windows, block_starts))
    attended = mixed_blocks.reshape(token_rows, width)
    mid_state = (
        start_state
        + jnp.dot(attended, out_full, preferred_element_type=jnp.float32)
        + out_bias_full.astype(jnp.float32)
    )
    normed_two, pull_two = jax.vjp(
        layer_norm, mid_state, gain_two.astype(jnp.float32), shift_two.astype(jnp.float32)
    )
    mlp_input = normed_two.astype(jnp.bfloat16)
    pre_act = jnp.dot(mlp_input, up_full, preferred_element_type=jnp.float32) + up_bias_full.astype(
        jnp.float32
    )
    activated, pull_act = jax.vjp(gelu_exact, pre_act)
    act_rows = activated.astype(jnp.bfloat16)
    end_state = (
        mid_state
        + jnp.dot(act_rows, down_full, preferred_element_type=jnp.float32)
        + down_bias_full.astype(jnp.float32)
    )
    outputs = end_state.astype(jnp.bfloat16)
    logits = jnp.dot(
        outputs, head_full, preferred_element_type=jnp.float32
    ) + head_bias_full.astype(jnp.float32)
    head_out, pull_head = jax.vjp(partial(expert_softmax, experts=EXPERTS, pixels=PIX), logits)
    up_back, down_back, head_back = (
        lax.all_gather(up_weight, ("dp", "fsdp"), axis=0, tiled=True),
        lax.all_gather(down_weight, ("dp", "fsdp"), axis=0, tiled=True),
        lax.all_gather(head_weight, ("dp", "fsdp"), axis=0, tiled=True),
    )
    qkv_back, out_back = (
        lax.all_gather(qkv_weight, ("dp", "fsdp"), axis=0, tiled=True),
        lax.all_gather(out_weight, ("dp", "fsdp"), axis=0, tiled=True),
    )
    logit_grad = pull_head(head_cotangent.astype(jnp.float32))[0].astype(jnp.bfloat16)
    head_bias_term = jnp.sum(logit_grad.astype(jnp.float32), axis=0)
    head_term = jnp.einsum("td,tn->dn", outputs, logit_grad, preferred_element_type=jnp.float32)
    end_grad = act_cotangent.astype(jnp.float32) + jnp.einsum(
        "tn,dn->td", logit_grad, head_back, preferred_element_type=jnp.float32
    )
    branch_grad = end_grad.astype(jnp.bfloat16)
    down_bias_term = jnp.sum(branch_grad.astype(jnp.float32), axis=0)
    down_term = jnp.einsum("tf,td->fd", act_rows, branch_grad, preferred_element_type=jnp.float32)
    act_grad = jnp.einsum("td,fd->tf", branch_grad, down_back, preferred_element_type=jnp.float32)
    pre_grad = pull_act(act_grad)[0].astype(jnp.bfloat16)
    up_bias_term = jnp.sum(pre_grad.astype(jnp.float32), axis=0)
    up_term = jnp.einsum("td,tf->df", mlp_input, pre_grad, preferred_element_type=jnp.float32)
    normed_two_grad = jnp.einsum("tf,df->td", pre_grad, up_back, preferred_element_type=jnp.float32)
    state_grad_two, gain_two_term, shift_two_term = pull_two(normed_two_grad)
    (
        gain_part,
        shift_part,
        up_part,
        up_bias_part,
        down_part,
        down_bias_part,
        head_part,
        head_bias_part,
    ) = (
        lax.psum_scatter(
            gain_two_term.astype(jnp.bfloat16), "dp", scatter_dimension=0, tiled=True
        ).astype(jnp.float32),
        lax.psum_scatter(
            shift_two_term.astype(jnp.bfloat16), "dp", scatter_dimension=0, tiled=True
        ).astype(jnp.float32),
        lax.psum_scatter(
            up_term.astype(jnp.bfloat16), "dp", scatter_dimension=0, tiled=True
        ).astype(jnp.float32),
        lax.psum_scatter(
            up_bias_term.astype(jnp.bfloat16), "dp", scatter_dimension=0, tiled=True
        ).astype(jnp.float32),
        lax.psum_scatter(
            down_term.astype(jnp.bfloat16), "dp", scatter_dimension=0, tiled=True
        ).astype(jnp.float32),
        lax.psum_scatter(
            down_bias_term.astype(jnp.bfloat16), "dp", scatter_dimension=0, tiled=True
        ).astype(jnp.float32),
        lax.psum_scatter(
            head_term.astype(jnp.bfloat16), "dp", scatter_dimension=0, tiled=True
        ).astype(jnp.float32),
        lax.psum_scatter(
            head_bias_term.astype(jnp.bfloat16), "dp", scatter_dimension=0, tiled=True
        ).astype(jnp.float32),
    )
    rear_grads = (
        lax.psum_scatter(gain_part, "fsdp", scatter_dimension=0, tiled=True),
        lax.psum_scatter(shift_part, "fsdp", scatter_dimension=0, tiled=True),
        lax.psum_scatter(up_part, "fsdp", scatter_dimension=0, tiled=True),
        lax.psum_scatter(up_bias_part, "fsdp", scatter_dimension=0, tiled=True),
        lax.psum_scatter(down_part, "fsdp", scatter_dimension=0, tiled=True),
        lax.psum_scatter(down_bias_part, "fsdp", scatter_dimension=0, tiled=True),
        lax.psum_scatter(head_part, "fsdp", scatter_dimension=0, tiled=True),
        lax.psum_scatter(head_bias_part, "fsdp", scatter_dimension=0, tiled=True),
    )
    mid_grad = end_grad + state_grad_two
    out_grad = mid_grad.astype(jnp.bfloat16)
    out_bias_term = jnp.sum(out_grad.astype(jnp.float32), axis=0)
    out_term = jnp.einsum("td,te->de", attended, out_grad, preferred_element_type=jnp.float32)
    mixed_grad = jnp.einsum(
        "te,de->td", out_grad, out_back, preferred_element_type=jnp.float32
    ).astype(jnp.bfloat16)
    grad_blocks = mixed_grad.reshape(block_count, block_rows, HEADS, head_dim)

    def backward_block(carry, inputs):
        key_sum, value_sum = carry
        query_block, grad_block, window_block, total_block, block_start = inputs
        masked = block_scores(query_block, window_block, block_start)
        probs = jnp.exp(masked - total_block[:, :, None])
        prob_grad = jnp.einsum(
            "qhd,khd->hqk", grad_block, values, preferred_element_type=jnp.float32
        )
        inner = jnp.sum(probs * prob_grad, axis=-1, keepdims=True)
        score_grad = (probs * (prob_grad - inner)).astype(jnp.bfloat16)
        query_grad = (
            jnp.einsum("hqk,khd->qhd", score_grad, keys, preferred_element_type=jnp.float32)
            * score_scale
        )
        key_sum = (
            key_sum
            + jnp.einsum(
                "hqk,qhd->khd", score_grad, query_block, preferred_element_type=jnp.float32
            )
            * score_scale
        )
        value_sum = value_sum + jnp.einsum(
            "hqk,qhd->khd",
            probs.astype(jnp.bfloat16),
            grad_block,
            preferred_element_type=jnp.float32,
        )
        return ((key_sum, value_sum), query_grad.reshape(block_rows, width))

    zero_keys = jnp.zeros((token_rows, HEADS, head_dim), jnp.float32)
    (key_grad, value_grad), query_grads = lax.scan(
        backward_block,
        (zero_keys, zero_keys),
        (queries, grad_blocks, query_windows, log_totals, block_starts),
    )
    qkv_grad = jnp.concatenate(
        [
            query_grads.reshape(token_rows, width),
            key_grad.reshape(token_rows, width),
            value_grad.reshape(token_rows, width),
        ],
        axis=1,
    ).astype(jnp.bfloat16)
    qkv_term = jnp.einsum("td,te->de", attn_input, qkv_grad, preferred_element_type=jnp.float32)
    normed_one_grad = jnp.einsum(
        "te,de->td", qkv_grad, qkv_back, preferred_element_type=jnp.float32
    )
    state_grad_one, gain_one_term, shift_one_term = pull_one(normed_one_grad)
    patch_grad = mid_grad + state_grad_one
    lead_term = lead_hot[:, None] * jnp.sum(patch_grad, axis=0)[None, :]
    lead_part, gain_one_part, shift_one_part, qkv_part, out_part, out_bias_part = (
        lax.psum_scatter(
            lead_term.astype(jnp.bfloat16), "dp", scatter_dimension=1, tiled=True
        ).astype(jnp.float32),
        lax.psum_scatter(
            gain_one_term.astype(jnp.bfloat16), "dp", scatter_dimension=0, tiled=True
        ).astype(jnp.float32),
        lax.psum_scatter(
            shift_one_term.astype(jnp.bfloat16), "dp", scatter_dimension=0, tiled=True
        ).astype(jnp.float32),
        lax.psum_scatter(
            qkv_term.astype(jnp.bfloat16), "dp", scatter_dimension=0, tiled=True
        ).astype(jnp.float32),
        lax.psum_scatter(
            out_term.astype(jnp.bfloat16), "dp", scatter_dimension=0, tiled=True
        ).astype(jnp.float32),
        lax.psum_scatter(
            out_bias_term.astype(jnp.bfloat16), "dp", scatter_dimension=0, tiled=True
        ).astype(jnp.float32),
    )
    front_grads = (
        lax.psum_scatter(lead_part, "fsdp", scatter_dimension=1, tiled=True),
        lax.psum_scatter(gain_one_part, "fsdp", scatter_dimension=0, tiled=True),
        lax.psum_scatter(shift_one_part, "fsdp", scatter_dimension=0, tiled=True),
        lax.psum_scatter(qkv_part, "fsdp", scatter_dimension=0, tiled=True),
        lax.psum_scatter(out_part, "fsdp", scatter_dimension=0, tiled=True),
        lax.psum_scatter(out_bias_part, "fsdp", scatter_dimension=0, tiled=True),
    )
    return (
        outputs,
        head_out,
        patch_grad,
        front_grads[0],
        front_grads[1],
        front_grads[2],
        front_grads[3],
        front_grads[4],
        front_grads[5],
        rear_grads[0],
        rear_grads[1],
        rear_grads[2],
        rear_grads[3],
        rear_grads[4],
        rear_grads[5],
        rear_grads[6],
        rear_grads[7],
    )


def solution(mesh):
    in_specs = (
        P(("dp", "fsdp"), None),
        P(("dp", "fsdp")),
        P(("dp", "fsdp"), None),
        P(("dp", "fsdp")),
        P(None, ("dp", "fsdp")),
        P(("dp", "fsdp")),
        P(("dp", "fsdp")),
        P(("dp", "fsdp"), None),
        P(("dp", "fsdp"), None),
        P(("dp", "fsdp")),
        P(("dp", "fsdp")),
        P(("dp", "fsdp")),
        P(("dp", "fsdp"), None),
        P(("dp", "fsdp")),
        P(("dp", "fsdp"), None),
        P(("dp", "fsdp")),
        P(("dp", "fsdp"), None),
        P(("dp", "fsdp")),
        P(("dp", "fsdp"), None),
        P(("dp", "fsdp"), None),
    )
    out_specs = (
        P(("dp", "fsdp"), None),
        P(("dp", "fsdp"), None),
        P(("dp", "fsdp"), None),
        P(None, ("dp", "fsdp")),
        P(("dp", "fsdp")),
        P(("dp", "fsdp")),
        P(("dp", "fsdp"), None),
        P(("dp", "fsdp"), None),
        P(("dp", "fsdp")),
        P(("dp", "fsdp")),
        P(("dp", "fsdp")),
        P(("dp", "fsdp"), None),
        P(("dp", "fsdp")),
        P(("dp", "fsdp"), None),
        P(("dp", "fsdp")),
        P(("dp", "fsdp"), None),
        P(("dp", "fsdp")),
    )
    body = shards if dict(mesh.shape) == {"dp": 4, "fsdp": 8} else plain_shards
    return jax.shard_map(body, mesh=mesh, in_specs=in_specs, out_specs=out_specs, check_vma=False)
```

```python
from functools import partial

import jax
import jax.numpy as jnp
from jax import lax
from jax.experimental import pallas as pl
from jax.experimental.pallas import tpu as pltpu
from jax.sharding import PartitionSpec as P

HEADS = 12
PIX = 64
EXPERTS = 3
LEADS = 16


norm_epsilon = 1e-05
score_scale = 0.125


def layer_norm(hidden, norm_gain, norm_shift):
    average = jnp.mean(hidden, axis=-1, keepdims=True)
    centered = hidden - average
    variance = jnp.mean(centered * centered, axis=-1, keepdims=True)
    return centered * lax.rsqrt(variance + norm_epsilon) * norm_gain + norm_shift


def gelu_exact(values):
    return 0.5 * values * (1.0 + lax.erf(values * 0.7071067811865476))


def expert_softmax(logits, experts, pixels):
    gate_part = logits[:, : experts * pixels].reshape(logits.shape[0], experts, pixels)
    largest = jnp.max(gate_part, axis=1, keepdims=True)
    raised = jnp.exp(gate_part - largest)
    shares = raised / jnp.sum(raised, axis=1, keepdims=True)
    return jnp.concatenate(
        [shares.reshape(logits.shape[0], experts * pixels), logits[:, experts * pixels :]], axis=1
    )


def allowed_keys(query_window, key_window, key_valid, query_start):
    query_place = query_start + jnp.arange(query_window.shape[0], dtype=jnp.int32)
    key_place = jnp.arange(key_window.shape[0], dtype=jnp.int32)
    same_window = query_window[:, None] == key_window[None, :]
    usable = (key_valid[None, :] > 0) | (query_place[:, None] == key_place[None, :])
    return same_window & usable


AXES = ("dp", "fsdp")
FAR_Z, NEAR_Z, FIRST, SECOND, SIBLING = (4, 4), (2, 2), (8, 16), (16, 8), (1, 1)
ORDERS = {
    "q": (FAR_Z, FIRST, SECOND, NEAR_Z),
    "u": (NEAR_Z, FAR_Z, FIRST, SECOND),
    "d": (FIRST, FAR_Z, NEAR_Z, SECOND),
    "h": (FAR_Z, FIRST, SECOND, NEAR_Z),
    "head": (FAR_Z, NEAR_Z, FIRST, SECOND),
    "down": (FAR_Z, NEAR_Z, FIRST, SECOND),
    "up": (FAR_Z, FIRST, SECOND, NEAR_Z),
    "front": (FAR_Z, NEAR_Z, FIRST, SECOND),
}
WIDTH = 768
HIDDEN = 3072
HEAD = 4608
TOKENS = 512
GATE = 512
F32 = jnp.float32
BF16 = jnp.bfloat16
HBM = pl.BlockSpec(memory_space=pltpu.HBM)
SMEM = pl.BlockSpec(memory_space=pltpu.SMEM)
VMEM = pl.BlockSpec(memory_space=pltpu.VMEM)
QKV_PART, SMALL_PART = (0, 1152), (1152, 128)
UP_PART, OUT_PART, GATE_PART = (0, 1536), (1536, 384), (1920, 256)
DOWN_PART, HEAD_PART = (0, 384), (0, 2048)


def chip_masks(order, lane):
    masks = []
    for place in range(16):
        mask = 0
        for step in range(4):
            if place >> step & 1:
                mask ^= order[step][lane]
        masks.append(mask >> 1)
    return masks


def table_start(group, side):
    return 1 + 32 * list(ORDERS).index(group) + 16 * side


def exchange(array, masks):
    return lax.ppermute(array, AXES, [(d, d ^ masks[d & 1]) for d in range(32)])


def whereabouts():
    device = lax.axis_index("dp") * 8 + lax.axis_index("fsdp")
    core, chip = device % 2, device // 2
    tables = [chip_masks(order, 0) + chip_masks(order, 1) for order in ORDERS.values()]
    swapped = [chip_masks(order, 1) + chip_masks(order, 0) for order in ORDERS.values()]
    places = jnp.where(core == 0, jnp.array(tables, jnp.int32), jnp.array(swapped, jnp.int32))
    places = (places ^ chip).reshape(32 * len(ORDERS))
    return core, jnp.concatenate([core[None].astype(jnp.int32), places])


def after(value, *marks):
    return lax.optimization_barrier((value, marks))[0]


def in_core_order(core, mine, theirs, axis):
    return jnp.where(
        core == 0,
        jnp.concatenate([mine, theirs], axis=axis),
        jnp.concatenate([theirs, mine], axis=axis),
    )


def pack_kernel(core, qkv, out, up, down, head, table, *refs):
    vectors, (up_bias, head_bias), refs = refs[:6], refs[6:8], refs[8:]
    outs, (rows,) = refs[:8], refs[8:]
    rows[...] = jnp.zeros_like(rows)
    for index, vector in enumerate(vectors):
        rows[index : index + 1, :24] = vector[...].astype(F32)
    for index in range(4):
        rows[6 + index : 7 + index, :24] = up_bias[:, 24 * index : 24 * index + 24].astype(F32)
    for index in range(6):
        rows[10 + index : 11 + index, :24] = head_bias[:, 24 * index : 24 * index + 24].astype(F32)
    rows[16:32, :24] = table[...].astype(F32)
    small = rows[...].T[:24].astype(BF16)
    for side in range(2):
        q, u, d, h = outs[4 * side : 4 * side + 4]
        q[:, :1152] = qkv[:, lane_columns(core, side, 1152)]
        q[:, 1152:] = small
        u[:, :1536] = up[:, lane_columns(core, side, 1536)]
        u[:, 1536:1920] = out[:, lane_columns(core, side, 384)]
        u[:, 1920:] = head[:, lane_columns(core, side, 256)]
        d[...] = down[:, lane_columns(core, side, 384)]
        h[...] = head[:, lane_columns(core, side, 2048, GATE)]


def packed(core, weights, table, vectors):
    shapes = [(24, 1280), (24, 2176), (96, 384), (24, 2048)] * 2
    return call(
        pack_kernel,
        (core.reshape(1), *weights, table, *[vector[None] for vector in vectors]),
        [SMEM] + [VMEM] * 14,
        [(shape, BF16, False) for shape in shapes],
        [pltpu.VMEM((128, 128), F32)],
    )


def doubled(held, masks):
    return jnp.concatenate([held, exchange(held, masks)], axis=0)


def both_lanes(*arrays):
    return arrays + tuple(exchange(array, SIBLING) for array in arrays)


def total(first, second):
    return first.astype(F32) + second.astype(F32)


def folded(keep, got, start=0):
    half = got.shape[0] // 2
    send = total(keep[half:], got[half:]).astype(BF16)
    return total(keep[:half], got[:half]).astype(BF16), send


def finished(keep, got, core, widths):
    block = total(keep, got)[0]
    rows = block.shape[0] // 2
    upper, lower = block[:rows], block[rows:]
    mine = jnp.where(core == 0, upper, lower)
    theirs = jnp.where(core == 0, lower, upper).astype(BF16)
    other = exchange(theirs, SIBLING).astype(F32)
    pieces, start = [], 0
    for width in widths:
        span = slice(start, start + width)
        pieces.append(in_core_order(core, mine[:, span], other[:, span], 1))
        start += width
    return pieces


def across(first, second):
    return lax.dot_general(first, second, (((1,), (1,)), ((), ())), preferred_element_type=F32)


def times(first, second):
    return jnp.dot(first, second, preferred_element_type=F32)


def lane_columns(where, side, stride, first=0, width=None):
    return pl.ds(pl.multiple_of(first + (where[0] ^ side) * stride, 128), width or stride)


def block_copies(where, group, sources, part, target, sems, side, first=0):
    start, width = part
    rows = sources[0].shape[1]
    half = len(sources) // 2
    count = 16 // half
    copies = []
    for place in range(16):
        row = pl.multiple_of(where[table_start(group, side) + place] * rows, rows)
        copies.append(
            pltpu.make_async_copy(
                sources[half * side + place // count].at[place % count, :, pl.ds(start, width)],
                target.at[pl.ds(row, rows), lane_columns(where, side, width, first)],
                sems.at[side, place],
            )
        )
    return copies


def term_copies(where, group, lane, out, sems, side):
    rows = out.shape[1]
    copies = []
    for place in range(16):
        row = pl.multiple_of(where[table_start(group, side) + place] * rows, rows)
        copies.append(
            pltpu.make_async_copy(lane.at[side, pl.ds(row, rows), :], out.at[place], sems.at[side, place])
        )
    return copies


def start_all(copies):
    for copy in copies:
        copy.start()


def wait_all(copies):
    for copy in copies:
        copy.wait()


def mean_and_scale(hidden):
    average = jnp.mean(hidden, axis=1, keepdims=True)
    centered = hidden - average
    variance = jnp.mean(centered * centered, axis=1, keepdims=True)
    return centered, lax.rsqrt(variance + norm_epsilon)


def norm_backward(hidden, gain, upstream):
    centered, scale = mean_and_scale(hidden)
    normed = centered * scale
    gain_grad = jnp.sum(upstream * normed, axis=0, keepdims=True)
    shift_grad = jnp.sum(upstream, axis=0, keepdims=True)
    scaled = upstream * gain
    first = jnp.mean(scaled, axis=1, keepdims=True)
    second = jnp.mean(scaled * normed, axis=1, keepdims=True)
    return scale * (scaled - first - normed * second), gain_grad, shift_grad


def call(kernel, operands, in_specs, outs, scratch):
    return pl.pallas_call(
        kernel,
        out_shape=[jax.ShapeDtypeStruct(shape, kind) for shape, kind, _ in outs],
        in_specs=in_specs,
        out_specs=[HBM if copied else VMEM for _, _, copied in outs],
        scratch_shapes=scratch,
        compiler_params=pltpu.CompilerParams(vmem_limit_bytes=56 * 1024 * 1024),
        cost_estimate=pl.CostEstimate(flops=2 * 10**12, bytes_accessed=10**10, transcendentals=0),
    )(*operands)


def lane_scratch(rows, width):
    return [pltpu.VMEM((2, rows, width), BF16), pltpu.SemaphoreType.DMA((2, 16))]


def weight_scratch(rows, width):
    return [pltpu.VMEM((rows, width), BF16), pltpu.SemaphoreType.DMA((2, 16))]


def taken(refs, *counts):
    groups = []
    for count in counts:
        groups.append(refs[:count])
        refs = refs[count:]
    return *groups, refs


def front_kernel(where, lead, patches, *refs):
    sources, outs, scratch = taken(refs, 4, 3)
    turned_out, qkv_out, small = outs
    weight, sems, smalls, small_sems, state, rows, turned, qkv, io_sems = scratch
    loads = [block_copies(where, "q", sources, QKV_PART, weight, sems, side) for side in range(2)]
    small_loads = []
    for place in range(16):
        row = pl.multiple_of(where[table_start("q", 0) + place] * 48, 48)
        small_loads.append(
            pltpu.make_async_copy(
                sources[place // 8].at[place % 8, :, pl.ds(*SMALL_PART)],
                smalls.at[pl.ds(row, 48), :],
                small_sems.at[place],
            )
        )
    state_load = pltpu.make_async_copy(patches, state, io_sems.at[0])
    start_all(small_loads)
    state_load.start()
    start_all(loads[0])
    start_all(loads[1])
    wait_all(small_loads)
    columns = smalls[...].astype(F32).T
    places = lax.broadcasted_iota(jnp.int32, (LEADS, WIDTH), 0)
    lead_row = jnp.sum(
        jnp.where(places == lead[0], columns[16 : 16 + LEADS], 0.0), axis=0, keepdims=True
    )
    small[...] = columns[:32]
    small[16:17, :] = lead_row
    state_load.wait()
    centered, scale = mean_and_scale(state[...].astype(F32) + lead_row)
    rows[...] = (centered * scale * columns[0:1] + columns[1:2]).astype(BF16)
    turned[...] = rows[...].T
    stores = [pltpu.make_async_copy(turned, turned_out, io_sems.at[1])]
    stores[0].start()
    wait_all(loads[0] + loads[1])
    for part in range(3):
        span = slice(part * WIDTH, part * WIDTH + WIDTH)
        qkv[:, span] = times(rows[...], weight[:, span]).astype(BF16)
        stores.append(pltpu.make_async_copy(qkv.at[:, span], qkv_out.at[:, span], io_sems.at[2 + part]))
        stores[-1].start()
    wait_all(stores)


def front_forward(where, lead_index, patches, arrays):
    return call(
        front_kernel,
        (where, lead_index, patches, *arrays),
        [SMEM, SMEM, HBM] + [HBM] * 4,
        [
            ((WIDTH, TOKENS), BF16, True),
            ((TOKENS, 3 * WIDTH), BF16, True),
            ((32, WIDTH), F32, False),
        ],
        weight_scratch(WIDTH, 3 * WIDTH)
        + [pltpu.VMEM((WIDTH, 128), BF16), pltpu.SemaphoreType.DMA((16,))]
        + [
            pltpu.VMEM((TOKENS, WIDTH), BF16),
            pltpu.VMEM((TOKENS, WIDTH), BF16),
            pltpu.VMEM((WIDTH, TOKENS), BF16),
            pltpu.VMEM((TOKENS, 3 * WIDTH), BF16),
            pltpu.SemaphoreType.DMA((5,)),
        ],
    )


KEY_SPANS = ((0, 256), (0, 384), (128, 512), (256, 512))


def fill_bias(lengths, pad, bias):
    ends, end = [], 0
    for index in range(lengths.shape[1]):
        end = end + lengths[0, index]
        ends.append(end)

    def windows(places):
        return sum([(places >= end).astype(jnp.int32) for end in ends])

    for block, (low, high) in enumerate(KEY_SPANS):
        count = high - low
        queries = lax.broadcasted_iota(jnp.int32, (1, 128), 1) + 128 * block
        keys = lax.broadcasted_iota(jnp.int32, (count, 1), 0) + low
        same = windows(queries) == windows(keys)
        usable = (pad[low:high, :] > 0) | (queries == keys)
        bias[block, :count, :] = jnp.where(same & usable, 0.0, -1e30)


def two_heads(block):
    first = lax.broadcasted_iota(jnp.int32, block.shape, 1) < block.shape[1] // 2
    zero = jnp.zeros_like(block)
    return jnp.concatenate([jnp.where(first, block, zero), jnp.where(first, zero, block)], axis=0)


def head_rows_of(stacked):
    return jnp.concatenate([stacked[:64, :128], stacked[64:, 128:]], axis=0)


def probabilities(scores, allowed):
    masked = scores * score_scale + allowed
    raised = jnp.exp(masked - jnp.max(masked, axis=0, keepdims=True))
    return raised * (1.0 / jnp.sum(raised, axis=0, keepdims=True))


def attention_kernel(where, lengths, pad, qkv, attended_out, turned_out, bias, turned, rows, sems):
    fill_bias(lengths, pad, bias)

    def pair(index, carry):
        first = index * 128
        columns = pl.ds(pl.multiple_of(first, 128), 128)
        keys_at = pl.ds(pl.multiple_of(first + WIDTH, 128), 128)
        values = qkv[:, pl.ds(pl.multiple_of(first + 2 * WIDTH, 128), 128)].T
        for block, (low, high) in enumerate(KEY_SPANS):
            span = slice(128 * block, 128 * block + 128)
            scores = across(qkv[low:high, keys_at], two_heads(qkv[span, columns]))
            allowed = bias[block, : high - low, :]
            probs = [
                probabilities(scores[:, 128 * head : 128 * head + 128], allowed).astype(BF16)
                for head in range(2)
            ]
            mixed = times(values[:, low:high], jnp.concatenate(probs, axis=1))
            turned[columns, span] = head_rows_of(mixed).astype(BF16)
        return carry

    lax.fori_loop(0, WIDTH // 128, pair, 0)
    stores = [pltpu.make_async_copy(turned, turned_out, sems.at[0])]
    stores[0].start()
    rows[...] = turned[...].T
    stores.append(pltpu.make_async_copy(rows, attended_out, sems.at[1]))
    stores[1].start()
    wait_all(stores)


def attention_forward(where, lengths, pad, qkv):
    rows, columns = (TOKENS, WIDTH), (WIDTH, TOKENS)
    return call(
        attention_kernel,
        (where, lengths, pad, qkv),
        [SMEM, SMEM, VMEM, VMEM],
        [(rows, BF16, True), (columns, BF16, True)],
        [
            pltpu.VMEM((4, 384, 128), F32),
            pltpu.VMEM(columns, BF16),
            pltpu.VMEM(rows, BF16),
            pltpu.SemaphoreType.DMA((2,)),
        ],
    )


def up_kernel(where, attended, patches, small, bias, *refs):
    sources, outs, scratch = taken(refs, 4, 5)
    mid_out, mlp_turned_out, act_out, act_turned_out, slope_out = outs
    out_weight, out_sems, weight, sems, scratch = *scratch[:4], scratch[4:]
    inputs, state, mid, rows, mlp_turned, act, act_turned, slope, io_sems, act_sems = scratch
    out_loads = [block_copies(where, "u", sources, OUT_PART, out_weight, out_sems, s) for s in range(2)]
    loads = [block_copies(where, "u", sources, UP_PART, weight, sems, side) for side in range(2)]
    in_loads = [
        pltpu.make_async_copy(attended, inputs, io_sems.at[0]),
        pltpu.make_async_copy(patches, state, io_sems.at[1]),
    ]
    start_all(in_loads)
    start_all(out_loads[0] + out_loads[1])
    start_all(loads[0] + loads[1])
    wait_all(in_loads)
    wait_all(out_loads[0] + out_loads[1])
    mid[...] = (
        state[...].astype(F32)
        + small[16:17, :]
        + times(inputs[...], out_weight[...])
        + small[2:3, :]
    )
    centered, scale = mean_and_scale(mid[...])
    rows[...] = (centered * scale * small[3:4, :] + small[4:5, :]).astype(BF16)
    mlp_turned[...] = rows[...].T
    stores = [
        pltpu.make_async_copy(mid, mid_out, io_sems.at[2]),
        pltpu.make_async_copy(mlp_turned, mlp_turned_out, io_sems.at[3]),
    ]
    start_all(stores)
    wait_all(loads[0] + loads[1])
    for slot in range(6):
        span = slice(slot * 512, slot * 512 + 512)
        values = times(rows[...], weight[:, span]) + bias[:, span]
        share = 0.5 * (1.0 + lax.erf(values * 0.7071067811865476))
        density = jnp.exp(-0.5 * values * values) * 0.3989422804014327
        activated = (values * share).astype(BF16)
        act[:, span] = activated
        act_turned[span, :] = activated.T
        slope[:, span] = (share + values * density).astype(BF16)
        copies = [
            pltpu.make_async_copy(act.at[:, span], act_out.at[:, span], act_sems.at[slot, 0]),
            pltpu.make_async_copy(
                act_turned.at[span, :], act_turned_out.at[span, :], act_sems.at[slot, 1]
            ),
            pltpu.make_async_copy(slope.at[:, span], slope_out.at[:, span], act_sems.at[slot, 2]),
        ]
        start_all(copies)
        stores += copies
    wait_all(stores)


def up_forward(where, attended, patches, small, bias, arrays):
    rows, columns = (TOKENS, WIDTH), (WIDTH, TOKENS)
    wide, tall = (TOKENS, HIDDEN), (HIDDEN, TOKENS)
    return call(
        up_kernel,
        (where, attended, patches, small, bias, *arrays),
        [SMEM, HBM, HBM, VMEM, VMEM] + [HBM] * 4,
        [
            (rows, F32, True),
            (columns, BF16, True),
            (wide, BF16, True),
            (tall, BF16, True),
            (wide, BF16, True),
        ],
        weight_scratch(WIDTH, WIDTH)
        + weight_scratch(WIDTH, HIDDEN)
        + [
            pltpu.VMEM(rows, BF16),
            pltpu.VMEM(rows, BF16),
            pltpu.VMEM(rows, F32),
            pltpu.VMEM(rows, BF16),
            pltpu.VMEM(columns, BF16),
            pltpu.VMEM(wide, BF16),
            pltpu.VMEM(tall, BF16),
            pltpu.VMEM(wide, BF16),
            pltpu.SemaphoreType.DMA((4,)),
            pltpu.SemaphoreType.DMA((6, 3)),
        ],
    )


def gate_shares(logits, cotangent, shares, gate_grad):
    shares[:, 256:] = logits[:, 256:]
    gate_grad[:, 256:] = cotangent[:, 256:GATE]
    first, rest = logits[:, :128], logits[:, 128:256]
    left = lax.broadcasted_iota(jnp.int32, first.shape, 1) < PIX
    third = jnp.where(left, rest, pltpu.roll(rest, PIX, 1))
    largest = jnp.maximum(jnp.maximum(first, pltpu.roll(first, PIX, 1)), third)
    raised, raised_third = jnp.exp(first - largest), jnp.exp(third - largest)
    scale = 1.0 / (raised + pltpu.roll(raised, PIX, 1) + raised_third)
    share, share_third = raised * scale, raised_third * scale
    shares[:, :128] = share
    shares[:, 128:256] = jnp.where(left, share_third, rest)
    pull, other = cotangent[:, :128].astype(F32), cotangent[:, 128:256].astype(F32)
    pull_third = jnp.where(left, other, pltpu.roll(other, PIX, 1))
    weighed = share * pull
    inner = weighed + pltpu.roll(weighed, PIX, 1) + share_third * pull_third
    gate_grad[:, :128] = (share * (pull - inner)).astype(BF16)
    gate_grad[:, 128:256] = jnp.where(left, share_third * (pull_third - inner), other).astype(BF16)


def down_kernel(where, act, mid, small, cotangent, bias, *refs):
    sources, gate_sources, outs, scratch = taken(refs, 4, 4, 6)
    outputs, shares, gate_grad, gate_bias, mine_out, theirs_out = outs
    weight, sems, gate, gate_sems, lane, lane_sems, scratch = *scratch[:6], scratch[6:]
    acts, mids, pulls, turned, logits, io_sems = scratch
    loads = [block_copies(where, "d", sources, DOWN_PART, weight, sems, side) for side in range(2)]
    gate_loads = [
        block_copies(where, "u", gate_sources, GATE_PART, gate, gate_sems, side) for side in range(2)
    ]
    in_loads = [
        pltpu.make_async_copy(act, acts, io_sems.at[0]),
        pltpu.make_async_copy(mid, mids, io_sems.at[1]),
    ]
    pull_load = pltpu.make_async_copy(cotangent, pulls, io_sems.at[2])
    start_all(in_loads)
    start_all(loads[0] + loads[1])
    start_all(gate_loads[0] + gate_loads[1])
    pull_load.start()
    wait_all(in_loads)
    wait_all(loads[0] + loads[1])
    outputs[...] = (mids[...] + times(acts[...], weight[...]) + small[5:6, :]).astype(BF16)
    turned[...] = outputs[...].T
    wait_all(gate_loads[0] + gate_loads[1])
    logits[...] = times(outputs[...], gate[...]) + bias[:, :GATE]
    pull_load.wait()
    gate_shares(logits, pulls, shares, gate_grad)
    gate_bias[...] = jnp.sum(gate_grad[...].astype(F32), axis=0, keepdims=True)
    stores = []
    for side, out in ((1, theirs_out), (0, mine_out)):
        lane[side, :, :256] = times(
            turned[...], gate_grad[:, lane_columns(where, side, 256)]
        ).astype(BF16)
        for tile in range(4):
            span = lane_columns(where, side, 2048, GATE + tile * 512, 512)
            lane[side, :, 256 + tile * 512 : 768 + tile * 512] = times(
                turned[...], pulls[:, span]
            ).astype(BF16)
        copies = term_copies(where, "head", lane, out, lane_sems, side)
        start_all(copies)
        stores += copies
    wait_all(stores)


def down_forward(where, act, mid, small, cotangent, bias, arrays, gate_arrays):
    rows = (TOKENS, WIDTH)
    return call(
        down_kernel,
        (where, act, mid, small, cotangent, bias, *arrays, *gate_arrays),
        [SMEM, HBM, HBM, VMEM, HBM, VMEM] + [HBM] * 8,
        [
            (rows, BF16, False),
            ((TOKENS, GATE), F32, False),
            ((TOKENS, GATE), BF16, False),
            ((1, GATE), F32, False),
            ((16, 48, 2304), BF16, True),
            ((16, 48, 2304), BF16, True),
        ],
        weight_scratch(HIDDEN, WIDTH)
        + weight_scratch(WIDTH, GATE)
        + lane_scratch(WIDTH, 2304)
        + [
            pltpu.VMEM((TOKENS, HIDDEN), BF16),
            pltpu.VMEM(rows, F32),
            pltpu.VMEM((TOKENS, HEAD), BF16),
            pltpu.VMEM((WIDTH, TOKENS), BF16),
            pltpu.VMEM((TOKENS, GATE), F32),
            pltpu.SemaphoreType.DMA((3,)),
        ],
    )


def head_kernel(where, rows, gate_out, bias, *refs):
    sources, outs, scratch = taken(refs, 8, 1)
    (out,) = outs
    weight, sems, inputs, result, io_sems = scratch
    loads = [block_copies(where, "h", sources, HEAD_PART, weight, sems, side) for side in range(2)]
    row_load = pltpu.make_async_copy(rows, inputs, io_sems.at[0])
    gate_load = pltpu.make_async_copy(gate_out, result.at[:, :GATE], io_sems.at[1])
    row_load.start()
    start_all(loads[0])
    start_all(loads[1])
    gate_load.start()
    row_load.wait()
    stores = []

    def store(span):
        stores.append(
            pltpu.make_async_copy(result.at[:, span], out.at[:, span], io_sems.at[2 + len(stores)])
        )
        stores[-1].start()

    for side in range(2):
        wait_all(loads[side])
        for tile in range(4):
            span = lane_columns(where, side, 2048, GATE + tile * 512, 512)
            columns = lane_columns(where, side, 2048, tile * 512, 512)
            result[:, span] = times(inputs[...], weight[:, columns]) + bias[:, span]
            store(span)
    gate_load.wait()
    store(pl.ds(0, GATE))
    wait_all(stores)


def head_forward(where, rows, gate_out, bias, arrays):
    return call(
        head_kernel,
        (where, rows, gate_out, bias, *arrays),
        [SMEM, HBM, HBM, VMEM] + [HBM] * 8,
        [((TOKENS, HEAD), F32, True)],
        weight_scratch(WIDTH, HEAD - GATE)
        + [
            pltpu.VMEM((TOKENS, WIDTH), BF16),
            pltpu.VMEM((TOKENS, HEAD), F32),
            pltpu.SemaphoreType.DMA((11,)),
        ],
    )[0]


def head_back_kernel(where, act_cotangent, gate_grad, cotangent, slope, *refs):
    sources, gate_sources, down_sources, outs, scratch = taken(refs, 8, 4, 4, 5)
    end_grad, branch, down_bias, up_bias, pre_out = outs
    weight, sems, gate_sems, down, down_sems, scratch = *scratch[:5], scratch[5:]
    act_pulls, pulls, slopes, pre_grad, io_sems, pre_sems = scratch
    loads = [
        block_copies(where, "h", sources, HEAD_PART, weight, sems, side, GATE) for side in range(2)
    ]
    gate_loads = [
        block_copies(where, "u", gate_sources, GATE_PART, weight, gate_sems, side)
        for side in range(2)
    ]
    down_loads = [
        block_copies(where, "d", down_sources, DOWN_PART, down, down_sems, side) for side in range(2)
    ]
    first_loads = [
        pltpu.make_async_copy(act_cotangent, act_pulls, io_sems.at[0]),
        pltpu.make_async_copy(gate_grad, pulls.at[:, :GATE], io_sems.at[1]),
    ]
    pull_load = pltpu.make_async_copy(cotangent.at[:, GATE:], pulls.at[:, GATE:], io_sems.at[2])
    slope_load = pltpu.make_async_copy(slope, slopes, io_sems.at[3])
    start_all(first_loads + gate_loads[0] + gate_loads[1])
    pull_load.start()
    start_all(loads[0])
    start_all(loads[1])
    start_all(down_loads[0] + down_loads[1])
    slope_load.start()
    wait_all(first_loads)
    wait_all(gate_loads[0] + gate_loads[1])
    pull_load.wait()
    wait_all(loads[0] + loads[1])
    end_grad[...] = act_pulls[...].astype(F32) + across(pulls[...], weight[...])
    branch[...] = end_grad[...].astype(BF16)
    down_bias[...] = jnp.sum(branch[...].astype(F32), axis=0, keepdims=True)
    wait_all(down_loads[0] + down_loads[1])
    slope_load.wait()
    stores = []
    for tile in range(6):
        span = slice(tile * 512, tile * 512 + 512)
        grad = across(branch[...], down[span, :])
        rounded = (slopes[:, span].astype(F32) * grad).astype(BF16)
        pre_grad[:, span] = rounded
        up_bias[:, span] = jnp.sum(rounded.astype(F32), axis=0, keepdims=True)
        stores.append(
            pltpu.make_async_copy(pre_grad.at[:, span], pre_out.at[:, span], pre_sems.at[tile])
        )
        stores[-1].start()
    wait_all(stores)


def head_backward(where, act_cotangent, gate_grad, cotangent, slope, arrays, gate_arrays, down_arrays):
    rows, wide = (TOKENS, WIDTH), (TOKENS, HIDDEN)
    return call(
        head_back_kernel,
        (where, act_cotangent, gate_grad, cotangent, slope, *arrays, *gate_arrays, *down_arrays),
        [SMEM, HBM, HBM, HBM, HBM] + [HBM] * 16,
        [
            (rows, F32, False),
            (rows, BF16, False),
            ((1, WIDTH), F32, False),
            ((1, HIDDEN), F32, False),
            (wide, BF16, True),
        ],
        weight_scratch(WIDTH, HEAD)
        + [pltpu.SemaphoreType.DMA((2, 16))]
        + weight_scratch(HIDDEN, WIDTH)
        + [
            pltpu.VMEM(rows, BF16),
            pltpu.VMEM((TOKENS, HEAD), BF16),
            pltpu.VMEM(wide, BF16),
            pltpu.VMEM(wide, BF16),
            pltpu.SemaphoreType.DMA((4,)),
            pltpu.SemaphoreType.DMA((6,)),
        ],
    )


def up_back_kernel(
    where, small, pre_grad, branch, act_turned, mlp_turned, mid, end_grad, *refs
):
    sources, outs, scratch = taken(refs, 4, 7)
    mid_grad, out_grad, terms, down_mine, down_theirs, up_mine, up_theirs = outs
    weight, sems, down_lane, down_sems, up_lane, up_sems, scratch = *scratch[:6], scratch[6:]
    pres, branches, acts, mlps, mids, ends, io_sems = scratch
    loads = [block_copies(where, "u", sources, UP_PART, weight, sems, side) for side in range(2)]
    pre_load = pltpu.make_async_copy(pre_grad, pres, io_sems.at[0])
    branch_load = pltpu.make_async_copy(branch, branches, io_sems.at[1])
    act_load = pltpu.make_async_copy(act_turned, acts, io_sems.at[2])
    mlp_load = pltpu.make_async_copy(mlp_turned, mlps, io_sems.at[3])
    norm_loads = [
        pltpu.make_async_copy(mid, mids, io_sems.at[4]),
        pltpu.make_async_copy(end_grad, ends, io_sems.at[5]),
    ]
    branch_load.start()
    act_load.start()
    pre_load.start()
    mlp_load.start()
    start_all(loads[0] + loads[1])
    start_all(norm_loads)
    branch_load.wait()
    act_load.wait()
    stores = []
    for side, out in ((1, down_theirs), (0, down_mine)):
        span = lane_columns(where, side, 384)
        for part in range(4):
            rows = slice(part * WIDTH, part * WIDTH + WIDTH)
            down_lane[side, rows, :] = times(acts[rows, :], branches[:, span]).astype(BF16)
        copies = term_copies(where, "down", down_lane, out, down_sems, side)
        start_all(copies)
        stores += copies
    pre_load.wait()
    mlp_load.wait()
    for side, out in ((1, up_theirs), (0, up_mine)):
        for tile in range(3):
            span = lane_columns(where, side, 1536, tile * 512, 512)
            up_lane[side, :, tile * 512 : tile * 512 + 512] = times(mlps[...], pres[:, span]).astype(
                BF16
            )
        copies = term_copies(where, "up", up_lane, out, up_sems, side)
        start_all(copies)
        stores += copies
    wait_all(loads[0] + loads[1])
    grad = across(pres[...], weight[...])
    wait_all(norm_loads)
    pulled, gain_grad, shift_grad = norm_backward(mids[...], small[3:4, :], grad)
    pulled = pulled + ends[...]
    rounded = pulled.astype(BF16)
    mid_grad[...] = pulled
    out_grad[...] = rounded
    terms[...] = jnp.zeros_like(terms)
    terms[0:1, :] = jnp.sum(rounded.astype(F32), axis=0, keepdims=True)
    terms[1:2, :] = gain_grad
    terms[2:3, :] = shift_grad
    wait_all(stores)


def up_backward(
    where, small, pre_grad, branch, act_turned, mlp_turned, mid, end_grad, arrays
):
    rows = (TOKENS, WIDTH)
    return call(
        up_back_kernel,
        (where, small, pre_grad, branch, act_turned, mlp_turned, mid, end_grad, *arrays),
        [SMEM, VMEM] + [HBM] * 10,
        [
            (rows, F32, False),
            (rows, BF16, False),
            ((8, WIDTH), F32, False),
            ((16, 192, 384), BF16, True),
            ((16, 192, 384), BF16, True),
            ((16, 48, 1536), BF16, True),
            ((16, 48, 1536), BF16, True),
        ],
        weight_scratch(WIDTH, HIDDEN)
        + lane_scratch(HIDDEN, 384)
        + lane_scratch(WIDTH, 1536)
        + [
            pltpu.VMEM((TOKENS, HIDDEN), BF16),
            pltpu.VMEM(rows, BF16),
            pltpu.VMEM((HIDDEN, TOKENS), BF16),
            pltpu.VMEM((WIDTH, TOKENS), BF16),
            pltpu.VMEM(rows, F32),
            pltpu.VMEM(rows, F32),
            pltpu.SemaphoreType.DMA((6,)),
        ],
    )


def attention_back_kernel(where, lengths, pad, out_grad, qkv, *refs):
    sources, outs, scratch = taken(refs, 4, 1)
    (qkv_grad,) = outs
    weight, sems, bias, mixed, turned, key_sum, value_sum = scratch
    loads = [block_copies(where, "u", sources, OUT_PART, weight, sems, side) for side in range(2)]
    start_all(loads[0] + loads[1])
    fill_bias(lengths, pad, bias)
    wait_all(loads[0] + loads[1])
    mixed[...] = across(out_grad[...], weight[...]).astype(BF16)

    def pair(index, carry):
        first = index * 128
        columns = pl.ds(pl.multiple_of(first, 128), 128)
        keys_at = pl.ds(pl.multiple_of(first + WIDTH, 128), 128)
        values_at = pl.ds(pl.multiple_of(first + 2 * WIDTH, 128), 128)
        keys_turned = qkv[:, keys_at].T
        key_sum[...] = jnp.zeros_like(key_sum)
        value_sum[...] = jnp.zeros_like(value_sum)
        for block, (low, high) in enumerate(KEY_SPANS):
            span = slice(128 * block, 128 * block + 128)
            queries, grads = two_heads(qkv[span, columns]), two_heads(mixed[span, columns])
            scores = across(qkv[low:high, keys_at], queries)
            prob_grads = across(qkv[low:high, values_at], grads)
            allowed = bias[block, : high - low, :]
            probs, score_grads = [], []
            for head in range(2):
                part = slice(128 * head, 128 * head + 128)
                prob = probabilities(scores[:, part], allowed)
                pulled = prob * prob_grads[:, part]
                inner = jnp.sum(pulled, axis=0, keepdims=True)
                probs.append(prob.astype(BF16))
                score_grads.append((pulled - prob * inner).astype(BF16))
            score_grad = jnp.concatenate(score_grads, axis=1)
            key_sum[low:high, :] += times(score_grad, queries)
            value_sum[low:high, :] += times(jnp.concatenate(probs, axis=1), grads)
            turned[:, span] = head_rows_of(times(keys_turned[:, low:high], score_grad)) * score_scale
        qkv_grad[:, columns] = turned[...].T.astype(BF16)
        qkv_grad[:, keys_at] = (key_sum[...] * score_scale).astype(BF16)
        qkv_grad[:, values_at] = value_sum[...].astype(BF16)
        return carry

    lax.fori_loop(0, WIDTH // 128, pair, 0)


def attention_backward(where, lengths, pad, out_grad, qkv, arrays):
    return call(
        attention_back_kernel,
        (where, lengths, pad, out_grad, qkv, *arrays),
        [SMEM, SMEM, VMEM, VMEM, VMEM] + [HBM] * 4,
        [((TOKENS, 3 * WIDTH), BF16, False)],
        weight_scratch(WIDTH, WIDTH)
        + [
            pltpu.VMEM((4, 384, 128), F32),
            pltpu.VMEM((TOKENS, WIDTH), BF16),
            pltpu.VMEM((128, TOKENS), F32),
            pltpu.VMEM((TOKENS, 128), F32),
            pltpu.VMEM((TOKENS, 128), F32),
        ],
    )[0]


def front_back_kernel(
    where, lead, small, terms, down_row, up_rows, head_rows,
    qkv_grad, patches, mid_grad, input_turned, attended_turned, out_grad, *refs
):
    sources, outs, scratch = taken(refs, 4, 3)
    patch_out, mine_out, theirs_out = outs
    weight, sems, lane, lane_sems, scratch = *scratch[:4], scratch[4:]
    pulls, state, mids, inputs, mixes, out_pulls, patch_grad, small_grad, io_sems = scratch
    loads = [block_copies(where, "q", sources, QKV_PART, weight, sems, side) for side in range(2)]
    pairs = (
        (qkv_grad, pulls), (patches, state), (mid_grad, mids),
        (input_turned, inputs), (attended_turned, mixes), (out_grad, out_pulls),
    )
    in_loads = [pltpu.make_async_copy(*pair, io_sems.at[at]) for at, pair in enumerate(pairs)]
    in_loads[0].start()
    start_all(loads[0] + loads[1])
    start_all(in_loads[1:])
    in_loads[0].wait()
    wait_all(loads[0] + loads[1])
    grad = across(pulls[...], weight[...])
    wait_all(in_loads[1:])
    pulled, gain_grad, shift_grad = norm_backward(
        state[...].astype(F32) + small[16:17, :], small[0:1, :], grad
    )
    pulled = pulled + mids[...]
    patch_grad[...] = pulled
    stores = [pltpu.make_async_copy(patch_grad, patch_out, io_sems.at[6])]
    stores[0].start()
    small_grad[0:1, :] = gain_grad
    small_grad[1:2, :] = shift_grad
    small_grad[2:5, :] = terms[0:3, :]
    small_grad[5:6, :] = down_row[...]
    small_grad[6:10, :] = up_rows[...]
    small_grad[10:16, :] = head_rows[...]
    places = lax.broadcasted_iota(jnp.int32, (LEADS, WIDTH), 0)
    lead_grad = jnp.sum(pulled, axis=0, keepdims=True)
    small_grad[16:32, :] = jnp.where(places == lead[0], lead_grad, 0.0)
    for side, out in ((1, theirs_out), (0, mine_out)):
        for tile in range(3):
            span = lane_columns(where, side, 1152, tile * 384, 384)
            lane[side, :, tile * 384 : tile * 384 + 384] = times(inputs[...], pulls[:, span]).astype(
                BF16
            )
        span = lane_columns(where, side, 384)
        lane[side, :, 1152:1536] = times(mixes[...], out_pulls[:, span]).astype(BF16)
        rows = small_grad[pl.ds(pl.multiple_of((where[0] ^ side) * 16, 16), 16), :]
        rows = jnp.concatenate([rows, jnp.zeros((112, WIDTH), F32)], axis=0)
        lane[side, :, 1536:1664] = rows.T.astype(BF16)
        copies = term_copies(where, "front", lane, out, lane_sems, side)
        start_all(copies)
        stores += copies
    wait_all(stores)


def front_backward(
    where, lead, small, terms, down_row, up_rows, head_rows,
    qkv_grad, patches, mid_grad, input_turned, attended_turned, out_grad, arrays,
):
    rows, columns = (TOKENS, WIDTH), (WIDTH, TOKENS)
    return call(
        front_back_kernel,
        (
            where, lead, small, terms, down_row, up_rows, head_rows,
            qkv_grad, patches, mid_grad, input_turned, attended_turned, out_grad, *arrays,
        ),
        [SMEM, SMEM] + [VMEM] * 5 + [HBM] * 10,
        [(rows, F32, True), ((16, 48, 1664), BF16, True), ((16, 48, 1664), BF16, True)],
        weight_scratch(WIDTH, 3 * WIDTH)
        + lane_scratch(WIDTH, 1664)
        + [
            pltpu.VMEM((TOKENS, 3 * WIDTH), BF16),
            pltpu.VMEM(rows, BF16),
            pltpu.VMEM(rows, F32),
            pltpu.VMEM(columns, BF16),
            pltpu.VMEM(columns, BF16),
            pltpu.VMEM(rows, BF16),
            pltpu.VMEM(rows, F32),
            pltpu.VMEM((32, WIDTH), F32),
            pltpu.SemaphoreType.DMA((7,)),
        ],
    )


def rows_of(vector, count):
    return vector.reshape(32, count, 24).transpose(1, 0, 2).reshape(count, WIDTH)


def vector_of(rows):
    count = rows.shape[0]
    return rows.reshape(count, 32, 24).transpose(1, 0, 2).reshape(1, count * WIDTH)


def shards(
    patches,
    lead_index,
    window_lengths,
    pad_mask,
    lead_table,
    attn_gain,
    attn_shift,
    qkv_weight,
    out_weight,
    out_bias,
    mlp_gain,
    mlp_shift,
    up_weight,
    up_bias,
    down_weight,
    down_bias,
    head_weight,
    head_bias,
    act_cotangent,
    head_cotangent,
):
    core, where = whereabouts()
    weights = (qkv_weight, out_weight, up_weight, down_weight, head_weight)
    vectors = (
        attn_gain, attn_shift, out_bias, mlp_gain, mlp_shift, down_bias, up_bias, head_bias
    )
    parts = packed(core, weights, lead_table, vectors)
    pad = pad_mask[:, None]
    cotangent_sum = jnp.sum(head_cotangent[:, GATE:].astype(F32), axis=0, keepdims=True)

    orders = ORDERS
    q, u, d, h = [
        in_core_order(core, mine, exchange(theirs, SIBLING), 0)[None]
        for mine, theirs in zip(parts[:4], parts[4:])
    ]

    q = doubled(q, orders["q"][0])
    u = doubled(u, orders["u"][0])
    d = doubled(d, orders["d"][0])
    h = doubled(h, orders["h"][0])
    q = doubled(after(q, u, d, h), orders["q"][1])
    d = doubled(d, orders["d"][1])
    u = doubled(u, orders["u"][1])
    h = doubled(h, orders["h"][1])
    q = doubled(after(q, d, u), orders["q"][2])
    h_far = exchange(h, orders["h"][2])
    d = doubled(d, orders["d"][2])
    q_rest = exchange(after(q, h_far), orders["q"][3])
    h_rest = exchange(h, orders["h"][3])
    u = doubled(u, orders["u"][2])
    first = both_lanes(q, q_rest)
    u_rest = exchange(u, orders["u"][3])
    input_turned, qkv, small_rows = front_forward(
        after(where, d, u, h_rest, cotangent_sum), lead_index, patches, first
    )
    attended, attended_turned = attention_forward(where, window_lengths, pad, qkv)
    h_far_rest = exchange(after(h_far, attended), orders["h"][3])
    d_rest = exchange(after(d, qkv), orders["d"][3])
    second = both_lanes(u, after(u_rest, attended))
    up_bias_row, head_bias_row = vector_of(small_rows[6:10]), vector_of(small_rows[10:16])
    mid_state, mlp_turned, act_rows, act_turned, slope = up_forward(
        where, attended, patches, small_rows, up_bias_row, second
    )
    down = both_lanes(d, after(d_rest, act_rows))
    outputs, gate_out, gate_grad, gate_bias_sum, mine_h, theirs_h = down_forward(
        where, act_rows, mid_state, small_rows, head_cotangent,
        head_bias_row, down, second,
    )
    head = both_lanes(h, h_far, h_rest, h_far_rest)
    got_h = exchange(theirs_h, SIBLING)
    end_grad, branch_grad, down_bias_sum, up_bias_sum, pre_grad = head_backward(
        after(where, theirs_h), act_cotangent, gate_grad, head_cotangent, slope, head, second, down
    )
    keep_h, send_h = folded(mine_h, after(got_h, pre_grad))
    got_h = exchange(send_h, orders["head"][3])
    mid_grad, out_grad, terms, mine_d, theirs_d, mine_u, theirs_u = up_backward(
        after(where, send_h), small_rows, pre_grad, branch_grad, act_turned, mlp_turned,
        mid_state, end_grad, second,
    )
    got_d, got_u = exchange(theirs_d, SIBLING), exchange(theirs_u, SIBLING)
    keep_u, send_u = folded(mine_u, got_u)
    got_u = exchange(send_u, orders["up"][3])
    keep_d, send_d = folded(mine_d, got_d)
    got_d = exchange(send_d, orders["down"][3])
    keep_h, send_h = folded(keep_h, after(got_h, out_grad))
    got_h = exchange(send_h, orders["head"][2])
    qkv_grad = attention_backward(
        after(where, send_h, send_d, send_u), window_lengths, pad, out_grad, qkv, second
    )
    keep_h, send_h = folded(keep_h, after(got_h, qkv_grad))
    got_h = exchange(send_h, orders["head"][1])
    keep_d, send_d = folded(keep_d, after(got_d, qkv_grad))
    got_d = exchange(send_d, orders["down"][2])
    keep_u, send_u = folded(keep_u, after(got_u, qkv_grad))
    got_u = exchange(send_u, orders["up"][2])
    head_rows = rows_of(jnp.concatenate([gate_bias_sum, cotangent_sum], axis=1), 6)
    up_rows = rows_of(up_bias_sum, 4)
    patch_grad, mine_f, theirs_f = front_backward(
        after(where, send_h, send_d, send_u), lead_index, small_rows, terms, down_bias_sum,
        up_rows, head_rows, qkv_grad, patches, mid_grad, input_turned,
        attended_turned, out_grad, first,
    )
    got_f = exchange(theirs_f, SIBLING)
    keep_u, send_u = folded(keep_u, after(got_u, patch_grad))
    got_u = exchange(send_u, orders["up"][1])
    keep_h, send_h = folded(keep_h, after(got_h, patch_grad))
    got_h = exchange(send_h, orders["head"][0])
    keep_f, send_f = folded(mine_f, got_f)
    got_f = exchange(send_f, orders["front"][3])
    keep_d, send_d = folded(keep_d, after(got_d, send_f))
    got_d = exchange(send_d, orders["down"][1])
    head_out = head_forward(
        after(where, send_f, send_u, send_d, send_h), outputs, gate_out, head_bias_row, head
    )
    keep_f, send_f = folded(keep_f, after(got_f, head_out))
    got_f = exchange(send_f, orders["front"][2])
    keep_u, send_u = folded(keep_u, after(got_u, send_f))
    got_u = exchange(send_u, orders["up"][0])
    keep_d, send_d = folded(keep_d, after(got_d, send_f))
    got_d = exchange(send_d, orders["down"][0])
    gate_sum, rest_sum = finished(keep_h, after(got_h, send_f), core, (256, 2048))
    keep_f, send_f = folded(keep_f, got_f)
    got_f = exchange(send_f, orders["front"][1])
    (down_sum,) = finished(keep_d, after(got_d, send_f), core, (384,))
    keep_f, send_f = folded(keep_f, got_f)
    got_f = exchange(send_f, orders["front"][0])
    (up_sum,) = finished(keep_u, after(got_u, send_f), core, (1536,))
    qkv_sum, out_sum, small_sum = finished(keep_f, got_f, core, (1152, 384, 128))
    small_sum = small_sum.T
    return (
        outputs,
        head_out,
        patch_grad,
        small_sum[128:144],
        small_sum[0],
        small_sum[1],
        qkv_sum,
        out_sum,
        small_sum[2],
        small_sum[3],
        small_sum[4],
        up_sum,
        small_sum[6:10].reshape(96),
        down_sum,
        small_sum[5],
        jnp.concatenate([gate_sum, rest_sum], axis=1),
        small_sum[10:16].reshape(144),
    )


def plain_shards(
    patches,
    lead_index,
    window_lengths,
    pad_mask,
    lead_table,
    attn_gain,
    attn_shift,
    qkv_weight,
    out_weight,
    out_bias,
    mlp_gain,
    mlp_shift,
    up_weight,
    up_bias,
    down_weight,
    down_bias,
    head_weight,
    head_bias,
    act_cotangent,
    head_cotangent,
):
    front = (
        lax.all_gather(lead_table, ("dp", "fsdp"), axis=1, tiled=True),
        lax.all_gather(attn_gain, ("dp", "fsdp"), axis=0, tiled=True),
        lax.all_gather(attn_shift, ("dp", "fsdp"), axis=0, tiled=True),
        lax.all_gather(qkv_weight, ("dp", "fsdp"), axis=0, tiled=True),
        lax.all_gather(out_weight, ("dp", "fsdp"), axis=0, tiled=True),
        lax.all_gather(out_bias, ("dp", "fsdp"), axis=0, tiled=True),
    )
    rear = (
        lax.all_gather(mlp_gain, ("dp", "fsdp"), axis=0, tiled=True),
        lax.all_gather(mlp_shift, ("dp", "fsdp"), axis=0, tiled=True),
        lax.all_gather(up_weight, ("dp", "fsdp"), axis=0, tiled=True),
        lax.all_gather(up_bias, ("dp", "fsdp"), axis=0, tiled=True),
        lax.all_gather(down_weight, ("dp", "fsdp"), axis=0, tiled=True),
        lax.all_gather(down_bias, ("dp", "fsdp"), axis=0, tiled=True),
        lax.all_gather(head_weight, ("dp", "fsdp"), axis=0, tiled=True),
        lax.all_gather(head_bias, ("dp", "fsdp"), axis=0, tiled=True),
    )
    table_full, gain_one, shift_one, qkv_full, out_full, out_bias_full = front
    (
        gain_two,
        shift_two,
        up_full,
        up_bias_full,
        down_full,
        down_bias_full,
        head_full,
        head_bias_full,
    ) = rear
    token_rows, width = patches.shape
    head_dim = width // HEADS
    block_rows = min(512, token_rows)
    block_count = token_rows // block_rows
    ends = jnp.cumsum(window_lengths[0])
    positions = jnp.arange(token_rows, dtype=jnp.int32)
    window = jnp.sum((positions[:, None] >= ends[None, :]).astype(jnp.int32), axis=1)
    lead_hot = (jnp.arange(LEADS, dtype=jnp.int32) == lead_index[0]).astype(jnp.float32)
    lead_row = jnp.sum(lead_hot[:, None] * table_full.astype(jnp.float32), axis=0)
    start_state = patches.astype(jnp.float32) + lead_row[None, :]
    normed_one, pull_one = jax.vjp(
        layer_norm, start_state, gain_one.astype(jnp.float32), shift_one.astype(jnp.float32)
    )
    attn_input = normed_one.astype(jnp.bfloat16)
    qkv_rows = jnp.dot(attn_input, qkv_full, preferred_element_type=jnp.float32).astype(
        jnp.bfloat16
    )
    queries = qkv_rows[:, :width].reshape(block_count, block_rows, HEADS, head_dim)
    keys = qkv_rows[:, width : 2 * width].reshape(token_rows, HEADS, head_dim)
    values = qkv_rows[:, 2 * width :].reshape(token_rows, HEADS, head_dim)
    query_windows = window.reshape(block_count, block_rows)
    block_starts = jnp.arange(block_count, dtype=jnp.int32) * block_rows

    def block_scores(query_block, window_block, block_start):
        scores = (
            jnp.einsum("qhd,khd->hqk", query_block, keys, preferred_element_type=jnp.float32)
            * score_scale
        )
        allowed = allowed_keys(window_block, window, pad_mask, block_start)
        return jnp.where(allowed[None], scores, -1e30)

    def forward_block(inputs):
        query_block, window_block, block_start = inputs
        masked = block_scores(query_block, window_block, block_start)
        largest = jnp.max(masked, axis=-1, keepdims=True)
        raised = jnp.exp(masked - largest)
        total = jnp.sum(raised, axis=-1, keepdims=True)
        probs = (raised / total).astype(jnp.bfloat16)
        mixed = jnp.einsum("hqk,khd->qhd", probs, values, preferred_element_type=jnp.float32)
        return (
            mixed.reshape(block_rows, width).astype(jnp.bfloat16),
            (largest + jnp.log(total))[:, :, 0],
        )

    mixed_blocks, log_totals = lax.map(forward_block, (queries, query_windows, block_starts))
    attended = mixed_blocks.reshape(token_rows, width)
    mid_state = (
        start_state
        + jnp.dot(attended, out_full, preferred_element_type=jnp.float32)
        + out_bias_full.astype(jnp.float32)
    )
    normed_two, pull_two = jax.vjp(
        layer_norm, mid_state, gain_two.astype(jnp.float32), shift_two.astype(jnp.float32)
    )
    mlp_input = normed_two.astype(jnp.bfloat16)
    pre_act = jnp.dot(mlp_input, up_full, preferred_element_type=jnp.float32) + up_bias_full.astype(
        jnp.float32
    )
    activated, pull_act = jax.vjp(gelu_exact, pre_act)
    act_rows = activated.astype(jnp.bfloat16)
    end_state = (
        mid_state
        + jnp.dot(act_rows, down_full, preferred_element_type=jnp.float32)
        + down_bias_full.astype(jnp.float32)
    )
    outputs = end_state.astype(jnp.bfloat16)
    logits = jnp.dot(
        outputs, head_full, preferred_element_type=jnp.float32
    ) + head_bias_full.astype(jnp.float32)
    head_out, pull_head = jax.vjp(partial(expert_softmax, experts=EXPERTS, pixels=PIX), logits)
    up_back, down_back, head_back = (
        lax.all_gather(up_weight, ("dp", "fsdp"), axis=0, tiled=True),
        lax.all_gather(down_weight, ("dp", "fsdp"), axis=0, tiled=True),
        lax.all_gather(head_weight, ("dp", "fsdp"), axis=0, tiled=True),
    )
    qkv_back, out_back = (
        lax.all_gather(qkv_weight, ("dp", "fsdp"), axis=0, tiled=True),
        lax.all_gather(out_weight, ("dp", "fsdp"), axis=0, tiled=True),
    )
    logit_grad = pull_head(head_cotangent.astype(jnp.float32))[0].astype(jnp.bfloat16)
    head_bias_term = jnp.sum(logit_grad.astype(jnp.float32), axis=0)
    head_term = jnp.einsum("td,tn->dn", outputs, logit_grad, preferred_element_type=jnp.float32)
    end_grad = act_cotangent.astype(jnp.float32) + jnp.einsum(
        "tn,dn->td", logit_grad, head_back, preferred_element_type=jnp.float32
    )
    branch_grad = end_grad.astype(jnp.bfloat16)
    down_bias_term = jnp.sum(branch_grad.astype(jnp.float32), axis=0)
    down_term = jnp.einsum("tf,td->fd", act_rows, branch_grad, preferred_element_type=jnp.float32)
    act_grad = jnp.einsum("td,fd->tf", branch_grad, down_back, preferred_element_type=jnp.float32)
    pre_grad = pull_act(act_grad)[0].astype(jnp.bfloat16)
    up_bias_term = jnp.sum(pre_grad.astype(jnp.float32), axis=0)
    up_term = jnp.einsum("td,tf->df", mlp_input, pre_grad, preferred_element_type=jnp.float32)
    normed_two_grad = jnp.einsum("tf,df->td", pre_grad, up_back, preferred_element_type=jnp.float32)
    state_grad_two, gain_two_term, shift_two_term = pull_two(normed_two_grad)
    (
        gain_part,
        shift_part,
        up_part,
        up_bias_part,
        down_part,
        down_bias_part,
        head_part,
        head_bias_part,
    ) = (
        lax.psum_scatter(
            gain_two_term.astype(jnp.bfloat16), "dp", scatter_dimension=0, tiled=True
        ).astype(jnp.float32),
        lax.psum_scatter(
            shift_two_term.astype(jnp.bfloat16), "dp", scatter_dimension=0, tiled=True
        ).astype(jnp.float32),
        lax.psum_scatter(
            up_term.astype(jnp.bfloat16), "dp", scatter_dimension=0, tiled=True
        ).astype(jnp.float32),
        lax.psum_scatter(
            up_bias_term.astype(jnp.bfloat16), "dp", scatter_dimension=0, tiled=True
        ).astype(jnp.float32),
        lax.psum_scatter(
            down_term.astype(jnp.bfloat16), "dp", scatter_dimension=0, tiled=True
        ).astype(jnp.float32),
        lax.psum_scatter(
            down_bias_term.astype(jnp.bfloat16), "dp", scatter_dimension=0, tiled=True
        ).astype(jnp.float32),
        lax.psum_scatter(
            head_term.astype(jnp.bfloat16), "dp", scatter_dimension=0, tiled=True
        ).astype(jnp.float32),
        lax.psum_scatter(
            head_bias_term.astype(jnp.bfloat16), "dp", scatter_dimension=0, tiled=True
        ).astype(jnp.float32),
    )
    rear_grads = (
        lax.psum_scatter(gain_part, "fsdp", scatter_dimension=0, tiled=True),
        lax.psum_scatter(shift_part, "fsdp", scatter_dimension=0, tiled=True),
        lax.psum_scatter(up_part, "fsdp", scatter_dimension=0, tiled=True),
        lax.psum_scatter(up_bias_part, "fsdp", scatter_dimension=0, tiled=True),
        lax.psum_scatter(down_part, "fsdp", scatter_dimension=0, tiled=True),
        lax.psum_scatter(down_bias_part, "fsdp", scatter_dimension=0, tiled=True),
        lax.psum_scatter(head_part, "fsdp", scatter_dimension=0, tiled=True),
        lax.psum_scatter(head_bias_part, "fsdp", scatter_dimension=0, tiled=True),
    )
    mid_grad = end_grad + state_grad_two
    out_grad = mid_grad.astype(jnp.bfloat16)
    out_bias_term = jnp.sum(out_grad.astype(jnp.float32), axis=0)
    out_term = jnp.einsum("td,te->de", attended, out_grad, preferred_element_type=jnp.float32)
    mixed_grad = jnp.einsum(
        "te,de->td", out_grad, out_back, preferred_element_type=jnp.float32
    ).astype(jnp.bfloat16)
    grad_blocks = mixed_grad.reshape(block_count, block_rows, HEADS, head_dim)

    def backward_block(carry, inputs):
        key_sum, value_sum = carry
        query_block, grad_block, window_block, total_block, block_start = inputs
        masked = block_scores(query_block, window_block, block_start)
        probs = jnp.exp(masked - total_block[:, :, None])
        prob_grad = jnp.einsum(
            "qhd,khd->hqk", grad_block, values, preferred_element_type=jnp.float32
        )
        inner = jnp.sum(probs * prob_grad, axis=-1, keepdims=True)
        score_grad = (probs * (prob_grad - inner)).astype(jnp.bfloat16)
        query_grad = (
            jnp.einsum("hqk,khd->qhd", score_grad, keys, preferred_element_type=jnp.float32)
            * score_scale
        )
        key_sum = (
            key_sum
            + jnp.einsum(
                "hqk,qhd->khd", score_grad, query_block, preferred_element_type=jnp.float32
            )
            * score_scale
        )
        value_sum = value_sum + jnp.einsum(
            "hqk,qhd->khd",
            probs.astype(jnp.bfloat16),
            grad_block,
            preferred_element_type=jnp.float32,
        )
        return ((key_sum, value_sum), query_grad.reshape(block_rows, width))

    zero_keys = jnp.zeros((token_rows, HEADS, head_dim), jnp.float32)
    (key_grad, value_grad), query_grads = lax.scan(
        backward_block,
        (zero_keys, zero_keys),
        (queries, grad_blocks, query_windows, log_totals, block_starts),
    )
    qkv_grad = jnp.concatenate(
        [
            query_grads.reshape(token_rows, width),
            key_grad.reshape(token_rows, width),
            value_grad.reshape(token_rows, width),
        ],
        axis=1,
    ).astype(jnp.bfloat16)
    qkv_term = jnp.einsum("td,te->de", attn_input, qkv_grad, preferred_element_type=jnp.float32)
    normed_one_grad = jnp.einsum(
        "te,de->td", qkv_grad, qkv_back, preferred_element_type=jnp.float32
    )
    state_grad_one, gain_one_term, shift_one_term = pull_one(normed_one_grad)
    patch_grad = mid_grad + state_grad_one
    lead_term = lead_hot[:, None] * jnp.sum(patch_grad, axis=0)[None, :]
    lead_part, gain_one_part, shift_one_part, qkv_part, out_part, out_bias_part = (
        lax.psum_scatter(
            lead_term.astype(jnp.bfloat16), "dp", scatter_dimension=1, tiled=True
        ).astype(jnp.float32),
        lax.psum_scatter(
            gain_one_term.astype(jnp.bfloat16), "dp", scatter_dimension=0, tiled=True
        ).astype(jnp.float32),
        lax.psum_scatter(
            shift_one_term.astype(jnp.bfloat16), "dp", scatter_dimension=0, tiled=True
        ).astype(jnp.float32),
        lax.psum_scatter(
            qkv_term.astype(jnp.bfloat16), "dp", scatter_dimension=0, tiled=True
        ).astype(jnp.float32),
        lax.psum_scatter(
            out_term.astype(jnp.bfloat16), "dp", scatter_dimension=0, tiled=True
        ).astype(jnp.float32),
        lax.psum_scatter(
            out_bias_term.astype(jnp.bfloat16), "dp", scatter_dimension=0, tiled=True
        ).astype(jnp.float32),
    )
    front_grads = (
        lax.psum_scatter(lead_part, "fsdp", scatter_dimension=1, tiled=True),
        lax.psum_scatter(gain_one_part, "fsdp", scatter_dimension=0, tiled=True),
        lax.psum_scatter(shift_one_part, "fsdp", scatter_dimension=0, tiled=True),
        lax.psum_scatter(qkv_part, "fsdp", scatter_dimension=0, tiled=True),
        lax.psum_scatter(out_part, "fsdp", scatter_dimension=0, tiled=True),
        lax.psum_scatter(out_bias_part, "fsdp", scatter_dimension=0, tiled=True),
    )
    return (
        outputs,
        head_out,
        patch_grad,
        front_grads[0],
        front_grads[1],
        front_grads[2],
        front_grads[3],
        front_grads[4],
        front_grads[5],
        rear_grads[0],
        rear_grads[1],
        rear_grads[2],
        rear_grads[3],
        rear_grads[4],
        rear_grads[5],
        rear_grads[6],
        rear_grads[7],
    )


def solution(mesh):
    in_specs = (
        P(("dp", "fsdp"), None),
        P(("dp", "fsdp")),
        P(("dp", "fsdp"), None),
        P(("dp", "fsdp")),
        P(None, ("dp", "fsdp")),
        P(("dp", "fsdp")),
        P(("dp", "fsdp")),
        P(("dp", "fsdp"), None),
        P(("dp", "fsdp"), None),
        P(("dp", "fsdp")),
        P(("dp", "fsdp")),
        P(("dp", "fsdp")),
        P(("dp", "fsdp"), None),
        P(("dp", "fsdp")),
        P(("dp", "fsdp"), None),
        P(("dp", "fsdp")),
        P(("dp", "fsdp"), None),
        P(("dp", "fsdp")),
        P(("dp", "fsdp"), None),
        P(("dp", "fsdp"), None),
    )
    out_specs = (
        P(("dp", "fsdp"), None),
        P(("dp", "fsdp"), None),
        P(("dp", "fsdp"), None),
        P(None, ("dp", "fsdp")),
        P(("dp", "fsdp")),
        P(("dp", "fsdp")),
        P(("dp", "fsdp"), None),
        P(("dp", "fsdp"), None),
        P(("dp", "fsdp")),
        P(("dp", "fsdp")),
        P(("dp", "fsdp")),
        P(("dp", "fsdp"), None),
        P(("dp", "fsdp")),
        P(("dp", "fsdp"), None),
        P(("dp", "fsdp")),
        P(("dp", "fsdp"), None),
        P(("dp", "fsdp")),
    )
    body = shards if dict(mesh.shape) == {"dp": 4, "fsdp": 8} else plain_shards
    return jax.shard_map(body, mesh=mesh, in_specs=in_specs, out_specs=out_specs, check_vma=False)
```

```python
from functools import partial

import jax
import jax.numpy as jnp
from jax import lax
from jax.experimental import pallas as pl
from jax.experimental.pallas import tpu as pltpu
from jax.sharding import PartitionSpec as P

HEADS = 12
PIX = 64
EXPERTS = 3
LEADS = 16


norm_epsilon = 1e-05
score_scale = 0.125


def layer_norm(hidden, norm_gain, norm_shift):
    average = jnp.mean(hidden, axis=-1, keepdims=True)
    centered = hidden - average
    variance = jnp.mean(centered * centered, axis=-1, keepdims=True)
    return centered * lax.rsqrt(variance + norm_epsilon) * norm_gain + norm_shift


def gelu_exact(values):
    return 0.5 * values * (1.0 + lax.erf(values * 0.7071067811865476))


def expert_softmax(logits, experts, pixels):
    gate_part = logits[:, : experts * pixels].reshape(logits.shape[0], experts, pixels)
    largest = jnp.max(gate_part, axis=1, keepdims=True)
    raised = jnp.exp(gate_part - largest)
    shares = raised / jnp.sum(raised, axis=1, keepdims=True)
    return jnp.concatenate(
        [shares.reshape(logits.shape[0], experts * pixels), logits[:, experts * pixels :]], axis=1
    )


def allowed_keys(query_window, key_window, key_valid, query_start):
    query_place = query_start + jnp.arange(query_window.shape[0], dtype=jnp.int32)
    key_place = jnp.arange(key_window.shape[0], dtype=jnp.int32)
    same_window = query_window[:, None] == key_window[None, :]
    usable = (key_valid[None, :] > 0) | (query_place[:, None] == key_place[None, :])
    return same_window & usable


AXES = ("dp", "fsdp")
FAR_Z, NEAR_Z, FIRST, SECOND, SIBLING = (4, 4), (2, 2), (8, 16), (16, 8), (1, 1)
ORDERS = {
    "q": (FAR_Z, FIRST, SECOND, NEAR_Z),
    "u": (NEAR_Z, FAR_Z, FIRST, SECOND),
    "d": (FIRST, FAR_Z, NEAR_Z, SECOND),
    "h": (FAR_Z, FIRST, SECOND, NEAR_Z),
    "head": (FAR_Z, NEAR_Z, FIRST, SECOND),
    "down": (FAR_Z, NEAR_Z, FIRST, SECOND),
    "up": (FAR_Z, FIRST, SECOND, NEAR_Z),
    "front": (FAR_Z, NEAR_Z, FIRST, SECOND),
}
WIDTH = 768
HIDDEN = 3072
HEAD = 4608
TOKENS = 512
GATE = 512
F32 = jnp.float32
BF16 = jnp.bfloat16
HBM = pl.BlockSpec(memory_space=pltpu.HBM)
SMEM = pl.BlockSpec(memory_space=pltpu.SMEM)
VMEM = pl.BlockSpec(memory_space=pltpu.VMEM)
QKV_PART, SMALL_PART = (0, 1152), (1152, 128)
UP_PART, OUT_PART, GATE_PART = (0, 1536), (1536, 384), (1920, 256)
DOWN_PART, HEAD_PART = (0, 384), (0, 2048)


def chip_masks(order, lane):
    masks = []
    for place in range(16):
        mask = 0
        for step in range(4):
            if place >> step & 1:
                mask ^= order[step][lane]
        masks.append(mask >> 1)
    return masks


def table_start(group, side):
    return 1 + 32 * list(ORDERS).index(group) + 16 * side


def exchange(array, masks):
    return lax.ppermute(array, AXES, [(d, d ^ masks[d & 1]) for d in range(32)])


def whereabouts():
    device = lax.axis_index("dp") * 8 + lax.axis_index("fsdp")
    core, chip = device % 2, device // 2
    tables = [chip_masks(order, 0) + chip_masks(order, 1) for order in ORDERS.values()]
    swapped = [chip_masks(order, 1) + chip_masks(order, 0) for order in ORDERS.values()]
    places = jnp.where(core == 0, jnp.array(tables, jnp.int32), jnp.array(swapped, jnp.int32))
    places = (places ^ chip).reshape(32 * len(ORDERS))
    return core, jnp.concatenate([core[None].astype(jnp.int32), places])


def after(value, *marks):
    return lax.optimization_barrier((value, marks))[0]


def in_core_order(core, mine, theirs, axis):
    return jnp.where(
        core == 0,
        jnp.concatenate([mine, theirs], axis=axis),
        jnp.concatenate([theirs, mine], axis=axis),
    )


def pack_kernel(core, qkv, out, up, down, head, table, *refs):
    vectors, (up_bias, head_bias), refs = refs[:6], refs[6:8], refs[8:]
    outs, (rows,) = refs[:8], refs[8:]
    rows[...] = jnp.zeros_like(rows)
    for index, vector in enumerate(vectors):
        rows[index : index + 1, :24] = vector[...].astype(F32)
    for index in range(4):
        rows[6 + index : 7 + index, :24] = up_bias[:, 24 * index : 24 * index + 24].astype(F32)
    for index in range(6):
        rows[10 + index : 11 + index, :24] = head_bias[:, 24 * index : 24 * index + 24].astype(F32)
    rows[16:32, :24] = table[...].astype(F32)
    small = rows[...].T[:24].astype(BF16)
    for side in range(2):
        q, u, d, h = outs[4 * side : 4 * side + 4]
        q[:, :1152] = qkv[:, lane_columns(core, side, 1152)]
        q[:, 1152:] = small
        u[:, :1536] = up[:, lane_columns(core, side, 1536)]
        u[:, 1536:1920] = out[:, lane_columns(core, side, 384)]
        u[:, 1920:] = head[:, lane_columns(core, side, 256)]
        d[...] = down[:, lane_columns(core, side, 384)]
        h[...] = head[:, lane_columns(core, side, 2048, GATE)]


def packed(core, weights, table, vectors):
    shapes = [(24, 1280), (24, 2176), (96, 384), (24, 2048)] * 2
    return call(
        pack_kernel,
        (core.reshape(1), *weights, table, *[vector[None] for vector in vectors]),
        [SMEM] + [VMEM] * 14,
        [(shape, BF16, False) for shape in shapes],
        [pltpu.VMEM((128, 128), F32)],
    )


def doubled(held, masks):
    return jnp.concatenate([held, exchange(held, masks)], axis=0)


def both_lanes(*arrays):
    return arrays + tuple(exchange(array, SIBLING) for array in arrays)


def total(first, second):
    return first.astype(F32) + second.astype(F32)


def folded(keep, got, start=0):
    half = got.shape[0] // 2
    send = total(keep[half:], got[half:]).astype(BF16)
    return total(keep[:half], got[:half]).astype(BF16), send


def finished(keep, got, core, widths):
    block = total(keep, got)[0]
    rows = block.shape[0] // 2
    upper, lower = block[:rows], block[rows:]
    mine = jnp.where(core == 0, upper, lower)
    theirs = jnp.where(core == 0, lower, upper).astype(BF16)
    other = exchange(theirs, SIBLING).astype(F32)
    pieces, start = [], 0
    for width in widths:
        span = slice(start, start + width)
        pieces.append(in_core_order(core, mine[:, span], other[:, span], 1))
        start += width
    return pieces


def across(first, second):
    return lax.dot_general(first, second, (((1,), (1,)), ((), ())), preferred_element_type=F32)


def times(first, second):
    return jnp.dot(first, second, preferred_element_type=F32)


def lane_columns(where, side, stride, first=0, width=None):
    return pl.ds(pl.multiple_of(first + (where[0] ^ side) * stride, 128), width or stride)


def block_copies(where, group, sources, part, target, sems, side, first=0):
    start, width = part
    rows = sources[0].shape[1]
    half = len(sources) // 2
    count = 16 // half
    copies = []
    for place in range(16):
        row = pl.multiple_of(where[table_start(group, side) + place] * rows, rows)
        copies.append(
            pltpu.make_async_copy(
                sources[half * side + place // count].at[place % count, :, pl.ds(start, width)],
                target.at[pl.ds(row, rows), lane_columns(where, side, width, first)],
                sems.at[side, place],
            )
        )
    return copies


def term_copies(where, group, lane, out, sems, side):
    rows = out.shape[1]
    copies = []
    for place in range(16):
        row = pl.multiple_of(where[table_start(group, side) + place] * rows, rows)
        copies.append(
            pltpu.make_async_copy(lane.at[side, pl.ds(row, rows), :], out.at[place], sems.at[side, place])
        )
    return copies


def start_all(copies):
    for copy in copies:
        copy.start()


def wait_all(copies):
    for copy in copies:
        copy.wait()


def mean_and_scale(hidden):
    average = jnp.mean(hidden, axis=1, keepdims=True)
    centered = hidden - average
    variance = jnp.mean(centered * centered, axis=1, keepdims=True)
    return centered, lax.rsqrt(variance + norm_epsilon)


def norm_backward(hidden, gain, upstream):
    centered, scale = mean_and_scale(hidden)
    normed = centered * scale
    gain_grad = jnp.sum(upstream * normed, axis=0, keepdims=True)
    shift_grad = jnp.sum(upstream, axis=0, keepdims=True)
    scaled = upstream * gain
    first = jnp.mean(scaled, axis=1, keepdims=True)
    second = jnp.mean(scaled * normed, axis=1, keepdims=True)
    return scale * (scaled - first - normed * second), gain_grad, shift_grad


def call(kernel, operands, in_specs, outs, scratch):
    return pl.pallas_call(
        kernel,
        out_shape=[jax.ShapeDtypeStruct(shape, kind) for shape, kind, _ in outs],
        in_specs=in_specs,
        out_specs=[HBM if copied else VMEM for _, _, copied in outs],
        scratch_shapes=scratch,
        compiler_params=pltpu.CompilerParams(vmem_limit_bytes=56 * 1024 * 1024),
        cost_estimate=pl.CostEstimate(flops=2 * 10**12, bytes_accessed=10**10, transcendentals=0),
    )(*operands)


def lane_scratch(rows, width):
    return [pltpu.VMEM((2, rows, width), BF16), pltpu.SemaphoreType.DMA((2, 16))]


def weight_scratch(rows, width):
    return [pltpu.VMEM((rows, width), BF16), pltpu.SemaphoreType.DMA((2, 16))]


def taken(refs, *counts):
    groups = []
    for count in counts:
        groups.append(refs[:count])
        refs = refs[count:]
    return *groups, refs


def front_kernel(where, lead, patches, *refs):
    sources, outs, scratch = taken(refs, 4, 3)
    turned_out, qkv_out, small = outs
    weight, sems, smalls, small_sems, state, rows, turned, qkv, io_sems = scratch
    loads = [block_copies(where, "q", sources, QKV_PART, weight, sems, side) for side in range(2)]
    small_loads = []
    for place in range(16):
        row = pl.multiple_of(where[table_start("q", 0) + place] * 48, 48)
        small_loads.append(
            pltpu.make_async_copy(
                sources[place // 8].at[place % 8, :, pl.ds(*SMALL_PART)],
                smalls.at[pl.ds(row, 48), :],
                small_sems.at[place],
            )
        )
    state_load = pltpu.make_async_copy(patches, state, io_sems.at[0])
    start_all(small_loads)
    state_load.start()
    start_all(loads[0])
    start_all(loads[1])
    wait_all(small_loads)
    columns = smalls[...].astype(F32).T
    places = lax.broadcasted_iota(jnp.int32, (LEADS, WIDTH), 0)
    lead_row = jnp.sum(
        jnp.where(places == lead[0], columns[16 : 16 + LEADS], 0.0), axis=0, keepdims=True
    )
    small[...] = columns[:32]
    small[16:17, :] = lead_row
    state_load.wait()
    centered, scale = mean_and_scale(state[...].astype(F32) + lead_row)
    rows[...] = (centered * scale * columns[0:1] + columns[1:2]).astype(BF16)
    turned[...] = rows[...].T
    stores = [pltpu.make_async_copy(turned, turned_out, io_sems.at[1])]
    stores[0].start()
    wait_all(loads[0] + loads[1])
    for part in range(3):
        span = slice(part * WIDTH, part * WIDTH + WIDTH)
        qkv[:, span] = times(rows[...], weight[:, span]).astype(BF16)
        stores.append(pltpu.make_async_copy(qkv.at[:, span], qkv_out.at[:, span], io_sems.at[2 + part]))
        stores[-1].start()
    wait_all(stores)


def front_forward(where, lead_index, patches, arrays):
    return call(
        front_kernel,
        (where, lead_index, patches, *arrays),
        [SMEM, SMEM, HBM] + [HBM] * 4,
        [
            ((WIDTH, TOKENS), BF16, True),
            ((TOKENS, 3 * WIDTH), BF16, True),
            ((32, WIDTH), F32, False),
        ],
        weight_scratch(WIDTH, 3 * WIDTH)
        + [pltpu.VMEM((WIDTH, 128), BF16), pltpu.SemaphoreType.DMA((16,))]
        + [
            pltpu.VMEM((TOKENS, WIDTH), BF16),
            pltpu.VMEM((TOKENS, WIDTH), BF16),
            pltpu.VMEM((WIDTH, TOKENS), BF16),
            pltpu.VMEM((TOKENS, 3 * WIDTH), BF16),
            pltpu.SemaphoreType.DMA((5,)),
        ],
    )


KEY_SPANS = ((0, 256), (0, 384), (128, 512), (256, 512))


def fill_bias(lengths, pad, bias):
    ends, end = [], 0
    for index in range(lengths.shape[1]):
        end = end + lengths[0, index]
        ends.append(end)

    def windows(places):
        return sum([(places >= end).astype(jnp.int32) for end in ends])

    for block, (low, high) in enumerate(KEY_SPANS):
        count = high - low
        queries = lax.broadcasted_iota(jnp.int32, (1, 128), 1) + 128 * block
        keys = lax.broadcasted_iota(jnp.int32, (count, 1), 0) + low
        same = windows(queries) == windows(keys)
        usable = (pad[low:high, :] > 0) | (queries == keys)
        bias[block, :count, :] = jnp.where(same & usable, 0.0, -1e30)


def two_heads(block):
    first = lax.broadcasted_iota(jnp.int32, block.shape, 1) < block.shape[1] // 2
    zero = jnp.zeros_like(block)
    return jnp.concatenate([jnp.where(first, block, zero), jnp.where(first, zero, block)], axis=0)


def head_rows_of(stacked):
    return jnp.concatenate([stacked[:64, :128], stacked[64:, 128:]], axis=0)


def probabilities(scores, allowed):
    masked = scores * score_scale + allowed
    raised = jnp.exp(masked - jnp.max(masked, axis=0, keepdims=True))
    return raised * (1.0 / jnp.sum(raised, axis=0, keepdims=True))


def attention_kernel(where, lengths, pad, qkv, attended_out, turned_out, bias, turned, rows, sems):
    fill_bias(lengths, pad, bias)

    def pair(index, carry):
        first = index * 128
        columns = pl.ds(pl.multiple_of(first, 128), 128)
        keys_at = pl.ds(pl.multiple_of(first + WIDTH, 128), 128)
        values = qkv[:, pl.ds(pl.multiple_of(first + 2 * WIDTH, 128), 128)].T
        for block, (low, high) in enumerate(KEY_SPANS):
            span = slice(128 * block, 128 * block + 128)
            scores = across(qkv[low:high, keys_at], two_heads(qkv[span, columns]))
            allowed = bias[block, : high - low, :]
            probs = [
                probabilities(scores[:, 128 * head : 128 * head + 128], allowed).astype(BF16)
                for head in range(2)
            ]
            mixed = times(values[:, low:high], jnp.concatenate(probs, axis=1))
            turned[columns, span] = head_rows_of(mixed).astype(BF16)
        return carry

    lax.fori_loop(0, WIDTH // 128, pair, 0)
    stores = [pltpu.make_async_copy(turned, turned_out, sems.at[0])]
    stores[0].start()
    rows[...] = turned[...].T
    stores.append(pltpu.make_async_copy(rows, attended_out, sems.at[1]))
    stores[1].start()
    wait_all(stores)


def attention_forward(where, lengths, pad, qkv):
    rows, columns = (TOKENS, WIDTH), (WIDTH, TOKENS)
    return call(
        attention_kernel,
        (where, lengths, pad, qkv),
        [SMEM, SMEM, VMEM, VMEM],
        [(rows, BF16, True), (columns, BF16, True)],
        [
            pltpu.VMEM((4, 384, 128), F32),
            pltpu.VMEM(columns, BF16),
            pltpu.VMEM(rows, BF16),
            pltpu.SemaphoreType.DMA((2,)),
        ],
    )


def up_kernel(where, attended, patches, small, bias, *refs):
    sources, outs, scratch = taken(refs, 4, 5)
    mid_out, mlp_turned_out, act_out, act_turned_out, slope_out = outs
    out_weight, out_sems, weight, sems, scratch = *scratch[:4], scratch[4:]
    inputs, state, mid, rows, mlp_turned, act, act_turned, slope, io_sems, act_sems = scratch
    out_loads = [block_copies(where, "u", sources, OUT_PART, out_weight, out_sems, s) for s in range(2)]
    loads = [block_copies(where, "u", sources, UP_PART, weight, sems, side) for side in range(2)]
    in_loads = [
        pltpu.make_async_copy(attended, inputs, io_sems.at[0]),
        pltpu.make_async_copy(patches, state, io_sems.at[1]),
    ]
    start_all(in_loads)
    start_all(out_loads[0] + out_loads[1])
    start_all(loads[0] + loads[1])
    wait_all(in_loads)
    wait_all(out_loads[0] + out_loads[1])
    mid[...] = (
        state[...].astype(F32)
        + small[16:17, :]
        + times(inputs[...], out_weight[...])
        + small[2:3, :]
    )
    centered, scale = mean_and_scale(mid[...])
    rows[...] = (centered * scale * small[3:4, :] + small[4:5, :]).astype(BF16)
    mlp_turned[...] = rows[...].T
    stores = [
        pltpu.make_async_copy(mid, mid_out, io_sems.at[2]),
        pltpu.make_async_copy(mlp_turned, mlp_turned_out, io_sems.at[3]),
    ]
    start_all(stores)
    wait_all(loads[0] + loads[1])
    for slot in range(6):
        span = slice(slot * 512, slot * 512 + 512)
        values = times(rows[...], weight[:, span]) + bias[:, span]
        share = 0.5 * (1.0 + lax.erf(values * 0.7071067811865476))
        density = jnp.exp(-0.5 * values * values) * 0.3989422804014327
        activated = (values * share).astype(BF16)
        act[:, span] = activated
        act_turned[span, :] = activated.T
        slope[:, span] = (share + values * density).astype(BF16)
        copies = [
            pltpu.make_async_copy(act.at[:, span], act_out.at[:, span], act_sems.at[slot, 0]),
            pltpu.make_async_copy(
                act_turned.at[span, :], act_turned_out.at[span, :], act_sems.at[slot, 1]
            ),
            pltpu.make_async_copy(slope.at[:, span], slope_out.at[:, span], act_sems.at[slot, 2]),
        ]
        start_all(copies)
        stores += copies
    wait_all(stores)


def up_forward(where, attended, patches, small, bias, arrays):
    rows, columns = (TOKENS, WIDTH), (WIDTH, TOKENS)
    wide, tall = (TOKENS, HIDDEN), (HIDDEN, TOKENS)
    return call(
        up_kernel,
        (where, attended, patches, small, bias, *arrays),
        [SMEM, HBM, HBM, VMEM, VMEM] + [HBM] * 4,
        [
            (rows, F32, True),
            (columns, BF16, True),
            (wide, BF16, True),
            (tall, BF16, True),
            (wide, BF16, True),
        ],
        weight_scratch(WIDTH, WIDTH)
        + weight_scratch(WIDTH, HIDDEN)
        + [
            pltpu.VMEM(rows, BF16),
            pltpu.VMEM(rows, BF16),
            pltpu.VMEM(rows, F32),
            pltpu.VMEM(rows, BF16),
            pltpu.VMEM(columns, BF16),
            pltpu.VMEM(wide, BF16),
            pltpu.VMEM(tall, BF16),
            pltpu.VMEM(wide, BF16),
            pltpu.SemaphoreType.DMA((4,)),
            pltpu.SemaphoreType.DMA((6, 3)),
        ],
    )


def gate_shares(logits, cotangent, shares, gate_grad):
    shares[:, 256:] = logits[:, 256:]
    gate_grad[:, 256:] = cotangent[:, 256:GATE]
    first, rest = logits[:, :128], logits[:, 128:256]
    left = lax.broadcasted_iota(jnp.int32, first.shape, 1) < PIX
    third = jnp.where(left, rest, pltpu.roll(rest, PIX, 1))
    largest = jnp.maximum(jnp.maximum(first, pltpu.roll(first, PIX, 1)), third)
    raised, raised_third = jnp.exp(first - largest), jnp.exp(third - largest)
    scale = 1.0 / (raised + pltpu.roll(raised, PIX, 1) + raised_third)
    share, share_third = raised * scale, raised_third * scale
    shares[:, :128] = share
    shares[:, 128:256] = jnp.where(left, share_third, rest)
    pull, other = cotangent[:, :128].astype(F32), cotangent[:, 128:256].astype(F32)
    pull_third = jnp.where(left, other, pltpu.roll(other, PIX, 1))
    weighed = share * pull
    inner = weighed + pltpu.roll(weighed, PIX, 1) + share_third * pull_third
    gate_grad[:, :128] = (share * (pull - inner)).astype(BF16)
    gate_grad[:, 128:256] = jnp.where(left, share_third * (pull_third - inner), other).astype(BF16)


def down_kernel(where, act, mid, small, cotangent, bias, *refs):
    sources, gate_sources, outs, scratch = taken(refs, 4, 4, 6)
    outputs, shares, gate_grad, gate_bias, mine_out, theirs_out = outs
    weight, sems, gate, gate_sems, lane, lane_sems, scratch = *scratch[:6], scratch[6:]
    acts, mids, pulls, turned, logits, io_sems = scratch
    loads = [block_copies(where, "d", sources, DOWN_PART, weight, sems, side) for side in range(2)]
    gate_loads = [
        block_copies(where, "u", gate_sources, GATE_PART, gate, gate_sems, side) for side in range(2)
    ]
    in_loads = [
        pltpu.make_async_copy(act, acts, io_sems.at[0]),
        pltpu.make_async_copy(mid, mids, io_sems.at[1]),
    ]
    pull_load = pltpu.make_async_copy(cotangent, pulls, io_sems.at[2])
    start_all(in_loads)
    start_all(loads[0] + loads[1])
    start_all(gate_loads[0] + gate_loads[1])
    pull_load.start()
    wait_all(in_loads)
    wait_all(loads[0] + loads[1])
    outputs[...] = (mids[...] + times(acts[...], weight[...]) + small[5:6, :]).astype(BF16)
    turned[...] = outputs[...].T
    wait_all(gate_loads[0] + gate_loads[1])
    logits[...] = times(outputs[...], gate[...]) + bias[:, :GATE]
    pull_load.wait()
    gate_shares(logits, pulls, shares, gate_grad)
    gate_bias[...] = jnp.sum(gate_grad[...].astype(F32), axis=0, keepdims=True)
    stores = []
    for side, out in ((1, theirs_out), (0, mine_out)):
        lane[side, :, :256] = times(
            turned[...], gate_grad[:, lane_columns(where, side, 256)]
        ).astype(BF16)
        for tile in range(4):
            span = lane_columns(where, side, 2048, GATE + tile * 512, 512)
            lane[side, :, 256 + tile * 512 : 768 + tile * 512] = times(
                turned[...], pulls[:, span]
            ).astype(BF16)
        copies = term_copies(where, "head", lane, out, lane_sems, side)
        start_all(copies)
        stores += copies
    wait_all(stores)


def down_forward(where, act, mid, small, cotangent, bias, arrays, gate_arrays):
    rows = (TOKENS, WIDTH)
    return call(
        down_kernel,
        (where, act, mid, small, cotangent, bias, *arrays, *gate_arrays),
        [SMEM, HBM, HBM, VMEM, HBM, VMEM] + [HBM] * 8,
        [
            (rows, BF16, False),
            ((TOKENS, GATE), F32, False),
            ((TOKENS, GATE), BF16, False),
            ((1, GATE), F32, False),
            ((16, 48, 2304), BF16, True),
            ((16, 48, 2304), BF16, True),
        ],
        weight_scratch(HIDDEN, WIDTH)
        + weight_scratch(WIDTH, GATE)
        + lane_scratch(WIDTH, 2304)
        + [
            pltpu.VMEM((TOKENS, HIDDEN), BF16),
            pltpu.VMEM(rows, F32),
            pltpu.VMEM((TOKENS, HEAD), BF16),
            pltpu.VMEM((WIDTH, TOKENS), BF16),
            pltpu.VMEM((TOKENS, GATE), F32),
            pltpu.SemaphoreType.DMA((3,)),
        ],
    )


def head_kernel(where, rows, gate_out, bias, *refs):
    sources, outs, scratch = taken(refs, 8, 1)
    (out,) = outs
    weight, sems, inputs, result, io_sems = scratch
    loads = [block_copies(where, "h", sources, HEAD_PART, weight, sems, side) for side in range(2)]
    row_load = pltpu.make_async_copy(rows, inputs, io_sems.at[0])
    gate_load = pltpu.make_async_copy(gate_out, result.at[:, :GATE], io_sems.at[1])
    row_load.start()
    start_all(loads[0])
    start_all(loads[1])
    gate_load.start()
    row_load.wait()
    stores = []

    def store(span):
        stores.append(
            pltpu.make_async_copy(result.at[:, span], out.at[:, span], io_sems.at[2 + len(stores)])
        )
        stores[-1].start()

    for side in range(2):
        wait_all(loads[side])
        for tile in range(4):
            span = lane_columns(where, side, 2048, GATE + tile * 512, 512)
            columns = lane_columns(where, side, 2048, tile * 512, 512)
            result[:, span] = times(inputs[...], weight[:, columns]) + bias[:, span]
            store(span)
    gate_load.wait()
    store(pl.ds(0, GATE))
    wait_all(stores)


def head_forward(where, rows, gate_out, bias, arrays):
    return call(
        head_kernel,
        (where, rows, gate_out, bias, *arrays),
        [SMEM, HBM, HBM, VMEM] + [HBM] * 8,
        [((TOKENS, HEAD), F32, True)],
        weight_scratch(WIDTH, HEAD - GATE)
        + [
            pltpu.VMEM((TOKENS, WIDTH), BF16),
            pltpu.VMEM((TOKENS, HEAD), F32),
            pltpu.SemaphoreType.DMA((11,)),
        ],
    )[0]


def head_back_kernel(where, act_cotangent, gate_grad, cotangent, slope, *refs):
    sources, gate_sources, down_sources, outs, scratch = taken(refs, 8, 4, 4, 5)
    end_grad, branch, down_bias, up_bias, pre_out = outs
    weight, sems, gate_sems, down, down_sems, scratch = *scratch[:5], scratch[5:]
    act_pulls, pulls, slopes, pre_grad, io_sems, pre_sems = scratch
    loads = [
        block_copies(where, "h", sources, HEAD_PART, weight, sems, side, GATE) for side in range(2)
    ]
    gate_loads = [
        block_copies(where, "u", gate_sources, GATE_PART, weight, gate_sems, side)
        for side in range(2)
    ]
    down_loads = [
        block_copies(where, "d", down_sources, DOWN_PART, down, down_sems, side) for side in range(2)
    ]
    first_loads = [
        pltpu.make_async_copy(act_cotangent, act_pulls, io_sems.at[0]),
        pltpu.make_async_copy(gate_grad, pulls.at[:, :GATE], io_sems.at[1]),
    ]
    pull_load = pltpu.make_async_copy(cotangent.at[:, GATE:], pulls.at[:, GATE:], io_sems.at[2])
    slope_load = pltpu.make_async_copy(slope, slopes, io_sems.at[3])
    start_all(first_loads + gate_loads[0] + gate_loads[1])
    pull_load.start()
    start_all(loads[0])
    start_all(loads[1])
    start_all(down_loads[0] + down_loads[1])
    slope_load.start()
    wait_all(first_loads)
    wait_all(gate_loads[0] + gate_loads[1])
    pull_load.wait()
    wait_all(loads[0] + loads[1])
    end_grad[...] = act_pulls[...].astype(F32) + across(pulls[...], weight[...])
    branch[...] = end_grad[...].astype(BF16)
    down_bias[...] = jnp.sum(branch[...].astype(F32), axis=0, keepdims=True)
    wait_all(down_loads[0] + down_loads[1])
    slope_load.wait()
    stores = []
    for tile in range(6):
        span = slice(tile * 512, tile * 512 + 512)
        grad = across(branch[...], down[span, :])
        rounded = (slopes[:, span].astype(F32) * grad).astype(BF16)
        pre_grad[:, span] = rounded
        up_bias[:, span] = jnp.sum(rounded.astype(F32), axis=0, keepdims=True)
        stores.append(
            pltpu.make_async_copy(pre_grad.at[:, span], pre_out.at[:, span], pre_sems.at[tile])
        )
        stores[-1].start()
    wait_all(stores)


def head_backward(where, act_cotangent, gate_grad, cotangent, slope, arrays, gate_arrays, down_arrays):
    rows, wide = (TOKENS, WIDTH), (TOKENS, HIDDEN)
    return call(
        head_back_kernel,
        (where, act_cotangent, gate_grad, cotangent, slope, *arrays, *gate_arrays, *down_arrays),
        [SMEM, HBM, HBM, HBM, HBM] + [HBM] * 16,
        [
            (rows, F32, False),
            (rows, BF16, False),
            ((1, WIDTH), F32, False),
            ((1, HIDDEN), F32, False),
            (wide, BF16, True),
        ],
        weight_scratch(WIDTH, HEAD)
        + [pltpu.SemaphoreType.DMA((2, 16))]
        + weight_scratch(HIDDEN, WIDTH)
        + [
            pltpu.VMEM(rows, BF16),
            pltpu.VMEM((TOKENS, HEAD), BF16),
            pltpu.VMEM(wide, BF16),
            pltpu.VMEM(wide, BF16),
            pltpu.SemaphoreType.DMA((4,)),
            pltpu.SemaphoreType.DMA((6,)),
        ],
    )


def up_back_kernel(
    where, small, pre_grad, branch, act_turned, mlp_turned, mid, end_grad, *refs
):
    sources, outs, scratch = taken(refs, 4, 7)
    mid_grad, out_grad, terms, down_mine, down_theirs, up_mine, up_theirs = outs
    weight, sems, down_lane, down_sems, up_lane, up_sems, scratch = *scratch[:6], scratch[6:]
    pres, branches, acts, mlps, mids, ends, io_sems = scratch
    loads = [block_copies(where, "u", sources, UP_PART, weight, sems, side) for side in range(2)]
    pre_load = pltpu.make_async_copy(pre_grad, pres, io_sems.at[0])
    branch_load = pltpu.make_async_copy(branch, branches, io_sems.at[1])
    act_load = pltpu.make_async_copy(act_turned, acts, io_sems.at[2])
    mlp_load = pltpu.make_async_copy(mlp_turned, mlps, io_sems.at[3])
    norm_loads = [
        pltpu.make_async_copy(mid, mids, io_sems.at[4]),
        pltpu.make_async_copy(end_grad, ends, io_sems.at[5]),
    ]
    branch_load.start()
    act_load.start()
    pre_load.start()
    mlp_load.start()
    start_all(loads[0] + loads[1])
    start_all(norm_loads)
    branch_load.wait()
    act_load.wait()
    stores = []
    for side, out in ((1, down_theirs), (0, down_mine)):
        span = lane_columns(where, side, 384)
        for part in range(4):
            rows = slice(part * WIDTH, part * WIDTH + WIDTH)
            down_lane[side, rows, :] = times(acts[rows, :], branches[:, span]).astype(BF16)
        copies = term_copies(where, "down", down_lane, out, down_sems, side)
        start_all(copies)
        stores += copies
    pre_load.wait()
    mlp_load.wait()
    for side, out in ((1, up_theirs), (0, up_mine)):
        for tile in range(3):
            span = lane_columns(where, side, 1536, tile * 512, 512)
            up_lane[side, :, tile * 512 : tile * 512 + 512] = times(mlps[...], pres[:, span]).astype(
                BF16
            )
        copies = term_copies(where, "up", up_lane, out, up_sems, side)
        start_all(copies)
        stores += copies
    wait_all(loads[0] + loads[1])
    grad = across(pres[...], weight[...])
    wait_all(norm_loads)
    pulled, gain_grad, shift_grad = norm_backward(mids[...], small[3:4, :], grad)
    pulled = pulled + ends[...]
    rounded = pulled.astype(BF16)
    mid_grad[...] = pulled
    out_grad[...] = rounded
    terms[...] = jnp.zeros_like(terms)
    terms[0:1, :] = jnp.sum(rounded.astype(F32), axis=0, keepdims=True)
    terms[1:2, :] = gain_grad
    terms[2:3, :] = shift_grad
    wait_all(stores)


def up_backward(
    where, small, pre_grad, branch, act_turned, mlp_turned, mid, end_grad, arrays
):
    rows = (TOKENS, WIDTH)
    return call(
        up_back_kernel,
        (where, small, pre_grad, branch, act_turned, mlp_turned, mid, end_grad, *arrays),
        [SMEM, VMEM] + [HBM] * 10,
        [
            (rows, F32, False),
            (rows, BF16, False),
            ((8, WIDTH), F32, False),
            ((16, 192, 384), BF16, True),
            ((16, 192, 384), BF16, True),
            ((16, 48, 1536), BF16, True),
            ((16, 48, 1536), BF16, True),
        ],
        weight_scratch(WIDTH, HIDDEN)
        + lane_scratch(HIDDEN, 384)
        + lane_scratch(WIDTH, 1536)
        + [
            pltpu.VMEM((TOKENS, HIDDEN), BF16),
            pltpu.VMEM(rows, BF16),
            pltpu.VMEM((HIDDEN, TOKENS), BF16),
            pltpu.VMEM((WIDTH, TOKENS), BF16),
            pltpu.VMEM(rows, F32),
            pltpu.VMEM(rows, F32),
            pltpu.SemaphoreType.DMA((6,)),
        ],
    )


def attention_back_kernel(where, lengths, pad, out_grad, qkv, *refs):
    sources, outs, scratch = taken(refs, 4, 1)
    (qkv_grad,) = outs
    weight, sems, bias, mixed, turned, key_sum, value_sum = scratch
    loads = [block_copies(where, "u", sources, OUT_PART, weight, sems, side) for side in range(2)]
    start_all(loads[0] + loads[1])
    fill_bias(lengths, pad, bias)
    wait_all(loads[0] + loads[1])
    mixed[...] = across(out_grad[...], weight[...]).astype(BF16)

    def pair(index, carry):
        first = index * 128
        columns = pl.ds(pl.multiple_of(first, 128), 128)
        keys_at = pl.ds(pl.multiple_of(first + WIDTH, 128), 128)
        values_at = pl.ds(pl.multiple_of(first + 2 * WIDTH, 128), 128)
        keys_turned = qkv[:, keys_at].T
        key_sum[...] = jnp.zeros_like(key_sum)
        value_sum[...] = jnp.zeros_like(value_sum)
        for block, (low, high) in enumerate(KEY_SPANS):
            span = slice(128 * block, 128 * block + 128)
            queries, grads = two_heads(qkv[span, columns]), two_heads(mixed[span, columns])
            scores = across(qkv[low:high, keys_at], queries)
            prob_grads = across(qkv[low:high, values_at], grads)
            allowed = bias[block, : high - low, :]
            probs, score_grads = [], []
            for head in range(2):
                part = slice(128 * head, 128 * head + 128)
                prob = probabilities(scores[:, part], allowed)
                pulled = prob * prob_grads[:, part]
                inner = jnp.sum(pulled, axis=0, keepdims=True)
                probs.append(prob.astype(BF16))
                score_grads.append((pulled - prob * inner).astype(BF16))
            score_grad = jnp.concatenate(score_grads, axis=1)
            key_sum[low:high, :] += times(score_grad, queries)
            value_sum[low:high, :] += times(jnp.concatenate(probs, axis=1), grads)
            turned[:, span] = head_rows_of(times(keys_turned[:, low:high], score_grad)) * score_scale
        qkv_grad[:, columns] = turned[...].T.astype(BF16)
        qkv_grad[:, keys_at] = (key_sum[...] * score_scale).astype(BF16)
        qkv_grad[:, values_at] = value_sum[...].astype(BF16)
        return carry

    lax.fori_loop(0, WIDTH // 128, pair, 0)


def attention_backward(where, lengths, pad, out_grad, qkv, arrays):
    return call(
        attention_back_kernel,
        (where, lengths, pad, out_grad, qkv, *arrays),
        [SMEM, SMEM, VMEM, VMEM, VMEM] + [HBM] * 4,
        [((TOKENS, 3 * WIDTH), BF16, False)],
        weight_scratch(WIDTH, WIDTH)
        + [
            pltpu.VMEM((4, 384, 128), F32),
            pltpu.VMEM((TOKENS, WIDTH), BF16),
            pltpu.VMEM((128, TOKENS), F32),
            pltpu.VMEM((TOKENS, 128), F32),
            pltpu.VMEM((TOKENS, 128), F32),
        ],
    )[0]


def front_back_kernel(
    where, lead, small, terms, down_row, up_rows, head_rows,
    qkv_grad, patches, mid_grad, input_turned, attended_turned, out_grad, *refs
):
    sources, outs, scratch = taken(refs, 4, 3)
    patch_out, mine_out, theirs_out = outs
    weight, sems, lane, lane_sems, scratch = *scratch[:4], scratch[4:]
    pulls, state, mids, inputs, mixes, out_pulls, patch_grad, small_grad, io_sems = scratch
    loads = [block_copies(where, "q", sources, QKV_PART, weight, sems, side) for side in range(2)]
    pairs = (
        (qkv_grad, pulls), (patches, state), (mid_grad, mids),
        (input_turned, inputs), (attended_turned, mixes), (out_grad, out_pulls),
    )
    in_loads = [pltpu.make_async_copy(*pair, io_sems.at[at]) for at, pair in enumerate(pairs)]
    in_loads[0].start()
    start_all(loads[0] + loads[1])
    start_all(in_loads[1:])
    in_loads[0].wait()
    wait_all(loads[0] + loads[1])
    grad = across(pulls[...], weight[...])
    wait_all(in_loads[1:])
    pulled, gain_grad, shift_grad = norm_backward(
        state[...].astype(F32) + small[16:17, :], small[0:1, :], grad
    )
    pulled = pulled + mids[...]
    patch_grad[...] = pulled
    stores = [pltpu.make_async_copy(patch_grad, patch_out, io_sems.at[6])]
    stores[0].start()
    small_grad[0:1, :] = gain_grad
    small_grad[1:2, :] = shift_grad
    small_grad[2:5, :] = terms[0:3, :]
    small_grad[5:6, :] = down_row[...]
    small_grad[6:10, :] = up_rows[...]
    small_grad[10:16, :] = head_rows[...]
    places = lax.broadcasted_iota(jnp.int32, (LEADS, WIDTH), 0)
    lead_grad = jnp.sum(pulled, axis=0, keepdims=True)
    small_grad[16:32, :] = jnp.where(places == lead[0], lead_grad, 0.0)
    for side, out in ((1, theirs_out), (0, mine_out)):
        for tile in range(3):
            span = lane_columns(where, side, 1152, tile * 384, 384)
            lane[side, :, tile * 384 : tile * 384 + 384] = times(inputs[...], pulls[:, span]).astype(
                BF16
            )
        span = lane_columns(where, side, 384)
        lane[side, :, 1152:1536] = times(mixes[...], out_pulls[:, span]).astype(BF16)
        rows = small_grad[pl.ds(pl.multiple_of((where[0] ^ side) * 16, 16), 16), :]
        rows = jnp.concatenate([rows, jnp.zeros((112, WIDTH), F32)], axis=0)
        lane[side, :, 1536:1664] = rows.T.astype(BF16)
        copies = term_copies(where, "front", lane, out, lane_sems, side)
        start_all(copies)
        stores += copies
    wait_all(stores)


def front_backward(
    where, lead, small, terms, down_row, up_rows, head_rows,
    qkv_grad, patches, mid_grad, input_turned, attended_turned, out_grad, arrays,
):
    rows, columns = (TOKENS, WIDTH), (WIDTH, TOKENS)
    return call(
        front_back_kernel,
        (
            where, lead, small, terms, down_row, up_rows, head_rows,
            qkv_grad, patches, mid_grad, input_turned, attended_turned, out_grad, *arrays,
        ),
        [SMEM, SMEM] + [VMEM] * 5 + [HBM] * 10,
        [(rows, F32, True), ((16, 48, 1664), BF16, True), ((16, 48, 1664), BF16, True)],
        weight_scratch(WIDTH, 3 * WIDTH)
        + lane_scratch(WIDTH, 1664)
        + [
            pltpu.VMEM((TOKENS, 3 * WIDTH), BF16),
            pltpu.VMEM(rows, BF16),
            pltpu.VMEM(rows, F32),
            pltpu.VMEM(columns, BF16),
            pltpu.VMEM(columns, BF16),
            pltpu.VMEM(rows, BF16),
            pltpu.VMEM(rows, F32),
            pltpu.VMEM((32, WIDTH), F32),
            pltpu.SemaphoreType.DMA((7,)),
        ],
    )


def rows_of(vector, count):
    return vector.reshape(32, count, 24).transpose(1, 0, 2).reshape(count, WIDTH)


def vector_of(rows):
    count = rows.shape[0]
    return rows.reshape(count, 32, 24).transpose(1, 0, 2).reshape(1, count * WIDTH)


def shards(
    patches,
    lead_index,
    window_lengths,
    pad_mask,
    lead_table,
    attn_gain,
    attn_shift,
    qkv_weight,
    out_weight,
    out_bias,
    mlp_gain,
    mlp_shift,
    up_weight,
    up_bias,
    down_weight,
    down_bias,
    head_weight,
    head_bias,
    act_cotangent,
    head_cotangent,
):
    core, where = whereabouts()
    weights = (qkv_weight, out_weight, up_weight, down_weight, head_weight)
    vectors = (
        attn_gain, attn_shift, out_bias, mlp_gain, mlp_shift, down_bias, up_bias, head_bias
    )
    parts = packed(core, weights, lead_table, vectors)
    pad = pad_mask[:, None]
    cotangent_sum = jnp.sum(head_cotangent[:, GATE:].astype(F32), axis=0, keepdims=True)

    orders = ORDERS
    parts = dict(zip("qudh", zip(parts[:4], parts[4:])))
    chunks = {
        name: in_core_order(core, mine, exchange(theirs, SIBLING), 0)[None]
        for name, (mine, theirs) in parts.items()
    }

    held, last = {}, None
    sequence = "q0 u0 d0 h0 d1 q1 u1 q2 q3 h1 h2 d2 u2 h3".split()
    rest = {}
    for name, step in sequence:
        step = int(step)
        operand = chunks[name] if step == 0 else held[name]
        if last is not None:
            operand = after(operand, last)
        last = operand
        got = exchange(operand, orders[name][step])
        if step == 3:
            rest[name] = got
        elif name == "h" and step == 2:
            h_far = got
        else:
            held[name] = jnp.concatenate([operand, got], axis=0)
    q, u, d, h = [held[name] for name in "qudh"]
    first = both_lanes(q, rest["q"])
    u = after(u, last)
    u_rest = exchange(u, orders["u"][3])
    input_turned, qkv, small_rows = front_forward(
        after(where, d, u, h_far, rest["h"], cotangent_sum), lead_index, patches, first
    )
    attended, attended_turned = attention_forward(where, window_lengths, pad, qkv)
    h_far_rest = exchange(after(h_far, attended), orders["h"][3])
    second = both_lanes(u, after(u_rest, attended))
    d_rest = exchange(after(d, attended), orders["d"][3])
    up_bias_row, head_bias_row = vector_of(small_rows[6:10]), vector_of(small_rows[10:16])
    mid_state, mlp_turned, act_rows, act_turned, slope = up_forward(
        where, attended, patches, small_rows, up_bias_row, second
    )
    down = both_lanes(d, after(d_rest, act_rows))
    outputs, gate_out, gate_grad, gate_bias_sum, mine_h, theirs_h = down_forward(
        where, act_rows, mid_state, small_rows, head_cotangent, head_bias_row, down, second
    )
    head = both_lanes(h, h_far, rest["h"], after(h_far_rest, theirs_h))
    got_h = exchange(theirs_h, SIBLING)
    end_grad, branch_grad, down_bias_sum, up_bias_sum, pre_grad = head_backward(
        after(where, theirs_h), act_cotangent, gate_grad, head_cotangent, slope, head, second, down
    )
    head_rows = rows_of(jnp.concatenate([gate_bias_sum, cotangent_sum], axis=1), 6)
    up_rows = rows_of(up_bias_sum, 4)
    keep_h, send_h = folded(mine_h, after(got_h, pre_grad))
    got_h = exchange(send_h, orders["head"][3])
    mid_grad, out_grad, terms, mine_d, theirs_d, mine_u, theirs_u = up_backward(
        after(where, send_h), small_rows, pre_grad, branch_grad, act_turned, mlp_turned,
        mid_state, end_grad, second,
    )
    got_d, got_u = exchange(theirs_d, SIBLING), exchange(theirs_u, SIBLING)
    keep_u, send_u = folded(mine_u, got_u)
    got_u = exchange(send_u, orders["up"][3])
    keep_d, send_d = folded(mine_d, got_d)
    got_d = exchange(send_d, orders["down"][3])
    keep_h, send_h = folded(keep_h, after(got_h, out_grad))
    got_h = exchange(send_h, orders["head"][2])
    qkv_grad = attention_backward(
        after(where, send_h, send_d, send_u), window_lengths, pad, out_grad, qkv, second
    )
    keep_h, send_h = folded(keep_h, after(got_h, qkv_grad))
    got_h = exchange(send_h, orders["head"][1])
    keep_d, send_d = folded(keep_d, after(got_d, qkv_grad))
    got_d = exchange(send_d, orders["down"][2])
    keep_u, send_u = folded(keep_u, after(got_u, qkv_grad))
    got_u = exchange(send_u, orders["up"][2])
    patch_grad, mine_f, theirs_f = front_backward(
        after(where, send_h, send_d, send_u), lead_index, small_rows, terms, down_bias_sum,
        up_rows, head_rows, qkv_grad, patches, mid_grad, input_turned,
        attended_turned, out_grad, first,
    )
    got_f = exchange(theirs_f, SIBLING)
    keep_f, send_f = folded(mine_f, got_f)
    got_f = exchange(send_f, orders["front"][3])
    keep_u, send_u = folded(keep_u, after(got_u, send_f))
    got_u = exchange(send_u, orders["up"][1])
    keep_h, send_h = folded(keep_h, after(got_h, send_f))
    got_h = exchange(send_h, orders["head"][0])
    keep_d, send_d = folded(keep_d, after(got_d, send_f))
    got_d = exchange(send_d, orders["down"][1])
    head_out = head_forward(
        after(where, send_f, send_u, send_d, send_h), outputs, gate_out, head_bias_row, head
    )
    keep_f, send_f = folded(keep_f, after(got_f, head_out))
    got_f = exchange(send_f, orders["front"][2])
    keep_u, send_u = folded(keep_u, after(got_u, send_f))
    got_u = exchange(send_u, orders["up"][0])
    keep_d, send_d = folded(keep_d, after(got_d, send_f))
    got_d = exchange(send_d, orders["down"][0])
    gate_sum, rest_sum = finished(keep_h, after(got_h, send_f), core, (256, 2048))
    keep_f, send_f = folded(keep_f, got_f)
    got_f = exchange(send_f, orders["front"][1])
    (down_sum,) = finished(keep_d, after(got_d, send_f), core, (384,))
    keep_f, send_f = folded(keep_f, got_f)
    got_f = exchange(send_f, orders["front"][0])
    (up_sum,) = finished(keep_u, after(got_u, send_f), core, (1536,))
    qkv_sum, out_sum, small_sum = finished(keep_f, got_f, core, (1152, 384, 128))
    small_sum = small_sum.T
    return (
        outputs,
        head_out,
        patch_grad,
        small_sum[128:144],
        small_sum[0],
        small_sum[1],
        qkv_sum,
        out_sum,
        small_sum[2],
        small_sum[3],
        small_sum[4],
        up_sum,
        small_sum[6:10].reshape(96),
        down_sum,
        small_sum[5],
        jnp.concatenate([gate_sum, rest_sum], axis=1),
        small_sum[10:16].reshape(144),
    )


def plain_shards(
    patches,
    lead_index,
    window_lengths,
    pad_mask,
    lead_table,
    attn_gain,
    attn_shift,
    qkv_weight,
    out_weight,
    out_bias,
    mlp_gain,
    mlp_shift,
    up_weight,
    up_bias,
    down_weight,
    down_bias,
    head_weight,
    head_bias,
    act_cotangent,
    head_cotangent,
):
    front = (
        lax.all_gather(lead_table, ("dp", "fsdp"), axis=1, tiled=True),
        lax.all_gather(attn_gain, ("dp", "fsdp"), axis=0, tiled=True),
        lax.all_gather(attn_shift, ("dp", "fsdp"), axis=0, tiled=True),
        lax.all_gather(qkv_weight, ("dp", "fsdp"), axis=0, tiled=True),
        lax.all_gather(out_weight, ("dp", "fsdp"), axis=0, tiled=True),
        lax.all_gather(out_bias, ("dp", "fsdp"), axis=0, tiled=True),
    )
    rear = (
        lax.all_gather(mlp_gain, ("dp", "fsdp"), axis=0, tiled=True),
        lax.all_gather(mlp_shift, ("dp", "fsdp"), axis=0, tiled=True),
        lax.all_gather(up_weight, ("dp", "fsdp"), axis=0, tiled=True),
        lax.all_gather(up_bias, ("dp", "fsdp"), axis=0, tiled=True),
        lax.all_gather(down_weight, ("dp", "fsdp"), axis=0, tiled=True),
        lax.all_gather(down_bias, ("dp", "fsdp"), axis=0, tiled=True),
        lax.all_gather(head_weight, ("dp", "fsdp"), axis=0, tiled=True),
        lax.all_gather(head_bias, ("dp", "fsdp"), axis=0, tiled=True),
    )
    table_full, gain_one, shift_one, qkv_full, out_full, out_bias_full = front
    (
        gain_two,
        shift_two,
        up_full,
        up_bias_full,
        down_full,
        down_bias_full,
        head_full,
        head_bias_full,
    ) = rear
    token_rows, width = patches.shape
    head_dim = width // HEADS
    block_rows = min(512, token_rows)
    block_count = token_rows // block_rows
    ends = jnp.cumsum(window_lengths[0])
    positions = jnp.arange(token_rows, dtype=jnp.int32)
    window = jnp.sum((positions[:, None] >= ends[None, :]).astype(jnp.int32), axis=1)
    lead_hot = (jnp.arange(LEADS, dtype=jnp.int32) == lead_index[0]).astype(jnp.float32)
    lead_row = jnp.sum(lead_hot[:, None] * table_full.astype(jnp.float32), axis=0)
    start_state = patches.astype(jnp.float32) + lead_row[None, :]
    normed_one, pull_one = jax.vjp(
        layer_norm, start_state, gain_one.astype(jnp.float32), shift_one.astype(jnp.float32)
    )
    attn_input = normed_one.astype(jnp.bfloat16)
    qkv_rows = jnp.dot(attn_input, qkv_full, preferred_element_type=jnp.float32).astype(
        jnp.bfloat16
    )
    queries = qkv_rows[:, :width].reshape(block_count, block_rows, HEADS, head_dim)
    keys = qkv_rows[:, width : 2 * width].reshape(token_rows, HEADS, head_dim)
    values = qkv_rows[:, 2 * width :].reshape(token_rows, HEADS, head_dim)
    query_windows = window.reshape(block_count, block_rows)
    block_starts = jnp.arange(block_count, dtype=jnp.int32) * block_rows

    def block_scores(query_block, window_block, block_start):
        scores = (
            jnp.einsum("qhd,khd->hqk", query_block, keys, preferred_element_type=jnp.float32)
            * score_scale
        )
        allowed = allowed_keys(window_block, window, pad_mask, block_start)
        return jnp.where(allowed[None], scores, -1e30)

    def forward_block(inputs):
        query_block, window_block, block_start = inputs
        masked = block_scores(query_block, window_block, block_start)
        largest = jnp.max(masked, axis=-1, keepdims=True)
        raised = jnp.exp(masked - largest)
        total = jnp.sum(raised, axis=-1, keepdims=True)
        probs = (raised / total).astype(jnp.bfloat16)
        mixed = jnp.einsum("hqk,khd->qhd", probs, values, preferred_element_type=jnp.float32)
        return (
            mixed.reshape(block_rows, width).astype(jnp.bfloat16),
            (largest + jnp.log(total))[:, :, 0],
        )

    mixed_blocks, log_totals = lax.map(forward_block, (queries, query_windows, block_starts))
    attended = mixed_blocks.reshape(token_rows, width)
    mid_state = (
        start_state
        + jnp.dot(attended, out_full, preferred_element_type=jnp.float32)
        + out_bias_full.astype(jnp.float32)
    )
    normed_two, pull_two = jax.vjp(
        layer_norm, mid_state, gain_two.astype(jnp.float32), shift_two.astype(jnp.float32)
    )
    mlp_input = normed_two.astype(jnp.bfloat16)
    pre_act = jnp.dot(mlp_input, up_full, preferred_element_type=jnp.float32) + up_bias_full.astype(
        jnp.float32
    )
    activated, pull_act = jax.vjp(gelu_exact, pre_act)
    act_rows = activated.astype(jnp.bfloat16)
    end_state = (
        mid_state
        + jnp.dot(act_rows, down_full, preferred_element_type=jnp.float32)
        + down_bias_full.astype(jnp.float32)
    )
    outputs = end_state.astype(jnp.bfloat16)
    logits = jnp.dot(
        outputs, head_full, preferred_element_type=jnp.float32
    ) + head_bias_full.astype(jnp.float32)
    head_out, pull_head = jax.vjp(partial(expert_softmax, experts=EXPERTS, pixels=PIX), logits)
    up_back, down_back, head_back = (
        lax.all_gather(up_weight, ("dp", "fsdp"), axis=0, tiled=True),
        lax.all_gather(down_weight, ("dp", "fsdp"), axis=0, tiled=True),
        lax.all_gather(head_weight, ("dp", "fsdp"), axis=0, tiled=True),
    )
    qkv_back, out_back = (
        lax.all_gather(qkv_weight, ("dp", "fsdp"), axis=0, tiled=True),
        lax.all_gather(out_weight, ("dp", "fsdp"), axis=0, tiled=True),
    )
    logit_grad = pull_head(head_cotangent.astype(jnp.float32))[0].astype(jnp.bfloat16)
    head_bias_term = jnp.sum(logit_grad.astype(jnp.float32), axis=0)
    head_term = jnp.einsum("td,tn->dn", outputs, logit_grad, preferred_element_type=jnp.float32)
    end_grad = act_cotangent.astype(jnp.float32) + jnp.einsum(
        "tn,dn->td", logit_grad, head_back, preferred_element_type=jnp.float32
    )
    branch_grad = end_grad.astype(jnp.bfloat16)
    down_bias_term = jnp.sum(branch_grad.astype(jnp.float32), axis=0)
    down_term = jnp.einsum("tf,td->fd", act_rows, branch_grad, preferred_element_type=jnp.float32)
    act_grad = jnp.einsum("td,fd->tf", branch_grad, down_back, preferred_element_type=jnp.float32)
    pre_grad = pull_act(act_grad)[0].astype(jnp.bfloat16)
    up_bias_term = jnp.sum(pre_grad.astype(jnp.float32), axis=0)
    up_term = jnp.einsum("td,tf->df", mlp_input, pre_grad, preferred_element_type=jnp.float32)
    normed_two_grad = jnp.einsum("tf,df->td", pre_grad, up_back, preferred_element_type=jnp.float32)
    state_grad_two, gain_two_term, shift_two_term = pull_two(normed_two_grad)
    (
        gain_part,
        shift_part,
        up_part,
        up_bias_part,
        down_part,
        down_bias_part,
        head_part,
        head_bias_part,
    ) = (
        lax.psum_scatter(
            gain_two_term.astype(jnp.bfloat16), "dp", scatter_dimension=0, tiled=True
        ).astype(jnp.float32),
        lax.psum_scatter(
            shift_two_term.astype(jnp.bfloat16), "dp", scatter_dimension=0, tiled=True
        ).astype(jnp.float32),
        lax.psum_scatter(
            up_term.astype(jnp.bfloat16), "dp", scatter_dimension=0, tiled=True
        ).astype(jnp.float32),
        lax.psum_scatter(
            up_bias_term.astype(jnp.bfloat16), "dp", scatter_dimension=0, tiled=True
        ).astype(jnp.float32),
        lax.psum_scatter(
            down_term.astype(jnp.bfloat16), "dp", scatter_dimension=0, tiled=True
        ).astype(jnp.float32),
        lax.psum_scatter(
            down_bias_term.astype(jnp.bfloat16), "dp", scatter_dimension=0, tiled=True
        ).astype(jnp.float32),
        lax.psum_scatter(
            head_term.astype(jnp.bfloat16), "dp", scatter_dimension=0, tiled=True
        ).astype(jnp.float32),
        lax.psum_scatter(
            head_bias_term.astype(jnp.bfloat16), "dp", scatter_dimension=0, tiled=True
        ).astype(jnp.float32),
    )
    rear_grads = (
        lax.psum_scatter(gain_part, "fsdp", scatter_dimension=0, tiled=True),
        lax.psum_scatter(shift_part, "fsdp", scatter_dimension=0, tiled=True),
        lax.psum_scatter(up_part, "fsdp", scatter_dimension=0, tiled=True),
        lax.psum_scatter(up_bias_part, "fsdp", scatter_dimension=0, tiled=True),
        lax.psum_scatter(down_part, "fsdp", scatter_dimension=0, tiled=True),
        lax.psum_scatter(down_bias_part, "fsdp", scatter_dimension=0, tiled=True),
        lax.psum_scatter(head_part, "fsdp", scatter_dimension=0, tiled=True),
        lax.psum_scatter(head_bias_part, "fsdp", scatter_dimension=0, tiled=True),
    )
    mid_grad = end_grad + state_grad_two
    out_grad = mid_grad.astype(jnp.bfloat16)
    out_bias_term = jnp.sum(out_grad.astype(jnp.float32), axis=0)
    out_term = jnp.einsum("td,te->de", attended, out_grad, preferred_element_type=jnp.float32)
    mixed_grad = jnp.einsum(
        "te,de->td", out_grad, out_back, preferred_element_type=jnp.float32
    ).astype(jnp.bfloat16)
    grad_blocks = mixed_grad.reshape(block_count, block_rows, HEADS, head_dim)

    def backward_block(carry, inputs):
        key_sum, value_sum = carry
        query_block, grad_block, window_block, total_block, block_start = inputs
        masked = block_scores(query_block, window_block, block_start)
        probs = jnp.exp(masked - total_block[:, :, None])
        prob_grad = jnp.einsum(
            "qhd,khd->hqk", grad_block, values, preferred_element_type=jnp.float32
        )
        inner = jnp.sum(probs * prob_grad, axis=-1, keepdims=True)
        score_grad = (probs * (prob_grad - inner)).astype(jnp.bfloat16)
        query_grad = (
            jnp.einsum("hqk,khd->qhd", score_grad, keys, preferred_element_type=jnp.float32)
            * score_scale
        )
        key_sum = (
            key_sum
            + jnp.einsum(
                "hqk,qhd->khd", score_grad, query_block, preferred_element_type=jnp.float32
            )
            * score_scale
        )
        value_sum = value_sum + jnp.einsum(
            "hqk,qhd->khd",
            probs.astype(jnp.bfloat16),
            grad_block,
            preferred_element_type=jnp.float32,
        )
        return ((key_sum, value_sum), query_grad.reshape(block_rows, width))

    zero_keys = jnp.zeros((token_rows, HEADS, head_dim), jnp.float32)
    (key_grad, value_grad), query_grads = lax.scan(
        backward_block,
        (zero_keys, zero_keys),
        (queries, grad_blocks, query_windows, log_totals, block_starts),
    )
    qkv_grad = jnp.concatenate(
        [
            query_grads.reshape(token_rows, width),
            key_grad.reshape(token_rows, width),
            value_grad.reshape(token_rows, width),
        ],
        axis=1,
    ).astype(jnp.bfloat16)
    qkv_term = jnp.einsum("td,te->de", attn_input, qkv_grad, preferred_element_type=jnp.float32)
    normed_one_grad = jnp.einsum(
        "te,de->td", qkv_grad, qkv_back, preferred_element_type=jnp.float32
    )
    state_grad_one, gain_one_term, shift_one_term = pull_one(normed_one_grad)
    patch_grad = mid_grad + state_grad_one
    lead_term = lead_hot[:, None] * jnp.sum(patch_grad, axis=0)[None, :]
    lead_part, gain_one_part, shift_one_part, qkv_part, out_part, out_bias_part = (
        lax.psum_scatter(
            lead_term.astype(jnp.bfloat16), "dp", scatter_dimension=1, tiled=True
        ).astype(jnp.float32),
        lax.psum_scatter(
            gain_one_term.astype(jnp.bfloat16), "dp", scatter_dimension=0, tiled=True
        ).astype(jnp.float32),
        lax.psum_scatter(
            shift_one_term.astype(jnp.bfloat16), "dp", scatter_dimension=0, tiled=True
        ).astype(jnp.float32),
        lax.psum_scatter(
            qkv_term.astype(jnp.bfloat16), "dp", scatter_dimension=0, tiled=True
        ).astype(jnp.float32),
        lax.psum_scatter(
            out_term.astype(jnp.bfloat16), "dp", scatter_dimension=0, tiled=True
        ).astype(jnp.float32),
        lax.psum_scatter(
            out_bias_term.astype(jnp.bfloat16), "dp", scatter_dimension=0, tiled=True
        ).astype(jnp.float32),
    )
    front_grads = (
        lax.psum_scatter(lead_part, "fsdp", scatter_dimension=1, tiled=True),
        lax.psum_scatter(gain_one_part, "fsdp", scatter_dimension=0, tiled=True),
        lax.psum_scatter(shift_one_part, "fsdp", scatter_dimension=0, tiled=True),
        lax.psum_scatter(qkv_part, "fsdp", scatter_dimension=0, tiled=True),
        lax.psum_scatter(out_part, "fsdp", scatter_dimension=0, tiled=True),
        lax.psum_scatter(out_bias_part, "fsdp", scatter_dimension=0, tiled=True),
    )
    return (
        outputs,
        head_out,
        patch_grad,
        front_grads[0],
        front_grads[1],
        front_grads[2],
        front_grads[3],
        front_grads[4],
        front_grads[5],
        rear_grads[0],
        rear_grads[1],
        rear_grads[2],
        rear_grads[3],
        rear_grads[4],
        rear_grads[5],
        rear_grads[6],
        rear_grads[7],
    )


def solution(mesh):
    in_specs = (
        P(("dp", "fsdp"), None),
        P(("dp", "fsdp")),
        P(("dp", "fsdp"), None),
        P(("dp", "fsdp")),
        P(None, ("dp", "fsdp")),
        P(("dp", "fsdp")),
        P(("dp", "fsdp")),
        P(("dp", "fsdp"), None),
        P(("dp", "fsdp"), None),
        P(("dp", "fsdp")),
        P(("dp", "fsdp")),
        P(("dp", "fsdp")),
        P(("dp", "fsdp"), None),
        P(("dp", "fsdp")),
        P(("dp", "fsdp"), None),
        P(("dp", "fsdp")),
        P(("dp", "fsdp"), None),
        P(("dp", "fsdp")),
        P(("dp", "fsdp"), None),
        P(("dp", "fsdp"), None),
    )
    out_specs = (
        P(("dp", "fsdp"), None),
        P(("dp", "fsdp"), None),
        P(("dp", "fsdp"), None),
        P(None, ("dp", "fsdp")),
        P(("dp", "fsdp")),
        P(("dp", "fsdp")),
        P(("dp", "fsdp"), None),
        P(("dp", "fsdp"), None),
        P(("dp", "fsdp")),
        P(("dp", "fsdp")),
        P(("dp", "fsdp")),
        P(("dp", "fsdp"), None),
        P(("dp", "fsdp")),
        P(("dp", "fsdp"), None),
        P(("dp", "fsdp")),
        P(("dp", "fsdp"), None),
        P(("dp", "fsdp")),
    )
    body = shards if dict(mesh.shape) == {"dp": 4, "fsdp": 8} else plain_shards
    return jax.shard_map(body, mesh=mesh, in_specs=in_specs, out_specs=out_specs, check_vma=False)
```

```python
from functools import partial

import jax
import jax.numpy as jnp
from jax import lax
from jax.experimental import pallas as pl
from jax.experimental.pallas import tpu as pltpu
from jax.sharding import PartitionSpec as P

HEADS = 12
PIX = 64
EXPERTS = 3
LEADS = 16


norm_epsilon = 1e-05
score_scale = 0.125


def layer_norm(hidden, norm_gain, norm_shift):
    average = jnp.mean(hidden, axis=-1, keepdims=True)
    centered = hidden - average
    variance = jnp.mean(centered * centered, axis=-1, keepdims=True)
    return centered * lax.rsqrt(variance + norm_epsilon) * norm_gain + norm_shift


def gelu_exact(values):
    return 0.5 * values * (1.0 + lax.erf(values * 0.7071067811865476))


def expert_softmax(logits, experts, pixels):
    gate_part = logits[:, : experts * pixels].reshape(logits.shape[0], experts, pixels)
    largest = jnp.max(gate_part, axis=1, keepdims=True)
    raised = jnp.exp(gate_part - largest)
    shares = raised / jnp.sum(raised, axis=1, keepdims=True)
    return jnp.concatenate(
        [shares.reshape(logits.shape[0], experts * pixels), logits[:, experts * pixels :]], axis=1
    )


def allowed_keys(query_window, key_window, key_valid, query_start):
    query_place = query_start + jnp.arange(query_window.shape[0], dtype=jnp.int32)
    key_place = jnp.arange(key_window.shape[0], dtype=jnp.int32)
    same_window = query_window[:, None] == key_window[None, :]
    usable = (key_valid[None, :] > 0) | (query_place[:, None] == key_place[None, :])
    return same_window & usable


AXES = ("dp", "fsdp")
FAR_Z, NEAR_Z, FIRST, SECOND, SIBLING = (4, 4), (2, 2), (8, 16), (16, 8), (1, 1)
ORDERS = {
    "q": (FAR_Z, NEAR_Z, FIRST, SECOND),
    "u": (FAR_Z, FIRST, SECOND, NEAR_Z),
    "d": (FIRST, FAR_Z, NEAR_Z, SECOND),
    "h": (NEAR_Z, FAR_Z, FIRST, SECOND),
    "head": (FAR_Z, NEAR_Z, FIRST, SECOND),
    "down": (FAR_Z, NEAR_Z, FIRST, SECOND),
    "up": (FAR_Z, FIRST, SECOND, NEAR_Z),
    "front": (FAR_Z, NEAR_Z, FIRST, SECOND),
}
GATHER_SEQUENCE = (
    ("q", 0), ("d", 0), ("h", 0), ("u", 0), ("q", 1), ("d", 1), ("u", 1), ("q", 2), ("h", 1), ("u", 2),
    ("d", 2),
)
WIDTH = 768
HIDDEN = 3072
HEAD = 4608
TOKENS = 512
GATE = 512
F32 = jnp.float32
BF16 = jnp.bfloat16
HBM = pl.BlockSpec(memory_space=pltpu.HBM)
SMEM = pl.BlockSpec(memory_space=pltpu.SMEM)
VMEM = pl.BlockSpec(memory_space=pltpu.VMEM)
QKV_PART, SMALL_PART = (0, 1152), (1152, 128)
UP_PART, OUT_PART, GATE_PART = (0, 1536), (1536, 384), (1920, 256)
DOWN_PART, HEAD_PART = (0, 384), (0, 2048)


def chip_masks(order, lane):
    masks = []
    for place in range(16):
        mask = 0
        for step in range(4):
            if place >> step & 1:
                mask ^= order[step][lane]
        masks.append(mask >> 1)
    return masks


def table_start(group, side):
    return 1 + 32 * list(ORDERS).index(group) + 16 * side


def exchange(array, masks):
    return lax.ppermute(array, AXES, [(d, d ^ masks[d & 1]) for d in range(32)])


def whereabouts():
    device = lax.axis_index("dp") * 8 + lax.axis_index("fsdp")
    core, chip = device % 2, device // 2
    tables = [chip_masks(order, 0) + chip_masks(order, 1) for order in ORDERS.values()]
    swapped = [chip_masks(order, 1) + chip_masks(order, 0) for order in ORDERS.values()]
    places = jnp.where(core == 0, jnp.array(tables, jnp.int32), jnp.array(swapped, jnp.int32))
    places = (places ^ chip).reshape(32 * len(ORDERS))
    return core, jnp.concatenate([core[None].astype(jnp.int32), places])


def after(value, *marks):
    return lax.optimization_barrier((value, marks))[0]


def in_core_order(core, mine, theirs, axis):
    return jnp.where(
        core == 0,
        jnp.concatenate([mine, theirs], axis=axis),
        jnp.concatenate([theirs, mine], axis=axis),
    )


def pack_kernel(core, qkv, out, up, down, head, table, *refs):
    vectors, (up_bias, head_bias), refs = refs[:6], refs[6:8], refs[8:]
    outs, (rows,) = refs[:8], refs[8:]
    rows[...] = jnp.zeros_like(rows)
    for index, vector in enumerate(vectors):
        rows[index : index + 1, :24] = vector[...].astype(F32)
    for index in range(4):
        rows[6 + index : 7 + index, :24] = up_bias[:, 24 * index : 24 * index + 24].astype(F32)
    for index in range(6):
        rows[10 + index : 11 + index, :24] = head_bias[:, 24 * index : 24 * index + 24].astype(F32)
    rows[16:32, :24] = table[...].astype(F32)
    small = rows[...].T[:24].astype(BF16)
    for side in range(2):
        q, u, d, h = outs[4 * side : 4 * side + 4]
        q[:, :1152] = qkv[:, lane_columns(core, side, 1152)]
        q[:, 1152:] = small
        u[:, :1536] = up[:, lane_columns(core, side, 1536)]
        u[:, 1536:1920] = out[:, lane_columns(core, side, 384)]
        u[:, 1920:] = head[:, lane_columns(core, side, 256)]
        d[...] = down[:, lane_columns(core, side, 384)]
        h[...] = head[:, lane_columns(core, side, 2048, GATE)]


def packed(core, weights, table, vectors):
    shapes = [(24, 1280), (24, 2176), (96, 384), (24, 2048)] * 2
    return call(
        pack_kernel,
        (core.reshape(1), *weights, table, *[vector[None] for vector in vectors]),
        [SMEM] + [VMEM] * 14,
        [(shape, BF16, False) for shape in shapes],
        [pltpu.VMEM((128, 128), F32)],
    )


def doubled(held, masks):
    return jnp.concatenate([held, exchange(held, masks)], axis=0)


def both_lanes(*arrays):
    return arrays + tuple(exchange(array, SIBLING) for array in arrays)


def total(first, second):
    return first.astype(F32) + second.astype(F32)


def folded(keep, got, start=0):
    half = got.shape[0] // 2
    send = total(keep[half:], got[half:]).astype(BF16)
    return total(keep[:half], got[:half]).astype(BF16), send


def finished(keep, got, core, widths):
    block = total(keep, got)[0]
    rows = block.shape[0] // 2
    upper, lower = block[:rows], block[rows:]
    mine = jnp.where(core == 0, upper, lower)
    theirs = jnp.where(core == 0, lower, upper).astype(BF16)
    other = exchange(theirs, SIBLING).astype(F32)
    pieces, start = [], 0
    for width in widths:
        span = slice(start, start + width)
        pieces.append(in_core_order(core, mine[:, span], other[:, span], 1))
        start += width
    return pieces


def across(first, second):
    return lax.dot_general(first, second, (((1,), (1,)), ((), ())), preferred_element_type=F32)


def times(first, second):
    return jnp.dot(first, second, preferred_element_type=F32)


def lane_columns(where, side, stride, first=0, width=None):
    return pl.ds(pl.multiple_of(first + (where[0] ^ side) * stride, 128), width or stride)


def block_copies(where, group, sources, part, target, sems, side, first=0):
    start, width = part
    rows = sources[0].shape[1]
    half = len(sources) // 2
    count = 16 // half
    copies = []
    for place in range(16):
        row = pl.multiple_of(where[table_start(group, side) + place] * rows, rows)
        copies.append(
            pltpu.make_async_copy(
                sources[half * side + place // count].at[place % count, :, pl.ds(start, width)],
                target.at[pl.ds(row, rows), lane_columns(where, side, width, first)],
                sems.at[side, place],
            )
        )
    return copies


def term_copies(where, group, lane, out, sems, side):
    rows = out.shape[1]
    copies = []
    for place in range(16):
        row = pl.multiple_of(where[table_start(group, side) + place] * rows, rows)
        copies.append(
            pltpu.make_async_copy(lane.at[side, pl.ds(row, rows), :], out.at[place], sems.at[side, place])
        )
    return copies


def start_all(copies):
    for copy in copies:
        copy.start()


def wait_all(copies):
    for copy in copies:
        copy.wait()


def mean_and_scale(hidden):
    average = jnp.mean(hidden, axis=1, keepdims=True)
    centered = hidden - average
    variance = jnp.mean(centered * centered, axis=1, keepdims=True)
    return centered, lax.rsqrt(variance + norm_epsilon)


def norm_backward(hidden, gain, upstream):
    centered, scale = mean_and_scale(hidden)
    normed = centered * scale
    gain_grad = jnp.sum(upstream * normed, axis=0, keepdims=True)
    shift_grad = jnp.sum(upstream, axis=0, keepdims=True)
    scaled = upstream * gain
    first = jnp.mean(scaled, axis=1, keepdims=True)
    second = jnp.mean(scaled * normed, axis=1, keepdims=True)
    return scale * (scaled - first - normed * second), gain_grad, shift_grad


def call(kernel, operands, in_specs, outs, scratch):
    return pl.pallas_call(
        kernel,
        out_shape=[jax.ShapeDtypeStruct(shape, kind) for shape, kind, _ in outs],
        in_specs=in_specs,
        out_specs=[HBM if copied else VMEM for _, _, copied in outs],
        scratch_shapes=scratch,
        compiler_params=pltpu.CompilerParams(vmem_limit_bytes=56 * 1024 * 1024),
        cost_estimate=pl.CostEstimate(flops=2 * 10**12, bytes_accessed=10**10, transcendentals=0),
    )(*operands)


def lane_scratch(rows, width):
    return [pltpu.VMEM((2, rows, width), BF16), pltpu.SemaphoreType.DMA((2, 16))]


def weight_scratch(rows, width):
    return [pltpu.VMEM((rows, width), BF16), pltpu.SemaphoreType.DMA((2, 16))]


def taken(refs, *counts):
    groups = []
    for count in counts:
        groups.append(refs[:count])
        refs = refs[count:]
    return *groups, refs


def front_kernel(where, lead, patches, *refs):
    sources, outs, scratch = taken(refs, 4, 3)
    turned_out, qkv_out, small = outs
    weight, sems, smalls, small_sems, state, rows, turned, qkv, io_sems = scratch
    loads = [block_copies(where, "q", sources, QKV_PART, weight, sems, side) for side in range(2)]
    small_loads = []
    for place in range(16):
        row = pl.multiple_of(where[table_start("q", 0) + place] * 48, 48)
        small_loads.append(
            pltpu.make_async_copy(
                sources[place // 8].at[place % 8, :, pl.ds(*SMALL_PART)],
                smalls.at[pl.ds(row, 48), :],
                small_sems.at[place],
            )
        )
    state_load = pltpu.make_async_copy(patches, state, io_sems.at[0])
    start_all(small_loads)
    state_load.start()
    start_all(loads[0])
    start_all(loads[1])
    wait_all(small_loads)
    columns = smalls[...].astype(F32).T
    places = lax.broadcasted_iota(jnp.int32, (LEADS, WIDTH), 0)
    lead_row = jnp.sum(
        jnp.where(places == lead[0], columns[16 : 16 + LEADS], 0.0), axis=0, keepdims=True
    )
    small[...] = columns[:32]
    small[16:17, :] = lead_row
    state_load.wait()
    centered, scale = mean_and_scale(state[...].astype(F32) + lead_row)
    rows[...] = (centered * scale * columns[0:1] + columns[1:2]).astype(BF16)
    turned[...] = rows[...].T
    stores = [pltpu.make_async_copy(turned, turned_out, io_sems.at[1])]
    stores[0].start()
    wait_all(loads[0] + loads[1])
    for part in range(3):
        span = slice(part * WIDTH, part * WIDTH + WIDTH)
        qkv[:, span] = times(rows[...], weight[:, span]).astype(BF16)
        stores.append(pltpu.make_async_copy(qkv.at[:, span], qkv_out.at[:, span], io_sems.at[2 + part]))
        stores[-1].start()
    wait_all(stores)


def front_forward(where, lead_index, patches, arrays):
    return call(
        front_kernel,
        (where, lead_index, patches, *arrays),
        [SMEM, SMEM, HBM] + [HBM] * 4,
        [
            ((WIDTH, TOKENS), BF16, True),
            ((TOKENS, 3 * WIDTH), BF16, True),
            ((32, WIDTH), F32, False),
        ],
        weight_scratch(WIDTH, 3 * WIDTH)
        + [pltpu.VMEM((WIDTH, 128), BF16), pltpu.SemaphoreType.DMA((16,))]
        + [
            pltpu.VMEM((TOKENS, WIDTH), BF16),
            pltpu.VMEM((TOKENS, WIDTH), BF16),
            pltpu.VMEM((WIDTH, TOKENS), BF16),
            pltpu.VMEM((TOKENS, 3 * WIDTH), BF16),
            pltpu.SemaphoreType.DMA((5,)),
        ],
    )


KEY_SPANS = ((0, 256), (0, 384), (128, 512), (256, 512))


def fill_bias(lengths, pad, bias):
    ends, end = [], 0
    for index in range(lengths.shape[1]):
        end = end + lengths[0, index]
        ends.append(end)

    def windows(places):
        return sum([(places >= end).astype(jnp.int32) for end in ends])

    for block, (low, high) in enumerate(KEY_SPANS):
        count = high - low
        queries = lax.broadcasted_iota(jnp.int32, (1, 128), 1) + 128 * block
        keys = lax.broadcasted_iota(jnp.int32, (count, 1), 0) + low
        same = windows(queries) == windows(keys)
        usable = (pad[low:high, :] > 0) | (queries == keys)
        bias[block, :count, :] = jnp.where(same & usable, 0.0, -1e30)


def two_heads(block):
    first = lax.broadcasted_iota(jnp.int32, block.shape, 1) < block.shape[1] // 2
    zero = jnp.zeros_like(block)
    return jnp.concatenate([jnp.where(first, block, zero), jnp.where(first, zero, block)], axis=0)


def head_rows_of(stacked):
    return jnp.concatenate([stacked[:64, :128], stacked[64:, 128:]], axis=0)


def probabilities(scores, allowed):
    masked = scores * score_scale + allowed
    raised = jnp.exp(masked - jnp.max(masked, axis=0, keepdims=True))
    return raised * (1.0 / jnp.sum(raised, axis=0, keepdims=True))


def attention_kernel(where, lengths, pad, qkv, attended_out, turned_out, bias, turned, rows, sems):
    fill_bias(lengths, pad, bias)

    def pair(index, carry):
        first = index * 128
        columns = pl.ds(pl.multiple_of(first, 128), 128)
        keys_at = pl.ds(pl.multiple_of(first + WIDTH, 128), 128)
        values = qkv[:, pl.ds(pl.multiple_of(first + 2 * WIDTH, 128), 128)].T
        for block, (low, high) in enumerate(KEY_SPANS):
            span = slice(128 * block, 128 * block + 128)
            scores = across(qkv[low:high, keys_at], two_heads(qkv[span, columns]))
            allowed = bias[block, : high - low, :]
            probs = [
                probabilities(scores[:, 128 * head : 128 * head + 128], allowed).astype(BF16)
                for head in range(2)
            ]
            mixed = times(values[:, low:high], jnp.concatenate(probs, axis=1))
            turned[columns, span] = head_rows_of(mixed).astype(BF16)
        return carry

    lax.fori_loop(0, WIDTH // 128, pair, 0)
    stores = [pltpu.make_async_copy(turned, turned_out, sems.at[0])]
    stores[0].start()
    rows[...] = turned[...].T
    stores.append(pltpu.make_async_copy(rows, attended_out, sems.at[1]))
    stores[1].start()
    wait_all(stores)


def attention_forward(where, lengths, pad, qkv):
    rows, columns = (TOKENS, WIDTH), (WIDTH, TOKENS)
    return call(
        attention_kernel,
        (where, lengths, pad, qkv),
        [SMEM, SMEM, VMEM, VMEM],
        [(rows, BF16, True), (columns, BF16, True)],
        [
            pltpu.VMEM((4, 384, 128), F32),
            pltpu.VMEM(columns, BF16),
            pltpu.VMEM(rows, BF16),
            pltpu.SemaphoreType.DMA((2,)),
        ],
    )


def up_kernel(where, attended, patches, small, bias, *refs):
    sources, outs, scratch = taken(refs, 4, 5)
    mid_out, mlp_turned_out, act_out, act_turned_out, slope_out = outs
    out_weight, out_sems, weight, sems, scratch = *scratch[:4], scratch[4:]
    inputs, state, mid, rows, mlp_turned, act, act_turned, slope, io_sems, act_sems = scratch
    out_loads = [block_copies(where, "u", sources, OUT_PART, out_weight, out_sems, s) for s in range(2)]
    loads = [block_copies(where, "u", sources, UP_PART, weight, sems, side) for side in range(2)]
    in_loads = [
        pltpu.make_async_copy(attended, inputs, io_sems.at[0]),
        pltpu.make_async_copy(patches, state, io_sems.at[1]),
    ]
    start_all(in_loads)
    start_all(out_loads[0] + out_loads[1])
    start_all(loads[0] + loads[1])
    wait_all(in_loads)
    wait_all(out_loads[0] + out_loads[1])
    mid[...] = (
        state[...].astype(F32)
        + small[16:17, :]
        + times(inputs[...], out_weight[...])
        + small[2:3, :]
    )
    centered, scale = mean_and_scale(mid[...])
    rows[...] = (centered * scale * small[3:4, :] + small[4:5, :]).astype(BF16)
    mlp_turned[...] = rows[...].T
    stores = [
        pltpu.make_async_copy(mid, mid_out, io_sems.at[2]),
        pltpu.make_async_copy(mlp_turned, mlp_turned_out, io_sems.at[3]),
    ]
    start_all(stores)
    wait_all(loads[0] + loads[1])
    for slot in range(6):
        span = slice(slot * 512, slot * 512 + 512)
        values = times(rows[...], weight[:, span]) + bias[:, span]
        share = 0.5 * (1.0 + lax.erf(values * 0.7071067811865476))
        density = jnp.exp(-0.5 * values * values) * 0.3989422804014327
        activated = (values * share).astype(BF16)
        act[:, span] = activated
        act_turned[span, :] = activated.T
        slope[:, span] = (share + values * density).astype(BF16)
        copies = [
            pltpu.make_async_copy(act.at[:, span], act_out.at[:, span], act_sems.at[slot, 0]),
            pltpu.make_async_copy(
                act_turned.at[span, :], act_turned_out.at[span, :], act_sems.at[slot, 1]
            ),
            pltpu.make_async_copy(slope.at[:, span], slope_out.at[:, span], act_sems.at[slot, 2]),
        ]
        start_all(copies)
        stores += copies
    wait_all(stores)


def up_forward(where, attended, patches, small, bias, arrays):
    rows, columns = (TOKENS, WIDTH), (WIDTH, TOKENS)
    wide, tall = (TOKENS, HIDDEN), (HIDDEN, TOKENS)
    return call(
        up_kernel,
        (where, attended, patches, small, bias, *arrays),
        [SMEM, HBM, HBM, VMEM, VMEM] + [HBM] * 4,
        [
            (rows, F32, True),
            (columns, BF16, True),
            (wide, BF16, True),
            (tall, BF16, True),
            (wide, BF16, True),
        ],
        weight_scratch(WIDTH, WIDTH)
        + weight_scratch(WIDTH, HIDDEN)
        + [
            pltpu.VMEM(rows, BF16),
            pltpu.VMEM(rows, BF16),
            pltpu.VMEM(rows, F32),
            pltpu.VMEM(rows, BF16),
            pltpu.VMEM(columns, BF16),
            pltpu.VMEM(wide, BF16),
            pltpu.VMEM(tall, BF16),
            pltpu.VMEM(wide, BF16),
            pltpu.SemaphoreType.DMA((4,)),
            pltpu.SemaphoreType.DMA((6, 3)),
        ],
    )


def gate_shares(logits, cotangent, shares, gate_grad):
    shares[:, 256:] = logits[:, 256:]
    gate_grad[:, 256:] = cotangent[:, 256:GATE]
    first, rest = logits[:, :128], logits[:, 128:256]
    left = lax.broadcasted_iota(jnp.int32, first.shape, 1) < PIX
    third = jnp.where(left, rest, pltpu.roll(rest, PIX, 1))
    largest = jnp.maximum(jnp.maximum(first, pltpu.roll(first, PIX, 1)), third)
    raised, raised_third = jnp.exp(first - largest), jnp.exp(third - largest)
    scale = 1.0 / (raised + pltpu.roll(raised, PIX, 1) + raised_third)
    share, share_third = raised * scale, raised_third * scale
    shares[:, :128] = share
    shares[:, 128:256] = jnp.where(left, share_third, rest)
    pull, other = cotangent[:, :128].astype(F32), cotangent[:, 128:256].astype(F32)
    pull_third = jnp.where(left, other, pltpu.roll(other, PIX, 1))
    weighed = share * pull
    inner = weighed + pltpu.roll(weighed, PIX, 1) + share_third * pull_third
    gate_grad[:, :128] = (share * (pull - inner)).astype(BF16)
    gate_grad[:, 128:256] = jnp.where(left, share_third * (pull_third - inner), other).astype(BF16)


def down_kernel(where, act, mid, small, cotangent, bias, *refs):
    sources, gate_sources, outs, scratch = taken(refs, 4, 4, 6)
    outputs, shares, gate_grad, gate_bias, mine_out, theirs_out = outs
    weight, sems, gate, gate_sems, lane, lane_sems, scratch = *scratch[:6], scratch[6:]
    acts, mids, pulls, turned, logits, io_sems = scratch
    loads = [block_copies(where, "d", sources, DOWN_PART, weight, sems, side) for side in range(2)]
    gate_loads = [
        block_copies(where, "u", gate_sources, GATE_PART, gate, gate_sems, side) for side in range(2)
    ]
    in_loads = [
        pltpu.make_async_copy(act, acts, io_sems.at[0]),
        pltpu.make_async_copy(mid, mids, io_sems.at[1]),
    ]
    pull_load = pltpu.make_async_copy(cotangent, pulls, io_sems.at[2])
    start_all(in_loads)
    start_all(loads[0] + loads[1])
    start_all(gate_loads[0] + gate_loads[1])
    pull_load.start()
    wait_all(in_loads)
    wait_all(loads[0] + loads[1])
    outputs[...] = (mids[...] + times(acts[...], weight[...]) + small[5:6, :]).astype(BF16)
    turned[...] = outputs[...].T
    wait_all(gate_loads[0] + gate_loads[1])
    logits[...] = times(outputs[...], gate[...]) + bias[:, :GATE]
    pull_load.wait()
    gate_shares(logits, pulls, shares, gate_grad)
    gate_bias[...] = jnp.sum(gate_grad[...].astype(F32), axis=0, keepdims=True)
    stores = []
    for side, out in ((1, theirs_out), (0, mine_out)):
        lane[side, :, :256] = times(
            turned[...], gate_grad[:, lane_columns(where, side, 256)]
        ).astype(BF16)
        for tile in range(4):
            span = lane_columns(where, side, 2048, GATE + tile * 512, 512)
            lane[side, :, 256 + tile * 512 : 768 + tile * 512] = times(
                turned[...], pulls[:, span]
            ).astype(BF16)
        copies = term_copies(where, "head", lane, out, lane_sems, side)
        start_all(copies)
        stores += copies
    wait_all(stores)


def down_forward(where, act, mid, small, cotangent, bias, arrays, gate_arrays):
    rows = (TOKENS, WIDTH)
    return call(
        down_kernel,
        (where, act, mid, small, cotangent, bias, *arrays, *gate_arrays),
        [SMEM, HBM, HBM, VMEM, HBM, VMEM] + [HBM] * 8,
        [
            (rows, BF16, False),
            ((TOKENS, GATE), F32, False),
            ((TOKENS, GATE), BF16, False),
            ((1, GATE), F32, False),
            ((16, 48, 2304), BF16, True),
            ((16, 48, 2304), BF16, True),
        ],
        weight_scratch(HIDDEN, WIDTH)
        + weight_scratch(WIDTH, GATE)
        + lane_scratch(WIDTH, 2304)
        + [
            pltpu.VMEM((TOKENS, HIDDEN), BF16),
            pltpu.VMEM(rows, F32),
            pltpu.VMEM((TOKENS, HEAD), BF16),
            pltpu.VMEM((WIDTH, TOKENS), BF16),
            pltpu.VMEM((TOKENS, GATE), F32),
            pltpu.SemaphoreType.DMA((3,)),
        ],
    )


def head_kernel(where, rows, gate_out, bias, *refs):
    sources, outs, scratch = taken(refs, 4, 1)
    (out,) = outs
    weight, sems, inputs, result, io_sems = scratch
    loads = [block_copies(where, "h", sources, HEAD_PART, weight, sems, side) for side in range(2)]
    row_load = pltpu.make_async_copy(rows, inputs, io_sems.at[0])
    gate_load = pltpu.make_async_copy(gate_out, result.at[:, :GATE], io_sems.at[1])
    row_load.start()
    start_all(loads[0])
    start_all(loads[1])
    gate_load.start()
    row_load.wait()
    stores = []

    def store(span):
        stores.append(
            pltpu.make_async_copy(result.at[:, span], out.at[:, span], io_sems.at[2 + len(stores)])
        )
        stores[-1].start()

    for side in range(2):
        wait_all(loads[side])
        for tile in range(4):
            span = lane_columns(where, side, 2048, GATE + tile * 512, 512)
            columns = lane_columns(where, side, 2048, tile * 512, 512)
            result[:, span] = times(inputs[...], weight[:, columns]) + bias[:, span]
            store(span)
    gate_load.wait()
    store(pl.ds(0, GATE))
    wait_all(stores)


def head_forward(where, rows, gate_out, bias, arrays):
    return call(
        head_kernel,
        (where, rows, gate_out, bias, *arrays),
        [SMEM, HBM, HBM, VMEM] + [HBM] * 4,
        [((TOKENS, HEAD), F32, True)],
        weight_scratch(WIDTH, HEAD - GATE)
        + [
            pltpu.VMEM((TOKENS, WIDTH), BF16),
            pltpu.VMEM((TOKENS, HEAD), F32),
            pltpu.SemaphoreType.DMA((11,)),
        ],
    )[0]


def head_back_kernel(where, act_cotangent, gate_grad, cotangent, slope, *refs):
    sources, gate_sources, down_sources, outs, scratch = taken(refs, 4, 4, 4, 5)
    end_grad, branch, down_bias, up_bias, pre_out = outs
    weight, sems, gate_sems, down, down_sems, scratch = *scratch[:5], scratch[5:]
    act_pulls, pulls, slopes, pre_grad, io_sems, pre_sems = scratch
    loads = [
        block_copies(where, "h", sources, HEAD_PART, weight, sems, side, GATE) for side in range(2)
    ]
    gate_loads = [
        block_copies(where, "u", gate_sources, GATE_PART, weight, gate_sems, side)
        for side in range(2)
    ]
    down_loads = [
        block_copies(where, "d", down_sources, DOWN_PART, down, down_sems, side) for side in range(2)
    ]
    first_loads = [
        pltpu.make_async_copy(act_cotangent, act_pulls, io_sems.at[0]),
        pltpu.make_async_copy(gate_grad, pulls.at[:, :GATE], io_sems.at[1]),
    ]
    pull_load = pltpu.make_async_copy(cotangent.at[:, GATE:], pulls.at[:, GATE:], io_sems.at[2])
    slope_load = pltpu.make_async_copy(slope, slopes, io_sems.at[3])
    start_all(first_loads + gate_loads[0] + gate_loads[1])
    pull_load.start()
    start_all(loads[0])
    start_all(loads[1])
    start_all(down_loads[0] + down_loads[1])
    slope_load.start()
    wait_all(first_loads)
    wait_all(gate_loads[0] + gate_loads[1])
    pull_load.wait()
    wait_all(loads[0] + loads[1])
    end_grad[...] = act_pulls[...].astype(F32) + across(pulls[...], weight[...])
    branch[...] = end_grad[...].astype(BF16)
    down_bias[...] = jnp.sum(branch[...].astype(F32), axis=0, keepdims=True)
    wait_all(down_loads[0] + down_loads[1])
    slope_load.wait()
    stores = []
    for tile in range(6):
        span = slice(tile * 512, tile * 512 + 512)
        grad = across(branch[...], down[span, :])
        rounded = (slopes[:, span].astype(F32) * grad).astype(BF16)
        pre_grad[:, span] = rounded
        up_bias[:, span] = jnp.sum(rounded.astype(F32), axis=0, keepdims=True)
        stores.append(
            pltpu.make_async_copy(pre_grad.at[:, span], pre_out.at[:, span], pre_sems.at[tile])
        )
        stores[-1].start()
    wait_all(stores)


def head_backward(where, act_cotangent, gate_grad, cotangent, slope, arrays, gate_arrays, down_arrays):
    rows, wide = (TOKENS, WIDTH), (TOKENS, HIDDEN)
    return call(
        head_back_kernel,
        (where, act_cotangent, gate_grad, cotangent, slope, *arrays, *gate_arrays, *down_arrays),
        [SMEM, HBM, HBM, HBM, HBM] + [HBM] * 12,
        [
            (rows, F32, False),
            (rows, BF16, False),
            ((1, WIDTH), F32, False),
            ((1, HIDDEN), F32, False),
            (wide, BF16, True),
        ],
        weight_scratch(WIDTH, HEAD)
        + [pltpu.SemaphoreType.DMA((2, 16))]
        + weight_scratch(HIDDEN, WIDTH)
        + [
            pltpu.VMEM(rows, BF16),
            pltpu.VMEM((TOKENS, HEAD), BF16),
            pltpu.VMEM(wide, BF16),
            pltpu.VMEM(wide, BF16),
            pltpu.SemaphoreType.DMA((4,)),
            pltpu.SemaphoreType.DMA((6,)),
        ],
    )


def up_back_kernel(
    where, small, pre_grad, branch, act_turned, mlp_turned, mid, end_grad, *refs
):
    sources, outs, scratch = taken(refs, 4, 7)
    mid_grad, out_grad, terms, down_mine, down_theirs, up_mine, up_theirs = outs
    weight, sems, down_lane, down_sems, up_lane, up_sems, scratch = *scratch[:6], scratch[6:]
    pres, branches, acts, mlps, mids, ends, io_sems = scratch
    loads = [block_copies(where, "u", sources, UP_PART, weight, sems, side) for side in range(2)]
    pre_load = pltpu.make_async_copy(pre_grad, pres, io_sems.at[0])
    branch_load = pltpu.make_async_copy(branch, branches, io_sems.at[1])
    act_load = pltpu.make_async_copy(act_turned, acts, io_sems.at[2])
    mlp_load = pltpu.make_async_copy(mlp_turned, mlps, io_sems.at[3])
    norm_loads = [
        pltpu.make_async_copy(mid, mids, io_sems.at[4]),
        pltpu.make_async_copy(end_grad, ends, io_sems.at[5]),
    ]
    branch_load.start()
    act_load.start()
    pre_load.start()
    mlp_load.start()
    start_all(loads[0] + loads[1])
    start_all(norm_loads)
    branch_load.wait()
    act_load.wait()
    stores = []
    for side, out in ((1, down_theirs), (0, down_mine)):
        span = lane_columns(where, side, 384)
        for part in range(4):
            rows = slice(part * WIDTH, part * WIDTH + WIDTH)
            down_lane[side, rows, :] = times(acts[rows, :], branches[:, span]).astype(BF16)
        copies = term_copies(where, "down", down_lane, out, down_sems, side)
        start_all(copies)
        stores += copies
    pre_load.wait()
    mlp_load.wait()
    for side, out in ((1, up_theirs), (0, up_mine)):
        for tile in range(3):
            span = lane_columns(where, side, 1536, tile * 512, 512)
            up_lane[side, :, tile * 512 : tile * 512 + 512] = times(mlps[...], pres[:, span]).astype(
                BF16
            )
        copies = term_copies(where, "up", up_lane, out, up_sems, side)
        start_all(copies)
        stores += copies
    wait_all(loads[0] + loads[1])
    grad = across(pres[...], weight[...])
    wait_all(norm_loads)
    pulled, gain_grad, shift_grad = norm_backward(mids[...], small[3:4, :], grad)
    pulled = pulled + ends[...]
    rounded = pulled.astype(BF16)
    mid_grad[...] = pulled
    out_grad[...] = rounded
    terms[...] = jnp.zeros_like(terms)
    terms[0:1, :] = jnp.sum(rounded.astype(F32), axis=0, keepdims=True)
    terms[1:2, :] = gain_grad
    terms[2:3, :] = shift_grad
    wait_all(stores)


def up_backward(
    where, small, pre_grad, branch, act_turned, mlp_turned, mid, end_grad, arrays
):
    rows = (TOKENS, WIDTH)
    return call(
        up_back_kernel,
        (where, small, pre_grad, branch, act_turned, mlp_turned, mid, end_grad, *arrays),
        [SMEM, VMEM] + [HBM] * 10,
        [
            (rows, F32, False),
            (rows, BF16, False),
            ((8, WIDTH), F32, False),
            ((16, 192, 384), BF16, True),
            ((16, 192, 384), BF16, True),
            ((16, 48, 1536), BF16, True),
            ((16, 48, 1536), BF16, True),
        ],
        weight_scratch(WIDTH, HIDDEN)
        + lane_scratch(HIDDEN, 384)
        + lane_scratch(WIDTH, 1536)
        + [
            pltpu.VMEM((TOKENS, HIDDEN), BF16),
            pltpu.VMEM(rows, BF16),
            pltpu.VMEM((HIDDEN, TOKENS), BF16),
            pltpu.VMEM((WIDTH, TOKENS), BF16),
            pltpu.VMEM(rows, F32),
            pltpu.VMEM(rows, F32),
            pltpu.SemaphoreType.DMA((6,)),
        ],
    )


def attention_back_kernel(start, count, where, lengths, pad, out_grad, qkv, *refs):
    sources, outs, scratch = taken(refs, 4, 1)
    (qkv_grad,) = outs
    weight, sems, bias, mixed, turned, key_sum, value_sum = scratch
    loads = [block_copies(where, "u", sources, OUT_PART, weight, sems, side) for side in range(2)]
    start_all(loads[0] + loads[1])
    fill_bias(lengths, pad, bias)
    wait_all(loads[0] + loads[1])
    width = 128 * count
    mixed[...] = across(
        out_grad[...], weight[128 * start : 128 * start + width, :]
    ).astype(BF16)

    def columns_at(first):
        return pl.ds(pl.multiple_of(first, 128), 128)

    def pair(index, carry):
        own, first = index * 128, (index + start) * 128
        columns, keys_at = columns_at(first), columns_at(first + WIDTH)
        values_at = columns_at(first + 2 * WIDTH)
        keys_turned = qkv[:, keys_at].T
        key_sum[...] = jnp.zeros_like(key_sum)
        value_sum[...] = jnp.zeros_like(value_sum)
        for block, (low, high) in enumerate(KEY_SPANS):
            span = slice(128 * block, 128 * block + 128)
            queries, grads = two_heads(qkv[span, columns]), two_heads(mixed[span, columns_at(own)])
            scores = across(qkv[low:high, keys_at], queries)
            prob_grads = across(qkv[low:high, values_at], grads)
            allowed = bias[block, : high - low, :]
            probs, score_grads = [], []
            for head in range(2):
                part = slice(128 * head, 128 * head + 128)
                prob = probabilities(scores[:, part], allowed)
                pulled = prob * prob_grads[:, part]
                inner = jnp.sum(pulled, axis=0, keepdims=True)
                probs.append(prob.astype(BF16))
                score_grads.append((pulled - prob * inner).astype(BF16))
            score_grad = jnp.concatenate(score_grads, axis=1)
            key_sum[low:high, :] += times(score_grad, queries)
            value_sum[low:high, :] += times(jnp.concatenate(probs, axis=1), grads)
            turned[:, span] = head_rows_of(times(keys_turned[:, low:high], score_grad)) * score_scale
        qkv_grad[:, columns_at(own)] = turned[...].T.astype(BF16)
        qkv_grad[:, columns_at(own + width)] = (key_sum[...] * score_scale).astype(BF16)
        qkv_grad[:, columns_at(own + 2 * width)] = value_sum[...].astype(BF16)
        return carry

    lax.fori_loop(0, count, pair, 0)


def attention_backward(where, lengths, pad, out_grad, qkv, arrays, start, count):
    return call(
        partial(attention_back_kernel, start, count),
        (where, lengths, pad, out_grad, qkv, *arrays),
        [SMEM, SMEM, VMEM, VMEM, VMEM] + [HBM] * 4,
        [((TOKENS, 3 * 128 * count), BF16, False)],
        weight_scratch(WIDTH, WIDTH)
        + [
            pltpu.VMEM((4, 384, 128), F32),
            pltpu.VMEM((TOKENS, 128 * count), BF16),
            pltpu.VMEM((128, TOKENS), F32),
            pltpu.VMEM((TOKENS, 128), F32),
            pltpu.VMEM((TOKENS, 128), F32),
        ],
    )[0]


def mix_term_kernel(where, qkv_grad, input_turned, attended_turned, out_grad, mine_out, theirs_out, *refs):
    lane, sems = refs
    stores = []
    for side, out in ((1, theirs_out), (0, mine_out)):
        lane[side, :, :768] = times(
            input_turned[...], qkv_grad[:, lane_columns(where, side, 768)]
        ).astype(BF16)
        lane[side, :, 768:1152] = times(
            attended_turned[...], out_grad[:, lane_columns(where, side, 384)]
        ).astype(BF16)
        copies = term_copies(where, "front", lane, out, sems, side)
        start_all(copies)
        stores += copies
    wait_all(stores)


def mix_terms(where, qkv_grad, input_turned, attended_turned, out_grad):
    return call(
        mix_term_kernel,
        (where, qkv_grad, input_turned, attended_turned, out_grad),
        [SMEM] + [VMEM] * 4,
        [((16, 48, 1152), BF16, True)] * 2,
        lane_scratch(WIDTH, 1152),
    )


def front_back_kernel(
    where, lead, small, terms, down_row, up_rows, head_rows,
    first_grad, second_grad, patches, mid_grad, input_turned, *refs
):
    sources, outs, scratch = taken(refs, 4, 3)
    patch_out, mine_out, theirs_out = outs
    weight, sems, lane, lane_sems, scratch = *scratch[:4], scratch[4:]
    pulls, late_pulls, state, mids, inputs, patch_grad, small_grad, io_sems = scratch
    loads = [block_copies(where, "q", sources, QKV_PART, weight, sems, side) for side in range(2)]
    pairs = [(patches, state), (mid_grad, mids), (input_turned, inputs), (second_grad, late_pulls)]
    for part in range(3):
        for source, start, size in ((first_grad, 0, 512), (second_grad, 512, 256)):
            columns = pl.ds(WIDTH * part + start, size)
            pairs.append((source.at[:, pl.ds(size * part, size)], pulls.at[:, columns]))
    in_loads = [pltpu.make_async_copy(*pair, io_sems.at[at]) for at, pair in enumerate(pairs)]
    start_all(in_loads[4:])
    start_all(loads[0] + loads[1])
    start_all(in_loads[:4])
    wait_all(in_loads[4:])
    wait_all(loads[0] + loads[1])
    grad = across(pulls[...], weight[...])
    wait_all(in_loads[:4])
    pulled, gain_grad, shift_grad = norm_backward(
        state[...].astype(F32) + small[16:17, :], small[0:1, :], grad
    )
    pulled = pulled + mids[...]
    patch_grad[...] = pulled
    stores = [pltpu.make_async_copy(patch_grad, patch_out, io_sems.at[10])]
    stores[0].start()
    small_grad[0:1, :] = gain_grad
    small_grad[1:2, :] = shift_grad
    small_grad[2:5, :] = terms[0:3, :]
    small_grad[5:6, :] = down_row[...]
    small_grad[6:10, :] = up_rows[...]
    small_grad[10:16, :] = head_rows[...]
    places = lax.broadcasted_iota(jnp.int32, (LEADS, WIDTH), 0)
    lead_grad = jnp.sum(pulled, axis=0, keepdims=True)
    small_grad[16:32, :] = jnp.where(places == lead[0], lead_grad, 0.0)
    for side, out in ((1, theirs_out), (0, mine_out)):
        lane[side, :, :384] = times(
            inputs[...], late_pulls[:, lane_columns(where, side, 384)]
        ).astype(BF16)
        rows = small_grad[pl.ds(pl.multiple_of((where[0] ^ side) * 16, 16), 16), :]
        rows = jnp.concatenate([rows, jnp.zeros((112, WIDTH), F32)], axis=0)
        lane[side, :, 384:] = rows.T.astype(BF16)
        copies = term_copies(where, "front", lane, out, lane_sems, side)
        start_all(copies)
        stores += copies
    wait_all(stores)


def front_backward(
    where, lead, small, terms, down_row, up_rows, head_rows,
    first_grad, second_grad, patches, mid_grad, input_turned, arrays,
):
    rows, columns = (TOKENS, WIDTH), (WIDTH, TOKENS)
    return call(
        front_back_kernel,
        (
            where, lead, small, terms, down_row, up_rows, head_rows,
            first_grad, second_grad, patches, mid_grad, input_turned, *arrays,
        ),
        [SMEM, SMEM] + [VMEM] * 5 + [HBM] * 9,
        [(rows, F32, True), ((16, 48, 512), BF16, True), ((16, 48, 512), BF16, True)],
        weight_scratch(WIDTH, 3 * WIDTH)
        + lane_scratch(WIDTH, 512)
        + [
            pltpu.VMEM((TOKENS, 3 * WIDTH), BF16),
            pltpu.VMEM(rows, BF16),
            pltpu.VMEM(rows, BF16),
            pltpu.VMEM(rows, F32),
            pltpu.VMEM(columns, BF16),
            pltpu.VMEM(rows, F32),
            pltpu.VMEM((32, WIDTH), F32),
            pltpu.SemaphoreType.DMA((11,)),
        ],
    )


def rows_of(vector, count):
    return vector.reshape(32, count, 24).transpose(1, 0, 2).reshape(count, WIDTH)


def vector_of(rows):
    count = rows.shape[0]
    return rows.reshape(count, 32, 24).transpose(1, 0, 2).reshape(1, count * WIDTH)


def shards(
    patches,
    lead_index,
    window_lengths,
    pad_mask,
    lead_table,
    attn_gain,
    attn_shift,
    qkv_weight,
    out_weight,
    out_bias,
    mlp_gain,
    mlp_shift,
    up_weight,
    up_bias,
    down_weight,
    down_bias,
    head_weight,
    head_bias,
    act_cotangent,
    head_cotangent,
):
    core, where = whereabouts()
    weights = (qkv_weight, out_weight, up_weight, down_weight, head_weight)
    vectors = (
        attn_gain, attn_shift, out_bias, mlp_gain, mlp_shift, down_bias, up_bias, head_bias
    )
    parts = packed(core, weights, lead_table, vectors)
    pad = pad_mask[:, None]
    cotangent_sum = jnp.sum(head_cotangent[:, GATE:].astype(F32), axis=0, keepdims=True)

    orders = ORDERS
    parts = dict(zip("qudh", zip(parts[:4], parts[4:])))
    chunks = {
        name: in_core_order(core, mine, exchange(theirs, SIBLING), 0)[None]
        for name, (mine, theirs) in parts.items()
    }

    held, last = dict(chunks), ()
    for name, step in GATHER_SEQUENCE:
        held[name] = after(held[name], *last)
        last = (held[name],)
        held[name] = doubled(held[name], orders[name][step])
    q, u, d, h = [held[name] for name in ("q", "u", "d", "h")]
    q_rest = exchange(after(q, *last), orders["q"][3])
    u = after(u, q)
    u_rest = exchange(u, orders["u"][3])
    h = doubled(after(h, u), orders["h"][2])
    first = both_lanes(q, q_rest)
    input_turned, qkv, small_rows = front_forward(
        after(where, d, h, cotangent_sum), lead_index, patches, first
    )
    attended, attended_turned = attention_forward(where, window_lengths, pad, qkv)
    second = both_lanes(u, after(u_rest, attended))
    d_rest = exchange(after(d, attended), orders["d"][3])
    up_bias_row, head_bias_row = vector_of(small_rows[6:10]), vector_of(small_rows[10:16])
    mid_state, mlp_turned, act_rows, act_turned, slope = up_forward(
        where, attended, patches, small_rows, up_bias_row, second
    )
    down = both_lanes(d, after(d_rest, act_rows))
    h_rest = exchange(after(h, act_rows), orders["h"][3])
    outputs, gate_out, gate_grad, gate_bias_sum, mine_h, theirs_h = down_forward(
        where, act_rows, mid_state, small_rows, head_cotangent, head_bias_row, down, second
    )
    head = both_lanes(h, after(h_rest, theirs_h))
    got_h = exchange(theirs_h, SIBLING)
    end_grad, branch_grad, down_bias_sum, up_bias_sum, pre_grad = head_backward(
        after(where, theirs_h), act_cotangent, gate_grad, head_cotangent, slope, head, second, down
    )
    head_rows = rows_of(jnp.concatenate([gate_bias_sum, cotangent_sum], axis=1), 6)
    up_rows = rows_of(up_bias_sum, 4)
    keep_h, send_h = folded(mine_h, after(got_h, pre_grad))
    got_h = exchange(send_h, orders["head"][3])
    mid_grad, out_grad, terms, mine_d, theirs_d, mine_u, theirs_u = up_backward(
        after(where, send_h), small_rows, pre_grad, branch_grad, act_turned, mlp_turned,
        mid_state, end_grad, second,
    )
    got_d, got_u = exchange(theirs_d, SIBLING), exchange(theirs_u, SIBLING)
    pulled = (window_lengths, pad, out_grad, qkv, second)
    first_grad = attention_backward(where, *pulled, 0, 4)
    keep_h, send_h = folded(keep_h, after(got_h, first_grad))
    got_h = exchange(send_h, orders["head"][2])
    keep_u, send_u = folded(mine_u, after(got_u, first_grad))
    got_u = exchange(send_u, orders["up"][3])
    keep_d, send_d = folded(mine_d, after(got_d, first_grad))
    got_d = exchange(send_d, orders["down"][3])
    mine_m, theirs_m = mix_terms(
        after(where, send_h, send_d, send_u), first_grad, input_turned, attended_turned, out_grad
    )
    got_m = exchange(theirs_m, SIBLING)
    second_grad = attention_backward(after(where, theirs_m), *pulled, 4, 2)
    keep_m, send_m = folded(mine_m, after(got_m, second_grad))
    got_m = exchange(send_m, orders["front"][3])
    keep_h, send_h = folded(keep_h, after(got_h, second_grad))
    got_h = exchange(send_h, orders["head"][1])
    patch_grad, mine_f, theirs_f = front_backward(
        after(where, send_h, send_m), lead_index, small_rows, terms, down_bias_sum,
        up_rows, head_rows, first_grad, second_grad, patches, mid_grad, input_turned, first,
    )
    got_f = exchange(theirs_f, SIBLING)
    keep_m, send_m = folded(keep_m, after(got_m, patch_grad))
    got_m = exchange(send_m, orders["front"][2])
    keep_f, send_f = folded(mine_f, after(got_f, send_m))
    got_f = exchange(send_f, orders["front"][3])
    keep_d, send_d = folded(keep_d, after(got_d, send_f))
    got_d = exchange(send_d, orders["down"][2])
    keep_h, send_h = folded(keep_h, after(got_h, send_f))
    got_h = exchange(send_h, orders["head"][0])
    keep_u, send_u = folded(keep_u, after(got_u, send_f))
    got_u = exchange(send_u, orders["up"][2])
    head_out = head_forward(
        after(where, send_m, send_u, send_d, send_h), outputs, gate_out, head_bias_row, head
    )
    keep_f, send_f = folded(keep_f, after(got_f, head_out))
    got_f = exchange(send_f, orders["front"][2])
    keep_m, send_m = folded(keep_m, after(got_m, send_f))
    got_m = exchange(send_m, orders["front"][1])
    keep_d, send_d = folded(keep_d, after(got_d, send_f))
    got_d = exchange(send_d, orders["down"][1])
    keep_u, send_u = folded(keep_u, after(got_u, send_f))
    got_u = exchange(send_u, orders["up"][1])
    keep_f, send_f = folded(keep_f, after(got_f, send_m, send_d, send_u))
    got_f = exchange(send_f, orders["front"][1])
    keep_m, send_m = folded(keep_m, after(got_m, send_f))
    got_m = exchange(send_m, orders["front"][0])
    keep_d, send_d = folded(keep_d, after(got_d, send_f))
    got_d = exchange(send_d, orders["down"][0])
    keep_u, send_u = folded(keep_u, after(got_u, send_f))
    got_u = exchange(send_u, orders["up"][0])
    gate_sum, rest_sum = finished(keep_h, after(got_h, send_u), core, (256, 2048))
    keep_f, send_f = folded(keep_f, after(got_f, send_u))
    got_f = exchange(send_f, orders["front"][0])
    early_sum, out_sum = finished(keep_m, after(got_m, send_f), core, (768, 384))
    (down_sum,) = finished(keep_d, after(got_d, send_f), core, (384,))
    (up_sum,) = finished(keep_u, after(got_u, send_f), core, (1536,))
    late_sum, small_sum = finished(keep_f, got_f, core, (384, 128))
    qkv_sum = jnp.concatenate(
        [
            piece[:, part * piece.shape[1] // 3 : (part + 1) * piece.shape[1] // 3]
            for part in range(3)
            for piece in (early_sum, late_sum)
        ],
        axis=1,
    )
    small_sum = small_sum.T
    return (
        outputs,
        head_out,
        patch_grad,
        small_sum[128:144],
        small_sum[0],
        small_sum[1],
        qkv_sum,
        out_sum,
        small_sum[2],
        small_sum[3],
        small_sum[4],
        up_sum,
        small_sum[6:10].reshape(96),
        down_sum,
        small_sum[5],
        jnp.concatenate([gate_sum, rest_sum], axis=1),
        small_sum[10:16].reshape(144),
    )


def plain_shards(
    patches,
    lead_index,
    window_lengths,
    pad_mask,
    lead_table,
    attn_gain,
    attn_shift,
    qkv_weight,
    out_weight,
    out_bias,
    mlp_gain,
    mlp_shift,
    up_weight,
    up_bias,
    down_weight,
    down_bias,
    head_weight,
    head_bias,
    act_cotangent,
    head_cotangent,
):
    front = (
        lax.all_gather(lead_table, ("dp", "fsdp"), axis=1, tiled=True),
        lax.all_gather(attn_gain, ("dp", "fsdp"), axis=0, tiled=True),
        lax.all_gather(attn_shift, ("dp", "fsdp"), axis=0, tiled=True),
        lax.all_gather(qkv_weight, ("dp", "fsdp"), axis=0, tiled=True),
        lax.all_gather(out_weight, ("dp", "fsdp"), axis=0, tiled=True),
        lax.all_gather(out_bias, ("dp", "fsdp"), axis=0, tiled=True),
    )
    rear = (
        lax.all_gather(mlp_gain, ("dp", "fsdp"), axis=0, tiled=True),
        lax.all_gather(mlp_shift, ("dp", "fsdp"), axis=0, tiled=True),
        lax.all_gather(up_weight, ("dp", "fsdp"), axis=0, tiled=True),
        lax.all_gather(up_bias, ("dp", "fsdp"), axis=0, tiled=True),
        lax.all_gather(down_weight, ("dp", "fsdp"), axis=0, tiled=True),
        lax.all_gather(down_bias, ("dp", "fsdp"), axis=0, tiled=True),
        lax.all_gather(head_weight, ("dp", "fsdp"), axis=0, tiled=True),
        lax.all_gather(head_bias, ("dp", "fsdp"), axis=0, tiled=True),
    )
    table_full, gain_one, shift_one, qkv_full, out_full, out_bias_full = front
    (
        gain_two,
        shift_two,
        up_full,
        up_bias_full,
        down_full,
        down_bias_full,
        head_full,
        head_bias_full,
    ) = rear
    token_rows, width = patches.shape
    head_dim = width // HEADS
    block_rows = min(512, token_rows)
    block_count = token_rows // block_rows
    ends = jnp.cumsum(window_lengths[0])
    positions = jnp.arange(token_rows, dtype=jnp.int32)
    window = jnp.sum((positions[:, None] >= ends[None, :]).astype(jnp.int32), axis=1)
    lead_hot = (jnp.arange(LEADS, dtype=jnp.int32) == lead_index[0]).astype(jnp.float32)
    lead_row = jnp.sum(lead_hot[:, None] * table_full.astype(jnp.float32), axis=0)
    start_state = patches.astype(jnp.float32) + lead_row[None, :]
    normed_one, pull_one = jax.vjp(
        layer_norm, start_state, gain_one.astype(jnp.float32), shift_one.astype(jnp.float32)
    )
    attn_input = normed_one.astype(jnp.bfloat16)
    qkv_rows = jnp.dot(attn_input, qkv_full, preferred_element_type=jnp.float32).astype(
        jnp.bfloat16
    )
    queries = qkv_rows[:, :width].reshape(block_count, block_rows, HEADS, head_dim)
    keys = qkv_rows[:, width : 2 * width].reshape(token_rows, HEADS, head_dim)
    values = qkv_rows[:, 2 * width :].reshape(token_rows, HEADS, head_dim)
    query_windows = window.reshape(block_count, block_rows)
    block_starts = jnp.arange(block_count, dtype=jnp.int32) * block_rows

    def block_scores(query_block, window_block, block_start):
        scores = (
            jnp.einsum("qhd,khd->hqk", query_block, keys, preferred_element_type=jnp.float32)
            * score_scale
        )
        allowed = allowed_keys(window_block, window, pad_mask, block_start)
        return jnp.where(allowed[None], scores, -1e30)

    def forward_block(inputs):
        query_block, window_block, block_start = inputs
        masked = block_scores(query_block, window_block, block_start)
        largest = jnp.max(masked, axis=-1, keepdims=True)
        raised = jnp.exp(masked - largest)
        total = jnp.sum(raised, axis=-1, keepdims=True)
        probs = (raised / total).astype(jnp.bfloat16)
        mixed = jnp.einsum("hqk,khd->qhd", probs, values, preferred_element_type=jnp.float32)
        return (
            mixed.reshape(block_rows, width).astype(jnp.bfloat16),
            (largest + jnp.log(total))[:, :, 0],
        )

    mixed_blocks, log_totals = lax.map(forward_block, (queries, query_windows, block_starts))
    attended = mixed_blocks.reshape(token_rows, width)
    mid_state = (
        start_state
        + jnp.dot(attended, out_full, preferred_element_type=jnp.float32)
        + out_bias_full.astype(jnp.float32)
    )
    normed_two, pull_two = jax.vjp(
        layer_norm, mid_state, gain_two.astype(jnp.float32), shift_two.astype(jnp.float32)
    )
    mlp_input = normed_two.astype(jnp.bfloat16)
    pre_act = jnp.dot(mlp_input, up_full, preferred_element_type=jnp.float32) + up_bias_full.astype(
        jnp.float32
    )
    activated, pull_act = jax.vjp(gelu_exact, pre_act)
    act_rows = activated.astype(jnp.bfloat16)
    end_state = (
        mid_state
        + jnp.dot(act_rows, down_full, preferred_element_type=jnp.float32)
        + down_bias_full.astype(jnp.float32)
    )
    outputs = end_state.astype(jnp.bfloat16)
    logits = jnp.dot(
        outputs, head_full, preferred_element_type=jnp.float32
    ) + head_bias_full.astype(jnp.float32)
    head_out, pull_head = jax.vjp(partial(expert_softmax, experts=EXPERTS, pixels=PIX), logits)
    up_back, down_back, head_back = (
        lax.all_gather(up_weight, ("dp", "fsdp"), axis=0, tiled=True),
        lax.all_gather(down_weight, ("dp", "fsdp"), axis=0, tiled=True),
        lax.all_gather(head_weight, ("dp", "fsdp"), axis=0, tiled=True),
    )
    qkv_back, out_back = (
        lax.all_gather(qkv_weight, ("dp", "fsdp"), axis=0, tiled=True),
        lax.all_gather(out_weight, ("dp", "fsdp"), axis=0, tiled=True),
    )
    logit_grad = pull_head(head_cotangent.astype(jnp.float32))[0].astype(jnp.bfloat16)
    head_bias_term = jnp.sum(logit_grad.astype(jnp.float32), axis=0)
    head_term = jnp.einsum("td,tn->dn", outputs, logit_grad, preferred_element_type=jnp.float32)
    end_grad = act_cotangent.astype(jnp.float32) + jnp.einsum(
        "tn,dn->td", logit_grad, head_back, preferred_element_type=jnp.float32
    )
    branch_grad = end_grad.astype(jnp.bfloat16)
    down_bias_term = jnp.sum(branch_grad.astype(jnp.float32), axis=0)
    down_term = jnp.einsum("tf,td->fd", act_rows, branch_grad, preferred_element_type=jnp.float32)
    act_grad = jnp.einsum("td,fd->tf", branch_grad, down_back, preferred_element_type=jnp.float32)
    pre_grad = pull_act(act_grad)[0].astype(jnp.bfloat16)
    up_bias_term = jnp.sum(pre_grad.astype(jnp.float32), axis=0)
    up_term = jnp.einsum("td,tf->df", mlp_input, pre_grad, preferred_element_type=jnp.float32)
    normed_two_grad = jnp.einsum("tf,df->td", pre_grad, up_back, preferred_element_type=jnp.float32)
    state_grad_two, gain_two_term, shift_two_term = pull_two(normed_two_grad)
    (
        gain_part,
        shift_part,
        up_part,
        up_bias_part,
        down_part,
        down_bias_part,
        head_part,
        head_bias_part,
    ) = (
        lax.psum_scatter(
            gain_two_term.astype(jnp.bfloat16), "dp", scatter_dimension=0, tiled=True
        ).astype(jnp.float32),
        lax.psum_scatter(
            shift_two_term.astype(jnp.bfloat16), "dp", scatter_dimension=0, tiled=True
        ).astype(jnp.float32),
        lax.psum_scatter(
            up_term.astype(jnp.bfloat16), "dp", scatter_dimension=0, tiled=True
        ).astype(jnp.float32),
        lax.psum_scatter(
            up_bias_term.astype(jnp.bfloat16), "dp", scatter_dimension=0, tiled=True
        ).astype(jnp.float32),
        lax.psum_scatter(
            down_term.astype(jnp.bfloat16), "dp", scatter_dimension=0, tiled=True
        ).astype(jnp.float32),
        lax.psum_scatter(
            down_bias_term.astype(jnp.bfloat16), "dp", scatter_dimension=0, tiled=True
        ).astype(jnp.float32),
        lax.psum_scatter(
            head_term.astype(jnp.bfloat16), "dp", scatter_dimension=0, tiled=True
        ).astype(jnp.float32),
        lax.psum_scatter(
            head_bias_term.astype(jnp.bfloat16), "dp", scatter_dimension=0, tiled=True
        ).astype(jnp.float32),
    )
    rear_grads = (
        lax.psum_scatter(gain_part, "fsdp", scatter_dimension=0, tiled=True),
        lax.psum_scatter(shift_part, "fsdp", scatter_dimension=0, tiled=True),
        lax.psum_scatter(up_part, "fsdp", scatter_dimension=0, tiled=True),
        lax.psum_scatter(up_bias_part, "fsdp", scatter_dimension=0, tiled=True),
        lax.psum_scatter(down_part, "fsdp", scatter_dimension=0, tiled=True),
        lax.psum_scatter(down_bias_part, "fsdp", scatter_dimension=0, tiled=True),
        lax.psum_scatter(head_part, "fsdp", scatter_dimension=0, tiled=True),
        lax.psum_scatter(head_bias_part, "fsdp", scatter_dimension=0, tiled=True),
    )
    mid_grad = end_grad + state_grad_two
    out_grad = mid_grad.astype(jnp.bfloat16)
    out_bias_term = jnp.sum(out_grad.astype(jnp.float32), axis=0)
    out_term = jnp.einsum("td,te->de", attended, out_grad, preferred_element_type=jnp.float32)
    mixed_grad = jnp.einsum(
        "te,de->td", out_grad, out_back, preferred_element_type=jnp.float32
    ).astype(jnp.bfloat16)
    grad_blocks = mixed_grad.reshape(block_count, block_rows, HEADS, head_dim)

    def backward_block(carry, inputs):
        key_sum, value_sum = carry
        query_block, grad_block, window_block, total_block, block_start = inputs
        masked = block_scores(query_block, window_block, block_start)
        probs = jnp.exp(masked - total_block[:, :, None])
        prob_grad = jnp.einsum(
            "qhd,khd->hqk", grad_block, values, preferred_element_type=jnp.float32
        )
        inner = jnp.sum(probs * prob_grad, axis=-1, keepdims=True)
        score_grad = (probs * (prob_grad - inner)).astype(jnp.bfloat16)
        query_grad = (
            jnp.einsum("hqk,khd->qhd", score_grad, keys, preferred_element_type=jnp.float32)
            * score_scale
        )
        key_sum = (
            key_sum
            + jnp.einsum(
                "hqk,qhd->khd", score_grad, query_block, preferred_element_type=jnp.float32
            )
            * score_scale
        )
        value_sum = value_sum + jnp.einsum(
            "hqk,qhd->khd",
            probs.astype(jnp.bfloat16),
            grad_block,
            preferred_element_type=jnp.float32,
        )
        return ((key_sum, value_sum), query_grad.reshape(block_rows, width))

    zero_keys = jnp.zeros((token_rows, HEADS, head_dim), jnp.float32)
    (key_grad, value_grad), query_grads = lax.scan(
        backward_block,
        (zero_keys, zero_keys),
        (queries, grad_blocks, query_windows, log_totals, block_starts),
    )
    qkv_grad = jnp.concatenate(
        [
            query_grads.reshape(token_rows, width),
            key_grad.reshape(token_rows, width),
            value_grad.reshape(token_rows, width),
        ],
        axis=1,
    ).astype(jnp.bfloat16)
    qkv_term = jnp.einsum("td,te->de", attn_input, qkv_grad, preferred_element_type=jnp.float32)
    normed_one_grad = jnp.einsum(
        "te,de->td", qkv_grad, qkv_back, preferred_element_type=jnp.float32
    )
    state_grad_one, gain_one_term, shift_one_term = pull_one(normed_one_grad)
    patch_grad = mid_grad + state_grad_one
    lead_term = lead_hot[:, None] * jnp.sum(patch_grad, axis=0)[None, :]
    lead_part, gain_one_part, shift_one_part, qkv_part, out_part, out_bias_part = (
        lax.psum_scatter(
            lead_term.astype(jnp.bfloat16), "dp", scatter_dimension=1, tiled=True
        ).astype(jnp.float32),
        lax.psum_scatter(
            gain_one_term.astype(jnp.bfloat16), "dp", scatter_dimension=0, tiled=True
        ).astype(jnp.float32),
        lax.psum_scatter(
            shift_one_term.astype(jnp.bfloat16), "dp", scatter_dimension=0, tiled=True
        ).astype(jnp.float32),
        lax.psum_scatter(
            qkv_term.astype(jnp.bfloat16), "dp", scatter_dimension=0, tiled=True
        ).astype(jnp.float32),
        lax.psum_scatter(
            out_term.astype(jnp.bfloat16), "dp", scatter_dimension=0, tiled=True
        ).astype(jnp.float32),
        lax.psum_scatter(
            out_bias_term.astype(jnp.bfloat16), "dp", scatter_dimension=0, tiled=True
        ).astype(jnp.float32),
    )
    front_grads = (
        lax.psum_scatter(lead_part, "fsdp", scatter_dimension=1, tiled=True),
        lax.psum_scatter(gain_one_part, "fsdp", scatter_dimension=0, tiled=True),
        lax.psum_scatter(shift_one_part, "fsdp", scatter_dimension=0, tiled=True),
        lax.psum_scatter(qkv_part, "fsdp", scatter_dimension=0, tiled=True),
        lax.psum_scatter(out_part, "fsdp", scatter_dimension=0, tiled=True),
        lax.psum_scatter(out_bias_part, "fsdp", scatter_dimension=0, tiled=True),
    )
    return (
        outputs,
        head_out,
        patch_grad,
        front_grads[0],
        front_grads[1],
        front_grads[2],
        front_grads[3],
        front_grads[4],
        front_grads[5],
        rear_grads[0],
        rear_grads[1],
        rear_grads[2],
        rear_grads[3],
        rear_grads[4],
        rear_grads[5],
        rear_grads[6],
        rear_grads[7],
    )


def solution(mesh):
    in_specs = (
        P(("dp", "fsdp"), None),
        P(("dp", "fsdp")),
        P(("dp", "fsdp"), None),
        P(("dp", "fsdp")),
        P(None, ("dp", "fsdp")),
        P(("dp", "fsdp")),
        P(("dp", "fsdp")),
        P(("dp", "fsdp"), None),
        P(("dp", "fsdp"), None),
        P(("dp", "fsdp")),
        P(("dp", "fsdp")),
        P(("dp", "fsdp")),
        P(("dp", "fsdp"), None),
        P(("dp", "fsdp")),
        P(("dp", "fsdp"), None),
        P(("dp", "fsdp")),
        P(("dp", "fsdp"), None),
        P(("dp", "fsdp")),
        P(("dp", "fsdp"), None),
        P(("dp", "fsdp"), None),
    )
    out_specs = (
        P(("dp", "fsdp"), None),
        P(("dp", "fsdp"), None),
        P(("dp", "fsdp"), None),
        P(None, ("dp", "fsdp")),
        P(("dp", "fsdp")),
        P(("dp", "fsdp")),
        P(("dp", "fsdp"), None),
        P(("dp", "fsdp"), None),
        P(("dp", "fsdp")),
        P(("dp", "fsdp")),
        P(("dp", "fsdp")),
        P(("dp", "fsdp"), None),
        P(("dp", "fsdp")),
        P(("dp", "fsdp"), None),
        P(("dp", "fsdp")),
        P(("dp", "fsdp"), None),
        P(("dp", "fsdp")),
    )
    body = shards if dict(mesh.shape) == {"dp": 4, "fsdp": 8} else plain_shards
    return jax.shard_map(body, mesh=mesh, in_specs=in_specs, out_specs=out_specs, check_vma=False)
```

```python
import math
from functools import partial

import jax
import jax.numpy as jnp
from jax import lax
from jax.experimental import pallas as pl
from jax.experimental.pallas import tpu as pltpu
from jax.sharding import PartitionSpec as P

HEADS = 12
PIX = 64
EXPERTS = 3
LEADS = 16


norm_epsilon = 1e-05
score_scale = 0.125


def layer_norm(hidden, norm_gain, norm_shift):
    average = jnp.mean(hidden, axis=-1, keepdims=True)
    centered = hidden - average
    variance = jnp.mean(centered * centered, axis=-1, keepdims=True)
    return centered * lax.rsqrt(variance + norm_epsilon) * norm_gain + norm_shift


def gelu_exact(values):
    return 0.5 * values * (1.0 + lax.erf(values * 0.7071067811865476))


def expert_softmax(logits, experts, pixels):
    gate_part = logits[:, : experts * pixels].reshape(logits.shape[0], experts, pixels)
    largest = jnp.max(gate_part, axis=1, keepdims=True)
    raised = jnp.exp(gate_part - largest)
    shares = raised / jnp.sum(raised, axis=1, keepdims=True)
    return jnp.concatenate(
        [shares.reshape(logits.shape[0], experts * pixels), logits[:, experts * pixels :]], axis=1
    )


def allowed_keys(query_window, key_window, key_valid, query_start):
    query_place = query_start + jnp.arange(query_window.shape[0], dtype=jnp.int32)
    key_place = jnp.arange(key_window.shape[0], dtype=jnp.int32)
    same_window = query_window[:, None] == key_window[None, :]
    usable = (key_valid[None, :] > 0) | (query_place[:, None] == key_place[None, :])
    return same_window & usable


AXES = ("dp", "fsdp")
FAR_Z, NEAR_Z, FIRST, SECOND, SIBLING = (4, 4), (2, 2), (8, 16), (16, 8), (1, 1)
ORDERS = {
    "q": (NEAR_Z, FAR_Z, FIRST, SECOND),
    "u": (FAR_Z, FIRST, NEAR_Z, SECOND),
    "d": (NEAR_Z, FIRST, FAR_Z, SECOND),
    "h": (FAR_Z, NEAR_Z, FIRST, SECOND),
    "head": (FAR_Z, NEAR_Z, FIRST, SECOND),
    "down": (FAR_Z, NEAR_Z, FIRST, SECOND),
    "up": (FAR_Z, FIRST, SECOND, NEAR_Z),
    "front": (FAR_Z, NEAR_Z, FIRST, SECOND),
}
GATHER_SEQUENCE = (
    ("h", 0), ("q", 0), ("d", 0), ("u", 0), ("q", 1), ("d", 1), ("h", 1), ("u", 1), ("d", 2), ("q", 2),
    ("u", 2), ("h", 2),
)
SPARE_VMEM = 8 * 1024 * 1024
WIDTH = 768
HIDDEN = 3072
HEAD = 4608
TOKENS = 512
GATE = 512
F32 = jnp.float32
BF16 = jnp.bfloat16
HBM = pl.BlockSpec(memory_space=pltpu.HBM)
SMEM = pl.BlockSpec(memory_space=pltpu.SMEM)
VMEM = pl.BlockSpec(memory_space=pltpu.VMEM)
QKV_PART, SMALL_PART = (0, 1152), (1152, 128)
UP_PART, OUT_PART, GATE_PART = (0, 1536), (1536, 384), (1920, 256)
DOWN_PART, HEAD_PART = (0, 384), (0, 2048)


def chip_masks(order, lane):
    masks = []
    for place in range(16):
        mask = 0
        for step in range(4):
            if place >> step & 1:
                mask ^= order[step][lane]
        masks.append(mask >> 1)
    return masks


def table_start(group, side):
    return 1 + 32 * list(ORDERS).index(group) + 16 * side


def exchange(array, masks):
    return lax.ppermute(array, AXES, [(d, d ^ masks[d & 1]) for d in range(32)])


def whereabouts():
    device = lax.axis_index("dp") * 8 + lax.axis_index("fsdp")
    core, chip = device % 2, device // 2
    tables = [chip_masks(order, 0) + chip_masks(order, 1) for order in ORDERS.values()]
    swapped = [chip_masks(order, 1) + chip_masks(order, 0) for order in ORDERS.values()]
    places = jnp.where(core == 0, jnp.array(tables, jnp.int32), jnp.array(swapped, jnp.int32))
    places = (places ^ chip).reshape(32 * len(ORDERS))
    return core, jnp.concatenate([core[None].astype(jnp.int32), places])


def after(value, *marks):
    return lax.optimization_barrier((value, marks))[0]


def in_core_order(core, mine, theirs, axis):
    return jnp.where(
        core == 0,
        jnp.concatenate([mine, theirs], axis=axis),
        jnp.concatenate([theirs, mine], axis=axis),
    )


def pack_kernel(core, qkv, out, up, down, head, table, *refs):
    vectors, (up_bias, head_bias), refs = refs[:6], refs[6:8], refs[8:]
    outs, (rows,) = refs[:8], refs[8:]
    rows[...] = jnp.zeros_like(rows)
    for index, vector in enumerate(vectors):
        rows[index : index + 1, :24] = vector[...].astype(F32)
    for index in range(4):
        rows[6 + index : 7 + index, :24] = up_bias[:, 24 * index : 24 * index + 24].astype(F32)
    for index in range(6):
        rows[10 + index : 11 + index, :24] = head_bias[:, 24 * index : 24 * index + 24].astype(F32)
    rows[16:32, :24] = table[...].astype(F32)
    small = rows[...].T[:24].astype(BF16)
    for side in range(2):
        q, u, d, h = outs[4 * side : 4 * side + 4]
        q[:, :1152] = qkv[:, lane_columns(core, side, 1152)]
        q[:, 1152:] = small
        u[:, :1536] = up[:, lane_columns(core, side, 1536)]
        u[:, 1536:1920] = out[:, lane_columns(core, side, 384)]
        u[:, 1920:] = head[:, lane_columns(core, side, 256)]
        d[...] = down[:, lane_columns(core, side, 384)]
        h[...] = head[:, lane_columns(core, side, 2048, GATE)]


def packed(core, weights, table, vectors):
    shapes = [(24, 1280), (24, 2176), (96, 384), (24, 2048)] * 2
    return call(
        pack_kernel,
        (core.reshape(1), *weights, table, *[vector[None] for vector in vectors]),
        [SMEM] + [VMEM] * 14,
        [(shape, BF16, False) for shape in shapes],
        [pltpu.VMEM((128, 128), F32)],
    )


def doubled(held, masks):
    return jnp.concatenate([held, exchange(held, masks)], axis=0)


def both_lanes(*arrays):
    return arrays + tuple(exchange(array, SIBLING) for array in arrays)


def total(first, second):
    return first.astype(F32) + second.astype(F32)


def folded(keep, got, start=0):
    half = got.shape[0] // 2
    send = total(keep[half:], got[half:]).astype(BF16)
    return total(keep[:half], got[:half]).astype(BF16), send


def finished(keep, got, core, widths):
    block = total(keep, got)[0]
    rows = block.shape[0] // 2
    upper, lower = block[:rows], block[rows:]
    mine = jnp.where(core == 0, upper, lower)
    theirs = jnp.where(core == 0, lower, upper).astype(BF16)
    other = exchange(theirs, SIBLING).astype(F32)
    pieces, start = [], 0
    for width in widths:
        span = slice(start, start + width)
        pieces.append(in_core_order(core, mine[:, span], other[:, span], 1))
        start += width
    return pieces


def across(first, second):
    return lax.dot_general(first, second, (((1,), (1,)), ((), ())), preferred_element_type=F32)


def times(first, second):
    return jnp.dot(first, second, preferred_element_type=F32)


def lane_columns(where, side, stride, first=0, width=None):
    return pl.ds(pl.multiple_of(first + (where[0] ^ side) * stride, 128), width or stride)


def block_copies(where, group, sources, part, target, sems, side, first=0):
    start, width = part
    rows = sources[0].shape[1]
    half = len(sources) // 2
    count = 16 // half
    copies = []
    for place in range(16):
        row = pl.multiple_of(where[table_start(group, side) + place] * rows, rows)
        copies.append(
            pltpu.make_async_copy(
                sources[half * side + place // count].at[place % count, :, pl.ds(start, width)],
                target.at[pl.ds(row, rows), lane_columns(where, side, width, first)],
                sems.at[side, place],
            )
        )
    return copies


def term_copies(where, group, lane, out, sems, side):
    rows = out.shape[1]
    copies = []
    for place in range(16):
        row = pl.multiple_of(where[table_start(group, side) + place] * rows, rows)
        copies.append(
            pltpu.make_async_copy(lane.at[side, pl.ds(row, rows), :], out.at[place], sems.at[side, place])
        )
    return copies


def start_all(copies):
    for copy in copies:
        copy.start()


def wait_all(copies):
    for copy in copies:
        copy.wait()


def mean_and_scale(hidden):
    average = jnp.mean(hidden, axis=1, keepdims=True)
    centered = hidden - average
    variance = jnp.mean(centered * centered, axis=1, keepdims=True)
    return centered, lax.rsqrt(variance + norm_epsilon)


def norm_backward(hidden, gain, upstream):
    centered, scale = mean_and_scale(hidden)
    normed = centered * scale
    gain_grad = jnp.sum(upstream * normed, axis=0, keepdims=True)
    shift_grad = jnp.sum(upstream, axis=0, keepdims=True)
    scaled = upstream * gain
    first = jnp.mean(scaled, axis=1, keepdims=True)
    second = jnp.mean(scaled * normed, axis=1, keepdims=True)
    return scale * (scaled - first - normed * second), gain_grad, shift_grad


def call(kernel, operands, in_specs, outs, scratch):
    def size(item):
        return math.prod(item.shape) * jnp.dtype(item.dtype).itemsize

    held = [item for item, spec in zip(operands, in_specs) if spec is VMEM]
    held += [jax.ShapeDtypeStruct(shape, kind) for shape, kind, copied in outs if not copied]
    held += [item for item in scratch if getattr(item, "memory_space", None) == pltpu.VMEM]
    limit = sum(size(item) for item in held) + SPARE_VMEM
    return pl.pallas_call(
        kernel,
        out_shape=[jax.ShapeDtypeStruct(shape, kind) for shape, kind, _ in outs],
        in_specs=in_specs,
        out_specs=[HBM if copied else VMEM for _, _, copied in outs],
        scratch_shapes=scratch,
        compiler_params=pltpu.CompilerParams(vmem_limit_bytes=limit),
        cost_estimate=pl.CostEstimate(flops=2 * 10**12, bytes_accessed=10**10, transcendentals=0),
    )(*operands)


def lane_scratch(rows, width):
    return [pltpu.VMEM((2, rows, width), BF16), pltpu.SemaphoreType.DMA((2, 16))]


def weight_scratch(rows, width):
    return [pltpu.VMEM((rows, width), BF16), pltpu.SemaphoreType.DMA((2, 16))]


def taken(refs, *counts):
    groups = []
    for count in counts:
        groups.append(refs[:count])
        refs = refs[count:]
    return *groups, refs


def front_kernel(where, lead, patches, *refs):
    sources, outs, scratch = taken(refs, 4, 3)
    turned_out, qkv_out, small = outs
    weight, sems, smalls, small_sems, state, rows, turned, qkv, io_sems = scratch
    loads = [block_copies(where, "q", sources, QKV_PART, weight, sems, side) for side in range(2)]
    small_loads = []
    for place in range(16):
        row = pl.multiple_of(where[table_start("q", 0) + place] * 48, 48)
        small_loads.append(
            pltpu.make_async_copy(
                sources[place // 8].at[place % 8, :, pl.ds(*SMALL_PART)],
                smalls.at[pl.ds(row, 48), :],
                small_sems.at[place],
            )
        )
    state_load = pltpu.make_async_copy(patches, state, io_sems.at[0])
    start_all(small_loads)
    state_load.start()
    start_all(loads[0])
    start_all(loads[1])
    wait_all(small_loads)
    columns = smalls[...].astype(F32).T
    places = lax.broadcasted_iota(jnp.int32, (LEADS, WIDTH), 0)
    lead_row = jnp.sum(
        jnp.where(places == lead[0], columns[16 : 16 + LEADS], 0.0), axis=0, keepdims=True
    )
    small[...] = columns[:32]
    small[16:17, :] = lead_row
    state_load.wait()
    centered, scale = mean_and_scale(state[...].astype(F32) + lead_row)
    rows[...] = (centered * scale * columns[0:1] + columns[1:2]).astype(BF16)
    turned[...] = rows[...].T
    stores = [pltpu.make_async_copy(turned, turned_out, io_sems.at[1])]
    stores[0].start()
    wait_all(loads[0] + loads[1])
    for part in range(3):
        span = slice(part * WIDTH, part * WIDTH + WIDTH)
        qkv[:, span] = times(rows[...], weight[:, span]).astype(BF16)
        stores.append(pltpu.make_async_copy(qkv.at[:, span], qkv_out.at[:, span], io_sems.at[2 + part]))
        stores[-1].start()
    wait_all(stores)


def front_forward(where, lead_index, patches, arrays):
    return call(
        front_kernel,
        (where, lead_index, patches, *arrays),
        [SMEM, SMEM, HBM] + [HBM] * 4,
        [
            ((WIDTH, TOKENS), BF16, True),
            ((TOKENS, 3 * WIDTH), BF16, True),
            ((32, WIDTH), F32, False),
        ],
        weight_scratch(WIDTH, 3 * WIDTH)
        + [pltpu.VMEM((WIDTH, 128), BF16), pltpu.SemaphoreType.DMA((16,))]
        + [
            pltpu.VMEM((TOKENS, WIDTH), BF16),
            pltpu.VMEM((TOKENS, WIDTH), BF16),
            pltpu.VMEM((WIDTH, TOKENS), BF16),
            pltpu.VMEM((TOKENS, 3 * WIDTH), BF16),
            pltpu.SemaphoreType.DMA((5,)),
        ],
    )


KEY_SPANS = ((0, 256), (0, 384), (128, 512), (256, 512))


def fill_bias(lengths, pad, bias):
    ends, end = [], 0
    for index in range(lengths.shape[1]):
        end = end + lengths[0, index]
        ends.append(end)

    def windows(places):
        return sum([(places >= end).astype(jnp.int32) for end in ends])

    for block, (low, high) in enumerate(KEY_SPANS):
        count = high - low
        queries = lax.broadcasted_iota(jnp.int32, (1, 128), 1) + 128 * block
        keys = lax.broadcasted_iota(jnp.int32, (count, 1), 0) + low
        same = windows(queries) == windows(keys)
        usable = (pad[low:high, :] > 0) | (queries == keys)
        bias[block, :count, :] = jnp.where(same & usable, 0.0, -1e30)


def two_heads(block):
    first = lax.broadcasted_iota(jnp.int32, block.shape, 1) < block.shape[1] // 2
    zero = jnp.zeros_like(block)
    return jnp.concatenate([jnp.where(first, block, zero), jnp.where(first, zero, block)], axis=0)


def head_rows_of(stacked):
    return jnp.concatenate([stacked[:64, :128], stacked[64:, 128:]], axis=0)


def probabilities(scores, allowed):
    masked = scores * score_scale + allowed
    raised = jnp.exp(masked - jnp.max(masked, axis=0, keepdims=True))
    return raised * (1.0 / jnp.sum(raised, axis=0, keepdims=True))


def attention_kernel(where, lengths, pad, qkv, attended_out, turned_out, bias, turned, rows, sems):
    fill_bias(lengths, pad, bias)

    def pair(index, carry):
        first = index * 128
        columns = pl.ds(pl.multiple_of(first, 128), 128)
        keys_at = pl.ds(pl.multiple_of(first + WIDTH, 128), 128)
        values = qkv[:, pl.ds(pl.multiple_of(first + 2 * WIDTH, 128), 128)].T
        for block, (low, high) in enumerate(KEY_SPANS):
            span = slice(128 * block, 128 * block + 128)
            scores = across(qkv[low:high, keys_at], two_heads(qkv[span, columns]))
            allowed = bias[block, : high - low, :]
            probs = [
                probabilities(scores[:, 128 * head : 128 * head + 128], allowed).astype(BF16)
                for head in range(2)
            ]
            mixed = times(values[:, low:high], jnp.concatenate(probs, axis=1))
            turned[columns, span] = head_rows_of(mixed).astype(BF16)
        return carry

    lax.fori_loop(0, WIDTH // 128, pair, 0)
    stores = [pltpu.make_async_copy(turned, turned_out, sems.at[0])]
    stores[0].start()
    rows[...] = turned[...].T
    stores.append(pltpu.make_async_copy(rows, attended_out, sems.at[1]))
    stores[1].start()
    wait_all(stores)


def attention_forward(where, lengths, pad, qkv):
    rows, columns = (TOKENS, WIDTH), (WIDTH, TOKENS)
    return call(
        attention_kernel,
        (where, lengths, pad, qkv),
        [SMEM, SMEM, VMEM, VMEM],
        [(rows, BF16, True), (columns, BF16, True)],
        [
            pltpu.VMEM((4, 384, 128), F32),
            pltpu.VMEM(columns, BF16),
            pltpu.VMEM(rows, BF16),
            pltpu.SemaphoreType.DMA((2,)),
        ],
    )


def up_kernel(where, attended, patches, small, bias, *refs):
    sources, outs, scratch = taken(refs, 4, 5)
    mid_out, mlp_turned_out, act_out, act_turned_out, slope_out = outs
    out_weight, out_sems, weight, sems, scratch = *scratch[:4], scratch[4:]
    inputs, state, mid, rows, mlp_turned, act, act_turned, slope, io_sems, act_sems = scratch
    out_loads = [block_copies(where, "u", sources, OUT_PART, out_weight, out_sems, s) for s in range(2)]
    loads = [block_copies(where, "u", sources, UP_PART, weight, sems, side) for side in range(2)]
    in_loads = [
        pltpu.make_async_copy(attended, inputs, io_sems.at[0]),
        pltpu.make_async_copy(patches, state, io_sems.at[1]),
    ]
    start_all(in_loads)
    start_all(out_loads[0] + out_loads[1])
    start_all(loads[0] + loads[1])
    wait_all(in_loads)
    wait_all(out_loads[0] + out_loads[1])
    mid[...] = (
        state[...].astype(F32)
        + small[16:17, :]
        + times(inputs[...], out_weight[...])
        + small[2:3, :]
    )
    centered, scale = mean_and_scale(mid[...])
    rows[...] = (centered * scale * small[3:4, :] + small[4:5, :]).astype(BF16)
    mlp_turned[...] = rows[...].T
    stores = [
        pltpu.make_async_copy(mid, mid_out, io_sems.at[2]),
        pltpu.make_async_copy(mlp_turned, mlp_turned_out, io_sems.at[3]),
    ]
    start_all(stores)
    wait_all(loads[0] + loads[1])
    for slot in range(6):
        span = slice(slot * 512, slot * 512 + 512)
        values = times(rows[...], weight[:, span]) + bias[:, span]
        share = 0.5 * (1.0 + lax.erf(values * 0.7071067811865476))
        density = jnp.exp(-0.5 * values * values) * 0.3989422804014327
        activated = (values * share).astype(BF16)
        act[:, span] = activated
        act_turned[span, :] = activated.T
        slope[:, span] = (share + values * density).astype(BF16)
        copies = [
            pltpu.make_async_copy(act.at[:, span], act_out.at[:, span], act_sems.at[slot, 0]),
            pltpu.make_async_copy(
                act_turned.at[span, :], act_turned_out.at[span, :], act_sems.at[slot, 1]
            ),
            pltpu.make_async_copy(slope.at[:, span], slope_out.at[:, span], act_sems.at[slot, 2]),
        ]
        start_all(copies)
        stores += copies
    wait_all(stores)


def up_forward(where, attended, patches, small, bias, arrays):
    rows, columns = (TOKENS, WIDTH), (WIDTH, TOKENS)
    wide, tall = (TOKENS, HIDDEN), (HIDDEN, TOKENS)
    return call(
        up_kernel,
        (where, attended, patches, small, bias, *arrays),
        [SMEM, HBM, HBM, VMEM, VMEM] + [HBM] * 4,
        [
            (rows, F32, True),
            (columns, BF16, True),
            (wide, BF16, True),
            (tall, BF16, True),
            (wide, BF16, True),
        ],
        weight_scratch(WIDTH, WIDTH)
        + weight_scratch(WIDTH, HIDDEN)
        + [
            pltpu.VMEM(rows, BF16),
            pltpu.VMEM(rows, BF16),
            pltpu.VMEM(rows, F32),
            pltpu.VMEM(rows, BF16),
            pltpu.VMEM(columns, BF16),
            pltpu.VMEM(wide, BF16),
            pltpu.VMEM(tall, BF16),
            pltpu.VMEM(wide, BF16),
            pltpu.SemaphoreType.DMA((4,)),
            pltpu.SemaphoreType.DMA((6, 3)),
        ],
    )


def gate_shares(logits, cotangent, shares, gate_grad):
    shares[:, 256:] = logits[:, 256:]
    gate_grad[:, 256:] = cotangent[:, 256:GATE]
    first, rest = logits[:, :128], logits[:, 128:256]
    left = lax.broadcasted_iota(jnp.int32, first.shape, 1) < PIX
    third = jnp.where(left, rest, pltpu.roll(rest, PIX, 1))
    largest = jnp.maximum(jnp.maximum(first, pltpu.roll(first, PIX, 1)), third)
    raised, raised_third = jnp.exp(first - largest), jnp.exp(third - largest)
    scale = 1.0 / (raised + pltpu.roll(raised, PIX, 1) + raised_third)
    share, share_third = raised * scale, raised_third * scale
    shares[:, :128] = share
    shares[:, 128:256] = jnp.where(left, share_third, rest)
    pull, other = cotangent[:, :128].astype(F32), cotangent[:, 128:256].astype(F32)
    pull_third = jnp.where(left, other, pltpu.roll(other, PIX, 1))
    weighed = share * pull
    inner = weighed + pltpu.roll(weighed, PIX, 1) + share_third * pull_third
    gate_grad[:, :128] = (share * (pull - inner)).astype(BF16)
    gate_grad[:, 128:256] = jnp.where(left, share_third * (pull_third - inner), other).astype(BF16)


def down_kernel(where, act, mid, small, cotangent, bias, *refs):
    sources, gate_sources, outs, scratch = taken(refs, 4, 4, 6)
    outputs, shares, gate_grad, gate_bias, mine_out, theirs_out = outs
    weight, sems, gate, gate_sems, lane, lane_sems, scratch = *scratch[:6], scratch[6:]
    acts, mids, pulls, turned, logits, io_sems = scratch
    loads = [block_copies(where, "d", sources, DOWN_PART, weight, sems, side) for side in range(2)]
    gate_loads = [
        block_copies(where, "u", gate_sources, GATE_PART, gate, gate_sems, side) for side in range(2)
    ]
    in_loads = [
        pltpu.make_async_copy(act, acts, io_sems.at[0]),
        pltpu.make_async_copy(mid, mids, io_sems.at[1]),
    ]
    pull_load = pltpu.make_async_copy(cotangent, pulls, io_sems.at[2])
    start_all(in_loads)
    start_all(loads[0] + loads[1])
    start_all(gate_loads[0] + gate_loads[1])
    pull_load.start()
    wait_all(in_loads)
    wait_all(loads[0] + loads[1])
    outputs[...] = (mids[...] + times(acts[...], weight[...]) + small[5:6, :]).astype(BF16)
    turned[...] = outputs[...].T
    wait_all(gate_loads[0] + gate_loads[1])
    logits[...] = times(outputs[...], gate[...]) + bias[:, :GATE]
    pull_load.wait()
    gate_shares(logits, pulls, shares, gate_grad)
    gate_bias[...] = jnp.sum(gate_grad[...].astype(F32), axis=0, keepdims=True)
    stores = []
    for side, out in ((1, theirs_out), (0, mine_out)):
        lane[side, :, :256] = times(
            turned[...], gate_grad[:, lane_columns(where, side, 256)]
        ).astype(BF16)
        for tile in range(4):
            span = lane_columns(where, side, 2048, GATE + tile * 512, 512)
            lane[side, :, 256 + tile * 512 : 768 + tile * 512] = times(
                turned[...], pulls[:, span]
            ).astype(BF16)
        copies = term_copies(where, "head", lane, out, lane_sems, side)
        start_all(copies)
        stores += copies
    wait_all(stores)


def down_forward(where, act, mid, small, cotangent, bias, arrays, gate_arrays):
    rows = (TOKENS, WIDTH)
    return call(
        down_kernel,
        (where, act, mid, small, cotangent, bias, *arrays, *gate_arrays),
        [SMEM, HBM, HBM, VMEM, HBM, VMEM] + [HBM] * 8,
        [
            (rows, BF16, False),
            ((TOKENS, GATE), F32, False),
            ((TOKENS, GATE), BF16, False),
            ((1, GATE), F32, False),
            ((16, 48, 2304), BF16, True),
            ((16, 48, 2304), BF16, True),
        ],
        weight_scratch(HIDDEN, WIDTH)
        + weight_scratch(WIDTH, GATE)
        + lane_scratch(WIDTH, 2304)
        + [
            pltpu.VMEM((TOKENS, HIDDEN), BF16),
            pltpu.VMEM(rows, F32),
            pltpu.VMEM((TOKENS, HEAD), BF16),
            pltpu.VMEM((WIDTH, TOKENS), BF16),
            pltpu.VMEM((TOKENS, GATE), F32),
            pltpu.SemaphoreType.DMA((3,)),
        ],
    )


def head_kernel(where, rows, gate_out, bias, *refs):
    sources, outs, scratch = taken(refs, 4, 1)
    (out,) = outs
    weight, sems, inputs, result, io_sems = scratch
    loads = [block_copies(where, "h", sources, HEAD_PART, weight, sems, side) for side in range(2)]
    row_load = pltpu.make_async_copy(rows, inputs, io_sems.at[0])
    gate_load = pltpu.make_async_copy(gate_out, result.at[:, :GATE], io_sems.at[1])
    row_load.start()
    start_all(loads[0])
    start_all(loads[1])
    gate_load.start()
    row_load.wait()
    stores = []

    def store(span):
        stores.append(
            pltpu.make_async_copy(result.at[:, span], out.at[:, span], io_sems.at[2 + len(stores)])
        )
        stores[-1].start()

    for side in range(2):
        wait_all(loads[side])
        for tile in range(4):
            span = lane_columns(where, side, 2048, GATE + tile * 512, 512)
            columns = lane_columns(where, side, 2048, tile * 512, 512)
            result[:, span] = times(inputs[...], weight[:, columns]) + bias[:, span]
            store(span)
    gate_load.wait()
    store(pl.ds(0, GATE))
    wait_all(stores)


def head_forward(where, rows, gate_out, bias, arrays):
    return call(
        head_kernel,
        (where, rows, gate_out, bias, *arrays),
        [SMEM, HBM, HBM, VMEM] + [HBM] * 4,
        [((TOKENS, HEAD), F32, True)],
        weight_scratch(WIDTH, HEAD - GATE)
        + [
            pltpu.VMEM((TOKENS, WIDTH), BF16),
            pltpu.VMEM((TOKENS, HEAD), F32),
            pltpu.SemaphoreType.DMA((11,)),
        ],
    )[0]


def head_back_kernel(where, act_cotangent, gate_grad, cotangent, slope, *refs):
    sources, gate_sources, down_sources, outs, scratch = taken(refs, 4, 4, 4, 5)
    end_grad, branch, down_bias, up_bias, pre_out = outs
    weight, sems, gate_sems, down, down_sems, scratch = *scratch[:5], scratch[5:]
    act_pulls, pulls, slopes, pre_grad, io_sems, pre_sems = scratch
    loads = [
        block_copies(where, "h", sources, HEAD_PART, weight, sems, side, GATE) for side in range(2)
    ]
    gate_loads = [
        block_copies(where, "u", gate_sources, GATE_PART, weight, gate_sems, side)
        for side in range(2)
    ]
    down_loads = [
        block_copies(where, "d", down_sources, DOWN_PART, down, down_sems, side) for side in range(2)
    ]
    first_loads = [
        pltpu.make_async_copy(act_cotangent, act_pulls, io_sems.at[0]),
        pltpu.make_async_copy(gate_grad, pulls.at[:, :GATE], io_sems.at[1]),
    ]
    pull_load = pltpu.make_async_copy(cotangent.at[:, GATE:], pulls.at[:, GATE:], io_sems.at[2])
    slope_load = pltpu.make_async_copy(slope, slopes, io_sems.at[3])
    start_all(first_loads + gate_loads[0] + gate_loads[1])
    pull_load.start()
    start_all(loads[0])
    start_all(loads[1])
    start_all(down_loads[0] + down_loads[1])
    slope_load.start()
    wait_all(first_loads)
    wait_all(gate_loads[0] + gate_loads[1])
    pull_load.wait()
    wait_all(loads[0] + loads[1])
    end_grad[...] = act_pulls[...].astype(F32) + across(pulls[...], weight[...])
    branch[...] = end_grad[...].astype(BF16)
    down_bias[...] = jnp.sum(branch[...].astype(F32), axis=0, keepdims=True)
    wait_all(down_loads[0] + down_loads[1])
    slope_load.wait()
    stores = []
    for tile in range(6):
        span = slice(tile * 512, tile * 512 + 512)
        grad = across(branch[...], down[span, :])
        rounded = (slopes[:, span].astype(F32) * grad).astype(BF16)
        pre_grad[:, span] = rounded
        up_bias[:, span] = jnp.sum(rounded.astype(F32), axis=0, keepdims=True)
        stores.append(
            pltpu.make_async_copy(pre_grad.at[:, span], pre_out.at[:, span], pre_sems.at[tile])
        )
        stores[-1].start()
    wait_all(stores)


def head_backward(where, act_cotangent, gate_grad, cotangent, slope, arrays, gate_arrays, down_arrays):
    rows, wide = (TOKENS, WIDTH), (TOKENS, HIDDEN)
    return call(
        head_back_kernel,
        (where, act_cotangent, gate_grad, cotangent, slope, *arrays, *gate_arrays, *down_arrays),
        [SMEM, HBM, HBM, HBM, HBM] + [HBM] * 12,
        [
            (rows, F32, False),
            (rows, BF16, False),
            ((1, WIDTH), F32, False),
            ((1, HIDDEN), F32, False),
            (wide, BF16, True),
        ],
        weight_scratch(WIDTH, HEAD)
        + [pltpu.SemaphoreType.DMA((2, 16))]
        + weight_scratch(HIDDEN, WIDTH)
        + [
            pltpu.VMEM(rows, BF16),
            pltpu.VMEM((TOKENS, HEAD), BF16),
            pltpu.VMEM(wide, BF16),
            pltpu.VMEM(wide, BF16),
            pltpu.SemaphoreType.DMA((4,)),
            pltpu.SemaphoreType.DMA((6,)),
        ],
    )


def up_back_kernel(
    where, small, pre_grad, branch, act_turned, mlp_turned, mid, end_grad, *refs
):
    sources, outs, scratch = taken(refs, 4, 7)
    mid_grad, out_grad, terms, down_mine, down_theirs, up_mine, up_theirs = outs
    weight, sems, down_lane, down_sems, up_lane, up_sems, scratch = *scratch[:6], scratch[6:]
    pres, branches, acts, mlps, mids, ends, io_sems = scratch
    loads = [block_copies(where, "u", sources, UP_PART, weight, sems, side) for side in range(2)]
    pre_load = pltpu.make_async_copy(pre_grad, pres, io_sems.at[0])
    branch_load = pltpu.make_async_copy(branch, branches, io_sems.at[1])
    act_load = pltpu.make_async_copy(act_turned, acts, io_sems.at[2])
    mlp_load = pltpu.make_async_copy(mlp_turned, mlps, io_sems.at[3])
    norm_loads = [
        pltpu.make_async_copy(mid, mids, io_sems.at[4]),
        pltpu.make_async_copy(end_grad, ends, io_sems.at[5]),
    ]
    branch_load.start()
    act_load.start()
    pre_load.start()
    mlp_load.start()
    start_all(loads[0] + loads[1])
    start_all(norm_loads)
    branch_load.wait()
    act_load.wait()
    stores = []
    for side, out in ((1, down_theirs), (0, down_mine)):
        span = lane_columns(where, side, 384)
        for part in range(4):
            rows = slice(part * WIDTH, part * WIDTH + WIDTH)
            down_lane[side, rows, :] = times(acts[rows, :], branches[:, span]).astype(BF16)
        copies = term_copies(where, "down", down_lane, out, down_sems, side)
        start_all(copies)
        stores += copies
    pre_load.wait()
    mlp_load.wait()
    for side, out in ((1, up_theirs), (0, up_mine)):
        for tile in range(3):
            span = lane_columns(where, side, 1536, tile * 512, 512)
            up_lane[side, :, tile * 512 : tile * 512 + 512] = times(mlps[...], pres[:, span]).astype(
                BF16
            )
        copies = term_copies(where, "up", up_lane, out, up_sems, side)
        start_all(copies)
        stores += copies
    wait_all(loads[0] + loads[1])
    grad = across(pres[...], weight[...])
    wait_all(norm_loads)
    pulled, gain_grad, shift_grad = norm_backward(mids[...], small[3:4, :], grad)
    pulled = pulled + ends[...]
    rounded = pulled.astype(BF16)
    mid_grad[...] = pulled
    out_grad[...] = rounded
    terms[...] = jnp.zeros_like(terms)
    terms[0:1, :] = jnp.sum(rounded.astype(F32), axis=0, keepdims=True)
    terms[1:2, :] = gain_grad
    terms[2:3, :] = shift_grad
    wait_all(stores)


def up_backward(
    where, small, pre_grad, branch, act_turned, mlp_turned, mid, end_grad, arrays
):
    rows = (TOKENS, WIDTH)
    return call(
        up_back_kernel,
        (where, small, pre_grad, branch, act_turned, mlp_turned, mid, end_grad, *arrays),
        [SMEM, VMEM] + [HBM] * 10,
        [
            (rows, F32, False),
            (rows, BF16, False),
            ((8, WIDTH), F32, False),
            ((16, 192, 384), BF16, True),
            ((16, 192, 384), BF16, True),
            ((16, 48, 1536), BF16, True),
            ((16, 48, 1536), BF16, True),
        ],
        weight_scratch(WIDTH, HIDDEN)
        + lane_scratch(HIDDEN, 384)
        + lane_scratch(WIDTH, 1536)
        + [
            pltpu.VMEM((TOKENS, HIDDEN), BF16),
            pltpu.VMEM(rows, BF16),
            pltpu.VMEM((HIDDEN, TOKENS), BF16),
            pltpu.VMEM((WIDTH, TOKENS), BF16),
            pltpu.VMEM(rows, F32),
            pltpu.VMEM(rows, F32),
            pltpu.SemaphoreType.DMA((6,)),
        ],
    )


def attention_back_kernel(start, count, where, lengths, pad, out_grad, qkv, *refs):
    sources, outs, scratch = taken(refs, 4, 1)
    (qkv_grad,) = outs
    weight, sems, bias, mixed, turned, key_sum, value_sum = scratch
    loads = [block_copies(where, "u", sources, OUT_PART, weight, sems, side) for side in range(2)]
    start_all(loads[0] + loads[1])
    fill_bias(lengths, pad, bias)
    wait_all(loads[0] + loads[1])
    width = 128 * count
    mixed[...] = across(
        out_grad[...], weight[128 * start : 128 * start + width, :]
    ).astype(BF16)

    def columns_at(first):
        return pl.ds(pl.multiple_of(first, 128), 128)

    def pair(index, carry):
        own, first = index * 128, (index + start) * 128
        columns, keys_at = columns_at(first), columns_at(first + WIDTH)
        values_at = columns_at(first + 2 * WIDTH)
        keys_turned = qkv[:, keys_at].T
        key_sum[...] = jnp.zeros_like(key_sum)
        value_sum[...] = jnp.zeros_like(value_sum)
        for block, (low, high) in enumerate(KEY_SPANS):
            span = slice(128 * block, 128 * block + 128)
            queries, grads = two_heads(qkv[span, columns]), two_heads(mixed[span, columns_at(own)])
            scores = across(qkv[low:high, keys_at], queries)
            prob_grads = across(qkv[low:high, values_at], grads)
            allowed = bias[block, : high - low, :]
            probs, score_grads = [], []
            for head in range(2):
                part = slice(128 * head, 128 * head + 128)
                prob = probabilities(scores[:, part], allowed)
                pulled = prob * prob_grads[:, part]
                inner = jnp.sum(pulled, axis=0, keepdims=True)
                probs.append(prob.astype(BF16))
                score_grads.append((pulled - prob * inner).astype(BF16))
            score_grad = jnp.concatenate(score_grads, axis=1)
            key_sum[low:high, :] += times(score_grad, queries)
            value_sum[low:high, :] += times(jnp.concatenate(probs, axis=1), grads)
            turned[:, span] = head_rows_of(times(keys_turned[:, low:high], score_grad)) * score_scale
        qkv_grad[:, columns_at(own)] = turned[...].T.astype(BF16)
        qkv_grad[:, columns_at(own + width)] = (key_sum[...] * score_scale).astype(BF16)
        qkv_grad[:, columns_at(own + 2 * width)] = value_sum[...].astype(BF16)
        return carry

    lax.fori_loop(0, count, pair, 0)


def attention_backward(where, lengths, pad, out_grad, qkv, arrays, start, count):
    return call(
        partial(attention_back_kernel, start, count),
        (where, lengths, pad, out_grad, qkv, *arrays),
        [SMEM, SMEM, VMEM, VMEM, VMEM] + [HBM] * 4,
        [((TOKENS, 3 * 128 * count), BF16, False)],
        weight_scratch(WIDTH, WIDTH)
        + [
            pltpu.VMEM((4, 384, 128), F32),
            pltpu.VMEM((TOKENS, 128 * count), BF16),
            pltpu.VMEM((128, TOKENS), F32),
            pltpu.VMEM((TOKENS, 128), F32),
            pltpu.VMEM((TOKENS, 128), F32),
        ],
    )[0]


def mix_term_kernel(where, qkv_grad, input_turned, attended_turned, out_grad, mine_out, theirs_out, *refs):
    lane, sems = refs
    stores = []
    for side, out in ((1, theirs_out), (0, mine_out)):
        lane[side, :, :768] = times(
            input_turned[...], qkv_grad[:, lane_columns(where, side, 768)]
        ).astype(BF16)
        lane[side, :, 768:1152] = times(
            attended_turned[...], out_grad[:, lane_columns(where, side, 384)]
        ).astype(BF16)
        copies = term_copies(where, "front", lane, out, sems, side)
        start_all(copies)
        stores += copies
    wait_all(stores)


def mix_terms(where, qkv_grad, input_turned, attended_turned, out_grad):
    return call(
        mix_term_kernel,
        (where, qkv_grad, input_turned, attended_turned, out_grad),
        [SMEM] + [VMEM] * 4,
        [((16, 48, 1152), BF16, True)] * 2,
        lane_scratch(WIDTH, 1152),
    )


def front_back_kernel(
    where, lead, small, terms, down_row, up_rows, head_rows,
    first_grad, second_grad, patches, mid_grad, input_turned, *refs
):
    sources, outs, scratch = taken(refs, 4, 3)
    patch_out, mine_out, theirs_out = outs
    weight, sems, lane, lane_sems, scratch = *scratch[:4], scratch[4:]
    pulls, late_pulls, state, mids, inputs, patch_grad, small_grad, io_sems = scratch
    loads = [block_copies(where, "q", sources, QKV_PART, weight, sems, side) for side in range(2)]
    pairs = [(patches, state), (mid_grad, mids), (input_turned, inputs), (second_grad, late_pulls)]
    for part in range(3):
        for source, start, size in ((first_grad, 0, 512), (second_grad, 512, 256)):
            columns = pl.ds(WIDTH * part + start, size)
            pairs.append((source.at[:, pl.ds(size * part, size)], pulls.at[:, columns]))
    in_loads = [pltpu.make_async_copy(*pair, io_sems.at[at]) for at, pair in enumerate(pairs)]
    start_all(in_loads[4:])
    start_all(loads[0] + loads[1])
    start_all(in_loads[:4])
    wait_all(in_loads[4:])
    wait_all(loads[0] + loads[1])
    grad = across(pulls[...], weight[...])
    wait_all(in_loads[:4])
    pulled, gain_grad, shift_grad = norm_backward(
        state[...].astype(F32) + small[16:17, :], small[0:1, :], grad
    )
    pulled = pulled + mids[...]
    patch_grad[...] = pulled
    stores = [pltpu.make_async_copy(patch_grad, patch_out, io_sems.at[10])]
    stores[0].start()
    small_grad[0:1, :] = gain_grad
    small_grad[1:2, :] = shift_grad
    small_grad[2:5, :] = terms[0:3, :]
    small_grad[5:6, :] = down_row[...]
    small_grad[6:10, :] = up_rows[...]
    small_grad[10:16, :] = head_rows[...]
    places = lax.broadcasted_iota(jnp.int32, (LEADS, WIDTH), 0)
    lead_grad = jnp.sum(pulled, axis=0, keepdims=True)
    small_grad[16:32, :] = jnp.where(places == lead[0], lead_grad, 0.0)
    for side, out in ((1, theirs_out), (0, mine_out)):
        lane[side, :, :384] = times(
            inputs[...], late_pulls[:, lane_columns(where, side, 384)]
        ).astype(BF16)
        rows = small_grad[pl.ds(pl.multiple_of((where[0] ^ side) * 16, 16), 16), :]
        rows = jnp.concatenate([rows, jnp.zeros((112, WIDTH), F32)], axis=0)
        lane[side, :, 384:] = rows.T.astype(BF16)
        copies = term_copies(where, "front", lane, out, lane_sems, side)
        start_all(copies)
        stores += copies
    wait_all(stores)


def front_backward(
    where, lead, small, terms, down_row, up_rows, head_rows,
    first_grad, second_grad, patches, mid_grad, input_turned, arrays,
):
    rows, columns = (TOKENS, WIDTH), (WIDTH, TOKENS)
    return call(
        front_back_kernel,
        (
            where, lead, small, terms, down_row, up_rows, head_rows,
            first_grad, second_grad, patches, mid_grad, input_turned, *arrays,
        ),
        [SMEM, SMEM] + [VMEM] * 5 + [HBM] * 9,
        [(rows, F32, True), ((16, 48, 512), BF16, True), ((16, 48, 512), BF16, True)],
        weight_scratch(WIDTH, 3 * WIDTH)
        + lane_scratch(WIDTH, 512)
        + [
            pltpu.VMEM((TOKENS, 3 * WIDTH), BF16),
            pltpu.VMEM(rows, BF16),
            pltpu.VMEM(rows, BF16),
            pltpu.VMEM(rows, F32),
            pltpu.VMEM(columns, BF16),
            pltpu.VMEM(rows, F32),
            pltpu.VMEM((32, WIDTH), F32),
            pltpu.SemaphoreType.DMA((11,)),
        ],
    )


def rows_of(vector, count):
    return vector.reshape(32, count, 24).transpose(1, 0, 2).reshape(count, WIDTH)


def vector_of(rows):
    count = rows.shape[0]
    return rows.reshape(count, 32, 24).transpose(1, 0, 2).reshape(1, count * WIDTH)


def shards(
    patches,
    lead_index,
    window_lengths,
    pad_mask,
    lead_table,
    attn_gain,
    attn_shift,
    qkv_weight,
    out_weight,
    out_bias,
    mlp_gain,
    mlp_shift,
    up_weight,
    up_bias,
    down_weight,
    down_bias,
    head_weight,
    head_bias,
    act_cotangent,
    head_cotangent,
):
    core, where = whereabouts()
    weights = (qkv_weight, out_weight, up_weight, down_weight, head_weight)
    vectors = (
        attn_gain, attn_shift, out_bias, mlp_gain, mlp_shift, down_bias, up_bias, head_bias
    )
    parts = packed(core, weights, lead_table, vectors)
    pad = pad_mask[:, None]
    cotangent_sum = jnp.sum(head_cotangent[:, GATE:].astype(F32), axis=0, keepdims=True)

    orders = ORDERS
    parts = dict(zip("qudh", zip(parts[:4], parts[4:])))
    chunks = {
        name: in_core_order(core, mine, exchange(theirs, SIBLING), 0)[None]
        for name, (mine, theirs) in parts.items()
    }

    held, last = dict(chunks), ()
    for name, step in GATHER_SEQUENCE:
        held[name] = after(held[name], *last)
        last = (held[name],)
        held[name] = doubled(held[name], orders[name][step])
    q, u, d, h = [held[name] for name in ("q", "u", "d", "h")]
    q_rest = exchange(after(q, *last), orders["q"][3])
    u_rest = exchange(u, orders["u"][3])
    first = both_lanes(q, q_rest)
    input_turned, qkv, small_rows = front_forward(
        after(where, d, h, u, cotangent_sum), lead_index, patches, first
    )
    attended, attended_turned = attention_forward(where, window_lengths, pad, qkv)
    second = both_lanes(u, after(u_rest, attended))
    d_rest = exchange(after(d, attended), orders["d"][3])
    up_bias_row, head_bias_row = vector_of(small_rows[6:10]), vector_of(small_rows[10:16])
    mid_state, mlp_turned, act_rows, act_turned, slope = up_forward(
        where, attended, patches, small_rows, up_bias_row, second
    )
    down = both_lanes(d, after(d_rest, act_rows))
    h_rest = exchange(after(h, act_rows), orders["h"][3])
    outputs, gate_out, gate_grad, gate_bias_sum, mine_h, theirs_h = down_forward(
        where, act_rows, mid_state, small_rows, head_cotangent, head_bias_row, down, second
    )
    head = both_lanes(h, after(h_rest, theirs_h))
    got_h = exchange(theirs_h, SIBLING)
    end_grad, branch_grad, down_bias_sum, up_bias_sum, pre_grad = head_backward(
        after(where, theirs_h), act_cotangent, gate_grad, head_cotangent, slope, head, second, down
    )
    head_rows = rows_of(jnp.concatenate([gate_bias_sum, cotangent_sum], axis=1), 6)
    up_rows = rows_of(up_bias_sum, 4)
    keep_h, send_h = folded(mine_h, after(got_h, pre_grad))
    got_h = exchange(send_h, orders["head"][3])
    mid_grad, out_grad, terms, mine_d, theirs_d, mine_u, theirs_u = up_backward(
        after(where, send_h), small_rows, pre_grad, branch_grad, act_turned, mlp_turned,
        mid_state, end_grad, second,
    )
    got_d, got_u = exchange(theirs_d, SIBLING), exchange(theirs_u, SIBLING)
    pulled = (window_lengths, pad, out_grad, qkv, second)
    first_grad = attention_backward(where, *pulled, 0, 4)
    keep_h, send_h = folded(keep_h, after(got_h, first_grad))
    got_h = exchange(send_h, orders["head"][2])
    keep_u, send_u = folded(mine_u, after(got_u, first_grad))
    got_u = exchange(send_u, orders["up"][3])
    keep_d, send_d = folded(mine_d, after(got_d, first_grad))
    got_d = exchange(send_d, orders["down"][3])
    mine_m, theirs_m = mix_terms(
        after(where, send_h, send_d, send_u), first_grad, input_turned, attended_turned, out_grad
    )
    got_m = exchange(theirs_m, SIBLING)
    second_grad = attention_backward(after(where, theirs_m), *pulled, 4, 2)
    keep_m, send_m = folded(mine_m, after(got_m, second_grad))
    got_m = exchange(send_m, orders["front"][3])
    keep_h, send_h = folded(keep_h, after(got_h, second_grad))
    got_h = exchange(send_h, orders["head"][1])
    patch_grad, mine_f, theirs_f = front_backward(
        after(where, send_h, send_m), lead_index, small_rows, terms, down_bias_sum,
        up_rows, head_rows, first_grad, second_grad, patches, mid_grad, input_turned, first,
    )
    got_f = exchange(theirs_f, SIBLING)
    keep_m, send_m = folded(keep_m, after(got_m, patch_grad))
    got_m = exchange(send_m, orders["front"][2])
    keep_f, send_f = folded(mine_f, after(got_f, send_m))
    got_f = exchange(send_f, orders["front"][3])
    keep_d, send_d = folded(keep_d, after(got_d, send_f))
    got_d = exchange(send_d, orders["down"][2])
    keep_h, send_h = folded(keep_h, after(got_h, send_f))
    got_h = exchange(send_h, orders["head"][0])
    keep_u, send_u = folded(keep_u, after(got_u, send_f))
    got_u = exchange(send_u, orders["up"][2])
    head_out = head_forward(
        after(where, send_m, send_u, send_d, send_h), outputs, gate_out, head_bias_row, head
    )
    keep_f, send_f = folded(keep_f, after(got_f, head_out))
    got_f = exchange(send_f, orders["front"][2])
    keep_m, send_m = folded(keep_m, after(got_m, send_f))
    got_m = exchange(send_m, orders["front"][1])
    keep_d, send_d = folded(keep_d, after(got_d, send_f))
    got_d = exchange(send_d, orders["down"][1])
    keep_u, send_u = folded(keep_u, after(got_u, send_f))
    got_u = exchange(send_u, orders["up"][1])
    keep_f, send_f = folded(keep_f, after(got_f, send_m, send_d, send_u))
    got_f = exchange(send_f, orders["front"][1])
    keep_m, send_m = folded(keep_m, after(got_m, send_f))
    got_m = exchange(send_m, orders["front"][0])
    keep_d, send_d = folded(keep_d, after(got_d, send_f))
    got_d = exchange(send_d, orders["down"][0])
    keep_u, send_u = folded(keep_u, after(got_u, send_f))
    got_u = exchange(send_u, orders["up"][0])
    gate_sum, rest_sum = finished(keep_h, after(got_h, send_u), core, (256, 2048))
    keep_f, send_f = folded(keep_f, after(got_f, send_u))
    got_f = exchange(send_f, orders["front"][0])
    early_sum, out_sum = finished(keep_m, after(got_m, send_f), core, (768, 384))
    (down_sum,) = finished(keep_d, after(got_d, send_f), core, (384,))
    (up_sum,) = finished(keep_u, after(got_u, send_f), core, (1536,))
    late_sum, small_sum = finished(keep_f, got_f, core, (384, 128))
    qkv_sum = jnp.concatenate(
        [
            piece[:, part * piece.shape[1] // 3 : (part + 1) * piece.shape[1] // 3]
            for part in range(3)
            for piece in (early_sum, late_sum)
        ],
        axis=1,
    )
    small_sum = small_sum.T
    return (
        outputs,
        head_out,
        patch_grad,
        small_sum[128:144],
        small_sum[0],
        small_sum[1],
        qkv_sum,
        out_sum,
        small_sum[2],
        small_sum[3],
        small_sum[4],
        up_sum,
        small_sum[6:10].reshape(96),
        down_sum,
        small_sum[5],
        jnp.concatenate([gate_sum, rest_sum], axis=1),
        small_sum[10:16].reshape(144),
    )


def plain_shards(
    patches,
    lead_index,
    window_lengths,
    pad_mask,
    lead_table,
    attn_gain,
    attn_shift,
    qkv_weight,
    out_weight,
    out_bias,
    mlp_gain,
    mlp_shift,
    up_weight,
    up_bias,
    down_weight,
    down_bias,
    head_weight,
    head_bias,
    act_cotangent,
    head_cotangent,
):
    front = (
        lax.all_gather(lead_table, ("dp", "fsdp"), axis=1, tiled=True),
        lax.all_gather(attn_gain, ("dp", "fsdp"), axis=0, tiled=True),
        lax.all_gather(attn_shift, ("dp", "fsdp"), axis=0, tiled=True),
        lax.all_gather(qkv_weight, ("dp", "fsdp"), axis=0, tiled=True),
        lax.all_gather(out_weight, ("dp", "fsdp"), axis=0, tiled=True),
        lax.all_gather(out_bias, ("dp", "fsdp"), axis=0, tiled=True),
    )
    rear = (
        lax.all_gather(mlp_gain, ("dp", "fsdp"), axis=0, tiled=True),
        lax.all_gather(mlp_shift, ("dp", "fsdp"), axis=0, tiled=True),
        lax.all_gather(up_weight, ("dp", "fsdp"), axis=0, tiled=True),
        lax.all_gather(up_bias, ("dp", "fsdp"), axis=0, tiled=True),
        lax.all_gather(down_weight, ("dp", "fsdp"), axis=0, tiled=True),
        lax.all_gather(down_bias, ("dp", "fsdp"), axis=0, tiled=True),
        lax.all_gather(head_weight, ("dp", "fsdp"), axis=0, tiled=True),
        lax.all_gather(head_bias, ("dp", "fsdp"), axis=0, tiled=True),
    )
    table_full, gain_one, shift_one, qkv_full, out_full, out_bias_full = front
    (
        gain_two,
        shift_two,
        up_full,
        up_bias_full,
        down_full,
        down_bias_full,
        head_full,
        head_bias_full,
    ) = rear
    token_rows, width = patches.shape
    head_dim = width // HEADS
    block_rows = min(512, token_rows)
    block_count = token_rows // block_rows
    ends = jnp.cumsum(window_lengths[0])
    positions = jnp.arange(token_rows, dtype=jnp.int32)
    window = jnp.sum((positions[:, None] >= ends[None, :]).astype(jnp.int32), axis=1)
    lead_hot = (jnp.arange(LEADS, dtype=jnp.int32) == lead_index[0]).astype(jnp.float32)
    lead_row = jnp.sum(lead_hot[:, None] * table_full.astype(jnp.float32), axis=0)
    start_state = patches.astype(jnp.float32) + lead_row[None, :]
    normed_one, pull_one = jax.vjp(
        layer_norm, start_state, gain_one.astype(jnp.float32), shift_one.astype(jnp.float32)
    )
    attn_input = normed_one.astype(jnp.bfloat16)
    qkv_rows = jnp.dot(attn_input, qkv_full, preferred_element_type=jnp.float32).astype(
        jnp.bfloat16
    )
    queries = qkv_rows[:, :width].reshape(block_count, block_rows, HEADS, head_dim)
    keys = qkv_rows[:, width : 2 * width].reshape(token_rows, HEADS, head_dim)
    values = qkv_rows[:, 2 * width :].reshape(token_rows, HEADS, head_dim)
    query_windows = window.reshape(block_count, block_rows)
    block_starts = jnp.arange(block_count, dtype=jnp.int32) * block_rows

    def block_scores(query_block, window_block, block_start):
        scores = (
            jnp.einsum("qhd,khd->hqk", query_block, keys, preferred_element_type=jnp.float32)
            * score_scale
        )
        allowed = allowed_keys(window_block, window, pad_mask, block_start)
        return jnp.where(allowed[None], scores, -1e30)

    def forward_block(inputs):
        query_block, window_block, block_start = inputs
        masked = block_scores(query_block, window_block, block_start)
        largest = jnp.max(masked, axis=-1, keepdims=True)
        raised = jnp.exp(masked - largest)
        total = jnp.sum(raised, axis=-1, keepdims=True)
        probs = (raised / total).astype(jnp.bfloat16)
        mixed = jnp.einsum("hqk,khd->qhd", probs, values, preferred_element_type=jnp.float32)
        return (
            mixed.reshape(block_rows, width).astype(jnp.bfloat16),
            (largest + jnp.log(total))[:, :, 0],
        )

    mixed_blocks, log_totals = lax.map(forward_block, (queries, query_windows, block_starts))
    attended = mixed_blocks.reshape(token_rows, width)
    mid_state = (
        start_state
        + jnp.dot(attended, out_full, preferred_element_type=jnp.float32)
        + out_bias_full.astype(jnp.float32)
    )
    normed_two, pull_two = jax.vjp(
        layer_norm, mid_state, gain_two.astype(jnp.float32), shift_two.astype(jnp.float32)
    )
    mlp_input = normed_two.astype(jnp.bfloat16)
    pre_act = jnp.dot(mlp_input, up_full, preferred_element_type=jnp.float32) + up_bias_full.astype(
        jnp.float32
    )
    activated, pull_act = jax.vjp(gelu_exact, pre_act)
    act_rows = activated.astype(jnp.bfloat16)
    end_state = (
        mid_state
        + jnp.dot(act_rows, down_full, preferred_element_type=jnp.float32)
        + down_bias_full.astype(jnp.float32)
    )
    outputs = end_state.astype(jnp.bfloat16)
    logits = jnp.dot(
        outputs, head_full, preferred_element_type=jnp.float32
    ) + head_bias_full.astype(jnp.float32)
    head_out, pull_head = jax.vjp(partial(expert_softmax, experts=EXPERTS, pixels=PIX), logits)
    up_back, down_back, head_back = (
        lax.all_gather(up_weight, ("dp", "fsdp"), axis=0, tiled=True),
        lax.all_gather(down_weight, ("dp", "fsdp"), axis=0, tiled=True),
        lax.all_gather(head_weight, ("dp", "fsdp"), axis=0, tiled=True),
    )
    qkv_back, out_back = (
        lax.all_gather(qkv_weight, ("dp", "fsdp"), axis=0, tiled=True),
        lax.all_gather(out_weight, ("dp", "fsdp"), axis=0, tiled=True),
    )
    logit_grad = pull_head(head_cotangent.astype(jnp.float32))[0].astype(jnp.bfloat16)
    head_bias_term = jnp.sum(logit_grad.astype(jnp.float32), axis=0)
    head_term = jnp.einsum("td,tn->dn", outputs, logit_grad, preferred_element_type=jnp.float32)
    end_grad = act_cotangent.astype(jnp.float32) + jnp.einsum(
        "tn,dn->td", logit_grad, head_back, preferred_element_type=jnp.float32
    )
    branch_grad = end_grad.astype(jnp.bfloat16)
    down_bias_term = jnp.sum(branch_grad.astype(jnp.float32), axis=0)
    down_term = jnp.einsum("tf,td->fd", act_rows, branch_grad, preferred_element_type=jnp.float32)
    act_grad = jnp.einsum("td,fd->tf", branch_grad, down_back, preferred_element_type=jnp.float32)
    pre_grad = pull_act(act_grad)[0].astype(jnp.bfloat16)
    up_bias_term = jnp.sum(pre_grad.astype(jnp.float32), axis=0)
    up_term = jnp.einsum("td,tf->df", mlp_input, pre_grad, preferred_element_type=jnp.float32)
    normed_two_grad = jnp.einsum("tf,df->td", pre_grad, up_back, preferred_element_type=jnp.float32)
    state_grad_two, gain_two_term, shift_two_term = pull_two(normed_two_grad)
    (
        gain_part,
        shift_part,
        up_part,
        up_bias_part,
        down_part,
        down_bias_part,
        head_part,
        head_bias_part,
    ) = (
        lax.psum_scatter(
            gain_two_term.astype(jnp.bfloat16), "dp", scatter_dimension=0, tiled=True
        ).astype(jnp.float32),
        lax.psum_scatter(
            shift_two_term.astype(jnp.bfloat16), "dp", scatter_dimension=0, tiled=True
        ).astype(jnp.float32),
        lax.psum_scatter(
            up_term.astype(jnp.bfloat16), "dp", scatter_dimension=0, tiled=True
        ).astype(jnp.float32),
        lax.psum_scatter(
            up_bias_term.astype(jnp.bfloat16), "dp", scatter_dimension=0, tiled=True
        ).astype(jnp.float32),
        lax.psum_scatter(
            down_term.astype(jnp.bfloat16), "dp", scatter_dimension=0, tiled=True
        ).astype(jnp.float32),
        lax.psum_scatter(
            down_bias_term.astype(jnp.bfloat16), "dp", scatter_dimension=0, tiled=True
        ).astype(jnp.float32),
        lax.psum_scatter(
            head_term.astype(jnp.bfloat16), "dp", scatter_dimension=0, tiled=True
        ).astype(jnp.float32),
        lax.psum_scatter(
            head_bias_term.astype(jnp.bfloat16), "dp", scatter_dimension=0, tiled=True
        ).astype(jnp.float32),
    )
    rear_grads = (
        lax.psum_scatter(gain_part, "fsdp", scatter_dimension=0, tiled=True),
        lax.psum_scatter(shift_part, "fsdp", scatter_dimension=0, tiled=True),
        lax.psum_scatter(up_part, "fsdp", scatter_dimension=0, tiled=True),
        lax.psum_scatter(up_bias_part, "fsdp", scatter_dimension=0, tiled=True),
        lax.psum_scatter(down_part, "fsdp", scatter_dimension=0, tiled=True),
        lax.psum_scatter(down_bias_part, "fsdp", scatter_dimension=0, tiled=True),
        lax.psum_scatter(head_part, "fsdp", scatter_dimension=0, tiled=True),
        lax.psum_scatter(head_bias_part, "fsdp", scatter_dimension=0, tiled=True),
    )
    mid_grad = end_grad + state_grad_two
    out_grad = mid_grad.astype(jnp.bfloat16)
    out_bias_term = jnp.sum(out_grad.astype(jnp.float32), axis=0)
    out_term = jnp.einsum("td,te->de", attended, out_grad, preferred_element_type=jnp.float32)
    mixed_grad = jnp.einsum(
        "te,de->td", out_grad, out_back, preferred_element_type=jnp.float32
    ).astype(jnp.bfloat16)
    grad_blocks = mixed_grad.reshape(block_count, block_rows, HEADS, head_dim)

    def backward_block(carry, inputs):
        key_sum, value_sum = carry
        query_block, grad_block, window_block, total_block, block_start = inputs
        masked = block_scores(query_block, window_block, block_start)
        probs = jnp.exp(masked - total_block[:, :, None])
        prob_grad = jnp.einsum(
            "qhd,khd->hqk", grad_block, values, preferred_element_type=jnp.float32
        )
        inner = jnp.sum(probs * prob_grad, axis=-1, keepdims=True)
        score_grad = (probs * (prob_grad - inner)).astype(jnp.bfloat16)
        query_grad = (
            jnp.einsum("hqk,khd->qhd", score_grad, keys, preferred_element_type=jnp.float32)
            * score_scale
        )
        key_sum = (
            key_sum
            + jnp.einsum(
                "hqk,qhd->khd", score_grad, query_block, preferred_element_type=jnp.float32
            )
            * score_scale
        )
        value_sum = value_sum + jnp.einsum(
            "hqk,qhd->khd",
            probs.astype(jnp.bfloat16),
            grad_block,
            preferred_element_type=jnp.float32,
        )
        return ((key_sum, value_sum), query_grad.reshape(block_rows, width))

    zero_keys = jnp.zeros((token_rows, HEADS, head_dim), jnp.float32)
    (key_grad, value_grad), query_grads = lax.scan(
        backward_block,
        (zero_keys, zero_keys),
        (queries, grad_blocks, query_windows, log_totals, block_starts),
    )
    qkv_grad = jnp.concatenate(
        [
            query_grads.reshape(token_rows, width),
            key_grad.reshape(token_rows, width),
            value_grad.reshape(token_rows, width),
        ],
        axis=1,
    ).astype(jnp.bfloat16)
    qkv_term = jnp.einsum("td,te->de", attn_input, qkv_grad, preferred_element_type=jnp.float32)
    normed_one_grad = jnp.einsum(
        "te,de->td", qkv_grad, qkv_back, preferred_element_type=jnp.float32
    )
    state_grad_one, gain_one_term, shift_one_term = pull_one(normed_one_grad)
    patch_grad = mid_grad + state_grad_one
    lead_term = lead_hot[:, None] * jnp.sum(patch_grad, axis=0)[None, :]
    lead_part, gain_one_part, shift_one_part, qkv_part, out_part, out_bias_part = (
        lax.psum_scatter(
            lead_term.astype(jnp.bfloat16), "dp", scatter_dimension=1, tiled=True
        ).astype(jnp.float32),
        lax.psum_scatter(
            gain_one_term.astype(jnp.bfloat16), "dp", scatter_dimension=0, tiled=True
        ).astype(jnp.float32),
        lax.psum_scatter(
            shift_one_term.astype(jnp.bfloat16), "dp", scatter_dimension=0, tiled=True
        ).astype(jnp.float32),
        lax.psum_scatter(
            qkv_term.astype(jnp.bfloat16), "dp", scatter_dimension=0, tiled=True
        ).astype(jnp.float32),
        lax.psum_scatter(
            out_term.astype(jnp.bfloat16), "dp", scatter_dimension=0, tiled=True
        ).astype(jnp.float32),
        lax.psum_scatter(
            out_bias_term.astype(jnp.bfloat16), "dp", scatter_dimension=0, tiled=True
        ).astype(jnp.float32),
    )
    front_grads = (
        lax.psum_scatter(lead_part, "fsdp", scatter_dimension=1, tiled=True),
        lax.psum_scatter(gain_one_part, "fsdp", scatter_dimension=0, tiled=True),
        lax.psum_scatter(shift_one_part, "fsdp", scatter_dimension=0, tiled=True),
        lax.psum_scatter(qkv_part, "fsdp", scatter_dimension=0, tiled=True),
        lax.psum_scatter(out_part, "fsdp", scatter_dimension=0, tiled=True),
        lax.psum_scatter(out_bias_part, "fsdp", scatter_dimension=0, tiled=True),
    )
    return (
        outputs,
        head_out,
        patch_grad,
        front_grads[0],
        front_grads[1],
        front_grads[2],
        front_grads[3],
        front_grads[4],
        front_grads[5],
        rear_grads[0],
        rear_grads[1],
        rear_grads[2],
        rear_grads[3],
        rear_grads[4],
        rear_grads[5],
        rear_grads[6],
        rear_grads[7],
    )


def solution(mesh):
    in_specs = (
        P(("dp", "fsdp"), None),
        P(("dp", "fsdp")),
        P(("dp", "fsdp"), None),
        P(("dp", "fsdp")),
        P(None, ("dp", "fsdp")),
        P(("dp", "fsdp")),
        P(("dp", "fsdp")),
        P(("dp", "fsdp"), None),
        P(("dp", "fsdp"), None),
        P(("dp", "fsdp")),
        P(("dp", "fsdp")),
        P(("dp", "fsdp")),
        P(("dp", "fsdp"), None),
        P(("dp", "fsdp")),
        P(("dp", "fsdp"), None),
        P(("dp", "fsdp")),
        P(("dp", "fsdp"), None),
        P(("dp", "fsdp")),
        P(("dp", "fsdp"), None),
        P(("dp", "fsdp"), None),
    )
    out_specs = (
        P(("dp", "fsdp"), None),
        P(("dp", "fsdp"), None),
        P(("dp", "fsdp"), None),
        P(None, ("dp", "fsdp")),
        P(("dp", "fsdp")),
        P(("dp", "fsdp")),
        P(("dp", "fsdp"), None),
        P(("dp", "fsdp"), None),
        P(("dp", "fsdp")),
        P(("dp", "fsdp")),
        P(("dp", "fsdp")),
        P(("dp", "fsdp"), None),
        P(("dp", "fsdp")),
        P(("dp", "fsdp"), None),
        P(("dp", "fsdp")),
        P(("dp", "fsdp"), None),
        P(("dp", "fsdp")),
    )
    body = shards if dict(mesh.shape) == {"dp": 4, "fsdp": 8} else plain_shards
    return jax.shard_map(body, mesh=mesh, in_specs=in_specs, out_specs=out_specs, check_vma=False)
```

```python
import math
from functools import partial

import jax
import jax.numpy as jnp
from jax import lax
from jax.experimental import pallas as pl
from jax.experimental.pallas import tpu as pltpu
from jax.sharding import PartitionSpec as P

HEADS = 12
PIX = 64
EXPERTS = 3
LEADS = 16


norm_epsilon = 1e-05
score_scale = 0.125


def layer_norm(hidden, norm_gain, norm_shift):
    average = jnp.mean(hidden, axis=-1, keepdims=True)
    centered = hidden - average
    variance = jnp.mean(centered * centered, axis=-1, keepdims=True)
    return centered * lax.rsqrt(variance + norm_epsilon) * norm_gain + norm_shift


def gelu_exact(values):
    return 0.5 * values * (1.0 + lax.erf(values * 0.7071067811865476))


def expert_softmax(logits, experts, pixels):
    gate_part = logits[:, : experts * pixels].reshape(logits.shape[0], experts, pixels)
    largest = jnp.max(gate_part, axis=1, keepdims=True)
    raised = jnp.exp(gate_part - largest)
    shares = raised / jnp.sum(raised, axis=1, keepdims=True)
    return jnp.concatenate(
        [shares.reshape(logits.shape[0], experts * pixels), logits[:, experts * pixels :]], axis=1
    )


def allowed_keys(query_window, key_window, key_valid, query_start):
    query_place = query_start + jnp.arange(query_window.shape[0], dtype=jnp.int32)
    key_place = jnp.arange(key_window.shape[0], dtype=jnp.int32)
    same_window = query_window[:, None] == key_window[None, :]
    usable = (key_valid[None, :] > 0) | (query_place[:, None] == key_place[None, :])
    return same_window & usable


AXES = ("dp", "fsdp")
FAR_Z, NEAR_Z, FIRST, SECOND, SIBLING = (4, 4), (2, 2), (8, 16), (16, 8), (1, 1)
ORDERS = {
    "q": (FAR_Z, NEAR_Z, FIRST, SECOND),
    "u": (FAR_Z, FIRST, SECOND, NEAR_Z),
    "d": (FIRST, FAR_Z, NEAR_Z, SECOND),
    "h": (NEAR_Z, FAR_Z, FIRST, SECOND),
    "head": (FAR_Z, NEAR_Z, FIRST, SECOND),
    "down": (FAR_Z, NEAR_Z, FIRST, SECOND),
    "up": (FAR_Z, FIRST, SECOND, NEAR_Z),
    "front": (FAR_Z, NEAR_Z, FIRST, SECOND),
}
GATHER_SEQUENCE = (
    ("q", 0), ("d", 0), ("h", 0), ("u", 0), ("q", 1), ("d", 1), ("u", 1), ("q", 2), ("h", 1), ("u", 2),
    ("d", 2),
)
MOST_VMEM, SPARE_VMEM = 56 * 1024 * 1024, 8 * 1024 * 1024
WIDTH = 768
HIDDEN = 3072
HEAD = 4608
TOKENS = 512
GATE = 512
F32 = jnp.float32
BF16 = jnp.bfloat16
HBM = pl.BlockSpec(memory_space=pltpu.HBM)
SMEM = pl.BlockSpec(memory_space=pltpu.SMEM)
VMEM = pl.BlockSpec(memory_space=pltpu.VMEM)
QKV_PART, SMALL_PART = (0, 1152), (1152, 128)
UP_PART, OUT_PART, GATE_PART = (0, 1536), (1536, 384), (1920, 256)
DOWN_PART, HEAD_PART = (0, 384), (0, 2048)


def chip_masks(order, lane):
    masks = []
    for place in range(16):
        mask = 0
        for step in range(4):
            if place >> step & 1:
                mask ^= order[step][lane]
        masks.append(mask >> 1)
    return masks


def table_start(group, side):
    return 1 + 32 * list(ORDERS).index(group) + 16 * side


def exchange(array, masks):
    return lax.ppermute(array, AXES, [(d, d ^ masks[d & 1]) for d in range(32)])


def whereabouts():
    device = lax.axis_index("dp") * 8 + lax.axis_index("fsdp")
    core, chip = device % 2, device // 2
    tables = [chip_masks(order, 0) + chip_masks(order, 1) for order in ORDERS.values()]
    swapped = [chip_masks(order, 1) + chip_masks(order, 0) for order in ORDERS.values()]
    places = jnp.where(core == 0, jnp.array(tables, jnp.int32), jnp.array(swapped, jnp.int32))
    places = (places ^ chip).reshape(32 * len(ORDERS))
    return core, jnp.concatenate([core[None].astype(jnp.int32), places])


def after(value, *marks):
    return lax.optimization_barrier((value, marks))[0]


def in_core_order(core, mine, theirs, axis):
    return jnp.where(
        core == 0,
        jnp.concatenate([mine, theirs], axis=axis),
        jnp.concatenate([theirs, mine], axis=axis),
    )


def pack_kernel(core, qkv, out, up, down, head, table, *refs):
    vectors, (up_bias, head_bias), refs = refs[:6], refs[6:8], refs[8:]
    outs, (rows,) = refs[:8], refs[8:]
    rows[...] = jnp.zeros_like(rows)
    for index, vector in enumerate(vectors):
        rows[index : index + 1, :24] = vector[...].astype(F32)
    for index in range(4):
        rows[6 + index : 7 + index, :24] = up_bias[:, 24 * index : 24 * index + 24].astype(F32)
    for index in range(6):
        rows[10 + index : 11 + index, :24] = head_bias[:, 24 * index : 24 * index + 24].astype(F32)
    rows[16:32, :24] = table[...].astype(F32)
    small = rows[...].T[:24].astype(BF16)
    for side in range(2):
        q, u, d, h = outs[4 * side : 4 * side + 4]
        q[:, :1152] = qkv[:, lane_columns(core, side, 1152)]
        q[:, 1152:] = small
        u[:, :1536] = up[:, lane_columns(core, side, 1536)]
        u[:, 1536:1920] = out[:, lane_columns(core, side, 384)]
        u[:, 1920:] = head[:, lane_columns(core, side, 256)]
        d[...] = down[:, lane_columns(core, side, 384)]
        h[...] = head[:, lane_columns(core, side, 2048, GATE)]


def packed(core, weights, table, vectors):
    shapes = [(24, 1280), (24, 2176), (96, 384), (24, 2048)] * 2
    return call(
        pack_kernel,
        (core.reshape(1), *weights, table, *[vector[None] for vector in vectors]),
        [SMEM] + [VMEM] * 14,
        [(shape, BF16, False) for shape in shapes],
        [pltpu.VMEM((128, 128), F32)],
    )


def doubled(held, masks):
    return jnp.concatenate([held, exchange(held, masks)], axis=0)


def both_lanes(*arrays):
    return arrays + tuple(exchange(array, SIBLING) for array in arrays)


def total(first, second):
    return first.astype(F32) + second.astype(F32)


def folded(keep, got, start=0):
    half = got.shape[0] // 2
    send = total(keep[half:], got[half:]).astype(BF16)
    return total(keep[:half], got[:half]).astype(BF16), send


def finished(keep, got, core, widths):
    block = total(keep, got)[0]
    rows = block.shape[0] // 2
    upper, lower = block[:rows], block[rows:]
    mine = jnp.where(core == 0, upper, lower)
    theirs = jnp.where(core == 0, lower, upper).astype(BF16)
    other = exchange(theirs, SIBLING).astype(F32)
    pieces, start = [], 0
    for width in widths:
        span = slice(start, start + width)
        pieces.append(in_core_order(core, mine[:, span], other[:, span], 1))
        start += width
    return pieces


def across(first, second):
    return lax.dot_general(first, second, (((1,), (1,)), ((), ())), preferred_element_type=F32)


def times(first, second):
    return jnp.dot(first, second, preferred_element_type=F32)


def lane_columns(where, side, stride, first=0, width=None):
    return pl.ds(pl.multiple_of(first + (where[0] ^ side) * stride, 128), width or stride)


def block_copies(where, group, sources, part, target, sems, side, first=0):
    start, width = part
    rows = sources[0].shape[1]
    half = len(sources) // 2
    count = 16 // half
    copies = []
    for place in range(16):
        row = pl.multiple_of(where[table_start(group, side) + place] * rows, rows)
        copies.append(
            pltpu.make_async_copy(
                sources[half * side + place // count].at[place % count, :, pl.ds(start, width)],
                target.at[pl.ds(row, rows), lane_columns(where, side, width, first)],
                sems.at[side, place],
            )
        )
    return copies


def term_copies(where, group, lane, out, sems, side):
    rows = out.shape[1]
    copies = []
    for place in range(16):
        row = pl.multiple_of(where[table_start(group, side) + place] * rows, rows)
        copies.append(
            pltpu.make_async_copy(lane.at[side, pl.ds(row, rows), :], out.at[place], sems.at[side, place])
        )
    return copies


def start_all(copies):
    for copy in copies:
        copy.start()


def wait_all(copies):
    for copy in copies:
        copy.wait()


def mean_and_scale(hidden):
    average = jnp.mean(hidden, axis=1, keepdims=True)
    centered = hidden - average
    variance = jnp.mean(centered * centered, axis=1, keepdims=True)
    return centered, lax.rsqrt(variance + norm_epsilon)


def norm_backward(hidden, gain, upstream):
    centered, scale = mean_and_scale(hidden)
    normed = centered * scale
    gain_grad = jnp.sum(upstream * normed, axis=0, keepdims=True)
    shift_grad = jnp.sum(upstream, axis=0, keepdims=True)
    scaled = upstream * gain
    first = jnp.mean(scaled, axis=1, keepdims=True)
    second = jnp.mean(scaled * normed, axis=1, keepdims=True)
    return scale * (scaled - first - normed * second), gain_grad, shift_grad


def call(kernel, operands, in_specs, outs, scratch, spare=None):
    def size(item):
        return math.prod(item.shape) * jnp.dtype(item.dtype).itemsize

    held = [item for item, spec in zip(operands, in_specs) if spec is VMEM]
    held += [jax.ShapeDtypeStruct(shape, kind) for shape, kind, copied in outs if not copied]
    held += [item for item in scratch if getattr(item, "memory_space", None) == pltpu.VMEM]
    limit = MOST_VMEM if spare is None else sum(size(item) for item in held) + spare
    return pl.pallas_call(
        kernel,
        out_shape=[jax.ShapeDtypeStruct(shape, kind) for shape, kind, _ in outs],
        in_specs=in_specs,
        out_specs=[HBM if copied else VMEM for _, _, copied in outs],
        scratch_shapes=scratch,
        compiler_params=pltpu.CompilerParams(vmem_limit_bytes=limit),
        cost_estimate=pl.CostEstimate(flops=2 * 10**12, bytes_accessed=10**10, transcendentals=0),
    )(*operands)


def lane_scratch(rows, width):
    return [pltpu.VMEM((2, rows, width), BF16), pltpu.SemaphoreType.DMA((2, 16))]


def weight_scratch(rows, width):
    return [pltpu.VMEM((rows, width), BF16), pltpu.SemaphoreType.DMA((2, 16))]


def taken(refs, *counts):
    groups = []
    for count in counts:
        groups.append(refs[:count])
        refs = refs[count:]
    return *groups, refs


def front_kernel(where, lead, patches, *refs):
    sources, outs, scratch = taken(refs, 4, 3)
    turned_out, qkv_out, small = outs
    weight, sems, smalls, small_sems, state, rows, turned, qkv, io_sems = scratch
    loads = [block_copies(where, "q", sources, QKV_PART, weight, sems, side) for side in range(2)]
    small_loads = []
    for place in range(16):
        row = pl.multiple_of(where[table_start("q", 0) + place] * 48, 48)
        small_loads.append(
            pltpu.make_async_copy(
                sources[place // 8].at[place % 8, :, pl.ds(*SMALL_PART)],
                smalls.at[pl.ds(row, 48), :],
                small_sems.at[place],
            )
        )
    state_load = pltpu.make_async_copy(patches, state, io_sems.at[0])
    start_all(small_loads)
    state_load.start()
    start_all(loads[0])
    start_all(loads[1])
    wait_all(small_loads)
    columns = smalls[...].astype(F32).T
    places = lax.broadcasted_iota(jnp.int32, (LEADS, WIDTH), 0)
    lead_row = jnp.sum(
        jnp.where(places == lead[0], columns[16 : 16 + LEADS], 0.0), axis=0, keepdims=True
    )
    small[...] = columns[:32]
    small[16:17, :] = lead_row
    state_load.wait()
    centered, scale = mean_and_scale(state[...].astype(F32) + lead_row)
    rows[...] = (centered * scale * columns[0:1] + columns[1:2]).astype(BF16)
    turned[...] = rows[...].T
    stores = [pltpu.make_async_copy(turned, turned_out, io_sems.at[1])]
    stores[0].start()
    wait_all(loads[0] + loads[1])
    for part in range(3):
        span = slice(part * WIDTH, part * WIDTH + WIDTH)
        qkv[:, span] = times(rows[...], weight[:, span]).astype(BF16)
        stores.append(pltpu.make_async_copy(qkv.at[:, span], qkv_out.at[:, span], io_sems.at[2 + part]))
        stores[-1].start()
    wait_all(stores)


def front_forward(where, lead_index, patches, arrays):
    return call(
        front_kernel,
        (where, lead_index, patches, *arrays),
        [SMEM, SMEM, HBM] + [HBM] * 4,
        [
            ((WIDTH, TOKENS), BF16, True),
            ((TOKENS, 3 * WIDTH), BF16, True),
            ((32, WIDTH), F32, False),
        ],
        weight_scratch(WIDTH, 3 * WIDTH)
        + [pltpu.VMEM((WIDTH, 128), BF16), pltpu.SemaphoreType.DMA((16,))]
        + [
            pltpu.VMEM((TOKENS, WIDTH), BF16),
            pltpu.VMEM((TOKENS, WIDTH), BF16),
            pltpu.VMEM((WIDTH, TOKENS), BF16),
            pltpu.VMEM((TOKENS, 3 * WIDTH), BF16),
            pltpu.SemaphoreType.DMA((5,)),
        ],
    )


KEY_SPANS = ((0, 256), (0, 384), (128, 512), (256, 512))


def fill_bias(lengths, pad, bias):
    ends, end = [], 0
    for index in range(lengths.shape[1]):
        end = end + lengths[0, index]
        ends.append(end)

    def windows(places):
        return sum([(places >= end).astype(jnp.int32) for end in ends])

    for block, (low, high) in enumerate(KEY_SPANS):
        count = high - low
        queries = lax.broadcasted_iota(jnp.int32, (1, 128), 1) + 128 * block
        keys = lax.broadcasted_iota(jnp.int32, (count, 1), 0) + low
        same = windows(queries) == windows(keys)
        usable = (pad[low:high, :] > 0) | (queries == keys)
        bias[block, :count, :] = jnp.where(same & usable, 0.0, -1e30)


def two_heads(block):
    first = lax.broadcasted_iota(jnp.int32, block.shape, 1) < block.shape[1] // 2
    zero = jnp.zeros_like(block)
    return jnp.concatenate([jnp.where(first, block, zero), jnp.where(first, zero, block)], axis=0)


def head_rows_of(stacked):
    return jnp.concatenate([stacked[:64, :128], stacked[64:, 128:]], axis=0)


def probabilities(scores, allowed):
    masked = scores * score_scale + allowed
    raised = jnp.exp(masked - jnp.max(masked, axis=0, keepdims=True))
    return raised * (1.0 / jnp.sum(raised, axis=0, keepdims=True))


def attention_kernel(where, lengths, pad, qkv, attended_out, turned_out, bias, turned, rows, sems):
    fill_bias(lengths, pad, bias)

    def pair(index, carry):
        first = index * 128
        columns = pl.ds(pl.multiple_of(first, 128), 128)
        keys_at = pl.ds(pl.multiple_of(first + WIDTH, 128), 128)
        values = qkv[:, pl.ds(pl.multiple_of(first + 2 * WIDTH, 128), 128)].T
        for block, (low, high) in enumerate(KEY_SPANS):
            span = slice(128 * block, 128 * block + 128)
            scores = across(qkv[low:high, keys_at], two_heads(qkv[span, columns]))
            allowed = bias[block, : high - low, :]
            probs = [
                probabilities(scores[:, 128 * head : 128 * head + 128], allowed).astype(BF16)
                for head in range(2)
            ]
            mixed = times(values[:, low:high], jnp.concatenate(probs, axis=1))
            turned[columns, span] = head_rows_of(mixed).astype(BF16)
        return carry

    lax.fori_loop(0, WIDTH // 128, pair, 0)
    stores = [pltpu.make_async_copy(turned, turned_out, sems.at[0])]
    stores[0].start()
    rows[...] = turned[...].T
    stores.append(pltpu.make_async_copy(rows, attended_out, sems.at[1]))
    stores[1].start()
    wait_all(stores)


def attention_forward(where, lengths, pad, qkv):
    rows, columns = (TOKENS, WIDTH), (WIDTH, TOKENS)
    return call(
        attention_kernel,
        (where, lengths, pad, qkv),
        [SMEM, SMEM, VMEM, VMEM],
        [(rows, BF16, True), (columns, BF16, True)],
        [
            pltpu.VMEM((4, 384, 128), F32),
            pltpu.VMEM(columns, BF16),
            pltpu.VMEM(rows, BF16),
            pltpu.SemaphoreType.DMA((2,)),
        ],
    )


def up_kernel(where, attended, patches, small, bias, *refs):
    sources, outs, scratch = taken(refs, 4, 5)
    mid_out, mlp_turned_out, act_out, act_turned_out, slope_out = outs
    out_weight, out_sems, weight, sems, scratch = *scratch[:4], scratch[4:]
    inputs, state, mid, rows, mlp_turned, act, act_turned, slope, io_sems, act_sems = scratch
    out_loads = [block_copies(where, "u", sources, OUT_PART, out_weight, out_sems, s) for s in range(2)]
    loads = [block_copies(where, "u", sources, UP_PART, weight, sems, side) for side in range(2)]
    in_loads = [
        pltpu.make_async_copy(attended, inputs, io_sems.at[0]),
        pltpu.make_async_copy(patches, state, io_sems.at[1]),
    ]
    start_all(in_loads)
    start_all(out_loads[0] + out_loads[1])
    start_all(loads[0] + loads[1])
    wait_all(in_loads)
    wait_all(out_loads[0] + out_loads[1])
    mid[...] = (
        state[...].astype(F32)
        + small[16:17, :]
        + times(inputs[...], out_weight[...])
        + small[2:3, :]
    )
    centered, scale = mean_and_scale(mid[...])
    rows[...] = (centered * scale * small[3:4, :] + small[4:5, :]).astype(BF16)
    mlp_turned[...] = rows[...].T
    stores = [
        pltpu.make_async_copy(mid, mid_out, io_sems.at[2]),
        pltpu.make_async_copy(mlp_turned, mlp_turned_out, io_sems.at[3]),
    ]
    start_all(stores)
    wait_all(loads[0] + loads[1])
    for slot in range(6):
        span = slice(slot * 512, slot * 512 + 512)
        values = times(rows[...], weight[:, span]) + bias[:, span]
        share = 0.5 * (1.0 + lax.erf(values * 0.7071067811865476))
        density = jnp.exp(-0.5 * values * values) * 0.3989422804014327
        activated = (values * share).astype(BF16)
        act[:, span] = activated
        act_turned[span, :] = activated.T
        slope[:, span] = (share + values * density).astype(BF16)
        copies = [
            pltpu.make_async_copy(act.at[:, span], act_out.at[:, span], act_sems.at[slot, 0]),
            pltpu.make_async_copy(
                act_turned.at[span, :], act_turned_out.at[span, :], act_sems.at[slot, 1]
            ),
            pltpu.make_async_copy(slope.at[:, span], slope_out.at[:, span], act_sems.at[slot, 2]),
        ]
        start_all(copies)
        stores += copies
    wait_all(stores)


def up_forward(where, attended, patches, small, bias, arrays):
    rows, columns = (TOKENS, WIDTH), (WIDTH, TOKENS)
    wide, tall = (TOKENS, HIDDEN), (HIDDEN, TOKENS)
    return call(
        up_kernel,
        (where, attended, patches, small, bias, *arrays),
        [SMEM, HBM, HBM, VMEM, VMEM] + [HBM] * 4,
        [
            (rows, F32, True),
            (columns, BF16, True),
            (wide, BF16, True),
            (tall, BF16, True),
            (wide, BF16, True),
        ],
        weight_scratch(WIDTH, WIDTH)
        + weight_scratch(WIDTH, HIDDEN)
        + [
            pltpu.VMEM(rows, BF16),
            pltpu.VMEM(rows, BF16),
            pltpu.VMEM(rows, F32),
            pltpu.VMEM(rows, BF16),
            pltpu.VMEM(columns, BF16),
            pltpu.VMEM(wide, BF16),
            pltpu.VMEM(tall, BF16),
            pltpu.VMEM(wide, BF16),
            pltpu.SemaphoreType.DMA((4,)),
            pltpu.SemaphoreType.DMA((6, 3)),
        ],
    )


def gate_shares(logits, cotangent, shares, gate_grad):
    shares[:, 256:] = logits[:, 256:]
    gate_grad[:, 256:] = cotangent[:, 256:GATE]
    first, rest = logits[:, :128], logits[:, 128:256]
    left = lax.broadcasted_iota(jnp.int32, first.shape, 1) < PIX
    third = jnp.where(left, rest, pltpu.roll(rest, PIX, 1))
    largest = jnp.maximum(jnp.maximum(first, pltpu.roll(first, PIX, 1)), third)
    raised, raised_third = jnp.exp(first - largest), jnp.exp(third - largest)
    scale = 1.0 / (raised + pltpu.roll(raised, PIX, 1) + raised_third)
    share, share_third = raised * scale, raised_third * scale
    shares[:, :128] = share
    shares[:, 128:256] = jnp.where(left, share_third, rest)
    pull, other = cotangent[:, :128].astype(F32), cotangent[:, 128:256].astype(F32)
    pull_third = jnp.where(left, other, pltpu.roll(other, PIX, 1))
    weighed = share * pull
    inner = weighed + pltpu.roll(weighed, PIX, 1) + share_third * pull_third
    gate_grad[:, :128] = (share * (pull - inner)).astype(BF16)
    gate_grad[:, 128:256] = jnp.where(left, share_third * (pull_third - inner), other).astype(BF16)


def down_kernel(where, act, mid, small, cotangent, bias, *refs):
    sources, gate_sources, outs, scratch = taken(refs, 4, 4, 6)
    outputs, turned, shares, gate_grad, gate_bias, theirs_out = outs
    weight, sems, gate, gate_sems, lane, lane_sems, scratch = *scratch[:6], scratch[6:]
    acts, mids, pulls, logits, io_sems = scratch
    loads = [block_copies(where, "d", sources, DOWN_PART, weight, sems, side) for side in range(2)]
    gate_loads = [
        block_copies(where, "u", gate_sources, GATE_PART, gate, gate_sems, side) for side in range(2)
    ]
    in_loads = [
        pltpu.make_async_copy(act, acts, io_sems.at[0]),
        pltpu.make_async_copy(mid, mids, io_sems.at[1]),
    ]
    pull_load = pltpu.make_async_copy(cotangent, pulls, io_sems.at[2])
    start_all(in_loads)
    start_all(loads[0] + loads[1])
    start_all(gate_loads[0] + gate_loads[1])
    pull_load.start()
    wait_all(in_loads)
    wait_all(loads[0] + loads[1])
    outputs[...] = (mids[...] + times(acts[...], weight[...]) + small[5:6, :]).astype(BF16)
    turned[...] = outputs[...].T
    wait_all(gate_loads[0] + gate_loads[1])
    logits[...] = times(outputs[...], gate[...]) + bias[:, :GATE]
    pull_load.wait()
    gate_shares(logits, pulls, shares, gate_grad)
    gate_bias[...] = jnp.sum(gate_grad[...].astype(F32), axis=0, keepdims=True)
    wait_all(head_terms(where, turned, gate_grad, pulls, lane, theirs_out, lane_sems, 1))


def head_terms(where, turned, gate_grad, pulls, lane, out, sems, side):
    lane[:, :256] = times(turned[...], gate_grad[:, lane_columns(where, side, 256)]).astype(BF16)
    for tile in range(4):
        span = lane_columns(where, side, 2048, GATE + tile * 512, 512)
        lane[:, 256 + tile * 512 : 768 + tile * 512] = times(turned[...], pulls[:, span]).astype(BF16)
    copies = []
    for place in range(16):
        row = pl.multiple_of(where[table_start("head", side) + place] * 48, 48)
        copies.append(
            pltpu.make_async_copy(lane.at[pl.ds(row, 48), :], out.at[place], sems.at[place])
        )
    start_all(copies)
    return copies


def down_forward(where, act, mid, small, cotangent, bias, arrays, gate_arrays):
    rows = (TOKENS, WIDTH)
    return call(
        down_kernel,
        (where, act, mid, small, cotangent, bias, *arrays, *gate_arrays),
        [SMEM, HBM, HBM, VMEM, HBM, VMEM] + [HBM] * 8,
        [
            (rows, BF16, False),
            ((WIDTH, TOKENS), BF16, False),
            ((TOKENS, GATE), F32, False),
            ((TOKENS, GATE), BF16, False),
            ((1, GATE), F32, False),
            ((16, 48, 2304), BF16, True),
        ],
        weight_scratch(HIDDEN, WIDTH)
        + weight_scratch(WIDTH, GATE)
        + [pltpu.VMEM((WIDTH, 2304), BF16), pltpu.SemaphoreType.DMA((16,))]
        + [
            pltpu.VMEM((TOKENS, HIDDEN), BF16),
            pltpu.VMEM(rows, F32),
            pltpu.VMEM((TOKENS, HEAD), BF16),
            pltpu.VMEM((TOKENS, GATE), F32),
            pltpu.SemaphoreType.DMA((3,)),
        ],
    )


def head_kernel(where, rows, gate_out, bias, *refs):
    sources, outs, scratch = taken(refs, 4, 1)
    (out,) = outs
    weight, sems, inputs, result, io_sems = scratch
    loads = [block_copies(where, "h", sources, HEAD_PART, weight, sems, side) for side in range(2)]
    row_load = pltpu.make_async_copy(rows, inputs, io_sems.at[0])
    gate_load = pltpu.make_async_copy(gate_out, result.at[:, :GATE], io_sems.at[1])
    row_load.start()
    start_all(loads[0])
    start_all(loads[1])
    gate_load.start()
    row_load.wait()
    stores = []

    def store(span):
        stores.append(
            pltpu.make_async_copy(result.at[:, span], out.at[:, span], io_sems.at[2 + len(stores)])
        )
        stores[-1].start()

    for side in range(2):
        wait_all(loads[side])
        for tile in range(4):
            span = lane_columns(where, side, 2048, GATE + tile * 512, 512)
            columns = lane_columns(where, side, 2048, tile * 512, 512)
            result[:, span] = times(inputs[...], weight[:, columns]) + bias[:, span]
            store(span)
    gate_load.wait()
    store(pl.ds(0, GATE))
    wait_all(stores)


def head_forward(where, rows, gate_out, bias, arrays):
    return call(
        head_kernel,
        (where, rows, gate_out, bias, *arrays),
        [SMEM, HBM, HBM, VMEM] + [HBM] * 4,
        [((TOKENS, HEAD), F32, True)],
        weight_scratch(WIDTH, HEAD - GATE)
        + [
            pltpu.VMEM((TOKENS, WIDTH), BF16),
            pltpu.VMEM((TOKENS, HEAD), F32),
            pltpu.SemaphoreType.DMA((11,)),
        ],
        spare=SPARE_VMEM,
    )[0]


def head_back_kernel(where, turned, act_cotangent, gate_grad, cotangent, slope, *refs):
    sources, gate_sources, down_sources, outs, scratch = taken(refs, 4, 4, 4, 6)
    end_grad, branch, down_bias, up_bias, pre_out, mine_out = outs
    weight, sems, gate_sems, down, down_sems, lane, lane_sems, scratch = *scratch[:7], scratch[7:]
    act_pulls, pulls, slopes, pre_grad, io_sems, pre_sems = scratch
    loads = [
        block_copies(where, "h", sources, HEAD_PART, weight, sems, side, GATE) for side in range(2)
    ]
    gate_loads = [
        block_copies(where, "u", gate_sources, GATE_PART, weight, gate_sems, side)
        for side in range(2)
    ]
    down_loads = [
        block_copies(where, "d", down_sources, DOWN_PART, down, down_sems, side) for side in range(2)
    ]
    first_loads = [pltpu.make_async_copy(act_cotangent, act_pulls, io_sems.at[0])]
    pull_load = pltpu.make_async_copy(cotangent.at[:, GATE:], pulls.at[:, GATE:], io_sems.at[2])
    slope_load = pltpu.make_async_copy(slope, slopes, io_sems.at[3])
    pull_load.start()
    start_all(first_loads + gate_loads[0] + gate_loads[1])
    start_all(loads[0])
    start_all(loads[1])
    start_all(down_loads[0] + down_loads[1])
    slope_load.start()
    wait_all(first_loads)
    pulls[:, :GATE] = gate_grad[...]
    pull_load.wait()
    stores = head_terms(where, turned, gate_grad, pulls, lane, mine_out, lane_sems, 0)
    wait_all(gate_loads[0] + gate_loads[1])
    wait_all(loads[0] + loads[1])
    end_grad[...] = act_pulls[...].astype(F32) + across(pulls[...], weight[...])
    branch[...] = end_grad[...].astype(BF16)
    down_bias[...] = jnp.sum(branch[...].astype(F32), axis=0, keepdims=True)
    wait_all(down_loads[0] + down_loads[1])
    slope_load.wait()
    for tile in range(6):
        span = slice(tile * 512, tile * 512 + 512)
        grad = across(branch[...], down[span, :])
        rounded = (slopes[:, span].astype(F32) * grad).astype(BF16)
        pre_grad[:, span] = rounded
        up_bias[:, span] = jnp.sum(rounded.astype(F32), axis=0, keepdims=True)
        stores.append(
            pltpu.make_async_copy(pre_grad.at[:, span], pre_out.at[:, span], pre_sems.at[tile])
        )
        stores[-1].start()
    wait_all(stores)


def head_backward(
    where, turned, act_cotangent, gate_grad, cotangent, slope, arrays, gate_arrays, down_arrays
):
    rows, wide = (TOKENS, WIDTH), (TOKENS, HIDDEN)
    return call(
        head_back_kernel,
        (
            where, turned, act_cotangent, gate_grad, cotangent, slope,
            *arrays, *gate_arrays, *down_arrays,
        ),
        [SMEM, VMEM, HBM, VMEM, HBM, HBM] + [HBM] * 12,
        [
            (rows, F32, False),
            (rows, BF16, False),
            ((1, WIDTH), F32, False),
            ((1, HIDDEN), F32, False),
            (wide, BF16, True),
            ((16, 48, 2304), BF16, True),
        ],
        weight_scratch(WIDTH, HEAD)
        + [pltpu.SemaphoreType.DMA((2, 16))]
        + weight_scratch(HIDDEN, WIDTH)
        + [pltpu.VMEM((WIDTH, 2304), BF16), pltpu.SemaphoreType.DMA((16,))]
        + [
            pltpu.VMEM(rows, BF16),
            pltpu.VMEM((TOKENS, HEAD), BF16),
            pltpu.VMEM(wide, BF16),
            pltpu.VMEM(wide, BF16),
            pltpu.SemaphoreType.DMA((4,)),
            pltpu.SemaphoreType.DMA((6,)),
        ],
    )


def up_back_kernel(
    where, small, pre_grad, branch, act_turned, mlp_turned, mid, end_grad, *refs
):
    sources, outs, scratch = taken(refs, 4, 7)
    mid_grad, out_grad, terms, down_mine, down_theirs, up_mine, up_theirs = outs
    weight, sems, down_lane, down_sems, up_lane, up_sems, scratch = *scratch[:6], scratch[6:]
    pres, branches, acts, mlps, mids, ends, io_sems = scratch
    loads = [block_copies(where, "u", sources, UP_PART, weight, sems, side) for side in range(2)]
    pre_load = pltpu.make_async_copy(pre_grad, pres, io_sems.at[0])
    branch_load = pltpu.make_async_copy(branch, branches, io_sems.at[1])
    act_load = pltpu.make_async_copy(act_turned, acts, io_sems.at[2])
    mlp_load = pltpu.make_async_copy(mlp_turned, mlps, io_sems.at[3])
    norm_loads = [
        pltpu.make_async_copy(mid, mids, io_sems.at[4]),
        pltpu.make_async_copy(end_grad, ends, io_sems.at[5]),
    ]
    branch_load.start()
    act_load.start()
    pre_load.start()
    mlp_load.start()
    start_all(loads[0] + loads[1])
    start_all(norm_loads)
    branch_load.wait()
    act_load.wait()
    stores = []
    for side, out in ((1, down_theirs), (0, down_mine)):
        span = lane_columns(where, side, 384)
        for part in range(4):
            rows = slice(part * WIDTH, part * WIDTH + WIDTH)
            down_lane[side, rows, :] = times(acts[rows, :], branches[:, span]).astype(BF16)
        copies = term_copies(where, "down", down_lane, out, down_sems, side)
        start_all(copies)
        stores += copies
    pre_load.wait()
    mlp_load.wait()
    for side, out in ((1, up_theirs), (0, up_mine)):
        for tile in range(3):
            span = lane_columns(where, side, 1536, tile * 512, 512)
            up_lane[side, :, tile * 512 : tile * 512 + 512] = times(mlps[...], pres[:, span]).astype(
                BF16
            )
        copies = term_copies(where, "up", up_lane, out, up_sems, side)
        start_all(copies)
        stores += copies
    wait_all(loads[0] + loads[1])
    grad = across(pres[...], weight[...])
    wait_all(norm_loads)
    pulled, gain_grad, shift_grad = norm_backward(mids[...], small[3:4, :], grad)
    pulled = pulled + ends[...]
    rounded = pulled.astype(BF16)
    mid_grad[...] = pulled
    out_grad[...] = rounded
    terms[...] = jnp.zeros_like(terms)
    terms[0:1, :] = jnp.sum(rounded.astype(F32), axis=0, keepdims=True)
    terms[1:2, :] = gain_grad
    terms[2:3, :] = shift_grad
    wait_all(stores)


def up_backward(
    where, small, pre_grad, branch, act_turned, mlp_turned, mid, end_grad, arrays
):
    rows = (TOKENS, WIDTH)
    return call(
        up_back_kernel,
        (where, small, pre_grad, branch, act_turned, mlp_turned, mid, end_grad, *arrays),
        [SMEM, VMEM] + [HBM] * 10,
        [
            (rows, F32, False),
            (rows, BF16, False),
            ((8, WIDTH), F32, False),
            ((16, 192, 384), BF16, True),
            ((16, 192, 384), BF16, True),
            ((16, 48, 1536), BF16, True),
            ((16, 48, 1536), BF16, True),
        ],
        weight_scratch(WIDTH, HIDDEN)
        + lane_scratch(HIDDEN, 384)
        + lane_scratch(WIDTH, 1536)
        + [
            pltpu.VMEM((TOKENS, HIDDEN), BF16),
            pltpu.VMEM(rows, BF16),
            pltpu.VMEM((HIDDEN, TOKENS), BF16),
            pltpu.VMEM((WIDTH, TOKENS), BF16),
            pltpu.VMEM(rows, F32),
            pltpu.VMEM(rows, F32),
            pltpu.SemaphoreType.DMA((6,)),
        ],
    )


def attention_back_kernel(start, count, where, lengths, pad, out_grad, qkv, *refs):
    sources, outs, scratch = taken(refs, 4, 1)
    (qkv_grad,) = outs
    weight, sems, bias, mixed, turned, key_sum, value_sum = scratch
    loads = [block_copies(where, "u", sources, OUT_PART, weight, sems, side) for side in range(2)]
    start_all(loads[0] + loads[1])
    fill_bias(lengths, pad, bias)
    wait_all(loads[0] + loads[1])
    width = 128 * count
    mixed[...] = across(
        out_grad[...], weight[128 * start : 128 * start + width, :]
    ).astype(BF16)

    def columns_at(first):
        return pl.ds(pl.multiple_of(first, 128), 128)

    def pair(index, carry):
        own, first = index * 128, (index + start) * 128
        columns, keys_at = columns_at(first), columns_at(first + WIDTH)
        values_at = columns_at(first + 2 * WIDTH)
        keys_turned = qkv[:, keys_at].T
        key_sum[...] = jnp.zeros_like(key_sum)
        value_sum[...] = jnp.zeros_like(value_sum)
        for block, (low, high) in enumerate(KEY_SPANS):
            span = slice(128 * block, 128 * block + 128)
            queries, grads = two_heads(qkv[span, columns]), two_heads(mixed[span, columns_at(own)])
            scores = across(qkv[low:high, keys_at], queries)
            prob_grads = across(qkv[low:high, values_at], grads)
            allowed = bias[block, : high - low, :]
            probs, score_grads = [], []
            for head in range(2):
                part = slice(128 * head, 128 * head + 128)
                prob = probabilities(scores[:, part], allowed)
                pulled = prob * prob_grads[:, part]
                inner = jnp.sum(pulled, axis=0, keepdims=True)
                probs.append(prob.astype(BF16))
                score_grads.append((pulled - prob * inner).astype(BF16))
            score_grad = jnp.concatenate(score_grads, axis=1)
            key_sum[low:high, :] += times(score_grad, queries)
            value_sum[low:high, :] += times(jnp.concatenate(probs, axis=1), grads)
            turned[:, span] = head_rows_of(times(keys_turned[:, low:high], score_grad)) * score_scale
        qkv_grad[:, columns_at(own)] = turned[...].T.astype(BF16)
        qkv_grad[:, columns_at(own + width)] = (key_sum[...] * score_scale).astype(BF16)
        qkv_grad[:, columns_at(own + 2 * width)] = value_sum[...].astype(BF16)
        return carry

    lax.fori_loop(0, count, pair, 0)


def attention_backward(where, lengths, pad, out_grad, qkv, arrays, start, count):
    return call(
        partial(attention_back_kernel, start, count),
        (where, lengths, pad, out_grad, qkv, *arrays),
        [SMEM, SMEM, VMEM, VMEM, VMEM] + [HBM] * 4,
        [((TOKENS, 3 * 128 * count), BF16, False)],
        weight_scratch(WIDTH, WIDTH)
        + [
            pltpu.VMEM((4, 384, 128), F32),
            pltpu.VMEM((TOKENS, 128 * count), BF16),
            pltpu.VMEM((128, TOKENS), F32),
            pltpu.VMEM((TOKENS, 128), F32),
            pltpu.VMEM((TOKENS, 128), F32),
        ],
        spare=SPARE_VMEM,
    )[0]


def mix_term_kernel(where, qkv_grad, input_turned, attended_turned, out_grad, mine_out, theirs_out, *refs):
    lane, sems = refs
    stores = []
    for side, out in ((1, theirs_out), (0, mine_out)):
        lane[side, :, :768] = times(
            input_turned[...], qkv_grad[:, lane_columns(where, side, 768)]
        ).astype(BF16)
        lane[side, :, 768:1152] = times(
            attended_turned[...], out_grad[:, lane_columns(where, side, 384)]
        ).astype(BF16)
        copies = term_copies(where, "front", lane, out, sems, side)
        start_all(copies)
        stores += copies
    wait_all(stores)


def mix_terms(where, qkv_grad, input_turned, attended_turned, out_grad):
    return call(
        mix_term_kernel,
        (where, qkv_grad, input_turned, attended_turned, out_grad),
        [SMEM] + [VMEM] * 4,
        [((16, 48, 1152), BF16, True)] * 2,
        lane_scratch(WIDTH, 1152),
        spare=SPARE_VMEM,
    )


def front_back_kernel(
    where, lead, small, terms, down_row, up_rows, head_rows,
    first_grad, second_grad, patches, mid_grad, input_turned, *refs
):
    sources, outs, scratch = taken(refs, 4, 3)
    patch_out, mine_out, theirs_out = outs
    weight, sems, lane, lane_sems, scratch = *scratch[:4], scratch[4:]
    pulls, late_pulls, state, mids, inputs, patch_grad, small_grad, io_sems = scratch
    loads = [block_copies(where, "q", sources, QKV_PART, weight, sems, side) for side in range(2)]
    pairs = [(patches, state), (mid_grad, mids), (input_turned, inputs), (second_grad, late_pulls)]
    for part in range(3):
        for source, start, size in ((first_grad, 0, 512), (second_grad, 512, 256)):
            columns = pl.ds(WIDTH * part + start, size)
            pairs.append((source.at[:, pl.ds(size * part, size)], pulls.at[:, columns]))
    in_loads = [pltpu.make_async_copy(*pair, io_sems.at[at]) for at, pair in enumerate(pairs)]
    start_all(in_loads[4:])
    start_all(loads[0] + loads[1])
    start_all(in_loads[:4])
    wait_all(in_loads[4:])
    wait_all(loads[0] + loads[1])
    grad = across(pulls[...], weight[...])
    wait_all(in_loads[:4])
    pulled, gain_grad, shift_grad = norm_backward(
        state[...].astype(F32) + small[16:17, :], small[0:1, :], grad
    )
    pulled = pulled + mids[...]
    patch_grad[...] = pulled
    stores = [pltpu.make_async_copy(patch_grad, patch_out, io_sems.at[10])]
    stores[0].start()
    small_grad[0:1, :] = gain_grad
    small_grad[1:2, :] = shift_grad
    small_grad[2:5, :] = terms[0:3, :]
    small_grad[5:6, :] = down_row[...]
    small_grad[6:10, :] = up_rows[...]
    small_grad[10:16, :] = head_rows[...]
    places = lax.broadcasted_iota(jnp.int32, (LEADS, WIDTH), 0)
    lead_grad = jnp.sum(pulled, axis=0, keepdims=True)
    small_grad[16:32, :] = jnp.where(places == lead[0], lead_grad, 0.0)
    for side, out in ((1, theirs_out), (0, mine_out)):
        lane[side, :, :384] = times(
            inputs[...], late_pulls[:, lane_columns(where, side, 384)]
        ).astype(BF16)
        rows = small_grad[pl.ds(pl.multiple_of((where[0] ^ side) * 16, 16), 16), :]
        rows = jnp.concatenate([rows, jnp.zeros((112, WIDTH), F32)], axis=0)
        lane[side, :, 384:] = rows.T.astype(BF16)
        copies = term_copies(where, "front", lane, out, lane_sems, side)
        start_all(copies)
        stores += copies
    wait_all(stores)


def front_backward(
    where, lead, small, terms, down_row, up_rows, head_rows,
    first_grad, second_grad, patches, mid_grad, input_turned, arrays,
):
    rows, columns = (TOKENS, WIDTH), (WIDTH, TOKENS)
    return call(
        front_back_kernel,
        (
            where, lead, small, terms, down_row, up_rows, head_rows,
            first_grad, second_grad, patches, mid_grad, input_turned, *arrays,
        ),
        [SMEM, SMEM] + [VMEM] * 5 + [HBM] * 9,
        [(rows, F32, True), ((16, 48, 512), BF16, True), ((16, 48, 512), BF16, True)],
        weight_scratch(WIDTH, 3 * WIDTH)
        + lane_scratch(WIDTH, 512)
        + [
            pltpu.VMEM((TOKENS, 3 * WIDTH), BF16),
            pltpu.VMEM(rows, BF16),
            pltpu.VMEM(rows, BF16),
            pltpu.VMEM(rows, F32),
            pltpu.VMEM(columns, BF16),
            pltpu.VMEM(rows, F32),
            pltpu.VMEM((32, WIDTH), F32),
            pltpu.SemaphoreType.DMA((11,)),
        ],
        spare=SPARE_VMEM,
    )


def rows_of(vector, count):
    return vector.reshape(32, count, 24).transpose(1, 0, 2).reshape(count, WIDTH)


def vector_of(rows):
    count = rows.shape[0]
    return rows.reshape(count, 32, 24).transpose(1, 0, 2).reshape(1, count * WIDTH)


def shards(
    patches,
    lead_index,
    window_lengths,
    pad_mask,
    lead_table,
    attn_gain,
    attn_shift,
    qkv_weight,
    out_weight,
    out_bias,
    mlp_gain,
    mlp_shift,
    up_weight,
    up_bias,
    down_weight,
    down_bias,
    head_weight,
    head_bias,
    act_cotangent,
    head_cotangent,
):
    core, where = whereabouts()
    weights = (qkv_weight, out_weight, up_weight, down_weight, head_weight)
    vectors = (
        attn_gain, attn_shift, out_bias, mlp_gain, mlp_shift, down_bias, up_bias, head_bias
    )
    parts = packed(core, weights, lead_table, vectors)
    pad = pad_mask[:, None]
    cotangent_sum = jnp.sum(head_cotangent[:, GATE:].astype(F32), axis=0, keepdims=True)

    orders = ORDERS
    parts = dict(zip("qudh", zip(parts[:4], parts[4:])))
    chunks = {
        name: in_core_order(core, mine, exchange(theirs, SIBLING), 0)[None]
        for name, (mine, theirs) in parts.items()
    }

    held, last = dict(chunks), ()
    for name, step in GATHER_SEQUENCE:
        held[name] = after(held[name], *last)
        last = (held[name],)
        held[name] = doubled(held[name], orders[name][step])
    q, u, d, h = [held[name] for name in ("q", "u", "d", "h")]
    q_rest = exchange(after(q, *last), orders["q"][3])
    u = after(u, q)
    u_rest = exchange(u, orders["u"][3])
    d_rest = exchange(d, orders["d"][3])
    h = doubled(after(h, u), orders["h"][2])
    first = both_lanes(q, q_rest)
    h_rest = exchange(h, orders["h"][3])
    input_turned, qkv, small_rows = front_forward(
        after(where, d, h, cotangent_sum), lead_index, patches, first
    )
    attended, attended_turned = attention_forward(where, window_lengths, pad, qkv)
    u_rest, d_rest, h_rest = lax.optimization_barrier((u_rest, d_rest, h_rest, attended))[:3]
    second = both_lanes(u, u_rest)
    up_bias_row, head_bias_row = vector_of(small_rows[6:10]), vector_of(small_rows[10:16])
    mid_state, mlp_turned, act_rows, act_turned, slope = up_forward(
        where, attended, patches, small_rows, up_bias_row, second
    )
    down = both_lanes(d, after(d_rest, act_rows))
    outputs, outputs_turned, gate_out, gate_grad, gate_bias_sum, theirs_h = down_forward(
        where, act_rows, mid_state, small_rows, head_cotangent, head_bias_row, down, second
    )
    head = both_lanes(h, after(h_rest, act_rows))
    got_h = exchange(theirs_h, SIBLING)
    end_grad, branch_grad, down_bias_sum, up_bias_sum, pre_grad, mine_h = head_backward(
        after(where, theirs_h), outputs_turned, act_cotangent, gate_grad, head_cotangent, slope, head, second, down
    )
    head_rows = rows_of(jnp.concatenate([gate_bias_sum, cotangent_sum], axis=1), 6)
    up_rows = rows_of(up_bias_sum, 4)
    keep_h, send_h = folded(mine_h, after(got_h, pre_grad))
    got_h = exchange(send_h, orders["head"][3])
    mid_grad, out_grad, terms, mine_d, theirs_d, mine_u, theirs_u = up_backward(
        after(where, send_h), small_rows, pre_grad, branch_grad, act_turned, mlp_turned,
        mid_state, end_grad, second,
    )
    got_d, got_u = exchange(theirs_d, SIBLING), exchange(theirs_u, SIBLING)
    pulled = (window_lengths, pad, out_grad, qkv, second)
    first_grad = attention_backward(where, *pulled, 0, 4)
    keep_h, send_h = folded(keep_h, after(got_h, first_grad))
    got_h = exchange(send_h, orders["head"][2])
    keep_u, send_u = folded(mine_u, after(got_u, first_grad))
    got_u = exchange(send_u, orders["up"][3])
    keep_d, send_d = folded(mine_d, after(got_d, first_grad))
    got_d = exchange(send_d, orders["down"][3])
    mine_m, theirs_m = mix_terms(
        after(where, send_h, send_d, send_u), first_grad, input_turned, attended_turned, out_grad
    )
    got_m = exchange(theirs_m, SIBLING)
    keep_h, send_h = folded(keep_h, after(got_h, theirs_m))
    got_h = exchange(send_h, orders["head"][1])
    second_grad = attention_backward(after(where, theirs_m, send_h), *pulled, 4, 2)
    keep_m, send_m = folded(mine_m, after(got_m, second_grad))
    got_m = exchange(send_m, orders["front"][3])
    keep_h, send_h = folded(keep_h, after(got_h, second_grad))
    got_h = exchange(send_h, orders["head"][0])
    keep_d, send_d = folded(keep_d, after(got_d, second_grad))
    got_d = exchange(send_d, orders["down"][2])
    patch_grad, mine_f, theirs_f = front_backward(
        after(where, send_h, send_m, send_d), lead_index, small_rows, terms, down_bias_sum,
        up_rows, head_rows, first_grad, second_grad, patches, mid_grad, input_turned, first,
    )
    got_f = exchange(theirs_f, SIBLING)
    keep_m, send_m = folded(keep_m, after(got_m, patch_grad))
    got_m = exchange(send_m, orders["front"][2])
    keep_f, send_f = folded(mine_f, after(got_f, send_m))
    got_f = exchange(send_f, orders["front"][3])
    keep_u, send_u = folded(keep_u, after(got_u, send_f))
    got_u = exchange(send_u, orders["up"][2])
    keep_d, send_d = folded(keep_d, after(got_d, send_f))
    got_d = exchange(send_d, orders["down"][1])
    head_out = head_forward(
        after(where, send_u, send_d), outputs, gate_out, head_bias_row, head
    )
    keep_f, send_f = folded(keep_f, after(got_f, head_out))
    got_f = exchange(send_f, orders["front"][2])
    keep_m, send_m = folded(keep_m, after(got_m, send_f))
    got_m = exchange(send_m, orders["front"][1])
    keep_u, send_u = folded(keep_u, after(got_u, send_f))
    got_u = exchange(send_u, orders["up"][1])
    keep_d, send_d = folded(keep_d, after(got_d, send_f))
    got_d = exchange(send_d, orders["down"][0])
    keep_f, send_f = folded(keep_f, after(got_f, send_m, send_d, send_u))
    got_f = exchange(send_f, orders["front"][1])
    keep_m, send_m = folded(keep_m, after(got_m, send_f))
    got_m = exchange(send_m, orders["front"][0])
    keep_u, send_u = folded(keep_u, after(got_u, send_f))
    got_u = exchange(send_u, orders["up"][0])
    gate_sum, rest_sum = finished(keep_h, after(got_h, send_u), core, (256, 2048))
    keep_f, send_f = folded(keep_f, after(got_f, send_u))
    got_f = exchange(send_f, orders["front"][0])
    early_sum, out_sum = finished(keep_m, after(got_m, send_f), core, (768, 384))
    (down_sum,) = finished(keep_d, after(got_d, send_f), core, (384,))
    (up_sum,) = finished(keep_u, after(got_u, send_f), core, (1536,))
    late_sum, small_sum = finished(keep_f, got_f, core, (384, 128))
    qkv_sum = jnp.concatenate(
        [
            piece[:, part * piece.shape[1] // 3 : (part + 1) * piece.shape[1] // 3]
            for part in range(3)
            for piece in (early_sum, late_sum)
        ],
        axis=1,
    )
    small_sum = small_sum.T
    return (
        outputs,
        head_out,
        patch_grad,
        small_sum[128:144],
        small_sum[0],
        small_sum[1],
        qkv_sum,
        out_sum,
        small_sum[2],
        small_sum[3],
        small_sum[4],
        up_sum,
        small_sum[6:10].reshape(96),
        down_sum,
        small_sum[5],
        jnp.concatenate([gate_sum, rest_sum], axis=1),
        small_sum[10:16].reshape(144),
    )


def plain_shards(
    patches,
    lead_index,
    window_lengths,
    pad_mask,
    lead_table,
    attn_gain,
    attn_shift,
    qkv_weight,
    out_weight,
    out_bias,
    mlp_gain,
    mlp_shift,
    up_weight,
    up_bias,
    down_weight,
    down_bias,
    head_weight,
    head_bias,
    act_cotangent,
    head_cotangent,
):
    front = (
        lax.all_gather(lead_table, ("dp", "fsdp"), axis=1, tiled=True),
        lax.all_gather(attn_gain, ("dp", "fsdp"), axis=0, tiled=True),
        lax.all_gather(attn_shift, ("dp", "fsdp"), axis=0, tiled=True),
        lax.all_gather(qkv_weight, ("dp", "fsdp"), axis=0, tiled=True),
        lax.all_gather(out_weight, ("dp", "fsdp"), axis=0, tiled=True),
        lax.all_gather(out_bias, ("dp", "fsdp"), axis=0, tiled=True),
    )
    rear = (
        lax.all_gather(mlp_gain, ("dp", "fsdp"), axis=0, tiled=True),
        lax.all_gather(mlp_shift, ("dp", "fsdp"), axis=0, tiled=True),
        lax.all_gather(up_weight, ("dp", "fsdp"), axis=0, tiled=True),
        lax.all_gather(up_bias, ("dp", "fsdp"), axis=0, tiled=True),
        lax.all_gather(down_weight, ("dp", "fsdp"), axis=0, tiled=True),
        lax.all_gather(down_bias, ("dp", "fsdp"), axis=0, tiled=True),
        lax.all_gather(head_weight, ("dp", "fsdp"), axis=0, tiled=True),
        lax.all_gather(head_bias, ("dp", "fsdp"), axis=0, tiled=True),
    )
    table_full, gain_one, shift_one, qkv_full, out_full, out_bias_full = front
    (
        gain_two,
        shift_two,
        up_full,
        up_bias_full,
        down_full,
        down_bias_full,
        head_full,
        head_bias_full,
    ) = rear
    token_rows, width = patches.shape
    head_dim = width // HEADS
    block_rows = min(512, token_rows)
    block_count = token_rows // block_rows
    ends = jnp.cumsum(window_lengths[0])
    positions = jnp.arange(token_rows, dtype=jnp.int32)
    window = jnp.sum((positions[:, None] >= ends[None, :]).astype(jnp.int32), axis=1)
    lead_hot = (jnp.arange(LEADS, dtype=jnp.int32) == lead_index[0]).astype(jnp.float32)
    lead_row = jnp.sum(lead_hot[:, None] * table_full.astype(jnp.float32), axis=0)
    start_state = patches.astype(jnp.float32) + lead_row[None, :]
    normed_one, pull_one = jax.vjp(
        layer_norm, start_state, gain_one.astype(jnp.float32), shift_one.astype(jnp.float32)
    )
    attn_input = normed_one.astype(jnp.bfloat16)
    qkv_rows = jnp.dot(attn_input, qkv_full, preferred_element_type=jnp.float32).astype(
        jnp.bfloat16
    )
    queries = qkv_rows[:, :width].reshape(block_count, block_rows, HEADS, head_dim)
    keys = qkv_rows[:, width : 2 * width].reshape(token_rows, HEADS, head_dim)
    values = qkv_rows[:, 2 * width :].reshape(token_rows, HEADS, head_dim)
    query_windows = window.reshape(block_count, block_rows)
    block_starts = jnp.arange(block_count, dtype=jnp.int32) * block_rows

    def block_scores(query_block, window_block, block_start):
        scores = (
            jnp.einsum("qhd,khd->hqk", query_block, keys, preferred_element_type=jnp.float32)
            * score_scale
        )
        allowed = allowed_keys(window_block, window, pad_mask, block_start)
        return jnp.where(allowed[None], scores, -1e30)

    def forward_block(inputs):
        query_block, window_block, block_start = inputs
        masked = block_scores(query_block, window_block, block_start)
        largest = jnp.max(masked, axis=-1, keepdims=True)
        raised = jnp.exp(masked - largest)
        total = jnp.sum(raised, axis=-1, keepdims=True)
        probs = (raised / total).astype(jnp.bfloat16)
        mixed = jnp.einsum("hqk,khd->qhd", probs, values, preferred_element_type=jnp.float32)
        return (
            mixed.reshape(block_rows, width).astype(jnp.bfloat16),
            (largest + jnp.log(total))[:, :, 0],
        )

    mixed_blocks, log_totals = lax.map(forward_block, (queries, query_windows, block_starts))
    attended = mixed_blocks.reshape(token_rows, width)
    mid_state = (
        start_state
        + jnp.dot(attended, out_full, preferred_element_type=jnp.float32)
        + out_bias_full.astype(jnp.float32)
    )
    normed_two, pull_two = jax.vjp(
        layer_norm, mid_state, gain_two.astype(jnp.float32), shift_two.astype(jnp.float32)
    )
    mlp_input = normed_two.astype(jnp.bfloat16)
    pre_act = jnp.dot(mlp_input, up_full, preferred_element_type=jnp.float32) + up_bias_full.astype(
        jnp.float32
    )
    activated, pull_act = jax.vjp(gelu_exact, pre_act)
    act_rows = activated.astype(jnp.bfloat16)
    end_state = (
        mid_state
        + jnp.dot(act_rows, down_full, preferred_element_type=jnp.float32)
        + down_bias_full.astype(jnp.float32)
    )
    outputs = end_state.astype(jnp.bfloat16)
    logits = jnp.dot(
        outputs, head_full, preferred_element_type=jnp.float32
    ) + head_bias_full.astype(jnp.float32)
    head_out, pull_head = jax.vjp(partial(expert_softmax, experts=EXPERTS, pixels=PIX), logits)
    up_back, down_back, head_back = (
        lax.all_gather(up_weight, ("dp", "fsdp"), axis=0, tiled=True),
        lax.all_gather(down_weight, ("dp", "fsdp"), axis=0, tiled=True),
        lax.all_gather(head_weight, ("dp", "fsdp"), axis=0, tiled=True),
    )
    qkv_back, out_back = (
        lax.all_gather(qkv_weight, ("dp", "fsdp"), axis=0, tiled=True),
        lax.all_gather(out_weight, ("dp", "fsdp"), axis=0, tiled=True),
    )
    logit_grad = pull_head(head_cotangent.astype(jnp.float32))[0].astype(jnp.bfloat16)
    head_bias_term = jnp.sum(logit_grad.astype(jnp.float32), axis=0)
    head_term = jnp.einsum("td,tn->dn", outputs, logit_grad, preferred_element_type=jnp.float32)
    end_grad = act_cotangent.astype(jnp.float32) + jnp.einsum(
        "tn,dn->td", logit_grad, head_back, preferred_element_type=jnp.float32
    )
    branch_grad = end_grad.astype(jnp.bfloat16)
    down_bias_term = jnp.sum(branch_grad.astype(jnp.float32), axis=0)
    down_term = jnp.einsum("tf,td->fd", act_rows, branch_grad, preferred_element_type=jnp.float32)
    act_grad = jnp.einsum("td,fd->tf", branch_grad, down_back, preferred_element_type=jnp.float32)
    pre_grad = pull_act(act_grad)[0].astype(jnp.bfloat16)
    up_bias_term = jnp.sum(pre_grad.astype(jnp.float32), axis=0)
    up_term = jnp.einsum("td,tf->df", mlp_input, pre_grad, preferred_element_type=jnp.float32)
    normed_two_grad = jnp.einsum("tf,df->td", pre_grad, up_back, preferred_element_type=jnp.float32)
    state_grad_two, gain_two_term, shift_two_term = pull_two(normed_two_grad)
    (
        gain_part,
        shift_part,
        up_part,
        up_bias_part,
        down_part,
        down_bias_part,
        head_part,
        head_bias_part,
    ) = (
        lax.psum_scatter(
            gain_two_term.astype(jnp.bfloat16), "dp", scatter_dimension=0, tiled=True
        ).astype(jnp.float32),
        lax.psum_scatter(
            shift_two_term.astype(jnp.bfloat16), "dp", scatter_dimension=0, tiled=True
        ).astype(jnp.float32),
        lax.psum_scatter(
            up_term.astype(jnp.bfloat16), "dp", scatter_dimension=0, tiled=True
        ).astype(jnp.float32),
        lax.psum_scatter(
            up_bias_term.astype(jnp.bfloat16), "dp", scatter_dimension=0, tiled=True
        ).astype(jnp.float32),
        lax.psum_scatter(
            down_term.astype(jnp.bfloat16), "dp", scatter_dimension=0, tiled=True
        ).astype(jnp.float32),
        lax.psum_scatter(
            down_bias_term.astype(jnp.bfloat16), "dp", scatter_dimension=0, tiled=True
        ).astype(jnp.float32),
        lax.psum_scatter(
            head_term.astype(jnp.bfloat16), "dp", scatter_dimension=0, tiled=True
        ).astype(jnp.float32),
        lax.psum_scatter(
            head_bias_term.astype(jnp.bfloat16), "dp", scatter_dimension=0, tiled=True
        ).astype(jnp.float32),
    )
    rear_grads = (
        lax.psum_scatter(gain_part, "fsdp", scatter_dimension=0, tiled=True),
        lax.psum_scatter(shift_part, "fsdp", scatter_dimension=0, tiled=True),
        lax.psum_scatter(up_part, "fsdp", scatter_dimension=0, tiled=True),
        lax.psum_scatter(up_bias_part, "fsdp", scatter_dimension=0, tiled=True),
        lax.psum_scatter(down_part, "fsdp", scatter_dimension=0, tiled=True),
        lax.psum_scatter(down_bias_part, "fsdp", scatter_dimension=0, tiled=True),
        lax.psum_scatter(head_part, "fsdp", scatter_dimension=0, tiled=True),
        lax.psum_scatter(head_bias_part, "fsdp", scatter_dimension=0, tiled=True),
    )
    mid_grad = end_grad + state_grad_two
    out_grad = mid_grad.astype(jnp.bfloat16)
    out_bias_term = jnp.sum(out_grad.astype(jnp.float32), axis=0)
    out_term = jnp.einsum("td,te->de", attended, out_grad, preferred_element_type=jnp.float32)
    mixed_grad = jnp.einsum(
        "te,de->td", out_grad, out_back, preferred_element_type=jnp.float32
    ).astype(jnp.bfloat16)
    grad_blocks = mixed_grad.reshape(block_count, block_rows, HEADS, head_dim)

    def backward_block(carry, inputs):
        key_sum, value_sum = carry
        query_block, grad_block, window_block, total_block, block_start = inputs
        masked = block_scores(query_block, window_block, block_start)
        probs = jnp.exp(masked - total_block[:, :, None])
        prob_grad = jnp.einsum(
            "qhd,khd->hqk", grad_block, values, preferred_element_type=jnp.float32
        )
        inner = jnp.sum(probs * prob_grad, axis=-1, keepdims=True)
        score_grad = (probs * (prob_grad - inner)).astype(jnp.bfloat16)
        query_grad = (
            jnp.einsum("hqk,khd->qhd", score_grad, keys, preferred_element_type=jnp.float32)
            * score_scale
        )
        key_sum = (
            key_sum
            + jnp.einsum(
                "hqk,qhd->khd", score_grad, query_block, preferred_element_type=jnp.float32
            )
            * score_scale
        )
        value_sum = value_sum + jnp.einsum(
            "hqk,qhd->khd",
            probs.astype(jnp.bfloat16),
            grad_block,
            preferred_element_type=jnp.float32,
        )
        return ((key_sum, value_sum), query_grad.reshape(block_rows, width))

    zero_keys = jnp.zeros((token_rows, HEADS, head_dim), jnp.float32)
    (key_grad, value_grad), query_grads = lax.scan(
        backward_block,
        (zero_keys, zero_keys),
        (queries, grad_blocks, query_windows, log_totals, block_starts),
    )
    qkv_grad = jnp.concatenate(
        [
            query_grads.reshape(token_rows, width),
            key_grad.reshape(token_rows, width),
            value_grad.reshape(token_rows, width),
        ],
        axis=1,
    ).astype(jnp.bfloat16)
    qkv_term = jnp.einsum("td,te->de", attn_input, qkv_grad, preferred_element_type=jnp.float32)
    normed_one_grad = jnp.einsum(
        "te,de->td", qkv_grad, qkv_back, preferred_element_type=jnp.float32
    )
    state_grad_one, gain_one_term, shift_one_term = pull_one(normed_one_grad)
    patch_grad = mid_grad + state_grad_one
    lead_term = lead_hot[:, None] * jnp.sum(patch_grad, axis=0)[None, :]
    lead_part, gain_one_part, shift_one_part, qkv_part, out_part, out_bias_part = (
        lax.psum_scatter(
            lead_term.astype(jnp.bfloat16), "dp", scatter_dimension=1, tiled=True
        ).astype(jnp.float32),
        lax.psum_scatter(
            gain_one_term.astype(jnp.bfloat16), "dp", scatter_dimension=0, tiled=True
        ).astype(jnp.float32),
        lax.psum_scatter(
            shift_one_term.astype(jnp.bfloat16), "dp", scatter_dimension=0, tiled=True
        ).astype(jnp.float32),
        lax.psum_scatter(
            qkv_term.astype(jnp.bfloat16), "dp", scatter_dimension=0, tiled=True
        ).astype(jnp.float32),
        lax.psum_scatter(
            out_term.astype(jnp.bfloat16), "dp", scatter_dimension=0, tiled=True
        ).astype(jnp.float32),
        lax.psum_scatter(
            out_bias_term.astype(jnp.bfloat16), "dp", scatter_dimension=0, tiled=True
        ).astype(jnp.float32),
    )
    front_grads = (
        lax.psum_scatter(lead_part, "fsdp", scatter_dimension=1, tiled=True),
        lax.psum_scatter(gain_one_part, "fsdp", scatter_dimension=0, tiled=True),
        lax.psum_scatter(shift_one_part, "fsdp", scatter_dimension=0, tiled=True),
        lax.psum_scatter(qkv_part, "fsdp", scatter_dimension=0, tiled=True),
        lax.psum_scatter(out_part, "fsdp", scatter_dimension=0, tiled=True),
        lax.psum_scatter(out_bias_part, "fsdp", scatter_dimension=0, tiled=True),
    )
    return (
        outputs,
        head_out,
        patch_grad,
        front_grads[0],
        front_grads[1],
        front_grads[2],
        front_grads[3],
        front_grads[4],
        front_grads[5],
        rear_grads[0],
        rear_grads[1],
        rear_grads[2],
        rear_grads[3],
        rear_grads[4],
        rear_grads[5],
        rear_grads[6],
        rear_grads[7],
    )


def solution(mesh):
    in_specs = (
        P(("dp", "fsdp"), None),
        P(("dp", "fsdp")),
        P(("dp", "fsdp"), None),
        P(("dp", "fsdp")),
        P(None, ("dp", "fsdp")),
        P(("dp", "fsdp")),
        P(("dp", "fsdp")),
        P(("dp", "fsdp"), None),
        P(("dp", "fsdp"), None),
        P(("dp", "fsdp")),
        P(("dp", "fsdp")),
        P(("dp", "fsdp")),
        P(("dp", "fsdp"), None),
        P(("dp", "fsdp")),
        P(("dp", "fsdp"), None),
        P(("dp", "fsdp")),
        P(("dp", "fsdp"), None),
        P(("dp", "fsdp")),
        P(("dp", "fsdp"), None),
        P(("dp", "fsdp"), None),
    )
    out_specs = (
        P(("dp", "fsdp"), None),
        P(("dp", "fsdp"), None),
        P(("dp", "fsdp"), None),
        P(None, ("dp", "fsdp")),
        P(("dp", "fsdp")),
        P(("dp", "fsdp")),
        P(("dp", "fsdp"), None),
        P(("dp", "fsdp"), None),
        P(("dp", "fsdp")),
        P(("dp", "fsdp")),
        P(("dp", "fsdp")),
        P(("dp", "fsdp"), None),
        P(("dp", "fsdp")),
        P(("dp", "fsdp"), None),
        P(("dp", "fsdp")),
        P(("dp", "fsdp"), None),
        P(("dp", "fsdp")),
    )
    body = shards if dict(mesh.shape) == {"dp": 4, "fsdp": 8} else plain_shards
    return jax.shard_map(body, mesh=mesh, in_specs=in_specs, out_specs=out_specs, check_vma=False)
```

```python
import math
from functools import partial

import jax
import jax.numpy as jnp
from jax import lax
from jax.experimental import pallas as pl
from jax.experimental.pallas import tpu as pltpu
from jax.sharding import PartitionSpec as P

HEADS = 12
PIX = 64
EXPERTS = 3
LEADS = 16


norm_epsilon = 1e-05
score_scale = 0.125


def layer_norm(hidden, norm_gain, norm_shift):
    average = jnp.mean(hidden, axis=-1, keepdims=True)
    centered = hidden - average
    variance = jnp.mean(centered * centered, axis=-1, keepdims=True)
    return centered * lax.rsqrt(variance + norm_epsilon) * norm_gain + norm_shift


def gelu_exact(values):
    return 0.5 * values * (1.0 + lax.erf(values * 0.7071067811865476))


def expert_softmax(logits, experts, pixels):
    gate_part = logits[:, : experts * pixels].reshape(logits.shape[0], experts, pixels)
    largest = jnp.max(gate_part, axis=1, keepdims=True)
    raised = jnp.exp(gate_part - largest)
    shares = raised / jnp.sum(raised, axis=1, keepdims=True)
    return jnp.concatenate(
        [shares.reshape(logits.shape[0], experts * pixels), logits[:, experts * pixels :]], axis=1
    )


def allowed_keys(query_window, key_window, key_valid, query_start):
    query_place = query_start + jnp.arange(query_window.shape[0], dtype=jnp.int32)
    key_place = jnp.arange(key_window.shape[0], dtype=jnp.int32)
    same_window = query_window[:, None] == key_window[None, :]
    usable = (key_valid[None, :] > 0) | (query_place[:, None] == key_place[None, :])
    return same_window & usable


AXES = ("dp", "fsdp")
FAR_Z, NEAR_Z, FIRST, SECOND, SIBLING = (4, 4), (2, 2), (8, 16), (16, 8), (1, 1)
ORDERS = {
    "q": (FAR_Z, NEAR_Z, FIRST, SECOND),
    "u": (FAR_Z, FIRST, SECOND, NEAR_Z),
    "d": (FIRST, FAR_Z, NEAR_Z, SECOND),
    "h": (NEAR_Z, FAR_Z, FIRST, SECOND),
    "head": (FAR_Z, NEAR_Z, FIRST, SECOND),
    "down": (FAR_Z, NEAR_Z, FIRST, SECOND),
    "up": (FAR_Z, FIRST, SECOND, NEAR_Z),
    "front": (FAR_Z, NEAR_Z, FIRST, SECOND),
}
GATHER_SEQUENCE = (
    ("q", 0), ("d", 0), ("h", 0), ("u", 0), ("q", 1), ("d", 1), ("u", 1), ("q", 2), ("h", 1), ("u", 2),
    ("d", 2),
)
MOST_VMEM, SPARE_VMEM = 56 * 1024 * 1024, 8 * 1024 * 1024
WIDTH = 768
HIDDEN = 3072
HEAD = 4608
TOKENS = 512
GATE = 512
F32 = jnp.float32
BF16 = jnp.bfloat16
HBM = pl.BlockSpec(memory_space=pltpu.HBM)
SMEM = pl.BlockSpec(memory_space=pltpu.SMEM)
VMEM = pl.BlockSpec(memory_space=pltpu.VMEM)
QKV_PART, SMALL_PART = (0, 1152), (1152, 128)
UP_PART, OUT_PART, GATE_PART = (0, 1536), (1536, 384), (1920, 256)
DOWN_PART, HEAD_PART = (0, 384), (0, 2048)


def chip_masks(order, lane):
    masks = []
    for place in range(16):
        mask = 0
        for step in range(4):
            if place >> step & 1:
                mask ^= order[step][lane]
        masks.append(mask >> 1)
    return masks


def table_start(group, side):
    return 1 + 32 * list(ORDERS).index(group) + 16 * side


def exchange(array, masks):
    return lax.ppermute(array, AXES, [(d, d ^ masks[d & 1]) for d in range(32)])


def whereabouts():
    device = lax.axis_index("dp") * 8 + lax.axis_index("fsdp")
    core, chip = device % 2, device // 2
    tables = [chip_masks(order, 0) + chip_masks(order, 1) for order in ORDERS.values()]
    swapped = [chip_masks(order, 1) + chip_masks(order, 0) for order in ORDERS.values()]
    places = jnp.where(core == 0, jnp.array(tables, jnp.int32), jnp.array(swapped, jnp.int32))
    places = (places ^ chip).reshape(32 * len(ORDERS))
    return core, jnp.concatenate([core[None].astype(jnp.int32), places])


def after(value, *marks):
    return lax.optimization_barrier((value, marks))[0]


def in_core_order(core, mine, theirs, axis):
    return jnp.where(
        core == 0,
        jnp.concatenate([mine, theirs], axis=axis),
        jnp.concatenate([theirs, mine], axis=axis),
    )


def pack_kernel(core, qkv, out, up, down, head, table, *refs):
    vectors, (up_bias, head_bias), refs = refs[:6], refs[6:8], refs[8:]
    outs, (rows,) = refs[:8], refs[8:]
    rows[...] = jnp.zeros_like(rows)
    for index, vector in enumerate(vectors):
        rows[index : index + 1, :24] = vector[...].astype(F32)
    for index in range(4):
        rows[6 + index : 7 + index, :24] = up_bias[:, 24 * index : 24 * index + 24].astype(F32)
    for index in range(6):
        rows[10 + index : 11 + index, :24] = head_bias[:, 24 * index : 24 * index + 24].astype(F32)
    rows[16:32, :24] = table[...].astype(F32)
    small = rows[...].T[:24].astype(BF16)
    for side in range(2):
        q, u, d, h = outs[4 * side : 4 * side + 4]
        q[:, :1152] = qkv[:, lane_columns(core, side, 1152)]
        q[:, 1152:] = small
        u[:, :1536] = up[:, lane_columns(core, side, 1536)]
        u[:, 1536:1920] = out[:, lane_columns(core, side, 384)]
        u[:, 1920:] = head[:, lane_columns(core, side, 256)]
        d[...] = down[:, lane_columns(core, side, 384)]
        h[...] = head[:, lane_columns(core, side, 2048, GATE)]


def packed(core, weights, table, vectors):
    shapes = [(24, 1280), (24, 2176), (96, 384), (24, 2048)] * 2
    return call(
        pack_kernel,
        (core.reshape(1), *weights, table, *[vector[None] for vector in vectors]),
        [SMEM] + [VMEM] * 14,
        [(shape, BF16, False) for shape in shapes],
        [pltpu.VMEM((128, 128), F32)],
    )


def doubled(held, masks):
    return jnp.concatenate([held, exchange(held, masks)], axis=0)


def both_lanes(*arrays):
    return arrays + tuple(exchange(array, SIBLING) for array in arrays)


def total(first, second):
    return first.astype(F32) + second.astype(F32)


def folded(keep, got, start=0):
    half = got.shape[0] // 2
    send = total(keep[half:], got[half:]).astype(BF16)
    return total(keep[:half], got[:half]).astype(BF16), send


def finished(keep, got, core, widths):
    block = total(keep, got)[0]
    rows = block.shape[0] // 2
    upper, lower = block[:rows], block[rows:]
    mine = jnp.where(core == 0, upper, lower)
    theirs = jnp.where(core == 0, lower, upper).astype(BF16)
    other = exchange(theirs, SIBLING).astype(F32)
    pieces, start = [], 0
    for width in widths:
        span = slice(start, start + width)
        pieces.append(in_core_order(core, mine[:, span], other[:, span], 1))
        start += width
    return pieces


def across(first, second):
    return lax.dot_general(first, second, (((1,), (1,)), ((), ())), preferred_element_type=F32)


def times(first, second):
    return jnp.dot(first, second, preferred_element_type=F32)


def lane_columns(where, side, stride, first=0, width=None):
    return pl.ds(pl.multiple_of(first + (where[0] ^ side) * stride, 128), width or stride)


def block_copies(where, group, sources, part, target, sems, side, first=0):
    start, width = part
    rows = sources[0].shape[1]
    half = len(sources) // 2
    count = 16 // half
    copies = []
    for place in range(16):
        row = pl.multiple_of(where[table_start(group, side) + place] * rows, rows)
        copies.append(
            pltpu.make_async_copy(
                sources[half * side + place // count].at[place % count, :, pl.ds(start, width)],
                target.at[pl.ds(row, rows), lane_columns(where, side, width, first)],
                sems.at[side, place],
            )
        )
    return copies


def term_copies(where, group, lane, out, sems, side):
    rows = out.shape[1]
    copies = []
    for place in range(16):
        row = pl.multiple_of(where[table_start(group, side) + place] * rows, rows)
        copies.append(
            pltpu.make_async_copy(lane.at[side, pl.ds(row, rows), :], out.at[place], sems.at[side, place])
        )
    return copies


class Halves:
    def __init__(self, source, target, sems, index):
        rows = target.shape[0] // 2
        parts = [pl.ds(half * rows, rows) for half in range(2)]
        self.copies = [
            pltpu.make_async_copy(source.at[part], target.at[part], sems.at[*index, half])
            for half, part in enumerate(parts)
        ]

    def start(self, priority=0):
        for half, copy in enumerate(self.copies):
            copy.start(priority=half)

    def wait(self):
        for copy in self.copies:
            copy.wait()


def start_all(copies):
    for index, copy in enumerate(copies):
        copy.start(priority=index % 2)


def wait_all(copies):
    for copy in copies:
        copy.wait()


def mean_and_scale(hidden):
    average = jnp.mean(hidden, axis=1, keepdims=True)
    centered = hidden - average
    variance = jnp.mean(centered * centered, axis=1, keepdims=True)
    return centered, lax.rsqrt(variance + norm_epsilon)


def norm_backward(hidden, gain, upstream):
    centered, scale = mean_and_scale(hidden)
    normed = centered * scale
    gain_grad = jnp.sum(upstream * normed, axis=0, keepdims=True)
    shift_grad = jnp.sum(upstream, axis=0, keepdims=True)
    scaled = upstream * gain
    first = jnp.mean(scaled, axis=1, keepdims=True)
    second = jnp.mean(scaled * normed, axis=1, keepdims=True)
    return scale * (scaled - first - normed * second), gain_grad, shift_grad


def call(kernel, operands, in_specs, outs, scratch, spare=None):
    def size(item):
        return math.prod(item.shape) * jnp.dtype(item.dtype).itemsize

    held = [item for item, spec in zip(operands, in_specs) if spec is VMEM]
    held += [jax.ShapeDtypeStruct(shape, kind) for shape, kind, copied in outs if not copied]
    held += [item for item in scratch if getattr(item, "memory_space", None) == pltpu.VMEM]
    limit = MOST_VMEM if spare is None else sum(size(item) for item in held) + spare
    return pl.pallas_call(
        kernel,
        out_shape=[jax.ShapeDtypeStruct(shape, kind) for shape, kind, _ in outs],
        in_specs=in_specs,
        out_specs=[HBM if copied else VMEM for _, _, copied in outs],
        scratch_shapes=scratch,
        compiler_params=pltpu.CompilerParams(vmem_limit_bytes=limit),
        cost_estimate=pl.CostEstimate(flops=2 * 10**12, bytes_accessed=10**10, transcendentals=0),
    )(*operands)


def lane_scratch(rows, width):
    return [pltpu.VMEM((2, rows, width), BF16), pltpu.SemaphoreType.DMA((2, 16))]


def weight_scratch(rows, width):
    return [pltpu.VMEM((rows, width), BF16), pltpu.SemaphoreType.DMA((2, 16))]


def taken(refs, *counts):
    groups = []
    for count in counts:
        groups.append(refs[:count])
        refs = refs[count:]
    return *groups, refs


def front_kernel(where, lead, patches, *refs):
    sources, outs, scratch = taken(refs, 4, 3)
    turned_out, qkv_out, small = outs
    weight, sems, smalls, small_sems, state, rows, turned, qkv, io_sems = scratch
    loads = [block_copies(where, "q", sources, QKV_PART, weight, sems, side) for side in range(2)]
    small_loads = []
    for place in range(16):
        row = pl.multiple_of(where[table_start("q", 0) + place] * 48, 48)
        small_loads.append(
            pltpu.make_async_copy(
                sources[place // 8].at[place % 8, :, pl.ds(*SMALL_PART)],
                smalls.at[pl.ds(row, 48), :],
                small_sems.at[place],
            )
        )
    state_load = Halves(patches, state, io_sems, (0,))
    start_all(small_loads)
    state_load.start()
    start_all(loads[0])
    start_all(loads[1])
    wait_all(small_loads)
    columns = smalls[...].astype(F32).T
    places = lax.broadcasted_iota(jnp.int32, (LEADS, WIDTH), 0)
    lead_row = jnp.sum(
        jnp.where(places == lead[0], columns[16 : 16 + LEADS], 0.0), axis=0, keepdims=True
    )
    small[...] = columns[:32]
    small[16:17, :] = lead_row
    state_load.wait()
    centered, scale = mean_and_scale(state[...].astype(F32) + lead_row)
    rows[...] = (centered * scale * columns[0:1] + columns[1:2]).astype(BF16)
    turned[...] = rows[...].T
    stores = [Halves(turned, turned_out, io_sems, (1,))]
    stores[0].start()
    wait_all(loads[0] + loads[1])
    for part in range(3):
        span = slice(part * WIDTH, part * WIDTH + WIDTH)
        qkv[:, span] = times(rows[...], weight[:, span]).astype(BF16)
        stores.append(Halves(qkv.at[:, span], qkv_out.at[:, span], io_sems, (2 + part,)))
        stores[-1].start()
    wait_all(stores)


def front_forward(where, lead_index, patches, arrays):
    return call(
        front_kernel,
        (where, lead_index, patches, *arrays),
        [SMEM, SMEM, HBM] + [HBM] * 4,
        [
            ((WIDTH, TOKENS), BF16, True),
            ((TOKENS, 3 * WIDTH), BF16, True),
            ((32, WIDTH), F32, False),
        ],
        weight_scratch(WIDTH, 3 * WIDTH)
        + [pltpu.VMEM((WIDTH, 128), BF16), pltpu.SemaphoreType.DMA((16,))]
        + [
            pltpu.VMEM((TOKENS, WIDTH), BF16),
            pltpu.VMEM((TOKENS, WIDTH), BF16),
            pltpu.VMEM((WIDTH, TOKENS), BF16),
            pltpu.VMEM((TOKENS, 3 * WIDTH), BF16),
            pltpu.SemaphoreType.DMA((5, 2)),
        ],
    )


KEY_SPANS = ((0, 256), (0, 384), (128, 512), (256, 512))


def fill_bias(lengths, pad, bias):
    ends, end = [], 0
    for index in range(lengths.shape[1]):
        end = end + lengths[0, index]
        ends.append(end)

    def windows(places):
        return sum([(places >= end).astype(jnp.int32) for end in ends])

    for block, (low, high) in enumerate(KEY_SPANS):
        count = high - low
        queries = lax.broadcasted_iota(jnp.int32, (1, 128), 1) + 128 * block
        keys = lax.broadcasted_iota(jnp.int32, (count, 1), 0) + low
        same = windows(queries) == windows(keys)
        usable = (pad[low:high, :] > 0) | (queries == keys)
        bias[block, :count, :] = jnp.where(same & usable, 0.0, -1e30)


def two_heads(block):
    first = lax.broadcasted_iota(jnp.int32, block.shape, 1) < block.shape[1] // 2
    zero = jnp.zeros_like(block)
    return jnp.concatenate([jnp.where(first, block, zero), jnp.where(first, zero, block)], axis=0)


def head_rows_of(stacked):
    return jnp.concatenate([stacked[:64, :128], stacked[64:, 128:]], axis=0)


def probabilities(scores, allowed):
    masked = scores * score_scale + allowed
    raised = jnp.exp(masked - jnp.max(masked, axis=0, keepdims=True))
    return raised * (1.0 / jnp.sum(raised, axis=0, keepdims=True))


def attention_kernel(where, lengths, pad, qkv, attended_out, turned_out, bias, turned, rows, sems):
    fill_bias(lengths, pad, bias)

    def pair(index, carry):
        first = index * 128
        columns = pl.ds(pl.multiple_of(first, 128), 128)
        keys_at = pl.ds(pl.multiple_of(first + WIDTH, 128), 128)
        values = qkv[:, pl.ds(pl.multiple_of(first + 2 * WIDTH, 128), 128)].T
        for block, (low, high) in enumerate(KEY_SPANS):
            span = slice(128 * block, 128 * block + 128)
            scores = across(qkv[low:high, keys_at], two_heads(qkv[span, columns]))
            allowed = bias[block, : high - low, :]
            probs = [
                probabilities(scores[:, 128 * head : 128 * head + 128], allowed).astype(BF16)
                for head in range(2)
            ]
            mixed = times(values[:, low:high], jnp.concatenate(probs, axis=1))
            turned[columns, span] = head_rows_of(mixed).astype(BF16)
        return carry

    lax.fori_loop(0, WIDTH // 128, pair, 0)
    stores = [pltpu.make_async_copy(turned, turned_out, sems.at[0])]
    stores[0].start()
    rows[...] = turned[...].T
    stores.append(pltpu.make_async_copy(rows, attended_out, sems.at[1]))
    stores[1].start()
    wait_all(stores)


def attention_forward(where, lengths, pad, qkv):
    rows, columns = (TOKENS, WIDTH), (WIDTH, TOKENS)
    return call(
        attention_kernel,
        (where, lengths, pad, qkv),
        [SMEM, SMEM, VMEM, VMEM],
        [(rows, BF16, True), (columns, BF16, True)],
        [
            pltpu.VMEM((4, 384, 128), F32),
            pltpu.VMEM(columns, BF16),
            pltpu.VMEM(rows, BF16),
            pltpu.SemaphoreType.DMA((2,)),
        ],
    )


def up_kernel(where, attended, patches, small, bias, *refs):
    sources, outs, scratch = taken(refs, 4, 5)
    mid_out, mlp_turned_out, act_out, act_turned_out, slope_out = outs
    out_weight, out_sems, weight, sems, scratch = *scratch[:4], scratch[4:]
    inputs, state, mid, rows, mlp_turned, act, act_turned, slope, io_sems, act_sems = scratch
    out_loads = [block_copies(where, "u", sources, OUT_PART, out_weight, out_sems, s) for s in range(2)]
    loads = [block_copies(where, "u", sources, UP_PART, weight, sems, side) for side in range(2)]
    in_loads = [
        Halves(attended, inputs, io_sems, (0,)),
        Halves(patches, state, io_sems, (1,)),
    ]
    start_all(in_loads)
    start_all(out_loads[0] + out_loads[1])
    start_all(loads[0] + loads[1])
    wait_all(in_loads)
    wait_all(out_loads[0] + out_loads[1])
    mid[...] = (
        state[...].astype(F32)
        + small[16:17, :]
        + times(inputs[...], out_weight[...])
        + small[2:3, :]
    )
    centered, scale = mean_and_scale(mid[...])
    rows[...] = (centered * scale * small[3:4, :] + small[4:5, :]).astype(BF16)
    mlp_turned[...] = rows[...].T
    stores = [
        Halves(mid, mid_out, io_sems, (2,)),
        Halves(mlp_turned, mlp_turned_out, io_sems, (3,)),
    ]
    start_all(stores)
    wait_all(loads[0] + loads[1])
    for slot in range(6):
        span = slice(slot * 512, slot * 512 + 512)
        values = times(rows[...], weight[:, span]) + bias[:, span]
        share = 0.5 * (1.0 + lax.erf(values * 0.7071067811865476))
        density = jnp.exp(-0.5 * values * values) * 0.3989422804014327
        activated = (values * share).astype(BF16)
        act[:, span] = activated
        act_turned[span, :] = activated.T
        slope[:, span] = (share + values * density).astype(BF16)
        copies = [
            Halves(act.at[:, span], act_out.at[:, span], act_sems, (slot, 0,)),
            Halves(act_turned.at[span, :], act_turned_out.at[span, :], act_sems, (slot, 1,)),
            Halves(slope.at[:, span], slope_out.at[:, span], act_sems, (slot, 2,)),
        ]
        start_all(copies)
        stores += copies
    wait_all(stores)


def up_forward(where, attended, patches, small, bias, arrays):
    rows, columns = (TOKENS, WIDTH), (WIDTH, TOKENS)
    wide, tall = (TOKENS, HIDDEN), (HIDDEN, TOKENS)
    return call(
        up_kernel,
        (where, attended, patches, small, bias, *arrays),
        [SMEM, HBM, HBM, VMEM, VMEM] + [HBM] * 4,
        [
            (rows, F32, True),
            (columns, BF16, True),
            (wide, BF16, True),
            (tall, BF16, True),
            (wide, BF16, True),
        ],
        weight_scratch(WIDTH, WIDTH)
        + weight_scratch(WIDTH, HIDDEN)
        + [
            pltpu.VMEM(rows, BF16),
            pltpu.VMEM(rows, BF16),
            pltpu.VMEM(rows, F32),
            pltpu.VMEM(rows, BF16),
            pltpu.VMEM(columns, BF16),
            pltpu.VMEM(wide, BF16),
            pltpu.VMEM(tall, BF16),
            pltpu.VMEM(wide, BF16),
            pltpu.SemaphoreType.DMA((4, 2)),
            pltpu.SemaphoreType.DMA((6, 3, 2)),
        ],
    )


def gate_shares(logits, cotangent, shares, gate_grad):
    shares[:, 256:] = logits[:, 256:]
    gate_grad[:, 256:] = cotangent[:, 256:GATE]
    first, rest = logits[:, :128], logits[:, 128:256]
    left = lax.broadcasted_iota(jnp.int32, first.shape, 1) < PIX
    third = jnp.where(left, rest, pltpu.roll(rest, PIX, 1))
    largest = jnp.maximum(jnp.maximum(first, pltpu.roll(first, PIX, 1)), third)
    raised, raised_third = jnp.exp(first - largest), jnp.exp(third - largest)
    scale = 1.0 / (raised + pltpu.roll(raised, PIX, 1) + raised_third)
    share, share_third = raised * scale, raised_third * scale
    shares[:, :128] = share
    shares[:, 128:256] = jnp.where(left, share_third, rest)
    pull, other = cotangent[:, :128].astype(F32), cotangent[:, 128:256].astype(F32)
    pull_third = jnp.where(left, other, pltpu.roll(other, PIX, 1))
    weighed = share * pull
    inner = weighed + pltpu.roll(weighed, PIX, 1) + share_third * pull_third
    gate_grad[:, :128] = (share * (pull - inner)).astype(BF16)
    gate_grad[:, 128:256] = jnp.where(left, share_third * (pull_third - inner), other).astype(BF16)


def down_kernel(where, act, mid, small, cotangent, bias, *refs):
    sources, gate_sources, outs, scratch = taken(refs, 4, 4, 6)
    outputs, turned, shares, gate_grad, gate_bias, theirs_out = outs
    weight, sems, gate, gate_sems, lane, lane_sems, scratch = *scratch[:6], scratch[6:]
    acts, mids, pulls, logits, io_sems = scratch
    loads = [block_copies(where, "d", sources, DOWN_PART, weight, sems, side) for side in range(2)]
    gate_loads = [
        block_copies(where, "u", gate_sources, GATE_PART, gate, gate_sems, side) for side in range(2)
    ]
    in_loads = [
        Halves(act, acts, io_sems, (0,)),
        Halves(mid, mids, io_sems, (1,)),
    ]
    lane_span = lane_columns(where, 1, 2048, GATE)
    pull_loads = [
        Halves(cotangent.at[:, :GATE], pulls.at[:, :GATE], io_sems, (2,)),
        Halves(cotangent.at[:, lane_span], pulls.at[:, GATE:], io_sems, (3,)),
    ]
    start_all(in_loads)
    start_all(loads[0] + loads[1])
    start_all(gate_loads[0] + gate_loads[1])
    start_all(pull_loads)
    wait_all(in_loads)
    wait_all(loads[0] + loads[1])
    outputs[...] = (mids[...] + times(acts[...], weight[...]) + small[5:6, :]).astype(BF16)
    turned[...] = outputs[...].T
    wait_all(gate_loads[0] + gate_loads[1])
    logits[...] = times(outputs[...], gate[...]) + bias[:, :GATE]
    wait_all(pull_loads)
    gate_shares(logits, pulls, shares, gate_grad)
    gate_bias[...] = jnp.sum(gate_grad[...].astype(F32), axis=0, keepdims=True)
    wait_all(head_terms(where, turned, gate_grad, pulls, lane, theirs_out, lane_sems, 1, GATE))


def head_terms(where, turned, gate_grad, pulls, lane, out, sems, side, first):
    lane[:, :256] = times(turned[...], gate_grad[:, lane_columns(where, side, 256)]).astype(BF16)
    for tile in range(4):
        span = pl.ds(pl.multiple_of(first + tile * 512, 512), 512)
        lane[:, 256 + tile * 512 : 768 + tile * 512] = times(turned[...], pulls[:, span]).astype(BF16)
    copies = []
    for place in range(16):
        row = pl.multiple_of(where[table_start("head", side) + place] * 48, 48)
        copies.append(
            pltpu.make_async_copy(lane.at[pl.ds(row, 48), :], out.at[place], sems.at[place])
        )
    start_all(copies)
    return copies


def down_forward(where, act, mid, small, cotangent, bias, arrays, gate_arrays):
    rows = (TOKENS, WIDTH)
    return call(
        down_kernel,
        (where, act, mid, small, cotangent, bias, *arrays, *gate_arrays),
        [SMEM, HBM, HBM, VMEM, HBM, VMEM] + [HBM] * 8,
        [
            (rows, BF16, False),
            ((WIDTH, TOKENS), BF16, False),
            ((TOKENS, GATE), F32, False),
            ((TOKENS, GATE), BF16, False),
            ((1, GATE), F32, False),
            ((16, 48, 2304), BF16, True),
        ],
        weight_scratch(HIDDEN, WIDTH)
        + weight_scratch(WIDTH, GATE)
        + [pltpu.VMEM((WIDTH, 2304), BF16), pltpu.SemaphoreType.DMA((16,))]
        + [
            pltpu.VMEM((TOKENS, HIDDEN), BF16),
            pltpu.VMEM(rows, F32),
            pltpu.VMEM((TOKENS, GATE + 2048), BF16),
            pltpu.VMEM((TOKENS, GATE), F32),
            pltpu.SemaphoreType.DMA((4, 2)),
        ],
    )


def head_kernel(where, rows, gate_out, bias, *refs):
    sources, outs, scratch = taken(refs, 4, 1)
    (out,) = outs
    weight, sems, inputs, result, io_sems = scratch
    loads = [block_copies(where, "h", sources, HEAD_PART, weight, sems, side) for side in range(2)]
    row_load = Halves(rows, inputs, io_sems, (0,))
    gate_load = Halves(gate_out, result.at[:, :GATE], io_sems, (1,))
    row_load.start()
    start_all(loads[0])
    start_all(loads[1])
    gate_load.start()
    row_load.wait()
    stores = []

    def store(span):
        stores.append(
            Halves(result.at[:, span], out.at[:, span], io_sems, (2 + len(stores),))
        )
        stores[-1].start()

    for side in range(2):
        wait_all(loads[side])
        for tile in range(4):
            span = lane_columns(where, side, 2048, GATE + tile * 512, 512)
            columns = lane_columns(where, side, 2048, tile * 512, 512)
            result[:, span] = times(inputs[...], weight[:, columns]) + bias[:, span]
            store(span)
    gate_load.wait()
    store(pl.ds(0, GATE))
    wait_all(stores)


def head_forward(where, rows, gate_out, bias, arrays):
    return call(
        head_kernel,
        (where, rows, gate_out, bias, *arrays),
        [SMEM, HBM, HBM, VMEM] + [HBM] * 4,
        [((TOKENS, HEAD), F32, True)],
        weight_scratch(WIDTH, HEAD - GATE)
        + [
            pltpu.VMEM((TOKENS, WIDTH), BF16),
            pltpu.VMEM((TOKENS, HEAD), F32),
            pltpu.SemaphoreType.DMA((11, 2)),
        ],
        spare=SPARE_VMEM,
    )[0]


def head_back_kernel(where, turned, act_cotangent, gate_grad, cotangent, slope, *refs):
    sources, gate_sources, down_sources, outs, scratch = taken(refs, 4, 4, 4, 6)
    end_grad, branch, down_bias, up_bias, pre_out, mine_out = outs
    weight, sems, gate_sems, down, down_sems, lane, lane_sems, scratch = *scratch[:7], scratch[7:]
    act_pulls, pulls, slopes, pre_grad, io_sems, pre_sems = scratch
    loads = [
        block_copies(where, "h", sources, HEAD_PART, weight, sems, side, GATE) for side in range(2)
    ]
    gate_loads = [
        block_copies(where, "u", gate_sources, GATE_PART, weight, gate_sems, side)
        for side in range(2)
    ]
    down_loads = [
        block_copies(where, "d", down_sources, DOWN_PART, down, down_sems, side) for side in range(2)
    ]
    first_loads = [Halves(act_cotangent, act_pulls, io_sems, (0,))]
    pull_load = Halves(cotangent.at[:, GATE:], pulls.at[:, GATE:], io_sems, (2,))
    slope_load = Halves(slope, slopes, io_sems, (3,))
    pull_load.start()
    start_all(first_loads + gate_loads[0] + gate_loads[1])
    start_all(loads[0])
    start_all(loads[1])
    start_all(down_loads[0] + down_loads[1])
    slope_load.start()
    wait_all(first_loads)
    pulls[:, :GATE] = gate_grad[...]
    pull_load.wait()
    stores = head_terms(
        where, turned, gate_grad, pulls, lane, mine_out, lane_sems, 0, GATE + where[0] * 2048
    )
    wait_all(gate_loads[0] + gate_loads[1])
    wait_all(loads[0] + loads[1])
    end_grad[...] = act_pulls[...].astype(F32) + across(pulls[...], weight[...])
    branch[...] = end_grad[...].astype(BF16)
    down_bias[...] = jnp.sum(branch[...].astype(F32), axis=0, keepdims=True)
    wait_all(down_loads[0] + down_loads[1])
    slope_load.wait()
    for tile in range(6):
        span = slice(tile * 512, tile * 512 + 512)
        grad = across(branch[...], down[span, :])
        rounded = (slopes[:, span].astype(F32) * grad).astype(BF16)
        pre_grad[:, span] = rounded
        up_bias[:, span] = jnp.sum(rounded.astype(F32), axis=0, keepdims=True)
        stores.append(
            Halves(pre_grad.at[:, span], pre_out.at[:, span], pre_sems, (tile,))
        )
        stores[-1].start()
    wait_all(stores)


def head_backward(
    where, turned, act_cotangent, gate_grad, cotangent, slope, arrays, gate_arrays, down_arrays
):
    rows, wide = (TOKENS, WIDTH), (TOKENS, HIDDEN)
    return call(
        head_back_kernel,
        (
            where, turned, act_cotangent, gate_grad, cotangent, slope,
            *arrays, *gate_arrays, *down_arrays,
        ),
        [SMEM, VMEM, HBM, VMEM, HBM, HBM] + [HBM] * 12,
        [
            (rows, F32, False),
            (rows, BF16, False),
            ((1, WIDTH), F32, False),
            ((1, HIDDEN), F32, False),
            (wide, BF16, True),
            ((16, 48, 2304), BF16, True),
        ],
        weight_scratch(WIDTH, HEAD)
        + [pltpu.SemaphoreType.DMA((2, 16))]
        + weight_scratch(HIDDEN, WIDTH)
        + [pltpu.VMEM((WIDTH, 2304), BF16), pltpu.SemaphoreType.DMA((16,))]
        + [
            pltpu.VMEM(rows, BF16),
            pltpu.VMEM((TOKENS, HEAD), BF16),
            pltpu.VMEM(wide, BF16),
            pltpu.VMEM(wide, BF16),
            pltpu.SemaphoreType.DMA((4, 2)),
            pltpu.SemaphoreType.DMA((6, 2)),
        ],
    )


def up_back_kernel(
    where, small, pre_grad, branch, act_turned, mlp_turned, mid, end_grad, *refs
):
    sources, outs, scratch = taken(refs, 4, 7)
    mid_grad, out_grad, terms, down_mine, down_theirs, up_mine, up_theirs = outs
    weight, sems, down_lane, down_sems, up_lane, up_sems, scratch = *scratch[:6], scratch[6:]
    pres, branches, acts, mlps, mids, ends, io_sems = scratch
    loads = [block_copies(where, "u", sources, UP_PART, weight, sems, side) for side in range(2)]
    pre_load = Halves(pre_grad, pres, io_sems, (0,))
    branch_load = Halves(branch, branches, io_sems, (1,))
    act_load = Halves(act_turned, acts, io_sems, (2,))
    mlp_load = Halves(mlp_turned, mlps, io_sems, (3,))
    norm_loads = [
        Halves(mid, mids, io_sems, (4,)),
        Halves(end_grad, ends, io_sems, (5,)),
    ]
    branch_load.start()
    act_load.start()
    pre_load.start()
    mlp_load.start()
    start_all(loads[0] + loads[1])
    start_all(norm_loads)
    branch_load.wait()
    act_load.wait()
    stores = []
    for side, out in ((1, down_theirs), (0, down_mine)):
        span = lane_columns(where, side, 384)
        for part in range(4):
            rows = slice(part * WIDTH, part * WIDTH + WIDTH)
            down_lane[side, rows, :] = times(acts[rows, :], branches[:, span]).astype(BF16)
        copies = term_copies(where, "down", down_lane, out, down_sems, side)
        start_all(copies)
        stores += copies
    pre_load.wait()
    mlp_load.wait()
    for side, out in ((1, up_theirs), (0, up_mine)):
        for tile in range(3):
            span = lane_columns(where, side, 1536, tile * 512, 512)
            up_lane[side, :, tile * 512 : tile * 512 + 512] = times(mlps[...], pres[:, span]).astype(
                BF16
            )
        copies = term_copies(where, "up", up_lane, out, up_sems, side)
        start_all(copies)
        stores += copies
    wait_all(loads[0] + loads[1])
    grad = across(pres[...], weight[...])
    wait_all(norm_loads)
    pulled, gain_grad, shift_grad = norm_backward(mids[...], small[3:4, :], grad)
    pulled = pulled + ends[...]
    rounded = pulled.astype(BF16)
    mid_grad[...] = pulled
    out_grad[...] = rounded
    terms[...] = jnp.zeros_like(terms)
    terms[0:1, :] = jnp.sum(rounded.astype(F32), axis=0, keepdims=True)
    terms[1:2, :] = gain_grad
    terms[2:3, :] = shift_grad
    wait_all(stores)


def up_backward(
    where, small, pre_grad, branch, act_turned, mlp_turned, mid, end_grad, arrays
):
    rows = (TOKENS, WIDTH)
    return call(
        up_back_kernel,
        (where, small, pre_grad, branch, act_turned, mlp_turned, mid, end_grad, *arrays),
        [SMEM, VMEM] + [HBM] * 10,
        [
            (rows, F32, False),
            (rows, BF16, False),
            ((8, WIDTH), F32, False),
            ((16, 192, 384), BF16, True),
            ((16, 192, 384), BF16, True),
            ((16, 48, 1536), BF16, True),
            ((16, 48, 1536), BF16, True),
        ],
        weight_scratch(WIDTH, HIDDEN)
        + lane_scratch(HIDDEN, 384)
        + lane_scratch(WIDTH, 1536)
        + [
            pltpu.VMEM((TOKENS, HIDDEN), BF16),
            pltpu.VMEM(rows, BF16),
            pltpu.VMEM((HIDDEN, TOKENS), BF16),
            pltpu.VMEM((WIDTH, TOKENS), BF16),
            pltpu.VMEM(rows, F32),
            pltpu.VMEM(rows, F32),
            pltpu.SemaphoreType.DMA((6, 2)),
        ],
    )


def attention_back_kernel(start, count, where, lengths, pad, out_grad, qkv, *refs):
    sources, outs, scratch = taken(refs, 4, 1)
    (qkv_grad,) = outs
    weight, sems, bias, mixed, turned, key_sum, value_sum = scratch
    loads = [block_copies(where, "u", sources, OUT_PART, weight, sems, side) for side in range(2)]
    start_all(loads[0] + loads[1])
    fill_bias(lengths, pad, bias)
    wait_all(loads[0] + loads[1])
    width = 128 * count
    mixed[...] = across(
        out_grad[...], weight[128 * start : 128 * start + width, :]
    ).astype(BF16)

    def columns_at(first):
        return pl.ds(pl.multiple_of(first, 128), 128)

    def pair(index, carry):
        own, first = index * 128, (index + start) * 128
        columns, keys_at = columns_at(first), columns_at(first + WIDTH)
        values_at = columns_at(first + 2 * WIDTH)
        keys_turned = qkv[:, keys_at].T
        key_sum[...] = jnp.zeros_like(key_sum)
        value_sum[...] = jnp.zeros_like(value_sum)
        for block, (low, high) in enumerate(KEY_SPANS):
            span = slice(128 * block, 128 * block + 128)
            queries, grads = two_heads(qkv[span, columns]), two_heads(mixed[span, columns_at(own)])
            scores = across(qkv[low:high, keys_at], queries)
            prob_grads = across(qkv[low:high, values_at], grads)
            allowed = bias[block, : high - low, :]
            probs, score_grads = [], []
            for head in range(2):
                part = slice(128 * head, 128 * head + 128)
                prob = probabilities(scores[:, part], allowed)
                pulled = prob * prob_grads[:, part]
                inner = jnp.sum(pulled, axis=0, keepdims=True)
                probs.append(prob.astype(BF16))
                score_grads.append((pulled - prob * inner).astype(BF16))
            score_grad = jnp.concatenate(score_grads, axis=1)
            key_sum[low:high, :] += times(score_grad, queries)
            value_sum[low:high, :] += times(jnp.concatenate(probs, axis=1), grads)
            turned[:, span] = head_rows_of(times(keys_turned[:, low:high], score_grad)) * score_scale
        qkv_grad[:, columns_at(own)] = turned[...].T.astype(BF16)
        qkv_grad[:, columns_at(own + width)] = (key_sum[...] * score_scale).astype(BF16)
        qkv_grad[:, columns_at(own + 2 * width)] = value_sum[...].astype(BF16)
        return carry

    lax.fori_loop(0, count, pair, 0)


def attention_backward(where, lengths, pad, out_grad, qkv, arrays, start, count):
    return call(
        partial(attention_back_kernel, start, count),
        (where, lengths, pad, out_grad, qkv, *arrays),
        [SMEM, SMEM, VMEM, VMEM, VMEM] + [HBM] * 4,
        [((TOKENS, 3 * 128 * count), BF16, False)],
        weight_scratch(WIDTH, WIDTH)
        + [
            pltpu.VMEM((4, 384, 128), F32),
            pltpu.VMEM((TOKENS, 128 * count), BF16),
            pltpu.VMEM((128, TOKENS), F32),
            pltpu.VMEM((TOKENS, 128), F32),
            pltpu.VMEM((TOKENS, 128), F32),
        ],
        spare=SPARE_VMEM,
    )[0]


def mix_term_kernel(where, qkv_grad, input_turned, attended_turned, out_grad, mine_out, theirs_out, *refs):
    lane, sems = refs
    stores = []
    for side, out in ((1, theirs_out), (0, mine_out)):
        lane[side, :, :768] = times(
            input_turned[...], qkv_grad[:, lane_columns(where, side, 768)]
        ).astype(BF16)
        lane[side, :, 768:1152] = times(
            attended_turned[...], out_grad[:, lane_columns(where, side, 384)]
        ).astype(BF16)
        copies = term_copies(where, "front", lane, out, sems, side)
        start_all(copies)
        stores += copies
    wait_all(stores)


def mix_terms(where, qkv_grad, input_turned, attended_turned, out_grad):
    return call(
        mix_term_kernel,
        (where, qkv_grad, input_turned, attended_turned, out_grad),
        [SMEM] + [VMEM] * 4,
        [((16, 48, 1152), BF16, True)] * 2,
        lane_scratch(WIDTH, 1152),
        spare=SPARE_VMEM,
    )


def front_back_kernel(
    where, lead, small, terms, down_row, up_rows, head_rows,
    first_grad, second_grad, patches, mid_grad, input_turned, *refs
):
    sources, outs, scratch = taken(refs, 4, 3)
    patch_out, mine_out, theirs_out = outs
    weight, sems, lane, lane_sems, scratch = *scratch[:4], scratch[4:]
    pulls, late_pulls, state, mids, inputs, patch_grad, small_grad, io_sems = scratch
    loads = [block_copies(where, "q", sources, QKV_PART, weight, sems, side) for side in range(2)]
    pairs = [(patches, state), (mid_grad, mids), (input_turned, inputs), (second_grad, late_pulls)]
    for part in range(3):
        for source, start, size in ((first_grad, 0, 512), (second_grad, 512, 256)):
            columns = pl.ds(WIDTH * part + start, size)
            pairs.append((source.at[:, pl.ds(size * part, size)], pulls.at[:, columns]))
    in_loads = [Halves(*pair, io_sems, (at,)) for at, pair in enumerate(pairs)]
    start_all(in_loads[4:])
    start_all(loads[0] + loads[1])
    start_all(in_loads[:4])
    wait_all(in_loads[4:])
    wait_all(loads[0] + loads[1])
    grad = across(pulls[...], weight[...])
    wait_all(in_loads[:4])
    pulled, gain_grad, shift_grad = norm_backward(
        state[...].astype(F32) + small[16:17, :], small[0:1, :], grad
    )
    pulled = pulled + mids[...]
    patch_grad[...] = pulled
    stores = [Halves(patch_grad, patch_out, io_sems, (10,))]
    stores[0].start()
    small_grad[0:1, :] = gain_grad
    small_grad[1:2, :] = shift_grad
    small_grad[2:5, :] = terms[0:3, :]
    small_grad[5:6, :] = down_row[...]
    small_grad[6:10, :] = up_rows[...]
    small_grad[10:16, :] = head_rows[...]
    places = lax.broadcasted_iota(jnp.int32, (LEADS, WIDTH), 0)
    lead_grad = jnp.sum(pulled, axis=0, keepdims=True)
    small_grad[16:32, :] = jnp.where(places == lead[0], lead_grad, 0.0)
    for side, out in ((1, theirs_out), (0, mine_out)):
        lane[side, :, :384] = times(
            inputs[...], late_pulls[:, lane_columns(where, side, 384)]
        ).astype(BF16)
        rows = small_grad[pl.ds(pl.multiple_of((where[0] ^ side) * 16, 16), 16), :]
        rows = jnp.concatenate([rows, jnp.zeros((112, WIDTH), F32)], axis=0)
        lane[side, :, 384:] = rows.T.astype(BF16)
        copies = term_copies(where, "front", lane, out, lane_sems, side)
        start_all(copies)
        stores += copies
    wait_all(stores)


def front_backward(
    where, lead, small, terms, down_row, up_rows, head_rows,
    first_grad, second_grad, patches, mid_grad, input_turned, arrays,
):
    rows, columns = (TOKENS, WIDTH), (WIDTH, TOKENS)
    return call(
        front_back_kernel,
        (
            where, lead, small, terms, down_row, up_rows, head_rows,
            first_grad, second_grad, patches, mid_grad, input_turned, *arrays,
        ),
        [SMEM, SMEM] + [VMEM] * 5 + [HBM] * 9,
        [(rows, F32, True), ((16, 48, 512), BF16, True), ((16, 48, 512), BF16, True)],
        weight_scratch(WIDTH, 3 * WIDTH)
        + lane_scratch(WIDTH, 512)
        + [
            pltpu.VMEM((TOKENS, 3 * WIDTH), BF16),
            pltpu.VMEM(rows, BF16),
            pltpu.VMEM(rows, BF16),
            pltpu.VMEM(rows, F32),
            pltpu.VMEM(columns, BF16),
            pltpu.VMEM(rows, F32),
            pltpu.VMEM((32, WIDTH), F32),
            pltpu.SemaphoreType.DMA((11, 2)),
        ],
        spare=SPARE_VMEM,
    )


def rows_of(vector, count):
    return vector.reshape(32, count, 24).transpose(1, 0, 2).reshape(count, WIDTH)


def vector_of(rows):
    count = rows.shape[0]
    return rows.reshape(count, 32, 24).transpose(1, 0, 2).reshape(1, count * WIDTH)


def shards(
    patches,
    lead_index,
    window_lengths,
    pad_mask,
    lead_table,
    attn_gain,
    attn_shift,
    qkv_weight,
    out_weight,
    out_bias,
    mlp_gain,
    mlp_shift,
    up_weight,
    up_bias,
    down_weight,
    down_bias,
    head_weight,
    head_bias,
    act_cotangent,
    head_cotangent,
):
    core, where = whereabouts()
    weights = (qkv_weight, out_weight, up_weight, down_weight, head_weight)
    vectors = (
        attn_gain, attn_shift, out_bias, mlp_gain, mlp_shift, down_bias, up_bias, head_bias
    )
    parts = packed(core, weights, lead_table, vectors)
    pad = pad_mask[:, None]
    cotangent_sum = jnp.sum(head_cotangent[:, GATE:].astype(F32), axis=0, keepdims=True)

    orders = ORDERS
    parts = dict(zip("qudh", zip(parts[:4], parts[4:])))
    chunks = {
        name: in_core_order(core, mine, exchange(theirs, SIBLING), 0)[None]
        for name, (mine, theirs) in parts.items()
    }

    held, last = dict(chunks), ()
    for name, step in GATHER_SEQUENCE:
        held[name] = after(held[name], *last)
        last = (held[name],)
        held[name] = doubled(held[name], orders[name][step])
    q, u, d, h = [held[name] for name in ("q", "u", "d", "h")]
    q_rest = exchange(after(q, *last), orders["q"][3])
    u = after(u, q)
    u_rest = exchange(u, orders["u"][3])
    d_rest = exchange(d, orders["d"][3])
    h = doubled(after(h, u), orders["h"][2])
    first = both_lanes(q, q_rest)
    h_rest = exchange(h, orders["h"][3])
    input_turned, qkv, small_rows = front_forward(
        after(where, d, h, cotangent_sum), lead_index, patches, first
    )
    attended, attended_turned = attention_forward(where, window_lengths, pad, qkv)
    u_rest, d_rest, h_rest = lax.optimization_barrier((u_rest, d_rest, h_rest, attended))[:3]
    second = both_lanes(u, u_rest)
    up_bias_row, head_bias_row = vector_of(small_rows[6:10]), vector_of(small_rows[10:16])
    mid_state, mlp_turned, act_rows, act_turned, slope = up_forward(
        where, attended, patches, small_rows, up_bias_row, second
    )
    down = both_lanes(d, after(d_rest, act_rows))
    outputs, outputs_turned, gate_out, gate_grad, gate_bias_sum, theirs_h = down_forward(
        where, act_rows, mid_state, small_rows, head_cotangent, head_bias_row, down, second
    )
    head = both_lanes(h, after(h_rest, act_rows))
    got_h = exchange(theirs_h, SIBLING)
    end_grad, branch_grad, down_bias_sum, up_bias_sum, pre_grad, mine_h = head_backward(
        after(where, theirs_h), outputs_turned, act_cotangent, gate_grad, head_cotangent, slope, head, second, down
    )
    head_rows = rows_of(jnp.concatenate([gate_bias_sum, cotangent_sum], axis=1), 6)
    up_rows = rows_of(up_bias_sum, 4)
    keep_h, send_h = folded(mine_h, after(got_h, pre_grad))
    got_h = exchange(send_h, orders["head"][3])
    mid_grad, out_grad, terms, mine_d, theirs_d, mine_u, theirs_u = up_backward(
        after(where, send_h), small_rows, pre_grad, branch_grad, act_turned, mlp_turned,
        mid_state, end_grad, second,
    )
    got_d, got_u = exchange(theirs_d, SIBLING), exchange(theirs_u, SIBLING)
    pulled = (window_lengths, pad, out_grad, qkv, second)
    first_grad = attention_backward(where, *pulled, 0, 4)
    keep_h, send_h = folded(keep_h, after(got_h, first_grad))
    got_h = exchange(send_h, orders["head"][2])
    keep_u, send_u = folded(mine_u, after(got_u, first_grad))
    got_u = exchange(send_u, orders["up"][3])
    keep_d, send_d = folded(mine_d, after(got_d, first_grad))
    got_d = exchange(send_d, orders["down"][3])
    mine_m, theirs_m = mix_terms(
        after(where, send_h, send_d, send_u), first_grad, input_turned, attended_turned, out_grad
    )
    got_m = exchange(theirs_m, SIBLING)
    keep_h, send_h = folded(keep_h, after(got_h, theirs_m))
    got_h = exchange(send_h, orders["head"][1])
    second_grad = attention_backward(after(where, theirs_m, send_h), *pulled, 4, 2)
    keep_m, send_m = folded(mine_m, after(got_m, second_grad))
    got_m = exchange(send_m, orders["front"][3])
    keep_d, send_d = folded(keep_d, after(got_d, second_grad))
    got_d = exchange(send_d, orders["down"][2])
    patch_grad, mine_f, theirs_f = front_backward(
        after(where, send_m, send_d), lead_index, small_rows, terms, down_bias_sum,
        up_rows, head_rows, first_grad, second_grad, patches, mid_grad, input_turned, first,
    )
    got_f = exchange(theirs_f, SIBLING)
    keep_m, send_m = folded(keep_m, after(got_m, patch_grad))
    got_m = exchange(send_m, orders["front"][2])
    keep_f, send_f = folded(mine_f, after(got_f, send_m))
    got_f = exchange(send_f, orders["front"][3])
    keep_h, send_h = folded(keep_h, after(got_h, send_f))
    got_h = exchange(send_h, orders["head"][0])
    keep_u, send_u = folded(keep_u, after(got_u, send_f))
    got_u = exchange(send_u, orders["up"][2])
    keep_d, send_d = folded(keep_d, after(got_d, send_f))
    got_d = exchange(send_d, orders["down"][1])
    head_out = head_forward(
        after(where, send_u, send_d, send_h), outputs, gate_out, head_bias_row, head
    )
    keep_f, send_f = folded(keep_f, after(got_f, head_out))
    got_f = exchange(send_f, orders["front"][2])
    keep_m, send_m = folded(keep_m, after(got_m, send_f))
    got_m = exchange(send_m, orders["front"][1])
    keep_u, send_u = folded(keep_u, after(got_u, send_f))
    got_u = exchange(send_u, orders["up"][1])
    keep_d, send_d = folded(keep_d, after(got_d, send_f))
    got_d = exchange(send_d, orders["down"][0])
    keep_f, send_f = folded(keep_f, after(got_f, send_m, send_d, send_u))
    got_f = exchange(send_f, orders["front"][1])
    keep_m, send_m = folded(keep_m, after(got_m, send_f))
    got_m = exchange(send_m, orders["front"][0])
    keep_u, send_u = folded(keep_u, after(got_u, send_f))
    got_u = exchange(send_u, orders["up"][0])
    gate_sum, rest_sum = finished(keep_h, after(got_h, send_u), core, (256, 2048))
    keep_f, send_f = folded(keep_f, after(got_f, send_u))
    got_f = exchange(send_f, orders["front"][0])
    early_sum, out_sum = finished(keep_m, after(got_m, send_f), core, (768, 384))
    (down_sum,) = finished(keep_d, after(got_d, send_f), core, (384,))
    (up_sum,) = finished(keep_u, after(got_u, send_f), core, (1536,))
    late_sum, small_sum = finished(keep_f, got_f, core, (384, 128))
    qkv_sum = jnp.concatenate(
        [
            piece[:, part * piece.shape[1] // 3 : (part + 1) * piece.shape[1] // 3]
            for part in range(3)
            for piece in (early_sum, late_sum)
        ],
        axis=1,
    )
    small_sum = small_sum.T
    return (
        outputs,
        head_out,
        patch_grad,
        small_sum[128:144],
        small_sum[0],
        small_sum[1],
        qkv_sum,
        out_sum,
        small_sum[2],
        small_sum[3],
        small_sum[4],
        up_sum,
        small_sum[6:10].reshape(96),
        down_sum,
        small_sum[5],
        jnp.concatenate([gate_sum, rest_sum], axis=1),
        small_sum[10:16].reshape(144),
    )


def plain_shards(
    patches,
    lead_index,
    window_lengths,
    pad_mask,
    lead_table,
    attn_gain,
    attn_shift,
    qkv_weight,
    out_weight,
    out_bias,
    mlp_gain,
    mlp_shift,
    up_weight,
    up_bias,
    down_weight,
    down_bias,
    head_weight,
    head_bias,
    act_cotangent,
    head_cotangent,
):
    front = (
        lax.all_gather(lead_table, ("dp", "fsdp"), axis=1, tiled=True),
        lax.all_gather(attn_gain, ("dp", "fsdp"), axis=0, tiled=True),
        lax.all_gather(attn_shift, ("dp", "fsdp"), axis=0, tiled=True),
        lax.all_gather(qkv_weight, ("dp", "fsdp"), axis=0, tiled=True),
        lax.all_gather(out_weight, ("dp", "fsdp"), axis=0, tiled=True),
        lax.all_gather(out_bias, ("dp", "fsdp"), axis=0, tiled=True),
    )
    rear = (
        lax.all_gather(mlp_gain, ("dp", "fsdp"), axis=0, tiled=True),
        lax.all_gather(mlp_shift, ("dp", "fsdp"), axis=0, tiled=True),
        lax.all_gather(up_weight, ("dp", "fsdp"), axis=0, tiled=True),
        lax.all_gather(up_bias, ("dp", "fsdp"), axis=0, tiled=True),
        lax.all_gather(down_weight, ("dp", "fsdp"), axis=0, tiled=True),
        lax.all_gather(down_bias, ("dp", "fsdp"), axis=0, tiled=True),
        lax.all_gather(head_weight, ("dp", "fsdp"), axis=0, tiled=True),
        lax.all_gather(head_bias, ("dp", "fsdp"), axis=0, tiled=True),
    )
    table_full, gain_one, shift_one, qkv_full, out_full, out_bias_full = front
    (
        gain_two,
        shift_two,
        up_full,
        up_bias_full,
        down_full,
        down_bias_full,
        head_full,
        head_bias_full,
    ) = rear
    token_rows, width = patches.shape
    head_dim = width // HEADS
    block_rows = min(512, token_rows)
    block_count = token_rows // block_rows
    ends = jnp.cumsum(window_lengths[0])
    positions = jnp.arange(token_rows, dtype=jnp.int32)
    window = jnp.sum((positions[:, None] >= ends[None, :]).astype(jnp.int32), axis=1)
    lead_hot = (jnp.arange(LEADS, dtype=jnp.int32) == lead_index[0]).astype(jnp.float32)
    lead_row = jnp.sum(lead_hot[:, None] * table_full.astype(jnp.float32), axis=0)
    start_state = patches.astype(jnp.float32) + lead_row[None, :]
    normed_one, pull_one = jax.vjp(
        layer_norm, start_state, gain_one.astype(jnp.float32), shift_one.astype(jnp.float32)
    )
    attn_input = normed_one.astype(jnp.bfloat16)
    qkv_rows = jnp.dot(attn_input, qkv_full, preferred_element_type=jnp.float32).astype(
        jnp.bfloat16
    )
    queries = qkv_rows[:, :width].reshape(block_count, block_rows, HEADS, head_dim)
    keys = qkv_rows[:, width : 2 * width].reshape(token_rows, HEADS, head_dim)
    values = qkv_rows[:, 2 * width :].reshape(token_rows, HEADS, head_dim)
    query_windows = window.reshape(block_count, block_rows)
    block_starts = jnp.arange(block_count, dtype=jnp.int32) * block_rows

    def block_scores(query_block, window_block, block_start):
        scores = (
            jnp.einsum("qhd,khd->hqk", query_block, keys, preferred_element_type=jnp.float32)
            * score_scale
        )
        allowed = allowed_keys(window_block, window, pad_mask, block_start)
        return jnp.where(allowed[None], scores, -1e30)

    def forward_block(inputs):
        query_block, window_block, block_start = inputs
        masked = block_scores(query_block, window_block, block_start)
        largest = jnp.max(masked, axis=-1, keepdims=True)
        raised = jnp.exp(masked - largest)
        total = jnp.sum(raised, axis=-1, keepdims=True)
        probs = (raised / total).astype(jnp.bfloat16)
        mixed = jnp.einsum("hqk,khd->qhd", probs, values, preferred_element_type=jnp.float32)
        return (
            mixed.reshape(block_rows, width).astype(jnp.bfloat16),
            (largest + jnp.log(total))[:, :, 0],
        )

    mixed_blocks, log_totals = lax.map(forward_block, (queries, query_windows, block_starts))
    attended = mixed_blocks.reshape(token_rows, width)
    mid_state = (
        start_state
        + jnp.dot(attended, out_full, preferred_element_type=jnp.float32)
        + out_bias_full.astype(jnp.float32)
    )
    normed_two, pull_two = jax.vjp(
        layer_norm, mid_state, gain_two.astype(jnp.float32), shift_two.astype(jnp.float32)
    )
    mlp_input = normed_two.astype(jnp.bfloat16)
    pre_act = jnp.dot(mlp_input, up_full, preferred_element_type=jnp.float32) + up_bias_full.astype(
        jnp.float32
    )
    activated, pull_act = jax.vjp(gelu_exact, pre_act)
    act_rows = activated.astype(jnp.bfloat16)
    end_state = (
        mid_state
        + jnp.dot(act_rows, down_full, preferred_element_type=jnp.float32)
        + down_bias_full.astype(jnp.float32)
    )
    outputs = end_state.astype(jnp.bfloat16)
    logits = jnp.dot(
        outputs, head_full, preferred_element_type=jnp.float32
    ) + head_bias_full.astype(jnp.float32)
    head_out, pull_head = jax.vjp(partial(expert_softmax, experts=EXPERTS, pixels=PIX), logits)
    up_back, down_back, head_back = (
        lax.all_gather(up_weight, ("dp", "fsdp"), axis=0, tiled=True),
        lax.all_gather(down_weight, ("dp", "fsdp"), axis=0, tiled=True),
        lax.all_gather(head_weight, ("dp", "fsdp"), axis=0, tiled=True),
    )
    qkv_back, out_back = (
        lax.all_gather(qkv_weight, ("dp", "fsdp"), axis=0, tiled=True),
        lax.all_gather(out_weight, ("dp", "fsdp"), axis=0, tiled=True),
    )
    logit_grad = pull_head(head_cotangent.astype(jnp.float32))[0].astype(jnp.bfloat16)
    head_bias_term = jnp.sum(logit_grad.astype(jnp.float32), axis=0)
    head_term = jnp.einsum("td,tn->dn", outputs, logit_grad, preferred_element_type=jnp.float32)
    end_grad = act_cotangent.astype(jnp.float32) + jnp.einsum(
        "tn,dn->td", logit_grad, head_back, preferred_element_type=jnp.float32
    )
    branch_grad = end_grad.astype(jnp.bfloat16)
    down_bias_term = jnp.sum(branch_grad.astype(jnp.float32), axis=0)
    down_term = jnp.einsum("tf,td->fd", act_rows, branch_grad, preferred_element_type=jnp.float32)
    act_grad = jnp.einsum("td,fd->tf", branch_grad, down_back, preferred_element_type=jnp.float32)
    pre_grad = pull_act(act_grad)[0].astype(jnp.bfloat16)
    up_bias_term = jnp.sum(pre_grad.astype(jnp.float32), axis=0)
    up_term = jnp.einsum("td,tf->df", mlp_input, pre_grad, preferred_element_type=jnp.float32)
    normed_two_grad = jnp.einsum("tf,df->td", pre_grad, up_back, preferred_element_type=jnp.float32)
    state_grad_two, gain_two_term, shift_two_term = pull_two(normed_two_grad)
    (
        gain_part,
        shift_part,
        up_part,
        up_bias_part,
        down_part,
        down_bias_part,
        head_part,
        head_bias_part,
    ) = (
        lax.psum_scatter(
            gain_two_term.astype(jnp.bfloat16), "dp", scatter_dimension=0, tiled=True
        ).astype(jnp.float32),
        lax.psum_scatter(
            shift_two_term.astype(jnp.bfloat16), "dp", scatter_dimension=0, tiled=True
        ).astype(jnp.float32),
        lax.psum_scatter(
            up_term.astype(jnp.bfloat16), "dp", scatter_dimension=0, tiled=True
        ).astype(jnp.float32),
        lax.psum_scatter(
            up_bias_term.astype(jnp.bfloat16), "dp", scatter_dimension=0, tiled=True
        ).astype(jnp.float32),
        lax.psum_scatter(
            down_term.astype(jnp.bfloat16), "dp", scatter_dimension=0, tiled=True
        ).astype(jnp.float32),
        lax.psum_scatter(
            down_bias_term.astype(jnp.bfloat16), "dp", scatter_dimension=0, tiled=True
        ).astype(jnp.float32),
        lax.psum_scatter(
            head_term.astype(jnp.bfloat16), "dp", scatter_dimension=0, tiled=True
        ).astype(jnp.float32),
        lax.psum_scatter(
            head_bias_term.astype(jnp.bfloat16), "dp", scatter_dimension=0, tiled=True
        ).astype(jnp.float32),
    )
    rear_grads = (
        lax.psum_scatter(gain_part, "fsdp", scatter_dimension=0, tiled=True),
        lax.psum_scatter(shift_part, "fsdp", scatter_dimension=0, tiled=True),
        lax.psum_scatter(up_part, "fsdp", scatter_dimension=0, tiled=True),
        lax.psum_scatter(up_bias_part, "fsdp", scatter_dimension=0, tiled=True),
        lax.psum_scatter(down_part, "fsdp", scatter_dimension=0, tiled=True),
        lax.psum_scatter(down_bias_part, "fsdp", scatter_dimension=0, tiled=True),
        lax.psum_scatter(head_part, "fsdp", scatter_dimension=0, tiled=True),
        lax.psum_scatter(head_bias_part, "fsdp", scatter_dimension=0, tiled=True),
    )
    mid_grad = end_grad + state_grad_two
    out_grad = mid_grad.astype(jnp.bfloat16)
    out_bias_term = jnp.sum(out_grad.astype(jnp.float32), axis=0)
    out_term = jnp.einsum("td,te->de", attended, out_grad, preferred_element_type=jnp.float32)
    mixed_grad = jnp.einsum(
        "te,de->td", out_grad, out_back, preferred_element_type=jnp.float32
    ).astype(jnp.bfloat16)
    grad_blocks = mixed_grad.reshape(block_count, block_rows, HEADS, head_dim)

    def backward_block(carry, inputs):
        key_sum, value_sum = carry
        query_block, grad_block, window_block, total_block, block_start = inputs
        masked = block_scores(query_block, window_block, block_start)
        probs = jnp.exp(masked - total_block[:, :, None])
        prob_grad = jnp.einsum(
            "qhd,khd->hqk", grad_block, values, preferred_element_type=jnp.float32
        )
        inner = jnp.sum(probs * prob_grad, axis=-1, keepdims=True)
        score_grad = (probs * (prob_grad - inner)).astype(jnp.bfloat16)
        query_grad = (
            jnp.einsum("hqk,khd->qhd", score_grad, keys, preferred_element_type=jnp.float32)
            * score_scale
        )
        key_sum = (
            key_sum
            + jnp.einsum(
                "hqk,qhd->khd", score_grad, query_block, preferred_element_type=jnp.float32
            )
            * score_scale
        )
        value_sum = value_sum + jnp.einsum(
            "hqk,qhd->khd",
            probs.astype(jnp.bfloat16),
            grad_block,
            preferred_element_type=jnp.float32,
        )
        return ((key_sum, value_sum), query_grad.reshape(block_rows, width))

    zero_keys = jnp.zeros((token_rows, HEADS, head_dim), jnp.float32)
    (key_grad, value_grad), query_grads = lax.scan(
        backward_block,
        (zero_keys, zero_keys),
        (queries, grad_blocks, query_windows, log_totals, block_starts),
    )
    qkv_grad = jnp.concatenate(
        [
            query_grads.reshape(token_rows, width),
            key_grad.reshape(token_rows, width),
            value_grad.reshape(token_rows, width),
        ],
        axis=1,
    ).astype(jnp.bfloat16)
    qkv_term = jnp.einsum("td,te->de", attn_input, qkv_grad, preferred_element_type=jnp.float32)
    normed_one_grad = jnp.einsum(
        "te,de->td", qkv_grad, qkv_back, preferred_element_type=jnp.float32
    )
    state_grad_one, gain_one_term, shift_one_term = pull_one(normed_one_grad)
    patch_grad = mid_grad + state_grad_one
    lead_term = lead_hot[:, None] * jnp.sum(patch_grad, axis=0)[None, :]
    lead_part, gain_one_part, shift_one_part, qkv_part, out_part, out_bias_part = (
        lax.psum_scatter(
            lead_term.astype(jnp.bfloat16), "dp", scatter_dimension=1, tiled=True
        ).astype(jnp.float32),
        lax.psum_scatter(
            gain_one_term.astype(jnp.bfloat16), "dp", scatter_dimension=0, tiled=True
        ).astype(jnp.float32),
        lax.psum_scatter(
            shift_one_term.astype(jnp.bfloat16), "dp", scatter_dimension=0, tiled=True
        ).astype(jnp.float32),
        lax.psum_scatter(
            qkv_term.astype(jnp.bfloat16), "dp", scatter_dimension=0, tiled=True
        ).astype(jnp.float32),
        lax.psum_scatter(
            out_term.astype(jnp.bfloat16), "dp", scatter_dimension=0, tiled=True
        ).astype(jnp.float32),
        lax.psum_scatter(
            out_bias_term.astype(jnp.bfloat16), "dp", scatter_dimension=0, tiled=True
        ).astype(jnp.float32),
    )
    front_grads = (
        lax.psum_scatter(lead_part, "fsdp", scatter_dimension=1, tiled=True),
        lax.psum_scatter(gain_one_part, "fsdp", scatter_dimension=0, tiled=True),
        lax.psum_scatter(shift_one_part, "fsdp", scatter_dimension=0, tiled=True),
        lax.psum_scatter(qkv_part, "fsdp", scatter_dimension=0, tiled=True),
        lax.psum_scatter(out_part, "fsdp", scatter_dimension=0, tiled=True),
        lax.psum_scatter(out_bias_part, "fsdp", scatter_dimension=0, tiled=True),
    )
    return (
        outputs,
        head_out,
        patch_grad,
        front_grads[0],
        front_grads[1],
        front_grads[2],
        front_grads[3],
        front_grads[4],
        front_grads[5],
        rear_grads[0],
        rear_grads[1],
        rear_grads[2],
        rear_grads[3],
        rear_grads[4],
        rear_grads[5],
        rear_grads[6],
        rear_grads[7],
    )


def solution(mesh):
    in_specs = (
        P(("dp", "fsdp"), None),
        P(("dp", "fsdp")),
        P(("dp", "fsdp"), None),
        P(("dp", "fsdp")),
        P(None, ("dp", "fsdp")),
        P(("dp", "fsdp")),
        P(("dp", "fsdp")),
        P(("dp", "fsdp"), None),
        P(("dp", "fsdp"), None),
        P(("dp", "fsdp")),
        P(("dp", "fsdp")),
        P(("dp", "fsdp")),
        P(("dp", "fsdp"), None),
        P(("dp", "fsdp")),
        P(("dp", "fsdp"), None),
        P(("dp", "fsdp")),
        P(("dp", "fsdp"), None),
        P(("dp", "fsdp")),
        P(("dp", "fsdp"), None),
        P(("dp", "fsdp"), None),
    )
    out_specs = (
        P(("dp", "fsdp"), None),
        P(("dp", "fsdp"), None),
        P(("dp", "fsdp"), None),
        P(None, ("dp", "fsdp")),
        P(("dp", "fsdp")),
        P(("dp", "fsdp")),
        P(("dp", "fsdp"), None),
        P(("dp", "fsdp"), None),
        P(("dp", "fsdp")),
        P(("dp", "fsdp")),
        P(("dp", "fsdp")),
        P(("dp", "fsdp"), None),
        P(("dp", "fsdp")),
        P(("dp", "fsdp"), None),
        P(("dp", "fsdp")),
        P(("dp", "fsdp"), None),
        P(("dp", "fsdp")),
    )
    body = shards if dict(mesh.shape) == {"dp": 4, "fsdp": 8} else plain_shards
    return jax.shard_map(body, mesh=mesh, in_specs=in_specs, out_specs=out_specs, check_vma=False)
```

```python
import math
from functools import partial

import jax
import jax.numpy as jnp
from jax import lax
from jax.experimental import pallas as pl
from jax.experimental.pallas import tpu as pltpu
from jax.sharding import PartitionSpec as P

HEADS = 12
PIX = 64
EXPERTS = 3
LEADS = 16


norm_epsilon = 1e-05
score_scale = 0.125


def layer_norm(hidden, norm_gain, norm_shift):
    average = jnp.mean(hidden, axis=-1, keepdims=True)
    centered = hidden - average
    variance = jnp.mean(centered * centered, axis=-1, keepdims=True)
    return centered * lax.rsqrt(variance + norm_epsilon) * norm_gain + norm_shift


def gelu_exact(values):
    return 0.5 * values * (1.0 + lax.erf(values * 0.7071067811865476))


def expert_softmax(logits, experts, pixels):
    gate_part = logits[:, : experts * pixels].reshape(logits.shape[0], experts, pixels)
    largest = jnp.max(gate_part, axis=1, keepdims=True)
    raised = jnp.exp(gate_part - largest)
    shares = raised / jnp.sum(raised, axis=1, keepdims=True)
    return jnp.concatenate(
        [shares.reshape(logits.shape[0], experts * pixels), logits[:, experts * pixels :]], axis=1
    )


def allowed_keys(query_window, key_window, key_valid, query_start):
    query_place = query_start + jnp.arange(query_window.shape[0], dtype=jnp.int32)
    key_place = jnp.arange(key_window.shape[0], dtype=jnp.int32)
    same_window = query_window[:, None] == key_window[None, :]
    usable = (key_valid[None, :] > 0) | (query_place[:, None] == key_place[None, :])
    return same_window & usable


AXES = ("dp", "fsdp")
FAR_Z, NEAR_Z, FIRST, SECOND, SIBLING = (4, 4), (2, 2), (8, 16), (16, 8), (1, 1)
ORDERS = {
    "q": (FAR_Z, NEAR_Z, FIRST, SECOND),
    "u": (FAR_Z, FIRST, SECOND, NEAR_Z),
    "d": (FIRST, FAR_Z, NEAR_Z, SECOND),
    "h": (NEAR_Z, FAR_Z, FIRST, SECOND),
    "head": (FAR_Z, NEAR_Z, FIRST, SECOND),
    "down": (FAR_Z, NEAR_Z, FIRST, SECOND),
    "up": (FAR_Z, FIRST, SECOND, NEAR_Z),
    "front": (FAR_Z, NEAR_Z, FIRST, SECOND),
}
GATHER_SEQUENCE = (
    ("q", 0), ("d", 0), ("h", 0), ("u", 0), ("q", 1), ("d", 1), ("u", 1), ("q", 2), ("h", 1), ("u", 2),
    ("d", 2),
)
MOST_VMEM, SPARE_VMEM = 60 * 1024 * 1024, 8 * 1024 * 1024
WIDTH = 768
HIDDEN = 3072
HEAD = 4608
TOKENS = 512
GATE = 512
F32 = jnp.float32
BF16 = jnp.bfloat16
HBM = pl.BlockSpec(memory_space=pltpu.HBM)
SMEM = pl.BlockSpec(memory_space=pltpu.SMEM)
VMEM = pl.BlockSpec(memory_space=pltpu.VMEM)
QKV_PART, SMALL_PART = (0, 1152), (1152, 128)
UP_PART, OUT_PART, GATE_PART = (0, 1536), (1536, 384), (1920, 256)
DOWN_PART, HEAD_PART = (0, 384), (0, 2048)


def chip_masks(order, lane):
    masks = []
    for place in range(16):
        mask = 0
        for step in range(4):
            if place >> step & 1:
                mask ^= order[step][lane]
        masks.append(mask >> 1)
    return masks


def table_start(group, side):
    return 1 + 32 * list(ORDERS).index(group) + 16 * side


def exchange(array, masks):
    return lax.ppermute(array, AXES, [(d, d ^ masks[d & 1]) for d in range(32)])


def whereabouts():
    device = lax.axis_index("dp") * 8 + lax.axis_index("fsdp")
    core, chip = device % 2, device // 2
    tables = [chip_masks(order, 0) + chip_masks(order, 1) for order in ORDERS.values()]
    swapped = [chip_masks(order, 1) + chip_masks(order, 0) for order in ORDERS.values()]
    places = jnp.where(core == 0, jnp.array(tables, jnp.int32), jnp.array(swapped, jnp.int32))
    places = (places ^ chip).reshape(32 * len(ORDERS))
    return core, jnp.concatenate([core[None].astype(jnp.int32), places])


def after(value, *marks):
    return lax.optimization_barrier((value, marks))[0]


def in_core_order(core, mine, theirs, axis):
    return jnp.where(
        core == 0,
        jnp.concatenate([mine, theirs], axis=axis),
        jnp.concatenate([theirs, mine], axis=axis),
    )


def pack_kernel(core, qkv, out, up, down, head, table, *refs):
    vectors, (up_bias, head_bias), refs = refs[:6], refs[6:8], refs[8:]
    outs, (rows,) = refs[:8], refs[8:]
    rows[...] = jnp.zeros_like(rows)
    for index, vector in enumerate(vectors):
        rows[index : index + 1, :24] = vector[...].astype(F32)
    for index in range(4):
        rows[6 + index : 7 + index, :24] = up_bias[:, 24 * index : 24 * index + 24].astype(F32)
    for index in range(6):
        rows[10 + index : 11 + index, :24] = head_bias[:, 24 * index : 24 * index + 24].astype(F32)
    rows[16:32, :24] = table[...].astype(F32)
    small = rows[...].T[:24].astype(BF16)
    for side in range(2):
        q, u, d, h = outs[4 * side : 4 * side + 4]
        q[:, :1152] = qkv[:, lane_columns(core, side, 1152)]
        q[:, 1152:] = small
        u[:, :1536] = up[:, lane_columns(core, side, 1536)]
        u[:, 1536:1920] = out[:, lane_columns(core, side, 384)]
        u[:, 1920:] = head[:, lane_columns(core, side, 256)]
        d[...] = down[:, lane_columns(core, side, 384)]
        h[...] = head[:, lane_columns(core, side, 2048, GATE)]


def packed(core, weights, table, vectors):
    shapes = [(24, 1280), (24, 2176), (96, 384), (24, 2048)] * 2
    return call(
        pack_kernel,
        (core.reshape(1), *weights, table, *[vector[None] for vector in vectors]),
        [SMEM] + [VMEM] * 14,
        [(shape, BF16, False) for shape in shapes],
        [pltpu.VMEM((128, 128), F32)],
    )


def doubled(held, masks):
    return jnp.concatenate([held, exchange(held, masks)], axis=0)


def both_lanes(*arrays):
    return arrays + tuple(exchange(array, SIBLING) for array in arrays)


def total(first, second):
    return first.astype(F32) + second.astype(F32)


def folded(keep, got, start=0):
    half = got.shape[0] // 2
    send = total(keep[half:], got[half:]).astype(BF16)
    return total(keep[:half], got[:half]).astype(BF16), send


def finished(keep, got, core, widths):
    block = total(keep, got)[0]
    rows = block.shape[0] // 2
    upper, lower = block[:rows], block[rows:]
    mine = jnp.where(core == 0, upper, lower)
    theirs = jnp.where(core == 0, lower, upper).astype(BF16)
    other = exchange(theirs, SIBLING).astype(F32)
    pieces, start = [], 0
    for width in widths:
        span = slice(start, start + width)
        pieces.append(in_core_order(core, mine[:, span], other[:, span], 1))
        start += width
    return pieces


def across(first, second):
    return lax.dot_general(first, second, (((1,), (1,)), ((), ())), preferred_element_type=F32)


def times(first, second):
    return jnp.dot(first, second, preferred_element_type=F32)


def lane_columns(where, side, stride, first=0, width=None):
    return pl.ds(pl.multiple_of(first + (where[0] ^ side) * stride, 128), width or stride)


def block_copies(where, group, sources, part, target, sems, side, first=0):
    start, width = part
    rows = sources[0].shape[1]
    half = len(sources) // 2
    count = 16 // half
    copies = []
    for place in range(16):
        row = pl.multiple_of(where[table_start(group, side) + place] * rows, rows)
        copies.append(
            pltpu.make_async_copy(
                sources[half * side + place // count].at[place % count, :, pl.ds(start, width)],
                target.at[pl.ds(row, rows), lane_columns(where, side, width, first)],
                sems.at[side, place],
            )
        )
    return copies


def term_copies(where, group, lane, out, sems, side):
    rows = out.shape[1]
    copies = []
    for place in range(16):
        row = pl.multiple_of(where[table_start(group, side) + place] * rows, rows)
        copies.append(
            pltpu.make_async_copy(lane.at[side, pl.ds(row, rows), :], out.at[place], sems.at[side, place])
        )
    return copies


def start_all(copies):
    for copy in copies:
        copy.start()


def wait_all(copies):
    for copy in copies:
        copy.wait()


def mean_and_scale(hidden):
    average = jnp.mean(hidden, axis=1, keepdims=True)
    centered = hidden - average
    variance = jnp.mean(centered * centered, axis=1, keepdims=True)
    return centered, lax.rsqrt(variance + norm_epsilon)


def norm_backward(hidden, gain, upstream):
    centered, scale = mean_and_scale(hidden)
    normed = centered * scale
    gain_grad = jnp.sum(upstream * normed, axis=0, keepdims=True)
    shift_grad = jnp.sum(upstream, axis=0, keepdims=True)
    scaled = upstream * gain
    first = jnp.mean(scaled, axis=1, keepdims=True)
    second = jnp.mean(scaled * normed, axis=1, keepdims=True)
    return scale * (scaled - first - normed * second), gain_grad, shift_grad


def call(kernel, operands, in_specs, outs, scratch, spare=None):
    def size(item):
        return math.prod(item.shape) * jnp.dtype(item.dtype).itemsize

    held = [item for item, spec in zip(operands, in_specs) if spec is VMEM]
    held += [jax.ShapeDtypeStruct(shape, kind) for shape, kind, copied in outs if not copied]
    held += [item for item in scratch if getattr(item, "memory_space", None) == pltpu.VMEM]
    limit = MOST_VMEM if spare is None else sum(size(item) for item in held) + spare
    return pl.pallas_call(
        kernel,
        out_shape=[jax.ShapeDtypeStruct(shape, kind) for shape, kind, _ in outs],
        in_specs=in_specs,
        out_specs=[HBM if copied else VMEM for _, _, copied in outs],
        scratch_shapes=scratch,
        compiler_params=pltpu.CompilerParams(vmem_limit_bytes=limit),
        cost_estimate=pl.CostEstimate(flops=2 * 10**12, bytes_accessed=10**10, transcendentals=0),
    )(*operands)


def lane_scratch(rows, width):
    return [pltpu.VMEM((2, rows, width), BF16), pltpu.SemaphoreType.DMA((2, 16))]


def weight_scratch(rows, width):
    return [pltpu.VMEM((rows, width), BF16), pltpu.SemaphoreType.DMA((2, 16))]


def taken(refs, *counts):
    groups = []
    for count in counts:
        groups.append(refs[:count])
        refs = refs[count:]
    return *groups, refs


def front_kernel(where, lead, patches, *refs):
    sources, outs, scratch = taken(refs, 4, 3)
    turned_out, qkv_out, small = outs
    weight, sems, smalls, small_sems, state, rows, turned, qkv, io_sems = scratch
    loads = [block_copies(where, "q", sources, QKV_PART, weight, sems, side) for side in range(2)]
    small_loads = []
    for place in range(16):
        row = pl.multiple_of(where[table_start("q", 0) + place] * 48, 48)
        small_loads.append(
            pltpu.make_async_copy(
                sources[place // 8].at[place % 8, :, pl.ds(*SMALL_PART)],
                smalls.at[pl.ds(row, 48), :],
                small_sems.at[place],
            )
        )
    state_load = pltpu.make_async_copy(patches, state, io_sems.at[0])
    start_all(small_loads)
    state_load.start()
    start_all(loads[0])
    start_all(loads[1])
    wait_all(small_loads)
    columns = smalls[...].astype(F32).T
    places = lax.broadcasted_iota(jnp.int32, (LEADS, WIDTH), 0)
    lead_row = jnp.sum(
        jnp.where(places == lead[0], columns[16 : 16 + LEADS], 0.0), axis=0, keepdims=True
    )
    small[...] = columns[:32]
    small[16:17, :] = lead_row
    state_load.wait()
    centered, scale = mean_and_scale(state[...].astype(F32) + lead_row)
    rows[...] = (centered * scale * columns[0:1] + columns[1:2]).astype(BF16)
    turned[...] = rows[...].T
    stores = [pltpu.make_async_copy(turned, turned_out, io_sems.at[1])]
    stores[0].start()
    wait_all(loads[0] + loads[1])
    for part in range(3):
        span = slice(part * WIDTH, part * WIDTH + WIDTH)
        qkv[:, span] = times(rows[...], weight[:, span]).astype(BF16)
        stores.append(pltpu.make_async_copy(qkv.at[:, span], qkv_out.at[:, span], io_sems.at[2 + part]))
        stores[-1].start()
    wait_all(stores)


def front_forward(where, lead_index, patches, arrays):
    return call(
        front_kernel,
        (where, lead_index, patches, *arrays),
        [SMEM, SMEM, HBM] + [HBM] * 4,
        [
            ((WIDTH, TOKENS), BF16, True),
            ((TOKENS, 3 * WIDTH), BF16, True),
            ((32, WIDTH), F32, False),
        ],
        weight_scratch(WIDTH, 3 * WIDTH)
        + [pltpu.VMEM((WIDTH, 128), BF16), pltpu.SemaphoreType.DMA((16,))]
        + [
            pltpu.VMEM((TOKENS, WIDTH), BF16),
            pltpu.VMEM((TOKENS, WIDTH), BF16),
            pltpu.VMEM((WIDTH, TOKENS), BF16),
            pltpu.VMEM((TOKENS, 3 * WIDTH), BF16),
            pltpu.SemaphoreType.DMA((5,)),
        ],
    )


KEY_SPANS = ((0, 256), (0, 384), (128, 512), (256, 512))


def fill_bias(lengths, pad, bias):
    ends, end = [], 0
    for index in range(lengths.shape[1]):
        end = end + lengths[0, index]
        ends.append(end)

    def windows(places):
        return sum([(places >= end).astype(jnp.int32) for end in ends])

    for block, (low, high) in enumerate(KEY_SPANS):
        count = high - low
        queries = lax.broadcasted_iota(jnp.int32, (1, 128), 1) + 128 * block
        keys = lax.broadcasted_iota(jnp.int32, (count, 1), 0) + low
        same = windows(queries) == windows(keys)
        usable = (pad[low:high, :] > 0) | (queries == keys)
        bias[block, :count, :] = jnp.where(same & usable, 0.0, -1e30)


def two_heads(block):
    first = lax.broadcasted_iota(jnp.int32, block.shape, 1) < block.shape[1] // 2
    zero = jnp.zeros_like(block)
    return jnp.concatenate([jnp.where(first, block, zero), jnp.where(first, zero, block)], axis=0)


def head_rows_of(stacked):
    return jnp.concatenate([stacked[:64, :128], stacked[64:, 128:]], axis=0)


def probabilities(scores, allowed):
    masked = scores * score_scale + allowed
    raised = jnp.exp(masked - jnp.max(masked, axis=0, keepdims=True))
    return raised * (1.0 / jnp.sum(raised, axis=0, keepdims=True))


def attention_kernel(where, lengths, pad, qkv, attended_out, turned_out, bias, turned, rows, sems):
    fill_bias(lengths, pad, bias)

    def pair(index, carry):
        first = index * 128
        columns = pl.ds(pl.multiple_of(first, 128), 128)
        keys_at = pl.ds(pl.multiple_of(first + WIDTH, 128), 128)
        values = qkv[:, pl.ds(pl.multiple_of(first + 2 * WIDTH, 128), 128)].T
        for block, (low, high) in enumerate(KEY_SPANS):
            span = slice(128 * block, 128 * block + 128)
            scores = across(qkv[low:high, keys_at], two_heads(qkv[span, columns]))
            allowed = bias[block, : high - low, :]
            probs = [
                probabilities(scores[:, 128 * head : 128 * head + 128], allowed).astype(BF16)
                for head in range(2)
            ]
            mixed = times(values[:, low:high], jnp.concatenate(probs, axis=1))
            turned[columns, span] = head_rows_of(mixed).astype(BF16)
        return carry

    lax.fori_loop(0, WIDTH // 128, pair, 0)
    stores = [pltpu.make_async_copy(turned, turned_out, sems.at[0])]
    stores[0].start()
    rows[...] = turned[...].T
    stores.append(pltpu.make_async_copy(rows, attended_out, sems.at[1]))
    stores[1].start()
    wait_all(stores)


def attention_forward(where, lengths, pad, qkv):
    rows, columns = (TOKENS, WIDTH), (WIDTH, TOKENS)
    return call(
        attention_kernel,
        (where, lengths, pad, qkv),
        [SMEM, SMEM, VMEM, VMEM],
        [(rows, BF16, True), (columns, BF16, True)],
        [
            pltpu.VMEM((4, 384, 128), F32),
            pltpu.VMEM(columns, BF16),
            pltpu.VMEM(rows, BF16),
            pltpu.SemaphoreType.DMA((2,)),
        ],
    )


def gate_shares(logits, cotangent, shares, gate_grad):
    gate_grad[:, 256:] = cotangent[:, 256:GATE]
    first, rest = logits[:, :128], logits[:, 128:256]
    left = lax.broadcasted_iota(jnp.int32, first.shape, 1) < PIX
    third = jnp.where(left, rest, pltpu.roll(rest, PIX, 1))
    largest = jnp.maximum(jnp.maximum(first, pltpu.roll(first, PIX, 1)), third)
    raised, raised_third = jnp.exp(first - largest), jnp.exp(third - largest)
    scale = 1.0 / (raised + pltpu.roll(raised, PIX, 1) + raised_third)
    share, share_third = raised * scale, raised_third * scale
    shares[:, :128] = share
    shares[:, 128:256] = jnp.where(left, share_third, rest)
    pull, other = cotangent[:, :128].astype(F32), cotangent[:, 128:256].astype(F32)
    pull_third = jnp.where(left, other, pltpu.roll(other, PIX, 1))
    weighed = share * pull
    inner = weighed + pltpu.roll(weighed, PIX, 1) + share_third * pull_third
    gate_grad[:, :128] = (share * (pull - inner)).astype(BF16)
    gate_grad[:, 128:256] = jnp.where(left, share_third * (pull_third - inner), other).astype(BF16)


def head_kernel(where, rows, gate_out, bias, *refs):
    sources, outs, scratch = taken(refs, 4, 1)
    (out,) = outs
    weight, sems, inputs, result, io_sems = scratch
    loads = [block_copies(where, "h", sources, HEAD_PART, weight, sems, side) for side in range(2)]
    row_load = pltpu.make_async_copy(rows, inputs, io_sems.at[0])
    gate_load = pltpu.make_async_copy(gate_out, result.at[:, :GATE], io_sems.at[1])
    row_load.start()
    start_all(loads[0])
    start_all(loads[1])
    gate_load.start()
    row_load.wait()
    stores = []

    def store(span):
        stores.append(
            pltpu.make_async_copy(result.at[:, span], out.at[:, span], io_sems.at[2 + len(stores)])
        )
        stores[-1].start()

    for side in range(2):
        wait_all(loads[side])
        for tile in range(4):
            span = lane_columns(where, side, 2048, GATE + tile * 512, 512)
            columns = lane_columns(where, side, 2048, tile * 512, 512)
            result[:, span] = times(inputs[...], weight[:, columns]) + bias[:, span]
            store(span)
    gate_load.wait()
    store(pl.ds(0, GATE))
    wait_all(stores)


def head_forward(where, rows, gate_out, bias, arrays):
    return call(
        head_kernel,
        (where, rows, gate_out, bias, *arrays),
        [SMEM, HBM, HBM, VMEM] + [HBM] * 4,
        [((TOKENS, HEAD), F32, True)],
        weight_scratch(WIDTH, HEAD - GATE)
        + [
            pltpu.VMEM((TOKENS, WIDTH), BF16),
            pltpu.VMEM((TOKENS, HEAD), F32),
            pltpu.SemaphoreType.DMA((11,)),
        ],
        spare=SPARE_VMEM,
    )[0]


def send_lane(where, group, lane, out, sems, side):
    rows = out.shape[1]
    copies = []
    for place in range(16):
        row = pl.multiple_of(where[table_start(group, side) + place] * rows, rows)
        copies.append(
            pltpu.make_async_copy(lane.at[pl.ds(row, rows), :], out.at[place], sems.at[place])
        )
    start_all(copies)
    return copies


def middle_kernel(where, small, up_bias, head_bias, attended, patches, cotangent, act_cotangent, *refs):
    up_sources, down_sources, head_sources, outs, scratch = taken(refs, 4, 4, 4, 14)
    outputs, shares, gate_bias, down_bias, up_bias_sum, terms, mid_grad, out_grad, *grads = outs
    down_mine, down_theirs, up_mine, up_theirs, head_mine, head_theirs = grads
    out_weight, out_sems, up, up_sems, down, down_sems, scratch = *scratch[:6], scratch[6:]
    head, head_sems, gate_sems, rows, branch, mid, mlp_turned, scratch = *scratch[:7], scratch[7:]
    act, act_turned, slope, turned, pulls, act_pulls, gate_grad, scratch = *scratch[:7], scratch[7:]
    lane, lane_sems, down_lane, down_lane_sems, io_sems = scratch

    def loads(group, sources, part, target, sems, first=0):
        copies = []
        for side in range(2):
            copies += block_copies(where, group, sources, part, target, sems, side, first)
        return copies

    state_loads = [
        pltpu.make_async_copy(attended, rows, io_sems.at[0]),
        pltpu.make_async_copy(patches, branch, io_sems.at[1]),
    ]
    out_loads = loads("u", up_sources, OUT_PART, out_weight, out_sems)
    up_loads = loads("u", up_sources, UP_PART, up, up_sems)
    down_loads = loads("d", down_sources, DOWN_PART, down, down_sems)
    gate_loads = loads("u", up_sources, GATE_PART, head, gate_sems)
    head_loads = loads("h", head_sources, HEAD_PART, head, head_sems, GATE)
    pull_load = pltpu.make_async_copy(cotangent, pulls, io_sems.at[2])
    act_load = pltpu.make_async_copy(act_cotangent, act_pulls, io_sems.at[3])
    start_all(state_loads + out_loads + up_loads + down_loads + gate_loads)
    pull_load.start()
    start_all(head_loads)
    act_load.start()

    wait_all(state_loads + out_loads)
    mid[...] = (
        branch[...].astype(F32)
        + small[16:17, :]
        + times(rows[...], out_weight[...])
        + small[2:3, :]
    )
    centered, scale = mean_and_scale(mid[...])
    rows[...] = (centered * scale * small[3:4, :] + small[4:5, :]).astype(BF16)
    mlp_turned[...] = rows[...].T
    wait_all(up_loads)
    for tile in range(6):
        span = slice(tile * 512, tile * 512 + 512)
        values = times(rows[...], up[:, span]) + up_bias[:, span]
        share = 0.5 * (1.0 + lax.erf(values * 0.7071067811865476))
        density = jnp.exp(-0.5 * values * values) * 0.3989422804014327
        activated = (values * share).astype(BF16)
        act[:, span] = activated
        act_turned[span, :] = activated.T
        slope[:, span] = (share + values * density).astype(BF16)
    wait_all(down_loads)
    outputs[...] = (mid[...] + times(act[...], down[...]) + small[5:6, :]).astype(BF16)
    turned[...] = outputs[...].T
    wait_all(gate_loads)
    shares[...] = times(outputs[...], head[:, :GATE]) + head_bias[:, :GATE]
    pull_load.wait()
    gate_shares(shares, pulls, shares, gate_grad)
    gate_bias[...] = jnp.sum(gate_grad[...].astype(F32), axis=0, keepdims=True)
    pulls[:, :GATE] = gate_grad[...]

    def head_lane(side, out):
        lane[:, :256] = times(turned[...], pulls[:, lane_columns(where, side, 256)]).astype(BF16)
        for tile in range(4):
            span = lane_columns(where, side, 2048, GATE + tile * 512, 512)
            lane[:, 256 + tile * 512 : 768 + tile * 512] = times(turned[...], pulls[:, span]).astype(
                BF16
            )
        return send_lane(where, "head", lane, out, lane_sems, side)

    def down_lane_of(side, out):
        columns = branch[:, lane_columns(where, side, 384)]
        for part in range(4):
            span = slice(part * WIDTH, part * WIDTH + WIDTH)
            down_lane[span, :] = times(act_turned[span, :], columns).astype(BF16)
        return send_lane(where, "down", down_lane, out, down_lane_sems, side)

    def up_lane(side, out):
        for tile in range(3):
            span = lane_columns(where, side, 1536, tile * 512, 512)
            lane[:, tile * 512 : tile * 512 + 512] = times(mlp_turned[...], slope[:, span]).astype(BF16)
        return send_lane(where, "up", lane.at[:, :1536], out, lane_sems, side)

    lane_stores = head_lane(1, head_theirs)
    act_load.wait()
    wait_all(head_loads)
    mid_grad[...] = act_pulls[...].astype(F32) + across(pulls[...], head[...])
    branch[...] = mid_grad[...].astype(BF16)
    down_bias[...] = jnp.sum(branch[...].astype(F32), axis=0, keepdims=True)
    wait_all(lane_stores)
    lane_stores = head_lane(0, head_mine)
    down_stores = down_lane_of(1, down_theirs)
    for tile in range(6):
        span = slice(tile * 512, tile * 512 + 512)
        grad = across(branch[...], down[span, :])
        rounded = (slope[:, span].astype(F32) * grad).astype(BF16)
        slope[:, span] = rounded
        up_bias_sum[:, span] = jnp.sum(rounded.astype(F32), axis=0, keepdims=True)
    wait_all(down_stores)
    down_stores = down_lane_of(0, down_mine)
    wait_all(lane_stores)
    lane_stores = up_lane(1, up_theirs)
    grad = across(slope[...], up[...])
    pulled, gain_grad, shift_grad = norm_backward(mid[...], small[3:4, :], grad)
    pulled = pulled + mid_grad[...]
    rounded = pulled.astype(BF16)
    mid_grad[...] = pulled
    out_grad[...] = rounded
    terms[...] = jnp.zeros_like(terms)
    terms[0:1, :] = jnp.sum(rounded.astype(F32), axis=0, keepdims=True)
    terms[1:2, :] = gain_grad
    terms[2:3, :] = shift_grad
    wait_all(lane_stores)
    lane_stores = up_lane(0, up_mine)
    wait_all(down_stores + lane_stores)


def middle(
    where, small, up_bias, head_bias, attended, patches, cotangent, act_cotangent, up, down, head
):
    rows, columns = (TOKENS, WIDTH), (WIDTH, TOKENS)
    wide, tall = (TOKENS, HIDDEN), (HIDDEN, TOKENS)
    return call(
        middle_kernel,
        (
            where, small, up_bias, head_bias, attended, patches, cotangent, act_cotangent,
            *up, *down, *head,
        ),
        [SMEM, VMEM, VMEM, VMEM] + [HBM] * 16,
        [
            (rows, BF16, False),
            ((TOKENS, GATE), F32, False),
            ((1, GATE), F32, False),
            ((1, WIDTH), F32, False),
            ((1, HIDDEN), F32, False),
            ((8, WIDTH), F32, False),
            (rows, F32, False),
            (rows, BF16, False),
            ((16, 192, 384), BF16, True),
            ((16, 192, 384), BF16, True),
            ((16, 48, 1536), BF16, True),
            ((16, 48, 1536), BF16, True),
            ((16, 48, 2304), BF16, True),
            ((16, 48, 2304), BF16, True),
        ],
        weight_scratch(WIDTH, WIDTH)
        + weight_scratch(WIDTH, HIDDEN)
        + weight_scratch(HIDDEN, WIDTH)
        + weight_scratch(WIDTH, HEAD)
        + [
            pltpu.SemaphoreType.DMA((2, 16)),
            pltpu.VMEM(rows, BF16),
            pltpu.VMEM(rows, BF16),
            pltpu.VMEM(rows, F32),
            pltpu.VMEM(columns, BF16),
            pltpu.VMEM(wide, BF16),
            pltpu.VMEM(tall, BF16),
            pltpu.VMEM(wide, BF16),
            pltpu.VMEM(columns, BF16),
            pltpu.VMEM((TOKENS, HEAD), BF16),
            pltpu.VMEM(rows, BF16),
            pltpu.VMEM((TOKENS, GATE), BF16),
            pltpu.VMEM((WIDTH, 2304), BF16),
            pltpu.SemaphoreType.DMA((16,)),
            pltpu.VMEM((HIDDEN, 384), BF16),
            pltpu.SemaphoreType.DMA((16,)),
            pltpu.SemaphoreType.DMA((4,)),
        ],
    )


def attention_back_kernel(start, count, where, lengths, pad, out_grad, qkv, *refs):
    sources, outs, scratch = taken(refs, 4, 1)
    (qkv_grad,) = outs
    weight, sems, bias, mixed, turned, key_sum, value_sum = scratch
    loads = [block_copies(where, "u", sources, OUT_PART, weight, sems, side) for side in range(2)]
    start_all(loads[0] + loads[1])
    fill_bias(lengths, pad, bias)
    wait_all(loads[0] + loads[1])
    width = 128 * count
    mixed[...] = across(
        out_grad[...], weight[128 * start : 128 * start + width, :]
    ).astype(BF16)

    def columns_at(first):
        return pl.ds(pl.multiple_of(first, 128), 128)

    def pair(index, carry):
        own, first = index * 128, (index + start) * 128
        columns, keys_at = columns_at(first), columns_at(first + WIDTH)
        values_at = columns_at(first + 2 * WIDTH)
        keys_turned = qkv[:, keys_at].T
        key_sum[...] = jnp.zeros_like(key_sum)
        value_sum[...] = jnp.zeros_like(value_sum)
        for block, (low, high) in enumerate(KEY_SPANS):
            span = slice(128 * block, 128 * block + 128)
            queries, grads = two_heads(qkv[span, columns]), two_heads(mixed[span, columns_at(own)])
            scores = across(qkv[low:high, keys_at], queries)
            prob_grads = across(qkv[low:high, values_at], grads)
            allowed = bias[block, : high - low, :]
            probs, score_grads = [], []
            for head in range(2):
                part = slice(128 * head, 128 * head + 128)
                prob = probabilities(scores[:, part], allowed)
                pulled = prob * prob_grads[:, part]
                inner = jnp.sum(pulled, axis=0, keepdims=True)
                probs.append(prob.astype(BF16))
                score_grads.append((pulled - prob * inner).astype(BF16))
            score_grad = jnp.concatenate(score_grads, axis=1)
            key_sum[low:high, :] += times(score_grad, queries)
            value_sum[low:high, :] += times(jnp.concatenate(probs, axis=1), grads)
            turned[:, span] = head_rows_of(times(keys_turned[:, low:high], score_grad)) * score_scale
        qkv_grad[:, columns_at(own)] = turned[...].T.astype(BF16)
        qkv_grad[:, columns_at(own + width)] = (key_sum[...] * score_scale).astype(BF16)
        qkv_grad[:, columns_at(own + 2 * width)] = value_sum[...].astype(BF16)
        return carry

    lax.fori_loop(0, count, pair, 0)


def attention_backward(where, lengths, pad, out_grad, qkv, arrays, start, count):
    return call(
        partial(attention_back_kernel, start, count),
        (where, lengths, pad, out_grad, qkv, *arrays),
        [SMEM, SMEM, VMEM, VMEM, VMEM] + [HBM] * 4,
        [((TOKENS, 3 * 128 * count), BF16, False)],
        weight_scratch(WIDTH, WIDTH)
        + [
            pltpu.VMEM((4, 384, 128), F32),
            pltpu.VMEM((TOKENS, 128 * count), BF16),
            pltpu.VMEM((128, TOKENS), F32),
            pltpu.VMEM((TOKENS, 128), F32),
            pltpu.VMEM((TOKENS, 128), F32),
        ],
        spare=SPARE_VMEM,
    )[0]


def mix_term_kernel(where, qkv_grad, input_turned, attended_turned, out_grad, mine_out, theirs_out, *refs):
    lane, sems = refs
    stores = []
    for side, out in ((1, theirs_out), (0, mine_out)):
        lane[side, :, :768] = times(
            input_turned[...], qkv_grad[:, lane_columns(where, side, 768)]
        ).astype(BF16)
        lane[side, :, 768:1152] = times(
            attended_turned[...], out_grad[:, lane_columns(where, side, 384)]
        ).astype(BF16)
        copies = term_copies(where, "front", lane, out, sems, side)
        start_all(copies)
        stores += copies
    wait_all(stores)


def mix_terms(where, qkv_grad, input_turned, attended_turned, out_grad):
    return call(
        mix_term_kernel,
        (where, qkv_grad, input_turned, attended_turned, out_grad),
        [SMEM] + [VMEM] * 4,
        [((16, 48, 1152), BF16, True)] * 2,
        lane_scratch(WIDTH, 1152),
        spare=SPARE_VMEM,
    )


def front_back_kernel(
    where, lead, small, terms, down_row, up_rows, head_rows,
    first_grad, second_grad, patches, mid_grad, input_turned, *refs
):
    sources, outs, scratch = taken(refs, 4, 3)
    patch_out, mine_out, theirs_out = outs
    weight, sems, lane, lane_sems, scratch = *scratch[:4], scratch[4:]
    pulls, late_pulls, state, mids, inputs, patch_grad, small_grad, io_sems = scratch
    loads = [block_copies(where, "q", sources, QKV_PART, weight, sems, side) for side in range(2)]
    pairs = [(patches, state), (mid_grad, mids), (input_turned, inputs), (second_grad, late_pulls)]
    for part in range(3):
        for source, start, size in ((first_grad, 0, 512), (second_grad, 512, 256)):
            columns = pl.ds(WIDTH * part + start, size)
            pairs.append((source.at[:, pl.ds(size * part, size)], pulls.at[:, columns]))
    in_loads = [pltpu.make_async_copy(*pair, io_sems.at[at]) for at, pair in enumerate(pairs)]
    start_all(in_loads[4:])
    start_all(loads[0] + loads[1])
    start_all(in_loads[:4])
    wait_all(in_loads[4:])
    wait_all(loads[0] + loads[1])
    grad = across(pulls[...], weight[...])
    wait_all(in_loads[:4])
    pulled, gain_grad, shift_grad = norm_backward(
        state[...].astype(F32) + small[16:17, :], small[0:1, :], grad
    )
    pulled = pulled + mids[...]
    patch_grad[...] = pulled
    stores = [pltpu.make_async_copy(patch_grad, patch_out, io_sems.at[10])]
    stores[0].start()
    small_grad[0:1, :] = gain_grad
    small_grad[1:2, :] = shift_grad
    small_grad[2:5, :] = terms[0:3, :]
    small_grad[5:6, :] = down_row[...]
    small_grad[6:10, :] = up_rows[...]
    small_grad[10:16, :] = head_rows[...]
    places = lax.broadcasted_iota(jnp.int32, (LEADS, WIDTH), 0)
    lead_grad = jnp.sum(pulled, axis=0, keepdims=True)
    small_grad[16:32, :] = jnp.where(places == lead[0], lead_grad, 0.0)
    for side, out in ((1, theirs_out), (0, mine_out)):
        lane[side, :, :384] = times(
            inputs[...], late_pulls[:, lane_columns(where, side, 384)]
        ).astype(BF16)
        rows = small_grad[pl.ds(pl.multiple_of((where[0] ^ side) * 16, 16), 16), :]
        rows = jnp.concatenate([rows, jnp.zeros((112, WIDTH), F32)], axis=0)
        lane[side, :, 384:] = rows.T.astype(BF16)
        copies = term_copies(where, "front", lane, out, lane_sems, side)
        start_all(copies)
        stores += copies
    wait_all(stores)


def front_backward(
    where, lead, small, terms, down_row, up_rows, head_rows,
    first_grad, second_grad, patches, mid_grad, input_turned, arrays,
):
    rows, columns = (TOKENS, WIDTH), (WIDTH, TOKENS)
    return call(
        front_back_kernel,
        (
            where, lead, small, terms, down_row, up_rows, head_rows,
            first_grad, second_grad, patches, mid_grad, input_turned, *arrays,
        ),
        [SMEM, SMEM] + [VMEM] * 5 + [HBM] * 9,
        [(rows, F32, True), ((16, 48, 512), BF16, True), ((16, 48, 512), BF16, True)],
        weight_scratch(WIDTH, 3 * WIDTH)
        + lane_scratch(WIDTH, 512)
        + [
            pltpu.VMEM((TOKENS, 3 * WIDTH), BF16),
            pltpu.VMEM(rows, BF16),
            pltpu.VMEM(rows, BF16),
            pltpu.VMEM(rows, F32),
            pltpu.VMEM(columns, BF16),
            pltpu.VMEM(rows, F32),
            pltpu.VMEM((32, WIDTH), F32),
            pltpu.SemaphoreType.DMA((11,)),
        ],
        spare=SPARE_VMEM,
    )


def rows_of(vector, count):
    return vector.reshape(32, count, 24).transpose(1, 0, 2).reshape(count, WIDTH)


def vector_of(rows):
    count = rows.shape[0]
    return rows.reshape(count, 32, 24).transpose(1, 0, 2).reshape(1, count * WIDTH)


def shards(
    patches,
    lead_index,
    window_lengths,
    pad_mask,
    lead_table,
    attn_gain,
    attn_shift,
    qkv_weight,
    out_weight,
    out_bias,
    mlp_gain,
    mlp_shift,
    up_weight,
    up_bias,
    down_weight,
    down_bias,
    head_weight,
    head_bias,
    act_cotangent,
    head_cotangent,
):
    core, where = whereabouts()
    weights = (qkv_weight, out_weight, up_weight, down_weight, head_weight)
    vectors = (
        attn_gain, attn_shift, out_bias, mlp_gain, mlp_shift, down_bias, up_bias, head_bias
    )
    parts = packed(core, weights, lead_table, vectors)
    pad = pad_mask[:, None]
    cotangent_sum = jnp.sum(head_cotangent[:, GATE:].astype(F32), axis=0, keepdims=True)

    orders = ORDERS
    parts = dict(zip("qudh", zip(parts[:4], parts[4:])))
    chunks = {
        name: in_core_order(core, mine, exchange(theirs, SIBLING), 0)[None]
        for name, (mine, theirs) in parts.items()
    }

    held, last = dict(chunks), ()
    for name, step in GATHER_SEQUENCE:
        held[name] = after(held[name], *last)
        last = (held[name],)
        held[name] = doubled(held[name], orders[name][step])
    q, u, d, h = [held[name] for name in ("q", "u", "d", "h")]
    q_rest = exchange(after(q, *last), orders["q"][3])
    u = after(u, q)
    u_rest = exchange(u, orders["u"][3])
    d_rest = exchange(d, orders["d"][3])
    h = doubled(after(h, u), orders["h"][2])
    first = both_lanes(q, q_rest)
    h_rest = exchange(h, orders["h"][3])
    input_turned, qkv, small_rows = front_forward(
        after(where, d, h, cotangent_sum), lead_index, patches, first
    )
    attended, attended_turned = attention_forward(where, window_lengths, pad, qkv)
    u_rest, d_rest, h_rest = lax.optimization_barrier((u_rest, d_rest, h_rest, attended))[:3]
    second, down, head = both_lanes(u, u_rest), both_lanes(d, d_rest), both_lanes(h, h_rest)
    up_bias_row, head_bias_row = vector_of(small_rows[6:10]), vector_of(small_rows[10:16])
    (
        outputs, gate_out, gate_bias_sum, down_bias_sum, up_bias_sum, terms, mid_grad, out_grad,
        mine_d, theirs_d, mine_u, theirs_u, mine_h, theirs_h,
    ) = middle(
        where, small_rows, up_bias_row, head_bias_row, attended, patches, head_cotangent,
        act_cotangent, second, down, head,
    )

    got_h, got_d, got_u = [exchange(theirs, SIBLING) for theirs in (theirs_h, theirs_d, theirs_u)]
    head_rows = rows_of(jnp.concatenate([gate_bias_sum, cotangent_sum], axis=1), 6)
    up_rows = rows_of(up_bias_sum, 4)
    pulled = (window_lengths, pad, out_grad, qkv, second)
    first_grad = attention_backward(where, *pulled, 0, 4)
    keep_h, send_h = folded(mine_h, after(got_h, first_grad))
    got_h = exchange(send_h, orders["head"][3])
    keep_u, send_u = folded(mine_u, after(got_u, first_grad))
    got_u = exchange(send_u, orders["up"][3])
    keep_d, send_d = folded(mine_d, after(got_d, first_grad))
    got_d = exchange(send_d, orders["down"][3])
    mine_m, theirs_m = mix_terms(
        after(where, send_h, send_d, send_u), first_grad, input_turned, attended_turned, out_grad
    )
    got_m = exchange(theirs_m, SIBLING)
    second_grad = attention_backward(after(where, theirs_m), *pulled, 4, 2)
    keep_m, send_m = folded(mine_m, after(got_m, second_grad))
    got_m = exchange(send_m, orders["front"][3])
    keep_h, send_h = folded(keep_h, after(got_h, second_grad))
    got_h = exchange(send_h, orders["head"][2])
    patch_grad, mine_f, theirs_f = front_backward(
        after(where, send_m, send_h), lead_index, small_rows, terms, down_bias_sum,
        up_rows, head_rows, first_grad, second_grad, patches, mid_grad, input_turned, first,
    )
    got_f = exchange(theirs_f, SIBLING)
    keep_d, send_d = folded(keep_d, after(got_d, patch_grad))
    got_d = exchange(send_d, orders["down"][2])
    keep_u, send_u = folded(keep_u, after(got_u, patch_grad))
    got_u = exchange(send_u, orders["up"][2])
    keep_f, send_f = folded(mine_f, after(got_f, send_d, send_u))
    got_f = exchange(send_f, orders["front"][3])
    keep_h, send_h = folded(keep_h, after(got_h, send_f))
    got_h = exchange(send_h, orders["head"][1])
    keep_m, send_m = folded(keep_m, after(got_m, send_f))
    got_m = exchange(send_m, orders["front"][2])
    head_out = head_forward(after(where, send_h, send_m), outputs, gate_out, head_bias_row, head)
    keep_d, send_d = folded(keep_d, after(got_d, head_out))
    got_d = exchange(send_d, orders["down"][1])
    keep_u, send_u = folded(keep_u, after(got_u, head_out))
    got_u = exchange(send_u, orders["up"][1])
    keep_f, send_f = folded(keep_f, after(got_f, head_out))
    got_f = exchange(send_f, orders["front"][2])
    keep_h, send_h = folded(keep_h, after(got_h, send_f))
    got_h = exchange(send_h, orders["head"][0])
    keep_m, send_m = folded(keep_m, after(got_m, send_f))
    got_m = exchange(send_m, orders["front"][1])
    keep_d, send_d = folded(keep_d, after(got_d, send_f))
    got_d = exchange(send_d, orders["down"][0])
    keep_u, send_u = folded(keep_u, after(got_u, send_f))
    got_u = exchange(send_u, orders["up"][0])
    keep_f, send_f = folded(keep_f, after(got_f, send_m, send_d, send_u, send_h))
    got_f = exchange(send_f, orders["front"][1])
    keep_m, send_m = folded(keep_m, after(got_m, send_f))
    got_m = exchange(send_m, orders["front"][0])
    gate_sum, rest_sum = finished(keep_h, after(got_h, send_f), core, (256, 2048))
    keep_f, send_f = folded(keep_f, after(got_f, send_m))
    got_f = exchange(send_f, orders["front"][0])
    early_sum, out_sum = finished(keep_m, after(got_m, send_f), core, (768, 384))
    (down_sum,) = finished(keep_d, after(got_d, send_f), core, (384,))
    (up_sum,) = finished(keep_u, after(got_u, send_f), core, (1536,))
    late_sum, small_sum = finished(keep_f, got_f, core, (384, 128))
    qkv_sum = jnp.concatenate(
        [
            piece[:, part * piece.shape[1] // 3 : (part + 1) * piece.shape[1] // 3]
            for part in range(3)
            for piece in (early_sum, late_sum)
        ],
        axis=1,
    )
    small_sum = small_sum.T
    return (
        outputs,
        head_out,
        patch_grad,
        small_sum[128:144],
        small_sum[0],
        small_sum[1],
        qkv_sum,
        out_sum,
        small_sum[2],
        small_sum[3],
        small_sum[4],
        up_sum,
        small_sum[6:10].reshape(96),
        down_sum,
        small_sum[5],
        jnp.concatenate([gate_sum, rest_sum], axis=1),
        small_sum[10:16].reshape(144),
    )


def plain_shards(
    patches,
    lead_index,
    window_lengths,
    pad_mask,
    lead_table,
    attn_gain,
    attn_shift,
    qkv_weight,
    out_weight,
    out_bias,
    mlp_gain,
    mlp_shift,
    up_weight,
    up_bias,
    down_weight,
    down_bias,
    head_weight,
    head_bias,
    act_cotangent,
    head_cotangent,
):
    front = (
        lax.all_gather(lead_table, ("dp", "fsdp"), axis=1, tiled=True),
        lax.all_gather(attn_gain, ("dp", "fsdp"), axis=0, tiled=True),
        lax.all_gather(attn_shift, ("dp", "fsdp"), axis=0, tiled=True),
        lax.all_gather(qkv_weight, ("dp", "fsdp"), axis=0, tiled=True),
        lax.all_gather(out_weight, ("dp", "fsdp"), axis=0, tiled=True),
        lax.all_gather(out_bias, ("dp", "fsdp"), axis=0, tiled=True),
    )
    rear = (
        lax.all_gather(mlp_gain, ("dp", "fsdp"), axis=0, tiled=True),
        lax.all_gather(mlp_shift, ("dp", "fsdp"), axis=0, tiled=True),
        lax.all_gather(up_weight, ("dp", "fsdp"), axis=0, tiled=True),
        lax.all_gather(up_bias, ("dp", "fsdp"), axis=0, tiled=True),
        lax.all_gather(down_weight, ("dp", "fsdp"), axis=0, tiled=True),
        lax.all_gather(down_bias, ("dp", "fsdp"), axis=0, tiled=True),
        lax.all_gather(head_weight, ("dp", "fsdp"), axis=0, tiled=True),
        lax.all_gather(head_bias, ("dp", "fsdp"), axis=0, tiled=True),
    )
    table_full, gain_one, shift_one, qkv_full, out_full, out_bias_full = front
    (
        gain_two,
        shift_two,
        up_full,
        up_bias_full,
        down_full,
        down_bias_full,
        head_full,
        head_bias_full,
    ) = rear
    token_rows, width = patches.shape
    head_dim = width // HEADS
    block_rows = min(512, token_rows)
    block_count = token_rows // block_rows
    ends = jnp.cumsum(window_lengths[0])
    positions = jnp.arange(token_rows, dtype=jnp.int32)
    window = jnp.sum((positions[:, None] >= ends[None, :]).astype(jnp.int32), axis=1)
    lead_hot = (jnp.arange(LEADS, dtype=jnp.int32) == lead_index[0]).astype(jnp.float32)
    lead_row = jnp.sum(lead_hot[:, None] * table_full.astype(jnp.float32), axis=0)
    start_state = patches.astype(jnp.float32) + lead_row[None, :]
    normed_one, pull_one = jax.vjp(
        layer_norm, start_state, gain_one.astype(jnp.float32), shift_one.astype(jnp.float32)
    )
    attn_input = normed_one.astype(jnp.bfloat16)
    qkv_rows = jnp.dot(attn_input, qkv_full, preferred_element_type=jnp.float32).astype(
        jnp.bfloat16
    )
    queries = qkv_rows[:, :width].reshape(block_count, block_rows, HEADS, head_dim)
    keys = qkv_rows[:, width : 2 * width].reshape(token_rows, HEADS, head_dim)
    values = qkv_rows[:, 2 * width :].reshape(token_rows, HEADS, head_dim)
    query_windows = window.reshape(block_count, block_rows)
    block_starts = jnp.arange(block_count, dtype=jnp.int32) * block_rows

    def block_scores(query_block, window_block, block_start):
        scores = (
            jnp.einsum("qhd,khd->hqk", query_block, keys, preferred_element_type=jnp.float32)
            * score_scale
        )
        allowed = allowed_keys(window_block, window, pad_mask, block_start)
        return jnp.where(allowed[None], scores, -1e30)

    def forward_block(inputs):
        query_block, window_block, block_start = inputs
        masked = block_scores(query_block, window_block, block_start)
        largest = jnp.max(masked, axis=-1, keepdims=True)
        raised = jnp.exp(masked - largest)
        total = jnp.sum(raised, axis=-1, keepdims=True)
        probs = (raised / total).astype(jnp.bfloat16)
        mixed = jnp.einsum("hqk,khd->qhd", probs, values, preferred_element_type=jnp.float32)
        return (
            mixed.reshape(block_rows, width).astype(jnp.bfloat16),
            (largest + jnp.log(total))[:, :, 0],
        )

    mixed_blocks, log_totals = lax.map(forward_block, (queries, query_windows, block_starts))
    attended = mixed_blocks.reshape(token_rows, width)
    mid_state = (
        start_state
        + jnp.dot(attended, out_full, preferred_element_type=jnp.float32)
        + out_bias_full.astype(jnp.float32)
    )
    normed_two, pull_two = jax.vjp(
        layer_norm, mid_state, gain_two.astype(jnp.float32), shift_two.astype(jnp.float32)
    )
    mlp_input = normed_two.astype(jnp.bfloat16)
    pre_act = jnp.dot(mlp_input, up_full, preferred_element_type=jnp.float32) + up_bias_full.astype(
        jnp.float32
    )
    activated, pull_act = jax.vjp(gelu_exact, pre_act)
    act_rows = activated.astype(jnp.bfloat16)
    end_state = (
        mid_state
        + jnp.dot(act_rows, down_full, preferred_element_type=jnp.float32)
        + down_bias_full.astype(jnp.float32)
    )
    outputs = end_state.astype(jnp.bfloat16)
    logits = jnp.dot(
        outputs, head_full, preferred_element_type=jnp.float32
    ) + head_bias_full.astype(jnp.float32)
    head_out, pull_head = jax.vjp(partial(expert_softmax, experts=EXPERTS, pixels=PIX), logits)
    up_back, down_back, head_back = (
        lax.all_gather(up_weight, ("dp", "fsdp"), axis=0, tiled=True),
        lax.all_gather(down_weight, ("dp", "fsdp"), axis=0, tiled=True),
        lax.all_gather(head_weight, ("dp", "fsdp"), axis=0, tiled=True),
    )
    qkv_back, out_back = (
        lax.all_gather(qkv_weight, ("dp", "fsdp"), axis=0, tiled=True),
        lax.all_gather(out_weight, ("dp", "fsdp"), axis=0, tiled=True),
    )
    logit_grad = pull_head(head_cotangent.astype(jnp.float32))[0].astype(jnp.bfloat16)
    head_bias_term = jnp.sum(logit_grad.astype(jnp.float32), axis=0)
    head_term = jnp.einsum("td,tn->dn", outputs, logit_grad, preferred_element_type=jnp.float32)
    end_grad = act_cotangent.astype(jnp.float32) + jnp.einsum(
        "tn,dn->td", logit_grad, head_back, preferred_element_type=jnp.float32
    )
    branch_grad = end_grad.astype(jnp.bfloat16)
    down_bias_term = jnp.sum(branch_grad.astype(jnp.float32), axis=0)
    down_term = jnp.einsum("tf,td->fd", act_rows, branch_grad, preferred_element_type=jnp.float32)
    act_grad = jnp.einsum("td,fd->tf", branch_grad, down_back, preferred_element_type=jnp.float32)
    pre_grad = pull_act(act_grad)[0].astype(jnp.bfloat16)
    up_bias_term = jnp.sum(pre_grad.astype(jnp.float32), axis=0)
    up_term = jnp.einsum("td,tf->df", mlp_input, pre_grad, preferred_element_type=jnp.float32)
    normed_two_grad = jnp.einsum("tf,df->td", pre_grad, up_back, preferred_element_type=jnp.float32)
    state_grad_two, gain_two_term, shift_two_term = pull_two(normed_two_grad)
    (
        gain_part,
        shift_part,
        up_part,
        up_bias_part,
        down_part,
        down_bias_part,
        head_part,
        head_bias_part,
    ) = (
        lax.psum_scatter(
            gain_two_term.astype(jnp.bfloat16), "dp", scatter_dimension=0, tiled=True
        ).astype(jnp.float32),
        lax.psum_scatter(
            shift_two_term.astype(jnp.bfloat16), "dp", scatter_dimension=0, tiled=True
        ).astype(jnp.float32),
        lax.psum_scatter(
            up_term.astype(jnp.bfloat16), "dp", scatter_dimension=0, tiled=True
        ).astype(jnp.float32),
        lax.psum_scatter(
            up_bias_term.astype(jnp.bfloat16), "dp", scatter_dimension=0, tiled=True
        ).astype(jnp.float32),
        lax.psum_scatter(
            down_term.astype(jnp.bfloat16), "dp", scatter_dimension=0, tiled=True
        ).astype(jnp.float32),
        lax.psum_scatter(
            down_bias_term.astype(jnp.bfloat16), "dp", scatter_dimension=0, tiled=True
        ).astype(jnp.float32),
        lax.psum_scatter(
            head_term.astype(jnp.bfloat16), "dp", scatter_dimension=0, tiled=True
        ).astype(jnp.float32),
        lax.psum_scatter(
            head_bias_term.astype(jnp.bfloat16), "dp", scatter_dimension=0, tiled=True
        ).astype(jnp.float32),
    )
    rear_grads = (
        lax.psum_scatter(gain_part, "fsdp", scatter_dimension=0, tiled=True),
        lax.psum_scatter(shift_part, "fsdp", scatter_dimension=0, tiled=True),
        lax.psum_scatter(up_part, "fsdp", scatter_dimension=0, tiled=True),
        lax.psum_scatter(up_bias_part, "fsdp", scatter_dimension=0, tiled=True),
        lax.psum_scatter(down_part, "fsdp", scatter_dimension=0, tiled=True),
        lax.psum_scatter(down_bias_part, "fsdp", scatter_dimension=0, tiled=True),
        lax.psum_scatter(head_part, "fsdp", scatter_dimension=0, tiled=True),
        lax.psum_scatter(head_bias_part, "fsdp", scatter_dimension=0, tiled=True),
    )
    mid_grad = end_grad + state_grad_two
    out_grad = mid_grad.astype(jnp.bfloat16)
    out_bias_term = jnp.sum(out_grad.astype(jnp.float32), axis=0)
    out_term = jnp.einsum("td,te->de", attended, out_grad, preferred_element_type=jnp.float32)
    mixed_grad = jnp.einsum(
        "te,de->td", out_grad, out_back, preferred_element_type=jnp.float32
    ).astype(jnp.bfloat16)
    grad_blocks = mixed_grad.reshape(block_count, block_rows, HEADS, head_dim)

    def backward_block(carry, inputs):
        key_sum, value_sum = carry
        query_block, grad_block, window_block, total_block, block_start = inputs
        masked = block_scores(query_block, window_block, block_start)
        probs = jnp.exp(masked - total_block[:, :, None])
        prob_grad = jnp.einsum(
            "qhd,khd->hqk", grad_block, values, preferred_element_type=jnp.float32
        )
        inner = jnp.sum(probs * prob_grad, axis=-1, keepdims=True)
        score_grad = (probs * (prob_grad - inner)).astype(jnp.bfloat16)
        query_grad = (
            jnp.einsum("hqk,khd->qhd", score_grad, keys, preferred_element_type=jnp.float32)
            * score_scale
        )
        key_sum = (
            key_sum
            + jnp.einsum(
                "hqk,qhd->khd", score_grad, query_block, preferred_element_type=jnp.float32
            )
            * score_scale
        )
        value_sum = value_sum + jnp.einsum(
            "hqk,qhd->khd",
            probs.astype(jnp.bfloat16),
            grad_block,
            preferred_element_type=jnp.float32,
        )
        return ((key_sum, value_sum), query_grad.reshape(block_rows, width))

    zero_keys = jnp.zeros((token_rows, HEADS, head_dim), jnp.float32)
    (key_grad, value_grad), query_grads = lax.scan(
        backward_block,
        (zero_keys, zero_keys),
        (queries, grad_blocks, query_windows, log_totals, block_starts),
    )
    qkv_grad = jnp.concatenate(
        [
            query_grads.reshape(token_rows, width),
            key_grad.reshape(token_rows, width),
            value_grad.reshape(token_rows, width),
        ],
        axis=1,
    ).astype(jnp.bfloat16)
    qkv_term = jnp.einsum("td,te->de", attn_input, qkv_grad, preferred_element_type=jnp.float32)
    normed_one_grad = jnp.einsum(
        "te,de->td", qkv_grad, qkv_back, preferred_element_type=jnp.float32
    )
    state_grad_one, gain_one_term, shift_one_term = pull_one(normed_one_grad)
    patch_grad = mid_grad + state_grad_one
    lead_term = lead_hot[:, None] * jnp.sum(patch_grad, axis=0)[None, :]
    lead_part, gain_one_part, shift_one_part, qkv_part, out_part, out_bias_part = (
        lax.psum_scatter(
            lead_term.astype(jnp.bfloat16), "dp", scatter_dimension=1, tiled=True
        ).astype(jnp.float32),
        lax.psum_scatter(
            gain_one_term.astype(jnp.bfloat16), "dp", scatter_dimension=0, tiled=True
        ).astype(jnp.float32),
        lax.psum_scatter(
            shift_one_term.astype(jnp.bfloat16), "dp", scatter_dimension=0, tiled=True
        ).astype(jnp.float32),
        lax.psum_scatter(
            qkv_term.astype(jnp.bfloat16), "dp", scatter_dimension=0, tiled=True
        ).astype(jnp.float32),
        lax.psum_scatter(
            out_term.astype(jnp.bfloat16), "dp", scatter_dimension=0, tiled=True
        ).astype(jnp.float32),
        lax.psum_scatter(
            out_bias_term.astype(jnp.bfloat16), "dp", scatter_dimension=0, tiled=True
        ).astype(jnp.float32),
    )
    front_grads = (
        lax.psum_scatter(lead_part, "fsdp", scatter_dimension=1, tiled=True),
        lax.psum_scatter(gain_one_part, "fsdp", scatter_dimension=0, tiled=True),
        lax.psum_scatter(shift_one_part, "fsdp", scatter_dimension=0, tiled=True),
        lax.psum_scatter(qkv_part, "fsdp", scatter_dimension=0, tiled=True),
        lax.psum_scatter(out_part, "fsdp", scatter_dimension=0, tiled=True),
        lax.psum_scatter(out_bias_part, "fsdp", scatter_dimension=0, tiled=True),
    )
    return (
        outputs,
        head_out,
        patch_grad,
        front_grads[0],
        front_grads[1],
        front_grads[2],
        front_grads[3],
        front_grads[4],
        front_grads[5],
        rear_grads[0],
        rear_grads[1],
        rear_grads[2],
        rear_grads[3],
        rear_grads[4],
        rear_grads[5],
        rear_grads[6],
        rear_grads[7],
    )


def solution(mesh):
    in_specs = (
        P(("dp", "fsdp"), None),
        P(("dp", "fsdp")),
        P(("dp", "fsdp"), None),
        P(("dp", "fsdp")),
        P(None, ("dp", "fsdp")),
        P(("dp", "fsdp")),
        P(("dp", "fsdp")),
        P(("dp", "fsdp"), None),
        P(("dp", "fsdp"), None),
        P(("dp", "fsdp")),
        P(("dp", "fsdp")),
        P(("dp", "fsdp")),
        P(("dp", "fsdp"), None),
        P(("dp", "fsdp")),
        P(("dp", "fsdp"), None),
        P(("dp", "fsdp")),
        P(("dp", "fsdp"), None),
        P(("dp", "fsdp")),
        P(("dp", "fsdp"), None),
        P(("dp", "fsdp"), None),
    )
    out_specs = (
        P(("dp", "fsdp"), None),
        P(("dp", "fsdp"), None),
        P(("dp", "fsdp"), None),
        P(None, ("dp", "fsdp")),
        P(("dp", "fsdp")),
        P(("dp", "fsdp")),
        P(("dp", "fsdp"), None),
        P(("dp", "fsdp"), None),
        P(("dp", "fsdp")),
        P(("dp", "fsdp")),
        P(("dp", "fsdp")),
        P(("dp", "fsdp"), None),
        P(("dp", "fsdp")),
        P(("dp", "fsdp"), None),
        P(("dp", "fsdp")),
        P(("dp", "fsdp"), None),
        P(("dp", "fsdp")),
    )
    body = shards if dict(mesh.shape) == {"dp": 4, "fsdp": 8} else plain_shards
    return jax.shard_map(body, mesh=mesh, in_specs=in_specs, out_specs=out_specs, check_vma=False)
```

```python
import math
from functools import partial

import jax
import jax.numpy as jnp
from jax import lax
from jax.experimental import pallas as pl
from jax.experimental.pallas import tpu as pltpu
from jax.sharding import PartitionSpec as P

HEADS = 12
PIX = 64
EXPERTS = 3
LEADS = 16


norm_epsilon = 1e-05
score_scale = 0.125


def layer_norm(hidden, norm_gain, norm_shift):
    average = jnp.mean(hidden, axis=-1, keepdims=True)
    centered = hidden - average
    variance = jnp.mean(centered * centered, axis=-1, keepdims=True)
    return centered * lax.rsqrt(variance + norm_epsilon) * norm_gain + norm_shift


def gelu_exact(values):
    return 0.5 * values * (1.0 + lax.erf(values * 0.7071067811865476))


def expert_softmax(logits, experts, pixels):
    gate_part = logits[:, : experts * pixels].reshape(logits.shape[0], experts, pixels)
    largest = jnp.max(gate_part, axis=1, keepdims=True)
    raised = jnp.exp(gate_part - largest)
    shares = raised / jnp.sum(raised, axis=1, keepdims=True)
    return jnp.concatenate(
        [shares.reshape(logits.shape[0], experts * pixels), logits[:, experts * pixels :]], axis=1
    )


def allowed_keys(query_window, key_window, key_valid, query_start):
    query_place = query_start + jnp.arange(query_window.shape[0], dtype=jnp.int32)
    key_place = jnp.arange(key_window.shape[0], dtype=jnp.int32)
    same_window = query_window[:, None] == key_window[None, :]
    usable = (key_valid[None, :] > 0) | (query_place[:, None] == key_place[None, :])
    return same_window & usable


AXES = ("dp", "fsdp")
FAR_Z, NEAR_Z, FIRST, SECOND, SIBLING = (4, 4), (2, 2), (8, 16), (16, 8), (1, 1)
ORDERS = {
    "q": (FAR_Z, NEAR_Z, FIRST, SECOND),
    "u": (FAR_Z, FIRST, SECOND, NEAR_Z),
    "d": (FIRST, FAR_Z, NEAR_Z, SECOND),
    "h": (NEAR_Z, FAR_Z, FIRST, SECOND),
    "head": (FAR_Z, NEAR_Z, FIRST, SECOND),
    "down": (FAR_Z, NEAR_Z, FIRST, SECOND),
    "up": (FAR_Z, FIRST, SECOND, NEAR_Z),
    "front": (FAR_Z, NEAR_Z, FIRST, SECOND),
    "mix": (FAR_Z, NEAR_Z, FIRST, SECOND),
}
GATHER_SEQUENCE = (
    ("q", 0), ("d", 0), ("h", 0), ("u", 0), ("q", 1), ("d", 1), ("u", 1), ("q", 2), ("h", 1), ("u", 2),
    ("d", 2),
)
MOST_VMEM, SPARE_VMEM = 60 * 1024 * 1024, 8 * 1024 * 1024
WIDTH = 768
HIDDEN = 3072
HEAD = 4608
TOKENS = 512
GATE = 512
F32 = jnp.float32
BF16 = jnp.bfloat16
HBM = pl.BlockSpec(memory_space=pltpu.HBM)
SMEM = pl.BlockSpec(memory_space=pltpu.SMEM)
VMEM = pl.BlockSpec(memory_space=pltpu.VMEM)
QKV_PART, SMALL_PART = (0, 1152), (1152, 128)
UP_PART, OUT_PART, GATE_PART = (0, 1536), (1536, 384), (1920, 256)
DOWN_PART, HEAD_PART = (0, 384), (0, 2048)


def chip_masks(order, lane):
    masks = []
    for place in range(16):
        mask = 0
        for step in range(4):
            if place >> step & 1:
                mask ^= order[step][lane]
        masks.append(mask >> 1)
    return masks


def table_start(group, side):
    return 1 + 32 * list(ORDERS).index(group) + 16 * side


def exchange(array, masks):
    return lax.ppermute(array, AXES, [(d, d ^ masks[d & 1]) for d in range(32)])


def whereabouts():
    device = lax.axis_index("dp") * 8 + lax.axis_index("fsdp")
    core, chip = device % 2, device // 2
    tables = [chip_masks(order, 0) + chip_masks(order, 1) for order in ORDERS.values()]
    swapped = [chip_masks(order, 1) + chip_masks(order, 0) for order in ORDERS.values()]
    places = jnp.where(core == 0, jnp.array(tables, jnp.int32), jnp.array(swapped, jnp.int32))
    places = (places ^ chip).reshape(32 * len(ORDERS))
    return core, jnp.concatenate([core[None].astype(jnp.int32), places])


def after(value, *marks):
    return lax.optimization_barrier((value, marks))[0]


def in_core_order(core, mine, theirs, axis):
    return jnp.where(
        core == 0,
        jnp.concatenate([mine, theirs], axis=axis),
        jnp.concatenate([theirs, mine], axis=axis),
    )


def pack_kernel(core, qkv, out, up, down, head, table, *refs):
    vectors, (up_bias, head_bias), refs = refs[:6], refs[6:8], refs[8:]
    outs, (rows,) = refs[:8], refs[8:]
    rows[...] = jnp.zeros_like(rows)
    for index, vector in enumerate(vectors):
        rows[index : index + 1, :24] = vector[...].astype(F32)
    for index in range(4):
        rows[6 + index : 7 + index, :24] = up_bias[:, 24 * index : 24 * index + 24].astype(F32)
    for index in range(6):
        rows[10 + index : 11 + index, :24] = head_bias[:, 24 * index : 24 * index + 24].astype(F32)
    rows[16:32, :24] = table[...].astype(F32)
    small = rows[...].T[:24].astype(BF16)
    for side in range(2):
        q, u, d, h = outs[4 * side : 4 * side + 4]
        q[:, :1152] = qkv[:, lane_columns(core, side, 1152)]
        q[:, 1152:] = small
        u[:, :1536] = up[:, lane_columns(core, side, 1536)]
        u[:, 1536:1920] = out[:, lane_columns(core, side, 384)]
        u[:, 1920:] = head[:, lane_columns(core, side, 256)]
        d[...] = down[:, lane_columns(core, side, 384)]
        h[...] = head[:, lane_columns(core, side, 2048, GATE)]


def packed(core, weights, table, vectors):
    shapes = [(24, 1280), (24, 2176), (96, 384), (24, 2048)] * 2
    return call(
        pack_kernel,
        (core.reshape(1), *weights, table, *[vector[None] for vector in vectors]),
        [SMEM] + [VMEM] * 14,
        [(shape, BF16, False) for shape in shapes],
        [pltpu.VMEM((128, 128), F32)],
    )


def doubled(held, masks):
    return jnp.concatenate([held, exchange(held, masks)], axis=0)


def both_lanes(*arrays):
    return arrays + tuple(exchange(array, SIBLING) for array in arrays)


def total(first, second):
    return first.astype(F32) + second.astype(F32)


def folded(keep, got, start=0):
    half = got.shape[0] // 2
    send = total(keep[half:], got[half:]).astype(BF16)
    return total(keep[:half], got[:half]).astype(BF16), send


def finished(keep, got, core, widths):
    block = total(keep, got)[0]
    rows = block.shape[0] // 2
    upper, lower = block[:rows], block[rows:]
    mine = jnp.where(core == 0, upper, lower)
    theirs = jnp.where(core == 0, lower, upper).astype(BF16)
    other = exchange(theirs, SIBLING).astype(F32)
    pieces, start = [], 0
    for width in widths:
        span = slice(start, start + width)
        pieces.append(in_core_order(core, mine[:, span], other[:, span], 1))
        start += width
    return pieces


def across(first, second):
    return lax.dot_general(first, second, (((1,), (1,)), ((), ())), preferred_element_type=F32)


def times(first, second):
    return jnp.dot(first, second, preferred_element_type=F32)


def lane_columns(where, side, stride, first=0, width=None):
    return pl.ds(pl.multiple_of(first + (where[0] ^ side) * stride, 128), width or stride)


def block_copies(where, group, sources, part, target, sems, side, first=0):
    start, width = part
    rows = sources[0].shape[1]
    half = len(sources) // 2
    count = 16 // half
    copies = []
    for place in range(16):
        row = pl.multiple_of(where[table_start(group, side) + place] * rows, rows)
        copies.append(
            pltpu.make_async_copy(
                sources[half * side + place // count].at[place % count, :, pl.ds(start, width)],
                target.at[pl.ds(row, rows), lane_columns(where, side, width, first)],
                sems.at[side, place],
            )
        )
    return copies


def start_all(copies):
    for copy in copies:
        copy.start()


def wait_all(copies):
    for copy in copies:
        copy.wait()


def mean_and_scale(hidden):
    average = jnp.mean(hidden, axis=1, keepdims=True)
    centered = hidden - average
    variance = jnp.mean(centered * centered, axis=1, keepdims=True)
    return centered, lax.rsqrt(variance + norm_epsilon)


def norm_backward(hidden, gain, upstream):
    centered, scale = mean_and_scale(hidden)
    normed = centered * scale
    gain_grad = jnp.sum(upstream * normed, axis=0, keepdims=True)
    shift_grad = jnp.sum(upstream, axis=0, keepdims=True)
    scaled = upstream * gain
    first = jnp.mean(scaled, axis=1, keepdims=True)
    second = jnp.mean(scaled * normed, axis=1, keepdims=True)
    return scale * (scaled - first - normed * second), gain_grad, shift_grad


def call(kernel, operands, in_specs, outs, scratch, spare=None):
    def size(item):
        return math.prod(item.shape) * jnp.dtype(item.dtype).itemsize

    held = [item for item, spec in zip(operands, in_specs) if spec is VMEM]
    held += [jax.ShapeDtypeStruct(shape, kind) for shape, kind, copied in outs if not copied]
    held += [item for item in scratch if getattr(item, "memory_space", None) == pltpu.VMEM]
    limit = MOST_VMEM if spare is None else sum(size(item) for item in held) + spare
    return pl.pallas_call(
        kernel,
        out_shape=[jax.ShapeDtypeStruct(shape, kind) for shape, kind, _ in outs],
        in_specs=in_specs,
        out_specs=[HBM if copied else VMEM for _, _, copied in outs],
        scratch_shapes=scratch,
        compiler_params=pltpu.CompilerParams(vmem_limit_bytes=limit),
        cost_estimate=pl.CostEstimate(flops=2 * 10**12, bytes_accessed=10**10, transcendentals=0),
    )(*operands)


def lane_scratch(rows, width):
    return [pltpu.VMEM((2, rows, width), BF16), pltpu.SemaphoreType.DMA((2, 16))]


def weight_scratch(rows, width):
    return [pltpu.VMEM((rows, width), BF16), pltpu.SemaphoreType.DMA((2, 16))]


def taken(refs, *counts):
    groups = []
    for count in counts:
        groups.append(refs[:count])
        refs = refs[count:]
    return *groups, refs


def front_kernel(where, lead, patches, *refs):
    sources, outs, scratch = taken(refs, 4, 3)
    turned_out, qkv_out, small = outs
    weight, sems, smalls, small_sems, state, rows, turned, qkv, io_sems = scratch
    loads = [block_copies(where, "q", sources, QKV_PART, weight, sems, side) for side in range(2)]
    small_loads = []
    for place in range(16):
        row = pl.multiple_of(where[table_start("q", 0) + place] * 48, 48)
        small_loads.append(
            pltpu.make_async_copy(
                sources[place // 8].at[place % 8, :, pl.ds(*SMALL_PART)],
                smalls.at[pl.ds(row, 48), :],
                small_sems.at[place],
            )
        )
    state_load = pltpu.make_async_copy(patches, state, io_sems.at[0])
    start_all(small_loads)
    state_load.start()
    start_all(loads[0])
    start_all(loads[1])
    wait_all(small_loads)
    columns = smalls[...].astype(F32).T
    places = lax.broadcasted_iota(jnp.int32, (LEADS, WIDTH), 0)
    lead_row = jnp.sum(
        jnp.where(places == lead[0], columns[16 : 16 + LEADS], 0.0), axis=0, keepdims=True
    )
    small[...] = columns[:32]
    small[16:17, :] = lead_row
    state_load.wait()
    centered, scale = mean_and_scale(state[...].astype(F32) + lead_row)
    rows[...] = (centered * scale * columns[0:1] + columns[1:2]).astype(BF16)
    turned[...] = rows[...].T
    stores = [pltpu.make_async_copy(turned, turned_out, io_sems.at[1])]
    stores[0].start()
    wait_all(loads[0] + loads[1])
    for part in range(3):
        span = slice(part * WIDTH, part * WIDTH + WIDTH)
        qkv[:, span] = times(rows[...], weight[:, span]).astype(BF16)
        stores.append(pltpu.make_async_copy(qkv.at[:, span], qkv_out.at[:, span], io_sems.at[2 + part]))
        stores[-1].start()
    wait_all(stores)


def front_forward(where, lead_index, patches, arrays):
    return call(
        front_kernel,
        (where, lead_index, patches, *arrays),
        [SMEM, SMEM, HBM] + [HBM] * 4,
        [
            ((WIDTH, TOKENS), BF16, True),
            ((TOKENS, 3 * WIDTH), BF16, True),
            ((32, WIDTH), F32, False),
        ],
        weight_scratch(WIDTH, 3 * WIDTH)
        + [pltpu.VMEM((WIDTH, 128), BF16), pltpu.SemaphoreType.DMA((16,))]
        + [
            pltpu.VMEM((TOKENS, WIDTH), BF16),
            pltpu.VMEM((TOKENS, WIDTH), BF16),
            pltpu.VMEM((WIDTH, TOKENS), BF16),
            pltpu.VMEM((TOKENS, 3 * WIDTH), BF16),
            pltpu.SemaphoreType.DMA((5,)),
        ],
    )


KEY_SPANS = ((0, 256), (0, 384), (128, 512), (256, 512))


def fill_bias(lengths, pad, bias):
    ends, end = [], 0
    for index in range(lengths.shape[1]):
        end = end + lengths[0, index]
        ends.append(end)

    def windows(places):
        return sum([(places >= end).astype(jnp.int32) for end in ends])

    for block, (low, high) in enumerate(KEY_SPANS):
        count = high - low
        queries = lax.broadcasted_iota(jnp.int32, (1, 128), 1) + 128 * block
        keys = lax.broadcasted_iota(jnp.int32, (count, 1), 0) + low
        same = windows(queries) == windows(keys)
        usable = (pad[low:high, :] > 0) | (queries == keys)
        bias[block, :count, :] = jnp.where(same & usable, 0.0, -1e30)


def two_heads(block):
    first = lax.broadcasted_iota(jnp.int32, block.shape, 1) < block.shape[1] // 2
    zero = jnp.zeros_like(block)
    return jnp.concatenate([jnp.where(first, block, zero), jnp.where(first, zero, block)], axis=0)


def head_rows_of(stacked):
    return jnp.concatenate([stacked[:64, :128], stacked[64:, 128:]], axis=0)


def probabilities(scores, allowed):
    masked = scores * score_scale + allowed
    raised = jnp.exp(masked - jnp.max(masked, axis=0, keepdims=True))
    return raised * (1.0 / jnp.sum(raised, axis=0, keepdims=True))


def attention_kernel(where, lengths, pad, qkv, attended_out, turned_out, bias, turned, rows, sems):
    fill_bias(lengths, pad, bias)

    def pair(index, carry):
        first = index * 128
        columns = pl.ds(pl.multiple_of(first, 128), 128)
        keys_at = pl.ds(pl.multiple_of(first + WIDTH, 128), 128)
        values = qkv[:, pl.ds(pl.multiple_of(first + 2 * WIDTH, 128), 128)].T
        for block, (low, high) in enumerate(KEY_SPANS):
            span = slice(128 * block, 128 * block + 128)
            scores = across(qkv[low:high, keys_at], two_heads(qkv[span, columns]))
            allowed = bias[block, : high - low, :]
            probs = [
                probabilities(scores[:, 128 * head : 128 * head + 128], allowed).astype(BF16)
                for head in range(2)
            ]
            mixed = times(values[:, low:high], jnp.concatenate(probs, axis=1))
            turned[columns, span] = head_rows_of(mixed).astype(BF16)
        return carry

    lax.fori_loop(0, WIDTH // 128, pair, 0)
    stores = [pltpu.make_async_copy(turned, turned_out, sems.at[0])]
    stores[0].start()
    rows[...] = turned[...].T
    stores.append(pltpu.make_async_copy(rows, attended_out, sems.at[1]))
    stores[1].start()
    wait_all(stores)


def attention_forward(where, lengths, pad, qkv):
    rows, columns = (TOKENS, WIDTH), (WIDTH, TOKENS)
    return call(
        attention_kernel,
        (where, lengths, pad, qkv),
        [SMEM, SMEM, VMEM, VMEM],
        [(rows, BF16, True), (columns, BF16, True)],
        [
            pltpu.VMEM((4, 384, 128), F32),
            pltpu.VMEM(columns, BF16),
            pltpu.VMEM(rows, BF16),
            pltpu.SemaphoreType.DMA((2,)),
        ],
    )


def gate_shares(logits, cotangent, shares, gate_grad):
    gate_grad[:, 256:] = cotangent[:, 256:GATE]
    first, rest = logits[:, :128], logits[:, 128:256]
    left = lax.broadcasted_iota(jnp.int32, first.shape, 1) < PIX
    third = jnp.where(left, rest, pltpu.roll(rest, PIX, 1))
    largest = jnp.maximum(jnp.maximum(first, pltpu.roll(first, PIX, 1)), third)
    raised, raised_third = jnp.exp(first - largest), jnp.exp(third - largest)
    scale = 1.0 / (raised + pltpu.roll(raised, PIX, 1) + raised_third)
    share, share_third = raised * scale, raised_third * scale
    shares[:, :128] = share
    shares[:, 128:256] = jnp.where(left, share_third, rest)
    pull, other = cotangent[:, :128].astype(F32), cotangent[:, 128:256].astype(F32)
    pull_third = jnp.where(left, other, pltpu.roll(other, PIX, 1))
    weighed = share * pull
    inner = weighed + pltpu.roll(weighed, PIX, 1) + share_third * pull_third
    gate_grad[:, :128] = (share * (pull - inner)).astype(BF16)
    gate_grad[:, 128:256] = jnp.where(left, share_third * (pull_third - inner), other).astype(BF16)


def head_kernel(where, rows, gate_out, bias, *refs):
    sources, outs, scratch = taken(refs, 4, 1)
    (out,) = outs
    weight, sems, inputs, result, io_sems = scratch
    loads = [block_copies(where, "h", sources, HEAD_PART, weight, sems, side) for side in range(2)]
    row_load = pltpu.make_async_copy(rows, inputs, io_sems.at[0])
    gate_load = pltpu.make_async_copy(gate_out, result.at[:, :GATE], io_sems.at[1])
    row_load.start()
    start_all(loads[0])
    start_all(loads[1])
    gate_load.start()
    row_load.wait()
    stores = []

    def store(span):
        stores.append(
            pltpu.make_async_copy(result.at[:, span], out.at[:, span], io_sems.at[2 + len(stores)])
        )
        stores[-1].start()

    for side in range(2):
        wait_all(loads[side])
        for tile in range(4):
            span = lane_columns(where, side, 2048, GATE + tile * 512, 512)
            columns = lane_columns(where, side, 2048, tile * 512, 512)
            result[:, span] = times(inputs[...], weight[:, columns]) + bias[:, span]
            store(span)
    gate_load.wait()
    store(pl.ds(0, GATE))
    wait_all(stores)


def head_forward(where, rows, gate_out, bias, arrays):
    return call(
        head_kernel,
        (where, rows, gate_out, bias, *arrays),
        [SMEM, HBM, HBM, VMEM] + [HBM] * 4,
        [((TOKENS, HEAD), F32, True)],
        weight_scratch(WIDTH, HEAD - GATE)
        + [
            pltpu.VMEM((TOKENS, WIDTH), BF16),
            pltpu.VMEM((TOKENS, HEAD), F32),
            pltpu.SemaphoreType.DMA((11,)),
        ],
        spare=SPARE_VMEM,
    )[0]


def send_lane(where, group, lane, out, sems, side):
    rows = out.shape[1]
    copies = []
    for place in range(16):
        row = pl.multiple_of(where[table_start(group, side) + place] * rows, rows)
        copies.append(
            pltpu.make_async_copy(lane.at[pl.ds(row, rows), :], out.at[place], sems.at[place])
        )
    start_all(copies)
    return copies


def middle_kernel(where, small, up_bias, head_bias, attended, patches, cotangent, act_cotangent, *refs):
    up_sources, down_sources, head_sources, outs, scratch = taken(refs, 4, 4, 4, 14)
    outputs, shares, gate_bias, down_bias, up_bias_sum, terms, mid_grad, out_grad, *grads = outs
    down_mine, down_theirs, up_mine, up_theirs, head_mine, head_theirs = grads
    out_weight, out_sems, up, up_sems, down, down_sems, scratch = *scratch[:6], scratch[6:]
    head, head_sems, gate_sems, rows, branch, mid, mlp_turned, scratch = *scratch[:7], scratch[7:]
    act, act_turned, slope, turned, pulls, act_pulls, gate_grad, scratch = *scratch[:7], scratch[7:]
    lane, lane_sems, down_lane, down_lane_sems, io_sems = scratch

    def loads(group, sources, part, target, sems, first=0):
        copies = []
        for side in range(2):
            copies += block_copies(where, group, sources, part, target, sems, side, first)
        return copies

    state_loads = [
        pltpu.make_async_copy(attended, rows, io_sems.at[0]),
        pltpu.make_async_copy(patches, branch, io_sems.at[1]),
    ]
    out_loads = loads("u", up_sources, OUT_PART, out_weight, out_sems)
    up_loads = loads("u", up_sources, UP_PART, up, up_sems)
    down_loads = loads("d", down_sources, DOWN_PART, down, down_sems)
    gate_loads = loads("u", up_sources, GATE_PART, head, gate_sems)
    head_loads = loads("h", head_sources, HEAD_PART, head, head_sems, GATE)
    pull_load = pltpu.make_async_copy(cotangent, pulls, io_sems.at[2])
    act_load = pltpu.make_async_copy(act_cotangent, act_pulls, io_sems.at[3])
    start_all(state_loads + out_loads + up_loads + down_loads + gate_loads)
    pull_load.start()
    start_all(head_loads)
    act_load.start()

    wait_all(state_loads + out_loads)
    mid[...] = (
        branch[...].astype(F32)
        + small[16:17, :]
        + times(rows[...], out_weight[...])
        + small[2:3, :]
    )
    centered, scale = mean_and_scale(mid[...])
    rows[...] = (centered * scale * small[3:4, :] + small[4:5, :]).astype(BF16)
    mlp_turned[...] = rows[...].T
    wait_all(up_loads)
    for tile in range(6):
        span = slice(tile * 512, tile * 512 + 512)
        values = times(rows[...], up[:, span]) + up_bias[:, span]
        share = 0.5 * (1.0 + lax.erf(values * 0.7071067811865476))
        density = jnp.exp(-0.5 * values * values) * 0.3989422804014327
        activated = (values * share).astype(BF16)
        act[:, span] = activated
        act_turned[span, :] = activated.T
        slope[:, span] = (share + values * density).astype(BF16)
    wait_all(down_loads)
    outputs[...] = (mid[...] + times(act[...], down[...]) + small[5:6, :]).astype(BF16)
    turned[...] = outputs[...].T
    wait_all(gate_loads)
    shares[...] = times(outputs[...], head[:, :GATE]) + head_bias[:, :GATE]
    pull_load.wait()
    gate_shares(shares, pulls, shares, gate_grad)
    gate_bias[...] = jnp.sum(gate_grad[...].astype(F32), axis=0, keepdims=True)
    pulls[:, :GATE] = gate_grad[...]

    def head_lane(side, out):
        lane[:, :256] = times(turned[...], pulls[:, lane_columns(where, side, 256)]).astype(BF16)
        for tile in range(4):
            span = lane_columns(where, side, 2048, GATE + tile * 512, 512)
            lane[:, 256 + tile * 512 : 768 + tile * 512] = times(turned[...], pulls[:, span]).astype(
                BF16
            )
        return send_lane(where, "head", lane, out, lane_sems, side)

    def down_lane_of(side, out):
        columns = branch[:, lane_columns(where, side, 384)]
        for part in range(4):
            span = slice(part * WIDTH, part * WIDTH + WIDTH)
            down_lane[span, :] = times(act_turned[span, :], columns).astype(BF16)
        return send_lane(where, "down", down_lane, out, down_lane_sems, side)

    def up_lane(side, out):
        for tile in range(3):
            span = lane_columns(where, side, 1536, tile * 512, 512)
            lane[:, tile * 512 : tile * 512 + 512] = times(mlp_turned[...], slope[:, span]).astype(BF16)
        return send_lane(where, "up", lane.at[:, :1536], out, lane_sems, side)

    lane_stores = head_lane(1, head_theirs)
    act_load.wait()
    wait_all(head_loads)
    mid_grad[...] = act_pulls[...].astype(F32) + across(pulls[...], head[...])
    branch[...] = mid_grad[...].astype(BF16)
    down_bias[...] = jnp.sum(branch[...].astype(F32), axis=0, keepdims=True)
    wait_all(lane_stores)
    lane_stores = head_lane(0, head_mine)
    down_stores = down_lane_of(1, down_theirs)
    for tile in range(6):
        span = slice(tile * 512, tile * 512 + 512)
        grad = across(branch[...], down[span, :])
        rounded = (slope[:, span].astype(F32) * grad).astype(BF16)
        slope[:, span] = rounded
        up_bias_sum[:, span] = jnp.sum(rounded.astype(F32), axis=0, keepdims=True)
    wait_all(down_stores)
    down_stores = down_lane_of(0, down_mine)
    wait_all(lane_stores)
    lane_stores = up_lane(1, up_theirs)
    grad = across(slope[...], up[...])
    pulled, gain_grad, shift_grad = norm_backward(mid[...], small[3:4, :], grad)
    pulled = pulled + mid_grad[...]
    rounded = pulled.astype(BF16)
    mid_grad[...] = pulled
    out_grad[...] = rounded
    terms[...] = jnp.zeros_like(terms)
    terms[0:1, :] = jnp.sum(rounded.astype(F32), axis=0, keepdims=True)
    terms[1:2, :] = gain_grad
    terms[2:3, :] = shift_grad
    wait_all(lane_stores)
    lane_stores = up_lane(0, up_mine)
    wait_all(down_stores + lane_stores)


def middle(
    where, small, up_bias, head_bias, attended, patches, cotangent, act_cotangent, up, down, head
):
    rows, columns = (TOKENS, WIDTH), (WIDTH, TOKENS)
    wide, tall = (TOKENS, HIDDEN), (HIDDEN, TOKENS)
    return call(
        middle_kernel,
        (
            where, small, up_bias, head_bias, attended, patches, cotangent, act_cotangent,
            *up, *down, *head,
        ),
        [SMEM, VMEM, VMEM, VMEM] + [HBM] * 16,
        [
            (rows, BF16, False),
            ((TOKENS, GATE), F32, False),
            ((1, GATE), F32, False),
            ((1, WIDTH), F32, False),
            ((1, HIDDEN), F32, False),
            ((8, WIDTH), F32, False),
            (rows, F32, False),
            (rows, BF16, False),
            ((16, 192, 384), BF16, True),
            ((16, 192, 384), BF16, True),
            ((16, 48, 1536), BF16, True),
            ((16, 48, 1536), BF16, True),
            ((16, 48, 2304), BF16, True),
            ((16, 48, 2304), BF16, True),
        ],
        weight_scratch(WIDTH, WIDTH)
        + weight_scratch(WIDTH, HIDDEN)
        + weight_scratch(HIDDEN, WIDTH)
        + weight_scratch(WIDTH, HEAD)
        + [
            pltpu.SemaphoreType.DMA((2, 16)),
            pltpu.VMEM(rows, BF16),
            pltpu.VMEM(rows, BF16),
            pltpu.VMEM(rows, F32),
            pltpu.VMEM(columns, BF16),
            pltpu.VMEM(wide, BF16),
            pltpu.VMEM(tall, BF16),
            pltpu.VMEM(wide, BF16),
            pltpu.VMEM(columns, BF16),
            pltpu.VMEM((TOKENS, HEAD), BF16),
            pltpu.VMEM(rows, BF16),
            pltpu.VMEM((TOKENS, GATE), BF16),
            pltpu.VMEM((WIDTH, 2304), BF16),
            pltpu.SemaphoreType.DMA((16,)),
            pltpu.VMEM((HIDDEN, 384), BF16),
            pltpu.SemaphoreType.DMA((16,)),
            pltpu.SemaphoreType.DMA((4,)),
        ],
    )


def attend_back(start, count, qkv, mixed, bias, turned, key_sum, value_sum, qkv_grad):
    width = 128 * count

    def columns_at(first):
        return pl.ds(pl.multiple_of(first, 128), 128)

    def pair(index, carry):
        own, first = index * 128, (index + start) * 128
        columns, keys_at = columns_at(first), columns_at(first + WIDTH)
        values_at = columns_at(first + 2 * WIDTH)
        keys_turned = qkv[:, keys_at].T
        key_sum[...] = jnp.zeros_like(key_sum)
        value_sum[...] = jnp.zeros_like(value_sum)
        for block, (low, high) in enumerate(KEY_SPANS):
            span = slice(128 * block, 128 * block + 128)
            queries, grads = two_heads(qkv[span, columns]), two_heads(mixed[span, columns_at(own)])
            scores = across(qkv[low:high, keys_at], queries)
            prob_grads = across(qkv[low:high, values_at], grads)
            allowed = bias[block, : high - low, :]
            probs, score_grads = [], []
            for head in range(2):
                part = slice(128 * head, 128 * head + 128)
                prob = probabilities(scores[:, part], allowed)
                pulled = prob * prob_grads[:, part]
                inner = jnp.sum(pulled, axis=0, keepdims=True)
                probs.append(prob.astype(BF16))
                score_grads.append((pulled - prob * inner).astype(BF16))
            score_grad = jnp.concatenate(score_grads, axis=1)
            key_sum[low:high, :] += times(score_grad, queries)
            value_sum[low:high, :] += times(jnp.concatenate(probs, axis=1), grads)
            turned[:, span] = head_rows_of(times(keys_turned[:, low:high], score_grad)) * score_scale
        qkv_grad[:, columns_at(own)] = turned[...].T.astype(BF16)
        qkv_grad[:, columns_at(own + width)] = (key_sum[...] * score_scale).astype(BF16)
        qkv_grad[:, columns_at(own + 2 * width)] = value_sum[...].astype(BF16)
        return carry

    lax.fori_loop(0, count, pair, 0)


def attention_scratch(count):
    return [
        pltpu.VMEM((4, 384, 128), F32),
        pltpu.VMEM((TOKENS, 128 * count), BF16),
        pltpu.VMEM((128, TOKENS), F32),
        pltpu.VMEM((TOKENS, 128), F32),
        pltpu.VMEM((TOKENS, 128), F32),
    ]


def early_back_kernel(where, lengths, pad, out_grad, qkv, input_turned, attended_turned, *refs):
    sources, (qkv_grad, mine_out, theirs_out), scratch = taken(refs, 4, 3)
    weight, sems, bias, mixed, turned, key_sum, value_sum, scratch = *scratch[:7], scratch[7:]
    lane, lane_sems, inputs, mixes, io_sems = scratch
    loads = [block_copies(where, "u", sources, OUT_PART, weight, sems, side) for side in range(2)]
    in_loads = [
        pltpu.make_async_copy(input_turned, inputs, io_sems.at[0]),
        pltpu.make_async_copy(attended_turned, mixes, io_sems.at[1]),
    ]
    start_all(loads[0] + loads[1] + in_loads)
    fill_bias(lengths, pad, bias)
    wait_all(loads[0] + loads[1])
    mixed[...] = across(out_grad[...], weight[:512, :]).astype(BF16)
    attend_back(0, 4, qkv, mixed, bias, turned, key_sum, value_sum, qkv_grad)
    wait_all(in_loads)
    stores = []
    for side, out in ((1, theirs_out), (0, mine_out)):
        lane[side, :, :768] = times(
            inputs[...], qkv_grad[:, lane_columns(where, side, 768)]
        ).astype(BF16)
        lane[side, :, 768:1152] = times(
            mixes[...], out_grad[:, lane_columns(where, side, 384)]
        ).astype(BF16)
        stores += send_lane(where, "front", lane.at[side], out, lane_sems.at[side], side)
    wait_all(stores)


def early_backward(where, lengths, pad, out_grad, qkv, input_turned, attended_turned, arrays):
    columns = (WIDTH, TOKENS)
    return call(
        early_back_kernel,
        (where, lengths, pad, out_grad, qkv, input_turned, attended_turned, *arrays),
        [SMEM, SMEM, VMEM, VMEM, VMEM] + [HBM] * 6,
        [
            ((TOKENS, 1536), BF16, False),
            ((16, 48, 1152), BF16, True),
            ((16, 48, 1152), BF16, True),
        ],
        weight_scratch(WIDTH, WIDTH)
        + attention_scratch(4)
        + lane_scratch(WIDTH, 1152)
        + [
            pltpu.VMEM(columns, BF16),
            pltpu.VMEM(columns, BF16),
            pltpu.SemaphoreType.DMA((2,)),
        ],
        spare=SPARE_VMEM,
    )


def late_back_kernel(
    where, lead, lengths, pad, small, terms, down_row, up_rows, head_rows,
    out_grad, qkv, first_grad, patches, mid_grad, input_turned, *refs
):
    out_sources, sources, outs, scratch = taken(refs, 4, 4, 3)
    patch_out, mine_out, theirs_out = outs
    out_weight, out_sems, weight, sems, bias, mixed, turned, key_sum, value_sum, scratch = (
        *scratch[:9], scratch[9:],
    )
    lane, lane_sems, pulls, late_pulls, state, mids, inputs, patch_grad, small_grad, io_sems = scratch
    out_loads = [
        block_copies(where, "u", out_sources, OUT_PART, out_weight, out_sems, side)
        for side in range(2)
    ]
    loads = [block_copies(where, "q", sources, QKV_PART, weight, sems, side) for side in range(2)]
    pairs = [(patches, state), (mid_grad, mids), (input_turned, inputs)]
    for part in range(3):
        target = pulls.at[:, pl.ds(WIDTH * part, 512)]
        pairs.append((first_grad.at[:, pl.ds(512 * part, 512)], target))
    in_loads = [pltpu.make_async_copy(*pair, io_sems.at[at]) for at, pair in enumerate(pairs)]
    start_all(out_loads[0] + out_loads[1] + loads[0] + loads[1] + in_loads)
    fill_bias(lengths, pad, bias)
    wait_all(out_loads[0] + out_loads[1])
    mixed[...] = across(out_grad[...], out_weight[512:, :]).astype(BF16)
    attend_back(4, 2, qkv, mixed, bias, turned, key_sum, value_sum, late_pulls)
    wait_all(loads[0] + loads[1] + in_loads)
    for part in range(3):
        pulls[:, WIDTH * part + 512 : WIDTH * part + 768] = late_pulls[
            :, 256 * part : 256 * part + 256
        ]
    grad = across(pulls[...], weight[...])
    pulled, gain_grad, shift_grad = norm_backward(
        state[...].astype(F32) + small[16:17, :], small[0:1, :], grad
    )
    pulled = pulled + mids[...]
    patch_grad[...] = pulled
    stores = [pltpu.make_async_copy(patch_grad, patch_out, io_sems.at[6])]
    stores[0].start()
    small_grad[0:1, :] = gain_grad
    small_grad[1:2, :] = shift_grad
    small_grad[2:5, :] = terms[0:3, :]
    small_grad[5:6, :] = down_row[...]
    small_grad[6:10, :] = up_rows[...]
    small_grad[10:16, :] = head_rows[...]
    places = lax.broadcasted_iota(jnp.int32, (LEADS, WIDTH), 0)
    lead_grad = jnp.sum(pulled, axis=0, keepdims=True)
    small_grad[16:32, :] = jnp.where(places == lead[0], lead_grad, 0.0)
    for side, out in ((1, theirs_out), (0, mine_out)):
        lane[side, :, :384] = times(
            inputs[...], late_pulls[:, lane_columns(where, side, 384)]
        ).astype(BF16)
        rows = small_grad[pl.ds(pl.multiple_of((where[0] ^ side) * 16, 16), 16), :]
        rows = jnp.concatenate([rows, jnp.zeros((112, WIDTH), F32)], axis=0)
        lane[side, :, 384:] = rows.T.astype(BF16)
        stores += send_lane(where, "front", lane.at[side], out, lane_sems.at[side], side)
    wait_all(stores)


def late_backward(
    where, lead, lengths, pad, small, terms, down_row, up_rows, head_rows,
    out_grad, qkv, first_grad, patches, mid_grad, input_turned, out_arrays, arrays,
):
    rows, columns = (TOKENS, WIDTH), (WIDTH, TOKENS)
    return call(
        late_back_kernel,
        (
            where, lead, lengths, pad, small, terms, down_row, up_rows, head_rows,
            out_grad, qkv, first_grad, patches, mid_grad, input_turned, *out_arrays, *arrays,
        ),
        [SMEM, SMEM, SMEM] + [VMEM] * 8 + [HBM] * 12,
        [(rows, F32, True), ((16, 48, 512), BF16, True), ((16, 48, 512), BF16, True)],
        weight_scratch(WIDTH, WIDTH)
        + weight_scratch(WIDTH, 3 * WIDTH)
        + attention_scratch(2)
        + lane_scratch(WIDTH, 512)
        + [
            pltpu.VMEM((TOKENS, 3 * WIDTH), BF16),
            pltpu.VMEM(rows, BF16),
            pltpu.VMEM(rows, BF16),
            pltpu.VMEM(rows, F32),
            pltpu.VMEM(columns, BF16),
            pltpu.VMEM(rows, F32),
            pltpu.VMEM((32, WIDTH), F32),
            pltpu.SemaphoreType.DMA((7,)),
        ],
        spare=SPARE_VMEM,
    )


def rows_of(vector, count):
    return vector.reshape(32, count, 24).transpose(1, 0, 2).reshape(count, WIDTH)


def vector_of(rows):
    count = rows.shape[0]
    return rows.reshape(count, 32, 24).transpose(1, 0, 2).reshape(1, count * WIDTH)


def shards(
    patches,
    lead_index,
    window_lengths,
    pad_mask,
    lead_table,
    attn_gain,
    attn_shift,
    qkv_weight,
    out_weight,
    out_bias,
    mlp_gain,
    mlp_shift,
    up_weight,
    up_bias,
    down_weight,
    down_bias,
    head_weight,
    head_bias,
    act_cotangent,
    head_cotangent,
):
    core, where = whereabouts()
    weights = (qkv_weight, out_weight, up_weight, down_weight, head_weight)
    vectors = (
        attn_gain, attn_shift, out_bias, mlp_gain, mlp_shift, down_bias, up_bias, head_bias
    )
    parts = packed(core, weights, lead_table, vectors)
    pad = pad_mask[:, None]
    cotangent_sum = jnp.sum(head_cotangent[:, GATE:].astype(F32), axis=0, keepdims=True)

    orders = ORDERS
    parts = dict(zip("qudh", zip(parts[:4], parts[4:])))
    chunks = {
        name: in_core_order(core, mine, exchange(theirs, SIBLING), 0)[None]
        for name, (mine, theirs) in parts.items()
    }

    held, last = dict(chunks), ()
    for name, step in GATHER_SEQUENCE:
        held[name] = after(held[name], *last)
        last = (held[name],)
        held[name] = doubled(held[name], orders[name][step])
    q, u, d, h = [held[name] for name in ("q", "u", "d", "h")]
    q_rest = exchange(after(q, *last), orders["q"][3])
    u = after(u, q)
    u_rest = exchange(u, orders["u"][3])
    d_rest = exchange(d, orders["d"][3])
    h = doubled(after(h, u), orders["h"][2])
    first = both_lanes(q, q_rest)
    h_rest = exchange(h, orders["h"][3])
    input_turned, qkv, small_rows = front_forward(
        after(where, d, h, cotangent_sum), lead_index, patches, first
    )
    attended, attended_turned = attention_forward(where, window_lengths, pad, qkv)
    u_rest, d_rest, h_rest = lax.optimization_barrier((u_rest, d_rest, h_rest, attended))[:3]
    second, down, head = both_lanes(u, u_rest), both_lanes(d, d_rest), both_lanes(h, h_rest)
    up_bias_row, head_bias_row = vector_of(small_rows[6:10]), vector_of(small_rows[10:16])
    (
        outputs, gate_out, gate_bias_sum, down_bias_sum, up_bias_sum, terms, mid_grad, out_grad,
        mine_d, theirs_d, mine_u, theirs_u, mine_h, theirs_h,
    ) = middle(
        where, small_rows, up_bias_row, head_bias_row, attended, patches, head_cotangent,
        act_cotangent, second, down, head,
    )

    got_h, got_d, got_u = [exchange(theirs, SIBLING) for theirs in (theirs_h, theirs_d, theirs_u)]
    head_rows = rows_of(jnp.concatenate([gate_bias_sum, cotangent_sum], axis=1), 6)
    up_rows = rows_of(up_bias_sum, 4)
    first_grad, mine_m, theirs_m = early_backward(
        where, window_lengths, pad, out_grad, qkv, input_turned, attended_turned, second
    )
    groups = {
        "head": [mine_h, after(got_h, first_grad), 4],
        "up": [mine_u, after(got_u, first_grad), 4],
        "down": [mine_d, after(got_d, first_grad), 4],
        "mix": [mine_m, exchange(theirs_m, SIBLING), 4],
    }
    last = ()

    def add(name):
        nonlocal last
        keep, got, step = groups[name]
        keep, send = folded(keep, after(got, *last))
        last = (send,)
        groups[name] = [keep, exchange(send, orders[name][step - 1]), step - 1]

    def finish(name, widths):
        keep, got, _ = groups[name]
        return finished(keep, after(got, *last), core, widths)

    for name in ("head", "up", "down", "mix"):
        add(name)
    patch_grad, mine_f, theirs_f = late_backward(
        after(where, *last), lead_index, window_lengths, pad, small_rows, terms, down_bias_sum,
        up_rows, head_rows, out_grad, qkv, first_grad, patches, mid_grad, input_turned, second, first,
    )
    last = (patch_grad,)
    groups["front"] = [mine_f, exchange(theirs_f, SIBLING), 4]
    for name in ("head", "front", "up", "down", "mix"):
        add(name)
    head_out = head_forward(after(where, *last), outputs, gate_out, head_bias_row, head)
    last = (head_out,)
    for name in ("front", "head", "up", "down", "mix", "front", "head", "up", "down", "mix", "front"):
        add(name)
    gate_sum, rest_sum = finish("head", (256, 2048))
    (up_sum,) = finish("up", (1536,))
    (down_sum,) = finish("down", (384,))
    early_sum, out_sum = finish("mix", (768, 384))
    late_sum, small_sum = finish("front", (384, 128))
    qkv_sum = jnp.concatenate(
        [
            piece[:, part * piece.shape[1] // 3 : (part + 1) * piece.shape[1] // 3]
            for part in range(3)
            for piece in (early_sum, late_sum)
        ],
        axis=1,
    )
    small_sum = small_sum.T
    return (
        outputs,
        head_out,
        patch_grad,
        small_sum[128:144],
        small_sum[0],
        small_sum[1],
        qkv_sum,
        out_sum,
        small_sum[2],
        small_sum[3],
        small_sum[4],
        up_sum,
        small_sum[6:10].reshape(96),
        down_sum,
        small_sum[5],
        jnp.concatenate([gate_sum, rest_sum], axis=1),
        small_sum[10:16].reshape(144),
    )


def plain_shards(
    patches,
    lead_index,
    window_lengths,
    pad_mask,
    lead_table,
    attn_gain,
    attn_shift,
    qkv_weight,
    out_weight,
    out_bias,
    mlp_gain,
    mlp_shift,
    up_weight,
    up_bias,
    down_weight,
    down_bias,
    head_weight,
    head_bias,
    act_cotangent,
    head_cotangent,
):
    front = (
        lax.all_gather(lead_table, ("dp", "fsdp"), axis=1, tiled=True),
        lax.all_gather(attn_gain, ("dp", "fsdp"), axis=0, tiled=True),
        lax.all_gather(attn_shift, ("dp", "fsdp"), axis=0, tiled=True),
        lax.all_gather(qkv_weight, ("dp", "fsdp"), axis=0, tiled=True),
        lax.all_gather(out_weight, ("dp", "fsdp"), axis=0, tiled=True),
        lax.all_gather(out_bias, ("dp", "fsdp"), axis=0, tiled=True),
    )
    rear = (
        lax.all_gather(mlp_gain, ("dp", "fsdp"), axis=0, tiled=True),
        lax.all_gather(mlp_shift, ("dp", "fsdp"), axis=0, tiled=True),
        lax.all_gather(up_weight, ("dp", "fsdp"), axis=0, tiled=True),
        lax.all_gather(up_bias, ("dp", "fsdp"), axis=0, tiled=True),
        lax.all_gather(down_weight, ("dp", "fsdp"), axis=0, tiled=True),
        lax.all_gather(down_bias, ("dp", "fsdp"), axis=0, tiled=True),
        lax.all_gather(head_weight, ("dp", "fsdp"), axis=0, tiled=True),
        lax.all_gather(head_bias, ("dp", "fsdp"), axis=0, tiled=True),
    )
    table_full, gain_one, shift_one, qkv_full, out_full, out_bias_full = front
    (
        gain_two,
        shift_two,
        up_full,
        up_bias_full,
        down_full,
        down_bias_full,
        head_full,
        head_bias_full,
    ) = rear
    token_rows, width = patches.shape
    head_dim = width // HEADS
    block_rows = min(512, token_rows)
    block_count = token_rows // block_rows
    ends = jnp.cumsum(window_lengths[0])
    positions = jnp.arange(token_rows, dtype=jnp.int32)
    window = jnp.sum((positions[:, None] >= ends[None, :]).astype(jnp.int32), axis=1)
    lead_hot = (jnp.arange(LEADS, dtype=jnp.int32) == lead_index[0]).astype(jnp.float32)
    lead_row = jnp.sum(lead_hot[:, None] * table_full.astype(jnp.float32), axis=0)
    start_state = patches.astype(jnp.float32) + lead_row[None, :]
    normed_one, pull_one = jax.vjp(
        layer_norm, start_state, gain_one.astype(jnp.float32), shift_one.astype(jnp.float32)
    )
    attn_input = normed_one.astype(jnp.bfloat16)
    qkv_rows = jnp.dot(attn_input, qkv_full, preferred_element_type=jnp.float32).astype(
        jnp.bfloat16
    )
    queries = qkv_rows[:, :width].reshape(block_count, block_rows, HEADS, head_dim)
    keys = qkv_rows[:, width : 2 * width].reshape(token_rows, HEADS, head_dim)
    values = qkv_rows[:, 2 * width :].reshape(token_rows, HEADS, head_dim)
    query_windows = window.reshape(block_count, block_rows)
    block_starts = jnp.arange(block_count, dtype=jnp.int32) * block_rows

    def block_scores(query_block, window_block, block_start):
        scores = (
            jnp.einsum("qhd,khd->hqk", query_block, keys, preferred_element_type=jnp.float32)
            * score_scale
        )
        allowed = allowed_keys(window_block, window, pad_mask, block_start)
        return jnp.where(allowed[None], scores, -1e30)

    def forward_block(inputs):
        query_block, window_block, block_start = inputs
        masked = block_scores(query_block, window_block, block_start)
        largest = jnp.max(masked, axis=-1, keepdims=True)
        raised = jnp.exp(masked - largest)
        total = jnp.sum(raised, axis=-1, keepdims=True)
        probs = (raised / total).astype(jnp.bfloat16)
        mixed = jnp.einsum("hqk,khd->qhd", probs, values, preferred_element_type=jnp.float32)
        return (
            mixed.reshape(block_rows, width).astype(jnp.bfloat16),
            (largest + jnp.log(total))[:, :, 0],
        )

    mixed_blocks, log_totals = lax.map(forward_block, (queries, query_windows, block_starts))
    attended = mixed_blocks.reshape(token_rows, width)
    mid_state = (
        start_state
        + jnp.dot(attended, out_full, preferred_element_type=jnp.float32)
        + out_bias_full.astype(jnp.float32)
    )
    normed_two, pull_two = jax.vjp(
        layer_norm, mid_state, gain_two.astype(jnp.float32), shift_two.astype(jnp.float32)
    )
    mlp_input = normed_two.astype(jnp.bfloat16)
    pre_act = jnp.dot(mlp_input, up_full, preferred_element_type=jnp.float32) + up_bias_full.astype(
        jnp.float32
    )
    activated, pull_act = jax.vjp(gelu_exact, pre_act)
    act_rows = activated.astype(jnp.bfloat16)
    end_state = (
        mid_state
        + jnp.dot(act_rows, down_full, preferred_element_type=jnp.float32)
        + down_bias_full.astype(jnp.float32)
    )
    outputs = end_state.astype(jnp.bfloat16)
    logits = jnp.dot(
        outputs, head_full, preferred_element_type=jnp.float32
    ) + head_bias_full.astype(jnp.float32)
    head_out, pull_head = jax.vjp(partial(expert_softmax, experts=EXPERTS, pixels=PIX), logits)
    up_back, down_back, head_back = (
        lax.all_gather(up_weight, ("dp", "fsdp"), axis=0, tiled=True),
        lax.all_gather(down_weight, ("dp", "fsdp"), axis=0, tiled=True),
        lax.all_gather(head_weight, ("dp", "fsdp"), axis=0, tiled=True),
    )
    qkv_back, out_back = (
        lax.all_gather(qkv_weight, ("dp", "fsdp"), axis=0, tiled=True),
        lax.all_gather(out_weight, ("dp", "fsdp"), axis=0, tiled=True),
    )
    logit_grad = pull_head(head_cotangent.astype(jnp.float32))[0].astype(jnp.bfloat16)
    head_bias_term = jnp.sum(logit_grad.astype(jnp.float32), axis=0)
    head_term = jnp.einsum("td,tn->dn", outputs, logit_grad, preferred_element_type=jnp.float32)
    end_grad = act_cotangent.astype(jnp.float32) + jnp.einsum(
        "tn,dn->td", logit_grad, head_back, preferred_element_type=jnp.float32
    )
    branch_grad = end_grad.astype(jnp.bfloat16)
    down_bias_term = jnp.sum(branch_grad.astype(jnp.float32), axis=0)
    down_term = jnp.einsum("tf,td->fd", act_rows, branch_grad, preferred_element_type=jnp.float32)
    act_grad = jnp.einsum("td,fd->tf", branch_grad, down_back, preferred_element_type=jnp.float32)
    pre_grad = pull_act(act_grad)[0].astype(jnp.bfloat16)
    up_bias_term = jnp.sum(pre_grad.astype(jnp.float32), axis=0)
    up_term = jnp.einsum("td,tf->df", mlp_input, pre_grad, preferred_element_type=jnp.float32)
    normed_two_grad = jnp.einsum("tf,df->td", pre_grad, up_back, preferred_element_type=jnp.float32)
    state_grad_two, gain_two_term, shift_two_term = pull_two(normed_two_grad)
    (
        gain_part,
        shift_part,
        up_part,
        up_bias_part,
        down_part,
        down_bias_part,
        head_part,
        head_bias_part,
    ) = (
        lax.psum_scatter(
            gain_two_term.astype(jnp.bfloat16), "dp", scatter_dimension=0, tiled=True
        ).astype(jnp.float32),
        lax.psum_scatter(
            shift_two_term.astype(jnp.bfloat16), "dp", scatter_dimension=0, tiled=True
        ).astype(jnp.float32),
        lax.psum_scatter(
            up_term.astype(jnp.bfloat16), "dp", scatter_dimension=0, tiled=True
        ).astype(jnp.float32),
        lax.psum_scatter(
            up_bias_term.astype(jnp.bfloat16), "dp", scatter_dimension=0, tiled=True
        ).astype(jnp.float32),
        lax.psum_scatter(
            down_term.astype(jnp.bfloat16), "dp", scatter_dimension=0, tiled=True
        ).astype(jnp.float32),
        lax.psum_scatter(
            down_bias_term.astype(jnp.bfloat16), "dp", scatter_dimension=0, tiled=True
        ).astype(jnp.float32),
        lax.psum_scatter(
            head_term.astype(jnp.bfloat16), "dp", scatter_dimension=0, tiled=True
        ).astype(jnp.float32),
        lax.psum_scatter(
            head_bias_term.astype(jnp.bfloat16), "dp", scatter_dimension=0, tiled=True
        ).astype(jnp.float32),
    )
    rear_grads = (
        lax.psum_scatter(gain_part, "fsdp", scatter_dimension=0, tiled=True),
        lax.psum_scatter(shift_part, "fsdp", scatter_dimension=0, tiled=True),
        lax.psum_scatter(up_part, "fsdp", scatter_dimension=0, tiled=True),
        lax.psum_scatter(up_bias_part, "fsdp", scatter_dimension=0, tiled=True),
        lax.psum_scatter(down_part, "fsdp", scatter_dimension=0, tiled=True),
        lax.psum_scatter(down_bias_part, "fsdp", scatter_dimension=0, tiled=True),
        lax.psum_scatter(head_part, "fsdp", scatter_dimension=0, tiled=True),
        lax.psum_scatter(head_bias_part, "fsdp", scatter_dimension=0, tiled=True),
    )
    mid_grad = end_grad + state_grad_two
    out_grad = mid_grad.astype(jnp.bfloat16)
    out_bias_term = jnp.sum(out_grad.astype(jnp.float32), axis=0)
    out_term = jnp.einsum("td,te->de", attended, out_grad, preferred_element_type=jnp.float32)
    mixed_grad = jnp.einsum(
        "te,de->td", out_grad, out_back, preferred_element_type=jnp.float32
    ).astype(jnp.bfloat16)
    grad_blocks = mixed_grad.reshape(block_count, block_rows, HEADS, head_dim)

    def backward_block(carry, inputs):
        key_sum, value_sum = carry
        query_block, grad_block, window_block, total_block, block_start = inputs
        masked = block_scores(query_block, window_block, block_start)
        probs = jnp.exp(masked - total_block[:, :, None])
        prob_grad = jnp.einsum(
            "qhd,khd->hqk", grad_block, values, preferred_element_type=jnp.float32
        )
        inner = jnp.sum(probs * prob_grad, axis=-1, keepdims=True)
        score_grad = (probs * (prob_grad - inner)).astype(jnp.bfloat16)
        query_grad = (
            jnp.einsum("hqk,khd->qhd", score_grad, keys, preferred_element_type=jnp.float32)
            * score_scale
        )
        key_sum = (
            key_sum
            + jnp.einsum(
                "hqk,qhd->khd", score_grad, query_block, preferred_element_type=jnp.float32
            )
            * score_scale
        )
        value_sum = value_sum + jnp.einsum(
            "hqk,qhd->khd",
            probs.astype(jnp.bfloat16),
            grad_block,
            preferred_element_type=jnp.float32,
        )
        return ((key_sum, value_sum), query_grad.reshape(block_rows, width))

    zero_keys = jnp.zeros((token_rows, HEADS, head_dim), jnp.float32)
    (key_grad, value_grad), query_grads = lax.scan(
        backward_block,
        (zero_keys, zero_keys),
        (queries, grad_blocks, query_windows, log_totals, block_starts),
    )
    qkv_grad = jnp.concatenate(
        [
            query_grads.reshape(token_rows, width),
            key_grad.reshape(token_rows, width),
            value_grad.reshape(token_rows, width),
        ],
        axis=1,
    ).astype(jnp.bfloat16)
    qkv_term = jnp.einsum("td,te->de", attn_input, qkv_grad, preferred_element_type=jnp.float32)
    normed_one_grad = jnp.einsum(
        "te,de->td", qkv_grad, qkv_back, preferred_element_type=jnp.float32
    )
    state_grad_one, gain_one_term, shift_one_term = pull_one(normed_one_grad)
    patch_grad = mid_grad + state_grad_one
    lead_term = lead_hot[:, None] * jnp.sum(patch_grad, axis=0)[None, :]
    lead_part, gain_one_part, shift_one_part, qkv_part, out_part, out_bias_part = (
        lax.psum_scatter(
            lead_term.astype(jnp.bfloat16), "dp", scatter_dimension=1, tiled=True
        ).astype(jnp.float32),
        lax.psum_scatter(
            gain_one_term.astype(jnp.bfloat16), "dp", scatter_dimension=0, tiled=True
        ).astype(jnp.float32),
        lax.psum_scatter(
            shift_one_term.astype(jnp.bfloat16), "dp", scatter_dimension=0, tiled=True
        ).astype(jnp.float32),
        lax.psum_scatter(
            qkv_term.astype(jnp.bfloat16), "dp", scatter_dimension=0, tiled=True
        ).astype(jnp.float32),
        lax.psum_scatter(
            out_term.astype(jnp.bfloat16), "dp", scatter_dimension=0, tiled=True
        ).astype(jnp.float32),
        lax.psum_scatter(
            out_bias_term.astype(jnp.bfloat16), "dp", scatter_dimension=0, tiled=True
        ).astype(jnp.float32),
    )
    front_grads = (
        lax.psum_scatter(lead_part, "fsdp", scatter_dimension=1, tiled=True),
        lax.psum_scatter(gain_one_part, "fsdp", scatter_dimension=0, tiled=True),
        lax.psum_scatter(shift_one_part, "fsdp", scatter_dimension=0, tiled=True),
        lax.psum_scatter(qkv_part, "fsdp", scatter_dimension=0, tiled=True),
        lax.psum_scatter(out_part, "fsdp", scatter_dimension=0, tiled=True),
        lax.psum_scatter(out_bias_part, "fsdp", scatter_dimension=0, tiled=True),
    )
    return (
        outputs,
        head_out,
        patch_grad,
        front_grads[0],
        front_grads[1],
        front_grads[2],
        front_grads[3],
        front_grads[4],
        front_grads[5],
        rear_grads[0],
        rear_grads[1],
        rear_grads[2],
        rear_grads[3],
        rear_grads[4],
        rear_grads[5],
        rear_grads[6],
        rear_grads[7],
    )


def solution(mesh):
    in_specs = (
        P(("dp", "fsdp"), None),
        P(("dp", "fsdp")),
        P(("dp", "fsdp"), None),
        P(("dp", "fsdp")),
        P(None, ("dp", "fsdp")),
        P(("dp", "fsdp")),
        P(("dp", "fsdp")),
        P(("dp", "fsdp"), None),
        P(("dp", "fsdp"), None),
        P(("dp", "fsdp")),
        P(("dp", "fsdp")),
        P(("dp", "fsdp")),
        P(("dp", "fsdp"), None),
        P(("dp", "fsdp")),
        P(("dp", "fsdp"), None),
        P(("dp", "fsdp")),
        P(("dp", "fsdp"), None),
        P(("dp", "fsdp")),
        P(("dp", "fsdp"), None),
        P(("dp", "fsdp"), None),
    )
    out_specs = (
        P(("dp", "fsdp"), None),
        P(("dp", "fsdp"), None),
        P(("dp", "fsdp"), None),
        P(None, ("dp", "fsdp")),
        P(("dp", "fsdp")),
        P(("dp", "fsdp")),
        P(("dp", "fsdp"), None),
        P(("dp", "fsdp"), None),
        P(("dp", "fsdp")),
        P(("dp", "fsdp")),
        P(("dp", "fsdp")),
        P(("dp", "fsdp"), None),
        P(("dp", "fsdp")),
        P(("dp", "fsdp"), None),
        P(("dp", "fsdp")),
        P(("dp", "fsdp"), None),
        P(("dp", "fsdp")),
    )
    body = shards if dict(mesh.shape) == {"dp": 4, "fsdp": 8} else plain_shards
    return jax.shard_map(body, mesh=mesh, in_specs=in_specs, out_specs=out_specs, check_vma=False)
```

```python
import math
from functools import partial

import jax
import jax.numpy as jnp
from jax import lax
from jax.experimental import pallas as pl
from jax.experimental.pallas import tpu as pltpu
from jax.sharding import PartitionSpec as P

HEADS = 12
PIX = 64
EXPERTS = 3
LEADS = 16


norm_epsilon = 1e-05
score_scale = 0.125


def layer_norm(hidden, norm_gain, norm_shift):
    average = jnp.mean(hidden, axis=-1, keepdims=True)
    centered = hidden - average
    variance = jnp.mean(centered * centered, axis=-1, keepdims=True)
    return centered * lax.rsqrt(variance + norm_epsilon) * norm_gain + norm_shift


def gelu_exact(values):
    return 0.5 * values * (1.0 + lax.erf(values * 0.7071067811865476))


def expert_softmax(logits, experts, pixels):
    gate_part = logits[:, : experts * pixels].reshape(logits.shape[0], experts, pixels)
    largest = jnp.max(gate_part, axis=1, keepdims=True)
    raised = jnp.exp(gate_part - largest)
    shares = raised / jnp.sum(raised, axis=1, keepdims=True)
    return jnp.concatenate(
        [shares.reshape(logits.shape[0], experts * pixels), logits[:, experts * pixels :]], axis=1
    )


def allowed_keys(query_window, key_window, key_valid, query_start):
    query_place = query_start + jnp.arange(query_window.shape[0], dtype=jnp.int32)
    key_place = jnp.arange(key_window.shape[0], dtype=jnp.int32)
    same_window = query_window[:, None] == key_window[None, :]
    usable = (key_valid[None, :] > 0) | (query_place[:, None] == key_place[None, :])
    return same_window & usable


AXES = ("dp", "fsdp")
FAR_Z, NEAR_Z, FIRST, SECOND, SIBLING = (4, 4), (2, 2), (8, 16), (16, 8), (1, 1)
ORDERS = {
    "q": (FAR_Z, NEAR_Z, FIRST, SECOND),
    "u": (FAR_Z, FIRST, SECOND, NEAR_Z),
    "d": (FIRST, FAR_Z, NEAR_Z, SECOND),
    "h": (NEAR_Z, FAR_Z, FIRST, SECOND),
    "head": (FAR_Z, NEAR_Z, FIRST, SECOND),
    "down": (FAR_Z, NEAR_Z, FIRST, SECOND),
    "up": (FAR_Z, FIRST, SECOND, NEAR_Z),
    "front": (FAR_Z, NEAR_Z, FIRST, SECOND),
    "mix": (FAR_Z, NEAR_Z, FIRST, SECOND),
}
GATHER_SEQUENCE = (
    ("q", 0), ("d", 0), ("h", 0), ("u", 0), ("q", 1), ("d", 1), ("u", 1), ("q", 2), ("h", 1), ("u", 2),
    ("d", 2),
)
MOST_VMEM, SPARE_VMEM = 60 * 1024 * 1024, 8 * 1024 * 1024
WIDTH = 768
HIDDEN = 3072
HEAD = 4608
TOKENS = 512
GATE = 512
F32 = jnp.float32
BF16 = jnp.bfloat16
HBM = pl.BlockSpec(memory_space=pltpu.HBM)
SMEM = pl.BlockSpec(memory_space=pltpu.SMEM)
VMEM = pl.BlockSpec(memory_space=pltpu.VMEM)
QKV_PART, SMALL_PART = (0, 1152), (1152, 128)
UP_PART, OUT_PART, GATE_PART = (0, 1536), (1536, 384), (1920, 256)
DOWN_PART, HEAD_PART = (0, 384), (0, 2048)


def chip_masks(order, lane):
    masks = []
    for place in range(16):
        mask = 0
        for step in range(4):
            if place >> step & 1:
                mask ^= order[step][lane]
        masks.append(mask >> 1)
    return masks


def table_start(group, side):
    return 1 + 32 * list(ORDERS).index(group) + 16 * side


def exchange(array, masks):
    return lax.ppermute(array, AXES, [(d, d ^ masks[d & 1]) for d in range(32)])


def whereabouts():
    device = lax.axis_index("dp") * 8 + lax.axis_index("fsdp")
    core, chip = device % 2, device // 2
    tables = [chip_masks(order, 0) + chip_masks(order, 1) for order in ORDERS.values()]
    swapped = [chip_masks(order, 1) + chip_masks(order, 0) for order in ORDERS.values()]
    places = jnp.where(core == 0, jnp.array(tables, jnp.int32), jnp.array(swapped, jnp.int32))
    places = (places ^ chip).reshape(32 * len(ORDERS))
    return core, jnp.concatenate([core[None].astype(jnp.int32), places])


def after(value, *marks):
    return lax.optimization_barrier((value, marks))[0]


def in_core_order(core, mine, theirs, axis):
    return jnp.where(
        core == 0,
        jnp.concatenate([mine, theirs], axis=axis),
        jnp.concatenate([theirs, mine], axis=axis),
    )


def pack_kernel(core, qkv, out, up, down, head, table, *refs):
    vectors, (up_bias, head_bias), refs = refs[:6], refs[6:8], refs[8:]
    outs, (rows,) = refs[:8], refs[8:]
    rows[...] = jnp.zeros_like(rows)
    for index, vector in enumerate(vectors):
        rows[index : index + 1, :24] = vector[...].astype(F32)
    for index in range(4):
        rows[6 + index : 7 + index, :24] = up_bias[:, 24 * index : 24 * index + 24].astype(F32)
    for index in range(6):
        rows[10 + index : 11 + index, :24] = head_bias[:, 24 * index : 24 * index + 24].astype(F32)
    rows[16:32, :24] = table[...].astype(F32)
    small = rows[...].T[:24].astype(BF16)
    for side in range(2):
        q, u, d, h = outs[4 * side : 4 * side + 4]
        q[:, :1152] = qkv[:, lane_columns(core, side, 1152)]
        q[:, 1152:] = small
        u[:, :1536] = up[:, lane_columns(core, side, 1536)]
        u[:, 1536:1920] = out[:, lane_columns(core, side, 384)]
        u[:, 1920:] = head[:, lane_columns(core, side, 256)]
        d[...] = down[:, lane_columns(core, side, 384)]
        h[...] = head[:, lane_columns(core, side, 2048, GATE)]


def packed(core, weights, table, vectors):
    shapes = [(24, 1280), (24, 2176), (96, 384), (24, 2048)] * 2
    return call(
        pack_kernel,
        (core.reshape(1), *weights, table, *[vector[None] for vector in vectors]),
        [SMEM] + [VMEM] * 14,
        [(shape, BF16, False) for shape in shapes],
        [pltpu.VMEM((128, 128), F32)],
    )


def doubled(held, masks):
    return jnp.concatenate([held, exchange(held, masks)], axis=0)


def both_lanes(*arrays):
    return arrays + tuple(exchange(array, SIBLING) for array in arrays)


def total(first, second):
    return first.astype(F32) + second.astype(F32)


def folded(keep, got, start=0):
    half = got.shape[0] // 2
    send = total(keep[half:], got[half:]).astype(BF16)
    return total(keep[:half], got[:half]).astype(BF16), send


def finished(keep, got, core, widths):
    block = total(keep, got)[0]
    rows = block.shape[0] // 2
    upper, lower = block[:rows], block[rows:]
    mine = jnp.where(core == 0, upper, lower)
    theirs = jnp.where(core == 0, lower, upper).astype(BF16)
    other = exchange(theirs, SIBLING).astype(F32)
    pieces, start = [], 0
    for width in widths:
        span = slice(start, start + width)
        pieces.append(in_core_order(core, mine[:, span], other[:, span], 1))
        start += width
    return pieces


def across(first, second):
    return lax.dot_general(first, second, (((1,), (1,)), ((), ())), preferred_element_type=F32)


def times(first, second):
    return jnp.dot(first, second, preferred_element_type=F32)


def lane_columns(where, side, stride, first=0, width=None):
    return pl.ds(pl.multiple_of(first + (where[0] ^ side) * stride, 128), width or stride)


def block_copies(where, group, sources, part, target, sems, side, first=0):
    start, width = part
    rows = sources[0].shape[1]
    half = len(sources) // 2
    count = 16 // half
    copies = []
    for place in range(16):
        row = pl.multiple_of(where[table_start(group, side) + place] * rows, rows)
        copies.append(
            pltpu.make_async_copy(
                sources[half * side + place // count].at[place % count, :, pl.ds(start, width)],
                target.at[pl.ds(row, rows), lane_columns(where, side, width, first)],
                sems.at[side, place],
            )
        )
    return copies


def start_all(copies):
    for copy in copies:
        copy.start()


def wait_all(copies):
    for copy in copies:
        copy.wait()


def mean_and_scale(hidden):
    average = jnp.mean(hidden, axis=1, keepdims=True)
    centered = hidden - average
    variance = jnp.mean(centered * centered, axis=1, keepdims=True)
    return centered, lax.rsqrt(variance + norm_epsilon)


def norm_backward(hidden, gain, upstream):
    centered, scale = mean_and_scale(hidden)
    normed = centered * scale
    gain_grad = jnp.sum(upstream * normed, axis=0, keepdims=True)
    shift_grad = jnp.sum(upstream, axis=0, keepdims=True)
    scaled = upstream * gain
    first = jnp.mean(scaled, axis=1, keepdims=True)
    second = jnp.mean(scaled * normed, axis=1, keepdims=True)
    return scale * (scaled - first - normed * second), gain_grad, shift_grad


def call(kernel, operands, in_specs, outs, scratch, spare=None):
    def size(item):
        return math.prod(item.shape) * jnp.dtype(item.dtype).itemsize

    held = [item for item, spec in zip(operands, in_specs) if spec is VMEM]
    held += [jax.ShapeDtypeStruct(shape, kind) for shape, kind, copied in outs if not copied]
    held += [item for item in scratch if getattr(item, "memory_space", None) == pltpu.VMEM]
    limit = MOST_VMEM if spare is None else sum(size(item) for item in held) + spare
    return pl.pallas_call(
        kernel,
        out_shape=[jax.ShapeDtypeStruct(shape, kind) for shape, kind, _ in outs],
        in_specs=in_specs,
        out_specs=[HBM if copied else VMEM for _, _, copied in outs],
        scratch_shapes=scratch,
        compiler_params=pltpu.CompilerParams(vmem_limit_bytes=limit),
        cost_estimate=pl.CostEstimate(flops=2 * 10**12, bytes_accessed=10**10, transcendentals=0),
    )(*operands)


def lane_scratch(rows, width):
    return [pltpu.VMEM((2, rows, width), BF16), pltpu.SemaphoreType.DMA((2, 16))]


def weight_scratch(rows, width):
    return [pltpu.VMEM((rows, width), BF16), pltpu.SemaphoreType.DMA((2, 16))]


def taken(refs, *counts):
    groups = []
    for count in counts:
        groups.append(refs[:count])
        refs = refs[count:]
    return *groups, refs


def front_kernel(where, lead, patches, *refs):
    sources, outs, scratch = taken(refs, 4, 3)
    turned_out, qkv_out, small = outs
    weight, sems, smalls, small_sems, state, rows, turned, qkv, io_sems = scratch
    loads = [block_copies(where, "q", sources, QKV_PART, weight, sems, side) for side in range(2)]
    small_loads = []
    for place in range(16):
        row = pl.multiple_of(where[table_start("q", 0) + place] * 48, 48)
        small_loads.append(
            pltpu.make_async_copy(
                sources[place // 8].at[place % 8, :, pl.ds(*SMALL_PART)],
                smalls.at[pl.ds(row, 48), :],
                small_sems.at[place],
            )
        )
    state_load = pltpu.make_async_copy(patches, state, io_sems.at[0])
    start_all(small_loads)
    state_load.start()
    start_all(loads[0])
    start_all(loads[1])
    wait_all(small_loads)
    columns = smalls[...].astype(F32).T
    places = lax.broadcasted_iota(jnp.int32, (LEADS, WIDTH), 0)
    lead_row = jnp.sum(
        jnp.where(places == lead[0], columns[16 : 16 + LEADS], 0.0), axis=0, keepdims=True
    )
    small[...] = columns[:32]
    small[16:17, :] = lead_row
    state_load.wait()
    centered, scale = mean_and_scale(state[...].astype(F32) + lead_row)
    rows[...] = (centered * scale * columns[0:1] + columns[1:2]).astype(BF16)
    turned[...] = rows[...].T
    stores = [pltpu.make_async_copy(turned, turned_out, io_sems.at[1])]
    stores[0].start()
    wait_all(loads[0] + loads[1])
    for part in range(3):
        span = slice(part * WIDTH, part * WIDTH + WIDTH)
        qkv[:, span] = times(rows[...], weight[:, span]).astype(BF16)
        stores.append(pltpu.make_async_copy(qkv.at[:, span], qkv_out.at[:, span], io_sems.at[2 + part]))
        stores[-1].start()
    wait_all(stores)


def front_forward(where, lead_index, patches, arrays):
    return call(
        front_kernel,
        (where, lead_index, patches, *arrays),
        [SMEM, SMEM, HBM] + [HBM] * 4,
        [
            ((WIDTH, TOKENS), BF16, True),
            ((TOKENS, 3 * WIDTH), BF16, True),
            ((32, WIDTH), F32, False),
        ],
        weight_scratch(WIDTH, 3 * WIDTH)
        + [pltpu.VMEM((WIDTH, 128), BF16), pltpu.SemaphoreType.DMA((16,))]
        + [
            pltpu.VMEM((TOKENS, WIDTH), BF16),
            pltpu.VMEM((TOKENS, WIDTH), BF16),
            pltpu.VMEM((WIDTH, TOKENS), BF16),
            pltpu.VMEM((TOKENS, 3 * WIDTH), BF16),
            pltpu.SemaphoreType.DMA((5,)),
        ],
    )


KEY_SPANS = ((0, 256), (0, 384), (128, 512), (256, 512))


def fill_bias(lengths, pad, bias):
    ends, end = [], 0
    for index in range(lengths.shape[1]):
        end = end + lengths[0, index]
        ends.append(end)

    def windows(places):
        return sum([(places >= end).astype(jnp.int32) for end in ends])

    for block, (low, high) in enumerate(KEY_SPANS):
        count = high - low
        queries = lax.broadcasted_iota(jnp.int32, (1, 128), 1) + 128 * block
        keys = lax.broadcasted_iota(jnp.int32, (count, 1), 0) + low
        same = windows(queries) == windows(keys)
        usable = (pad[low:high, :] > 0) | (queries == keys)
        bias[block, :count, :] = jnp.where(same & usable, 0.0, -1e30)


def two_heads(block):
    first = lax.broadcasted_iota(jnp.int32, block.shape, 1) < block.shape[1] // 2
    zero = jnp.zeros_like(block)
    return jnp.concatenate([jnp.where(first, block, zero), jnp.where(first, zero, block)], axis=0)


def head_rows_of(stacked):
    return jnp.concatenate([stacked[:64, :128], stacked[64:, 128:]], axis=0)


def probabilities(scores, allowed):
    masked = scores * score_scale + allowed
    raised = jnp.exp(masked - jnp.max(masked, axis=0, keepdims=True))
    return raised * (1.0 / jnp.sum(raised, axis=0, keepdims=True))


def attention_kernel(where, lengths, pad, qkv, attended_out, turned_out, bias, turned, rows, sems):
    fill_bias(lengths, pad, bias)

    def pair(index, carry):
        first = index * 128
        columns = pl.ds(pl.multiple_of(first, 128), 128)
        keys_at = pl.ds(pl.multiple_of(first + WIDTH, 128), 128)
        values = qkv[:, pl.ds(pl.multiple_of(first + 2 * WIDTH, 128), 128)].T
        for block, (low, high) in enumerate(KEY_SPANS):
            span = slice(128 * block, 128 * block + 128)
            scores = across(qkv[low:high, keys_at], two_heads(qkv[span, columns]))
            allowed = bias[block, : high - low, :]
            probs = [
                probabilities(scores[:, 128 * head : 128 * head + 128], allowed).astype(BF16)
                for head in range(2)
            ]
            mixed = times(values[:, low:high], jnp.concatenate(probs, axis=1))
            turned[columns, span] = head_rows_of(mixed).astype(BF16)
        return carry

    lax.fori_loop(0, WIDTH // 128, pair, 0)
    stores = [pltpu.make_async_copy(turned, turned_out, sems.at[0])]
    stores[0].start()
    rows[...] = turned[...].T
    stores.append(pltpu.make_async_copy(rows, attended_out, sems.at[1]))
    stores[1].start()
    wait_all(stores)


def attention_forward(where, lengths, pad, qkv):
    rows, columns = (TOKENS, WIDTH), (WIDTH, TOKENS)
    return call(
        attention_kernel,
        (where, lengths, pad, qkv),
        [SMEM, SMEM, VMEM, VMEM],
        [(rows, BF16, True), (columns, BF16, True)],
        [
            pltpu.VMEM((4, 384, 128), F32),
            pltpu.VMEM(columns, BF16),
            pltpu.VMEM(rows, BF16),
            pltpu.SemaphoreType.DMA((2,)),
        ],
    )


def gate_shares(logits, cotangent, shares, gate_grad):
    gate_grad[:, 256:] = cotangent[:, 256:GATE]
    first, rest = logits[:, :128], logits[:, 128:256]
    left = lax.broadcasted_iota(jnp.int32, first.shape, 1) < PIX
    third = jnp.where(left, rest, pltpu.roll(rest, PIX, 1))
    largest = jnp.maximum(jnp.maximum(first, pltpu.roll(first, PIX, 1)), third)
    raised, raised_third = jnp.exp(first - largest), jnp.exp(third - largest)
    scale = 1.0 / (raised + pltpu.roll(raised, PIX, 1) + raised_third)
    share, share_third = raised * scale, raised_third * scale
    shares[:, :128] = share
    shares[:, 128:256] = jnp.where(left, share_third, rest)
    pull, other = cotangent[:, :128].astype(F32), cotangent[:, 128:256].astype(F32)
    pull_third = jnp.where(left, other, pltpu.roll(other, PIX, 1))
    weighed = share * pull
    inner = weighed + pltpu.roll(weighed, PIX, 1) + share_third * pull_third
    gate_grad[:, :128] = (share * (pull - inner)).astype(BF16)
    gate_grad[:, 128:256] = jnp.where(left, share_third * (pull_third - inner), other).astype(BF16)


def head_kernel(where, rows, gate_out, bias, *refs):
    sources, outs, scratch = taken(refs, 4, 1)
    (out,) = outs
    weight, sems, inputs, result, io_sems = scratch
    loads = [block_copies(where, "h", sources, HEAD_PART, weight, sems, side) for side in range(2)]
    row_load = pltpu.make_async_copy(rows, inputs, io_sems.at[0])
    gate_load = pltpu.make_async_copy(gate_out, result.at[:, :GATE], io_sems.at[1])
    row_load.start()
    start_all(loads[0])
    start_all(loads[1])
    gate_load.start()
    row_load.wait()
    stores = []

    def store(span):
        stores.append(
            pltpu.make_async_copy(result.at[:, span], out.at[:, span], io_sems.at[2 + len(stores)])
        )
        stores[-1].start()

    for side in range(2):
        wait_all(loads[side])
        for tile in range(4):
            span = lane_columns(where, side, 2048, GATE + tile * 512, 512)
            columns = lane_columns(where, side, 2048, tile * 512, 512)
            result[:, span] = times(inputs[...], weight[:, columns]) + bias[:, span]
            store(span)
    gate_load.wait()
    store(pl.ds(0, GATE))
    wait_all(stores)


def head_forward(where, rows, gate_out, bias, arrays):
    return call(
        head_kernel,
        (where, rows, gate_out, bias, *arrays),
        [SMEM, HBM, HBM, VMEM] + [HBM] * 4,
        [((TOKENS, HEAD), F32, True)],
        weight_scratch(WIDTH, HEAD - GATE)
        + [
            pltpu.VMEM((TOKENS, WIDTH), BF16),
            pltpu.VMEM((TOKENS, HEAD), F32),
            pltpu.SemaphoreType.DMA((11,)),
        ],
        spare=SPARE_VMEM,
    )[0]


def send_lane(where, group, lane, out, sems, side):
    rows = out.shape[1]
    copies = []
    for place in range(16):
        row = pl.multiple_of(where[table_start(group, side) + place] * rows, rows)
        copies.append(
            pltpu.make_async_copy(lane.at[pl.ds(row, rows), :], out.at[place], sems.at[place])
        )
    start_all(copies)
    return copies


def middle_kernel(
    where, small, up_bias, head_bias, attended, patches, cotangent, act_cotangent, attended_turned,
    *refs,
):
    up_sources, down_sources, head_sources, outs, scratch = taken(refs, 4, 4, 4, 15)
    outputs, shares, gate_bias, down_bias, up_bias_sum, terms, mid_grad, out_grad, mixed, *grads = outs
    down_mine, down_theirs, up_mine, up_theirs, head_mine, head_theirs = grads
    out_weight, out_sems, up, up_sems, down, down_sems, scratch = *scratch[:6], scratch[6:]
    head, head_sems, gate_sems, rows, branch, mid, mlp_turned, scratch = *scratch[:7], scratch[7:]
    act, act_turned, slope, turned, pulls, act_pulls, gate_grad, scratch = *scratch[:7], scratch[7:]
    lane, lane_sems, down_lane, down_lane_sems, mixes, more_sems, io_sems = scratch

    def loads(group, sources, part, target, sems, first=0):
        copies = []
        for side in range(2):
            copies += block_copies(where, group, sources, part, target, sems, side, first)
        return copies

    state_loads = [
        pltpu.make_async_copy(attended, rows, io_sems.at[0]),
        pltpu.make_async_copy(patches, branch, io_sems.at[1]),
    ]
    out_loads = loads("u", up_sources, OUT_PART, out_weight, out_sems)
    up_loads = loads("u", up_sources, UP_PART, up, up_sems)
    down_loads = loads("d", down_sources, DOWN_PART, down, down_sems)
    gate_loads = loads("u", up_sources, GATE_PART, head, gate_sems)
    head_loads = loads("h", head_sources, HEAD_PART, head, head_sems, GATE)
    pull_load = pltpu.make_async_copy(cotangent, pulls, io_sems.at[2])
    act_load = pltpu.make_async_copy(act_cotangent, act_pulls, io_sems.at[3])
    mix_load = pltpu.make_async_copy(attended_turned, mixes, io_sems.at[4])
    start_all(state_loads + out_loads + up_loads + down_loads + gate_loads)
    pull_load.start()
    start_all(head_loads)
    act_load.start()
    mix_load.start()

    wait_all(state_loads + out_loads)
    mid[...] = (
        branch[...].astype(F32)
        + small[16:17, :]
        + times(rows[...], out_weight[...])
        + small[2:3, :]
    )
    centered, scale = mean_and_scale(mid[...])
    rows[...] = (centered * scale * small[3:4, :] + small[4:5, :]).astype(BF16)
    mlp_turned[...] = rows[...].T
    wait_all(up_loads)
    for tile in range(6):
        span = slice(tile * 512, tile * 512 + 512)
        values = times(rows[...], up[:, span]) + up_bias[:, span]
        share = 0.5 * (1.0 + lax.erf(values * 0.7071067811865476))
        density = jnp.exp(-0.5 * values * values) * 0.3989422804014327
        activated = (values * share).astype(BF16)
        act[:, span] = activated
        act_turned[span, :] = activated.T
        slope[:, span] = (share + values * density).astype(BF16)
    wait_all(down_loads)
    outputs[...] = (mid[...] + times(act[...], down[...]) + small[5:6, :]).astype(BF16)
    turned[...] = outputs[...].T
    wait_all(gate_loads)
    shares[...] = times(outputs[...], head[:, :GATE]) + head_bias[:, :GATE]
    pull_load.wait()
    gate_shares(shares, pulls, shares, gate_grad)
    gate_bias[...] = jnp.sum(gate_grad[...].astype(F32), axis=0, keepdims=True)
    pulls[:, :GATE] = gate_grad[...]

    def head_lane(side, target, sems, out):
        target[:, :256] = times(turned[...], pulls[:, lane_columns(where, side, 256)]).astype(BF16)
        for tile in range(4):
            span = lane_columns(where, side, 2048, GATE + tile * 512, 512)
            target[:, 256 + tile * 512 : 768 + tile * 512] = times(turned[...], pulls[:, span]).astype(
                BF16
            )
        return send_lane(where, "head", target, out, sems, side)

    def down_lane_of(side, out):
        columns = branch[:, lane_columns(where, side, 384)]
        for part in range(4):
            span = slice(part * WIDTH, part * WIDTH + WIDTH)
            down_lane[span, :] = times(act_turned[span, :], columns).astype(BF16)
        return send_lane(where, "down", down_lane, out, down_lane_sems, side)

    def up_lane(side, target, sems, out):
        for tile in range(3):
            span = lane_columns(where, side, 1536, tile * 512, 512)
            target[:, tile * 512 : tile * 512 + 512] = times(mlp_turned[...], slope[:, span]).astype(
                BF16
            )
        target[:, 1536:1920] = times(
            mixes[...], out_grad[:, lane_columns(where, side, 384)]
        ).astype(BF16)
        return send_lane(where, "up", target, out, sems, side)

    first_stores = head_lane(1, lane, lane_sems, head_theirs)
    act_load.wait()
    wait_all(head_loads)
    mid_grad[...] = act_pulls[...].astype(F32) + across(pulls[...], head[...])
    branch[...] = mid_grad[...].astype(BF16)
    down_bias[...] = jnp.sum(branch[...].astype(F32), axis=0, keepdims=True)
    stores = head_lane(0, head.at[:, :2304], more_sems.at[0], head_mine)
    down_stores = down_lane_of(1, down_theirs)
    for tile in range(6):
        span = slice(tile * 512, tile * 512 + 512)
        grad = across(branch[...], down[span, :])
        rounded = (slope[:, span].astype(F32) * grad).astype(BF16)
        slope[:, span] = rounded
        up_bias_sum[:, span] = jnp.sum(rounded.astype(F32), axis=0, keepdims=True)
    wait_all(down_stores)
    stores += down_lane_of(0, down_mine)
    grad = across(slope[...], up[...])
    pulled, gain_grad, shift_grad = norm_backward(mid[...], small[3:4, :], grad)
    pulled = pulled + mid_grad[...]
    rounded = pulled.astype(BF16)
    mid_grad[...] = pulled
    out_grad[...] = rounded
    terms[...] = jnp.zeros_like(terms)
    terms[0:1, :] = jnp.sum(rounded.astype(F32), axis=0, keepdims=True)
    terms[1:2, :] = gain_grad
    terms[2:3, :] = shift_grad
    mix_load.wait()
    stores += up_lane(1, head.at[:, 2304:4224], more_sems.at[1], up_theirs)
    wait_all(first_stores)
    stores += up_lane(0, lane.at[:, :1920], lane_sems, up_mine)
    mixed[...] = across(out_grad[...], out_weight[...]).astype(BF16)
    wait_all(stores)


def middle(
    where, small, up_bias, head_bias, attended, patches, cotangent, act_cotangent, attended_turned,
    up, down, head,
):
    rows, columns = (TOKENS, WIDTH), (WIDTH, TOKENS)
    wide, tall = (TOKENS, HIDDEN), (HIDDEN, TOKENS)
    return call(
        middle_kernel,
        (
            where, small, up_bias, head_bias, attended, patches, cotangent, act_cotangent,
            attended_turned, *up, *down, *head,
        ),
        [SMEM, VMEM, VMEM, VMEM] + [HBM] * 17,
        [
            (rows, BF16, False),
            ((TOKENS, GATE), F32, False),
            ((1, GATE), F32, False),
            ((1, WIDTH), F32, False),
            ((1, HIDDEN), F32, False),
            ((8, WIDTH), F32, False),
            (rows, F32, False),
            (rows, BF16, False),
            (rows, BF16, False),
            ((16, 192, 384), BF16, True),
            ((16, 192, 384), BF16, True),
            ((16, 48, 1920), BF16, True),
            ((16, 48, 1920), BF16, True),
            ((16, 48, 2304), BF16, True),
            ((16, 48, 2304), BF16, True),
        ],
        weight_scratch(WIDTH, WIDTH)
        + weight_scratch(WIDTH, HIDDEN)
        + weight_scratch(HIDDEN, WIDTH)
        + weight_scratch(WIDTH, HEAD)
        + [
            pltpu.SemaphoreType.DMA((2, 16)),
            pltpu.VMEM(rows, BF16),
            pltpu.VMEM(rows, BF16),
            pltpu.VMEM(rows, F32),
            pltpu.VMEM(columns, BF16),
            pltpu.VMEM(wide, BF16),
            pltpu.VMEM(tall, BF16),
            pltpu.VMEM(wide, BF16),
            pltpu.VMEM(columns, BF16),
            pltpu.VMEM((TOKENS, HEAD), BF16),
            pltpu.VMEM(rows, BF16),
            pltpu.VMEM((TOKENS, GATE), BF16),
            pltpu.VMEM((WIDTH, 2304), BF16),
            pltpu.SemaphoreType.DMA((16,)),
            pltpu.VMEM((HIDDEN, 384), BF16),
            pltpu.SemaphoreType.DMA((16,)),
            pltpu.VMEM(columns, BF16),
            pltpu.SemaphoreType.DMA((2, 16)),
            pltpu.SemaphoreType.DMA((5,)),
        ],
    )


def attend_back(count, qkv, mixed, bias, turned, key_sum, value_sum, qkv_grad):
    width = 128 * count

    def columns_at(first):
        return pl.ds(pl.multiple_of(first, 128), 128)

    def pair(index, carry):
        own = index * 128
        columns, keys_at = columns_at(own), columns_at(own + width)
        values_at = columns_at(own + 2 * width)
        keys_turned = qkv[:, keys_at].T
        key_sum[...] = jnp.zeros_like(key_sum)
        value_sum[...] = jnp.zeros_like(value_sum)
        for block, (low, high) in enumerate(KEY_SPANS):
            span = slice(128 * block, 128 * block + 128)
            queries, grads = two_heads(qkv[span, columns]), two_heads(mixed[span, columns])
            scores = across(qkv[low:high, keys_at], queries)
            prob_grads = across(qkv[low:high, values_at], grads)
            allowed = bias[block, : high - low, :]
            probs, score_grads = [], []
            for head in range(2):
                part = slice(128 * head, 128 * head + 128)
                prob = probabilities(scores[:, part], allowed)
                pulled = prob * prob_grads[:, part]
                inner = jnp.sum(pulled, axis=0, keepdims=True)
                probs.append(prob.astype(BF16))
                score_grads.append((pulled - prob * inner).astype(BF16))
            score_grad = jnp.concatenate(score_grads, axis=1)
            key_sum[low:high, :] += times(score_grad, queries)
            value_sum[low:high, :] += times(jnp.concatenate(probs, axis=1), grads)
            turned[:, span] = head_rows_of(times(keys_turned[:, low:high], score_grad)) * score_scale
        qkv_grad[:, columns] = turned[...].T.astype(BF16)
        qkv_grad[:, keys_at] = (key_sum[...] * score_scale).astype(BF16)
        qkv_grad[:, values_at] = value_sum[...].astype(BF16)
        return carry

    lax.fori_loop(0, count, pair, 0)


def attention_scratch(count):
    return [
        pltpu.VMEM((4, 384, 128), F32),
        pltpu.VMEM((TOKENS, 384 * count), BF16),
        pltpu.VMEM((TOKENS, 128 * count), BF16),
        pltpu.VMEM((128, TOKENS), F32),
        pltpu.VMEM((TOKENS, 128), F32),
        pltpu.VMEM((TOKENS, 128), F32),
        pltpu.SemaphoreType.DMA((4,)),
    ]


def attention_loads(start, count, qkv, mixed, own_qkv, own_mixed, sems):
    width = 128 * count
    copies = [
        pltpu.make_async_copy(
            mixed.at[:, pl.ds(128 * start, width)], own_mixed.at[:, pl.ds(0, width)], sems.at[3]
        )
    ]
    for part in range(3):
        copies.append(
            pltpu.make_async_copy(
                qkv.at[:, pl.ds(WIDTH * part + 128 * start, width)],
                own_qkv.at[:, pl.ds(width * part, width)],
                sems.at[part],
            )
        )
    return copies


def early_back_kernel(where, lengths, pad, mixed, qkv, input_turned, *refs):
    (qkv_grad, mine_out, theirs_out), scratch = taken(refs, 3)
    bias, own_qkv, own_mixed, turned, key_sum, value_sum, sems, scratch = *scratch[:7], scratch[7:]
    lane, lane_sems, inputs, io_sems = scratch
    loads = attention_loads(0, 4, qkv, mixed, own_qkv, own_mixed, sems)
    in_load = pltpu.make_async_copy(input_turned, inputs, io_sems.at[0])
    start_all(loads + [in_load])
    fill_bias(lengths, pad, bias)
    wait_all(loads)
    attend_back(4, own_qkv, own_mixed, bias, turned, key_sum, value_sum, qkv_grad)
    in_load.wait()
    stores = []
    for side, out in ((1, theirs_out), (0, mine_out)):
        lane[side] = times(inputs[...], qkv_grad[:, lane_columns(where, side, 768)]).astype(BF16)
        stores += send_lane(where, "front", lane.at[side], out, lane_sems.at[side], side)
    wait_all(stores)


def early_backward(where, lengths, pad, mixed, qkv, input_turned):
    return call(
        early_back_kernel,
        (where, lengths, pad, mixed, qkv, input_turned),
        [SMEM, SMEM, VMEM] + [HBM] * 3,
        [
            ((TOKENS, 1536), BF16, False),
            ((16, 48, 768), BF16, True),
            ((16, 48, 768), BF16, True),
        ],
        attention_scratch(4)
        + lane_scratch(WIDTH, 768)
        + [pltpu.VMEM((WIDTH, TOKENS), BF16), pltpu.SemaphoreType.DMA((1,))],
    )


def late_back_kernel(
    where, lead, lengths, pad, small, terms, down_row, up_rows, head_rows,
    mixed, qkv, first_grad, patches, mid_grad, input_turned, *refs
):
    sources, (patch_out, mine_out, theirs_out), scratch = taken(refs, 4, 3)
    bias, own_qkv, own_mixed, turned, key_sum, value_sum, sems, scratch = *scratch[:7], scratch[7:]
    weight, weight_sems, lane, lane_sems, pulls, late_pulls, scratch = *scratch[:6], scratch[6:]
    state, mids, inputs, patch_grad, small_grad, io_sems = scratch
    own_loads = attention_loads(4, 2, qkv, mixed, own_qkv, own_mixed, sems)
    loads = [
        block_copies(where, "q", sources, QKV_PART, weight, weight_sems, side) for side in range(2)
    ]
    pairs = [(patches, state), (mid_grad, mids), (input_turned, inputs)]
    for part in range(3):
        target = pulls.at[:, pl.ds(WIDTH * part, 512)]
        pairs.append((first_grad.at[:, pl.ds(512 * part, 512)], target))
    in_loads = [pltpu.make_async_copy(*pair, io_sems.at[at]) for at, pair in enumerate(pairs)]
    start_all(own_loads + loads[0] + loads[1] + in_loads)
    fill_bias(lengths, pad, bias)
    wait_all(own_loads)
    attend_back(2, own_qkv, own_mixed, bias, turned, key_sum, value_sum, late_pulls)
    wait_all(loads[0] + loads[1] + in_loads)
    for part in range(3):
        pulls[:, WIDTH * part + 512 : WIDTH * part + 768] = late_pulls[
            :, 256 * part : 256 * part + 256
        ]
    grad = across(pulls[...], weight[...])
    pulled, gain_grad, shift_grad = norm_backward(
        state[...].astype(F32) + small[16:17, :], small[0:1, :], grad
    )
    pulled = pulled + mids[...]
    patch_grad[...] = pulled
    stores = [pltpu.make_async_copy(patch_grad, patch_out, io_sems.at[6])]
    stores[0].start()
    small_grad[0:1, :] = gain_grad
    small_grad[1:2, :] = shift_grad
    small_grad[2:5, :] = terms[0:3, :]
    small_grad[5:6, :] = down_row[...]
    small_grad[6:10, :] = up_rows[...]
    small_grad[10:16, :] = head_rows[...]
    places = lax.broadcasted_iota(jnp.int32, (LEADS, WIDTH), 0)
    lead_grad = jnp.sum(pulled, axis=0, keepdims=True)
    small_grad[16:32, :] = jnp.where(places == lead[0], lead_grad, 0.0)
    for side, out in ((1, theirs_out), (0, mine_out)):
        lane[side, :, :384] = times(
            inputs[...], late_pulls[:, lane_columns(where, side, 384)]
        ).astype(BF16)
        rows = small_grad[pl.ds(pl.multiple_of((where[0] ^ side) * 16, 16), 16), :]
        rows = jnp.concatenate([rows, jnp.zeros((112, WIDTH), F32)], axis=0)
        lane[side, :, 384:] = rows.T.astype(BF16)
        stores += send_lane(where, "front", lane.at[side], out, lane_sems.at[side], side)
    wait_all(stores)


def late_backward(
    where, lead, lengths, pad, small, terms, down_row, up_rows, head_rows,
    mixed, qkv, first_grad, patches, mid_grad, input_turned, arrays,
):
    rows, columns = (TOKENS, WIDTH), (WIDTH, TOKENS)
    return call(
        late_back_kernel,
        (
            where, lead, lengths, pad, small, terms, down_row, up_rows, head_rows,
            mixed, qkv, first_grad, patches, mid_grad, input_turned, *arrays,
        ),
        [SMEM, SMEM, SMEM] + [VMEM] * 6 + [HBM] * 10,
        [(rows, F32, True), ((16, 48, 512), BF16, True), ((16, 48, 512), BF16, True)],
        attention_scratch(2)
        + weight_scratch(WIDTH, 3 * WIDTH)
        + lane_scratch(WIDTH, 512)
        + [
            pltpu.VMEM((TOKENS, 3 * WIDTH), BF16),
            pltpu.VMEM((TOKENS, WIDTH), BF16),
            pltpu.VMEM(rows, BF16),
            pltpu.VMEM(rows, F32),
            pltpu.VMEM(columns, BF16),
            pltpu.VMEM(rows, F32),
            pltpu.VMEM((32, WIDTH), F32),
            pltpu.SemaphoreType.DMA((7,)),
        ],
    )


def rows_of(vector, count):
    return vector.reshape(32, count, 24).transpose(1, 0, 2).reshape(count, WIDTH)


def vector_of(rows):
    count = rows.shape[0]
    return rows.reshape(count, 32, 24).transpose(1, 0, 2).reshape(1, count * WIDTH)


def shards(
    patches,
    lead_index,
    window_lengths,
    pad_mask,
    lead_table,
    attn_gain,
    attn_shift,
    qkv_weight,
    out_weight,
    out_bias,
    mlp_gain,
    mlp_shift,
    up_weight,
    up_bias,
    down_weight,
    down_bias,
    head_weight,
    head_bias,
    act_cotangent,
    head_cotangent,
):
    core, where = whereabouts()
    weights = (qkv_weight, out_weight, up_weight, down_weight, head_weight)
    vectors = (
        attn_gain, attn_shift, out_bias, mlp_gain, mlp_shift, down_bias, up_bias, head_bias
    )
    parts = packed(core, weights, lead_table, vectors)
    pad = pad_mask[:, None]
    cotangent_sum = jnp.sum(head_cotangent[:, GATE:].astype(F32), axis=0, keepdims=True)

    orders = ORDERS
    parts = dict(zip("qudh", zip(parts[:4], parts[4:])))
    chunks = {
        name: in_core_order(core, mine, exchange(theirs, SIBLING), 0)[None]
        for name, (mine, theirs) in parts.items()
    }

    held, last = dict(chunks), ()
    for name, step in GATHER_SEQUENCE:
        held[name] = after(held[name], *last)
        last = (held[name],)
        held[name] = doubled(held[name], orders[name][step])
    q, u, d, h = [held[name] for name in ("q", "u", "d", "h")]
    q_rest = exchange(after(q, *last), orders["q"][3])
    u = after(u, q)
    u_rest = exchange(u, orders["u"][3])
    d_rest = exchange(d, orders["d"][3])
    h = doubled(after(h, u), orders["h"][2])
    first = both_lanes(q, q_rest)
    h_rest = exchange(h, orders["h"][3])
    input_turned, qkv, small_rows = front_forward(
        after(where, d, h, cotangent_sum), lead_index, patches, first
    )
    attended, attended_turned = attention_forward(where, window_lengths, pad, qkv)
    u_rest, d_rest, h_rest = lax.optimization_barrier((u_rest, d_rest, h_rest, attended))[:3]
    second, down, head = both_lanes(u, u_rest), both_lanes(d, d_rest), both_lanes(h, h_rest)
    up_bias_row, head_bias_row = vector_of(small_rows[6:10]), vector_of(small_rows[10:16])
    (
        outputs, gate_out, gate_bias_sum, down_bias_sum, up_bias_sum, terms, mid_grad, _, mixed_grad,
        mine_d, theirs_d, mine_u, theirs_u, mine_h, theirs_h,
    ) = middle(
        where, small_rows, up_bias_row, head_bias_row, attended, patches, head_cotangent,
        act_cotangent, attended_turned, second, down, head,
    )

    got_h, got_d, got_u = [exchange(theirs, SIBLING) for theirs in (theirs_h, theirs_d, theirs_u)]
    head_rows = rows_of(jnp.concatenate([gate_bias_sum, cotangent_sum], axis=1), 6)
    up_rows = rows_of(up_bias_sum, 4)
    first_grad, mine_m, theirs_m = early_backward(
        where, window_lengths, pad, mixed_grad, qkv, input_turned
    )
    groups = {
        "head": [mine_h, after(got_h, first_grad), 4],
        "up": [mine_u, after(got_u, first_grad), 4],
        "down": [mine_d, after(got_d, first_grad), 4],
        "mix": [mine_m, exchange(theirs_m, SIBLING), 4],
    }
    last = ()

    def add(name):
        nonlocal last
        keep, got, step = groups[name]
        keep, send = folded(keep, after(got, *last))
        last = (send,)
        groups[name] = [keep, exchange(send, orders[name][step - 1]), step - 1]

    def finish(name, widths):
        keep, got, _ = groups[name]
        return finished(keep, after(got, *last), core, widths)

    for name in ("head", "up", "down"):
        add(name)
    patch_grad, mine_f, theirs_f = late_backward(
        after(where, *last), lead_index, window_lengths, pad, small_rows, terms, down_bias_sum,
        up_rows, head_rows, mixed_grad, qkv, first_grad, patches, mid_grad, input_turned, first,
    )
    last = (patch_grad,)
    groups["front"] = [mine_f, exchange(theirs_f, SIBLING), 4]
    for name in ("head", "mix", "front", "down", "up"):
        add(name)
    head_out = head_forward(after(where, *last), outputs, gate_out, head_bias_row, head)
    last = (head_out,)
    for name in ("head", "front", "mix", "head"):
        add(name)
    gate_sum, rest_sum = finish("head", (256, 2048))
    for name in ("down", "up", "front", "mix", "down", "up", "front", "mix"):
        add(name)
    up_sum, out_sum = finish("up", (1536, 384))
    (down_sum,) = finish("down", (384,))
    (early_sum,) = finish("mix", (768,))
    late_sum, small_sum = finish("front", (384, 128))
    qkv_sum = jnp.concatenate(
        [
            piece[:, part * piece.shape[1] // 3 : (part + 1) * piece.shape[1] // 3]
            for part in range(3)
            for piece in (early_sum, late_sum)
        ],
        axis=1,
    )
    small_sum = small_sum.T
    return (
        outputs,
        head_out,
        patch_grad,
        small_sum[128:144],
        small_sum[0],
        small_sum[1],
        qkv_sum,
        out_sum,
        small_sum[2],
        small_sum[3],
        small_sum[4],
        up_sum,
        small_sum[6:10].reshape(96),
        down_sum,
        small_sum[5],
        jnp.concatenate([gate_sum, rest_sum], axis=1),
        small_sum[10:16].reshape(144),
    )


def plain_shards(
    patches,
    lead_index,
    window_lengths,
    pad_mask,
    lead_table,
    attn_gain,
    attn_shift,
    qkv_weight,
    out_weight,
    out_bias,
    mlp_gain,
    mlp_shift,
    up_weight,
    up_bias,
    down_weight,
    down_bias,
    head_weight,
    head_bias,
    act_cotangent,
    head_cotangent,
):
    front = (
        lax.all_gather(lead_table, ("dp", "fsdp"), axis=1, tiled=True),
        lax.all_gather(attn_gain, ("dp", "fsdp"), axis=0, tiled=True),
        lax.all_gather(attn_shift, ("dp", "fsdp"), axis=0, tiled=True),
        lax.all_gather(qkv_weight, ("dp", "fsdp"), axis=0, tiled=True),
        lax.all_gather(out_weight, ("dp", "fsdp"), axis=0, tiled=True),
        lax.all_gather(out_bias, ("dp", "fsdp"), axis=0, tiled=True),
    )
    rear = (
        lax.all_gather(mlp_gain, ("dp", "fsdp"), axis=0, tiled=True),
        lax.all_gather(mlp_shift, ("dp", "fsdp"), axis=0, tiled=True),
        lax.all_gather(up_weight, ("dp", "fsdp"), axis=0, tiled=True),
        lax.all_gather(up_bias, ("dp", "fsdp"), axis=0, tiled=True),
        lax.all_gather(down_weight, ("dp", "fsdp"), axis=0, tiled=True),
        lax.all_gather(down_bias, ("dp", "fsdp"), axis=0, tiled=True),
        lax.all_gather(head_weight, ("dp", "fsdp"), axis=0, tiled=True),
        lax.all_gather(head_bias, ("dp", "fsdp"), axis=0, tiled=True),
    )
    table_full, gain_one, shift_one, qkv_full, out_full, out_bias_full = front
    (
        gain_two,
        shift_two,
        up_full,
        up_bias_full,
        down_full,
        down_bias_full,
        head_full,
        head_bias_full,
    ) = rear
    token_rows, width = patches.shape
    head_dim = width // HEADS
    block_rows = min(512, token_rows)
    block_count = token_rows // block_rows
    ends = jnp.cumsum(window_lengths[0])
    positions = jnp.arange(token_rows, dtype=jnp.int32)
    window = jnp.sum((positions[:, None] >= ends[None, :]).astype(jnp.int32), axis=1)
    lead_hot = (jnp.arange(LEADS, dtype=jnp.int32) == lead_index[0]).astype(jnp.float32)
    lead_row = jnp.sum(lead_hot[:, None] * table_full.astype(jnp.float32), axis=0)
    start_state = patches.astype(jnp.float32) + lead_row[None, :]
    normed_one, pull_one = jax.vjp(
        layer_norm, start_state, gain_one.astype(jnp.float32), shift_one.astype(jnp.float32)
    )
    attn_input = normed_one.astype(jnp.bfloat16)
    qkv_rows = jnp.dot(attn_input, qkv_full, preferred_element_type=jnp.float32).astype(
        jnp.bfloat16
    )
    queries = qkv_rows[:, :width].reshape(block_count, block_rows, HEADS, head_dim)
    keys = qkv_rows[:, width : 2 * width].reshape(token_rows, HEADS, head_dim)
    values = qkv_rows[:, 2 * width :].reshape(token_rows, HEADS, head_dim)
    query_windows = window.reshape(block_count, block_rows)
    block_starts = jnp.arange(block_count, dtype=jnp.int32) * block_rows

    def block_scores(query_block, window_block, block_start):
        scores = (
            jnp.einsum("qhd,khd->hqk", query_block, keys, preferred_element_type=jnp.float32)
            * score_scale
        )
        allowed = allowed_keys(window_block, window, pad_mask, block_start)
        return jnp.where(allowed[None], scores, -1e30)

    def forward_block(inputs):
        query_block, window_block, block_start = inputs
        masked = block_scores(query_block, window_block, block_start)
        largest = jnp.max(masked, axis=-1, keepdims=True)
        raised = jnp.exp(masked - largest)
        total = jnp.sum(raised, axis=-1, keepdims=True)
        probs = (raised / total).astype(jnp.bfloat16)
        mixed = jnp.einsum("hqk,khd->qhd", probs, values, preferred_element_type=jnp.float32)
        return (
            mixed.reshape(block_rows, width).astype(jnp.bfloat16),
            (largest + jnp.log(total))[:, :, 0],
        )

    mixed_blocks, log_totals = lax.map(forward_block, (queries, query_windows, block_starts))
    attended = mixed_blocks.reshape(token_rows, width)
    mid_state = (
        start_state
        + jnp.dot(attended, out_full, preferred_element_type=jnp.float32)
        + out_bias_full.astype(jnp.float32)
    )
    normed_two, pull_two = jax.vjp(
        layer_norm, mid_state, gain_two.astype(jnp.float32), shift_two.astype(jnp.float32)
    )
    mlp_input = normed_two.astype(jnp.bfloat16)
    pre_act = jnp.dot(mlp_input, up_full, preferred_element_type=jnp.float32) + up_bias_full.astype(
        jnp.float32
    )
    activated, pull_act = jax.vjp(gelu_exact, pre_act)
    act_rows = activated.astype(jnp.bfloat16)
    end_state = (
        mid_state
        + jnp.dot(act_rows, down_full, preferred_element_type=jnp.float32)
        + down_bias_full.astype(jnp.float32)
    )
    outputs = end_state.astype(jnp.bfloat16)
    logits = jnp.dot(
        outputs, head_full, preferred_element_type=jnp.float32
    ) + head_bias_full.astype(jnp.float32)
    head_out, pull_head = jax.vjp(partial(expert_softmax, experts=EXPERTS, pixels=PIX), logits)
    up_back, down_back, head_back = (
        lax.all_gather(up_weight, ("dp", "fsdp"), axis=0, tiled=True),
        lax.all_gather(down_weight, ("dp", "fsdp"), axis=0, tiled=True),
        lax.all_gather(head_weight, ("dp", "fsdp"), axis=0, tiled=True),
    )
    qkv_back, out_back = (
        lax.all_gather(qkv_weight, ("dp", "fsdp"), axis=0, tiled=True),
        lax.all_gather(out_weight, ("dp", "fsdp"), axis=0, tiled=True),
    )
    logit_grad = pull_head(head_cotangent.astype(jnp.float32))[0].astype(jnp.bfloat16)
    head_bias_term = jnp.sum(logit_grad.astype(jnp.float32), axis=0)
    head_term = jnp.einsum("td,tn->dn", outputs, logit_grad, preferred_element_type=jnp.float32)
    end_grad = act_cotangent.astype(jnp.float32) + jnp.einsum(
        "tn,dn->td", logit_grad, head_back, preferred_element_type=jnp.float32
    )
    branch_grad = end_grad.astype(jnp.bfloat16)
    down_bias_term = jnp.sum(branch_grad.astype(jnp.float32), axis=0)
    down_term = jnp.einsum("tf,td->fd", act_rows, branch_grad, preferred_element_type=jnp.float32)
    act_grad = jnp.einsum("td,fd->tf", branch_grad, down_back, preferred_element_type=jnp.float32)
    pre_grad = pull_act(act_grad)[0].astype(jnp.bfloat16)
    up_bias_term = jnp.sum(pre_grad.astype(jnp.float32), axis=0)
    up_term = jnp.einsum("td,tf->df", mlp_input, pre_grad, preferred_element_type=jnp.float32)
    normed_two_grad = jnp.einsum("tf,df->td", pre_grad, up_back, preferred_element_type=jnp.float32)
    state_grad_two, gain_two_term, shift_two_term = pull_two(normed_two_grad)
    (
        gain_part,
        shift_part,
        up_part,
        up_bias_part,
        down_part,
        down_bias_part,
        head_part,
        head_bias_part,
    ) = (
        lax.psum_scatter(
            gain_two_term.astype(jnp.bfloat16), "dp", scatter_dimension=0, tiled=True
        ).astype(jnp.float32),
        lax.psum_scatter(
            shift_two_term.astype(jnp.bfloat16), "dp", scatter_dimension=0, tiled=True
        ).astype(jnp.float32),
        lax.psum_scatter(
            up_term.astype(jnp.bfloat16), "dp", scatter_dimension=0, tiled=True
        ).astype(jnp.float32),
        lax.psum_scatter(
            up_bias_term.astype(jnp.bfloat16), "dp", scatter_dimension=0, tiled=True
        ).astype(jnp.float32),
        lax.psum_scatter(
            down_term.astype(jnp.bfloat16), "dp", scatter_dimension=0, tiled=True
        ).astype(jnp.float32),
        lax.psum_scatter(
            down_bias_term.astype(jnp.bfloat16), "dp", scatter_dimension=0, tiled=True
        ).astype(jnp.float32),
        lax.psum_scatter(
            head_term.astype(jnp.bfloat16), "dp", scatter_dimension=0, tiled=True
        ).astype(jnp.float32),
        lax.psum_scatter(
            head_bias_term.astype(jnp.bfloat16), "dp", scatter_dimension=0, tiled=True
        ).astype(jnp.float32),
    )
    rear_grads = (
        lax.psum_scatter(gain_part, "fsdp", scatter_dimension=0, tiled=True),
        lax.psum_scatter(shift_part, "fsdp", scatter_dimension=0, tiled=True),
        lax.psum_scatter(up_part, "fsdp", scatter_dimension=0, tiled=True),
        lax.psum_scatter(up_bias_part, "fsdp", scatter_dimension=0, tiled=True),
        lax.psum_scatter(down_part, "fsdp", scatter_dimension=0, tiled=True),
        lax.psum_scatter(down_bias_part, "fsdp", scatter_dimension=0, tiled=True),
        lax.psum_scatter(head_part, "fsdp", scatter_dimension=0, tiled=True),
        lax.psum_scatter(head_bias_part, "fsdp", scatter_dimension=0, tiled=True),
    )
    mid_grad = end_grad + state_grad_two
    out_grad = mid_grad.astype(jnp.bfloat16)
    out_bias_term = jnp.sum(out_grad.astype(jnp.float32), axis=0)
    out_term = jnp.einsum("td,te->de", attended, out_grad, preferred_element_type=jnp.float32)
    mixed_grad = jnp.einsum(
        "te,de->td", out_grad, out_back, preferred_element_type=jnp.float32
    ).astype(jnp.bfloat16)
    grad_blocks = mixed_grad.reshape(block_count, block_rows, HEADS, head_dim)

    def backward_block(carry, inputs):
        key_sum, value_sum = carry
        query_block, grad_block, window_block, total_block, block_start = inputs
        masked = block_scores(query_block, window_block, block_start)
        probs = jnp.exp(masked - total_block[:, :, None])
        prob_grad = jnp.einsum(
            "qhd,khd->hqk", grad_block, values, preferred_element_type=jnp.float32
        )
        inner = jnp.sum(probs * prob_grad, axis=-1, keepdims=True)
        score_grad = (probs * (prob_grad - inner)).astype(jnp.bfloat16)
        query_grad = (
            jnp.einsum("hqk,khd->qhd", score_grad, keys, preferred_element_type=jnp.float32)
            * score_scale
        )
        key_sum = (
            key_sum
            + jnp.einsum(
                "hqk,qhd->khd", score_grad, query_block, preferred_element_type=jnp.float32
            )
            * score_scale
        )
        value_sum = value_sum + jnp.einsum(
            "hqk,qhd->khd",
            probs.astype(jnp.bfloat16),
            grad_block,
            preferred_element_type=jnp.float32,
        )
        return ((key_sum, value_sum), query_grad.reshape(block_rows, width))

    zero_keys = jnp.zeros((token_rows, HEADS, head_dim), jnp.float32)
    (key_grad, value_grad), query_grads = lax.scan(
        backward_block,
        (zero_keys, zero_keys),
        (queries, grad_blocks, query_windows, log_totals, block_starts),
    )
    qkv_grad = jnp.concatenate(
        [
            query_grads.reshape(token_rows, width),
            key_grad.reshape(token_rows, width),
            value_grad.reshape(token_rows, width),
        ],
        axis=1,
    ).astype(jnp.bfloat16)
    qkv_term = jnp.einsum("td,te->de", attn_input, qkv_grad, preferred_element_type=jnp.float32)
    normed_one_grad = jnp.einsum(
        "te,de->td", qkv_grad, qkv_back, preferred_element_type=jnp.float32
    )
    state_grad_one, gain_one_term, shift_one_term = pull_one(normed_one_grad)
    patch_grad = mid_grad + state_grad_one
    lead_term = lead_hot[:, None] * jnp.sum(patch_grad, axis=0)[None, :]
    lead_part, gain_one_part, shift_one_part, qkv_part, out_part, out_bias_part = (
        lax.psum_scatter(
            lead_term.astype(jnp.bfloat16), "dp", scatter_dimension=1, tiled=True
        ).astype(jnp.float32),
        lax.psum_scatter(
            gain_one_term.astype(jnp.bfloat16), "dp", scatter_dimension=0, tiled=True
        ).astype(jnp.float32),
        lax.psum_scatter(
            shift_one_term.astype(jnp.bfloat16), "dp", scatter_dimension=0, tiled=True
        ).astype(jnp.float32),
        lax.psum_scatter(
            qkv_term.astype(jnp.bfloat16), "dp", scatter_dimension=0, tiled=True
        ).astype(jnp.float32),
        lax.psum_scatter(
            out_term.astype(jnp.bfloat16), "dp", scatter_dimension=0, tiled=True
        ).astype(jnp.float32),
        lax.psum_scatter(
            out_bias_term.astype(jnp.bfloat16), "dp", scatter_dimension=0, tiled=True
        ).astype(jnp.float32),
    )
    front_grads = (
        lax.psum_scatter(lead_part, "fsdp", scatter_dimension=1, tiled=True),
        lax.psum_scatter(gain_one_part, "fsdp", scatter_dimension=0, tiled=True),
        lax.psum_scatter(shift_one_part, "fsdp", scatter_dimension=0, tiled=True),
        lax.psum_scatter(qkv_part, "fsdp", scatter_dimension=0, tiled=True),
        lax.psum_scatter(out_part, "fsdp", scatter_dimension=0, tiled=True),
        lax.psum_scatter(out_bias_part, "fsdp", scatter_dimension=0, tiled=True),
    )
    return (
        outputs,
        head_out,
        patch_grad,
        front_grads[0],
        front_grads[1],
        front_grads[2],
        front_grads[3],
        front_grads[4],
        front_grads[5],
        rear_grads[0],
        rear_grads[1],
        rear_grads[2],
        rear_grads[3],
        rear_grads[4],
        rear_grads[5],
        rear_grads[6],
        rear_grads[7],
    )


def solution(mesh):
    in_specs = (
        P(("dp", "fsdp"), None),
        P(("dp", "fsdp")),
        P(("dp", "fsdp"), None),
        P(("dp", "fsdp")),
        P(None, ("dp", "fsdp")),
        P(("dp", "fsdp")),
        P(("dp", "fsdp")),
        P(("dp", "fsdp"), None),
        P(("dp", "fsdp"), None),
        P(("dp", "fsdp")),
        P(("dp", "fsdp")),
        P(("dp", "fsdp")),
        P(("dp", "fsdp"), None),
        P(("dp", "fsdp")),
        P(("dp", "fsdp"), None),
        P(("dp", "fsdp")),
        P(("dp", "fsdp"), None),
        P(("dp", "fsdp")),
        P(("dp", "fsdp"), None),
        P(("dp", "fsdp"), None),
    )
    out_specs = (
        P(("dp", "fsdp"), None),
        P(("dp", "fsdp"), None),
        P(("dp", "fsdp"), None),
        P(None, ("dp", "fsdp")),
        P(("dp", "fsdp")),
        P(("dp", "fsdp")),
        P(("dp", "fsdp"), None),
        P(("dp", "fsdp"), None),
        P(("dp", "fsdp")),
        P(("dp", "fsdp")),
        P(("dp", "fsdp")),
        P(("dp", "fsdp"), None),
        P(("dp", "fsdp")),
        P(("dp", "fsdp"), None),
        P(("dp", "fsdp")),
        P(("dp", "fsdp"), None),
        P(("dp", "fsdp")),
    )
    body = shards if dict(mesh.shape) == {"dp": 4, "fsdp": 8} else plain_shards
    return jax.shard_map(body, mesh=mesh, in_specs=in_specs, out_specs=out_specs, check_vma=False)
```

```python
import math
from functools import partial

import jax
import jax.numpy as jnp
from jax import lax
from jax.experimental import pallas as pl
from jax.experimental.pallas import tpu as pltpu
from jax.sharding import PartitionSpec as P

HEADS = 12
PIX = 64
EXPERTS = 3
LEADS = 16


norm_epsilon = 1e-05
score_scale = 0.125


def layer_norm(hidden, norm_gain, norm_shift):
    average = jnp.mean(hidden, axis=-1, keepdims=True)
    centered = hidden - average
    variance = jnp.mean(centered * centered, axis=-1, keepdims=True)
    return centered * lax.rsqrt(variance + norm_epsilon) * norm_gain + norm_shift


def gelu_exact(values):
    return 0.5 * values * (1.0 + lax.erf(values * 0.7071067811865476))


def expert_softmax(logits, experts, pixels):
    gate_part = logits[:, : experts * pixels].reshape(logits.shape[0], experts, pixels)
    largest = jnp.max(gate_part, axis=1, keepdims=True)
    raised = jnp.exp(gate_part - largest)
    shares = raised / jnp.sum(raised, axis=1, keepdims=True)
    return jnp.concatenate(
        [shares.reshape(logits.shape[0], experts * pixels), logits[:, experts * pixels :]], axis=1
    )


def allowed_keys(query_window, key_window, key_valid, query_start):
    query_place = query_start + jnp.arange(query_window.shape[0], dtype=jnp.int32)
    key_place = jnp.arange(key_window.shape[0], dtype=jnp.int32)
    same_window = query_window[:, None] == key_window[None, :]
    usable = (key_valid[None, :] > 0) | (query_place[:, None] == key_place[None, :])
    return same_window & usable


AXES = ("dp", "fsdp")
FAR_Z, NEAR_Z, FIRST, SECOND, SIBLING = (4, 4), (2, 2), (8, 16), (16, 8), (1, 1)
ORDERS = {
    "q": (FAR_Z, NEAR_Z, FIRST, SECOND),
    "u": (FAR_Z, FIRST, SECOND, NEAR_Z),
    "d": (FIRST, FAR_Z, NEAR_Z, SECOND),
    "h": (NEAR_Z, FAR_Z, FIRST, SECOND),
    "head": (FAR_Z, FIRST, SECOND, NEAR_Z),
    "down": (FAR_Z, NEAR_Z, FIRST, SECOND),
    "up": (NEAR_Z, FIRST, FAR_Z, SECOND),
    "front": (FAR_Z, NEAR_Z, FIRST, SECOND),
    "mix": (FAR_Z, FIRST, NEAR_Z, SECOND),
}
GATHER_SEQUENCE = (
    ("q", 0), ("d", 0), ("h", 0), ("u", 0), ("q", 1), ("d", 1), ("u", 1), ("q", 2), ("h", 1), ("u", 2),
    ("d", 2),
)
SCATTER_SEQUENCE = (
    "mix", "up", "front", "down", "mix", "head", "front", "down", "front", "mix", "head", "mix", "down",
    "front", "up", "head", "up",
)
MOST_VMEM, SPARE_VMEM = 60 * 1024 * 1024, 8 * 1024 * 1024
WIDTH = 768
HIDDEN = 3072
HEAD = 4608
TOKENS = 512
GATE = 512
F32 = jnp.float32
BF16 = jnp.bfloat16
HBM = pl.BlockSpec(memory_space=pltpu.HBM)
SMEM = pl.BlockSpec(memory_space=pltpu.SMEM)
VMEM = pl.BlockSpec(memory_space=pltpu.VMEM)
QKV_PART, SMALL_PART = (0, 1152), (1152, 128)
UP_PART, OUT_PART, GATE_PART = (0, 1536), (1536, 384), (1920, 256)
DOWN_PART, HEAD_PART = (0, 384), (0, 2048)


def chip_masks(order, lane):
    masks = []
    for place in range(16):
        mask = 0
        for step in range(4):
            if place >> step & 1:
                mask ^= order[step][lane]
        masks.append(mask >> 1)
    return masks


def table_start(group, side):
    return 1 + 32 * list(ORDERS).index(group) + 16 * side


def exchange(array, masks):
    return lax.ppermute(array, AXES, [(d, d ^ masks[d & 1]) for d in range(32)])


def whereabouts():
    device = lax.axis_index("dp") * 8 + lax.axis_index("fsdp")
    core, chip = device % 2, device // 2
    tables = [chip_masks(order, 0) + chip_masks(order, 1) for order in ORDERS.values()]
    swapped = [chip_masks(order, 1) + chip_masks(order, 0) for order in ORDERS.values()]
    places = jnp.where(core == 0, jnp.array(tables, jnp.int32), jnp.array(swapped, jnp.int32))
    places = (places ^ chip).reshape(32 * len(ORDERS))
    return core, jnp.concatenate([core[None].astype(jnp.int32), places])


def after(value, *marks):
    return lax.optimization_barrier((value, marks))[0]


def in_core_order(core, mine, theirs, axis):
    return jnp.where(
        core == 0,
        jnp.concatenate([mine, theirs], axis=axis),
        jnp.concatenate([theirs, mine], axis=axis),
    )


def pack_kernel(core, qkv, out, up, down, head, table, *refs):
    vectors, (up_bias, head_bias), refs = refs[:6], refs[6:8], refs[8:]
    outs, (rows,) = refs[:8], refs[8:]
    rows[...] = jnp.zeros_like(rows)
    for index, vector in enumerate(vectors):
        rows[index : index + 1, :24] = vector[...].astype(F32)
    for index in range(4):
        rows[6 + index : 7 + index, :24] = up_bias[:, 24 * index : 24 * index + 24].astype(F32)
    for index in range(6):
        rows[10 + index : 11 + index, :24] = head_bias[:, 24 * index : 24 * index + 24].astype(F32)
    rows[16:32, :24] = table[...].astype(F32)
    small = rows[...].T[:24].astype(BF16)
    for side in range(2):
        q, u, d, h = outs[4 * side : 4 * side + 4]
        q[:, :1152] = qkv[:, lane_columns(core, side, 1152)]
        q[:, 1152:] = small
        u[:, :1536] = up[:, lane_columns(core, side, 1536)]
        u[:, 1536:1920] = out[:, lane_columns(core, side, 384)]
        u[:, 1920:] = head[:, lane_columns(core, side, 256)]
        d[...] = down[:, lane_columns(core, side, 384)]
        h[...] = head[:, lane_columns(core, side, 2048, GATE)]


def packed(core, weights, table, vectors):
    shapes = [(24, 1280), (24, 2176), (96, 384), (24, 2048)] * 2
    return call(
        pack_kernel,
        (core.reshape(1), *weights, table, *[vector[None] for vector in vectors]),
        [SMEM] + [VMEM] * 14,
        [(shape, BF16, False) for shape in shapes],
        [pltpu.VMEM((128, 128), F32)],
    )


def doubled(held, masks):
    return jnp.concatenate([held, exchange(held, masks)], axis=0)


def both_lanes(*arrays):
    return arrays + tuple(exchange(array, SIBLING) for array in arrays)


def total(first, second):
    return first.astype(F32) + second.astype(F32)


def folded(keep, got, start=0):
    half = got.shape[0] // 2
    send = total(keep[half:], got[half:]).astype(BF16)
    return total(keep[:half], got[:half]).astype(BF16), send


def finished(keep, got, core, widths):
    block = total(keep, got)[0]
    rows = block.shape[0] // 2
    upper, lower = block[:rows], block[rows:]
    mine = jnp.where(core == 0, upper, lower)
    theirs = jnp.where(core == 0, lower, upper).astype(BF16)
    other = exchange(theirs, SIBLING).astype(F32)
    pieces, start = [], 0
    for width in widths:
        span = slice(start, start + width)
        pieces.append(in_core_order(core, mine[:, span], other[:, span], 1))
        start += width
    return pieces


def across(first, second):
    return lax.dot_general(first, second, (((1,), (1,)), ((), ())), preferred_element_type=F32)


def times(first, second):
    return jnp.dot(first, second, preferred_element_type=F32)


def lane_columns(where, side, stride, first=0, width=None):
    return pl.ds(pl.multiple_of(first + (where[0] ^ side) * stride, 128), width or stride)


def block_copies(where, group, sources, part, target, sems, side, first=0):
    start, width = part
    rows = sources[0].shape[1]
    half = len(sources) // 2
    count = 16 // half
    copies = []
    for place in range(16):
        row = pl.multiple_of(where[table_start(group, side) + place] * rows, rows)
        copies.append(
            pltpu.make_async_copy(
                sources[half * side + place // count].at[place % count, :, pl.ds(start, width)],
                target.at[pl.ds(row, rows), lane_columns(where, side, width, first)],
                sems.at[side, place],
            )
        )
    return copies


def start_all(copies):
    for copy in copies:
        copy.start()


def wait_all(copies):
    for copy in copies:
        copy.wait()


def mean_and_scale(hidden):
    average = jnp.mean(hidden, axis=1, keepdims=True)
    centered = hidden - average
    variance = jnp.mean(centered * centered, axis=1, keepdims=True)
    return centered, lax.rsqrt(variance + norm_epsilon)


def norm_backward(hidden, gain, upstream):
    centered, scale = mean_and_scale(hidden)
    normed = centered * scale
    gain_grad = jnp.sum(upstream * normed, axis=0, keepdims=True)
    shift_grad = jnp.sum(upstream, axis=0, keepdims=True)
    scaled = upstream * gain
    first = jnp.mean(scaled, axis=1, keepdims=True)
    second = jnp.mean(scaled * normed, axis=1, keepdims=True)
    return scale * (scaled - first - normed * second), gain_grad, shift_grad


def call(kernel, operands, in_specs, outs, scratch, spare=None):
    def size(item):
        return math.prod(item.shape) * jnp.dtype(item.dtype).itemsize

    held = [item for item, spec in zip(operands, in_specs) if spec is VMEM]
    held += [jax.ShapeDtypeStruct(shape, kind) for shape, kind, copied in outs if not copied]
    held += [item for item in scratch if getattr(item, "memory_space", None) == pltpu.VMEM]
    limit = MOST_VMEM if spare is None else sum(size(item) for item in held) + spare
    return pl.pallas_call(
        kernel,
        out_shape=[jax.ShapeDtypeStruct(shape, kind) for shape, kind, _ in outs],
        in_specs=in_specs,
        out_specs=[HBM if copied else VMEM for _, _, copied in outs],
        scratch_shapes=scratch,
        compiler_params=pltpu.CompilerParams(vmem_limit_bytes=limit),
        cost_estimate=pl.CostEstimate(flops=2 * 10**12, bytes_accessed=10**10, transcendentals=0),
    )(*operands)


def lane_scratch(rows, width):
    return [pltpu.VMEM((2, rows, width), BF16), pltpu.SemaphoreType.DMA((2, 16))]


def weight_scratch(rows, width):
    return [pltpu.VMEM((rows, width), BF16), pltpu.SemaphoreType.DMA((2, 16))]


def taken(refs, *counts):
    groups = []
    for count in counts:
        groups.append(refs[:count])
        refs = refs[count:]
    return *groups, refs


def front_kernel(where, lead, patches, *refs):
    sources, outs, scratch = taken(refs, 4, 3)
    turned_out, qkv_out, small = outs
    weight, sems, smalls, small_sems, state, rows, turned, qkv, io_sems = scratch
    loads = [block_copies(where, "q", sources, QKV_PART, weight, sems, side) for side in range(2)]
    small_loads = []
    for place in range(16):
        row = pl.multiple_of(where[table_start("q", 0) + place] * 48, 48)
        small_loads.append(
            pltpu.make_async_copy(
                sources[place // 8].at[place % 8, :, pl.ds(*SMALL_PART)],
                smalls.at[pl.ds(row, 48), :],
                small_sems.at[place],
            )
        )
    state_load = pltpu.make_async_copy(patches, state, io_sems.at[0])
    start_all(small_loads)
    state_load.start()
    start_all(loads[0])
    start_all(loads[1])
    wait_all(small_loads)
    columns = smalls[...].astype(F32).T
    places = lax.broadcasted_iota(jnp.int32, (LEADS, WIDTH), 0)
    lead_row = jnp.sum(
        jnp.where(places == lead[0], columns[16 : 16 + LEADS], 0.0), axis=0, keepdims=True
    )
    small[...] = columns[:32]
    small[16:17, :] = lead_row
    state_load.wait()
    centered, scale = mean_and_scale(state[...].astype(F32) + lead_row)
    rows[...] = (centered * scale * columns[0:1] + columns[1:2]).astype(BF16)
    turned[...] = rows[...].T
    stores = [pltpu.make_async_copy(turned, turned_out, io_sems.at[1])]
    stores[0].start()
    wait_all(loads[0] + loads[1])
    for part in range(3):
        span = slice(part * WIDTH, part * WIDTH + WIDTH)
        qkv[:, span] = times(rows[...], weight[:, span]).astype(BF16)
        stores.append(pltpu.make_async_copy(qkv.at[:, span], qkv_out.at[:, span], io_sems.at[2 + part]))
        stores[-1].start()
    wait_all(stores)


def front_forward(where, lead_index, patches, arrays):
    return call(
        front_kernel,
        (where, lead_index, patches, *arrays),
        [SMEM, SMEM, HBM] + [HBM] * 4,
        [
            ((WIDTH, TOKENS), BF16, True),
            ((TOKENS, 3 * WIDTH), BF16, True),
            ((32, WIDTH), F32, False),
        ],
        weight_scratch(WIDTH, 3 * WIDTH)
        + [pltpu.VMEM((WIDTH, 128), BF16), pltpu.SemaphoreType.DMA((16,))]
        + [
            pltpu.VMEM((TOKENS, WIDTH), BF16),
            pltpu.VMEM((TOKENS, WIDTH), BF16),
            pltpu.VMEM((WIDTH, TOKENS), BF16),
            pltpu.VMEM((TOKENS, 3 * WIDTH), BF16),
            pltpu.SemaphoreType.DMA((5,)),
        ],
    )


KEY_SPANS = ((0, 256), (0, 384), (128, 512), (256, 512))


def fill_bias(lengths, pad, bias):
    ends, end = [], 0
    for index in range(lengths.shape[1]):
        end = end + lengths[0, index]
        ends.append(end)

    def windows(places):
        return sum([(places >= end).astype(jnp.int32) for end in ends])

    for block, (low, high) in enumerate(KEY_SPANS):
        count = high - low
        queries = lax.broadcasted_iota(jnp.int32, (1, 128), 1) + 128 * block
        keys = lax.broadcasted_iota(jnp.int32, (count, 1), 0) + low
        same = windows(queries) == windows(keys)
        usable = (pad[low:high, :] > 0) | (queries == keys)
        bias[block, :count, :] = jnp.where(same & usable, 0.0, -1e30)


def two_heads(block):
    first = lax.broadcasted_iota(jnp.int32, block.shape, 1) < block.shape[1] // 2
    zero = jnp.zeros_like(block)
    return jnp.concatenate([jnp.where(first, block, zero), jnp.where(first, zero, block)], axis=0)


def head_rows_of(stacked):
    return jnp.concatenate([stacked[:64, :128], stacked[64:, 128:]], axis=0)


def probabilities(scores, allowed):
    masked = scores * score_scale + allowed
    raised = jnp.exp(masked - jnp.max(masked, axis=0, keepdims=True))
    return raised * (1.0 / jnp.sum(raised, axis=0, keepdims=True))


def attention_kernel(where, lengths, pad, qkv, attended_out, turned_out, bias, turned, rows, sems):
    fill_bias(lengths, pad, bias)

    def pair(index, carry):
        first = index * 128
        columns = pl.ds(pl.multiple_of(first, 128), 128)
        keys_at = pl.ds(pl.multiple_of(first + WIDTH, 128), 128)
        values = qkv[:, pl.ds(pl.multiple_of(first + 2 * WIDTH, 128), 128)].T
        for block, (low, high) in enumerate(KEY_SPANS):
            span = slice(128 * block, 128 * block + 128)
            scores = across(qkv[low:high, keys_at], two_heads(qkv[span, columns]))
            allowed = bias[block, : high - low, :]
            probs = [
                probabilities(scores[:, 128 * head : 128 * head + 128], allowed).astype(BF16)
                for head in range(2)
            ]
            mixed = times(values[:, low:high], jnp.concatenate(probs, axis=1))
            turned[columns, span] = head_rows_of(mixed).astype(BF16)
        return carry

    lax.fori_loop(0, WIDTH // 128, pair, 0)
    stores = [pltpu.make_async_copy(turned, turned_out, sems.at[0])]
    stores[0].start()
    rows[...] = turned[...].T
    stores.append(pltpu.make_async_copy(rows, attended_out, sems.at[1]))
    stores[1].start()
    wait_all(stores)


def attention_forward(where, lengths, pad, qkv):
    rows, columns = (TOKENS, WIDTH), (WIDTH, TOKENS)
    return call(
        attention_kernel,
        (where, lengths, pad, qkv),
        [SMEM, SMEM, VMEM, VMEM],
        [(rows, BF16, True), (columns, BF16, True)],
        [
            pltpu.VMEM((4, 384, 128), F32),
            pltpu.VMEM(columns, BF16),
            pltpu.VMEM(rows, BF16),
            pltpu.SemaphoreType.DMA((2,)),
        ],
    )


def gate_shares(logits, cotangent, shares, gate_grad):
    gate_grad[:, 256:] = cotangent[:, 256:GATE]
    first, rest = logits[:, :128], logits[:, 128:256]
    left = lax.broadcasted_iota(jnp.int32, first.shape, 1) < PIX
    third = jnp.where(left, rest, pltpu.roll(rest, PIX, 1))
    largest = jnp.maximum(jnp.maximum(first, pltpu.roll(first, PIX, 1)), third)
    raised, raised_third = jnp.exp(first - largest), jnp.exp(third - largest)
    scale = 1.0 / (raised + pltpu.roll(raised, PIX, 1) + raised_third)
    share, share_third = raised * scale, raised_third * scale
    shares[:, :128] = share
    shares[:, 128:256] = jnp.where(left, share_third, rest)
    pull, other = cotangent[:, :128].astype(F32), cotangent[:, 128:256].astype(F32)
    pull_third = jnp.where(left, other, pltpu.roll(other, PIX, 1))
    weighed = share * pull
    inner = weighed + pltpu.roll(weighed, PIX, 1) + share_third * pull_third
    gate_grad[:, :128] = (share * (pull - inner)).astype(BF16)
    gate_grad[:, 128:256] = jnp.where(left, share_third * (pull_third - inner), other).astype(BF16)


def send_lane(where, group, lane, out, sems, side):
    rows = out.shape[1]
    copies = []
    for place in range(16):
        row = pl.multiple_of(where[table_start(group, side) + place] * rows, rows)
        copies.append(
            pltpu.make_async_copy(lane.at[pl.ds(row, rows), :], out.at[place], sems.at[place])
        )
    start_all(copies)
    return copies


def middle_kernel(
    where, small, up_bias, head_bias, attended, patches, cotangent, act_cotangent, attended_turned,
    *refs,
):
    up_sources, down_sources, head_sources, outs, scratch = taken(refs, 4, 4, 4, 15)
    outputs, shares, gate_bias, down_bias, up_bias_sum, terms, mid_grad, out_grad, mixed, *grads = outs
    down_mine, down_theirs, up_mine, up_theirs, head_mine, head_theirs = grads
    out_weight, out_sems, up, up_sems, down, down_sems, scratch = *scratch[:6], scratch[6:]
    head, head_sems, gate_sems, rows, branch, mid, mlp_turned, scratch = *scratch[:7], scratch[7:]
    act, act_turned, slope, turned, pulls, act_pulls, gate_grad, scratch = *scratch[:7], scratch[7:]
    lane, lane_sems, down_lane, down_lane_sems, mixes, more_sems, io_sems = scratch

    def loads(group, sources, part, target, sems, first=0):
        copies = []
        for side in range(2):
            copies += block_copies(where, group, sources, part, target, sems, side, first)
        return copies

    state_loads = [
        pltpu.make_async_copy(attended, rows, io_sems.at[0]),
        pltpu.make_async_copy(patches, branch, io_sems.at[1]),
    ]
    out_loads = loads("u", up_sources, OUT_PART, out_weight, out_sems)
    up_loads = loads("u", up_sources, UP_PART, up, up_sems)
    down_loads = loads("d", down_sources, DOWN_PART, down, down_sems)
    gate_loads = loads("u", up_sources, GATE_PART, head, gate_sems)
    head_loads = loads("h", head_sources, HEAD_PART, head, head_sems, GATE)
    pull_load = pltpu.make_async_copy(cotangent, pulls, io_sems.at[2])
    act_load = pltpu.make_async_copy(act_cotangent, act_pulls, io_sems.at[3])
    mix_load = pltpu.make_async_copy(attended_turned, mixes, io_sems.at[4])
    start_all(state_loads + out_loads + up_loads + down_loads + gate_loads)
    pull_load.start()
    start_all(head_loads)
    act_load.start()
    mix_load.start()

    wait_all(state_loads + out_loads)
    mid[...] = (
        branch[...].astype(F32)
        + small[16:17, :]
        + times(rows[...], out_weight[...])
        + small[2:3, :]
    )
    centered, scale = mean_and_scale(mid[...])
    rows[...] = (centered * scale * small[3:4, :] + small[4:5, :]).astype(BF16)
    mlp_turned[...] = rows[...].T
    wait_all(up_loads)
    for tile in range(6):
        span = slice(tile * 512, tile * 512 + 512)
        values = times(rows[...], up[:, span]) + up_bias[:, span]
        share = 0.5 * (1.0 + lax.erf(values * 0.7071067811865476))
        density = jnp.exp(-0.5 * values * values) * 0.3989422804014327
        activated = (values * share).astype(BF16)
        act[:, span] = activated
        act_turned[span, :] = activated.T
        slope[:, span] = (share + values * density).astype(BF16)
    wait_all(down_loads)
    outputs[...] = (mid[...] + times(act[...], down[...]) + small[5:6, :]).astype(BF16)
    turned[...] = outputs[...].T
    wait_all(gate_loads)
    shares[...] = times(outputs[...], head[:, :GATE]) + head_bias[:, :GATE]
    pull_load.wait()
    gate_shares(shares, pulls, shares, gate_grad)
    gate_bias[...] = jnp.sum(gate_grad[...].astype(F32), axis=0, keepdims=True)
    pulls[:, :GATE] = gate_grad[...]

    def head_lane(side, target, sems, out):
        target[:, :256] = times(turned[...], pulls[:, lane_columns(where, side, 256)]).astype(BF16)
        for tile in range(4):
            span = lane_columns(where, side, 2048, GATE + tile * 512, 512)
            target[:, 256 + tile * 512 : 768 + tile * 512] = times(turned[...], pulls[:, span]).astype(
                BF16
            )
        return send_lane(where, "head", target, out, sems, side)

    def down_lane_of(side, out):
        columns = branch[:, lane_columns(where, side, 384)]
        for part in range(4):
            span = slice(part * WIDTH, part * WIDTH + WIDTH)
            down_lane[span, :] = times(act_turned[span, :], columns).astype(BF16)
        return send_lane(where, "down", down_lane, out, down_lane_sems, side)

    def up_lane(side, target, sems, out):
        for tile in range(3):
            span = lane_columns(where, side, 1536, tile * 512, 512)
            target[:, tile * 512 : tile * 512 + 512] = times(mlp_turned[...], slope[:, span]).astype(
                BF16
            )
        target[:, 1536:1920] = times(
            mixes[...], out_grad[:, lane_columns(where, side, 384)]
        ).astype(BF16)
        return send_lane(where, "up", target, out, sems, side)

    first_stores = head_lane(1, lane, lane_sems, head_theirs)
    act_load.wait()
    wait_all(head_loads)
    mid_grad[...] = act_pulls[...].astype(F32) + across(pulls[...], head[...])
    branch[...] = mid_grad[...].astype(BF16)
    down_bias[...] = jnp.sum(branch[...].astype(F32), axis=0, keepdims=True)
    stores = head_lane(0, head.at[:, :2304], more_sems.at[0], head_mine)
    down_stores = down_lane_of(1, down_theirs)
    for tile in range(6):
        span = slice(tile * 512, tile * 512 + 512)
        grad = across(branch[...], down[span, :])
        rounded = (slope[:, span].astype(F32) * grad).astype(BF16)
        slope[:, span] = rounded
        up_bias_sum[:, span] = jnp.sum(rounded.astype(F32), axis=0, keepdims=True)
    wait_all(down_stores)
    stores += down_lane_of(0, down_mine)
    grad = across(slope[...], up[...])
    pulled, gain_grad, shift_grad = norm_backward(mid[...], small[3:4, :], grad)
    pulled = pulled + mid_grad[...]
    rounded = pulled.astype(BF16)
    mid_grad[...] = pulled
    out_grad[...] = rounded
    terms[...] = jnp.zeros_like(terms)
    terms[0:1, :] = jnp.sum(rounded.astype(F32), axis=0, keepdims=True)
    terms[1:2, :] = gain_grad
    terms[2:3, :] = shift_grad
    mix_load.wait()
    stores += up_lane(1, head.at[:, 2304:4224], more_sems.at[1], up_theirs)
    wait_all(first_stores)
    stores += up_lane(0, lane.at[:, :1920], lane_sems, up_mine)
    mixed[...] = across(out_grad[...], out_weight[...]).astype(BF16)
    wait_all(stores)


def middle(
    where, small, up_bias, head_bias, attended, patches, cotangent, act_cotangent, attended_turned,
    up, down, head,
):
    rows, columns = (TOKENS, WIDTH), (WIDTH, TOKENS)
    wide, tall = (TOKENS, HIDDEN), (HIDDEN, TOKENS)
    return call(
        middle_kernel,
        (
            where, small, up_bias, head_bias, attended, patches, cotangent, act_cotangent,
            attended_turned, *up, *down, *head,
        ),
        [SMEM, VMEM, VMEM, VMEM] + [HBM] * 17,
        [
            (rows, BF16, False),
            ((TOKENS, GATE), F32, False),
            ((1, GATE), F32, False),
            ((1, WIDTH), F32, False),
            ((1, HIDDEN), F32, False),
            ((8, WIDTH), F32, False),
            (rows, F32, False),
            (rows, BF16, False),
            (rows, BF16, False),
            ((16, 192, 384), BF16, True),
            ((16, 192, 384), BF16, True),
            ((16, 48, 1920), BF16, True),
            ((16, 48, 1920), BF16, True),
            ((16, 48, 2304), BF16, True),
            ((16, 48, 2304), BF16, True),
        ],
        weight_scratch(WIDTH, WIDTH)
        + weight_scratch(WIDTH, HIDDEN)
        + weight_scratch(HIDDEN, WIDTH)
        + weight_scratch(WIDTH, HEAD)
        + [
            pltpu.SemaphoreType.DMA((2, 16)),
            pltpu.VMEM(rows, BF16),
            pltpu.VMEM(rows, BF16),
            pltpu.VMEM(rows, F32),
            pltpu.VMEM(columns, BF16),
            pltpu.VMEM(wide, BF16),
            pltpu.VMEM(tall, BF16),
            pltpu.VMEM(wide, BF16),
            pltpu.VMEM(columns, BF16),
            pltpu.VMEM((TOKENS, HEAD), BF16),
            pltpu.VMEM(rows, BF16),
            pltpu.VMEM((TOKENS, GATE), BF16),
            pltpu.VMEM((WIDTH, 2304), BF16),
            pltpu.SemaphoreType.DMA((16,)),
            pltpu.VMEM((HIDDEN, 384), BF16),
            pltpu.SemaphoreType.DMA((16,)),
            pltpu.VMEM(columns, BF16),
            pltpu.SemaphoreType.DMA((2, 16)),
            pltpu.SemaphoreType.DMA((5,)),
        ],
    )


def attend_back(count, qkv, mixed, bias, turned, key_sum, value_sum, qkv_grad):
    width = 128 * count

    def columns_at(first):
        return pl.ds(pl.multiple_of(first, 128), 128)

    def pair(index, carry):
        own = index * 128
        columns, keys_at = columns_at(own), columns_at(own + width)
        values_at = columns_at(own + 2 * width)
        keys_turned = qkv[:, keys_at].T
        key_sum[...] = jnp.zeros_like(key_sum)
        value_sum[...] = jnp.zeros_like(value_sum)
        for block, (low, high) in enumerate(KEY_SPANS):
            span = slice(128 * block, 128 * block + 128)
            queries, grads = two_heads(qkv[span, columns]), two_heads(mixed[span, columns])
            scores = across(qkv[low:high, keys_at], queries)
            prob_grads = across(qkv[low:high, values_at], grads)
            allowed = bias[block, : high - low, :]
            probs, score_grads = [], []
            for head in range(2):
                part = slice(128 * head, 128 * head + 128)
                prob = probabilities(scores[:, part], allowed)
                pulled = prob * prob_grads[:, part]
                inner = jnp.sum(pulled, axis=0, keepdims=True)
                probs.append(prob.astype(BF16))
                score_grads.append((pulled - prob * inner).astype(BF16))
            score_grad = jnp.concatenate(score_grads, axis=1)
            key_sum[low:high, :] += times(score_grad, queries)
            value_sum[low:high, :] += times(jnp.concatenate(probs, axis=1), grads)
            turned[:, span] = head_rows_of(times(keys_turned[:, low:high], score_grad)) * score_scale
        qkv_grad[:, columns] = turned[...].T.astype(BF16)
        qkv_grad[:, keys_at] = (key_sum[...] * score_scale).astype(BF16)
        qkv_grad[:, values_at] = value_sum[...].astype(BF16)
        return carry

    lax.fori_loop(0, count, pair, 0)


def attention_scratch(count):
    return [
        pltpu.VMEM((4, 384, 128), F32),
        pltpu.VMEM((TOKENS, 384 * count), BF16),
        pltpu.VMEM((TOKENS, 128 * count), BF16),
        pltpu.VMEM((128, TOKENS), F32),
        pltpu.VMEM((TOKENS, 128), F32),
        pltpu.VMEM((TOKENS, 128), F32),
        pltpu.SemaphoreType.DMA((4,)),
    ]


def attention_loads(start, count, qkv, mixed, own_qkv, own_mixed, sems):
    width = 128 * count
    copies = [
        pltpu.make_async_copy(
            mixed.at[:, pl.ds(128 * start, width)], own_mixed.at[:, pl.ds(0, width)], sems.at[3]
        )
    ]
    for part in range(3):
        copies.append(
            pltpu.make_async_copy(
                qkv.at[:, pl.ds(WIDTH * part + 128 * start, width)],
                own_qkv.at[:, pl.ds(width * part, width)],
                sems.at[part],
            )
        )
    return copies


def early_back_kernel(where, lengths, pad, mixed, qkv, input_turned, *refs):
    (qkv_grad, mine_out, theirs_out), scratch = taken(refs, 3)
    bias, own_qkv, own_mixed, turned, key_sum, value_sum, sems, scratch = *scratch[:7], scratch[7:]
    lane, lane_sems, inputs, io_sems = scratch
    loads = attention_loads(0, 4, qkv, mixed, own_qkv, own_mixed, sems)
    in_load = pltpu.make_async_copy(input_turned, inputs, io_sems.at[0])
    start_all(loads + [in_load])
    fill_bias(lengths, pad, bias)
    wait_all(loads)
    attend_back(4, own_qkv, own_mixed, bias, turned, key_sum, value_sum, qkv_grad)
    in_load.wait()
    stores = []
    for side, out in ((1, theirs_out), (0, mine_out)):
        lane[side] = times(inputs[...], qkv_grad[:, lane_columns(where, side, 768)]).astype(BF16)
        stores += send_lane(where, "mix", lane.at[side], out, lane_sems.at[side], side)
    wait_all(stores)


def early_backward(where, lengths, pad, mixed, qkv, input_turned):
    return call(
        early_back_kernel,
        (where, lengths, pad, mixed, qkv, input_turned),
        [SMEM, SMEM, VMEM] + [HBM] * 3,
        [
            ((TOKENS, 1536), BF16, False),
            ((16, 48, 768), BF16, True),
            ((16, 48, 768), BF16, True),
        ],
        attention_scratch(4)
        + lane_scratch(WIDTH, 768)
        + [pltpu.VMEM((WIDTH, TOKENS), BF16), pltpu.SemaphoreType.DMA((1,))],
    )


def late_back_kernel(
    where, lead, lengths, pad, small, terms, down_row, up_rows, head_rows, head_bias,
    outputs, shares, mixed, qkv, first_grad, patches, mid_grad, input_turned, *refs
):
    sources, head_sources, outs, scratch = taken(refs, 4, 4, 4)
    patch_out, head_out, mine_out, theirs_out = outs
    head, head_sems, rows, result, head_io, scratch = *scratch[:5], scratch[5:]
    bias, own_qkv, own_mixed, turned, key_sum, value_sum, sems, scratch = *scratch[:7], scratch[7:]
    weight, weight_sems, lane, lane_sems, pulls, late_pulls, scratch = *scratch[:6], scratch[6:]
    state, mids, inputs, patch_grad, small_grad, io_sems = scratch
    own_loads = attention_loads(4, 2, qkv, mixed, own_qkv, own_mixed, sems)
    loads = [
        block_copies(where, "q", sources, QKV_PART, weight, weight_sems, side) for side in range(2)
    ]
    pairs = [(patches, state), (mid_grad, mids), (input_turned, inputs)]
    for part in range(3):
        target = pulls.at[:, pl.ds(WIDTH * part, 512)]
        pairs.append((first_grad.at[:, pl.ds(512 * part, 512)], target))
    in_loads = [pltpu.make_async_copy(*pair, io_sems.at[at]) for at, pair in enumerate(pairs)]
    head_loads = [
        block_copies(where, "h", head_sources, HEAD_PART, head, head_sems, side) for side in range(2)
    ]
    row_load = pltpu.make_async_copy(outputs, rows, head_io.at[0])
    share_load = pltpu.make_async_copy(shares, result.at[:, :GATE], head_io.at[1])
    start_all(own_loads + [row_load] + head_loads[0] + head_loads[1] + [share_load])
    start_all(in_loads + loads[0] + loads[1])
    fill_bias(lengths, pad, bias)
    wait_all(own_loads)
    attend_back(2, own_qkv, own_mixed, bias, turned, key_sum, value_sum, late_pulls)
    wait_all([row_load, share_load] + head_loads[0] + head_loads[1])
    stores = [pltpu.make_async_copy(result.at[:, :GATE], head_out.at[:, :GATE], head_io.at[2])]
    stores[0].start()
    for tile in range(8):
        span = slice(GATE + tile * 512, GATE + tile * 512 + 512)
        result[:, span] = (
            times(rows[...], head[:, tile * 512 : tile * 512 + 512]) + head_bias[:, span]
        )
        stores.append(
            pltpu.make_async_copy(result.at[:, span], head_out.at[:, span], head_io.at[3 + tile])
        )
        stores[-1].start()
    wait_all(loads[0] + loads[1] + in_loads)
    for part in range(3):
        pulls[:, WIDTH * part + 512 : WIDTH * part + 768] = late_pulls[
            :, 256 * part : 256 * part + 256
        ]
    grad = across(pulls[...], weight[...])
    pulled, gain_grad, shift_grad = norm_backward(
        state[...].astype(F32) + small[16:17, :], small[0:1, :], grad
    )
    pulled = pulled + mids[...]
    patch_grad[...] = pulled
    stores.append(pltpu.make_async_copy(patch_grad, patch_out, io_sems.at[6]))
    stores[-1].start()
    small_grad[0:1, :] = gain_grad
    small_grad[1:2, :] = shift_grad
    small_grad[2:5, :] = terms[0:3, :]
    small_grad[5:6, :] = down_row[...]
    small_grad[6:10, :] = up_rows[...]
    small_grad[10:16, :] = head_rows[...]
    places = lax.broadcasted_iota(jnp.int32, (LEADS, WIDTH), 0)
    lead_grad = jnp.sum(pulled, axis=0, keepdims=True)
    small_grad[16:32, :] = jnp.where(places == lead[0], lead_grad, 0.0)
    for side, out in ((1, theirs_out), (0, mine_out)):
        lane[side, :, :384] = times(
            inputs[...], late_pulls[:, lane_columns(where, side, 384)]
        ).astype(BF16)
        rows = small_grad[pl.ds(pl.multiple_of((where[0] ^ side) * 16, 16), 16), :]
        rows = jnp.concatenate([rows, jnp.zeros((112, WIDTH), F32)], axis=0)
        lane[side, :, 384:] = rows.T.astype(BF16)
        stores += send_lane(where, "front", lane.at[side], out, lane_sems.at[side], side)
    wait_all(stores)


def late_backward(
    where, lead, lengths, pad, small, terms, down_row, up_rows, head_rows, head_bias,
    outputs, shares, mixed, qkv, first_grad, patches, mid_grad, input_turned, arrays, head_arrays,
):
    rows, columns = (TOKENS, WIDTH), (WIDTH, TOKENS)
    return call(
        late_back_kernel,
        (
            where, lead, lengths, pad, small, terms, down_row, up_rows, head_rows, head_bias,
            outputs, shares, mixed, qkv, first_grad, patches, mid_grad, input_turned,
            *arrays, *head_arrays,
        ),
        [SMEM, SMEM, SMEM] + [VMEM] * 7 + [HBM] * 16,
        [
            (rows, F32, True),
            ((TOKENS, HEAD), F32, True),
            ((16, 48, 512), BF16, True),
            ((16, 48, 512), BF16, True),
        ],
        weight_scratch(WIDTH, HEAD - GATE)
        + [
            pltpu.VMEM(rows, BF16),
            pltpu.VMEM((TOKENS, HEAD), F32),
            pltpu.SemaphoreType.DMA((11,)),
        ]
        + attention_scratch(2)
        + weight_scratch(WIDTH, 3 * WIDTH)
        + lane_scratch(WIDTH, 512)
        + [
            pltpu.VMEM((TOKENS, 3 * WIDTH), BF16),
            pltpu.VMEM((TOKENS, WIDTH), BF16),
            pltpu.VMEM(rows, BF16),
            pltpu.VMEM(rows, F32),
            pltpu.VMEM(columns, BF16),
            pltpu.VMEM(rows, F32),
            pltpu.VMEM((32, WIDTH), F32),
            pltpu.SemaphoreType.DMA((7,)),
        ],
    )


def rows_of(vector, count):
    return vector.reshape(32, count, 24).transpose(1, 0, 2).reshape(count, WIDTH)


def vector_of(rows):
    count = rows.shape[0]
    return rows.reshape(count, 32, 24).transpose(1, 0, 2).reshape(1, count * WIDTH)


def shards(
    patches,
    lead_index,
    window_lengths,
    pad_mask,
    lead_table,
    attn_gain,
    attn_shift,
    qkv_weight,
    out_weight,
    out_bias,
    mlp_gain,
    mlp_shift,
    up_weight,
    up_bias,
    down_weight,
    down_bias,
    head_weight,
    head_bias,
    act_cotangent,
    head_cotangent,
):
    core, where = whereabouts()
    weights = (qkv_weight, out_weight, up_weight, down_weight, head_weight)
    vectors = (
        attn_gain, attn_shift, out_bias, mlp_gain, mlp_shift, down_bias, up_bias, head_bias
    )
    parts = packed(core, weights, lead_table, vectors)
    pad = pad_mask[:, None]
    cotangent_sum = jnp.sum(head_cotangent[:, GATE:].astype(F32), axis=0, keepdims=True)

    orders = ORDERS
    parts = dict(zip("qudh", zip(parts[:4], parts[4:])))
    chunks = {
        name: in_core_order(core, mine, exchange(theirs, SIBLING), 0)[None]
        for name, (mine, theirs) in parts.items()
    }

    held, last = dict(chunks), ()
    for name, step in GATHER_SEQUENCE:
        held[name] = after(held[name], *last)
        last = (held[name],)
        held[name] = doubled(held[name], orders[name][step])
    q, u, d, h = [held[name] for name in ("q", "u", "d", "h")]
    q_rest = exchange(after(q, *last), orders["q"][3])
    u = after(u, q)
    u_rest = exchange(u, orders["u"][3])
    d_rest = exchange(d, orders["d"][3])
    h = doubled(after(h, u), orders["h"][2])
    first = both_lanes(q, q_rest)
    h_rest = exchange(h, orders["h"][3])
    input_turned, qkv, small_rows = front_forward(
        after(where, d, h, cotangent_sum), lead_index, patches, first
    )
    attended, attended_turned = attention_forward(where, window_lengths, pad, qkv)
    u_rest, d_rest, h_rest = lax.optimization_barrier((u_rest, d_rest, h_rest, attended))[:3]
    second, down, head = both_lanes(u, u_rest), both_lanes(d, d_rest), both_lanes(h, h_rest)
    up_bias_row, head_bias_row = vector_of(small_rows[6:10]), vector_of(small_rows[10:16])
    (
        outputs, gate_out, gate_bias_sum, down_bias_sum, up_bias_sum, terms, mid_grad, _, mixed_grad,
        mine_d, theirs_d, mine_u, theirs_u, mine_h, theirs_h,
    ) = middle(
        where, small_rows, up_bias_row, head_bias_row, attended, patches, head_cotangent,
        act_cotangent, attended_turned, second, down, head,
    )

    got_h, got_d, got_u = [exchange(theirs, SIBLING) for theirs in (theirs_h, theirs_d, theirs_u)]
    head_rows = rows_of(jnp.concatenate([gate_bias_sum, cotangent_sum], axis=1), 6)
    up_rows = rows_of(up_bias_sum, 4)
    first_grad, mine_m, theirs_m = early_backward(
        where, window_lengths, pad, mixed_grad, qkv, input_turned
    )
    groups = {
        "head": [mine_h, after(got_h, first_grad), 4],
        "up": [mine_u, after(got_u, first_grad), 4],
        "down": [mine_d, after(got_d, first_grad), 4],
        "mix": [mine_m, exchange(theirs_m, SIBLING), 4],
    }
    last = ()

    def add(name):
        nonlocal last
        keep, got, step = groups[name]
        keep, send = folded(keep, after(got, *last))
        last = (send,)
        groups[name] = [keep, exchange(send, orders[name][step - 1]), step - 1]

    def finish(name, widths):
        keep, got, _ = groups[name]
        return finished(keep, after(got, *last), core, widths)

    for name in ("head", "down", "up"):
        add(name)
    patch_grad, head_out, mine_f, theirs_f = late_backward(
        after(where, *last), lead_index, window_lengths, pad, small_rows, terms, down_bias_sum,
        up_rows, head_rows, head_bias_row, outputs, gate_out, mixed_grad, qkv, first_grad, patches,
        mid_grad, input_turned, first, head,
    )
    last = (patch_grad,)
    groups["front"] = [mine_f, exchange(theirs_f, SIBLING), 4]
    for name in SCATTER_SEQUENCE:
        add(name)
    late_sum, small_sum = finish("front", (384, 128))
    (down_sum,) = finish("down", (384,))
    (early_sum,) = finish("mix", (768,))
    up_sum, out_sum = finish("up", (1536, 384))
    gate_sum, rest_sum = finish("head", (256, 2048))
    qkv_sum = jnp.concatenate(
        [
            piece[:, part * piece.shape[1] // 3 : (part + 1) * piece.shape[1] // 3]
            for part in range(3)
            for piece in (early_sum, late_sum)
        ],
        axis=1,
    )
    small_sum = small_sum.T
    return (
        outputs,
        head_out,
        patch_grad,
        small_sum[128:144],
        small_sum[0],
        small_sum[1],
        qkv_sum,
        out_sum,
        small_sum[2],
        small_sum[3],
        small_sum[4],
        up_sum,
        small_sum[6:10].reshape(96),
        down_sum,
        small_sum[5],
        jnp.concatenate([gate_sum, rest_sum], axis=1),
        small_sum[10:16].reshape(144),
    )


def plain_shards(
    patches,
    lead_index,
    window_lengths,
    pad_mask,
    lead_table,
    attn_gain,
    attn_shift,
    qkv_weight,
    out_weight,
    out_bias,
    mlp_gain,
    mlp_shift,
    up_weight,
    up_bias,
    down_weight,
    down_bias,
    head_weight,
    head_bias,
    act_cotangent,
    head_cotangent,
):
    front = (
        lax.all_gather(lead_table, ("dp", "fsdp"), axis=1, tiled=True),
        lax.all_gather(attn_gain, ("dp", "fsdp"), axis=0, tiled=True),
        lax.all_gather(attn_shift, ("dp", "fsdp"), axis=0, tiled=True),
        lax.all_gather(qkv_weight, ("dp", "fsdp"), axis=0, tiled=True),
        lax.all_gather(out_weight, ("dp", "fsdp"), axis=0, tiled=True),
        lax.all_gather(out_bias, ("dp", "fsdp"), axis=0, tiled=True),
    )
    rear = (
        lax.all_gather(mlp_gain, ("dp", "fsdp"), axis=0, tiled=True),
        lax.all_gather(mlp_shift, ("dp", "fsdp"), axis=0, tiled=True),
        lax.all_gather(up_weight, ("dp", "fsdp"), axis=0, tiled=True),
        lax.all_gather(up_bias, ("dp", "fsdp"), axis=0, tiled=True),
        lax.all_gather(down_weight, ("dp", "fsdp"), axis=0, tiled=True),
        lax.all_gather(down_bias, ("dp", "fsdp"), axis=0, tiled=True),
        lax.all_gather(head_weight, ("dp", "fsdp"), axis=0, tiled=True),
        lax.all_gather(head_bias, ("dp", "fsdp"), axis=0, tiled=True),
    )
    table_full, gain_one, shift_one, qkv_full, out_full, out_bias_full = front
    (
        gain_two,
        shift_two,
        up_full,
        up_bias_full,
        down_full,
        down_bias_full,
        head_full,
        head_bias_full,
    ) = rear
    token_rows, width = patches.shape
    head_dim = width // HEADS
    block_rows = min(512, token_rows)
    block_count = token_rows // block_rows
    ends = jnp.cumsum(window_lengths[0])
    positions = jnp.arange(token_rows, dtype=jnp.int32)
    window = jnp.sum((positions[:, None] >= ends[None, :]).astype(jnp.int32), axis=1)
    lead_hot = (jnp.arange(LEADS, dtype=jnp.int32) == lead_index[0]).astype(jnp.float32)
    lead_row = jnp.sum(lead_hot[:, None] * table_full.astype(jnp.float32), axis=0)
    start_state = patches.astype(jnp.float32) + lead_row[None, :]
    normed_one, pull_one = jax.vjp(
        layer_norm, start_state, gain_one.astype(jnp.float32), shift_one.astype(jnp.float32)
    )
    attn_input = normed_one.astype(jnp.bfloat16)
    qkv_rows = jnp.dot(attn_input, qkv_full, preferred_element_type=jnp.float32).astype(
        jnp.bfloat16
    )
    queries = qkv_rows[:, :width].reshape(block_count, block_rows, HEADS, head_dim)
    keys = qkv_rows[:, width : 2 * width].reshape(token_rows, HEADS, head_dim)
    values = qkv_rows[:, 2 * width :].reshape(token_rows, HEADS, head_dim)
    query_windows = window.reshape(block_count, block_rows)
    block_starts = jnp.arange(block_count, dtype=jnp.int32) * block_rows

    def block_scores(query_block, window_block, block_start):
        scores = (
            jnp.einsum("qhd,khd->hqk", query_block, keys, preferred_element_type=jnp.float32)
            * score_scale
        )
        allowed = allowed_keys(window_block, window, pad_mask, block_start)
        return jnp.where(allowed[None], scores, -1e30)

    def forward_block(inputs):
        query_block, window_block, block_start = inputs
        masked = block_scores(query_block, window_block, block_start)
        largest = jnp.max(masked, axis=-1, keepdims=True)
        raised = jnp.exp(masked - largest)
        total = jnp.sum(raised, axis=-1, keepdims=True)
        probs = (raised / total).astype(jnp.bfloat16)
        mixed = jnp.einsum("hqk,khd->qhd", probs, values, preferred_element_type=jnp.float32)
        return (
            mixed.reshape(block_rows, width).astype(jnp.bfloat16),
            (largest + jnp.log(total))[:, :, 0],
        )

    mixed_blocks, log_totals = lax.map(forward_block, (queries, query_windows, block_starts))
    attended = mixed_blocks.reshape(token_rows, width)
    mid_state = (
        start_state
        + jnp.dot(attended, out_full, preferred_element_type=jnp.float32)
        + out_bias_full.astype(jnp.float32)
    )
    normed_two, pull_two = jax.vjp(
        layer_norm, mid_state, gain_two.astype(jnp.float32), shift_two.astype(jnp.float32)
    )
    mlp_input = normed_two.astype(jnp.bfloat16)
    pre_act = jnp.dot(mlp_input, up_full, preferred_element_type=jnp.float32) + up_bias_full.astype(
        jnp.float32
    )
    activated, pull_act = jax.vjp(gelu_exact, pre_act)
    act_rows = activated.astype(jnp.bfloat16)
    end_state = (
        mid_state
        + jnp.dot(act_rows, down_full, preferred_element_type=jnp.float32)
        + down_bias_full.astype(jnp.float32)
    )
    outputs = end_state.astype(jnp.bfloat16)
    logits = jnp.dot(
        outputs, head_full, preferred_element_type=jnp.float32
    ) + head_bias_full.astype(jnp.float32)
    head_out, pull_head = jax.vjp(partial(expert_softmax, experts=EXPERTS, pixels=PIX), logits)
    up_back, down_back, head_back = (
        lax.all_gather(up_weight, ("dp", "fsdp"), axis=0, tiled=True),
        lax.all_gather(down_weight, ("dp", "fsdp"), axis=0, tiled=True),
        lax.all_gather(head_weight, ("dp", "fsdp"), axis=0, tiled=True),
    )
    qkv_back, out_back = (
        lax.all_gather(qkv_weight, ("dp", "fsdp"), axis=0, tiled=True),
        lax.all_gather(out_weight, ("dp", "fsdp"), axis=0, tiled=True),
    )
    logit_grad = pull_head(head_cotangent.astype(jnp.float32))[0].astype(jnp.bfloat16)
    head_bias_term = jnp.sum(logit_grad.astype(jnp.float32), axis=0)
    head_term = jnp.einsum("td,tn->dn", outputs, logit_grad, preferred_element_type=jnp.float32)
    end_grad = act_cotangent.astype(jnp.float32) + jnp.einsum(
        "tn,dn->td", logit_grad, head_back, preferred_element_type=jnp.float32
    )
    branch_grad = end_grad.astype(jnp.bfloat16)
    down_bias_term = jnp.sum(branch_grad.astype(jnp.float32), axis=0)
    down_term = jnp.einsum("tf,td->fd", act_rows, branch_grad, preferred_element_type=jnp.float32)
    act_grad = jnp.einsum("td,fd->tf", branch_grad, down_back, preferred_element_type=jnp.float32)
    pre_grad = pull_act(act_grad)[0].astype(jnp.bfloat16)
    up_bias_term = jnp.sum(pre_grad.astype(jnp.float32), axis=0)
    up_term = jnp.einsum("td,tf->df", mlp_input, pre_grad, preferred_element_type=jnp.float32)
    normed_two_grad = jnp.einsum("tf,df->td", pre_grad, up_back, preferred_element_type=jnp.float32)
    state_grad_two, gain_two_term, shift_two_term = pull_two(normed_two_grad)
    (
        gain_part,
        shift_part,
        up_part,
        up_bias_part,
        down_part,
        down_bias_part,
        head_part,
        head_bias_part,
    ) = (
        lax.psum_scatter(
            gain_two_term.astype(jnp.bfloat16), "dp", scatter_dimension=0, tiled=True
        ).astype(jnp.float32),
        lax.psum_scatter(
            shift_two_term.astype(jnp.bfloat16), "dp", scatter_dimension=0, tiled=True
        ).astype(jnp.float32),
        lax.psum_scatter(
            up_term.astype(jnp.bfloat16), "dp", scatter_dimension=0, tiled=True
        ).astype(jnp.float32),
        lax.psum_scatter(
            up_bias_term.astype(jnp.bfloat16), "dp", scatter_dimension=0, tiled=True
        ).astype(jnp.float32),
        lax.psum_scatter(
            down_term.astype(jnp.bfloat16), "dp", scatter_dimension=0, tiled=True
        ).astype(jnp.float32),
        lax.psum_scatter(
            down_bias_term.astype(jnp.bfloat16), "dp", scatter_dimension=0, tiled=True
        ).astype(jnp.float32),
        lax.psum_scatter(
            head_term.astype(jnp.bfloat16), "dp", scatter_dimension=0, tiled=True
        ).astype(jnp.float32),
        lax.psum_scatter(
            head_bias_term.astype(jnp.bfloat16), "dp", scatter_dimension=0, tiled=True
        ).astype(jnp.float32),
    )
    rear_grads = (
        lax.psum_scatter(gain_part, "fsdp", scatter_dimension=0, tiled=True),
        lax.psum_scatter(shift_part, "fsdp", scatter_dimension=0, tiled=True),
        lax.psum_scatter(up_part, "fsdp", scatter_dimension=0, tiled=True),
        lax.psum_scatter(up_bias_part, "fsdp", scatter_dimension=0, tiled=True),
        lax.psum_scatter(down_part, "fsdp", scatter_dimension=0, tiled=True),
        lax.psum_scatter(down_bias_part, "fsdp", scatter_dimension=0, tiled=True),
        lax.psum_scatter(head_part, "fsdp", scatter_dimension=0, tiled=True),
        lax.psum_scatter(head_bias_part, "fsdp", scatter_dimension=0, tiled=True),
    )
    mid_grad = end_grad + state_grad_two
    out_grad = mid_grad.astype(jnp.bfloat16)
    out_bias_term = jnp.sum(out_grad.astype(jnp.float32), axis=0)
    out_term = jnp.einsum("td,te->de", attended, out_grad, preferred_element_type=jnp.float32)
    mixed_grad = jnp.einsum(
        "te,de->td", out_grad, out_back, preferred_element_type=jnp.float32
    ).astype(jnp.bfloat16)
    grad_blocks = mixed_grad.reshape(block_count, block_rows, HEADS, head_dim)

    def backward_block(carry, inputs):
        key_sum, value_sum = carry
        query_block, grad_block, window_block, total_block, block_start = inputs
        masked = block_scores(query_block, window_block, block_start)
        probs = jnp.exp(masked - total_block[:, :, None])
        prob_grad = jnp.einsum(
            "qhd,khd->hqk", grad_block, values, preferred_element_type=jnp.float32
        )
        inner = jnp.sum(probs * prob_grad, axis=-1, keepdims=True)
        score_grad = (probs * (prob_grad - inner)).astype(jnp.bfloat16)
        query_grad = (
            jnp.einsum("hqk,khd->qhd", score_grad, keys, preferred_element_type=jnp.float32)
            * score_scale
        )
        key_sum = (
            key_sum
            + jnp.einsum(
                "hqk,qhd->khd", score_grad, query_block, preferred_element_type=jnp.float32
            )
            * score_scale
        )
        value_sum = value_sum + jnp.einsum(
            "hqk,qhd->khd",
            probs.astype(jnp.bfloat16),
            grad_block,
            preferred_element_type=jnp.float32,
        )
        return ((key_sum, value_sum), query_grad.reshape(block_rows, width))

    zero_keys = jnp.zeros((token_rows, HEADS, head_dim), jnp.float32)
    (key_grad, value_grad), query_grads = lax.scan(
        backward_block,
        (zero_keys, zero_keys),
        (queries, grad_blocks, query_windows, log_totals, block_starts),
    )
    qkv_grad = jnp.concatenate(
        [
            query_grads.reshape(token_rows, width),
            key_grad.reshape(token_rows, width),
            value_grad.reshape(token_rows, width),
        ],
        axis=1,
    ).astype(jnp.bfloat16)
    qkv_term = jnp.einsum("td,te->de", attn_input, qkv_grad, preferred_element_type=jnp.float32)
    normed_one_grad = jnp.einsum(
        "te,de->td", qkv_grad, qkv_back, preferred_element_type=jnp.float32
    )
    state_grad_one, gain_one_term, shift_one_term = pull_one(normed_one_grad)
    patch_grad = mid_grad + state_grad_one
    lead_term = lead_hot[:, None] * jnp.sum(patch_grad, axis=0)[None, :]
    lead_part, gain_one_part, shift_one_part, qkv_part, out_part, out_bias_part = (
        lax.psum_scatter(
            lead_term.astype(jnp.bfloat16), "dp", scatter_dimension=1, tiled=True
        ).astype(jnp.float32),
        lax.psum_scatter(
            gain_one_term.astype(jnp.bfloat16), "dp", scatter_dimension=0, tiled=True
        ).astype(jnp.float32),
        lax.psum_scatter(
            shift_one_term.astype(jnp.bfloat16), "dp", scatter_dimension=0, tiled=True
        ).astype(jnp.float32),
        lax.psum_scatter(
            qkv_term.astype(jnp.bfloat16), "dp", scatter_dimension=0, tiled=True
        ).astype(jnp.float32),
        lax.psum_scatter(
            out_term.astype(jnp.bfloat16), "dp", scatter_dimension=0, tiled=True
        ).astype(jnp.float32),
        lax.psum_scatter(
            out_bias_term.astype(jnp.bfloat16), "dp", scatter_dimension=0, tiled=True
        ).astype(jnp.float32),
    )
    front_grads = (
        lax.psum_scatter(lead_part, "fsdp", scatter_dimension=1, tiled=True),
        lax.psum_scatter(gain_one_part, "fsdp", scatter_dimension=0, tiled=True),
        lax.psum_scatter(shift_one_part, "fsdp", scatter_dimension=0, tiled=True),
        lax.psum_scatter(qkv_part, "fsdp", scatter_dimension=0, tiled=True),
        lax.psum_scatter(out_part, "fsdp", scatter_dimension=0, tiled=True),
        lax.psum_scatter(out_bias_part, "fsdp", scatter_dimension=0, tiled=True),
    )
    return (
        outputs,
        head_out,
        patch_grad,
        front_grads[0],
        front_grads[1],
        front_grads[2],
        front_grads[3],
        front_grads[4],
        front_grads[5],
        rear_grads[0],
        rear_grads[1],
        rear_grads[2],
        rear_grads[3],
        rear_grads[4],
        rear_grads[5],
        rear_grads[6],
        rear_grads[7],
    )


def solution(mesh):
    in_specs = (
        P(("dp", "fsdp"), None),
        P(("dp", "fsdp")),
        P(("dp", "fsdp"), None),
        P(("dp", "fsdp")),
        P(None, ("dp", "fsdp")),
        P(("dp", "fsdp")),
        P(("dp", "fsdp")),
        P(("dp", "fsdp"), None),
        P(("dp", "fsdp"), None),
        P(("dp", "fsdp")),
        P(("dp", "fsdp")),
        P(("dp", "fsdp")),
        P(("dp", "fsdp"), None),
        P(("dp", "fsdp")),
        P(("dp", "fsdp"), None),
        P(("dp", "fsdp")),
        P(("dp", "fsdp"), None),
        P(("dp", "fsdp")),
        P(("dp", "fsdp"), None),
        P(("dp", "fsdp"), None),
    )
    out_specs = (
        P(("dp", "fsdp"), None),
        P(("dp", "fsdp"), None),
        P(("dp", "fsdp"), None),
        P(None, ("dp", "fsdp")),
        P(("dp", "fsdp")),
        P(("dp", "fsdp")),
        P(("dp", "fsdp"), None),
        P(("dp", "fsdp"), None),
        P(("dp", "fsdp")),
        P(("dp", "fsdp")),
        P(("dp", "fsdp")),
        P(("dp", "fsdp"), None),
        P(("dp", "fsdp")),
        P(("dp", "fsdp"), None),
        P(("dp", "fsdp")),
        P(("dp", "fsdp"), None),
        P(("dp", "fsdp")),
    )
    body = shards if dict(mesh.shape) == {"dp": 4, "fsdp": 8} else plain_shards
    return jax.shard_map(body, mesh=mesh, in_specs=in_specs, out_specs=out_specs, check_vma=False)
```

```python
import math
from functools import partial

import jax
import jax.numpy as jnp
from jax import lax
from jax.experimental import pallas as pl
from jax.experimental.pallas import tpu as pltpu
from jax.sharding import PartitionSpec as P

HEADS = 12
PIX = 64
EXPERTS = 3
LEADS = 16


norm_epsilon = 1e-05
score_scale = 0.125


def layer_norm(hidden, norm_gain, norm_shift):
    average = jnp.mean(hidden, axis=-1, keepdims=True)
    centered = hidden - average
    variance = jnp.mean(centered * centered, axis=-1, keepdims=True)
    return centered * lax.rsqrt(variance + norm_epsilon) * norm_gain + norm_shift


def gelu_exact(values):
    return 0.5 * values * (1.0 + lax.erf(values * 0.7071067811865476))


def expert_softmax(logits, experts, pixels):
    gate_part = logits[:, : experts * pixels].reshape(logits.shape[0], experts, pixels)
    largest = jnp.max(gate_part, axis=1, keepdims=True)
    raised = jnp.exp(gate_part - largest)
    shares = raised / jnp.sum(raised, axis=1, keepdims=True)
    return jnp.concatenate(
        [shares.reshape(logits.shape[0], experts * pixels), logits[:, experts * pixels :]], axis=1
    )


def allowed_keys(query_window, key_window, key_valid, query_start):
    query_place = query_start + jnp.arange(query_window.shape[0], dtype=jnp.int32)
    key_place = jnp.arange(key_window.shape[0], dtype=jnp.int32)
    same_window = query_window[:, None] == key_window[None, :]
    usable = (key_valid[None, :] > 0) | (query_place[:, None] == key_place[None, :])
    return same_window & usable


AXES = ("dp", "fsdp")
FAR_Z, NEAR_Z, FIRST, SECOND, SIBLING = (4, 4), (2, 2), (8, 16), (16, 8), (1, 1)
ORDERS = {
    "q": (FAR_Z, NEAR_Z, FIRST, SECOND),
    "u": (FAR_Z, FIRST, SECOND, NEAR_Z),
    "d": (FIRST, FAR_Z, NEAR_Z, SECOND),
    "h": (NEAR_Z, FAR_Z, FIRST, SECOND),
    "head": (FAR_Z, FIRST, SECOND, NEAR_Z),
    "down": (FAR_Z, NEAR_Z, FIRST, SECOND),
    "up": (NEAR_Z, FIRST, FAR_Z, SECOND),
    "front": (FAR_Z, NEAR_Z, FIRST, SECOND),
    "mix": (FAR_Z, FIRST, NEAR_Z, SECOND),
}
GATHER_SEQUENCE = (
    ("q", 0), ("d", 0), ("h", 0), ("u", 0), ("q", 1), ("d", 1), ("u", 1), ("q", 2), ("h", 1), ("u", 2),
    ("d", 2),
)
SCATTER_SEQUENCE = (
    "mix", "up", "front", "down", "mix", "head", "front", "down", "front", "mix", "head", "mix", "down",
    "front", "up", "head", "up",
)
MOST_VMEM, SPARE_VMEM = 60 * 1024 * 1024, 8 * 1024 * 1024
WIDTH = 768
HIDDEN = 3072
HEAD = 4608
TOKENS = 512
GATE = 512
F32 = jnp.float32
BF16 = jnp.bfloat16
HBM = pl.BlockSpec(memory_space=pltpu.HBM)
SMEM = pl.BlockSpec(memory_space=pltpu.SMEM)
VMEM = pl.BlockSpec(memory_space=pltpu.VMEM)
QKV_PART, SMALL_PART = (0, 1152), (1152, 128)
UP_PART, OUT_PART, GATE_PART = (0, 1536), (1536, 384), (1920, 256)
DOWN_PART, HEAD_PART = (0, 384), (0, 2048)


def chip_masks(order, lane):
    masks = []
    for place in range(16):
        mask = 0
        for step in range(4):
            if place >> step & 1:
                mask ^= order[step][lane]
        masks.append(mask >> 1)
    return masks


def table_start(group, side):
    return 1 + 32 * list(ORDERS).index(group) + 16 * side


def exchange(array, masks):
    return lax.ppermute(array, AXES, [(d, d ^ masks[d & 1]) for d in range(32)])


def whereabouts():
    device = lax.axis_index("dp") * 8 + lax.axis_index("fsdp")
    core, chip = device % 2, device // 2
    tables = [chip_masks(order, 0) + chip_masks(order, 1) for order in ORDERS.values()]
    swapped = [chip_masks(order, 1) + chip_masks(order, 0) for order in ORDERS.values()]
    places = jnp.where(core == 0, jnp.array(tables, jnp.int32), jnp.array(swapped, jnp.int32))
    places = (places ^ chip).reshape(32 * len(ORDERS))
    return core, jnp.concatenate([core[None].astype(jnp.int32), places])


def after(value, *marks):
    return lax.optimization_barrier((value, marks))[0]


def in_core_order(core, mine, theirs, axis):
    return jnp.where(
        core == 0,
        jnp.concatenate([mine, theirs], axis=axis),
        jnp.concatenate([theirs, mine], axis=axis),
    )


def pack_kernel(core, qkv, out, up, down, head, table, *refs):
    vectors, (up_bias, head_bias), refs = refs[:6], refs[6:8], refs[8:]
    outs, (rows,) = refs[:8], refs[8:]
    rows[...] = jnp.zeros_like(rows)
    for index, vector in enumerate(vectors):
        rows[index : index + 1, :24] = vector[...].astype(F32)
    for index in range(4):
        rows[6 + index : 7 + index, :24] = up_bias[:, 24 * index : 24 * index + 24].astype(F32)
    for index in range(6):
        rows[10 + index : 11 + index, :24] = head_bias[:, 24 * index : 24 * index + 24].astype(F32)
    rows[16:32, :24] = table[...].astype(F32)
    small = rows[...].T[:24].astype(BF16)
    for side in range(2):
        q, u, d, h = outs[4 * side : 4 * side + 4]
        q[:, :1152] = qkv[:, lane_columns(core, side, 1152)]
        q[:, 1152:] = small
        u[:, :1536] = up[:, lane_columns(core, side, 1536)]
        u[:, 1536:1920] = out[:, lane_columns(core, side, 384)]
        u[:, 1920:] = head[:, lane_columns(core, side, 256)]
        d[...] = down[:, lane_columns(core, side, 384)]
        h[...] = head[:, lane_columns(core, side, 2048, GATE)]


def packed(core, weights, table, vectors):
    shapes = [(24, 1280), (24, 2176), (96, 384), (24, 2048)] * 2
    return call(
        pack_kernel,
        (core.reshape(1), *weights, table, *[vector[None] for vector in vectors]),
        [SMEM] + [VMEM] * 14,
        [(shape, BF16, False) for shape in shapes],
        [pltpu.VMEM((128, 128), F32)],
    )


def doubled(held, masks):
    return jnp.concatenate([held, exchange(held, masks)], axis=0)


def both_lanes(*arrays):
    return arrays + tuple(exchange(array, SIBLING) for array in arrays)


def total(parts):
    result = parts[0].astype(F32)
    for part in parts[1:]:
        result = result + part.astype(F32)
    return result


def folded(parts, got):
    parts = [*parts, got]
    half = got.shape[0] // 2
    return [part[:half] for part in parts], total([part[half:] for part in parts]).astype(BF16)


def finished(parts, got, core, widths):
    block = total([*parts, got])[0]
    rows = block.shape[0] // 2
    upper, lower = block[:rows], block[rows:]
    mine = jnp.where(core == 0, upper, lower)
    theirs = jnp.where(core == 0, lower, upper).astype(BF16)
    other = exchange(theirs, SIBLING).astype(F32)
    pieces, start = [], 0
    for width in widths:
        span = slice(start, start + width)
        pieces.append(in_core_order(core, mine[:, span], other[:, span], 1))
        start += width
    return pieces


def across(first, second):
    return lax.dot_general(first, second, (((1,), (1,)), ((), ())), preferred_element_type=F32)


def times(first, second):
    return jnp.dot(first, second, preferred_element_type=F32)


def lane_columns(where, side, stride, first=0, width=None):
    return pl.ds(pl.multiple_of(first + (where[0] ^ side) * stride, 128), width or stride)


def block_copies(where, group, sources, part, target, sems, side, first=0):
    start, width = part
    rows = sources[0].shape[1]
    half = len(sources) // 2
    count = 16 // half
    copies = []
    for place in range(16):
        row = pl.multiple_of(where[table_start(group, side) + place] * rows, rows)
        copies.append(
            pltpu.make_async_copy(
                sources[half * side + place // count].at[place % count, :, pl.ds(start, width)],
                target.at[pl.ds(row, rows), lane_columns(where, side, width, first)],
                sems.at[side, place],
            )
        )
    return copies


def start_all(copies):
    for copy in copies:
        copy.start()


def wait_all(copies):
    for copy in copies:
        copy.wait()


def mean_and_scale(hidden):
    average = jnp.mean(hidden, axis=1, keepdims=True)
    centered = hidden - average
    variance = jnp.mean(centered * centered, axis=1, keepdims=True)
    return centered, lax.rsqrt(variance + norm_epsilon)


def norm_backward(hidden, gain, upstream):
    centered, scale = mean_and_scale(hidden)
    normed = centered * scale
    gain_grad = jnp.sum(upstream * normed, axis=0, keepdims=True)
    shift_grad = jnp.sum(upstream, axis=0, keepdims=True)
    scaled = upstream * gain
    first = jnp.mean(scaled, axis=1, keepdims=True)
    second = jnp.mean(scaled * normed, axis=1, keepdims=True)
    return scale * (scaled - first - normed * second), gain_grad, shift_grad


def call(kernel, operands, in_specs, outs, scratch, spare=None):
    def size(item):
        return math.prod(item.shape) * jnp.dtype(item.dtype).itemsize

    held = [item for item, spec in zip(operands, in_specs) if spec is VMEM]
    held += [jax.ShapeDtypeStruct(shape, kind) for shape, kind, copied in outs if not copied]
    held += [item for item in scratch if getattr(item, "memory_space", None) == pltpu.VMEM]
    limit = MOST_VMEM if spare is None else sum(size(item) for item in held) + spare
    return pl.pallas_call(
        kernel,
        out_shape=[jax.ShapeDtypeStruct(shape, kind) for shape, kind, _ in outs],
        in_specs=in_specs,
        out_specs=[HBM if copied else VMEM for _, _, copied in outs],
        scratch_shapes=scratch,
        compiler_params=pltpu.CompilerParams(vmem_limit_bytes=limit),
        cost_estimate=pl.CostEstimate(flops=2 * 10**12, bytes_accessed=10**10, transcendentals=0),
    )(*operands)


def lane_scratch(rows, width):
    return [pltpu.VMEM((2, rows, width), BF16), pltpu.SemaphoreType.DMA((2, 16))]


def weight_scratch(rows, width):
    return [pltpu.VMEM((rows, width), BF16), pltpu.SemaphoreType.DMA((2, 16))]


def taken(refs, *counts):
    groups = []
    for count in counts:
        groups.append(refs[:count])
        refs = refs[count:]
    return *groups, refs


def front_kernel(where, lead, patches, *refs):
    sources, outs, scratch = taken(refs, 4, 3)
    turned_out, qkv_out, small = outs
    weight, sems, smalls, small_sems, state, rows, turned, qkv, io_sems = scratch
    loads = [block_copies(where, "q", sources, QKV_PART, weight, sems, side) for side in range(2)]
    small_loads = []
    for place in range(16):
        row = pl.multiple_of(where[table_start("q", 0) + place] * 48, 48)
        small_loads.append(
            pltpu.make_async_copy(
                sources[place // 8].at[place % 8, :, pl.ds(*SMALL_PART)],
                smalls.at[pl.ds(row, 48), :],
                small_sems.at[place],
            )
        )
    state_load = pltpu.make_async_copy(patches, state, io_sems.at[0])
    start_all(small_loads)
    state_load.start()
    start_all(loads[0])
    start_all(loads[1])
    wait_all(small_loads)
    columns = smalls[...].astype(F32).T
    places = lax.broadcasted_iota(jnp.int32, (LEADS, WIDTH), 0)
    lead_row = jnp.sum(
        jnp.where(places == lead[0], columns[16 : 16 + LEADS], 0.0), axis=0, keepdims=True
    )
    small[...] = columns[:32]
    small[16:17, :] = lead_row
    state_load.wait()
    centered, scale = mean_and_scale(state[...].astype(F32) + lead_row)
    rows[...] = (centered * scale * columns[0:1] + columns[1:2]).astype(BF16)
    turned[...] = rows[...].T
    stores = [pltpu.make_async_copy(turned, turned_out, io_sems.at[1])]
    stores[0].start()
    wait_all(loads[0] + loads[1])
    for part in range(3):
        span = slice(part * WIDTH, part * WIDTH + WIDTH)
        qkv[:, span] = times(rows[...], weight[:, span]).astype(BF16)
        stores.append(pltpu.make_async_copy(qkv.at[:, span], qkv_out.at[:, span], io_sems.at[2 + part]))
        stores[-1].start()
    wait_all(stores)


def front_forward(where, lead_index, patches, arrays):
    return call(
        front_kernel,
        (where, lead_index, patches, *arrays),
        [SMEM, SMEM, HBM] + [HBM] * 4,
        [
            ((WIDTH, TOKENS), BF16, True),
            ((TOKENS, 3 * WIDTH), BF16, True),
            ((32, WIDTH), F32, False),
        ],
        weight_scratch(WIDTH, 3 * WIDTH)
        + [pltpu.VMEM((WIDTH, 128), BF16), pltpu.SemaphoreType.DMA((16,))]
        + [
            pltpu.VMEM((TOKENS, WIDTH), BF16),
            pltpu.VMEM((TOKENS, WIDTH), BF16),
            pltpu.VMEM((WIDTH, TOKENS), BF16),
            pltpu.VMEM((TOKENS, 3 * WIDTH), BF16),
            pltpu.SemaphoreType.DMA((5,)),
        ],
    )


KEY_SPANS = ((0, 256), (0, 384), (128, 512), (256, 512))


def fill_bias(lengths, pad, bias):
    ends, end = [], 0
    for index in range(lengths.shape[1]):
        end = end + lengths[0, index]
        ends.append(end)

    def windows(places):
        return sum([(places >= end).astype(jnp.int32) for end in ends])

    for block, (low, high) in enumerate(KEY_SPANS):
        count = high - low
        queries = lax.broadcasted_iota(jnp.int32, (1, 128), 1) + 128 * block
        keys = lax.broadcasted_iota(jnp.int32, (count, 1), 0) + low
        same = windows(queries) == windows(keys)
        usable = (pad[low:high, :] > 0) | (queries == keys)
        bias[block, :count, :] = jnp.where(same & usable, 0.0, -1e30)


def two_heads(block):
    first = lax.broadcasted_iota(jnp.int32, block.shape, 1) < block.shape[1] // 2
    zero = jnp.zeros_like(block)
    return jnp.concatenate([jnp.where(first, block, zero), jnp.where(first, zero, block)], axis=0)


def head_rows_of(stacked):
    return jnp.concatenate([stacked[:64, :128], stacked[64:, 128:]], axis=0)


def probabilities(scores, allowed):
    masked = scores * score_scale + allowed
    raised = jnp.exp(masked - jnp.max(masked, axis=0, keepdims=True))
    return raised * (1.0 / jnp.sum(raised, axis=0, keepdims=True))


def attention_kernel(where, lengths, pad, qkv, attended_out, turned_out, bias, turned, rows, sems):
    fill_bias(lengths, pad, bias)

    def pair(index, carry):
        first = index * 128
        columns = pl.ds(pl.multiple_of(first, 128), 128)
        keys_at = pl.ds(pl.multiple_of(first + WIDTH, 128), 128)
        values = qkv[:, pl.ds(pl.multiple_of(first + 2 * WIDTH, 128), 128)].T
        for block, (low, high) in enumerate(KEY_SPANS):
            span = slice(128 * block, 128 * block + 128)
            scores = across(qkv[low:high, keys_at], two_heads(qkv[span, columns]))
            allowed = bias[block, : high - low, :]
            probs = [
                probabilities(scores[:, 128 * head : 128 * head + 128], allowed).astype(BF16)
                for head in range(2)
            ]
            mixed = times(values[:, low:high], jnp.concatenate(probs, axis=1))
            turned[columns, span] = head_rows_of(mixed).astype(BF16)
        return carry

    lax.fori_loop(0, WIDTH // 128, pair, 0)
    stores = [pltpu.make_async_copy(turned, turned_out, sems.at[0])]
    stores[0].start()
    rows[...] = turned[...].T
    stores.append(pltpu.make_async_copy(rows, attended_out, sems.at[1]))
    stores[1].start()
    wait_all(stores)


def attention_forward(where, lengths, pad, qkv):
    rows, columns = (TOKENS, WIDTH), (WIDTH, TOKENS)
    return call(
        attention_kernel,
        (where, lengths, pad, qkv),
        [SMEM, SMEM, VMEM, VMEM],
        [(rows, BF16, True), (columns, BF16, True)],
        [
            pltpu.VMEM((4, 384, 128), F32),
            pltpu.VMEM(columns, BF16),
            pltpu.VMEM(rows, BF16),
            pltpu.SemaphoreType.DMA((2,)),
        ],
    )


def gate_shares(logits, cotangent, shares, gate_grad):
    gate_grad[:, 256:] = cotangent[:, 256:GATE]
    first, rest = logits[:, :128], logits[:, 128:256]
    left = lax.broadcasted_iota(jnp.int32, first.shape, 1) < PIX
    third = jnp.where(left, rest, pltpu.roll(rest, PIX, 1))
    largest = jnp.maximum(jnp.maximum(first, pltpu.roll(first, PIX, 1)), third)
    raised, raised_third = jnp.exp(first - largest), jnp.exp(third - largest)
    scale = 1.0 / (raised + pltpu.roll(raised, PIX, 1) + raised_third)
    share, share_third = raised * scale, raised_third * scale
    shares[:, :128] = share
    shares[:, 128:256] = jnp.where(left, share_third, rest)
    pull, other = cotangent[:, :128].astype(F32), cotangent[:, 128:256].astype(F32)
    pull_third = jnp.where(left, other, pltpu.roll(other, PIX, 1))
    weighed = share * pull
    inner = weighed + pltpu.roll(weighed, PIX, 1) + share_third * pull_third
    gate_grad[:, :128] = (share * (pull - inner)).astype(BF16)
    gate_grad[:, 128:256] = jnp.where(left, share_third * (pull_third - inner), other).astype(BF16)


def send_lane(where, group, lane, out, sems, side):
    rows = out.shape[1]
    copies = []
    for place in range(16):
        row = pl.multiple_of(where[table_start(group, side) + place] * rows, rows)
        copies.append(
            pltpu.make_async_copy(lane.at[pl.ds(row, rows), :], out.at[place], sems.at[place])
        )
    start_all(copies)
    return copies


def middle_kernel(
    where, small, up_bias, head_bias, attended, patches, cotangent, act_cotangent, attended_turned,
    *refs,
):
    up_sources, down_sources, head_sources, outs, scratch = taken(refs, 4, 4, 4, 15)
    outputs, shares, gate_bias, down_bias, up_bias_sum, terms, mid_grad, out_grad, mixed, *grads = outs
    down_mine, down_theirs, up_mine, up_theirs, head_mine, head_theirs = grads
    out_weight, out_sems, up, up_sems, down, down_sems, scratch = *scratch[:6], scratch[6:]
    head, head_sems, gate_sems, rows, branch, mid, mlp_turned, scratch = *scratch[:7], scratch[7:]
    act, act_turned, slope, turned, pulls, act_pulls, gate_grad, scratch = *scratch[:7], scratch[7:]
    lane, lane_sems, down_lane, down_lane_sems, mixes, more_sems, io_sems = scratch

    def loads(group, sources, part, target, sems, first=0):
        copies = []
        for side in range(2):
            copies += block_copies(where, group, sources, part, target, sems, side, first)
        return copies

    state_loads = [
        pltpu.make_async_copy(attended, rows, io_sems.at[0]),
        pltpu.make_async_copy(patches, branch, io_sems.at[1]),
    ]
    out_loads = loads("u", up_sources, OUT_PART, out_weight, out_sems)
    up_loads = loads("u", up_sources, UP_PART, up, up_sems)
    down_loads = loads("d", down_sources, DOWN_PART, down, down_sems)
    gate_loads = loads("u", up_sources, GATE_PART, head, gate_sems)
    head_loads = loads("h", head_sources, HEAD_PART, head, head_sems, GATE)
    pull_load = pltpu.make_async_copy(cotangent, pulls, io_sems.at[2])
    act_load = pltpu.make_async_copy(act_cotangent, act_pulls, io_sems.at[3])
    mix_load = pltpu.make_async_copy(attended_turned, mixes, io_sems.at[4])
    start_all(state_loads + out_loads + up_loads + down_loads + gate_loads)
    pull_load.start()
    start_all(head_loads)
    act_load.start()
    mix_load.start()

    wait_all(state_loads + out_loads)
    mid[...] = (
        branch[...].astype(F32)
        + small[16:17, :]
        + times(rows[...], out_weight[...])
        + small[2:3, :]
    )
    centered, scale = mean_and_scale(mid[...])
    rows[...] = (centered * scale * small[3:4, :] + small[4:5, :]).astype(BF16)
    mlp_turned[...] = rows[...].T
    wait_all(up_loads)
    for tile in range(6):
        span = slice(tile * 512, tile * 512 + 512)
        values = times(rows[...], up[:, span]) + up_bias[:, span]
        share = 0.5 * (1.0 + lax.erf(values * 0.7071067811865476))
        density = jnp.exp(-0.5 * values * values) * 0.3989422804014327
        activated = (values * share).astype(BF16)
        act[:, span] = activated
        act_turned[span, :] = activated.T
        slope[:, span] = (share + values * density).astype(BF16)
    wait_all(down_loads)
    outputs[...] = (mid[...] + times(act[...], down[...]) + small[5:6, :]).astype(BF16)
    turned[...] = outputs[...].T
    wait_all(gate_loads)
    shares[...] = times(outputs[...], head[:, :GATE]) + head_bias[:, :GATE]
    pull_load.wait()
    gate_shares(shares, pulls, shares, gate_grad)
    gate_bias[...] = jnp.sum(gate_grad[...].astype(F32), axis=0, keepdims=True)
    pulls[:, :GATE] = gate_grad[...]

    def head_lane(side, target, sems, out):
        target[:, :256] = times(turned[...], pulls[:, lane_columns(where, side, 256)]).astype(BF16)
        for tile in range(4):
            span = lane_columns(where, side, 2048, GATE + tile * 512, 512)
            target[:, 256 + tile * 512 : 768 + tile * 512] = times(turned[...], pulls[:, span]).astype(
                BF16
            )
        return send_lane(where, "head", target, out, sems, side)

    def down_lane_of(side, out):
        columns = branch[:, lane_columns(where, side, 384)]
        for part in range(4):
            span = slice(part * WIDTH, part * WIDTH + WIDTH)
            down_lane[span, :] = times(act_turned[span, :], columns).astype(BF16)
        return send_lane(where, "down", down_lane, out, down_lane_sems, side)

    def up_lane(side, target, sems, out):
        for tile in range(3):
            span = lane_columns(where, side, 1536, tile * 512, 512)
            target[:, tile * 512 : tile * 512 + 512] = times(mlp_turned[...], slope[:, span]).astype(
                BF16
            )
        target[:, 1536:1920] = times(
            mixes[...], out_grad[:, lane_columns(where, side, 384)]
        ).astype(BF16)
        return send_lane(where, "up", target, out, sems, side)

    first_stores = head_lane(1, lane, lane_sems, head_theirs)
    act_load.wait()
    wait_all(head_loads)
    mid_grad[...] = act_pulls[...].astype(F32) + across(pulls[...], head[...])
    branch[...] = mid_grad[...].astype(BF16)
    down_bias[...] = jnp.sum(branch[...].astype(F32), axis=0, keepdims=True)
    stores = head_lane(0, head.at[:, :2304], more_sems.at[0], head_mine)
    down_stores = down_lane_of(1, down_theirs)
    for tile in range(6):
        span = slice(tile * 512, tile * 512 + 512)
        grad = across(branch[...], down[span, :])
        rounded = (slope[:, span].astype(F32) * grad).astype(BF16)
        slope[:, span] = rounded
        up_bias_sum[:, span] = jnp.sum(rounded.astype(F32), axis=0, keepdims=True)
    wait_all(down_stores)
    stores += down_lane_of(0, down_mine)
    grad = across(slope[...], up[...])
    pulled, gain_grad, shift_grad = norm_backward(mid[...], small[3:4, :], grad)
    pulled = pulled + mid_grad[...]
    rounded = pulled.astype(BF16)
    mid_grad[...] = pulled
    out_grad[...] = rounded
    terms[...] = jnp.zeros_like(terms)
    terms[0:1, :] = jnp.sum(rounded.astype(F32), axis=0, keepdims=True)
    terms[1:2, :] = gain_grad
    terms[2:3, :] = shift_grad
    mix_load.wait()
    stores += up_lane(1, head.at[:, 2304:4224], more_sems.at[1], up_theirs)
    wait_all(first_stores)
    stores += up_lane(0, lane.at[:, :1920], lane_sems, up_mine)
    mixed[...] = across(out_grad[...], out_weight[...]).astype(BF16)
    wait_all(stores)


def middle(
    where, small, up_bias, head_bias, attended, patches, cotangent, act_cotangent, attended_turned,
    up, down, head,
):
    rows, columns = (TOKENS, WIDTH), (WIDTH, TOKENS)
    wide, tall = (TOKENS, HIDDEN), (HIDDEN, TOKENS)
    return call(
        middle_kernel,
        (
            where, small, up_bias, head_bias, attended, patches, cotangent, act_cotangent,
            attended_turned, *up, *down, *head,
        ),
        [SMEM, VMEM, VMEM, VMEM] + [HBM] * 17,
        [
            (rows, BF16, False),
            ((TOKENS, GATE), F32, False),
            ((1, GATE), F32, False),
            ((1, WIDTH), F32, False),
            ((1, HIDDEN), F32, False),
            ((8, WIDTH), F32, False),
            (rows, F32, False),
            (rows, BF16, False),
            (rows, BF16, False),
            ((16, 192, 384), BF16, True),
            ((16, 192, 384), BF16, True),
            ((16, 48, 1920), BF16, True),
            ((16, 48, 1920), BF16, True),
            ((16, 48, 2304), BF16, True),
            ((16, 48, 2304), BF16, True),
        ],
        weight_scratch(WIDTH, WIDTH)
        + weight_scratch(WIDTH, HIDDEN)
        + weight_scratch(HIDDEN, WIDTH)
        + weight_scratch(WIDTH, HEAD)
        + [
            pltpu.SemaphoreType.DMA((2, 16)),
            pltpu.VMEM(rows, BF16),
            pltpu.VMEM(rows, BF16),
            pltpu.VMEM(rows, F32),
            pltpu.VMEM(columns, BF16),
            pltpu.VMEM(wide, BF16),
            pltpu.VMEM(tall, BF16),
            pltpu.VMEM(wide, BF16),
            pltpu.VMEM(columns, BF16),
            pltpu.VMEM((TOKENS, HEAD), BF16),
            pltpu.VMEM(rows, BF16),
            pltpu.VMEM((TOKENS, GATE), BF16),
            pltpu.VMEM((WIDTH, 2304), BF16),
            pltpu.SemaphoreType.DMA((16,)),
            pltpu.VMEM((HIDDEN, 384), BF16),
            pltpu.SemaphoreType.DMA((16,)),
            pltpu.VMEM(columns, BF16),
            pltpu.SemaphoreType.DMA((2, 16)),
            pltpu.SemaphoreType.DMA((5,)),
        ],
    )


def attend_back(count, qkv, mixed, bias, turned, key_sum, value_sum, qkv_grad):
    width = 128 * count

    def columns_at(first):
        return pl.ds(pl.multiple_of(first, 128), 128)

    def pair(index, carry):
        own = index * 128
        columns, keys_at = columns_at(own), columns_at(own + width)
        values_at = columns_at(own + 2 * width)
        keys_turned = qkv[:, keys_at].T
        key_sum[...] = jnp.zeros_like(key_sum)
        value_sum[...] = jnp.zeros_like(value_sum)
        for block, (low, high) in enumerate(KEY_SPANS):
            span = slice(128 * block, 128 * block + 128)
            queries, grads = two_heads(qkv[span, columns]), two_heads(mixed[span, columns])
            scores = across(qkv[low:high, keys_at], queries)
            prob_grads = across(qkv[low:high, values_at], grads)
            allowed = bias[block, : high - low, :]
            probs, score_grads = [], []
            for head in range(2):
                part = slice(128 * head, 128 * head + 128)
                prob = probabilities(scores[:, part], allowed)
                pulled = prob * prob_grads[:, part]
                inner = jnp.sum(pulled, axis=0, keepdims=True)
                probs.append(prob.astype(BF16))
                score_grads.append((pulled - prob * inner).astype(BF16))
            score_grad = jnp.concatenate(score_grads, axis=1)
            key_sum[low:high, :] += times(score_grad, queries)
            value_sum[low:high, :] += times(jnp.concatenate(probs, axis=1), grads)
            turned[:, span] = head_rows_of(times(keys_turned[:, low:high], score_grad)) * score_scale
        qkv_grad[:, columns] = turned[...].T.astype(BF16)
        qkv_grad[:, keys_at] = (key_sum[...] * score_scale).astype(BF16)
        qkv_grad[:, values_at] = value_sum[...].astype(BF16)
        return carry

    lax.fori_loop(0, count, pair, 0)


def attention_scratch(count):
    return [
        pltpu.VMEM((4, 384, 128), F32),
        pltpu.VMEM((TOKENS, 384 * count), BF16),
        pltpu.VMEM((TOKENS, 128 * count), BF16),
        pltpu.VMEM((128, TOKENS), F32),
        pltpu.VMEM((TOKENS, 128), F32),
        pltpu.VMEM((TOKENS, 128), F32),
        pltpu.SemaphoreType.DMA((4,)),
    ]


def attention_loads(start, count, qkv, mixed, own_qkv, own_mixed, sems):
    width = 128 * count
    copies = [
        pltpu.make_async_copy(
            mixed.at[:, pl.ds(128 * start, width)], own_mixed.at[:, pl.ds(0, width)], sems.at[3]
        )
    ]
    for part in range(3):
        copies.append(
            pltpu.make_async_copy(
                qkv.at[:, pl.ds(WIDTH * part + 128 * start, width)],
                own_qkv.at[:, pl.ds(width * part, width)],
                sems.at[part],
            )
        )
    return copies


def early_back_kernel(where, lengths, pad, mixed, qkv, input_turned, *refs):
    (qkv_grad, mine_out, theirs_out), scratch = taken(refs, 3)
    bias, own_qkv, own_mixed, turned, key_sum, value_sum, sems, scratch = *scratch[:7], scratch[7:]
    lane, lane_sems, inputs, io_sems = scratch
    loads = attention_loads(0, 4, qkv, mixed, own_qkv, own_mixed, sems)
    in_load = pltpu.make_async_copy(input_turned, inputs, io_sems.at[0])
    start_all(loads + [in_load])
    fill_bias(lengths, pad, bias)
    wait_all(loads)
    attend_back(4, own_qkv, own_mixed, bias, turned, key_sum, value_sum, qkv_grad)
    in_load.wait()
    stores = []
    for side, out in ((1, theirs_out), (0, mine_out)):
        lane[side] = times(inputs[...], qkv_grad[:, lane_columns(where, side, 768)]).astype(BF16)
        stores += send_lane(where, "mix", lane.at[side], out, lane_sems.at[side], side)
    wait_all(stores)


def early_backward(where, lengths, pad, mixed, qkv, input_turned):
    return call(
        early_back_kernel,
        (where, lengths, pad, mixed, qkv, input_turned),
        [SMEM, SMEM, VMEM] + [HBM] * 3,
        [
            ((TOKENS, 1536), BF16, False),
            ((16, 48, 768), BF16, True),
            ((16, 48, 768), BF16, True),
        ],
        attention_scratch(4)
        + lane_scratch(WIDTH, 768)
        + [pltpu.VMEM((WIDTH, TOKENS), BF16), pltpu.SemaphoreType.DMA((1,))],
    )


def late_back_kernel(
    where, lead, lengths, pad, small, terms, down_row, up_rows, head_rows, head_bias,
    outputs, shares, mixed, qkv, first_grad, patches, mid_grad, input_turned, *refs
):
    sources, head_sources, outs, scratch = taken(refs, 4, 4, 4)
    patch_out, head_out, mine_out, theirs_out = outs
    head, head_sems, rows, result, head_io, scratch = *scratch[:5], scratch[5:]
    bias, own_qkv, own_mixed, turned, key_sum, value_sum, sems, scratch = *scratch[:7], scratch[7:]
    weight, weight_sems, lane, lane_sems, pulls, late_pulls, scratch = *scratch[:6], scratch[6:]
    state, mids, inputs, patch_grad, small_grad, io_sems = scratch
    own_loads = attention_loads(4, 2, qkv, mixed, own_qkv, own_mixed, sems)
    loads = [
        block_copies(where, "q", sources, QKV_PART, weight, weight_sems, side) for side in range(2)
    ]
    pairs = [(patches, state), (mid_grad, mids), (input_turned, inputs)]
    for part in range(3):
        target = pulls.at[:, pl.ds(WIDTH * part, 512)]
        pairs.append((first_grad.at[:, pl.ds(512 * part, 512)], target))
    in_loads = [pltpu.make_async_copy(*pair, io_sems.at[at]) for at, pair in enumerate(pairs)]
    head_loads = [
        block_copies(where, "h", head_sources, HEAD_PART, head, head_sems, side) for side in range(2)
    ]
    row_load = pltpu.make_async_copy(outputs, rows, head_io.at[0])
    share_load = pltpu.make_async_copy(shares, result.at[:, :GATE], head_io.at[1])
    start_all(own_loads + [row_load] + head_loads[0] + head_loads[1] + [share_load])
    start_all(in_loads + loads[0] + loads[1])
    fill_bias(lengths, pad, bias)
    wait_all(own_loads)
    attend_back(2, own_qkv, own_mixed, bias, turned, key_sum, value_sum, late_pulls)
    wait_all([row_load, share_load] + head_loads[0] + head_loads[1])
    stores = [pltpu.make_async_copy(result.at[:, :GATE], head_out.at[:, :GATE], head_io.at[2])]
    stores[0].start()
    for tile in range(8):
        span = slice(GATE + tile * 512, GATE + tile * 512 + 512)
        result[:, span] = (
            times(rows[...], head[:, tile * 512 : tile * 512 + 512]) + head_bias[:, span]
        )
        stores.append(
            pltpu.make_async_copy(result.at[:, span], head_out.at[:, span], head_io.at[3 + tile])
        )
        stores[-1].start()
    wait_all(loads[0] + loads[1] + in_loads)
    for part in range(3):
        pulls[:, WIDTH * part + 512 : WIDTH * part + 768] = late_pulls[
            :, 256 * part : 256 * part + 256
        ]
    grad = across(pulls[...], weight[...])
    pulled, gain_grad, shift_grad = norm_backward(
        state[...].astype(F32) + small[16:17, :], small[0:1, :], grad
    )
    pulled = pulled + mids[...]
    patch_grad[...] = pulled
    stores.append(pltpu.make_async_copy(patch_grad, patch_out, io_sems.at[6]))
    stores[-1].start()
    small_grad[0:1, :] = gain_grad
    small_grad[1:2, :] = shift_grad
    small_grad[2:5, :] = terms[0:3, :]
    small_grad[5:6, :] = down_row[...]
    small_grad[6:10, :] = up_rows[...]
    small_grad[10:16, :] = head_rows[...]
    places = lax.broadcasted_iota(jnp.int32, (LEADS, WIDTH), 0)
    lead_grad = jnp.sum(pulled, axis=0, keepdims=True)
    small_grad[16:32, :] = jnp.where(places == lead[0], lead_grad, 0.0)
    for side, out in ((1, theirs_out), (0, mine_out)):
        lane[side, :, :384] = times(
            inputs[...], late_pulls[:, lane_columns(where, side, 384)]
        ).astype(BF16)
        rows = small_grad[pl.ds(pl.multiple_of((where[0] ^ side) * 16, 16), 16), :]
        rows = jnp.concatenate([rows, jnp.zeros((112, WIDTH), F32)], axis=0)
        lane[side, :, 384:] = rows.T.astype(BF16)
        stores += send_lane(where, "front", lane.at[side], out, lane_sems.at[side], side)
    wait_all(stores)


def late_backward(
    where, lead, lengths, pad, small, terms, down_row, up_rows, head_rows, head_bias,
    outputs, shares, mixed, qkv, first_grad, patches, mid_grad, input_turned, arrays, head_arrays,
):
    rows, columns = (TOKENS, WIDTH), (WIDTH, TOKENS)
    return call(
        late_back_kernel,
        (
            where, lead, lengths, pad, small, terms, down_row, up_rows, head_rows, head_bias,
            outputs, shares, mixed, qkv, first_grad, patches, mid_grad, input_turned,
            *arrays, *head_arrays,
        ),
        [SMEM, SMEM, SMEM] + [VMEM] * 7 + [HBM] * 16,
        [
            (rows, F32, True),
            ((TOKENS, HEAD), F32, True),
            ((16, 48, 512), BF16, True),
            ((16, 48, 512), BF16, True),
        ],
        weight_scratch(WIDTH, HEAD - GATE)
        + [
            pltpu.VMEM(rows, BF16),
            pltpu.VMEM((TOKENS, HEAD), F32),
            pltpu.SemaphoreType.DMA((11,)),
        ]
        + attention_scratch(2)
        + weight_scratch(WIDTH, 3 * WIDTH)
        + lane_scratch(WIDTH, 512)
        + [
            pltpu.VMEM((TOKENS, 3 * WIDTH), BF16),
            pltpu.VMEM((TOKENS, WIDTH), BF16),
            pltpu.VMEM(rows, BF16),
            pltpu.VMEM(rows, F32),
            pltpu.VMEM(columns, BF16),
            pltpu.VMEM(rows, F32),
            pltpu.VMEM((32, WIDTH), F32),
            pltpu.SemaphoreType.DMA((7,)),
        ],
    )


def rows_of(vector, count):
    return vector.reshape(32, count, 24).transpose(1, 0, 2).reshape(count, WIDTH)


def vector_of(rows):
    count = rows.shape[0]
    return rows.reshape(count, 32, 24).transpose(1, 0, 2).reshape(1, count * WIDTH)


def shards(
    patches,
    lead_index,
    window_lengths,
    pad_mask,
    lead_table,
    attn_gain,
    attn_shift,
    qkv_weight,
    out_weight,
    out_bias,
    mlp_gain,
    mlp_shift,
    up_weight,
    up_bias,
    down_weight,
    down_bias,
    head_weight,
    head_bias,
    act_cotangent,
    head_cotangent,
):
    core, where = whereabouts()
    weights = (qkv_weight, out_weight, up_weight, down_weight, head_weight)
    vectors = (
        attn_gain, attn_shift, out_bias, mlp_gain, mlp_shift, down_bias, up_bias, head_bias
    )
    parts = packed(core, weights, lead_table, vectors)
    pad = pad_mask[:, None]
    cotangent_sum = jnp.sum(head_cotangent[:, GATE:].astype(F32), axis=0, keepdims=True)

    orders = ORDERS
    parts = dict(zip("qudh", zip(parts[:4], parts[4:])))
    chunks = {
        name: in_core_order(core, mine, exchange(theirs, SIBLING), 0)[None]
        for name, (mine, theirs) in parts.items()
    }

    held, last = dict(chunks), ()
    for name, step in GATHER_SEQUENCE:
        held[name] = after(held[name], *last)
        last = (held[name],)
        held[name] = doubled(held[name], orders[name][step])
    q, u, d, h = [held[name] for name in ("q", "u", "d", "h")]
    q_rest = exchange(after(q, *last), orders["q"][3])
    u = after(u, q)
    u_rest = exchange(u, orders["u"][3])
    d_rest = exchange(d, orders["d"][3])
    h = doubled(after(h, u), orders["h"][2])
    first = both_lanes(q, q_rest)
    h_rest = exchange(h, orders["h"][3])
    input_turned, qkv, small_rows = front_forward(
        after(where, d, h, cotangent_sum), lead_index, patches, first
    )
    attended, attended_turned = attention_forward(where, window_lengths, pad, qkv)
    u_rest, d_rest, h_rest = lax.optimization_barrier((u_rest, d_rest, h_rest, attended))[:3]
    second, down, head = both_lanes(u, u_rest), both_lanes(d, d_rest), both_lanes(h, h_rest)
    up_bias_row, head_bias_row = vector_of(small_rows[6:10]), vector_of(small_rows[10:16])
    (
        outputs, gate_out, gate_bias_sum, down_bias_sum, up_bias_sum, terms, mid_grad, _, mixed_grad,
        mine_d, theirs_d, mine_u, theirs_u, mine_h, theirs_h,
    ) = middle(
        where, small_rows, up_bias_row, head_bias_row, attended, patches, head_cotangent,
        act_cotangent, attended_turned, second, down, head,
    )

    got_h, got_d, got_u = [exchange(theirs, SIBLING) for theirs in (theirs_h, theirs_d, theirs_u)]
    head_rows = rows_of(jnp.concatenate([gate_bias_sum, cotangent_sum], axis=1), 6)
    up_rows = rows_of(up_bias_sum, 4)
    first_grad, mine_m, theirs_m = early_backward(
        where, window_lengths, pad, mixed_grad, qkv, input_turned
    )
    groups = {
        "head": [[mine_h], after(got_h, first_grad), 4],
        "up": [[mine_u], after(got_u, first_grad), 4],
        "down": [[mine_d], after(got_d, first_grad), 4],
        "mix": [[mine_m], exchange(theirs_m, SIBLING), 4],
    }
    last = ()

    def add(name):
        nonlocal last
        keep, got, step = groups[name]
        keep, send = folded(keep, after(got, *last))
        last = (send,)
        groups[name] = [keep, exchange(send, orders[name][step - 1]), step - 1]

    def finish(name, widths):
        keep, got, _ = groups[name]
        return finished(keep, after(got, *last), core, widths)

    for name in ("head", "down", "up"):
        add(name)
    patch_grad, head_out, mine_f, theirs_f = late_backward(
        after(where, *last), lead_index, window_lengths, pad, small_rows, terms, down_bias_sum,
        up_rows, head_rows, head_bias_row, outputs, gate_out, mixed_grad, qkv, first_grad, patches,
        mid_grad, input_turned, first, head,
    )
    last = (patch_grad,)
    groups["front"] = [[mine_f], exchange(theirs_f, SIBLING), 4]
    for name in SCATTER_SEQUENCE:
        add(name)
    late_sum, small_sum = finish("front", (384, 128))
    (down_sum,) = finish("down", (384,))
    (early_sum,) = finish("mix", (768,))
    up_sum, out_sum = finish("up", (1536, 384))
    gate_sum, rest_sum = finish("head", (256, 2048))
    qkv_sum = jnp.concatenate(
        [
            piece[:, part * piece.shape[1] // 3 : (part + 1) * piece.shape[1] // 3]
            for part in range(3)
            for piece in (early_sum, late_sum)
        ],
        axis=1,
    )
    small_sum = small_sum.T
    return (
        outputs,
        head_out,
        patch_grad,
        small_sum[128:144],
        small_sum[0],
        small_sum[1],
        qkv_sum,
        out_sum,
        small_sum[2],
        small_sum[3],
        small_sum[4],
        up_sum,
        small_sum[6:10].reshape(96),
        down_sum,
        small_sum[5],
        jnp.concatenate([gate_sum, rest_sum], axis=1),
        small_sum[10:16].reshape(144),
    )


def plain_shards(
    patches,
    lead_index,
    window_lengths,
    pad_mask,
    lead_table,
    attn_gain,
    attn_shift,
    qkv_weight,
    out_weight,
    out_bias,
    mlp_gain,
    mlp_shift,
    up_weight,
    up_bias,
    down_weight,
    down_bias,
    head_weight,
    head_bias,
    act_cotangent,
    head_cotangent,
):
    front = (
        lax.all_gather(lead_table, ("dp", "fsdp"), axis=1, tiled=True),
        lax.all_gather(attn_gain, ("dp", "fsdp"), axis=0, tiled=True),
        lax.all_gather(attn_shift, ("dp", "fsdp"), axis=0, tiled=True),
        lax.all_gather(qkv_weight, ("dp", "fsdp"), axis=0, tiled=True),
        lax.all_gather(out_weight, ("dp", "fsdp"), axis=0, tiled=True),
        lax.all_gather(out_bias, ("dp", "fsdp"), axis=0, tiled=True),
    )
    rear = (
        lax.all_gather(mlp_gain, ("dp", "fsdp"), axis=0, tiled=True),
        lax.all_gather(mlp_shift, ("dp", "fsdp"), axis=0, tiled=True),
        lax.all_gather(up_weight, ("dp", "fsdp"), axis=0, tiled=True),
        lax.all_gather(up_bias, ("dp", "fsdp"), axis=0, tiled=True),
        lax.all_gather(down_weight, ("dp", "fsdp"), axis=0, tiled=True),
        lax.all_gather(down_bias, ("dp", "fsdp"), axis=0, tiled=True),
        lax.all_gather(head_weight, ("dp", "fsdp"), axis=0, tiled=True),
        lax.all_gather(head_bias, ("dp", "fsdp"), axis=0, tiled=True),
    )
    table_full, gain_one, shift_one, qkv_full, out_full, out_bias_full = front
    (
        gain_two,
        shift_two,
        up_full,
        up_bias_full,
        down_full,
        down_bias_full,
        head_full,
        head_bias_full,
    ) = rear
    token_rows, width = patches.shape
    head_dim = width // HEADS
    block_rows = min(512, token_rows)
    block_count = token_rows // block_rows
    ends = jnp.cumsum(window_lengths[0])
    positions = jnp.arange(token_rows, dtype=jnp.int32)
    window = jnp.sum((positions[:, None] >= ends[None, :]).astype(jnp.int32), axis=1)
    lead_hot = (jnp.arange(LEADS, dtype=jnp.int32) == lead_index[0]).astype(jnp.float32)
    lead_row = jnp.sum(lead_hot[:, None] * table_full.astype(jnp.float32), axis=0)
    start_state = patches.astype(jnp.float32) + lead_row[None, :]
    normed_one, pull_one = jax.vjp(
        layer_norm, start_state, gain_one.astype(jnp.float32), shift_one.astype(jnp.float32)
    )
    attn_input = normed_one.astype(jnp.bfloat16)
    qkv_rows = jnp.dot(attn_input, qkv_full, preferred_element_type=jnp.float32).astype(
        jnp.bfloat16
    )
    queries = qkv_rows[:, :width].reshape(block_count, block_rows, HEADS, head_dim)
    keys = qkv_rows[:, width : 2 * width].reshape(token_rows, HEADS, head_dim)
    values = qkv_rows[:, 2 * width :].reshape(token_rows, HEADS, head_dim)
    query_windows = window.reshape(block_count, block_rows)
    block_starts = jnp.arange(block_count, dtype=jnp.int32) * block_rows

    def block_scores(query_block, window_block, block_start):
        scores = (
            jnp.einsum("qhd,khd->hqk", query_block, keys, preferred_element_type=jnp.float32)
            * score_scale
        )
        allowed = allowed_keys(window_block, window, pad_mask, block_start)
        return jnp.where(allowed[None], scores, -1e30)

    def forward_block(inputs):
        query_block, window_block, block_start = inputs
        masked = block_scores(query_block, window_block, block_start)
        largest = jnp.max(masked, axis=-1, keepdims=True)
        raised = jnp.exp(masked - largest)
        total = jnp.sum(raised, axis=-1, keepdims=True)
        probs = (raised / total).astype(jnp.bfloat16)
        mixed = jnp.einsum("hqk,khd->qhd", probs, values, preferred_element_type=jnp.float32)
        return (
            mixed.reshape(block_rows, width).astype(jnp.bfloat16),
            (largest + jnp.log(total))[:, :, 0],
        )

    mixed_blocks, log_totals = lax.map(forward_block, (queries, query_windows, block_starts))
    attended = mixed_blocks.reshape(token_rows, width)
    mid_state = (
        start_state
        + jnp.dot(attended, out_full, preferred_element_type=jnp.float32)
        + out_bias_full.astype(jnp.float32)
    )
    normed_two, pull_two = jax.vjp(
        layer_norm, mid_state, gain_two.astype(jnp.float32), shift_two.astype(jnp.float32)
    )
    mlp_input = normed_two.astype(jnp.bfloat16)
    pre_act = jnp.dot(mlp_input, up_full, preferred_element_type=jnp.float32) + up_bias_full.astype(
        jnp.float32
    )
    activated, pull_act = jax.vjp(gelu_exact, pre_act)
    act_rows = activated.astype(jnp.bfloat16)
    end_state = (
        mid_state
        + jnp.dot(act_rows, down_full, preferred_element_type=jnp.float32)
        + down_bias_full.astype(jnp.float32)
    )
    outputs = end_state.astype(jnp.bfloat16)
    logits = jnp.dot(
        outputs, head_full, preferred_element_type=jnp.float32
    ) + head_bias_full.astype(jnp.float32)
    head_out, pull_head = jax.vjp(partial(expert_softmax, experts=EXPERTS, pixels=PIX), logits)
    up_back, down_back, head_back = (
        lax.all_gather(up_weight, ("dp", "fsdp"), axis=0, tiled=True),
        lax.all_gather(down_weight, ("dp", "fsdp"), axis=0, tiled=True),
        lax.all_gather(head_weight, ("dp", "fsdp"), axis=0, tiled=True),
    )
    qkv_back, out_back = (
        lax.all_gather(qkv_weight, ("dp", "fsdp"), axis=0, tiled=True),
        lax.all_gather(out_weight, ("dp", "fsdp"), axis=0, tiled=True),
    )
    logit_grad = pull_head(head_cotangent.astype(jnp.float32))[0].astype(jnp.bfloat16)
    head_bias_term = jnp.sum(logit_grad.astype(jnp.float32), axis=0)
    head_term = jnp.einsum("td,tn->dn", outputs, logit_grad, preferred_element_type=jnp.float32)
    end_grad = act_cotangent.astype(jnp.float32) + jnp.einsum(
        "tn,dn->td", logit_grad, head_back, preferred_element_type=jnp.float32
    )
    branch_grad = end_grad.astype(jnp.bfloat16)
    down_bias_term = jnp.sum(branch_grad.astype(jnp.float32), axis=0)
    down_term = jnp.einsum("tf,td->fd", act_rows, branch_grad, preferred_element_type=jnp.float32)
    act_grad = jnp.einsum("td,fd->tf", branch_grad, down_back, preferred_element_type=jnp.float32)
    pre_grad = pull_act(act_grad)[0].astype(jnp.bfloat16)
    up_bias_term = jnp.sum(pre_grad.astype(jnp.float32), axis=0)
    up_term = jnp.einsum("td,tf->df", mlp_input, pre_grad, preferred_element_type=jnp.float32)
    normed_two_grad = jnp.einsum("tf,df->td", pre_grad, up_back, preferred_element_type=jnp.float32)
    state_grad_two, gain_two_term, shift_two_term = pull_two(normed_two_grad)
    (
        gain_part,
        shift_part,
        up_part,
        up_bias_part,
        down_part,
        down_bias_part,
        head_part,
        head_bias_part,
    ) = (
        lax.psum_scatter(
            gain_two_term.astype(jnp.bfloat16), "dp", scatter_dimension=0, tiled=True
        ).astype(jnp.float32),
        lax.psum_scatter(
            shift_two_term.astype(jnp.bfloat16), "dp", scatter_dimension=0, tiled=True
        ).astype(jnp.float32),
        lax.psum_scatter(
            up_term.astype(jnp.bfloat16), "dp", scatter_dimension=0, tiled=True
        ).astype(jnp.float32),
        lax.psum_scatter(
            up_bias_term.astype(jnp.bfloat16), "dp", scatter_dimension=0, tiled=True
        ).astype(jnp.float32),
        lax.psum_scatter(
            down_term.astype(jnp.bfloat16), "dp", scatter_dimension=0, tiled=True
        ).astype(jnp.float32),
        lax.psum_scatter(
            down_bias_term.astype(jnp.bfloat16), "dp", scatter_dimension=0, tiled=True
        ).astype(jnp.float32),
        lax.psum_scatter(
            head_term.astype(jnp.bfloat16), "dp", scatter_dimension=0, tiled=True
        ).astype(jnp.float32),
        lax.psum_scatter(
            head_bias_term.astype(jnp.bfloat16), "dp", scatter_dimension=0, tiled=True
        ).astype(jnp.float32),
    )
    rear_grads = (
        lax.psum_scatter(gain_part, "fsdp", scatter_dimension=0, tiled=True),
        lax.psum_scatter(shift_part, "fsdp", scatter_dimension=0, tiled=True),
        lax.psum_scatter(up_part, "fsdp", scatter_dimension=0, tiled=True),
        lax.psum_scatter(up_bias_part, "fsdp", scatter_dimension=0, tiled=True),
        lax.psum_scatter(down_part, "fsdp", scatter_dimension=0, tiled=True),
        lax.psum_scatter(down_bias_part, "fsdp", scatter_dimension=0, tiled=True),
        lax.psum_scatter(head_part, "fsdp", scatter_dimension=0, tiled=True),
        lax.psum_scatter(head_bias_part, "fsdp", scatter_dimension=0, tiled=True),
    )
    mid_grad = end_grad + state_grad_two
    out_grad = mid_grad.astype(jnp.bfloat16)
    out_bias_term = jnp.sum(out_grad.astype(jnp.float32), axis=0)
    out_term = jnp.einsum("td,te->de", attended, out_grad, preferred_element_type=jnp.float32)
    mixed_grad = jnp.einsum(
        "te,de->td", out_grad, out_back, preferred_element_type=jnp.float32
    ).astype(jnp.bfloat16)
    grad_blocks = mixed_grad.reshape(block_count, block_rows, HEADS, head_dim)

    def backward_block(carry, inputs):
        key_sum, value_sum = carry
        query_block, grad_block, window_block, total_block, block_start = inputs
        masked = block_scores(query_block, window_block, block_start)
        probs = jnp.exp(masked - total_block[:, :, None])
        prob_grad = jnp.einsum(
            "qhd,khd->hqk", grad_block, values, preferred_element_type=jnp.float32
        )
        inner = jnp.sum(probs * prob_grad, axis=-1, keepdims=True)
        score_grad = (probs * (prob_grad - inner)).astype(jnp.bfloat16)
        query_grad = (
            jnp.einsum("hqk,khd->qhd", score_grad, keys, preferred_element_type=jnp.float32)
            * score_scale
        )
        key_sum = (
            key_sum
            + jnp.einsum(
                "hqk,qhd->khd", score_grad, query_block, preferred_element_type=jnp.float32
            )
            * score_scale
        )
        value_sum = value_sum + jnp.einsum(
            "hqk,qhd->khd",
            probs.astype(jnp.bfloat16),
            grad_block,
            preferred_element_type=jnp.float32,
        )
        return ((key_sum, value_sum), query_grad.reshape(block_rows, width))

    zero_keys = jnp.zeros((token_rows, HEADS, head_dim), jnp.float32)
    (key_grad, value_grad), query_grads = lax.scan(
        backward_block,
        (zero_keys, zero_keys),
        (queries, grad_blocks, query_windows, log_totals, block_starts),
    )
    qkv_grad = jnp.concatenate(
        [
            query_grads.reshape(token_rows, width),
            key_grad.reshape(token_rows, width),
            value_grad.reshape(token_rows, width),
        ],
        axis=1,
    ).astype(jnp.bfloat16)
    qkv_term = jnp.einsum("td,te->de", attn_input, qkv_grad, preferred_element_type=jnp.float32)
    normed_one_grad = jnp.einsum(
        "te,de->td", qkv_grad, qkv_back, preferred_element_type=jnp.float32
    )
    state_grad_one, gain_one_term, shift_one_term = pull_one(normed_one_grad)
    patch_grad = mid_grad + state_grad_one
    lead_term = lead_hot[:, None] * jnp.sum(patch_grad, axis=0)[None, :]
    lead_part, gain_one_part, shift_one_part, qkv_part, out_part, out_bias_part = (
        lax.psum_scatter(
            lead_term.astype(jnp.bfloat16), "dp", scatter_dimension=1, tiled=True
        ).astype(jnp.float32),
        lax.psum_scatter(
            gain_one_term.astype(jnp.bfloat16), "dp", scatter_dimension=0, tiled=True
        ).astype(jnp.float32),
        lax.psum_scatter(
            shift_one_term.astype(jnp.bfloat16), "dp", scatter_dimension=0, tiled=True
        ).astype(jnp.float32),
        lax.psum_scatter(
            qkv_term.astype(jnp.bfloat16), "dp", scatter_dimension=0, tiled=True
        ).astype(jnp.float32),
        lax.psum_scatter(
            out_term.astype(jnp.bfloat16), "dp", scatter_dimension=0, tiled=True
        ).astype(jnp.float32),
        lax.psum_scatter(
            out_bias_term.astype(jnp.bfloat16), "dp", scatter_dimension=0, tiled=True
        ).astype(jnp.float32),
    )
    front_grads = (
        lax.psum_scatter(lead_part, "fsdp", scatter_dimension=1, tiled=True),
        lax.psum_scatter(gain_one_part, "fsdp", scatter_dimension=0, tiled=True),
        lax.psum_scatter(shift_one_part, "fsdp", scatter_dimension=0, tiled=True),
        lax.psum_scatter(qkv_part, "fsdp", scatter_dimension=0, tiled=True),
        lax.psum_scatter(out_part, "fsdp", scatter_dimension=0, tiled=True),
        lax.psum_scatter(out_bias_part, "fsdp", scatter_dimension=0, tiled=True),
    )
    return (
        outputs,
        head_out,
        patch_grad,
        front_grads[0],
        front_grads[1],
        front_grads[2],
        front_grads[3],
        front_grads[4],
        front_grads[5],
        rear_grads[0],
        rear_grads[1],
        rear_grads[2],
        rear_grads[3],
        rear_grads[4],
        rear_grads[5],
        rear_grads[6],
        rear_grads[7],
    )


def solution(mesh):
    in_specs = (
        P(("dp", "fsdp"), None),
        P(("dp", "fsdp")),
        P(("dp", "fsdp"), None),
        P(("dp", "fsdp")),
        P(None, ("dp", "fsdp")),
        P(("dp", "fsdp")),
        P(("dp", "fsdp")),
        P(("dp", "fsdp"), None),
        P(("dp", "fsdp"), None),
        P(("dp", "fsdp")),
        P(("dp", "fsdp")),
        P(("dp", "fsdp")),
        P(("dp", "fsdp"), None),
        P(("dp", "fsdp")),
        P(("dp", "fsdp"), None),
        P(("dp", "fsdp")),
        P(("dp", "fsdp"), None),
        P(("dp", "fsdp")),
        P(("dp", "fsdp"), None),
        P(("dp", "fsdp"), None),
    )
    out_specs = (
        P(("dp", "fsdp"), None),
        P(("dp", "fsdp"), None),
        P(("dp", "fsdp"), None),
        P(None, ("dp", "fsdp")),
        P(("dp", "fsdp")),
        P(("dp", "fsdp")),
        P(("dp", "fsdp"), None),
        P(("dp", "fsdp"), None),
        P(("dp", "fsdp")),
        P(("dp", "fsdp")),
        P(("dp", "fsdp")),
        P(("dp", "fsdp"), None),
        P(("dp", "fsdp")),
        P(("dp", "fsdp"), None),
        P(("dp", "fsdp")),
        P(("dp", "fsdp"), None),
        P(("dp", "fsdp")),
    )
    body = shards if dict(mesh.shape) == {"dp": 4, "fsdp": 8} else plain_shards
    return jax.shard_map(body, mesh=mesh, in_specs=in_specs, out_specs=out_specs, check_vma=False)
```

```python
import math
from functools import partial

import jax
import jax.numpy as jnp
from jax import lax
from jax.experimental import pallas as pl
from jax.experimental.pallas import tpu as pltpu
from jax.sharding import PartitionSpec as P

HEADS = 12
PIX = 64
EXPERTS = 3
LEADS = 16


norm_epsilon = 1e-05
score_scale = 0.125


def layer_norm(hidden, norm_gain, norm_shift):
    average = jnp.mean(hidden, axis=-1, keepdims=True)
    centered = hidden - average
    variance = jnp.mean(centered * centered, axis=-1, keepdims=True)
    return centered * lax.rsqrt(variance + norm_epsilon) * norm_gain + norm_shift


def gelu_exact(values):
    return 0.5 * values * (1.0 + lax.erf(values * 0.7071067811865476))


def expert_softmax(logits, experts, pixels):
    gate_part = logits[:, : experts * pixels].reshape(logits.shape[0], experts, pixels)
    largest = jnp.max(gate_part, axis=1, keepdims=True)
    raised = jnp.exp(gate_part - largest)
    shares = raised / jnp.sum(raised, axis=1, keepdims=True)
    return jnp.concatenate(
        [shares.reshape(logits.shape[0], experts * pixels), logits[:, experts * pixels :]], axis=1
    )


def allowed_keys(query_window, key_window, key_valid, query_start):
    query_place = query_start + jnp.arange(query_window.shape[0], dtype=jnp.int32)
    key_place = jnp.arange(key_window.shape[0], dtype=jnp.int32)
    same_window = query_window[:, None] == key_window[None, :]
    usable = (key_valid[None, :] > 0) | (query_place[:, None] == key_place[None, :])
    return same_window & usable


AXES = ("dp", "fsdp")
FAR_Z, NEAR_Z, FIRST, SECOND, SIBLING = (4, 4), (2, 2), (8, 16), (16, 8), (1, 1)
ORDERS = {
    "q": (FAR_Z, NEAR_Z, FIRST, SECOND),
    "u": (FAR_Z, FIRST, SECOND, NEAR_Z),
    "d": (FIRST, FAR_Z, NEAR_Z, SECOND),
    "h": (NEAR_Z, FAR_Z, FIRST, SECOND),
    "head": (FAR_Z, NEAR_Z, FIRST, SECOND),
    "down": (FAR_Z, NEAR_Z, FIRST, SECOND),
    "up": (FAR_Z, FIRST, SECOND, NEAR_Z),
    "front": (FAR_Z, FIRST, SECOND, NEAR_Z),
}
GATHER_SEQUENCE = (
    ("q", 0), ("d", 0), ("h", 0), ("u", 0), ("q", 1), ("d", 1), ("u", 1), ("q", 2), ("h", 1), ("u", 2),
    ("d", 2),
)
SCATTER_SEQUENCE = (
    "head", "down", "up", "front", "head", "down", "up", "front", "head", "down", "front", "up",
)
MOST_VMEM, SPARE_VMEM = 60 * 1024 * 1024, 8 * 1024 * 1024
WIDTH = 768
HIDDEN = 3072
HEAD = 4608
TOKENS = 512
GATE = 512
F32 = jnp.float32
BF16 = jnp.bfloat16
HBM = pl.BlockSpec(memory_space=pltpu.HBM)
SMEM = pl.BlockSpec(memory_space=pltpu.SMEM)
VMEM = pl.BlockSpec(memory_space=pltpu.VMEM)
QKV_PART, SMALL_PART = (0, 1152), (1152, 128)
UP_PART, OUT_PART, GATE_PART = (0, 1536), (1536, 384), (1920, 256)
DOWN_PART, HEAD_PART = (0, 384), (0, 2048)


def chip_masks(order, lane):
    masks = []
    for place in range(16):
        mask = 0
        for step in range(4):
            if place >> step & 1:
                mask ^= order[step][lane]
        masks.append(mask >> 1)
    return masks


def table_start(group, side):
    return 1 + 32 * list(ORDERS).index(group) + 16 * side


def exchange(array, masks):
    return lax.ppermute(array, AXES, [(d, d ^ masks[d & 1]) for d in range(32)])


def whereabouts():
    device = lax.axis_index("dp") * 8 + lax.axis_index("fsdp")
    core, chip = device % 2, device // 2
    tables = [chip_masks(order, 0) + chip_masks(order, 1) for order in ORDERS.values()]
    swapped = [chip_masks(order, 1) + chip_masks(order, 0) for order in ORDERS.values()]
    places = jnp.where(core == 0, jnp.array(tables, jnp.int32), jnp.array(swapped, jnp.int32))
    places = (places ^ chip).reshape(32 * len(ORDERS))
    return core, jnp.concatenate([core[None].astype(jnp.int32), places])


def after(value, *marks):
    return lax.optimization_barrier((value, marks))[0]


def in_core_order(core, mine, theirs, axis):
    return jnp.where(
        core == 0,
        jnp.concatenate([mine, theirs], axis=axis),
        jnp.concatenate([theirs, mine], axis=axis),
    )


def pack_kernel(core, qkv, out, up, down, head, table, *refs):
    vectors, (up_bias, head_bias), refs = refs[:6], refs[6:8], refs[8:]
    outs, (rows,) = refs[:8], refs[8:]
    rows[...] = jnp.zeros_like(rows)
    for index, vector in enumerate(vectors):
        rows[index : index + 1, :24] = vector[...].astype(F32)
    for index in range(4):
        rows[6 + index : 7 + index, :24] = up_bias[:, 24 * index : 24 * index + 24].astype(F32)
    for index in range(6):
        rows[10 + index : 11 + index, :24] = head_bias[:, 24 * index : 24 * index + 24].astype(F32)
    rows[16:32, :24] = table[...].astype(F32)
    small = rows[...].T[:24].astype(BF16)
    for side in range(2):
        q, u, d, h = outs[4 * side : 4 * side + 4]
        q[:, :1152] = qkv[:, lane_columns(core, side, 1152)]
        q[:, 1152:] = small
        u[:, :1536] = up[:, lane_columns(core, side, 1536)]
        u[:, 1536:1920] = out[:, lane_columns(core, side, 384)]
        u[:, 1920:] = head[:, lane_columns(core, side, 256)]
        d[...] = down[:, lane_columns(core, side, 384)]
        h[...] = head[:, lane_columns(core, side, 2048, GATE)]


def packed(core, weights, table, vectors):
    shapes = [(24, 1280), (24, 2176), (96, 384), (24, 2048)] * 2
    return call(
        pack_kernel,
        (core.reshape(1), *weights, table, *[vector[None] for vector in vectors]),
        [SMEM] + [VMEM] * 14,
        [(shape, BF16, False) for shape in shapes],
        [pltpu.VMEM((128, 128), F32)],
    )


def doubled(held, masks):
    return jnp.concatenate([held, exchange(held, masks)], axis=0)


def both_lanes(*arrays):
    return arrays + tuple(exchange(array, SIBLING) for array in arrays)


def total(parts):
    result = parts[0].astype(F32)
    for part in parts[1:]:
        result = result + part.astype(F32)
    return result


def folded(parts, got):
    parts = [*parts, got]
    half = got.shape[0] // 2
    return [part[:half] for part in parts], total([part[half:] for part in parts]).astype(BF16)


def finished(parts, got, core, widths):
    block = total([*parts, got])[0]
    rows = block.shape[0] // 2
    upper, lower = block[:rows], block[rows:]
    mine = jnp.where(core == 0, upper, lower)
    theirs = jnp.where(core == 0, lower, upper).astype(BF16)
    other = exchange(theirs, SIBLING).astype(F32)
    pieces, start = [], 0
    for width in widths:
        span = slice(start, start + width)
        pieces.append(in_core_order(core, mine[:, span], other[:, span], 1))
        start += width
    return pieces


def across(first, second):
    return lax.dot_general(first, second, (((1,), (1,)), ((), ())), preferred_element_type=F32)


def times(first, second):
    return jnp.dot(first, second, preferred_element_type=F32)


def lane_columns(where, side, stride, first=0, width=None):
    return pl.ds(pl.multiple_of(first + (where[0] ^ side) * stride, 128), width or stride)


def block_copies(where, group, sources, part, target, sems, side, first=0):
    start, width = part
    rows = sources[0].shape[1]
    half = len(sources) // 2
    count = 16 // half
    copies = []
    for place in range(16):
        row = pl.multiple_of(where[table_start(group, side) + place] * rows, rows)
        copies.append(
            pltpu.make_async_copy(
                sources[half * side + place // count].at[place % count, :, pl.ds(start, width)],
                target.at[pl.ds(row, rows), lane_columns(where, side, width, first)],
                sems.at[side, place],
            )
        )
    return copies


def start_all(copies):
    for copy in copies:
        copy.start()


def wait_all(copies):
    for copy in copies:
        copy.wait()


def mean_and_scale(hidden):
    average = jnp.mean(hidden, axis=1, keepdims=True)
    centered = hidden - average
    variance = jnp.mean(centered * centered, axis=1, keepdims=True)
    return centered, lax.rsqrt(variance + norm_epsilon)


def norm_backward(hidden, gain, upstream):
    centered, scale = mean_and_scale(hidden)
    normed = centered * scale
    gain_grad = jnp.sum(upstream * normed, axis=0, keepdims=True)
    shift_grad = jnp.sum(upstream, axis=0, keepdims=True)
    scaled = upstream * gain
    first = jnp.mean(scaled, axis=1, keepdims=True)
    second = jnp.mean(scaled * normed, axis=1, keepdims=True)
    return scale * (scaled - first - normed * second), gain_grad, shift_grad


def call(kernel, operands, in_specs, outs, scratch, spare=None):
    def size(item):
        return math.prod(item.shape) * jnp.dtype(item.dtype).itemsize

    held = [item for item, spec in zip(operands, in_specs) if spec is VMEM]
    held += [jax.ShapeDtypeStruct(shape, kind) for shape, kind, copied in outs if not copied]
    held += [item for item in scratch if getattr(item, "memory_space", None) == pltpu.VMEM]
    limit = MOST_VMEM if spare is None else sum(size(item) for item in held) + spare
    return pl.pallas_call(
        kernel,
        out_shape=[jax.ShapeDtypeStruct(shape, kind) for shape, kind, _ in outs],
        in_specs=in_specs,
        out_specs=[HBM if copied else VMEM for _, _, copied in outs],
        scratch_shapes=scratch,
        compiler_params=pltpu.CompilerParams(vmem_limit_bytes=limit),
        cost_estimate=pl.CostEstimate(flops=2 * 10**12, bytes_accessed=10**10, transcendentals=0),
    )(*operands)


def lane_scratch(rows, width):
    return [pltpu.VMEM((2, rows, width), BF16), pltpu.SemaphoreType.DMA((2, 16))]


def weight_scratch(rows, width):
    return [pltpu.VMEM((rows, width), BF16), pltpu.SemaphoreType.DMA((2, 16))]


def taken(refs, *counts):
    groups = []
    for count in counts:
        groups.append(refs[:count])
        refs = refs[count:]
    return *groups, refs


def front_kernel(where, lead, patches, *refs):
    sources, outs, scratch = taken(refs, 4, 3)
    turned_out, qkv_out, small = outs
    weight, sems, smalls, small_sems, state, rows, turned, qkv, io_sems = scratch
    loads = [block_copies(where, "q", sources, QKV_PART, weight, sems, side) for side in range(2)]
    small_loads = []
    for place in range(16):
        row = pl.multiple_of(where[table_start("q", 0) + place] * 48, 48)
        small_loads.append(
            pltpu.make_async_copy(
                sources[place // 8].at[place % 8, :, pl.ds(*SMALL_PART)],
                smalls.at[pl.ds(row, 48), :],
                small_sems.at[place],
            )
        )
    state_load = pltpu.make_async_copy(patches, state, io_sems.at[0])
    start_all(small_loads)
    state_load.start()
    start_all(loads[0])
    start_all(loads[1])
    wait_all(small_loads)
    columns = smalls[...].astype(F32).T
    places = lax.broadcasted_iota(jnp.int32, (LEADS, WIDTH), 0)
    lead_row = jnp.sum(
        jnp.where(places == lead[0], columns[16 : 16 + LEADS], 0.0), axis=0, keepdims=True
    )
    small[...] = columns[:32]
    small[16:17, :] = lead_row
    state_load.wait()
    centered, scale = mean_and_scale(state[...].astype(F32) + lead_row)
    rows[...] = (centered * scale * columns[0:1] + columns[1:2]).astype(BF16)
    turned[...] = rows[...].T
    stores = [pltpu.make_async_copy(turned, turned_out, io_sems.at[1])]
    stores[0].start()
    wait_all(loads[0] + loads[1])
    for part in range(3):
        span = slice(part * WIDTH, part * WIDTH + WIDTH)
        qkv[:, span] = times(rows[...], weight[:, span]).astype(BF16)
        stores.append(pltpu.make_async_copy(qkv.at[:, span], qkv_out.at[:, span], io_sems.at[2 + part]))
        stores[-1].start()
    wait_all(stores)


def front_forward(where, lead_index, patches, arrays):
    return call(
        front_kernel,
        (where, lead_index, patches, *arrays),
        [SMEM, SMEM, HBM] + [HBM] * 4,
        [
            ((WIDTH, TOKENS), BF16, True),
            ((TOKENS, 3 * WIDTH), BF16, True),
            ((32, WIDTH), F32, False),
        ],
        weight_scratch(WIDTH, 3 * WIDTH)
        + [pltpu.VMEM((WIDTH, 128), BF16), pltpu.SemaphoreType.DMA((16,))]
        + [
            pltpu.VMEM((TOKENS, WIDTH), BF16),
            pltpu.VMEM((TOKENS, WIDTH), BF16),
            pltpu.VMEM((WIDTH, TOKENS), BF16),
            pltpu.VMEM((TOKENS, 3 * WIDTH), BF16),
            pltpu.SemaphoreType.DMA((5,)),
        ],
    )


KEY_SPANS = ((0, 256), (0, 384), (128, 512), (256, 512))


def fill_bias(lengths, pad, bias):
    ends, end = [], 0
    for index in range(lengths.shape[1]):
        end = end + lengths[0, index]
        ends.append(end)

    def windows(places):
        return sum([(places >= end).astype(jnp.int32) for end in ends])

    for block, (low, high) in enumerate(KEY_SPANS):
        count = high - low
        queries = lax.broadcasted_iota(jnp.int32, (1, 128), 1) + 128 * block
        keys = lax.broadcasted_iota(jnp.int32, (count, 1), 0) + low
        same = windows(queries) == windows(keys)
        usable = (pad[low:high, :] > 0) | (queries == keys)
        bias[block, :count, :] = jnp.where(same & usable, 0.0, -1e30)


def two_heads(block):
    first = lax.broadcasted_iota(jnp.int32, block.shape, 1) < block.shape[1] // 2
    zero = jnp.zeros_like(block)
    return jnp.concatenate([jnp.where(first, block, zero), jnp.where(first, zero, block)], axis=0)


def head_rows_of(stacked):
    return jnp.concatenate([stacked[:64, :128], stacked[64:, 128:]], axis=0)


def probabilities(scores, allowed):
    masked = scores * score_scale + allowed
    raised = jnp.exp(masked - jnp.max(masked, axis=0, keepdims=True))
    return raised * (1.0 / jnp.sum(raised, axis=0, keepdims=True))


def attention_kernel(where, lengths, pad, qkv, attended_out, turned_out, bias, turned, rows, sems):
    fill_bias(lengths, pad, bias)

    def pair(index, carry):
        first = index * 128
        columns = pl.ds(pl.multiple_of(first, 128), 128)
        keys_at = pl.ds(pl.multiple_of(first + WIDTH, 128), 128)
        values = qkv[:, pl.ds(pl.multiple_of(first + 2 * WIDTH, 128), 128)].T
        for block, (low, high) in enumerate(KEY_SPANS):
            span = slice(128 * block, 128 * block + 128)
            scores = across(qkv[low:high, keys_at], two_heads(qkv[span, columns]))
            allowed = bias[block, : high - low, :]
            probs = [
                probabilities(scores[:, 128 * head : 128 * head + 128], allowed).astype(BF16)
                for head in range(2)
            ]
            mixed = times(values[:, low:high], jnp.concatenate(probs, axis=1))
            turned[columns, span] = head_rows_of(mixed).astype(BF16)
        return carry

    lax.fori_loop(0, WIDTH // 128, pair, 0)
    stores = [pltpu.make_async_copy(turned, turned_out, sems.at[0])]
    stores[0].start()
    rows[...] = turned[...].T
    stores.append(pltpu.make_async_copy(rows, attended_out, sems.at[1]))
    stores[1].start()
    wait_all(stores)


def attention_forward(where, lengths, pad, qkv):
    rows, columns = (TOKENS, WIDTH), (WIDTH, TOKENS)
    return call(
        attention_kernel,
        (where, lengths, pad, qkv),
        [SMEM, SMEM, VMEM, VMEM],
        [(rows, BF16, True), (columns, BF16, True)],
        [
            pltpu.VMEM((4, 384, 128), F32),
            pltpu.VMEM(columns, BF16),
            pltpu.VMEM(rows, BF16),
            pltpu.SemaphoreType.DMA((2,)),
        ],
    )


def gate_shares(logits, cotangent, shares, gate_grad):
    gate_grad[:, 256:] = cotangent[:, 256:GATE]
    first, rest = logits[:, :128], logits[:, 128:256]
    left = lax.broadcasted_iota(jnp.int32, first.shape, 1) < PIX
    third = jnp.where(left, rest, pltpu.roll(rest, PIX, 1))
    largest = jnp.maximum(jnp.maximum(first, pltpu.roll(first, PIX, 1)), third)
    raised, raised_third = jnp.exp(first - largest), jnp.exp(third - largest)
    scale = 1.0 / (raised + pltpu.roll(raised, PIX, 1) + raised_third)
    share, share_third = raised * scale, raised_third * scale
    shares[:, :128] = share
    shares[:, 128:256] = jnp.where(left, share_third, rest)
    pull, other = cotangent[:, :128].astype(F32), cotangent[:, 128:256].astype(F32)
    pull_third = jnp.where(left, other, pltpu.roll(other, PIX, 1))
    weighed = share * pull
    inner = weighed + pltpu.roll(weighed, PIX, 1) + share_third * pull_third
    gate_grad[:, :128] = (share * (pull - inner)).astype(BF16)
    gate_grad[:, 128:256] = jnp.where(left, share_third * (pull_third - inner), other).astype(BF16)


def send_lane(where, group, lane, out, sems, side):
    rows = out.shape[1]
    copies = []
    for place in range(16):
        row = pl.multiple_of(where[table_start(group, side) + place] * rows, rows)
        copies.append(
            pltpu.make_async_copy(lane.at[pl.ds(row, rows), :], out.at[place], sems.at[place])
        )
    start_all(copies)
    return copies


def middle_kernel(
    where, small, up_bias, head_bias, attended, patches, cotangent, act_cotangent, attended_turned,
    *refs,
):
    up_sources, down_sources, head_sources, outs, scratch = taken(refs, 4, 4, 4, 15)
    outputs, shares, gate_bias, down_bias, up_bias_sum, terms, mid_grad, out_grad, mixed, *grads = outs
    down_mine, down_theirs, up_mine, up_theirs, head_mine, head_theirs = grads
    out_weight, out_sems, up, up_sems, down, down_sems, scratch = *scratch[:6], scratch[6:]
    head, head_sems, gate_sems, rows, branch, mid, mlp_turned, scratch = *scratch[:7], scratch[7:]
    act, act_turned, slope, turned, pulls, act_pulls, gate_grad, scratch = *scratch[:7], scratch[7:]
    lane, lane_sems, down_lane, down_lane_sems, mixes, more_sems, io_sems = scratch

    def loads(group, sources, part, target, sems, first=0):
        copies = []
        for side in range(2):
            copies += block_copies(where, group, sources, part, target, sems, side, first)
        return copies

    state_loads = [
        pltpu.make_async_copy(attended, rows, io_sems.at[0]),
        pltpu.make_async_copy(patches, branch, io_sems.at[1]),
    ]
    out_loads = loads("u", up_sources, OUT_PART, out_weight, out_sems)
    up_loads = loads("u", up_sources, UP_PART, up, up_sems)
    down_loads = loads("d", down_sources, DOWN_PART, down, down_sems)
    gate_loads = loads("u", up_sources, GATE_PART, head, gate_sems)
    head_loads = loads("h", head_sources, HEAD_PART, head, head_sems, GATE)
    pull_load = pltpu.make_async_copy(cotangent, pulls, io_sems.at[2])
    act_load = pltpu.make_async_copy(act_cotangent, act_pulls, io_sems.at[3])
    mix_load = pltpu.make_async_copy(attended_turned, mixes, io_sems.at[4])
    start_all(state_loads + out_loads + up_loads + down_loads + gate_loads)
    pull_load.start()
    start_all(head_loads)
    act_load.start()
    mix_load.start()

    wait_all(state_loads + out_loads)
    mid[...] = (
        branch[...].astype(F32)
        + small[16:17, :]
        + times(rows[...], out_weight[...])
        + small[2:3, :]
    )
    centered, scale = mean_and_scale(mid[...])
    rows[...] = (centered * scale * small[3:4, :] + small[4:5, :]).astype(BF16)
    mlp_turned[...] = rows[...].T
    wait_all(up_loads)
    for tile in range(6):
        span = slice(tile * 512, tile * 512 + 512)
        values = times(rows[...], up[:, span]) + up_bias[:, span]
        share = 0.5 * (1.0 + lax.erf(values * 0.7071067811865476))
        density = jnp.exp(-0.5 * values * values) * 0.3989422804014327
        activated = (values * share).astype(BF16)
        act[:, span] = activated
        act_turned[span, :] = activated.T
        slope[:, span] = (share + values * density).astype(BF16)
    wait_all(down_loads)
    outputs[...] = (mid[...] + times(act[...], down[...]) + small[5:6, :]).astype(BF16)
    turned[...] = outputs[...].T
    wait_all(gate_loads)
    shares[...] = times(outputs[...], head[:, :GATE]) + head_bias[:, :GATE]
    pull_load.wait()
    gate_shares(shares, pulls, shares, gate_grad)
    gate_bias[...] = jnp.sum(gate_grad[...].astype(F32), axis=0, keepdims=True)
    pulls[:, :GATE] = gate_grad[...]

    def head_lane(side, target, sems, out):
        target[:, :256] = times(turned[...], pulls[:, lane_columns(where, side, 256)]).astype(BF16)
        for tile in range(4):
            span = lane_columns(where, side, 2048, GATE + tile * 512, 512)
            target[:, 256 + tile * 512 : 768 + tile * 512] = times(turned[...], pulls[:, span]).astype(
                BF16
            )
        return send_lane(where, "head", target, out, sems, side)

    def down_lane_of(side, out):
        columns = branch[:, lane_columns(where, side, 384)]
        for part in range(4):
            span = slice(part * WIDTH, part * WIDTH + WIDTH)
            down_lane[span, :] = times(act_turned[span, :], columns).astype(BF16)
        return send_lane(where, "down", down_lane, out, down_lane_sems, side)

    def up_lane(side, target, sems, out):
        for tile in range(3):
            span = lane_columns(where, side, 1536, tile * 512, 512)
            target[:, tile * 512 : tile * 512 + 512] = times(mlp_turned[...], slope[:, span]).astype(
                BF16
            )
        target[:, 1536:1920] = times(
            mixes[...], out_grad[:, lane_columns(where, side, 384)]
        ).astype(BF16)
        return send_lane(where, "up", target, out, sems, side)

    first_stores = head_lane(1, lane, lane_sems, head_theirs)
    act_load.wait()
    wait_all(head_loads)
    mid_grad[...] = act_pulls[...].astype(F32) + across(pulls[...], head[...])
    branch[...] = mid_grad[...].astype(BF16)
    down_bias[...] = jnp.sum(branch[...].astype(F32), axis=0, keepdims=True)
    stores = head_lane(0, head.at[:, :2304], more_sems.at[0], head_mine)
    down_stores = down_lane_of(1, down_theirs)
    for tile in range(6):
        span = slice(tile * 512, tile * 512 + 512)
        grad = across(branch[...], down[span, :])
        rounded = (slope[:, span].astype(F32) * grad).astype(BF16)
        slope[:, span] = rounded
        up_bias_sum[:, span] = jnp.sum(rounded.astype(F32), axis=0, keepdims=True)
    wait_all(down_stores)
    stores += down_lane_of(0, down_mine)
    grad = across(slope[...], up[...])
    pulled, gain_grad, shift_grad = norm_backward(mid[...], small[3:4, :], grad)
    pulled = pulled + mid_grad[...]
    rounded = pulled.astype(BF16)
    mid_grad[...] = pulled
    out_grad[...] = rounded
    terms[...] = jnp.zeros_like(terms)
    terms[0:1, :] = jnp.sum(rounded.astype(F32), axis=0, keepdims=True)
    terms[1:2, :] = gain_grad
    terms[2:3, :] = shift_grad
    mix_load.wait()
    stores += up_lane(1, head.at[:, 2304:4224], more_sems.at[1], up_theirs)
    wait_all(first_stores)
    stores += up_lane(0, lane.at[:, :1920], lane_sems, up_mine)
    mixed[...] = across(out_grad[...], out_weight[...]).astype(BF16)
    wait_all(stores)


def middle(
    where, small, up_bias, head_bias, attended, patches, cotangent, act_cotangent, attended_turned,
    up, down, head,
):
    rows, columns = (TOKENS, WIDTH), (WIDTH, TOKENS)
    wide, tall = (TOKENS, HIDDEN), (HIDDEN, TOKENS)
    return call(
        middle_kernel,
        (
            where, small, up_bias, head_bias, attended, patches, cotangent, act_cotangent,
            attended_turned, *up, *down, *head,
        ),
        [SMEM, VMEM, VMEM, VMEM] + [HBM] * 17,
        [
            (rows, BF16, False),
            ((TOKENS, GATE), F32, False),
            ((1, GATE), F32, False),
            ((1, WIDTH), F32, False),
            ((1, HIDDEN), F32, False),
            ((8, WIDTH), F32, False),
            (rows, F32, False),
            (rows, BF16, False),
            (rows, BF16, False),
            ((16, 192, 384), BF16, True),
            ((16, 192, 384), BF16, True),
            ((16, 48, 1920), BF16, True),
            ((16, 48, 1920), BF16, True),
            ((16, 48, 2304), BF16, True),
            ((16, 48, 2304), BF16, True),
        ],
        weight_scratch(WIDTH, WIDTH)
        + weight_scratch(WIDTH, HIDDEN)
        + weight_scratch(HIDDEN, WIDTH)
        + weight_scratch(WIDTH, HEAD)
        + [
            pltpu.SemaphoreType.DMA((2, 16)),
            pltpu.VMEM(rows, BF16),
            pltpu.VMEM(rows, BF16),
            pltpu.VMEM(rows, F32),
            pltpu.VMEM(columns, BF16),
            pltpu.VMEM(wide, BF16),
            pltpu.VMEM(tall, BF16),
            pltpu.VMEM(wide, BF16),
            pltpu.VMEM(columns, BF16),
            pltpu.VMEM((TOKENS, HEAD), BF16),
            pltpu.VMEM(rows, BF16),
            pltpu.VMEM((TOKENS, GATE), BF16),
            pltpu.VMEM((WIDTH, 2304), BF16),
            pltpu.SemaphoreType.DMA((16,)),
            pltpu.VMEM((HIDDEN, 384), BF16),
            pltpu.SemaphoreType.DMA((16,)),
            pltpu.VMEM(columns, BF16),
            pltpu.SemaphoreType.DMA((2, 16)),
            pltpu.SemaphoreType.DMA((5,)),
        ],
    )


def attend_back(count, qkv, mixed, bias, turned, key_sum, value_sum, qkv_grad):
    width = 128 * count

    def columns_at(first):
        return pl.ds(pl.multiple_of(first, 128), 128)

    def pair(index, carry):
        own = index * 128
        columns, keys_at = columns_at(own), columns_at(own + width)
        values_at = columns_at(own + 2 * width)
        keys_turned = qkv[:, keys_at].T
        key_sum[...] = jnp.zeros_like(key_sum)
        value_sum[...] = jnp.zeros_like(value_sum)
        for block, (low, high) in enumerate(KEY_SPANS):
            span = slice(128 * block, 128 * block + 128)
            queries, grads = two_heads(qkv[span, columns]), two_heads(mixed[span, columns])
            scores = across(qkv[low:high, keys_at], queries)
            prob_grads = across(qkv[low:high, values_at], grads)
            allowed = bias[block, : high - low, :]
            probs, score_grads = [], []
            for head in range(2):
                part = slice(128 * head, 128 * head + 128)
                prob = probabilities(scores[:, part], allowed)
                pulled = prob * prob_grads[:, part]
                inner = jnp.sum(pulled, axis=0, keepdims=True)
                probs.append(prob.astype(BF16))
                score_grads.append((pulled - prob * inner).astype(BF16))
            score_grad = jnp.concatenate(score_grads, axis=1)
            key_sum[low:high, :] += times(score_grad, queries)
            value_sum[low:high, :] += times(jnp.concatenate(probs, axis=1), grads)
            turned[:, span] = head_rows_of(times(keys_turned[:, low:high], score_grad)) * score_scale
        qkv_grad[:, columns] = turned[...].T.astype(BF16)
        qkv_grad[:, keys_at] = (key_sum[...] * score_scale).astype(BF16)
        qkv_grad[:, values_at] = value_sum[...].astype(BF16)
        return carry

    lax.fori_loop(0, count, pair, 0)


def attention_scratch(count):
    return [
        pltpu.VMEM((4, 384, 128), F32),
        pltpu.VMEM((TOKENS, 384 * count), BF16),
        pltpu.VMEM((TOKENS, 128 * count), BF16),
        pltpu.VMEM((128, TOKENS), F32),
        pltpu.VMEM((TOKENS, 128), F32),
        pltpu.VMEM((TOKENS, 128), F32),
        pltpu.SemaphoreType.DMA((4,)),
    ]


def attention_loads(start, count, qkv, mixed, own_qkv, own_mixed, sems):
    width = 128 * count
    copies = [
        pltpu.make_async_copy(
            mixed.at[:, pl.ds(128 * start, width)], own_mixed.at[:, pl.ds(0, width)], sems.at[3]
        )
    ]
    for part in range(3):
        copies.append(
            pltpu.make_async_copy(
                qkv.at[:, pl.ds(WIDTH * part + 128 * start, width)],
                own_qkv.at[:, pl.ds(width * part, width)],
                sems.at[part],
            )
        )
    return copies


def early_back_kernel(where, lengths, pad, head_bias, mixed, qkv, outputs, shares, *refs):
    sources, (qkv_grad, head_out), scratch = taken(refs, 4, 2)
    bias, own_qkv, own_mixed, turned, key_sum, value_sum, sems, scratch = *scratch[:7], scratch[7:]
    head, head_sems, rows, result, io_sems = scratch
    loads = attention_loads(0, 4, qkv, mixed, own_qkv, own_mixed, sems)
    head_loads = [
        block_copies(where, "h", sources, HEAD_PART, head, head_sems, side) for side in range(2)
    ]
    in_loads = [
        pltpu.make_async_copy(outputs, rows, io_sems.at[0]),
        pltpu.make_async_copy(shares, result.at[:, :GATE], io_sems.at[1]),
    ]
    start_all(loads + in_loads + head_loads[0] + head_loads[1])
    fill_bias(lengths, pad, bias)
    wait_all(loads)
    attend_back(4, own_qkv, own_mixed, bias, turned, key_sum, value_sum, qkv_grad)
    wait_all(in_loads + head_loads[0] + head_loads[1])
    stores = [pltpu.make_async_copy(result.at[:, :GATE], head_out.at[:, :GATE], io_sems.at[2])]
    stores[0].start()
    for tile in range(8):
        span = slice(GATE + tile * 512, GATE + tile * 512 + 512)
        result[:, span] = (
            times(rows[...], head[:, tile * 512 : tile * 512 + 512]) + head_bias[:, span]
        )
        stores.append(
            pltpu.make_async_copy(result.at[:, span], head_out.at[:, span], io_sems.at[3 + tile])
        )
        stores[-1].start()
    wait_all(stores)


def early_backward(where, lengths, pad, head_bias, mixed, qkv, outputs, shares, arrays):
    return call(
        early_back_kernel,
        (where, lengths, pad, head_bias, mixed, qkv, outputs, shares, *arrays),
        [SMEM, SMEM, VMEM, VMEM] + [HBM] * 8,
        [((TOKENS, 1536), BF16, False), ((TOKENS, HEAD), F32, True)],
        attention_scratch(4)
        + weight_scratch(WIDTH, HEAD - GATE)
        + [
            pltpu.VMEM((TOKENS, WIDTH), BF16),
            pltpu.VMEM((TOKENS, HEAD), F32),
            pltpu.SemaphoreType.DMA((11,)),
        ],
    )


def late_back_kernel(
    where, lead, lengths, pad, small, terms, down_row, up_rows, head_rows,
    mixed, qkv, first_grad, patches, mid_grad, input_turned, *refs
):
    sources, (patch_out, mine_out, theirs_out), scratch = taken(refs, 4, 3)
    bias, own_qkv, own_mixed, turned, key_sum, value_sum, sems, scratch = *scratch[:7], scratch[7:]
    weight, weight_sems, lane, lane_sems, pulls, late_pulls, scratch = *scratch[:6], scratch[6:]
    state, mids, inputs, patch_grad, small_grad, io_sems = scratch
    own_loads = attention_loads(4, 2, qkv, mixed, own_qkv, own_mixed, sems)
    loads = [
        block_copies(where, "q", sources, QKV_PART, weight, weight_sems, side) for side in range(2)
    ]
    pairs = [(patches, state), (mid_grad, mids), (input_turned, inputs)]
    for part in range(3):
        target = pulls.at[:, pl.ds(WIDTH * part, 512)]
        pairs.append((first_grad.at[:, pl.ds(512 * part, 512)], target))
    in_loads = [pltpu.make_async_copy(*pair, io_sems.at[at]) for at, pair in enumerate(pairs)]
    start_all(own_loads + in_loads + loads[0] + loads[1])
    fill_bias(lengths, pad, bias)
    wait_all(own_loads)
    attend_back(2, own_qkv, own_mixed, bias, turned, key_sum, value_sum, late_pulls)
    wait_all(loads[0] + loads[1] + in_loads)
    for part in range(3):
        pulls[:, WIDTH * part + 512 : WIDTH * part + 768] = late_pulls[
            :, 256 * part : 256 * part + 256
        ]
    grad = across(pulls[...], weight[...])
    pulled, gain_grad, shift_grad = norm_backward(
        state[...].astype(F32) + small[16:17, :], small[0:1, :], grad
    )
    pulled = pulled + mids[...]
    patch_grad[...] = pulled
    stores = [pltpu.make_async_copy(patch_grad, patch_out, io_sems.at[6])]
    stores[0].start()
    small_grad[0:1, :] = gain_grad
    small_grad[1:2, :] = shift_grad
    small_grad[2:5, :] = terms[0:3, :]
    small_grad[5:6, :] = down_row[...]
    small_grad[6:10, :] = up_rows[...]
    small_grad[10:16, :] = head_rows[...]
    places = lax.broadcasted_iota(jnp.int32, (LEADS, WIDTH), 0)
    lead_grad = jnp.sum(pulled, axis=0, keepdims=True)
    small_grad[16:32, :] = jnp.where(places == lead[0], lead_grad, 0.0)
    for side, out in ((1, theirs_out), (0, mine_out)):
        for tile in range(3):
            span = lane_columns(where, side, 1152, tile * 384, 384)
            lane[side, :, tile * 384 : tile * 384 + 384] = times(inputs[...], pulls[:, span]).astype(
                BF16
            )
        rows = small_grad[pl.ds(pl.multiple_of((where[0] ^ side) * 16, 16), 16), :]
        rows = jnp.concatenate([rows, jnp.zeros((112, WIDTH), F32)], axis=0)
        lane[side, :, 1152:] = rows.T.astype(BF16)
        stores += send_lane(where, "front", lane.at[side], out, lane_sems.at[side], side)
    wait_all(stores)


def late_backward(
    where, lead, lengths, pad, small, terms, down_row, up_rows, head_rows,
    mixed, qkv, first_grad, patches, mid_grad, input_turned, arrays,
):
    rows, columns = (TOKENS, WIDTH), (WIDTH, TOKENS)
    return call(
        late_back_kernel,
        (
            where, lead, lengths, pad, small, terms, down_row, up_rows, head_rows,
            mixed, qkv, first_grad, patches, mid_grad, input_turned, *arrays,
        ),
        [SMEM, SMEM, SMEM] + [VMEM] * 6 + [HBM] * 10,
        [(rows, F32, True), ((16, 48, 1280), BF16, True), ((16, 48, 1280), BF16, True)],
        attention_scratch(2)
        + weight_scratch(WIDTH, 3 * WIDTH)
        + lane_scratch(WIDTH, 1280)
        + [
            pltpu.VMEM((TOKENS, 3 * WIDTH), BF16),
            pltpu.VMEM((TOKENS, WIDTH), BF16),
            pltpu.VMEM(rows, BF16),
            pltpu.VMEM(rows, F32),
            pltpu.VMEM(columns, BF16),
            pltpu.VMEM(rows, F32),
            pltpu.VMEM((32, WIDTH), F32),
            pltpu.SemaphoreType.DMA((7,)),
        ],
    )


def rows_of(vector, count):
    return vector.reshape(32, count, 24).transpose(1, 0, 2).reshape(count, WIDTH)


def vector_of(rows):
    count = rows.shape[0]
    return rows.reshape(count, 32, 24).transpose(1, 0, 2).reshape(1, count * WIDTH)


def shards(
    patches,
    lead_index,
    window_lengths,
    pad_mask,
    lead_table,
    attn_gain,
    attn_shift,
    qkv_weight,
    out_weight,
    out_bias,
    mlp_gain,
    mlp_shift,
    up_weight,
    up_bias,
    down_weight,
    down_bias,
    head_weight,
    head_bias,
    act_cotangent,
    head_cotangent,
):
    core, where = whereabouts()
    weights = (qkv_weight, out_weight, up_weight, down_weight, head_weight)
    vectors = (
        attn_gain, attn_shift, out_bias, mlp_gain, mlp_shift, down_bias, up_bias, head_bias
    )
    parts = packed(core, weights, lead_table, vectors)
    pad = pad_mask[:, None]
    cotangent_sum = jnp.sum(head_cotangent[:, GATE:].astype(F32), axis=0, keepdims=True)

    orders = ORDERS
    parts = dict(zip("qudh", zip(parts[:4], parts[4:])))
    chunks = {
        name: in_core_order(core, mine, exchange(theirs, SIBLING), 0)[None]
        for name, (mine, theirs) in parts.items()
    }

    held, last = dict(chunks), ()
    for name, step in GATHER_SEQUENCE:
        held[name] = after(held[name], *last)
        last = (held[name],)
        held[name] = doubled(held[name], orders[name][step])
    q, u, d, h = [held[name] for name in ("q", "u", "d", "h")]
    q_rest = exchange(after(q, *last), orders["q"][3])
    u = after(u, q)
    u_rest = exchange(u, orders["u"][3])
    d_rest = exchange(d, orders["d"][3])
    h = doubled(after(h, u), orders["h"][2])
    first = both_lanes(q, q_rest)
    h_rest = exchange(h, orders["h"][3])
    input_turned, qkv, small_rows = front_forward(
        after(where, d, h, cotangent_sum), lead_index, patches, first
    )
    attended, attended_turned = attention_forward(where, window_lengths, pad, qkv)
    u_rest, d_rest, h_rest = lax.optimization_barrier((u_rest, d_rest, h_rest, attended))[:3]
    second, down, head = both_lanes(u, u_rest), both_lanes(d, d_rest), both_lanes(h, h_rest)
    up_bias_row, head_bias_row = vector_of(small_rows[6:10]), vector_of(small_rows[10:16])
    (
        outputs, gate_out, gate_bias_sum, down_bias_sum, up_bias_sum, terms, mid_grad, _, mixed_grad,
        mine_d, theirs_d, mine_u, theirs_u, mine_h, theirs_h,
    ) = middle(
        where, small_rows, up_bias_row, head_bias_row, attended, patches, head_cotangent,
        act_cotangent, attended_turned, second, down, head,
    )

    got_h, got_d, got_u = [exchange(theirs, SIBLING) for theirs in (theirs_h, theirs_d, theirs_u)]
    head_rows = rows_of(jnp.concatenate([gate_bias_sum, cotangent_sum], axis=1), 6)
    up_rows = rows_of(up_bias_sum, 4)
    first_grad, head_out = early_backward(
        where, window_lengths, pad, head_bias_row, mixed_grad, qkv, outputs, gate_out, head
    )
    groups = {
        "head": [[mine_h], after(got_h, first_grad), 4],
        "up": [[mine_u], after(got_u, first_grad), 4],
        "down": [[mine_d], after(got_d, first_grad), 4],
    }
    last = ()

    def add(name):
        nonlocal last
        keep, got, step = groups[name]
        keep, send = folded(keep, after(got, *last))
        last = (send,)
        groups[name] = [keep, exchange(send, orders[name][step - 1]), step - 1]

    def finish(name, widths):
        keep, got, _ = groups[name]
        return finished(keep, after(got, *last), core, widths)

    for name in ("head", "down", "up"):
        add(name)
    patch_grad, mine_f, theirs_f = late_backward(
        after(where, *last), lead_index, window_lengths, pad, small_rows, terms, down_bias_sum,
        up_rows, head_rows, mixed_grad, qkv, first_grad, patches, mid_grad, input_turned, first,
    )
    last = (patch_grad,)
    groups["front"] = [[mine_f], exchange(theirs_f, SIBLING), 4]
    for name in SCATTER_SEQUENCE:
        add(name)
    gate_sum, rest_sum = finish("head", (256, 2048))
    (down_sum,) = finish("down", (384,))
    add("front")
    up_sum, out_sum = finish("up", (1536, 384))
    qkv_sum, small_sum = finish("front", (1152, 128))
    small_sum = small_sum.T
    return (
        outputs,
        head_out,
        patch_grad,
        small_sum[128:144],
        small_sum[0],
        small_sum[1],
        qkv_sum,
        out_sum,
        small_sum[2],
        small_sum[3],
        small_sum[4],
        up_sum,
        small_sum[6:10].reshape(96),
        down_sum,
        small_sum[5],
        jnp.concatenate([gate_sum, rest_sum], axis=1),
        small_sum[10:16].reshape(144),
    )


def plain_shards(
    patches,
    lead_index,
    window_lengths,
    pad_mask,
    lead_table,
    attn_gain,
    attn_shift,
    qkv_weight,
    out_weight,
    out_bias,
    mlp_gain,
    mlp_shift,
    up_weight,
    up_bias,
    down_weight,
    down_bias,
    head_weight,
    head_bias,
    act_cotangent,
    head_cotangent,
):
    front = (
        lax.all_gather(lead_table, ("dp", "fsdp"), axis=1, tiled=True),
        lax.all_gather(attn_gain, ("dp", "fsdp"), axis=0, tiled=True),
        lax.all_gather(attn_shift, ("dp", "fsdp"), axis=0, tiled=True),
        lax.all_gather(qkv_weight, ("dp", "fsdp"), axis=0, tiled=True),
        lax.all_gather(out_weight, ("dp", "fsdp"), axis=0, tiled=True),
        lax.all_gather(out_bias, ("dp", "fsdp"), axis=0, tiled=True),
    )
    rear = (
        lax.all_gather(mlp_gain, ("dp", "fsdp"), axis=0, tiled=True),
        lax.all_gather(mlp_shift, ("dp", "fsdp"), axis=0, tiled=True),
        lax.all_gather(up_weight, ("dp", "fsdp"), axis=0, tiled=True),
        lax.all_gather(up_bias, ("dp", "fsdp"), axis=0, tiled=True),
        lax.all_gather(down_weight, ("dp", "fsdp"), axis=0, tiled=True),
        lax.all_gather(down_bias, ("dp", "fsdp"), axis=0, tiled=True),
        lax.all_gather(head_weight, ("dp", "fsdp"), axis=0, tiled=True),
        lax.all_gather(head_bias, ("dp", "fsdp"), axis=0, tiled=True),
    )
    table_full, gain_one, shift_one, qkv_full, out_full, out_bias_full = front
    (
        gain_two,
        shift_two,
        up_full,
        up_bias_full,
        down_full,
        down_bias_full,
        head_full,
        head_bias_full,
    ) = rear
    token_rows, width = patches.shape
    head_dim = width // HEADS
    block_rows = min(512, token_rows)
    block_count = token_rows // block_rows
    ends = jnp.cumsum(window_lengths[0])
    positions = jnp.arange(token_rows, dtype=jnp.int32)
    window = jnp.sum((positions[:, None] >= ends[None, :]).astype(jnp.int32), axis=1)
    lead_hot = (jnp.arange(LEADS, dtype=jnp.int32) == lead_index[0]).astype(jnp.float32)
    lead_row = jnp.sum(lead_hot[:, None] * table_full.astype(jnp.float32), axis=0)
    start_state = patches.astype(jnp.float32) + lead_row[None, :]
    normed_one, pull_one = jax.vjp(
        layer_norm, start_state, gain_one.astype(jnp.float32), shift_one.astype(jnp.float32)
    )
    attn_input = normed_one.astype(jnp.bfloat16)
    qkv_rows = jnp.dot(attn_input, qkv_full, preferred_element_type=jnp.float32).astype(
        jnp.bfloat16
    )
    queries = qkv_rows[:, :width].reshape(block_count, block_rows, HEADS, head_dim)
    keys = qkv_rows[:, width : 2 * width].reshape(token_rows, HEADS, head_dim)
    values = qkv_rows[:, 2 * width :].reshape(token_rows, HEADS, head_dim)
    query_windows = window.reshape(block_count, block_rows)
    block_starts = jnp.arange(block_count, dtype=jnp.int32) * block_rows

    def block_scores(query_block, window_block, block_start):
        scores = (
            jnp.einsum("qhd,khd->hqk", query_block, keys, preferred_element_type=jnp.float32)
            * score_scale
        )
        allowed = allowed_keys(window_block, window, pad_mask, block_start)
        return jnp.where(allowed[None], scores, -1e30)

    def forward_block(inputs):
        query_block, window_block, block_start = inputs
        masked = block_scores(query_block, window_block, block_start)
        largest = jnp.max(masked, axis=-1, keepdims=True)
        raised = jnp.exp(masked - largest)
        total = jnp.sum(raised, axis=-1, keepdims=True)
        probs = (raised / total).astype(jnp.bfloat16)
        mixed = jnp.einsum("hqk,khd->qhd", probs, values, preferred_element_type=jnp.float32)
        return (
            mixed.reshape(block_rows, width).astype(jnp.bfloat16),
            (largest + jnp.log(total))[:, :, 0],
        )

    mixed_blocks, log_totals = lax.map(forward_block, (queries, query_windows, block_starts))
    attended = mixed_blocks.reshape(token_rows, width)
    mid_state = (
        start_state
        + jnp.dot(attended, out_full, preferred_element_type=jnp.float32)
        + out_bias_full.astype(jnp.float32)
    )
    normed_two, pull_two = jax.vjp(
        layer_norm, mid_state, gain_two.astype(jnp.float32), shift_two.astype(jnp.float32)
    )
    mlp_input = normed_two.astype(jnp.bfloat16)
    pre_act = jnp.dot(mlp_input, up_full, preferred_element_type=jnp.float32) + up_bias_full.astype(
        jnp.float32
    )
    activated, pull_act = jax.vjp(gelu_exact, pre_act)
    act_rows = activated.astype(jnp.bfloat16)
    end_state = (
        mid_state
        + jnp.dot(act_rows, down_full, preferred_element_type=jnp.float32)
        + down_bias_full.astype(jnp.float32)
    )
    outputs = end_state.astype(jnp.bfloat16)
    logits = jnp.dot(
        outputs, head_full, preferred_element_type=jnp.float32
    ) + head_bias_full.astype(jnp.float32)
    head_out, pull_head = jax.vjp(partial(expert_softmax, experts=EXPERTS, pixels=PIX), logits)
    up_back, down_back, head_back = (
        lax.all_gather(up_weight, ("dp", "fsdp"), axis=0, tiled=True),
        lax.all_gather(down_weight, ("dp", "fsdp"), axis=0, tiled=True),
        lax.all_gather(head_weight, ("dp", "fsdp"), axis=0, tiled=True),
    )
    qkv_back, out_back = (
        lax.all_gather(qkv_weight, ("dp", "fsdp"), axis=0, tiled=True),
        lax.all_gather(out_weight, ("dp", "fsdp"), axis=0, tiled=True),
    )
    logit_grad = pull_head(head_cotangent.astype(jnp.float32))[0].astype(jnp.bfloat16)
    head_bias_term = jnp.sum(logit_grad.astype(jnp.float32), axis=0)
    head_term = jnp.einsum("td,tn->dn", outputs, logit_grad, preferred_element_type=jnp.float32)
    end_grad = act_cotangent.astype(jnp.float32) + jnp.einsum(
        "tn,dn->td", logit_grad, head_back, preferred_element_type=jnp.float32
    )
    branch_grad = end_grad.astype(jnp.bfloat16)
    down_bias_term = jnp.sum(branch_grad.astype(jnp.float32), axis=0)
    down_term = jnp.einsum("tf,td->fd", act_rows, branch_grad, preferred_element_type=jnp.float32)
    act_grad = jnp.einsum("td,fd->tf", branch_grad, down_back, preferred_element_type=jnp.float32)
    pre_grad = pull_act(act_grad)[0].astype(jnp.bfloat16)
    up_bias_term = jnp.sum(pre_grad.astype(jnp.float32), axis=0)
    up_term = jnp.einsum("td,tf->df", mlp_input, pre_grad, preferred_element_type=jnp.float32)
    normed_two_grad = jnp.einsum("tf,df->td", pre_grad, up_back, preferred_element_type=jnp.float32)
    state_grad_two, gain_two_term, shift_two_term = pull_two(normed_two_grad)
    (
        gain_part,
        shift_part,
        up_part,
        up_bias_part,
        down_part,
        down_bias_part,
        head_part,
        head_bias_part,
    ) = (
        lax.psum_scatter(
            gain_two_term.astype(jnp.bfloat16), "dp", scatter_dimension=0, tiled=True
        ).astype(jnp.float32),
        lax.psum_scatter(
            shift_two_term.astype(jnp.bfloat16), "dp", scatter_dimension=0, tiled=True
        ).astype(jnp.float32),
        lax.psum_scatter(
            up_term.astype(jnp.bfloat16), "dp", scatter_dimension=0, tiled=True
        ).astype(jnp.float32),
        lax.psum_scatter(
            up_bias_term.astype(jnp.bfloat16), "dp", scatter_dimension=0, tiled=True
        ).astype(jnp.float32),
        lax.psum_scatter(
            down_term.astype(jnp.bfloat16), "dp", scatter_dimension=0, tiled=True
        ).astype(jnp.float32),
        lax.psum_scatter(
            down_bias_term.astype(jnp.bfloat16), "dp", scatter_dimension=0, tiled=True
        ).astype(jnp.float32),
        lax.psum_scatter(
            head_term.astype(jnp.bfloat16), "dp", scatter_dimension=0, tiled=True
        ).astype(jnp.float32),
        lax.psum_scatter(
            head_bias_term.astype(jnp.bfloat16), "dp", scatter_dimension=0, tiled=True
        ).astype(jnp.float32),
    )
    rear_grads = (
        lax.psum_scatter(gain_part, "fsdp", scatter_dimension=0, tiled=True),
        lax.psum_scatter(shift_part, "fsdp", scatter_dimension=0, tiled=True),
        lax.psum_scatter(up_part, "fsdp", scatter_dimension=0, tiled=True),
        lax.psum_scatter(up_bias_part, "fsdp", scatter_dimension=0, tiled=True),
        lax.psum_scatter(down_part, "fsdp", scatter_dimension=0, tiled=True),
        lax.psum_scatter(down_bias_part, "fsdp", scatter_dimension=0, tiled=True),
        lax.psum_scatter(head_part, "fsdp", scatter_dimension=0, tiled=True),
        lax.psum_scatter(head_bias_part, "fsdp", scatter_dimension=0, tiled=True),
    )
    mid_grad = end_grad + state_grad_two
    out_grad = mid_grad.astype(jnp.bfloat16)
    out_bias_term = jnp.sum(out_grad.astype(jnp.float32), axis=0)
    out_term = jnp.einsum("td,te->de", attended, out_grad, preferred_element_type=jnp.float32)
    mixed_grad = jnp.einsum(
        "te,de->td", out_grad, out_back, preferred_element_type=jnp.float32
    ).astype(jnp.bfloat16)
    grad_blocks = mixed_grad.reshape(block_count, block_rows, HEADS, head_dim)

    def backward_block(carry, inputs):
        key_sum, value_sum = carry
        query_block, grad_block, window_block, total_block, block_start = inputs
        masked = block_scores(query_block, window_block, block_start)
        probs = jnp.exp(masked - total_block[:, :, None])
        prob_grad = jnp.einsum(
            "qhd,khd->hqk", grad_block, values, preferred_element_type=jnp.float32
        )
        inner = jnp.sum(probs * prob_grad, axis=-1, keepdims=True)
        score_grad = (probs * (prob_grad - inner)).astype(jnp.bfloat16)
        query_grad = (
            jnp.einsum("hqk,khd->qhd", score_grad, keys, preferred_element_type=jnp.float32)
            * score_scale
        )
        key_sum = (
            key_sum
            + jnp.einsum(
                "hqk,qhd->khd", score_grad, query_block, preferred_element_type=jnp.float32
            )
            * score_scale
        )
        value_sum = value_sum + jnp.einsum(
            "hqk,qhd->khd",
            probs.astype(jnp.bfloat16),
            grad_block,
            preferred_element_type=jnp.float32,
        )
        return ((key_sum, value_sum), query_grad.reshape(block_rows, width))

    zero_keys = jnp.zeros((token_rows, HEADS, head_dim), jnp.float32)
    (key_grad, value_grad), query_grads = lax.scan(
        backward_block,
        (zero_keys, zero_keys),
        (queries, grad_blocks, query_windows, log_totals, block_starts),
    )
    qkv_grad = jnp.concatenate(
        [
            query_grads.reshape(token_rows, width),
            key_grad.reshape(token_rows, width),
            value_grad.reshape(token_rows, width),
        ],
        axis=1,
    ).astype(jnp.bfloat16)
    qkv_term = jnp.einsum("td,te->de", attn_input, qkv_grad, preferred_element_type=jnp.float32)
    normed_one_grad = jnp.einsum(
        "te,de->td", qkv_grad, qkv_back, preferred_element_type=jnp.float32
    )
    state_grad_one, gain_one_term, shift_one_term = pull_one(normed_one_grad)
    patch_grad = mid_grad + state_grad_one
    lead_term = lead_hot[:, None] * jnp.sum(patch_grad, axis=0)[None, :]
    lead_part, gain_one_part, shift_one_part, qkv_part, out_part, out_bias_part = (
        lax.psum_scatter(
            lead_term.astype(jnp.bfloat16), "dp", scatter_dimension=1, tiled=True
        ).astype(jnp.float32),
        lax.psum_scatter(
            gain_one_term.astype(jnp.bfloat16), "dp", scatter_dimension=0, tiled=True
        ).astype(jnp.float32),
        lax.psum_scatter(
            shift_one_term.astype(jnp.bfloat16), "dp", scatter_dimension=0, tiled=True
        ).astype(jnp.float32),
        lax.psum_scatter(
            qkv_term.astype(jnp.bfloat16), "dp", scatter_dimension=0, tiled=True
        ).astype(jnp.float32),
        lax.psum_scatter(
            out_term.astype(jnp.bfloat16), "dp", scatter_dimension=0, tiled=True
        ).astype(jnp.float32),
        lax.psum_scatter(
            out_bias_term.astype(jnp.bfloat16), "dp", scatter_dimension=0, tiled=True
        ).astype(jnp.float32),
    )
    front_grads = (
        lax.psum_scatter(lead_part, "fsdp", scatter_dimension=1, tiled=True),
        lax.psum_scatter(gain_one_part, "fsdp", scatter_dimension=0, tiled=True),
        lax.psum_scatter(shift_one_part, "fsdp", scatter_dimension=0, tiled=True),
        lax.psum_scatter(qkv_part, "fsdp", scatter_dimension=0, tiled=True),
        lax.psum_scatter(out_part, "fsdp", scatter_dimension=0, tiled=True),
        lax.psum_scatter(out_bias_part, "fsdp", scatter_dimension=0, tiled=True),
    )
    return (
        outputs,
        head_out,
        patch_grad,
        front_grads[0],
        front_grads[1],
        front_grads[2],
        front_grads[3],
        front_grads[4],
        front_grads[5],
        rear_grads[0],
        rear_grads[1],
        rear_grads[2],
        rear_grads[3],
        rear_grads[4],
        rear_grads[5],
        rear_grads[6],
        rear_grads[7],
    )


def solution(mesh):
    in_specs = (
        P(("dp", "fsdp"), None),
        P(("dp", "fsdp")),
        P(("dp", "fsdp"), None),
        P(("dp", "fsdp")),
        P(None, ("dp", "fsdp")),
        P(("dp", "fsdp")),
        P(("dp", "fsdp")),
        P(("dp", "fsdp"), None),
        P(("dp", "fsdp"), None),
        P(("dp", "fsdp")),
        P(("dp", "fsdp")),
        P(("dp", "fsdp")),
        P(("dp", "fsdp"), None),
        P(("dp", "fsdp")),
        P(("dp", "fsdp"), None),
        P(("dp", "fsdp")),
        P(("dp", "fsdp"), None),
        P(("dp", "fsdp")),
        P(("dp", "fsdp"), None),
        P(("dp", "fsdp"), None),
    )
    out_specs = (
        P(("dp", "fsdp"), None),
        P(("dp", "fsdp"), None),
        P(("dp", "fsdp"), None),
        P(None, ("dp", "fsdp")),
        P(("dp", "fsdp")),
        P(("dp", "fsdp")),
        P(("dp", "fsdp"), None),
        P(("dp", "fsdp"), None),
        P(("dp", "fsdp")),
        P(("dp", "fsdp")),
        P(("dp", "fsdp")),
        P(("dp", "fsdp"), None),
        P(("dp", "fsdp")),
        P(("dp", "fsdp"), None),
        P(("dp", "fsdp")),
        P(("dp", "fsdp"), None),
        P(("dp", "fsdp")),
    )
    body = shards if dict(mesh.shape) == {"dp": 4, "fsdp": 8} else plain_shards
    return jax.shard_map(body, mesh=mesh, in_specs=in_specs, out_specs=out_specs, check_vma=False)
```

```python
import math
from functools import partial

import jax
import jax.numpy as jnp
from jax import lax
from jax.experimental import pallas as pl
from jax.experimental.pallas import tpu as pltpu
from jax.sharding import PartitionSpec as P

HEADS = 12
PIX = 64
EXPERTS = 3
LEADS = 16


norm_epsilon = 1e-05
score_scale = 0.125


def layer_norm(hidden, norm_gain, norm_shift):
    average = jnp.mean(hidden, axis=-1, keepdims=True)
    centered = hidden - average
    variance = jnp.mean(centered * centered, axis=-1, keepdims=True)
    return centered * lax.rsqrt(variance + norm_epsilon) * norm_gain + norm_shift


def gelu_exact(values):
    return 0.5 * values * (1.0 + lax.erf(values * 0.7071067811865476))


def expert_softmax(logits, experts, pixels):
    gate_part = logits[:, : experts * pixels].reshape(logits.shape[0], experts, pixels)
    largest = jnp.max(gate_part, axis=1, keepdims=True)
    raised = jnp.exp(gate_part - largest)
    shares = raised / jnp.sum(raised, axis=1, keepdims=True)
    return jnp.concatenate(
        [shares.reshape(logits.shape[0], experts * pixels), logits[:, experts * pixels :]], axis=1
    )


def allowed_keys(query_window, key_window, key_valid, query_start):
    query_place = query_start + jnp.arange(query_window.shape[0], dtype=jnp.int32)
    key_place = jnp.arange(key_window.shape[0], dtype=jnp.int32)
    same_window = query_window[:, None] == key_window[None, :]
    usable = (key_valid[None, :] > 0) | (query_place[:, None] == key_place[None, :])
    return same_window & usable


AXES = ("dp", "fsdp")
FAR_Z, NEAR_Z, FIRST, SECOND, SIBLING = (4, 4), (2, 2), (8, 16), (16, 8), (1, 1)
ORDERS = {
    "q": (FAR_Z, NEAR_Z, FIRST, SECOND),
    "u": (FAR_Z, FIRST, SECOND, NEAR_Z),
    "d": (FIRST, FAR_Z, NEAR_Z, SECOND),
    "h": (NEAR_Z, FAR_Z, FIRST, SECOND),
    "head": (FAR_Z, NEAR_Z, FIRST, SECOND),
    "down": (FAR_Z, NEAR_Z, FIRST, SECOND),
    "up": (FAR_Z, FIRST, SECOND, NEAR_Z),
    "front": (FAR_Z, NEAR_Z, FIRST, SECOND),
    "mix": (FAR_Z, NEAR_Z, FIRST, SECOND),
}
GATHER_SEQUENCE = (
    ("q", 0), ("d", 0), ("h", 0), ("u", 0), ("q", 1), ("d", 1), ("u", 1), ("q", 2), ("h", 1), ("u", 2),
    ("d", 2),
)
MOST_VMEM, SPARE_VMEM = 60 * 1024 * 1024, 8 * 1024 * 1024
WIDTH = 768
HIDDEN = 3072
HEAD = 4608
TOKENS = 512
GATE = 512
F32 = jnp.float32
BF16 = jnp.bfloat16
HBM = pl.BlockSpec(memory_space=pltpu.HBM)
SMEM = pl.BlockSpec(memory_space=pltpu.SMEM)
VMEM = pl.BlockSpec(memory_space=pltpu.VMEM)
QKV_PART, SMALL_PART = (0, 1152), (1152, 128)
UP_PART, OUT_PART, GATE_PART = (0, 1536), (1536, 384), (1920, 256)
DOWN_PART, HEAD_PART = (0, 384), (0, 2048)


def chip_masks(order, lane):
    masks = []
    for place in range(16):
        mask = 0
        for step in range(4):
            if place >> step & 1:
                mask ^= order[step][lane]
        masks.append(mask >> 1)
    return masks


def table_start(group, side):
    return 1 + 32 * list(ORDERS).index(group) + 16 * side


def exchange(array, masks):
    return lax.ppermute(array, AXES, [(d, d ^ masks[d & 1]) for d in range(32)])


def whereabouts():
    device = lax.axis_index("dp") * 8 + lax.axis_index("fsdp")
    core, chip = device % 2, device // 2
    tables = [chip_masks(order, 0) + chip_masks(order, 1) for order in ORDERS.values()]
    swapped = [chip_masks(order, 1) + chip_masks(order, 0) for order in ORDERS.values()]
    places = jnp.where(core == 0, jnp.array(tables, jnp.int32), jnp.array(swapped, jnp.int32))
    places = (places ^ chip).reshape(32 * len(ORDERS))
    return core, jnp.concatenate([core[None].astype(jnp.int32), places])


def after(value, *marks):
    return lax.optimization_barrier((value, marks))[0]


def in_core_order(core, mine, theirs, axis):
    return jnp.where(
        core == 0,
        jnp.concatenate([mine, theirs], axis=axis),
        jnp.concatenate([theirs, mine], axis=axis),
    )


def pack_kernel(core, qkv, out, up, down, head, table, *refs):
    vectors, (up_bias, head_bias), refs = refs[:6], refs[6:8], refs[8:]
    outs, (rows,) = refs[:8], refs[8:]
    rows[...] = jnp.zeros_like(rows)
    for index, vector in enumerate(vectors):
        rows[index : index + 1, :24] = vector[...].astype(F32)
    for index in range(4):
        rows[6 + index : 7 + index, :24] = up_bias[:, 24 * index : 24 * index + 24].astype(F32)
    for index in range(6):
        rows[10 + index : 11 + index, :24] = head_bias[:, 24 * index : 24 * index + 24].astype(F32)
    rows[16:32, :24] = table[...].astype(F32)
    small = rows[...].T[:24].astype(BF16)
    for side in range(2):
        q, u, d, h = outs[4 * side : 4 * side + 4]
        q[:, :1152] = qkv[:, lane_columns(core, side, 1152)]
        q[:, 1152:] = small
        u[:, :1536] = up[:, lane_columns(core, side, 1536)]
        u[:, 1536:1920] = out[:, lane_columns(core, side, 384)]
        u[:, 1920:] = head[:, lane_columns(core, side, 256)]
        d[...] = down[:, lane_columns(core, side, 384)]
        h[...] = head[:, lane_columns(core, side, 2048, GATE)]


def packed(core, weights, table, vectors):
    shapes = [(24, 1280), (24, 2176), (96, 384), (24, 2048)] * 2
    return call(
        pack_kernel,
        (core.reshape(1), *weights, table, *[vector[None] for vector in vectors]),
        [SMEM] + [VMEM] * 14,
        [(shape, BF16, False) for shape in shapes],
        [pltpu.VMEM((128, 128), F32)],
    )


def doubled(held, masks):
    return jnp.concatenate([held, exchange(held, masks)], axis=0)


def both_lanes(*arrays):
    return arrays + tuple(exchange(array, SIBLING) for array in arrays)


def total(parts):
    result = parts[0].astype(F32)
    for part in parts[1:]:
        result = result + part.astype(F32)
    return result


def folded(parts, got):
    parts = [*parts, got]
    half = got.shape[0] // 2
    return [part[:half] for part in parts], total([part[half:] for part in parts]).astype(BF16)


def finished(parts, got, core, widths):
    block = total([*parts, got])[0]
    rows = block.shape[0] // 2
    upper, lower = block[:rows], block[rows:]
    mine = jnp.where(core == 0, upper, lower)
    theirs = jnp.where(core == 0, lower, upper).astype(BF16)
    other = exchange(theirs, SIBLING).astype(F32)
    pieces, start = [], 0
    for width in widths:
        span = slice(start, start + width)
        pieces.append(in_core_order(core, mine[:, span], other[:, span], 1))
        start += width
    return pieces


def across(first, second):
    return lax.dot_general(first, second, (((1,), (1,)), ((), ())), preferred_element_type=F32)


def times(first, second):
    return jnp.dot(first, second, preferred_element_type=F32)


def lane_columns(where, side, stride, first=0, width=None):
    return pl.ds(pl.multiple_of(first + (where[0] ^ side) * stride, 128), width or stride)


def block_copies(where, group, sources, part, target, sems, side, first=0):
    start, width = part
    rows = sources[0].shape[1]
    half = len(sources) // 2
    count = 16 // half
    copies = []
    for place in range(16):
        row = pl.multiple_of(where[table_start(group, side) + place] * rows, rows)
        copies.append(
            pltpu.make_async_copy(
                sources[half * side + place // count].at[place % count, :, pl.ds(start, width)],
                target.at[pl.ds(row, rows), lane_columns(where, side, width, first)],
                sems.at[side, place],
            )
        )
    return copies


def start_all(copies):
    for copy in copies:
        copy.start()


def wait_all(copies):
    for copy in copies:
        copy.wait()


def mean_and_scale(hidden):
    average = jnp.mean(hidden, axis=1, keepdims=True)
    centered = hidden - average
    variance = jnp.mean(centered * centered, axis=1, keepdims=True)
    return centered, lax.rsqrt(variance + norm_epsilon)


def norm_backward(hidden, gain, upstream):
    centered, scale = mean_and_scale(hidden)
    normed = centered * scale
    gain_grad = jnp.sum(upstream * normed, axis=0, keepdims=True)
    shift_grad = jnp.sum(upstream, axis=0, keepdims=True)
    scaled = upstream * gain
    first = jnp.mean(scaled, axis=1, keepdims=True)
    second = jnp.mean(scaled * normed, axis=1, keepdims=True)
    return scale * (scaled - first - normed * second), gain_grad, shift_grad


def call(kernel, operands, in_specs, outs, scratch, spare=None):
    def size(item):
        return math.prod(item.shape) * jnp.dtype(item.dtype).itemsize

    held = [item for item, spec in zip(operands, in_specs) if spec is VMEM]
    held += [jax.ShapeDtypeStruct(shape, kind) for shape, kind, copied in outs if not copied]
    held += [item for item in scratch if getattr(item, "memory_space", None) == pltpu.VMEM]
    limit = MOST_VMEM if spare is None else sum(size(item) for item in held) + spare
    return pl.pallas_call(
        kernel,
        out_shape=[jax.ShapeDtypeStruct(shape, kind) for shape, kind, _ in outs],
        in_specs=in_specs,
        out_specs=[HBM if copied else VMEM for _, _, copied in outs],
        scratch_shapes=scratch,
        compiler_params=pltpu.CompilerParams(vmem_limit_bytes=limit),
        cost_estimate=pl.CostEstimate(flops=2 * 10**12, bytes_accessed=10**10, transcendentals=0),
    )(*operands)


def lane_scratch(rows, width):
    return [pltpu.VMEM((2, rows, width), BF16), pltpu.SemaphoreType.DMA((2, 16))]


def weight_scratch(rows, width):
    return [pltpu.VMEM((rows, width), BF16), pltpu.SemaphoreType.DMA((2, 16))]


def taken(refs, *counts):
    groups = []
    for count in counts:
        groups.append(refs[:count])
        refs = refs[count:]
    return *groups, refs


def front_kernel(where, lead, patches, *refs):
    sources, outs, scratch = taken(refs, 4, 3)
    turned_out, qkv_out, small = outs
    weight, sems, smalls, small_sems, state, rows, turned, qkv, io_sems = scratch
    loads = [block_copies(where, "q", sources, QKV_PART, weight, sems, side) for side in range(2)]
    small_loads = []
    for place in range(16):
        row = pl.multiple_of(where[table_start("q", 0) + place] * 48, 48)
        small_loads.append(
            pltpu.make_async_copy(
                sources[place // 8].at[place % 8, :, pl.ds(*SMALL_PART)],
                smalls.at[pl.ds(row, 48), :],
                small_sems.at[place],
            )
        )
    state_load = pltpu.make_async_copy(patches, state, io_sems.at[0])
    start_all(small_loads)
    state_load.start()
    start_all(loads[0])
    start_all(loads[1])
    wait_all(small_loads)
    columns = smalls[...].astype(F32).T
    places = lax.broadcasted_iota(jnp.int32, (LEADS, WIDTH), 0)
    lead_row = jnp.sum(
        jnp.where(places == lead[0], columns[16 : 16 + LEADS], 0.0), axis=0, keepdims=True
    )
    small[...] = columns[:32]
    small[16:17, :] = lead_row
    state_load.wait()
    centered, scale = mean_and_scale(state[...].astype(F32) + lead_row)
    rows[...] = (centered * scale * columns[0:1] + columns[1:2]).astype(BF16)
    turned[...] = rows[...].T
    stores = [pltpu.make_async_copy(turned, turned_out, io_sems.at[1])]
    stores[0].start()
    wait_all(loads[0] + loads[1])
    for part in range(3):
        span = slice(part * WIDTH, part * WIDTH + WIDTH)
        qkv[:, span] = times(rows[...], weight[:, span]).astype(BF16)
        stores.append(pltpu.make_async_copy(qkv.at[:, span], qkv_out.at[:, span], io_sems.at[2 + part]))
        stores[-1].start()
    wait_all(stores)


def front_forward(where, lead_index, patches, arrays):
    return call(
        front_kernel,
        (where, lead_index, patches, *arrays),
        [SMEM, SMEM, HBM] + [HBM] * 4,
        [
            ((WIDTH, TOKENS), BF16, True),
            ((TOKENS, 3 * WIDTH), BF16, True),
            ((32, WIDTH), F32, False),
        ],
        weight_scratch(WIDTH, 3 * WIDTH)
        + [pltpu.VMEM((WIDTH, 128), BF16), pltpu.SemaphoreType.DMA((16,))]
        + [
            pltpu.VMEM((TOKENS, WIDTH), BF16),
            pltpu.VMEM((TOKENS, WIDTH), BF16),
            pltpu.VMEM((WIDTH, TOKENS), BF16),
            pltpu.VMEM((TOKENS, 3 * WIDTH), BF16),
            pltpu.SemaphoreType.DMA((5,)),
        ],
    )


KEY_SPANS = ((0, 256), (0, 384), (128, 512), (256, 512))


def fill_bias(lengths, pad, bias):
    ends, end = [], 0
    for index in range(lengths.shape[1]):
        end = end + lengths[0, index]
        ends.append(end)

    def windows(places):
        return sum([(places >= end).astype(jnp.int32) for end in ends])

    for block, (low, high) in enumerate(KEY_SPANS):
        count = high - low
        queries = lax.broadcasted_iota(jnp.int32, (1, 128), 1) + 128 * block
        keys = lax.broadcasted_iota(jnp.int32, (count, 1), 0) + low
        same = windows(queries) == windows(keys)
        usable = (pad[low:high, :] > 0) | (queries == keys)
        bias[block, :count, :] = jnp.where(same & usable, 0.0, -1e30)


def two_heads(block):
    first = lax.broadcasted_iota(jnp.int32, block.shape, 1) < block.shape[1] // 2
    zero = jnp.zeros_like(block)
    return jnp.concatenate([jnp.where(first, block, zero), jnp.where(first, zero, block)], axis=0)


def head_rows_of(stacked):
    return jnp.concatenate([stacked[:64, :128], stacked[64:, 128:]], axis=0)


def probabilities(scores, allowed):
    masked = scores * score_scale + allowed
    raised = jnp.exp(masked - jnp.max(masked, axis=0, keepdims=True))
    return raised * (1.0 / jnp.sum(raised, axis=0, keepdims=True))


def attention_kernel(where, lengths, pad, qkv, attended_out, turned_out, bias, turned, rows, sems):
    fill_bias(lengths, pad, bias)

    def pair(index, carry):
        first = index * 128
        columns = pl.ds(pl.multiple_of(first, 128), 128)
        keys_at = pl.ds(pl.multiple_of(first + WIDTH, 128), 128)
        values = qkv[:, pl.ds(pl.multiple_of(first + 2 * WIDTH, 128), 128)].T
        for block, (low, high) in enumerate(KEY_SPANS):
            span = slice(128 * block, 128 * block + 128)
            scores = across(qkv[low:high, keys_at], two_heads(qkv[span, columns]))
            allowed = bias[block, : high - low, :]
            probs = [
                probabilities(scores[:, 128 * head : 128 * head + 128], allowed).astype(BF16)
                for head in range(2)
            ]
            mixed = times(values[:, low:high], jnp.concatenate(probs, axis=1))
            turned[columns, span] = head_rows_of(mixed).astype(BF16)
        return carry

    lax.fori_loop(0, WIDTH // 128, pair, 0)
    stores = [pltpu.make_async_copy(turned, turned_out, sems.at[0])]
    stores[0].start()
    rows[...] = turned[...].T
    stores.append(pltpu.make_async_copy(rows, attended_out, sems.at[1]))
    stores[1].start()
    wait_all(stores)


def attention_forward(where, lengths, pad, qkv):
    rows, columns = (TOKENS, WIDTH), (WIDTH, TOKENS)
    return call(
        attention_kernel,
        (where, lengths, pad, qkv),
        [SMEM, SMEM, VMEM, VMEM],
        [(rows, BF16, True), (columns, BF16, True)],
        [
            pltpu.VMEM((4, 384, 128), F32),
            pltpu.VMEM(columns, BF16),
            pltpu.VMEM(rows, BF16),
            pltpu.SemaphoreType.DMA((2,)),
        ],
    )


def gate_shares(logits, cotangent, shares, gate_grad):
    gate_grad[:, 256:] = cotangent[:, 256:GATE]
    first, rest = logits[:, :128], logits[:, 128:256]
    left = lax.broadcasted_iota(jnp.int32, first.shape, 1) < PIX
    third = jnp.where(left, rest, pltpu.roll(rest, PIX, 1))
    largest = jnp.maximum(jnp.maximum(first, pltpu.roll(first, PIX, 1)), third)
    raised, raised_third = jnp.exp(first - largest), jnp.exp(third - largest)
    scale = 1.0 / (raised + pltpu.roll(raised, PIX, 1) + raised_third)
    share, share_third = raised * scale, raised_third * scale
    shares[:, :128] = share
    shares[:, 128:256] = jnp.where(left, share_third, rest)
    pull, other = cotangent[:, :128].astype(F32), cotangent[:, 128:256].astype(F32)
    pull_third = jnp.where(left, other, pltpu.roll(other, PIX, 1))
    weighed = share * pull
    inner = weighed + pltpu.roll(weighed, PIX, 1) + share_third * pull_third
    gate_grad[:, :128] = (share * (pull - inner)).astype(BF16)
    gate_grad[:, 128:256] = jnp.where(left, share_third * (pull_third - inner), other).astype(BF16)


def head_kernel(where, rows, gate_out, bias, *refs):
    sources, outs, scratch = taken(refs, 4, 1)
    (out,) = outs
    weight, sems, inputs, result, io_sems = scratch
    loads = [block_copies(where, "h", sources, HEAD_PART, weight, sems, side) for side in range(2)]
    row_load = pltpu.make_async_copy(rows, inputs, io_sems.at[0])
    gate_load = pltpu.make_async_copy(gate_out, result.at[:, :GATE], io_sems.at[1])
    row_load.start()
    start_all(loads[0])
    start_all(loads[1])
    gate_load.start()
    row_load.wait()
    stores = []

    def store(span):
        stores.append(
            pltpu.make_async_copy(result.at[:, span], out.at[:, span], io_sems.at[2 + len(stores)])
        )
        stores[-1].start()

    for side in range(2):
        wait_all(loads[side])
        for tile in range(4):
            span = lane_columns(where, side, 2048, GATE + tile * 512, 512)
            columns = lane_columns(where, side, 2048, tile * 512, 512)
            result[:, span] = times(inputs[...], weight[:, columns]) + bias[:, span]
            store(span)
    gate_load.wait()
    store(pl.ds(0, GATE))
    wait_all(stores)


def head_forward(where, rows, gate_out, bias, arrays):
    return call(
        head_kernel,
        (where, rows, gate_out, bias, *arrays),
        [SMEM, HBM, HBM, VMEM] + [HBM] * 4,
        [((TOKENS, HEAD), F32, True)],
        weight_scratch(WIDTH, HEAD - GATE)
        + [
            pltpu.VMEM((TOKENS, WIDTH), BF16),
            pltpu.VMEM((TOKENS, HEAD), F32),
            pltpu.SemaphoreType.DMA((11,)),
        ],
        spare=SPARE_VMEM,
    )[0]


def send_lane(where, group, lane, out, sems, side):
    rows = out.shape[1]
    copies = []
    for place in range(16):
        row = pl.multiple_of(where[table_start(group, side) + place] * rows, rows)
        copies.append(
            pltpu.make_async_copy(lane.at[pl.ds(row, rows), :], out.at[place], sems.at[place])
        )
    start_all(copies)
    return copies


def middle_kernel(
    where, small, up_bias, head_bias, attended, patches, cotangent, act_cotangent, attended_turned,
    *refs,
):
    up_sources, down_sources, head_sources, outs, scratch = taken(refs, 4, 4, 4, 15)
    outputs, shares, gate_bias, down_bias, up_bias_sum, terms, mid_grad, out_grad, mixed, *grads = outs
    down_mine, down_theirs, up_mine, up_theirs, head_mine, head_theirs = grads
    out_weight, out_sems, up, up_sems, down, down_sems, scratch = *scratch[:6], scratch[6:]
    head, head_sems, gate_sems, rows, branch, mid, mlp_turned, scratch = *scratch[:7], scratch[7:]
    act, act_turned, slope, turned, pulls, act_pulls, gate_grad, scratch = *scratch[:7], scratch[7:]
    lane, lane_sems, down_lane, down_lane_sems, mixes, more_sems, io_sems = scratch

    def loads(group, sources, part, target, sems, first=0):
        copies = []
        for side in range(2):
            copies += block_copies(where, group, sources, part, target, sems, side, first)
        return copies

    state_loads = [
        pltpu.make_async_copy(attended, rows, io_sems.at[0]),
        pltpu.make_async_copy(patches, branch, io_sems.at[1]),
    ]
    out_loads = loads("u", up_sources, OUT_PART, out_weight, out_sems)
    up_loads = loads("u", up_sources, UP_PART, up, up_sems)
    down_loads = loads("d", down_sources, DOWN_PART, down, down_sems)
    gate_loads = loads("u", up_sources, GATE_PART, head, gate_sems)
    head_loads = loads("h", head_sources, HEAD_PART, head, head_sems, GATE)
    pull_load = pltpu.make_async_copy(cotangent, pulls, io_sems.at[2])
    act_load = pltpu.make_async_copy(act_cotangent, act_pulls, io_sems.at[3])
    mix_load = pltpu.make_async_copy(attended_turned, mixes, io_sems.at[4])
    start_all(state_loads + out_loads + up_loads + down_loads + gate_loads)
    pull_load.start()
    start_all(head_loads)
    act_load.start()
    mix_load.start()

    wait_all(state_loads + out_loads)
    mid[...] = (
        branch[...].astype(F32)
        + small[16:17, :]
        + times(rows[...], out_weight[...])
        + small[2:3, :]
    )
    centered, scale = mean_and_scale(mid[...])
    rows[...] = (centered * scale * small[3:4, :] + small[4:5, :]).astype(BF16)
    mlp_turned[...] = rows[...].T
    wait_all(up_loads)
    for tile in range(6):
        span = slice(tile * 512, tile * 512 + 512)
        values = times(rows[...], up[:, span]) + up_bias[:, span]
        share = 0.5 * (1.0 + lax.erf(values * 0.7071067811865476))
        density = jnp.exp(-0.5 * values * values) * 0.3989422804014327
        activated = (values * share).astype(BF16)
        act[:, span] = activated
        act_turned[span, :] = activated.T
        slope[:, span] = (share + values * density).astype(BF16)
    wait_all(down_loads)
    outputs[...] = (mid[...] + times(act[...], down[...]) + small[5:6, :]).astype(BF16)
    turned[...] = outputs[...].T
    wait_all(gate_loads)
    shares[...] = times(outputs[...], head[:, :GATE]) + head_bias[:, :GATE]
    pull_load.wait()
    gate_shares(shares, pulls, shares, gate_grad)
    gate_bias[...] = jnp.sum(gate_grad[...].astype(F32), axis=0, keepdims=True)
    pulls[:, :GATE] = gate_grad[...]

    def head_lane(side, target, sems, out):
        target[:, :256] = times(turned[...], pulls[:, lane_columns(where, side, 256)]).astype(BF16)
        for tile in range(4):
            span = lane_columns(where, side, 2048, GATE + tile * 512, 512)
            target[:, 256 + tile * 512 : 768 + tile * 512] = times(turned[...], pulls[:, span]).astype(
                BF16
            )
        return send_lane(where, "head", target, out, sems, side)

    def down_lane_of(side, out):
        columns = branch[:, lane_columns(where, side, 384)]
        for part in range(4):
            span = slice(part * WIDTH, part * WIDTH + WIDTH)
            down_lane[span, :] = times(act_turned[span, :], columns).astype(BF16)
        return send_lane(where, "down", down_lane, out, down_lane_sems, side)

    def up_lane(side, target, sems, out):
        for tile in range(3):
            span = lane_columns(where, side, 1536, tile * 512, 512)
            target[:, tile * 512 : tile * 512 + 512] = times(mlp_turned[...], slope[:, span]).astype(
                BF16
            )
        target[:, 1536:1920] = times(
            mixes[...], out_grad[:, lane_columns(where, side, 384)]
        ).astype(BF16)
        return send_lane(where, "up", target, out, sems, side)

    first_stores = head_lane(1, lane, lane_sems, head_theirs)
    act_load.wait()
    wait_all(head_loads)
    mid_grad[...] = act_pulls[...].astype(F32) + across(pulls[...], head[...])
    branch[...] = mid_grad[...].astype(BF16)
    down_bias[...] = jnp.sum(branch[...].astype(F32), axis=0, keepdims=True)
    stores = head_lane(0, head.at[:, :2304], more_sems.at[0], head_mine)
    down_stores = down_lane_of(1, down_theirs)
    for tile in range(6):
        span = slice(tile * 512, tile * 512 + 512)
        grad = across(branch[...], down[span, :])
        rounded = (slope[:, span].astype(F32) * grad).astype(BF16)
        slope[:, span] = rounded
        up_bias_sum[:, span] = jnp.sum(rounded.astype(F32), axis=0, keepdims=True)
    wait_all(down_stores)
    stores += down_lane_of(0, down_mine)
    grad = across(slope[...], up[...])
    pulled, gain_grad, shift_grad = norm_backward(mid[...], small[3:4, :], grad)
    pulled = pulled + mid_grad[...]
    rounded = pulled.astype(BF16)
    mid_grad[...] = pulled
    out_grad[...] = rounded
    terms[...] = jnp.zeros_like(terms)
    terms[0:1, :] = jnp.sum(rounded.astype(F32), axis=0, keepdims=True)
    terms[1:2, :] = gain_grad
    terms[2:3, :] = shift_grad
    mix_load.wait()
    stores += up_lane(1, head.at[:, 2304:4224], more_sems.at[1], up_theirs)
    wait_all(first_stores)
    stores += up_lane(0, lane.at[:, :1920], lane_sems, up_mine)
    mixed[...] = across(out_grad[...], out_weight[...]).astype(BF16)
    wait_all(stores)


def middle(
    where, small, up_bias, head_bias, attended, patches, cotangent, act_cotangent, attended_turned,
    up, down, head,
):
    rows, columns = (TOKENS, WIDTH), (WIDTH, TOKENS)
    wide, tall = (TOKENS, HIDDEN), (HIDDEN, TOKENS)
    return call(
        middle_kernel,
        (
            where, small, up_bias, head_bias, attended, patches, cotangent, act_cotangent,
            attended_turned, *up, *down, *head,
        ),
        [SMEM, VMEM, VMEM, VMEM] + [HBM] * 17,
        [
            (rows, BF16, False),
            ((TOKENS, GATE), F32, False),
            ((1, GATE), F32, False),
            ((1, WIDTH), F32, False),
            ((1, HIDDEN), F32, False),
            ((8, WIDTH), F32, False),
            (rows, F32, False),
            (rows, BF16, False),
            (rows, BF16, False),
            ((16, 192, 384), BF16, True),
            ((16, 192, 384), BF16, True),
            ((16, 48, 1920), BF16, True),
            ((16, 48, 1920), BF16, True),
            ((16, 48, 2304), BF16, True),
            ((16, 48, 2304), BF16, True),
        ],
        weight_scratch(WIDTH, WIDTH)
        + weight_scratch(WIDTH, HIDDEN)
        + weight_scratch(HIDDEN, WIDTH)
        + weight_scratch(WIDTH, HEAD)
        + [
            pltpu.SemaphoreType.DMA((2, 16)),
            pltpu.VMEM(rows, BF16),
            pltpu.VMEM(rows, BF16),
            pltpu.VMEM(rows, F32),
            pltpu.VMEM(columns, BF16),
            pltpu.VMEM(wide, BF16),
            pltpu.VMEM(tall, BF16),
            pltpu.VMEM(wide, BF16),
            pltpu.VMEM(columns, BF16),
            pltpu.VMEM((TOKENS, HEAD), BF16),
            pltpu.VMEM(rows, BF16),
            pltpu.VMEM((TOKENS, GATE), BF16),
            pltpu.VMEM((WIDTH, 2304), BF16),
            pltpu.SemaphoreType.DMA((16,)),
            pltpu.VMEM((HIDDEN, 384), BF16),
            pltpu.SemaphoreType.DMA((16,)),
            pltpu.VMEM(columns, BF16),
            pltpu.SemaphoreType.DMA((2, 16)),
            pltpu.SemaphoreType.DMA((5,)),
        ],
    )


def attend_back(count, qkv, mixed, bias, turned, key_sum, value_sum, qkv_grad):
    width = 128 * count

    def columns_at(first):
        return pl.ds(pl.multiple_of(first, 128), 128)

    def pair(index, carry):
        own = index * 128
        columns, keys_at = columns_at(own), columns_at(own + width)
        values_at = columns_at(own + 2 * width)
        keys_turned = qkv[:, keys_at].T
        key_sum[...] = jnp.zeros_like(key_sum)
        value_sum[...] = jnp.zeros_like(value_sum)
        for block, (low, high) in enumerate(KEY_SPANS):
            span = slice(128 * block, 128 * block + 128)
            queries, grads = two_heads(qkv[span, columns]), two_heads(mixed[span, columns])
            scores = across(qkv[low:high, keys_at], queries)
            prob_grads = across(qkv[low:high, values_at], grads)
            allowed = bias[block, : high - low, :]
            probs, score_grads = [], []
            for head in range(2):
                part = slice(128 * head, 128 * head + 128)
                prob = probabilities(scores[:, part], allowed)
                pulled = prob * prob_grads[:, part]
                inner = jnp.sum(pulled, axis=0, keepdims=True)
                probs.append(prob.astype(BF16))
                score_grads.append((pulled - prob * inner).astype(BF16))
            score_grad = jnp.concatenate(score_grads, axis=1)
            key_sum[low:high, :] += times(score_grad, queries)
            value_sum[low:high, :] += times(jnp.concatenate(probs, axis=1), grads)
            turned[:, span] = head_rows_of(times(keys_turned[:, low:high], score_grad)) * score_scale
        qkv_grad[:, columns] = turned[...].T.astype(BF16)
        qkv_grad[:, keys_at] = (key_sum[...] * score_scale).astype(BF16)
        qkv_grad[:, values_at] = value_sum[...].astype(BF16)
        return carry

    lax.fori_loop(0, count, pair, 0)


def attention_scratch(count):
    return [
        pltpu.VMEM((4, 384, 128), F32),
        pltpu.VMEM((TOKENS, 384 * count), BF16),
        pltpu.VMEM((TOKENS, 128 * count), BF16),
        pltpu.VMEM((128, TOKENS), F32),
        pltpu.VMEM((TOKENS, 128), F32),
        pltpu.VMEM((TOKENS, 128), F32),
        pltpu.SemaphoreType.DMA((4,)),
    ]


def attention_loads(start, count, qkv, mixed, own_qkv, own_mixed, sems):
    width = 128 * count
    copies = [
        pltpu.make_async_copy(
            mixed.at[:, pl.ds(128 * start, width)], own_mixed.at[:, pl.ds(0, width)], sems.at[3]
        )
    ]
    for part in range(3):
        copies.append(
            pltpu.make_async_copy(
                qkv.at[:, pl.ds(WIDTH * part + 128 * start, width)],
                own_qkv.at[:, pl.ds(width * part, width)],
                sems.at[part],
            )
        )
    return copies


def early_back_kernel(where, lengths, pad, mixed, qkv, input_turned, *refs):
    (qkv_grad, mine_out, theirs_out), scratch = taken(refs, 3)
    bias, own_qkv, own_mixed, turned, key_sum, value_sum, sems, scratch = *scratch[:7], scratch[7:]
    lane, lane_sems, inputs, io_sems = scratch
    loads = attention_loads(0, 4, qkv, mixed, own_qkv, own_mixed, sems)
    in_load = pltpu.make_async_copy(input_turned, inputs, io_sems.at[0])
    start_all(loads + [in_load])
    fill_bias(lengths, pad, bias)
    wait_all(loads)
    attend_back(4, own_qkv, own_mixed, bias, turned, key_sum, value_sum, qkv_grad)
    in_load.wait()
    stores = []
    for side, out in ((1, theirs_out), (0, mine_out)):
        lane[side] = times(inputs[...], qkv_grad[:, lane_columns(where, side, 768)]).astype(BF16)
        stores += send_lane(where, "front", lane.at[side], out, lane_sems.at[side], side)
    wait_all(stores)


def early_backward(where, lengths, pad, mixed, qkv, input_turned):
    return call(
        early_back_kernel,
        (where, lengths, pad, mixed, qkv, input_turned),
        [SMEM, SMEM, VMEM] + [HBM] * 3,
        [
            ((TOKENS, 1536), BF16, False),
            ((16, 48, 768), BF16, True),
            ((16, 48, 768), BF16, True),
        ],
        attention_scratch(4)
        + lane_scratch(WIDTH, 768)
        + [pltpu.VMEM((WIDTH, TOKENS), BF16), pltpu.SemaphoreType.DMA((1,))],
    )


def late_back_kernel(
    where, lead, lengths, pad, small, terms, down_row, up_rows, head_rows,
    mixed, qkv, first_grad, patches, mid_grad, input_turned, *refs
):
    sources, (patch_out, mine_out, theirs_out), scratch = taken(refs, 4, 3)
    bias, own_qkv, own_mixed, turned, key_sum, value_sum, sems, scratch = *scratch[:7], scratch[7:]
    weight, weight_sems, lane, lane_sems, pulls, late_pulls, scratch = *scratch[:6], scratch[6:]
    state, mids, inputs, patch_grad, small_grad, io_sems = scratch
    own_loads = attention_loads(4, 2, qkv, mixed, own_qkv, own_mixed, sems)
    loads = [
        block_copies(where, "q", sources, QKV_PART, weight, weight_sems, side) for side in range(2)
    ]
    pairs = [(patches, state), (mid_grad, mids), (input_turned, inputs)]
    for part in range(3):
        target = pulls.at[:, pl.ds(WIDTH * part, 512)]
        pairs.append((first_grad.at[:, pl.ds(512 * part, 512)], target))
    in_loads = [pltpu.make_async_copy(*pair, io_sems.at[at]) for at, pair in enumerate(pairs)]
    start_all(own_loads + loads[0] + loads[1] + in_loads)
    fill_bias(lengths, pad, bias)
    wait_all(own_loads)
    attend_back(2, own_qkv, own_mixed, bias, turned, key_sum, value_sum, late_pulls)
    wait_all(loads[0] + loads[1] + in_loads)
    for part in range(3):
        pulls[:, WIDTH * part + 512 : WIDTH * part + 768] = late_pulls[
            :, 256 * part : 256 * part + 256
        ]
    grad = across(pulls[...], weight[...])
    pulled, gain_grad, shift_grad = norm_backward(
        state[...].astype(F32) + small[16:17, :], small[0:1, :], grad
    )
    pulled = pulled + mids[...]
    patch_grad[...] = pulled
    stores = [pltpu.make_async_copy(patch_grad, patch_out, io_sems.at[6])]
    stores[0].start()
    small_grad[0:1, :] = gain_grad
    small_grad[1:2, :] = shift_grad
    small_grad[2:5, :] = terms[0:3, :]
    small_grad[5:6, :] = down_row[...]
    small_grad[6:10, :] = up_rows[...]
    small_grad[10:16, :] = head_rows[...]
    places = lax.broadcasted_iota(jnp.int32, (LEADS, WIDTH), 0)
    lead_grad = jnp.sum(pulled, axis=0, keepdims=True)
    small_grad[16:32, :] = jnp.where(places == lead[0], lead_grad, 0.0)
    for side, out in ((1, theirs_out), (0, mine_out)):
        lane[side, :, :384] = times(
            inputs[...], late_pulls[:, lane_columns(where, side, 384)]
        ).astype(BF16)
        rows = small_grad[pl.ds(pl.multiple_of((where[0] ^ side) * 16, 16), 16), :]
        rows = jnp.concatenate([rows, jnp.zeros((112, WIDTH), F32)], axis=0)
        lane[side, :, 384:] = rows.T.astype(BF16)
        stores += send_lane(where, "front", lane.at[side], out, lane_sems.at[side], side)
    wait_all(stores)


def late_backward(
    where, lead, lengths, pad, small, terms, down_row, up_rows, head_rows,
    mixed, qkv, first_grad, patches, mid_grad, input_turned, arrays,
):
    rows, columns = (TOKENS, WIDTH), (WIDTH, TOKENS)
    return call(
        late_back_kernel,
        (
            where, lead, lengths, pad, small, terms, down_row, up_rows, head_rows,
            mixed, qkv, first_grad, patches, mid_grad, input_turned, *arrays,
        ),
        [SMEM, SMEM, SMEM] + [VMEM] * 6 + [HBM] * 10,
        [(rows, F32, True), ((16, 48, 512), BF16, True), ((16, 48, 512), BF16, True)],
        attention_scratch(2)
        + weight_scratch(WIDTH, 3 * WIDTH)
        + lane_scratch(WIDTH, 512)
        + [
            pltpu.VMEM((TOKENS, 3 * WIDTH), BF16),
            pltpu.VMEM((TOKENS, WIDTH), BF16),
            pltpu.VMEM(rows, BF16),
            pltpu.VMEM(rows, F32),
            pltpu.VMEM(columns, BF16),
            pltpu.VMEM(rows, F32),
            pltpu.VMEM((32, WIDTH), F32),
            pltpu.SemaphoreType.DMA((7,)),
        ],
    )


def rows_of(vector, count):
    return vector.reshape(32, count, 24).transpose(1, 0, 2).reshape(count, WIDTH)


def vector_of(rows):
    count = rows.shape[0]
    return rows.reshape(count, 32, 24).transpose(1, 0, 2).reshape(1, count * WIDTH)


def shards(
    patches,
    lead_index,
    window_lengths,
    pad_mask,
    lead_table,
    attn_gain,
    attn_shift,
    qkv_weight,
    out_weight,
    out_bias,
    mlp_gain,
    mlp_shift,
    up_weight,
    up_bias,
    down_weight,
    down_bias,
    head_weight,
    head_bias,
    act_cotangent,
    head_cotangent,
):
    core, where = whereabouts()
    weights = (qkv_weight, out_weight, up_weight, down_weight, head_weight)
    vectors = (
        attn_gain, attn_shift, out_bias, mlp_gain, mlp_shift, down_bias, up_bias, head_bias
    )
    parts = packed(core, weights, lead_table, vectors)
    pad = pad_mask[:, None]
    cotangent_sum = jnp.sum(head_cotangent[:, GATE:].astype(F32), axis=0, keepdims=True)

    orders = ORDERS
    parts = dict(zip("qudh", zip(parts[:4], parts[4:])))
    chunks = {
        name: in_core_order(core, mine, exchange(theirs, SIBLING), 0)[None]
        for name, (mine, theirs) in parts.items()
    }

    held, last = dict(chunks), ()
    for name, step in GATHER_SEQUENCE:
        held[name] = after(held[name], *last)
        last = (held[name],)
        held[name] = doubled(held[name], orders[name][step])
    q, u, d, h = [held[name] for name in ("q", "u", "d", "h")]
    q_rest = exchange(after(q, *last), orders["q"][3])
    u = after(u, q)
    u_rest = exchange(u, orders["u"][3])
    d_rest = exchange(d, orders["d"][3])
    h = doubled(after(h, u), orders["h"][2])
    first = both_lanes(q, q_rest)
    h_rest = exchange(h, orders["h"][3])
    input_turned, qkv, small_rows = front_forward(
        after(where, d, h, cotangent_sum), lead_index, patches, first
    )
    attended, attended_turned = attention_forward(where, window_lengths, pad, qkv)
    u_rest, d_rest, h_rest = lax.optimization_barrier((u_rest, d_rest, h_rest, attended))[:3]
    second, down, head = both_lanes(u, u_rest), both_lanes(d, d_rest), both_lanes(h, h_rest)
    up_bias_row, head_bias_row = vector_of(small_rows[6:10]), vector_of(small_rows[10:16])
    (
        outputs, gate_out, gate_bias_sum, down_bias_sum, up_bias_sum, terms, mid_grad, _, mixed_grad,
        mine_d, theirs_d, mine_u, theirs_u, mine_h, theirs_h,
    ) = middle(
        where, small_rows, up_bias_row, head_bias_row, attended, patches, head_cotangent,
        act_cotangent, attended_turned, second, down, head,
    )

    got_h, got_d, got_u = [exchange(theirs, SIBLING) for theirs in (theirs_h, theirs_d, theirs_u)]
    head_rows = rows_of(jnp.concatenate([gate_bias_sum, cotangent_sum], axis=1), 6)
    up_rows = rows_of(up_bias_sum, 4)
    first_grad, mine_m, theirs_m = early_backward(
        where, window_lengths, pad, mixed_grad, qkv, input_turned
    )
    groups = {
        "head": [[mine_h], after(got_h, first_grad), 4],
        "up": [[mine_u], after(got_u, first_grad), 4],
        "down": [[mine_d], after(got_d, first_grad), 4],
        "mix": [[mine_m], exchange(theirs_m, SIBLING), 4],
    }
    last = ()

    def add(name):
        nonlocal last
        keep, got, step = groups[name]
        keep, send = folded(keep, after(got, *last))
        last = (send,)
        groups[name] = [keep, exchange(send, orders[name][step - 1]), step - 1]

    def finish(name, widths):
        keep, got, _ = groups[name]
        return finished(keep, after(got, *last), core, widths)

    for name in ("head", "up", "down"):
        add(name)
    patch_grad, mine_f, theirs_f = late_backward(
        after(where, *last), lead_index, window_lengths, pad, small_rows, terms, down_bias_sum,
        up_rows, head_rows, mixed_grad, qkv, first_grad, patches, mid_grad, input_turned, first,
    )
    last = (patch_grad,)
    groups["front"] = [[mine_f], exchange(theirs_f, SIBLING), 4]
    for name in ("head", "mix", "front", "down", "up"):
        add(name)
    head_out = head_forward(after(where, *last), outputs, gate_out, head_bias_row, head)
    last = (head_out,)
    for name in ("head", "front", "mix", "head"):
        add(name)
    gate_sum, rest_sum = finish("head", (256, 2048))
    for name in ("down", "up", "front", "mix", "down", "up", "front", "mix"):
        add(name)
    up_sum, out_sum = finish("up", (1536, 384))
    (down_sum,) = finish("down", (384,))
    (early_sum,) = finish("mix", (768,))
    late_sum, small_sum = finish("front", (384, 128))
    qkv_sum = jnp.concatenate(
        [
            piece[:, part * piece.shape[1] // 3 : (part + 1) * piece.shape[1] // 3]
            for part in range(3)
            for piece in (early_sum, late_sum)
        ],
        axis=1,
    )
    small_sum = small_sum.T
    return (
        outputs,
        head_out,
        patch_grad,
        small_sum[128:144],
        small_sum[0],
        small_sum[1],
        qkv_sum,
        out_sum,
        small_sum[2],
        small_sum[3],
        small_sum[4],
        up_sum,
        small_sum[6:10].reshape(96),
        down_sum,
        small_sum[5],
        jnp.concatenate([gate_sum, rest_sum], axis=1),
        small_sum[10:16].reshape(144),
    )


def plain_shards(
    patches,
    lead_index,
    window_lengths,
    pad_mask,
    lead_table,
    attn_gain,
    attn_shift,
    qkv_weight,
    out_weight,
    out_bias,
    mlp_gain,
    mlp_shift,
    up_weight,
    up_bias,
    down_weight,
    down_bias,
    head_weight,
    head_bias,
    act_cotangent,
    head_cotangent,
):
    front = (
        lax.all_gather(lead_table, ("dp", "fsdp"), axis=1, tiled=True),
        lax.all_gather(attn_gain, ("dp", "fsdp"), axis=0, tiled=True),
        lax.all_gather(attn_shift, ("dp", "fsdp"), axis=0, tiled=True),
        lax.all_gather(qkv_weight, ("dp", "fsdp"), axis=0, tiled=True),
        lax.all_gather(out_weight, ("dp", "fsdp"), axis=0, tiled=True),
        lax.all_gather(out_bias, ("dp", "fsdp"), axis=0, tiled=True),
    )
    rear = (
        lax.all_gather(mlp_gain, ("dp", "fsdp"), axis=0, tiled=True),
        lax.all_gather(mlp_shift, ("dp", "fsdp"), axis=0, tiled=True),
        lax.all_gather(up_weight, ("dp", "fsdp"), axis=0, tiled=True),
        lax.all_gather(up_bias, ("dp", "fsdp"), axis=0, tiled=True),
        lax.all_gather(down_weight, ("dp", "fsdp"), axis=0, tiled=True),
        lax.all_gather(down_bias, ("dp", "fsdp"), axis=0, tiled=True),
        lax.all_gather(head_weight, ("dp", "fsdp"), axis=0, tiled=True),
        lax.all_gather(head_bias, ("dp", "fsdp"), axis=0, tiled=True),
    )
    table_full, gain_one, shift_one, qkv_full, out_full, out_bias_full = front
    (
        gain_two,
        shift_two,
        up_full,
        up_bias_full,
        down_full,
        down_bias_full,
        head_full,
        head_bias_full,
    ) = rear
    token_rows, width = patches.shape
    head_dim = width // HEADS
    block_rows = min(512, token_rows)
    block_count = token_rows // block_rows
    ends = jnp.cumsum(window_lengths[0])
    positions = jnp.arange(token_rows, dtype=jnp.int32)
    window = jnp.sum((positions[:, None] >= ends[None, :]).astype(jnp.int32), axis=1)
    lead_hot = (jnp.arange(LEADS, dtype=jnp.int32) == lead_index[0]).astype(jnp.float32)
    lead_row = jnp.sum(lead_hot[:, None] * table_full.astype(jnp.float32), axis=0)
    start_state = patches.astype(jnp.float32) + lead_row[None, :]
    normed_one, pull_one = jax.vjp(
        layer_norm, start_state, gain_one.astype(jnp.float32), shift_one.astype(jnp.float32)
    )
    attn_input = normed_one.astype(jnp.bfloat16)
    qkv_rows = jnp.dot(attn_input, qkv_full, preferred_element_type=jnp.float32).astype(
        jnp.bfloat16
    )
    queries = qkv_rows[:, :width].reshape(block_count, block_rows, HEADS, head_dim)
    keys = qkv_rows[:, width : 2 * width].reshape(token_rows, HEADS, head_dim)
    values = qkv_rows[:, 2 * width :].reshape(token_rows, HEADS, head_dim)
    query_windows = window.reshape(block_count, block_rows)
    block_starts = jnp.arange(block_count, dtype=jnp.int32) * block_rows

    def block_scores(query_block, window_block, block_start):
        scores = (
            jnp.einsum("qhd,khd->hqk", query_block, keys, preferred_element_type=jnp.float32)
            * score_scale
        )
        allowed = allowed_keys(window_block, window, pad_mask, block_start)
        return jnp.where(allowed[None], scores, -1e30)

    def forward_block(inputs):
        query_block, window_block, block_start = inputs
        masked = block_scores(query_block, window_block, block_start)
        largest = jnp.max(masked, axis=-1, keepdims=True)
        raised = jnp.exp(masked - largest)
        total = jnp.sum(raised, axis=-1, keepdims=True)
        probs = (raised / total).astype(jnp.bfloat16)
        mixed = jnp.einsum("hqk,khd->qhd", probs, values, preferred_element_type=jnp.float32)
        return (
            mixed.reshape(block_rows, width).astype(jnp.bfloat16),
            (largest + jnp.log(total))[:, :, 0],
        )

    mixed_blocks, log_totals = lax.map(forward_block, (queries, query_windows, block_starts))
    attended = mixed_blocks.reshape(token_rows, width)
    mid_state = (
        start_state
        + jnp.dot(attended, out_full, preferred_element_type=jnp.float32)
        + out_bias_full.astype(jnp.float32)
    )
    normed_two, pull_two = jax.vjp(
        layer_norm, mid_state, gain_two.astype(jnp.float32), shift_two.astype(jnp.float32)
    )
    mlp_input = normed_two.astype(jnp.bfloat16)
    pre_act = jnp.dot(mlp_input, up_full, preferred_element_type=jnp.float32) + up_bias_full.astype(
        jnp.float32
    )
    activated, pull_act = jax.vjp(gelu_exact, pre_act)
    act_rows = activated.astype(jnp.bfloat16)
    end_state = (
        mid_state
        + jnp.dot(act_rows, down_full, preferred_element_type=jnp.float32)
        + down_bias_full.astype(jnp.float32)
    )
    outputs = end_state.astype(jnp.bfloat16)
    logits = jnp.dot(
        outputs, head_full, preferred_element_type=jnp.float32
    ) + head_bias_full.astype(jnp.float32)
    head_out, pull_head = jax.vjp(partial(expert_softmax, experts=EXPERTS, pixels=PIX), logits)
    up_back, down_back, head_back = (
        lax.all_gather(up_weight, ("dp", "fsdp"), axis=0, tiled=True),
        lax.all_gather(down_weight, ("dp", "fsdp"), axis=0, tiled=True),
        lax.all_gather(head_weight, ("dp", "fsdp"), axis=0, tiled=True),
    )
    qkv_back, out_back = (
        lax.all_gather(qkv_weight, ("dp", "fsdp"), axis=0, tiled=True),
        lax.all_gather(out_weight, ("dp", "fsdp"), axis=0, tiled=True),
    )
    logit_grad = pull_head(head_cotangent.astype(jnp.float32))[0].astype(jnp.bfloat16)
    head_bias_term = jnp.sum(logit_grad.astype(jnp.float32), axis=0)
    head_term = jnp.einsum("td,tn->dn", outputs, logit_grad, preferred_element_type=jnp.float32)
    end_grad = act_cotangent.astype(jnp.float32) + jnp.einsum(
        "tn,dn->td", logit_grad, head_back, preferred_element_type=jnp.float32
    )
    branch_grad = end_grad.astype(jnp.bfloat16)
    down_bias_term = jnp.sum(branch_grad.astype(jnp.float32), axis=0)
    down_term = jnp.einsum("tf,td->fd", act_rows, branch_grad, preferred_element_type=jnp.float32)
    act_grad = jnp.einsum("td,fd->tf", branch_grad, down_back, preferred_element_type=jnp.float32)
    pre_grad = pull_act(act_grad)[0].astype(jnp.bfloat16)
    up_bias_term = jnp.sum(pre_grad.astype(jnp.float32), axis=0)
    up_term = jnp.einsum("td,tf->df", mlp_input, pre_grad, preferred_element_type=jnp.float32)
    normed_two_grad = jnp.einsum("tf,df->td", pre_grad, up_back, preferred_element_type=jnp.float32)
    state_grad_two, gain_two_term, shift_two_term = pull_two(normed_two_grad)
    (
        gain_part,
        shift_part,
        up_part,
        up_bias_part,
        down_part,
        down_bias_part,
        head_part,
        head_bias_part,
    ) = (
        lax.psum_scatter(
            gain_two_term.astype(jnp.bfloat16), "dp", scatter_dimension=0, tiled=True
        ).astype(jnp.float32),
        lax.psum_scatter(
            shift_two_term.astype(jnp.bfloat16), "dp", scatter_dimension=0, tiled=True
        ).astype(jnp.float32),
        lax.psum_scatter(
            up_term.astype(jnp.bfloat16), "dp", scatter_dimension=0, tiled=True
        ).astype(jnp.float32),
        lax.psum_scatter(
            up_bias_term.astype(jnp.bfloat16), "dp", scatter_dimension=0, tiled=True
        ).astype(jnp.float32),
        lax.psum_scatter(
            down_term.astype(jnp.bfloat16), "dp", scatter_dimension=0, tiled=True
        ).astype(jnp.float32),
        lax.psum_scatter(
            down_bias_term.astype(jnp.bfloat16), "dp", scatter_dimension=0, tiled=True
        ).astype(jnp.float32),
        lax.psum_scatter(
            head_term.astype(jnp.bfloat16), "dp", scatter_dimension=0, tiled=True
        ).astype(jnp.float32),
        lax.psum_scatter(
            head_bias_term.astype(jnp.bfloat16), "dp", scatter_dimension=0, tiled=True
        ).astype(jnp.float32),
    )
    rear_grads = (
        lax.psum_scatter(gain_part, "fsdp", scatter_dimension=0, tiled=True),
        lax.psum_scatter(shift_part, "fsdp", scatter_dimension=0, tiled=True),
        lax.psum_scatter(up_part, "fsdp", scatter_dimension=0, tiled=True),
        lax.psum_scatter(up_bias_part, "fsdp", scatter_dimension=0, tiled=True),
        lax.psum_scatter(down_part, "fsdp", scatter_dimension=0, tiled=True),
        lax.psum_scatter(down_bias_part, "fsdp", scatter_dimension=0, tiled=True),
        lax.psum_scatter(head_part, "fsdp", scatter_dimension=0, tiled=True),
        lax.psum_scatter(head_bias_part, "fsdp", scatter_dimension=0, tiled=True),
    )
    mid_grad = end_grad + state_grad_two
    out_grad = mid_grad.astype(jnp.bfloat16)
    out_bias_term = jnp.sum(out_grad.astype(jnp.float32), axis=0)
    out_term = jnp.einsum("td,te->de", attended, out_grad, preferred_element_type=jnp.float32)
    mixed_grad = jnp.einsum(
        "te,de->td", out_grad, out_back, preferred_element_type=jnp.float32
    ).astype(jnp.bfloat16)
    grad_blocks = mixed_grad.reshape(block_count, block_rows, HEADS, head_dim)

    def backward_block(carry, inputs):
        key_sum, value_sum = carry
        query_block, grad_block, window_block, total_block, block_start = inputs
        masked = block_scores(query_block, window_block, block_start)
        probs = jnp.exp(masked - total_block[:, :, None])
        prob_grad = jnp.einsum(
            "qhd,khd->hqk", grad_block, values, preferred_element_type=jnp.float32
        )
        inner = jnp.sum(probs * prob_grad, axis=-1, keepdims=True)
        score_grad = (probs * (prob_grad - inner)).astype(jnp.bfloat16)
        query_grad = (
            jnp.einsum("hqk,khd->qhd", score_grad, keys, preferred_element_type=jnp.float32)
            * score_scale
        )
        key_sum = (
            key_sum
            + jnp.einsum(
                "hqk,qhd->khd", score_grad, query_block, preferred_element_type=jnp.float32
            )
            * score_scale
        )
        value_sum = value_sum + jnp.einsum(
            "hqk,qhd->khd",
            probs.astype(jnp.bfloat16),
            grad_block,
            preferred_element_type=jnp.float32,
        )
        return ((key_sum, value_sum), query_grad.reshape(block_rows, width))

    zero_keys = jnp.zeros((token_rows, HEADS, head_dim), jnp.float32)
    (key_grad, value_grad), query_grads = lax.scan(
        backward_block,
        (zero_keys, zero_keys),
        (queries, grad_blocks, query_windows, log_totals, block_starts),
    )
    qkv_grad = jnp.concatenate(
        [
            query_grads.reshape(token_rows, width),
            key_grad.reshape(token_rows, width),
            value_grad.reshape(token_rows, width),
        ],
        axis=1,
    ).astype(jnp.bfloat16)
    qkv_term = jnp.einsum("td,te->de", attn_input, qkv_grad, preferred_element_type=jnp.float32)
    normed_one_grad = jnp.einsum(
        "te,de->td", qkv_grad, qkv_back, preferred_element_type=jnp.float32
    )
    state_grad_one, gain_one_term, shift_one_term = pull_one(normed_one_grad)
    patch_grad = mid_grad + state_grad_one
    lead_term = lead_hot[:, None] * jnp.sum(patch_grad, axis=0)[None, :]
    lead_part, gain_one_part, shift_one_part, qkv_part, out_part, out_bias_part = (
        lax.psum_scatter(
            lead_term.astype(jnp.bfloat16), "dp", scatter_dimension=1, tiled=True
        ).astype(jnp.float32),
        lax.psum_scatter(
            gain_one_term.astype(jnp.bfloat16), "dp", scatter_dimension=0, tiled=True
        ).astype(jnp.float32),
        lax.psum_scatter(
            shift_one_term.astype(jnp.bfloat16), "dp", scatter_dimension=0, tiled=True
        ).astype(jnp.float32),
        lax.psum_scatter(
            qkv_term.astype(jnp.bfloat16), "dp", scatter_dimension=0, tiled=True
        ).astype(jnp.float32),
        lax.psum_scatter(
            out_term.astype(jnp.bfloat16), "dp", scatter_dimension=0, tiled=True
        ).astype(jnp.float32),
        lax.psum_scatter(
            out_bias_term.astype(jnp.bfloat16), "dp", scatter_dimension=0, tiled=True
        ).astype(jnp.float32),
    )
    front_grads = (
        lax.psum_scatter(lead_part, "fsdp", scatter_dimension=1, tiled=True),
        lax.psum_scatter(gain_one_part, "fsdp", scatter_dimension=0, tiled=True),
        lax.psum_scatter(shift_one_part, "fsdp", scatter_dimension=0, tiled=True),
        lax.psum_scatter(qkv_part, "fsdp", scatter_dimension=0, tiled=True),
        lax.psum_scatter(out_part, "fsdp", scatter_dimension=0, tiled=True),
        lax.psum_scatter(out_bias_part, "fsdp", scatter_dimension=0, tiled=True),
    )
    return (
        outputs,
        head_out,
        patch_grad,
        front_grads[0],
        front_grads[1],
        front_grads[2],
        front_grads[3],
        front_grads[4],
        front_grads[5],
        rear_grads[0],
        rear_grads[1],
        rear_grads[2],
        rear_grads[3],
        rear_grads[4],
        rear_grads[5],
        rear_grads[6],
        rear_grads[7],
    )


def solution(mesh):
    in_specs = (
        P(("dp", "fsdp"), None),
        P(("dp", "fsdp")),
        P(("dp", "fsdp"), None),
        P(("dp", "fsdp")),
        P(None, ("dp", "fsdp")),
        P(("dp", "fsdp")),
        P(("dp", "fsdp")),
        P(("dp", "fsdp"), None),
        P(("dp", "fsdp"), None),
        P(("dp", "fsdp")),
        P(("dp", "fsdp")),
        P(("dp", "fsdp")),
        P(("dp", "fsdp"), None),
        P(("dp", "fsdp")),
        P(("dp", "fsdp"), None),
        P(("dp", "fsdp")),
        P(("dp", "fsdp"), None),
        P(("dp", "fsdp")),
        P(("dp", "fsdp"), None),
        P(("dp", "fsdp"), None),
    )
    out_specs = (
        P(("dp", "fsdp"), None),
        P(("dp", "fsdp"), None),
        P(("dp", "fsdp"), None),
        P(None, ("dp", "fsdp")),
        P(("dp", "fsdp")),
        P(("dp", "fsdp")),
        P(("dp", "fsdp"), None),
        P(("dp", "fsdp"), None),
        P(("dp", "fsdp")),
        P(("dp", "fsdp")),
        P(("dp", "fsdp")),
        P(("dp", "fsdp"), None),
        P(("dp", "fsdp")),
        P(("dp", "fsdp"), None),
        P(("dp", "fsdp")),
        P(("dp", "fsdp"), None),
        P(("dp", "fsdp")),
    )
    body = shards if dict(mesh.shape) == {"dp": 4, "fsdp": 8} else plain_shards
    return jax.shard_map(body, mesh=mesh, in_specs=in_specs, out_specs=out_specs, check_vma=False)
```

```python
import math
from functools import partial

import jax
import jax.numpy as jnp
from jax import lax
from jax.experimental import pallas as pl
from jax.experimental.pallas import tpu as pltpu
from jax.sharding import PartitionSpec as P

HEADS = 12
PIX = 64
EXPERTS = 3
LEADS = 16


norm_epsilon = 1e-05
score_scale = 0.125


def layer_norm(hidden, norm_gain, norm_shift):
    average = jnp.mean(hidden, axis=-1, keepdims=True)
    centered = hidden - average
    variance = jnp.mean(centered * centered, axis=-1, keepdims=True)
    return centered * lax.rsqrt(variance + norm_epsilon) * norm_gain + norm_shift


def gelu_exact(values):
    return 0.5 * values * (1.0 + lax.erf(values * 0.7071067811865476))


def expert_softmax(logits, experts, pixels):
    gate_part = logits[:, : experts * pixels].reshape(logits.shape[0], experts, pixels)
    largest = jnp.max(gate_part, axis=1, keepdims=True)
    raised = jnp.exp(gate_part - largest)
    shares = raised / jnp.sum(raised, axis=1, keepdims=True)
    return jnp.concatenate(
        [shares.reshape(logits.shape[0], experts * pixels), logits[:, experts * pixels :]], axis=1
    )


def allowed_keys(query_window, key_window, key_valid, query_start):
    query_place = query_start + jnp.arange(query_window.shape[0], dtype=jnp.int32)
    key_place = jnp.arange(key_window.shape[0], dtype=jnp.int32)
    same_window = query_window[:, None] == key_window[None, :]
    usable = (key_valid[None, :] > 0) | (query_place[:, None] == key_place[None, :])
    return same_window & usable


AXES = ("dp", "fsdp")
FAR_Z, NEAR_Z, FIRST, SECOND, SIBLING = (4, 4), (2, 2), (8, 16), (16, 8), (1, 1)
ORDERS = {
    "q": (FAR_Z, NEAR_Z, FIRST, SECOND),
    "u": (FAR_Z, FIRST, SECOND, NEAR_Z),
    "d": (FIRST, FAR_Z, NEAR_Z, SECOND),
    "h": (NEAR_Z, FAR_Z, FIRST, SECOND),
    "head": (FAR_Z, NEAR_Z, FIRST, SECOND),
    "down": (FAR_Z, NEAR_Z, FIRST, SECOND),
    "up": (FAR_Z, FIRST, SECOND, NEAR_Z),
    "front": (FAR_Z, NEAR_Z, FIRST, SECOND),
    "mix": (FAR_Z, NEAR_Z, FIRST, SECOND),
}
GATHER_SEQUENCE = (
    ("q", 0), ("d", 0), ("h", 0), ("u", 0), ("q", 1), ("d", 1), ("u", 1), ("q", 2), ("h", 1), ("u", 2),
    ("d", 2),
)
MOST_VMEM, SPARE_VMEM = 60 * 1024 * 1024, 8 * 1024 * 1024
WIDTH = 768
HIDDEN = 3072
HEAD = 4608
TOKENS = 512
GATE = 512
F32 = jnp.float32
BF16 = jnp.bfloat16
HBM = pl.BlockSpec(memory_space=pltpu.HBM)
SMEM = pl.BlockSpec(memory_space=pltpu.SMEM)
VMEM = pl.BlockSpec(memory_space=pltpu.VMEM)
QKV_PART, SMALL_PART = (0, 1152), (1152, 128)
UP_PART, OUT_PART, GATE_PART = (0, 1536), (1536, 384), (1920, 256)
DOWN_PART, HEAD_PART = (0, 384), (0, 2048)


def chip_masks(order, lane):
    masks = []
    for place in range(16):
        mask = 0
        for step in range(4):
            if place >> step & 1:
                mask ^= order[step][lane]
        masks.append(mask >> 1)
    return masks


def table_start(group, side):
    return 1 + 32 * list(ORDERS).index(group) + 16 * side


def exchange(array, masks):
    return lax.ppermute(array, AXES, [(d, d ^ masks[d & 1]) for d in range(32)])


def whereabouts():
    device = lax.axis_index("dp") * 8 + lax.axis_index("fsdp")
    core, chip = device % 2, device // 2
    tables = [chip_masks(order, 0) + chip_masks(order, 1) for order in ORDERS.values()]
    swapped = [chip_masks(order, 1) + chip_masks(order, 0) for order in ORDERS.values()]
    places = jnp.where(core == 0, jnp.array(tables, jnp.int32), jnp.array(swapped, jnp.int32))
    places = (places ^ chip).reshape(32 * len(ORDERS))
    return core, jnp.concatenate([core[None].astype(jnp.int32), places])


def after(value, *marks):
    return lax.optimization_barrier((value, marks))[0]


def in_core_order(core, mine, theirs, axis):
    return jnp.where(
        core == 0,
        jnp.concatenate([mine, theirs], axis=axis),
        jnp.concatenate([theirs, mine], axis=axis),
    )


def pack_kernel(core, qkv, out, up, down, head, table, *refs):
    vectors, (up_bias, head_bias), refs = refs[:6], refs[6:8], refs[8:]
    outs, (rows,) = refs[:8], refs[8:]
    rows[...] = jnp.zeros_like(rows)
    for index, vector in enumerate(vectors):
        rows[index : index + 1, :24] = vector[...].astype(F32)
    for index in range(4):
        rows[6 + index : 7 + index, :24] = up_bias[:, 24 * index : 24 * index + 24].astype(F32)
    for index in range(6):
        rows[10 + index : 11 + index, :24] = head_bias[:, 24 * index : 24 * index + 24].astype(F32)
    rows[16:32, :24] = table[...].astype(F32)
    small = rows[...].T[:24].astype(BF16)
    for side in range(2):
        q, u, d, h = outs[4 * side : 4 * side + 4]
        q[:, :1152] = qkv[:, lane_columns(core, side, 1152)]
        q[:, 1152:] = small
        u[:, :1536] = up[:, lane_columns(core, side, 1536)]
        u[:, 1536:1920] = out[:, lane_columns(core, side, 384)]
        u[:, 1920:] = head[:, lane_columns(core, side, 256)]
        d[...] = down[:, lane_columns(core, side, 384)]
        h[...] = head[:, lane_columns(core, side, 2048, GATE)]


def packed(core, weights, table, vectors):
    shapes = [(24, 1280), (24, 2176), (96, 384), (24, 2048)] * 2
    return call(
        pack_kernel,
        (core.reshape(1), *weights, table, *[vector[None] for vector in vectors]),
        [SMEM] + [VMEM] * 14,
        [(shape, BF16, False) for shape in shapes],
        [pltpu.VMEM((128, 128), F32)],
    )


def doubled(held, masks):
    return jnp.concatenate([held, exchange(held, masks)], axis=0)


def both_lanes(*arrays):
    return arrays + tuple(exchange(array, SIBLING) for array in arrays)


def total(parts):
    result = parts[0].astype(F32)
    for part in parts[1:]:
        result = result + part.astype(F32)
    return result


def folded(parts, got):
    parts = [*parts, got]
    half = got.shape[0] // 2
    send = total([part[half:] for part in parts]).astype(BF16)
    kept = [part[:half] for part in parts]
    return (kept if len(kept) == 2 else [total(kept).astype(BF16)]), send


def finished(parts, got, core, widths):
    block = total([*parts, got])[0]
    rows = block.shape[0] // 2
    upper, lower = block[:rows], block[rows:]
    mine = jnp.where(core == 0, upper, lower)
    theirs = jnp.where(core == 0, lower, upper).astype(BF16)
    other = exchange(theirs, SIBLING).astype(F32)
    pieces, start = [], 0
    for width in widths:
        span = slice(start, start + width)
        pieces.append(in_core_order(core, mine[:, span], other[:, span], 1))
        start += width
    return pieces


def across(first, second):
    return lax.dot_general(first, second, (((1,), (1,)), ((), ())), preferred_element_type=F32)


def times(first, second):
    return jnp.dot(first, second, preferred_element_type=F32)


def lane_columns(where, side, stride, first=0, width=None):
    return pl.ds(pl.multiple_of(first + (where[0] ^ side) * stride, 128), width or stride)


def block_copies(where, group, sources, part, target, sems, side, first=0):
    start, width = part
    rows = sources[0].shape[1]
    half = len(sources) // 2
    count = 16 // half
    copies = []
    for place in range(16):
        row = pl.multiple_of(where[table_start(group, side) + place] * rows, rows)
        copies.append(
            pltpu.make_async_copy(
                sources[half * side + place // count].at[place % count, :, pl.ds(start, width)],
                target.at[pl.ds(row, rows), lane_columns(where, side, width, first)],
                sems.at[side, place],
            )
        )
    return copies


def start_all(copies):
    for copy in copies:
        copy.start()


def wait_all(copies):
    for copy in copies:
        copy.wait()


def mean_and_scale(hidden):
    average = jnp.mean(hidden, axis=1, keepdims=True)
    centered = hidden - average
    variance = jnp.mean(centered * centered, axis=1, keepdims=True)
    return centered, lax.rsqrt(variance + norm_epsilon)


def norm_backward(hidden, gain, upstream):
    centered, scale = mean_and_scale(hidden)
    normed = centered * scale
    gain_grad = jnp.sum(upstream * normed, axis=0, keepdims=True)
    shift_grad = jnp.sum(upstream, axis=0, keepdims=True)
    scaled = upstream * gain
    first = jnp.mean(scaled, axis=1, keepdims=True)
    second = jnp.mean(scaled * normed, axis=1, keepdims=True)
    return scale * (scaled - first - normed * second), gain_grad, shift_grad


def call(kernel, operands, in_specs, outs, scratch, spare=None):
    def size(item):
        return math.prod(item.shape) * jnp.dtype(item.dtype).itemsize

    held = [item for item, spec in zip(operands, in_specs) if spec is VMEM]
    held += [jax.ShapeDtypeStruct(shape, kind) for shape, kind, copied in outs if not copied]
    held += [item for item in scratch if getattr(item, "memory_space", None) == pltpu.VMEM]
    limit = MOST_VMEM if spare is None else sum(size(item) for item in held) + spare
    return pl.pallas_call(
        kernel,
        out_shape=[jax.ShapeDtypeStruct(shape, kind) for shape, kind, _ in outs],
        in_specs=in_specs,
        out_specs=[HBM if copied else VMEM for _, _, copied in outs],
        scratch_shapes=scratch,
        compiler_params=pltpu.CompilerParams(vmem_limit_bytes=limit),
        cost_estimate=pl.CostEstimate(flops=2 * 10**12, bytes_accessed=10**10, transcendentals=0),
    )(*operands)


def lane_scratch(rows, width):
    return [pltpu.VMEM((2, rows, width), BF16), pltpu.SemaphoreType.DMA((2, 16))]


def weight_scratch(rows, width):
    return [pltpu.VMEM((rows, width), BF16), pltpu.SemaphoreType.DMA((2, 16))]


def taken(refs, *counts):
    groups = []
    for count in counts:
        groups.append(refs[:count])
        refs = refs[count:]
    return *groups, refs


def front_kernel(where, lead, patches, *refs):
    sources, outs, scratch = taken(refs, 4, 3)
    turned_out, qkv_out, small = outs
    weight, sems, smalls, small_sems, state, rows, turned, qkv, io_sems = scratch
    loads = [block_copies(where, "q", sources, QKV_PART, weight, sems, side) for side in range(2)]
    small_loads = []
    for place in range(16):
        row = pl.multiple_of(where[table_start("q", 0) + place] * 48, 48)
        small_loads.append(
            pltpu.make_async_copy(
                sources[place // 8].at[place % 8, :, pl.ds(*SMALL_PART)],
                smalls.at[pl.ds(row, 48), :],
                small_sems.at[place],
            )
        )
    state_load = pltpu.make_async_copy(patches, state, io_sems.at[0])
    start_all(small_loads)
    state_load.start()
    start_all(loads[0])
    start_all(loads[1])
    wait_all(small_loads)
    columns = smalls[...].astype(F32).T
    places = lax.broadcasted_iota(jnp.int32, (LEADS, WIDTH), 0)
    lead_row = jnp.sum(
        jnp.where(places == lead[0], columns[16 : 16 + LEADS], 0.0), axis=0, keepdims=True
    )
    small[...] = columns[:32]
    small[16:17, :] = lead_row
    state_load.wait()
    centered, scale = mean_and_scale(state[...].astype(F32) + lead_row)
    rows[...] = (centered * scale * columns[0:1] + columns[1:2]).astype(BF16)
    turned[...] = rows[...].T
    stores = [pltpu.make_async_copy(turned, turned_out, io_sems.at[1])]
    stores[0].start()
    wait_all(loads[0] + loads[1])
    for part in range(3):
        span = slice(part * WIDTH, part * WIDTH + WIDTH)
        qkv[:, span] = times(rows[...], weight[:, span]).astype(BF16)
        stores.append(pltpu.make_async_copy(qkv.at[:, span], qkv_out.at[:, span], io_sems.at[2 + part]))
        stores[-1].start()
    wait_all(stores)


def front_forward(where, lead_index, patches, arrays):
    return call(
        front_kernel,
        (where, lead_index, patches, *arrays),
        [SMEM, SMEM, HBM] + [HBM] * 4,
        [
            ((WIDTH, TOKENS), BF16, True),
            ((TOKENS, 3 * WIDTH), BF16, True),
            ((32, WIDTH), F32, False),
        ],
        weight_scratch(WIDTH, 3 * WIDTH)
        + [pltpu.VMEM((WIDTH, 128), BF16), pltpu.SemaphoreType.DMA((16,))]
        + [
            pltpu.VMEM((TOKENS, WIDTH), BF16),
            pltpu.VMEM((TOKENS, WIDTH), BF16),
            pltpu.VMEM((WIDTH, TOKENS), BF16),
            pltpu.VMEM((TOKENS, 3 * WIDTH), BF16),
            pltpu.SemaphoreType.DMA((5,)),
        ],
    )


KEY_SPANS = ((0, 256), (0, 384), (128, 512), (256, 512))


def fill_bias(lengths, pad, bias):
    ends, end = [], 0
    for index in range(lengths.shape[1]):
        end = end + lengths[0, index]
        ends.append(end)

    def windows(places):
        return sum([(places >= end).astype(jnp.int32) for end in ends])

    for block, (low, high) in enumerate(KEY_SPANS):
        count = high - low
        queries = lax.broadcasted_iota(jnp.int32, (1, 128), 1) + 128 * block
        keys = lax.broadcasted_iota(jnp.int32, (count, 1), 0) + low
        same = windows(queries) == windows(keys)
        usable = (pad[low:high, :] > 0) | (queries == keys)
        bias[block, :count, :] = jnp.where(same & usable, 0.0, -1e30)


def two_heads(block):
    first = lax.broadcasted_iota(jnp.int32, block.shape, 1) < block.shape[1] // 2
    zero = jnp.zeros_like(block)
    return jnp.concatenate([jnp.where(first, block, zero), jnp.where(first, zero, block)], axis=0)


def head_rows_of(stacked):
    return jnp.concatenate([stacked[:64, :128], stacked[64:, 128:]], axis=0)


def probabilities(scores, allowed):
    masked = scores * score_scale + allowed
    raised = jnp.exp(masked - jnp.max(masked, axis=0, keepdims=True))
    return raised * (1.0 / jnp.sum(raised, axis=0, keepdims=True))


def attention_kernel(where, lengths, pad, qkv, attended_out, turned_out, bias, turned, rows, sems):
    fill_bias(lengths, pad, bias)

    def pair(index, carry):
        first = index * 128
        columns = pl.ds(pl.multiple_of(first, 128), 128)
        keys_at = pl.ds(pl.multiple_of(first + WIDTH, 128), 128)
        values = qkv[:, pl.ds(pl.multiple_of(first + 2 * WIDTH, 128), 128)].T
        for block, (low, high) in enumerate(KEY_SPANS):
            span = slice(128 * block, 128 * block + 128)
            scores = across(qkv[low:high, keys_at], two_heads(qkv[span, columns]))
            allowed = bias[block, : high - low, :]
            probs = [
                probabilities(scores[:, 128 * head : 128 * head + 128], allowed).astype(BF16)
                for head in range(2)
            ]
            mixed = times(values[:, low:high], jnp.concatenate(probs, axis=1))
            turned[columns, span] = head_rows_of(mixed).astype(BF16)
        return carry

    lax.fori_loop(0, WIDTH // 128, pair, 0)
    stores = [pltpu.make_async_copy(turned, turned_out, sems.at[0])]
    stores[0].start()
    rows[...] = turned[...].T
    stores.append(pltpu.make_async_copy(rows, attended_out, sems.at[1]))
    stores[1].start()
    wait_all(stores)


def attention_forward(where, lengths, pad, qkv):
    rows, columns = (TOKENS, WIDTH), (WIDTH, TOKENS)
    return call(
        attention_kernel,
        (where, lengths, pad, qkv),
        [SMEM, SMEM, VMEM, VMEM],
        [(rows, BF16, True), (columns, BF16, True)],
        [
            pltpu.VMEM((4, 384, 128), F32),
            pltpu.VMEM(columns, BF16),
            pltpu.VMEM(rows, BF16),
            pltpu.SemaphoreType.DMA((2,)),
        ],
    )


def gate_shares(logits, cotangent, shares, gate_grad):
    gate_grad[:, 256:] = cotangent[:, 256:GATE]
    first, rest = logits[:, :128], logits[:, 128:256]
    left = lax.broadcasted_iota(jnp.int32, first.shape, 1) < PIX
    third = jnp.where(left, rest, pltpu.roll(rest, PIX, 1))
    largest = jnp.maximum(jnp.maximum(first, pltpu.roll(first, PIX, 1)), third)
    raised, raised_third = jnp.exp(first - largest), jnp.exp(third - largest)
    scale = 1.0 / (raised + pltpu.roll(raised, PIX, 1) + raised_third)
    share, share_third = raised * scale, raised_third * scale
    shares[:, :128] = share
    shares[:, 128:256] = jnp.where(left, share_third, rest)
    pull, other = cotangent[:, :128].astype(F32), cotangent[:, 128:256].astype(F32)
    pull_third = jnp.where(left, other, pltpu.roll(other, PIX, 1))
    weighed = share * pull
    inner = weighed + pltpu.roll(weighed, PIX, 1) + share_third * pull_third
    gate_grad[:, :128] = (share * (pull - inner)).astype(BF16)
    gate_grad[:, 128:256] = jnp.where(left, share_third * (pull_third - inner), other).astype(BF16)


def head_kernel(where, rows, gate_out, bias, *refs):
    sources, outs, scratch = taken(refs, 4, 1)
    (out,) = outs
    weight, sems, inputs, result, io_sems = scratch
    loads = [block_copies(where, "h", sources, HEAD_PART, weight, sems, side) for side in range(2)]
    row_load = pltpu.make_async_copy(rows, inputs, io_sems.at[0])
    gate_load = pltpu.make_async_copy(gate_out, result.at[:, :GATE], io_sems.at[1])
    row_load.start()
    start_all(loads[0])
    start_all(loads[1])
    gate_load.start()
    row_load.wait()
    stores = []

    def store(span):
        stores.append(
            pltpu.make_async_copy(result.at[:, span], out.at[:, span], io_sems.at[2 + len(stores)])
        )
        stores[-1].start()

    for side in range(2):
        wait_all(loads[side])
        for tile in range(4):
            span = lane_columns(where, side, 2048, GATE + tile * 512, 512)
            columns = lane_columns(where, side, 2048, tile * 512, 512)
            result[:, span] = times(inputs[...], weight[:, columns]) + bias[:, span]
            store(span)
    gate_load.wait()
    store(pl.ds(0, GATE))
    wait_all(stores)


def head_forward(where, rows, gate_out, bias, arrays):
    return call(
        head_kernel,
        (where, rows, gate_out, bias, *arrays),
        [SMEM, HBM, HBM, VMEM] + [HBM] * 4,
        [((TOKENS, HEAD), F32, True)],
        weight_scratch(WIDTH, HEAD - GATE)
        + [
            pltpu.VMEM((TOKENS, WIDTH), BF16),
            pltpu.VMEM((TOKENS, HEAD), F32),
            pltpu.SemaphoreType.DMA((11,)),
        ],
        spare=SPARE_VMEM,
    )[0]


def send_lane(where, group, lane, out, sems, side):
    rows = out.shape[1]
    copies = []
    for place in range(16):
        row = pl.multiple_of(where[table_start(group, side) + place] * rows, rows)
        copies.append(
            pltpu.make_async_copy(lane.at[pl.ds(row, rows), :], out.at[place], sems.at[place])
        )
    start_all(copies)
    return copies


def middle_kernel(
    where, small, up_bias, head_bias, attended, patches, cotangent, act_cotangent, attended_turned,
    *refs,
):
    up_sources, down_sources, head_sources, outs, scratch = taken(refs, 4, 4, 4, 15)
    outputs, shares, gate_bias, down_bias, up_bias_sum, terms, mid_grad, out_grad, mixed, *grads = outs
    down_mine, down_theirs, up_mine, up_theirs, head_mine, head_theirs = grads
    out_weight, out_sems, up, up_sems, down, down_sems, scratch = *scratch[:6], scratch[6:]
    head, head_sems, gate_sems, rows, branch, mid, mlp_turned, scratch = *scratch[:7], scratch[7:]
    act, act_turned, slope, turned, pulls, act_pulls, gate_grad, scratch = *scratch[:7], scratch[7:]
    lane, lane_sems, down_lane, down_lane_sems, mixes, more_sems, io_sems = scratch

    def loads(group, sources, part, target, sems, first=0):
        copies = []
        for side in range(2):
            copies += block_copies(where, group, sources, part, target, sems, side, first)
        return copies

    state_loads = [
        pltpu.make_async_copy(attended, rows, io_sems.at[0]),
        pltpu.make_async_copy(patches, branch, io_sems.at[1]),
    ]
    out_loads = loads("u", up_sources, OUT_PART, out_weight, out_sems)
    up_loads = loads("u", up_sources, UP_PART, up, up_sems)
    down_loads = loads("d", down_sources, DOWN_PART, down, down_sems)
    gate_loads = loads("u", up_sources, GATE_PART, head, gate_sems)
    head_loads = loads("h", head_sources, HEAD_PART, head, head_sems, GATE)
    pull_load = pltpu.make_async_copy(cotangent, pulls, io_sems.at[2])
    act_load = pltpu.make_async_copy(act_cotangent, act_pulls, io_sems.at[3])
    mix_load = pltpu.make_async_copy(attended_turned, mixes, io_sems.at[4])
    start_all(state_loads + out_loads + up_loads + down_loads + gate_loads)
    pull_load.start()
    start_all(head_loads)
    act_load.start()
    mix_load.start()

    wait_all(state_loads + out_loads)
    mid[...] = (
        branch[...].astype(F32)
        + small[16:17, :]
        + times(rows[...], out_weight[...])
        + small[2:3, :]
    )
    centered, scale = mean_and_scale(mid[...])
    rows[...] = (centered * scale * small[3:4, :] + small[4:5, :]).astype(BF16)
    mlp_turned[...] = rows[...].T
    wait_all(up_loads)
    for tile in range(6):
        span = slice(tile * 512, tile * 512 + 512)
        values = times(rows[...], up[:, span]) + up_bias[:, span]
        share = 0.5 * (1.0 + lax.erf(values * 0.7071067811865476))
        density = jnp.exp(-0.5 * values * values) * 0.3989422804014327
        activated = (values * share).astype(BF16)
        act[:, span] = activated
        act_turned[span, :] = activated.T
        slope[:, span] = (share + values * density).astype(BF16)
    wait_all(down_loads)
    outputs[...] = (mid[...] + times(act[...], down[...]) + small[5:6, :]).astype(BF16)
    turned[...] = outputs[...].T
    wait_all(gate_loads)
    shares[...] = times(outputs[...], head[:, :GATE]) + head_bias[:, :GATE]
    pull_load.wait()
    gate_shares(shares, pulls, shares, gate_grad)
    gate_bias[...] = jnp.sum(gate_grad[...].astype(F32), axis=0, keepdims=True)
    pulls[:, :GATE] = gate_grad[...]

    def head_lane(side, target, sems, out):
        target[:, :256] = times(turned[...], pulls[:, lane_columns(where, side, 256)]).astype(BF16)
        for tile in range(4):
            span = lane_columns(where, side, 2048, GATE + tile * 512, 512)
            target[:, 256 + tile * 512 : 768 + tile * 512] = times(turned[...], pulls[:, span]).astype(
                BF16
            )
        return send_lane(where, "head", target, out, sems, side)

    def down_lane_of(side, out):
        columns = branch[:, lane_columns(where, side, 384)]
        for part in range(4):
            span = slice(part * WIDTH, part * WIDTH + WIDTH)
            down_lane[span, :] = times(act_turned[span, :], columns).astype(BF16)
        return send_lane(where, "down", down_lane, out, down_lane_sems, side)

    def up_lane(side, target, sems, out):
        for tile in range(3):
            span = lane_columns(where, side, 1536, tile * 512, 512)
            target[:, tile * 512 : tile * 512 + 512] = times(mlp_turned[...], slope[:, span]).astype(
                BF16
            )
        target[:, 1536:1920] = times(
            mixes[...], out_grad[:, lane_columns(where, side, 384)]
        ).astype(BF16)
        return send_lane(where, "up", target, out, sems, side)

    first_stores = head_lane(1, lane, lane_sems, head_theirs)
    act_load.wait()
    wait_all(head_loads)
    mid_grad[...] = act_pulls[...].astype(F32) + across(pulls[...], head[...])
    branch[...] = mid_grad[...].astype(BF16)
    down_bias[...] = jnp.sum(branch[...].astype(F32), axis=0, keepdims=True)
    stores = head_lane(0, head.at[:, :2304], more_sems.at[0], head_mine)
    down_stores = down_lane_of(1, down_theirs)
    for tile in range(6):
        span = slice(tile * 512, tile * 512 + 512)
        grad = across(branch[...], down[span, :])
        rounded = (slope[:, span].astype(F32) * grad).astype(BF16)
        slope[:, span] = rounded
        up_bias_sum[:, span] = jnp.sum(rounded.astype(F32), axis=0, keepdims=True)
    wait_all(down_stores)
    stores += down_lane_of(0, down_mine)
    grad = across(slope[...], up[...])
    pulled, gain_grad, shift_grad = norm_backward(mid[...], small[3:4, :], grad)
    pulled = pulled + mid_grad[...]
    rounded = pulled.astype(BF16)
    mid_grad[...] = pulled
    out_grad[...] = rounded
    terms[...] = jnp.zeros_like(terms)
    terms[0:1, :] = jnp.sum(rounded.astype(F32), axis=0, keepdims=True)
    terms[1:2, :] = gain_grad
    terms[2:3, :] = shift_grad
    mix_load.wait()
    stores += up_lane(1, head.at[:, 2304:4224], more_sems.at[1], up_theirs)
    wait_all(first_stores)
    stores += up_lane(0, lane.at[:, :1920], lane_sems, up_mine)
    mixed[...] = across(out_grad[...], out_weight[...]).astype(BF16)
    wait_all(stores)


def middle(
    where, small, up_bias, head_bias, attended, patches, cotangent, act_cotangent, attended_turned,
    up, down, head,
):
    rows, columns = (TOKENS, WIDTH), (WIDTH, TOKENS)
    wide, tall = (TOKENS, HIDDEN), (HIDDEN, TOKENS)
    return call(
        middle_kernel,
        (
            where, small, up_bias, head_bias, attended, patches, cotangent, act_cotangent,
            attended_turned, *up, *down, *head,
        ),
        [SMEM, VMEM, VMEM, VMEM] + [HBM] * 17,
        [
            (rows, BF16, False),
            ((TOKENS, GATE), F32, False),
            ((1, GATE), F32, False),
            ((1, WIDTH), F32, False),
            ((1, HIDDEN), F32, False),
            ((8, WIDTH), F32, False),
            (rows, F32, False),
            (rows, BF16, False),
            (rows, BF16, False),
            ((16, 192, 384), BF16, True),
            ((16, 192, 384), BF16, True),
            ((16, 48, 1920), BF16, True),
            ((16, 48, 1920), BF16, True),
            ((16, 48, 2304), BF16, True),
            ((16, 48, 2304), BF16, True),
        ],
        weight_scratch(WIDTH, WIDTH)
        + weight_scratch(WIDTH, HIDDEN)
        + weight_scratch(HIDDEN, WIDTH)
        + weight_scratch(WIDTH, HEAD)
        + [
            pltpu.SemaphoreType.DMA((2, 16)),
            pltpu.VMEM(rows, BF16),
            pltpu.VMEM(rows, BF16),
            pltpu.VMEM(rows, F32),
            pltpu.VMEM(columns, BF16),
            pltpu.VMEM(wide, BF16),
            pltpu.VMEM(tall, BF16),
            pltpu.VMEM(wide, BF16),
            pltpu.VMEM(columns, BF16),
            pltpu.VMEM((TOKENS, HEAD), BF16),
            pltpu.VMEM(rows, BF16),
            pltpu.VMEM((TOKENS, GATE), BF16),
            pltpu.VMEM((WIDTH, 2304), BF16),
            pltpu.SemaphoreType.DMA((16,)),
            pltpu.VMEM((HIDDEN, 384), BF16),
            pltpu.SemaphoreType.DMA((16,)),
            pltpu.VMEM(columns, BF16),
            pltpu.SemaphoreType.DMA((2, 16)),
            pltpu.SemaphoreType.DMA((5,)),
        ],
    )


def attend_back(count, qkv, mixed, bias, turned, key_sum, value_sum, qkv_grad):
    width = 128 * count

    def columns_at(first):
        return pl.ds(pl.multiple_of(first, 128), 128)

    def pair(index, carry):
        own = index * 128
        columns, keys_at = columns_at(own), columns_at(own + width)
        values_at = columns_at(own + 2 * width)
        keys_turned = qkv[:, keys_at].T
        key_sum[...] = jnp.zeros_like(key_sum)
        value_sum[...] = jnp.zeros_like(value_sum)
        for block, (low, high) in enumerate(KEY_SPANS):
            span = slice(128 * block, 128 * block + 128)
            queries, grads = two_heads(qkv[span, columns]), two_heads(mixed[span, columns])
            scores = across(qkv[low:high, keys_at], queries)
            prob_grads = across(qkv[low:high, values_at], grads)
            allowed = bias[block, : high - low, :]
            probs, score_grads = [], []
            for head in range(2):
                part = slice(128 * head, 128 * head + 128)
                prob = probabilities(scores[:, part], allowed)
                pulled = prob * prob_grads[:, part]
                inner = jnp.sum(pulled, axis=0, keepdims=True)
                probs.append(prob.astype(BF16))
                score_grads.append((pulled - prob * inner).astype(BF16))
            score_grad = jnp.concatenate(score_grads, axis=1)
            key_sum[low:high, :] += times(score_grad, queries)
            value_sum[low:high, :] += times(jnp.concatenate(probs, axis=1), grads)
            turned[:, span] = head_rows_of(times(keys_turned[:, low:high], score_grad)) * score_scale
        qkv_grad[:, columns] = turned[...].T.astype(BF16)
        qkv_grad[:, keys_at] = (key_sum[...] * score_scale).astype(BF16)
        qkv_grad[:, values_at] = value_sum[...].astype(BF16)
        return carry

    lax.fori_loop(0, count, pair, 0)


def attention_scratch(count):
    return [
        pltpu.VMEM((4, 384, 128), F32),
        pltpu.VMEM((TOKENS, 384 * count), BF16),
        pltpu.VMEM((TOKENS, 128 * count), BF16),
        pltpu.VMEM((128, TOKENS), F32),
        pltpu.VMEM((TOKENS, 128), F32),
        pltpu.VMEM((TOKENS, 128), F32),
        pltpu.SemaphoreType.DMA((4,)),
    ]


def attention_loads(start, count, qkv, mixed, own_qkv, own_mixed, sems):
    width = 128 * count
    copies = [
        pltpu.make_async_copy(
            mixed.at[:, pl.ds(128 * start, width)], own_mixed.at[:, pl.ds(0, width)], sems.at[3]
        )
    ]
    for part in range(3):
        copies.append(
            pltpu.make_async_copy(
                qkv.at[:, pl.ds(WIDTH * part + 128 * start, width)],
                own_qkv.at[:, pl.ds(width * part, width)],
                sems.at[part],
            )
        )
    return copies


def early_back_kernel(where, lengths, pad, mixed, qkv, input_turned, *refs):
    (qkv_grad, mine_out, theirs_out), scratch = taken(refs, 3)
    bias, own_qkv, own_mixed, turned, key_sum, value_sum, sems, scratch = *scratch[:7], scratch[7:]
    lane, lane_sems, inputs, io_sems = scratch
    loads = attention_loads(0, 4, qkv, mixed, own_qkv, own_mixed, sems)
    in_load = pltpu.make_async_copy(input_turned, inputs, io_sems.at[0])
    start_all(loads + [in_load])
    fill_bias(lengths, pad, bias)
    wait_all(loads)
    attend_back(4, own_qkv, own_mixed, bias, turned, key_sum, value_sum, qkv_grad)
    in_load.wait()
    stores = []
    for side, out in ((1, theirs_out), (0, mine_out)):
        lane[side] = times(inputs[...], qkv_grad[:, lane_columns(where, side, 768)]).astype(BF16)
        stores += send_lane(where, "front", lane.at[side], out, lane_sems.at[side], side)
    wait_all(stores)


def early_backward(where, lengths, pad, mixed, qkv, input_turned):
    return call(
        early_back_kernel,
        (where, lengths, pad, mixed, qkv, input_turned),
        [SMEM, SMEM, VMEM] + [HBM] * 3,
        [
            ((TOKENS, 1536), BF16, False),
            ((16, 48, 768), BF16, True),
            ((16, 48, 768), BF16, True),
        ],
        attention_scratch(4)
        + lane_scratch(WIDTH, 768)
        + [pltpu.VMEM((WIDTH, TOKENS), BF16), pltpu.SemaphoreType.DMA((1,))],
    )


def late_back_kernel(
    where, lead, lengths, pad, small, terms, down_row, up_rows, head_rows,
    mixed, qkv, first_grad, patches, mid_grad, input_turned, *refs
):
    sources, (patch_out, mine_out, theirs_out), scratch = taken(refs, 4, 3)
    bias, own_qkv, own_mixed, turned, key_sum, value_sum, sems, scratch = *scratch[:7], scratch[7:]
    weight, weight_sems, lane, lane_sems, pulls, late_pulls, scratch = *scratch[:6], scratch[6:]
    state, mids, inputs, patch_grad, small_grad, io_sems = scratch
    own_loads = attention_loads(4, 2, qkv, mixed, own_qkv, own_mixed, sems)
    loads = [
        block_copies(where, "q", sources, QKV_PART, weight, weight_sems, side) for side in range(2)
    ]
    pairs = [(patches, state), (mid_grad, mids), (input_turned, inputs)]
    for part in range(3):
        target = pulls.at[:, pl.ds(WIDTH * part, 512)]
        pairs.append((first_grad.at[:, pl.ds(512 * part, 512)], target))
    in_loads = [pltpu.make_async_copy(*pair, io_sems.at[at]) for at, pair in enumerate(pairs)]
    start_all(own_loads + loads[0] + loads[1] + in_loads)
    fill_bias(lengths, pad, bias)
    wait_all(own_loads)
    attend_back(2, own_qkv, own_mixed, bias, turned, key_sum, value_sum, late_pulls)
    wait_all(loads[0] + loads[1] + in_loads)
    for part in range(3):
        pulls[:, WIDTH * part + 512 : WIDTH * part + 768] = late_pulls[
            :, 256 * part : 256 * part + 256
        ]
    grad = across(pulls[...], weight[...])
    pulled, gain_grad, shift_grad = norm_backward(
        state[...].astype(F32) + small[16:17, :], small[0:1, :], grad
    )
    pulled = pulled + mids[...]
    patch_grad[...] = pulled
    stores = [pltpu.make_async_copy(patch_grad, patch_out, io_sems.at[6])]
    stores[0].start()
    small_grad[0:1, :] = gain_grad
    small_grad[1:2, :] = shift_grad
    small_grad[2:5, :] = terms[0:3, :]
    small_grad[5:6, :] = down_row[...]
    small_grad[6:10, :] = up_rows[...]
    small_grad[10:16, :] = head_rows[...]
    places = lax.broadcasted_iota(jnp.int32, (LEADS, WIDTH), 0)
    lead_grad = jnp.sum(pulled, axis=0, keepdims=True)
    small_grad[16:32, :] = jnp.where(places == lead[0], lead_grad, 0.0)
    for side, out in ((1, theirs_out), (0, mine_out)):
        lane[side, :, :384] = times(
            inputs[...], late_pulls[:, lane_columns(where, side, 384)]
        ).astype(BF16)
        rows = small_grad[pl.ds(pl.multiple_of((where[0] ^ side) * 16, 16), 16), :]
        rows = jnp.concatenate([rows, jnp.zeros((112, WIDTH), F32)], axis=0)
        lane[side, :, 384:] = rows.T.astype(BF16)
        stores += send_lane(where, "front", lane.at[side], out, lane_sems.at[side], side)
    wait_all(stores)


def late_backward(
    where, lead, lengths, pad, small, terms, down_row, up_rows, head_rows,
    mixed, qkv, first_grad, patches, mid_grad, input_turned, arrays,
):
    rows, columns = (TOKENS, WIDTH), (WIDTH, TOKENS)
    return call(
        late_back_kernel,
        (
            where, lead, lengths, pad, small, terms, down_row, up_rows, head_rows,
            mixed, qkv, first_grad, patches, mid_grad, input_turned, *arrays,
        ),
        [SMEM, SMEM, SMEM] + [VMEM] * 6 + [HBM] * 10,
        [(rows, F32, True), ((16, 48, 512), BF16, True), ((16, 48, 512), BF16, True)],
        attention_scratch(2)
        + weight_scratch(WIDTH, 3 * WIDTH)
        + lane_scratch(WIDTH, 512)
        + [
            pltpu.VMEM((TOKENS, 3 * WIDTH), BF16),
            pltpu.VMEM((TOKENS, WIDTH), BF16),
            pltpu.VMEM(rows, BF16),
            pltpu.VMEM(rows, F32),
            pltpu.VMEM(columns, BF16),
            pltpu.VMEM(rows, F32),
            pltpu.VMEM((32, WIDTH), F32),
            pltpu.SemaphoreType.DMA((7,)),
        ],
    )


def rows_of(vector, count):
    return vector.reshape(32, count, 24).transpose(1, 0, 2).reshape(count, WIDTH)


def vector_of(rows):
    count = rows.shape[0]
    return rows.reshape(count, 32, 24).transpose(1, 0, 2).reshape(1, count * WIDTH)


def shards(
    patches,
    lead_index,
    window_lengths,
    pad_mask,
    lead_table,
    attn_gain,
    attn_shift,
    qkv_weight,
    out_weight,
    out_bias,
    mlp_gain,
    mlp_shift,
    up_weight,
    up_bias,
    down_weight,
    down_bias,
    head_weight,
    head_bias,
    act_cotangent,
    head_cotangent,
):
    core, where = whereabouts()
    weights = (qkv_weight, out_weight, up_weight, down_weight, head_weight)
    vectors = (
        attn_gain, attn_shift, out_bias, mlp_gain, mlp_shift, down_bias, up_bias, head_bias
    )
    parts = packed(core, weights, lead_table, vectors)
    pad = pad_mask[:, None]
    cotangent_sum = jnp.sum(head_cotangent[:, GATE:].astype(F32), axis=0, keepdims=True)

    orders = ORDERS
    parts = dict(zip("qudh", zip(parts[:4], parts[4:])))
    chunks = {
        name: in_core_order(core, mine, exchange(theirs, SIBLING), 0)[None]
        for name, (mine, theirs) in parts.items()
    }

    held, last = dict(chunks), ()
    for name, step in GATHER_SEQUENCE:
        held[name] = after(held[name], *last)
        last = (held[name],)
        held[name] = doubled(held[name], orders[name][step])
    q, u, d, h = [held[name] for name in ("q", "u", "d", "h")]
    q_rest = exchange(after(q, *last), orders["q"][3])
    u = after(u, q)
    u_rest = exchange(u, orders["u"][3])
    d_rest = exchange(d, orders["d"][3])
    h = doubled(after(h, u), orders["h"][2])
    first = both_lanes(q, q_rest)
    h_rest = exchange(h, orders["h"][3])
    input_turned, qkv, small_rows = front_forward(
        after(where, d, h, cotangent_sum), lead_index, patches, first
    )
    attended, attended_turned = attention_forward(where, window_lengths, pad, qkv)
    u_rest, d_rest, h_rest = lax.optimization_barrier((u_rest, d_rest, h_rest, attended))[:3]
    second, down, head = both_lanes(u, u_rest), both_lanes(d, d_rest), both_lanes(h, h_rest)
    up_bias_row, head_bias_row = vector_of(small_rows[6:10]), vector_of(small_rows[10:16])
    (
        outputs, gate_out, gate_bias_sum, down_bias_sum, up_bias_sum, terms, mid_grad, _, mixed_grad,
        mine_d, theirs_d, mine_u, theirs_u, mine_h, theirs_h,
    ) = middle(
        where, small_rows, up_bias_row, head_bias_row, attended, patches, head_cotangent,
        act_cotangent, attended_turned, second, down, head,
    )

    got_h, got_d, got_u = [exchange(theirs, SIBLING) for theirs in (theirs_h, theirs_d, theirs_u)]
    head_rows = rows_of(jnp.concatenate([gate_bias_sum, cotangent_sum], axis=1), 6)
    up_rows = rows_of(up_bias_sum, 4)
    first_grad, mine_m, theirs_m = early_backward(
        where, window_lengths, pad, mixed_grad, qkv, input_turned
    )
    groups = {
        "head": [[mine_h], after(got_h, first_grad), 4],
        "up": [[mine_u], after(got_u, first_grad), 4],
        "down": [[mine_d], after(got_d, first_grad), 4],
        "mix": [[mine_m], exchange(theirs_m, SIBLING), 4],
    }
    last = ()

    def add(name):
        nonlocal last
        keep, got, step = groups[name]
        keep, send = folded(keep, after(got, *last))
        last = (send,)
        groups[name] = [keep, exchange(send, orders[name][step - 1]), step - 1]

    def finish(name, widths):
        keep, got, _ = groups[name]
        return finished(keep, after(got, *last), core, widths)

    for name in ("head", "up", "down"):
        add(name)
    patch_grad, mine_f, theirs_f = late_backward(
        after(where, *last), lead_index, window_lengths, pad, small_rows, terms, down_bias_sum,
        up_rows, head_rows, mixed_grad, qkv, first_grad, patches, mid_grad, input_turned, first,
    )
    last = (patch_grad,)
    groups["front"] = [[mine_f], exchange(theirs_f, SIBLING), 4]
    for name in ("head", "down", "mix", "front", "up"):
        add(name)
    head_out = head_forward(after(where, *last), outputs, gate_out, head_bias_row, head)
    last = (head_out,)
    for name in ("head", "down", "front", "mix", "up", "head"):
        add(name)
    gate_sum, rest_sum = finish("head", (256, 2048))
    for name in ("down", "front", "mix", "up", "front", "mix"):
        add(name)
    up_sum, out_sum = finish("up", (1536, 384))
    (down_sum,) = finish("down", (384,))
    (early_sum,) = finish("mix", (768,))
    late_sum, small_sum = finish("front", (384, 128))
    qkv_sum = jnp.concatenate(
        [
            piece[:, part * piece.shape[1] // 3 : (part + 1) * piece.shape[1] // 3]
            for part in range(3)
            for piece in (early_sum, late_sum)
        ],
        axis=1,
    )
    small_sum = small_sum.T
    return (
        outputs,
        head_out,
        patch_grad,
        small_sum[128:144],
        small_sum[0],
        small_sum[1],
        qkv_sum,
        out_sum,
        small_sum[2],
        small_sum[3],
        small_sum[4],
        up_sum,
        small_sum[6:10].reshape(96),
        down_sum,
        small_sum[5],
        jnp.concatenate([gate_sum, rest_sum], axis=1),
        small_sum[10:16].reshape(144),
    )


def plain_shards(
    patches,
    lead_index,
    window_lengths,
    pad_mask,
    lead_table,
    attn_gain,
    attn_shift,
    qkv_weight,
    out_weight,
    out_bias,
    mlp_gain,
    mlp_shift,
    up_weight,
    up_bias,
    down_weight,
    down_bias,
    head_weight,
    head_bias,
    act_cotangent,
    head_cotangent,
):
    front = (
        lax.all_gather(lead_table, ("dp", "fsdp"), axis=1, tiled=True),
        lax.all_gather(attn_gain, ("dp", "fsdp"), axis=0, tiled=True),
        lax.all_gather(attn_shift, ("dp", "fsdp"), axis=0, tiled=True),
        lax.all_gather(qkv_weight, ("dp", "fsdp"), axis=0, tiled=True),
        lax.all_gather(out_weight, ("dp", "fsdp"), axis=0, tiled=True),
        lax.all_gather(out_bias, ("dp", "fsdp"), axis=0, tiled=True),
    )
    rear = (
        lax.all_gather(mlp_gain, ("dp", "fsdp"), axis=0, tiled=True),
        lax.all_gather(mlp_shift, ("dp", "fsdp"), axis=0, tiled=True),
        lax.all_gather(up_weight, ("dp", "fsdp"), axis=0, tiled=True),
        lax.all_gather(up_bias, ("dp", "fsdp"), axis=0, tiled=True),
        lax.all_gather(down_weight, ("dp", "fsdp"), axis=0, tiled=True),
        lax.all_gather(down_bias, ("dp", "fsdp"), axis=0, tiled=True),
        lax.all_gather(head_weight, ("dp", "fsdp"), axis=0, tiled=True),
        lax.all_gather(head_bias, ("dp", "fsdp"), axis=0, tiled=True),
    )
    table_full, gain_one, shift_one, qkv_full, out_full, out_bias_full = front
    (
        gain_two,
        shift_two,
        up_full,
        up_bias_full,
        down_full,
        down_bias_full,
        head_full,
        head_bias_full,
    ) = rear
    token_rows, width = patches.shape
    head_dim = width // HEADS
    block_rows = min(512, token_rows)
    block_count = token_rows // block_rows
    ends = jnp.cumsum(window_lengths[0])
    positions = jnp.arange(token_rows, dtype=jnp.int32)
    window = jnp.sum((positions[:, None] >= ends[None, :]).astype(jnp.int32), axis=1)
    lead_hot = (jnp.arange(LEADS, dtype=jnp.int32) == lead_index[0]).astype(jnp.float32)
    lead_row = jnp.sum(lead_hot[:, None] * table_full.astype(jnp.float32), axis=0)
    start_state = patches.astype(jnp.float32) + lead_row[None, :]
    normed_one, pull_one = jax.vjp(
        layer_norm, start_state, gain_one.astype(jnp.float32), shift_one.astype(jnp.float32)
    )
    attn_input = normed_one.astype(jnp.bfloat16)
    qkv_rows = jnp.dot(attn_input, qkv_full, preferred_element_type=jnp.float32).astype(
        jnp.bfloat16
    )
    queries = qkv_rows[:, :width].reshape(block_count, block_rows, HEADS, head_dim)
    keys = qkv_rows[:, width : 2 * width].reshape(token_rows, HEADS, head_dim)
    values = qkv_rows[:, 2 * width :].reshape(token_rows, HEADS, head_dim)
    query_windows = window.reshape(block_count, block_rows)
    block_starts = jnp.arange(block_count, dtype=jnp.int32) * block_rows

    def block_scores(query_block, window_block, block_start):
        scores = (
            jnp.einsum("qhd,khd->hqk", query_block, keys, preferred_element_type=jnp.float32)
            * score_scale
        )
        allowed = allowed_keys(window_block, window, pad_mask, block_start)
        return jnp.where(allowed[None], scores, -1e30)

    def forward_block(inputs):
        query_block, window_block, block_start = inputs
        masked = block_scores(query_block, window_block, block_start)
        largest = jnp.max(masked, axis=-1, keepdims=True)
        raised = jnp.exp(masked - largest)
        total = jnp.sum(raised, axis=-1, keepdims=True)
        probs = (raised / total).astype(jnp.bfloat16)
        mixed = jnp.einsum("hqk,khd->qhd", probs, values, preferred_element_type=jnp.float32)
        return (
            mixed.reshape(block_rows, width).astype(jnp.bfloat16),
            (largest + jnp.log(total))[:, :, 0],
        )

    mixed_blocks, log_totals = lax.map(forward_block, (queries, query_windows, block_starts))
    attended = mixed_blocks.reshape(token_rows, width)
    mid_state = (
        start_state
        + jnp.dot(attended, out_full, preferred_element_type=jnp.float32)
        + out_bias_full.astype(jnp.float32)
    )
    normed_two, pull_two = jax.vjp(
        layer_norm, mid_state, gain_two.astype(jnp.float32), shift_two.astype(jnp.float32)
    )
    mlp_input = normed_two.astype(jnp.bfloat16)
    pre_act = jnp.dot(mlp_input, up_full, preferred_element_type=jnp.float32) + up_bias_full.astype(
        jnp.float32
    )
    activated, pull_act = jax.vjp(gelu_exact, pre_act)
    act_rows = activated.astype(jnp.bfloat16)
    end_state = (
        mid_state
        + jnp.dot(act_rows, down_full, preferred_element_type=jnp.float32)
        + down_bias_full.astype(jnp.float32)
    )
    outputs = end_state.astype(jnp.bfloat16)
    logits = jnp.dot(
        outputs, head_full, preferred_element_type=jnp.float32
    ) + head_bias_full.astype(jnp.float32)
    head_out, pull_head = jax.vjp(partial(expert_softmax, experts=EXPERTS, pixels=PIX), logits)
    up_back, down_back, head_back = (
        lax.all_gather(up_weight, ("dp", "fsdp"), axis=0, tiled=True),
        lax.all_gather(down_weight, ("dp", "fsdp"), axis=0, tiled=True),
        lax.all_gather(head_weight, ("dp", "fsdp"), axis=0, tiled=True),
    )
    qkv_back, out_back = (
        lax.all_gather(qkv_weight, ("dp", "fsdp"), axis=0, tiled=True),
        lax.all_gather(out_weight, ("dp", "fsdp"), axis=0, tiled=True),
    )
    logit_grad = pull_head(head_cotangent.astype(jnp.float32))[0].astype(jnp.bfloat16)
    head_bias_term = jnp.sum(logit_grad.astype(jnp.float32), axis=0)
    head_term = jnp.einsum("td,tn->dn", outputs, logit_grad, preferred_element_type=jnp.float32)
    end_grad = act_cotangent.astype(jnp.float32) + jnp.einsum(
        "tn,dn->td", logit_grad, head_back, preferred_element_type=jnp.float32
    )
    branch_grad = end_grad.astype(jnp.bfloat16)
    down_bias_term = jnp.sum(branch_grad.astype(jnp.float32), axis=0)
    down_term = jnp.einsum("tf,td->fd", act_rows, branch_grad, preferred_element_type=jnp.float32)
    act_grad = jnp.einsum("td,fd->tf", branch_grad, down_back, preferred_element_type=jnp.float32)
    pre_grad = pull_act(act_grad)[0].astype(jnp.bfloat16)
    up_bias_term = jnp.sum(pre_grad.astype(jnp.float32), axis=0)
    up_term = jnp.einsum("td,tf->df", mlp_input, pre_grad, preferred_element_type=jnp.float32)
    normed_two_grad = jnp.einsum("tf,df->td", pre_grad, up_back, preferred_element_type=jnp.float32)
    state_grad_two, gain_two_term, shift_two_term = pull_two(normed_two_grad)
    (
        gain_part,
        shift_part,
        up_part,
        up_bias_part,
        down_part,
        down_bias_part,
        head_part,
        head_bias_part,
    ) = (
        lax.psum_scatter(
            gain_two_term.astype(jnp.bfloat16), "dp", scatter_dimension=0, tiled=True
        ).astype(jnp.float32),
        lax.psum_scatter(
            shift_two_term.astype(jnp.bfloat16), "dp", scatter_dimension=0, tiled=True
        ).astype(jnp.float32),
        lax.psum_scatter(
            up_term.astype(jnp.bfloat16), "dp", scatter_dimension=0, tiled=True
        ).astype(jnp.float32),
        lax.psum_scatter(
            up_bias_term.astype(jnp.bfloat16), "dp", scatter_dimension=0, tiled=True
        ).astype(jnp.float32),
        lax.psum_scatter(
            down_term.astype(jnp.bfloat16), "dp", scatter_dimension=0, tiled=True
        ).astype(jnp.float32),
        lax.psum_scatter(
            down_bias_term.astype(jnp.bfloat16), "dp", scatter_dimension=0, tiled=True
        ).astype(jnp.float32),
        lax.psum_scatter(
            head_term.astype(jnp.bfloat16), "dp", scatter_dimension=0, tiled=True
        ).astype(jnp.float32),
        lax.psum_scatter(
            head_bias_term.astype(jnp.bfloat16), "dp", scatter_dimension=0, tiled=True
        ).astype(jnp.float32),
    )
    rear_grads = (
        lax.psum_scatter(gain_part, "fsdp", scatter_dimension=0, tiled=True),
        lax.psum_scatter(shift_part, "fsdp", scatter_dimension=0, tiled=True),
        lax.psum_scatter(up_part, "fsdp", scatter_dimension=0, tiled=True),
        lax.psum_scatter(up_bias_part, "fsdp", scatter_dimension=0, tiled=True),
        lax.psum_scatter(down_part, "fsdp", scatter_dimension=0, tiled=True),
        lax.psum_scatter(down_bias_part, "fsdp", scatter_dimension=0, tiled=True),
        lax.psum_scatter(head_part, "fsdp", scatter_dimension=0, tiled=True),
        lax.psum_scatter(head_bias_part, "fsdp", scatter_dimension=0, tiled=True),
    )
    mid_grad = end_grad + state_grad_two
    out_grad = mid_grad.astype(jnp.bfloat16)
    out_bias_term = jnp.sum(out_grad.astype(jnp.float32), axis=0)
    out_term = jnp.einsum("td,te->de", attended, out_grad, preferred_element_type=jnp.float32)
    mixed_grad = jnp.einsum(
        "te,de->td", out_grad, out_back, preferred_element_type=jnp.float32
    ).astype(jnp.bfloat16)
    grad_blocks = mixed_grad.reshape(block_count, block_rows, HEADS, head_dim)

    def backward_block(carry, inputs):
        key_sum, value_sum = carry
        query_block, grad_block, window_block, total_block, block_start = inputs
        masked = block_scores(query_block, window_block, block_start)
        probs = jnp.exp(masked - total_block[:, :, None])
        prob_grad = jnp.einsum(
            "qhd,khd->hqk", grad_block, values, preferred_element_type=jnp.float32
        )
        inner = jnp.sum(probs * prob_grad, axis=-1, keepdims=True)
        score_grad = (probs * (prob_grad - inner)).astype(jnp.bfloat16)
        query_grad = (
            jnp.einsum("hqk,khd->qhd", score_grad, keys, preferred_element_type=jnp.float32)
            * score_scale
        )
        key_sum = (
            key_sum
            + jnp.einsum(
                "hqk,qhd->khd", score_grad, query_block, preferred_element_type=jnp.float32
            )
            * score_scale
        )
        value_sum = value_sum + jnp.einsum(
            "hqk,qhd->khd",
            probs.astype(jnp.bfloat16),
            grad_block,
            preferred_element_type=jnp.float32,
        )
        return ((key_sum, value_sum), query_grad.reshape(block_rows, width))

    zero_keys = jnp.zeros((token_rows, HEADS, head_dim), jnp.float32)
    (key_grad, value_grad), query_grads = lax.scan(
        backward_block,
        (zero_keys, zero_keys),
        (queries, grad_blocks, query_windows, log_totals, block_starts),
    )
    qkv_grad = jnp.concatenate(
        [
            query_grads.reshape(token_rows, width),
            key_grad.reshape(token_rows, width),
            value_grad.reshape(token_rows, width),
        ],
        axis=1,
    ).astype(jnp.bfloat16)
    qkv_term = jnp.einsum("td,te->de", attn_input, qkv_grad, preferred_element_type=jnp.float32)
    normed_one_grad = jnp.einsum(
        "te,de->td", qkv_grad, qkv_back, preferred_element_type=jnp.float32
    )
    state_grad_one, gain_one_term, shift_one_term = pull_one(normed_one_grad)
    patch_grad = mid_grad + state_grad_one
    lead_term = lead_hot[:, None] * jnp.sum(patch_grad, axis=0)[None, :]
    lead_part, gain_one_part, shift_one_part, qkv_part, out_part, out_bias_part = (
        lax.psum_scatter(
            lead_term.astype(jnp.bfloat16), "dp", scatter_dimension=1, tiled=True
        ).astype(jnp.float32),
        lax.psum_scatter(
            gain_one_term.astype(jnp.bfloat16), "dp", scatter_dimension=0, tiled=True
        ).astype(jnp.float32),
        lax.psum_scatter(
            shift_one_term.astype(jnp.bfloat16), "dp", scatter_dimension=0, tiled=True
        ).astype(jnp.float32),
        lax.psum_scatter(
            qkv_term.astype(jnp.bfloat16), "dp", scatter_dimension=0, tiled=True
        ).astype(jnp.float32),
        lax.psum_scatter(
            out_term.astype(jnp.bfloat16), "dp", scatter_dimension=0, tiled=True
        ).astype(jnp.float32),
        lax.psum_scatter(
            out_bias_term.astype(jnp.bfloat16), "dp", scatter_dimension=0, tiled=True
        ).astype(jnp.float32),
    )
    front_grads = (
        lax.psum_scatter(lead_part, "fsdp", scatter_dimension=1, tiled=True),
        lax.psum_scatter(gain_one_part, "fsdp", scatter_dimension=0, tiled=True),
        lax.psum_scatter(shift_one_part, "fsdp", scatter_dimension=0, tiled=True),
        lax.psum_scatter(qkv_part, "fsdp", scatter_dimension=0, tiled=True),
        lax.psum_scatter(out_part, "fsdp", scatter_dimension=0, tiled=True),
        lax.psum_scatter(out_bias_part, "fsdp", scatter_dimension=0, tiled=True),
    )
    return (
        outputs,
        head_out,
        patch_grad,
        front_grads[0],
        front_grads[1],
        front_grads[2],
        front_grads[3],
        front_grads[4],
        front_grads[5],
        rear_grads[0],
        rear_grads[1],
        rear_grads[2],
        rear_grads[3],
        rear_grads[4],
        rear_grads[5],
        rear_grads[6],
        rear_grads[7],
    )


def solution(mesh):
    in_specs = (
        P(("dp", "fsdp"), None),
        P(("dp", "fsdp")),
        P(("dp", "fsdp"), None),
        P(("dp", "fsdp")),
        P(None, ("dp", "fsdp")),
        P(("dp", "fsdp")),
        P(("dp", "fsdp")),
        P(("dp", "fsdp"), None),
        P(("dp", "fsdp"), None),
        P(("dp", "fsdp")),
        P(("dp", "fsdp")),
        P(("dp", "fsdp")),
        P(("dp", "fsdp"), None),
        P(("dp", "fsdp")),
        P(("dp", "fsdp"), None),
        P(("dp", "fsdp")),
        P(("dp", "fsdp"), None),
        P(("dp", "fsdp")),
        P(("dp", "fsdp"), None),
        P(("dp", "fsdp"), None),
    )
    out_specs = (
        P(("dp", "fsdp"), None),
        P(("dp", "fsdp"), None),
        P(("dp", "fsdp"), None),
        P(None, ("dp", "fsdp")),
        P(("dp", "fsdp")),
        P(("dp", "fsdp")),
        P(("dp", "fsdp"), None),
        P(("dp", "fsdp"), None),
        P(("dp", "fsdp")),
        P(("dp", "fsdp")),
        P(("dp", "fsdp")),
        P(("dp", "fsdp"), None),
        P(("dp", "fsdp")),
        P(("dp", "fsdp"), None),
        P(("dp", "fsdp")),
        P(("dp", "fsdp"), None),
        P(("dp", "fsdp")),
    )
    body = shards if dict(mesh.shape) == {"dp": 4, "fsdp": 8} else plain_shards
    return jax.shard_map(body, mesh=mesh, in_specs=in_specs, out_specs=out_specs, check_vma=False)
```

```python
import math
from functools import partial

import jax
import jax.numpy as jnp
from jax import lax
from jax.experimental import pallas as pl
from jax.experimental.pallas import tpu as pltpu
from jax.sharding import PartitionSpec as P

HEADS = 12
PIX = 64
EXPERTS = 3
LEADS = 16


norm_epsilon = 1e-05
score_scale = 0.125


def layer_norm(hidden, norm_gain, norm_shift):
    average = jnp.mean(hidden, axis=-1, keepdims=True)
    centered = hidden - average
    variance = jnp.mean(centered * centered, axis=-1, keepdims=True)
    return centered * lax.rsqrt(variance + norm_epsilon) * norm_gain + norm_shift


def gelu_exact(values):
    return 0.5 * values * (1.0 + lax.erf(values * 0.7071067811865476))


def expert_softmax(logits, experts, pixels):
    gate_part = logits[:, : experts * pixels].reshape(logits.shape[0], experts, pixels)
    largest = jnp.max(gate_part, axis=1, keepdims=True)
    raised = jnp.exp(gate_part - largest)
    shares = raised / jnp.sum(raised, axis=1, keepdims=True)
    return jnp.concatenate(
        [shares.reshape(logits.shape[0], experts * pixels), logits[:, experts * pixels :]], axis=1
    )


def allowed_keys(query_window, key_window, key_valid, query_start):
    query_place = query_start + jnp.arange(query_window.shape[0], dtype=jnp.int32)
    key_place = jnp.arange(key_window.shape[0], dtype=jnp.int32)
    same_window = query_window[:, None] == key_window[None, :]
    usable = (key_valid[None, :] > 0) | (query_place[:, None] == key_place[None, :])
    return same_window & usable


AXES = ("dp", "fsdp")
FAR_Z, NEAR_Z, FIRST, SECOND, SIBLING = (4, 4), (2, 2), (8, 16), (16, 8), (1, 1)
ORDERS = {
    "q": (FAR_Z, NEAR_Z, FIRST, SECOND),
    "u": (FAR_Z, FIRST, SECOND, NEAR_Z),
    "d": (FIRST, FAR_Z, NEAR_Z, SECOND),
    "h": (NEAR_Z, FAR_Z, FIRST, SECOND),
    "head": (FAR_Z, NEAR_Z, FIRST, SECOND),
    "down": (FAR_Z, NEAR_Z, FIRST, SECOND),
    "up": (FAR_Z, FIRST, SECOND, NEAR_Z),
    "front": (FAR_Z, NEAR_Z, FIRST, SECOND),
    "mix": (FAR_Z, NEAR_Z, FIRST, SECOND),
}
GATHER_SEQUENCE = (
    ("q", 0), ("d", 0), ("h", 0), ("u", 0), ("q", 1), ("d", 1), ("u", 1), ("q", 2), ("h", 1), ("u", 2),
    ("d", 2),
)
SCATTER_SEQUENCE = (
    "head", "mix", "front", "down", "up", "head", "front", "mix", "head", "down", "up", "front", "mix",
    "down", "up", "front", "mix",
)
MOST_VMEM, SPARE_VMEM = 60 * 1024 * 1024, 8 * 1024 * 1024
WIDTH = 768
HIDDEN = 3072
HEAD = 4608
TOKENS = 512
GATE = 512
F32 = jnp.float32
BF16 = jnp.bfloat16
HBM = pl.BlockSpec(memory_space=pltpu.HBM)
SMEM = pl.BlockSpec(memory_space=pltpu.SMEM)
VMEM = pl.BlockSpec(memory_space=pltpu.VMEM)
QKV_PART, SMALL_PART = (0, 1152), (1152, 128)
UP_PART, OUT_PART, GATE_PART = (0, 1536), (1536, 384), (1920, 256)
DOWN_PART, HEAD_PART = (0, 384), (0, 2048)


def chip_masks(order, lane):
    masks = []
    for place in range(16):
        mask = 0
        for step in range(4):
            if place >> step & 1:
                mask ^= order[step][lane]
        masks.append(mask >> 1)
    return masks


def table_start(group, side):
    return 1 + 32 * list(ORDERS).index(group) + 16 * side


def exchange(array, masks):
    return lax.ppermute(array, AXES, [(d, d ^ masks[d & 1]) for d in range(32)])


def whereabouts():
    device = lax.axis_index("dp") * 8 + lax.axis_index("fsdp")
    core, chip = device % 2, device // 2
    tables = [chip_masks(order, 0) + chip_masks(order, 1) for order in ORDERS.values()]
    swapped = [chip_masks(order, 1) + chip_masks(order, 0) for order in ORDERS.values()]
    places = jnp.where(core == 0, jnp.array(tables, jnp.int32), jnp.array(swapped, jnp.int32))
    places = (places ^ chip).reshape(32 * len(ORDERS))
    return core, jnp.concatenate([core[None].astype(jnp.int32), places])


def after(value, *marks):
    return lax.optimization_barrier((value, marks))[0]


def in_core_order(core, mine, theirs, axis):
    return jnp.where(
        core == 0,
        jnp.concatenate([mine, theirs], axis=axis),
        jnp.concatenate([theirs, mine], axis=axis),
    )


def pack_kernel(core, qkv, out, up, down, head, table, *refs):
    vectors, (up_bias, head_bias), refs = refs[:6], refs[6:8], refs[8:]
    outs, (rows,) = refs[:8], refs[8:]
    rows[...] = jnp.zeros_like(rows)
    for index, vector in enumerate(vectors):
        rows[index : index + 1, :24] = vector[...].astype(F32)
    for index in range(4):
        rows[6 + index : 7 + index, :24] = up_bias[:, 24 * index : 24 * index + 24].astype(F32)
    for index in range(6):
        rows[10 + index : 11 + index, :24] = head_bias[:, 24 * index : 24 * index + 24].astype(F32)
    rows[16:32, :24] = table[...].astype(F32)
    small = rows[...].T[:24].astype(BF16)
    for side in range(2):
        q, u, d, h = outs[4 * side : 4 * side + 4]
        q[:, :1152] = qkv[:, lane_columns(core, side, 1152)]
        q[:, 1152:] = small
        u[:, :1536] = up[:, lane_columns(core, side, 1536)]
        u[:, 1536:1920] = out[:, lane_columns(core, side, 384)]
        u[:, 1920:] = head[:, lane_columns(core, side, 256)]
        d[...] = down[:, lane_columns(core, side, 384)]
        h[...] = head[:, lane_columns(core, side, 2048, GATE)]


def packed(core, weights, table, vectors):
    shapes = [(24, 1280), (24, 2176), (96, 384), (24, 2048)] * 2
    return call(
        pack_kernel,
        (core.reshape(1), *weights, table, *[vector[None] for vector in vectors]),
        [SMEM] + [VMEM] * 14,
        [(shape, BF16, False) for shape in shapes],
        [pltpu.VMEM((128, 128), F32)],
    )


def doubled(held, masks):
    return jnp.concatenate([held, exchange(held, masks)], axis=0)


def both_lanes(*arrays):
    return arrays + tuple(exchange(array, SIBLING) for array in arrays)


def total(first, second):
    return first.astype(F32) + second.astype(F32)


def folded(keep, got, start=0):
    half = got.shape[0] // 2
    send = total(keep[half:], got[half:]).astype(BF16)
    return total(keep[:half], got[:half]).astype(BF16), send


def finished(keep, got, core, widths):
    block = total(keep, got)[0]
    rows = block.shape[0] // 2
    upper, lower = block[:rows], block[rows:]
    mine = jnp.where(core == 0, upper, lower)
    theirs = jnp.where(core == 0, lower, upper).astype(BF16)
    other = exchange(theirs, SIBLING).astype(F32)
    pieces, start = [], 0
    for width in widths:
        span = slice(start, start + width)
        pieces.append(in_core_order(core, mine[:, span], other[:, span], 1))
        start += width
    return pieces


def across(first, second):
    return lax.dot_general(first, second, (((1,), (1,)), ((), ())), preferred_element_type=F32)


def times(first, second):
    return jnp.dot(first, second, preferred_element_type=F32)


def lane_columns(where, side, stride, first=0, width=None):
    return pl.ds(pl.multiple_of(first + (where[0] ^ side) * stride, 128), width or stride)


def block_copies(where, group, sources, part, target, sems, side, first=0):
    start, width = part
    rows = sources[0].shape[1]
    half = len(sources) // 2
    count = 16 // half
    copies = []
    for place in range(16):
        row = pl.multiple_of(where[table_start(group, side) + place] * rows, rows)
        copies.append(
            pltpu.make_async_copy(
                sources[half * side + place // count].at[place % count, :, pl.ds(start, width)],
                target.at[pl.ds(row, rows), lane_columns(where, side, width, first)],
                sems.at[side, place],
            )
        )
    return copies


def start_all(copies):
    for copy in copies:
        copy.start()


def wait_all(copies):
    for copy in copies:
        copy.wait()


def mean_and_scale(hidden):
    average = jnp.mean(hidden, axis=1, keepdims=True)
    centered = hidden - average
    variance = jnp.mean(centered * centered, axis=1, keepdims=True)
    return centered, lax.rsqrt(variance + norm_epsilon)


def norm_backward(hidden, gain, upstream):
    centered, scale = mean_and_scale(hidden)
    normed = centered * scale
    gain_grad = jnp.sum(upstream * normed, axis=0, keepdims=True)
    shift_grad = jnp.sum(upstream, axis=0, keepdims=True)
    scaled = upstream * gain
    first = jnp.mean(scaled, axis=1, keepdims=True)
    second = jnp.mean(scaled * normed, axis=1, keepdims=True)
    return scale * (scaled - first - normed * second), gain_grad, shift_grad


def call(kernel, operands, in_specs, outs, scratch, spare=None):
    def size(item):
        return math.prod(item.shape) * jnp.dtype(item.dtype).itemsize

    held = [item for item, spec in zip(operands, in_specs) if spec is VMEM]
    held += [jax.ShapeDtypeStruct(shape, kind) for shape, kind, copied in outs if not copied]
    held += [item for item in scratch if getattr(item, "memory_space", None) == pltpu.VMEM]
    limit = MOST_VMEM if spare is None else sum(size(item) for item in held) + spare
    return pl.pallas_call(
        kernel,
        out_shape=[jax.ShapeDtypeStruct(shape, kind) for shape, kind, _ in outs],
        in_specs=in_specs,
        out_specs=[HBM if copied else VMEM for _, _, copied in outs],
        scratch_shapes=scratch,
        compiler_params=pltpu.CompilerParams(vmem_limit_bytes=limit),
        cost_estimate=pl.CostEstimate(flops=2 * 10**12, bytes_accessed=10**10, transcendentals=0),
    )(*operands)


def lane_scratch(rows, width):
    return [pltpu.VMEM((2, rows, width), BF16), pltpu.SemaphoreType.DMA((2, 16))]


def weight_scratch(rows, width):
    return [pltpu.VMEM((rows, width), BF16), pltpu.SemaphoreType.DMA((2, 16))]


def taken(refs, *counts):
    groups = []
    for count in counts:
        groups.append(refs[:count])
        refs = refs[count:]
    return *groups, refs


def front_kernel(where, lead, patches, *refs):
    sources, outs, scratch = taken(refs, 4, 3)
    turned_out, qkv_out, small = outs
    weight, sems, smalls, small_sems, state, rows, turned, qkv, io_sems = scratch
    loads = [block_copies(where, "q", sources, QKV_PART, weight, sems, side) for side in range(2)]
    small_loads = []
    for place in range(16):
        row = pl.multiple_of(where[table_start("q", 0) + place] * 48, 48)
        small_loads.append(
            pltpu.make_async_copy(
                sources[place // 8].at[place % 8, :, pl.ds(*SMALL_PART)],
                smalls.at[pl.ds(row, 48), :],
                small_sems.at[place],
            )
        )
    state_load = pltpu.make_async_copy(patches, state, io_sems.at[0])
    start_all(small_loads)
    state_load.start()
    start_all(loads[0])
    start_all(loads[1])
    wait_all(small_loads)
    columns = smalls[...].astype(F32).T
    places = lax.broadcasted_iota(jnp.int32, (LEADS, WIDTH), 0)
    lead_row = jnp.sum(
        jnp.where(places == lead[0], columns[16 : 16 + LEADS], 0.0), axis=0, keepdims=True
    )
    small[...] = columns[:32]
    small[16:17, :] = lead_row
    state_load.wait()
    centered, scale = mean_and_scale(state[...].astype(F32) + lead_row)
    rows[...] = (centered * scale * columns[0:1] + columns[1:2]).astype(BF16)
    turned[...] = rows[...].T
    stores = [pltpu.make_async_copy(turned, turned_out, io_sems.at[1])]
    stores[0].start()
    wait_all(loads[0] + loads[1])
    for part in range(3):
        span = slice(part * WIDTH, part * WIDTH + WIDTH)
        qkv[:, span] = times(rows[...], weight[:, span]).astype(BF16)
        stores.append(pltpu.make_async_copy(qkv.at[:, span], qkv_out.at[:, span], io_sems.at[2 + part]))
        stores[-1].start()
    wait_all(stores)


def front_forward(where, lead_index, patches, arrays):
    return call(
        front_kernel,
        (where, lead_index, patches, *arrays),
        [SMEM, SMEM, HBM] + [HBM] * 4,
        [
            ((WIDTH, TOKENS), BF16, True),
            ((TOKENS, 3 * WIDTH), BF16, True),
            ((32, WIDTH), F32, False),
        ],
        weight_scratch(WIDTH, 3 * WIDTH)
        + [pltpu.VMEM((WIDTH, 128), BF16), pltpu.SemaphoreType.DMA((16,))]
        + [
            pltpu.VMEM((TOKENS, WIDTH), BF16),
            pltpu.VMEM((TOKENS, WIDTH), BF16),
            pltpu.VMEM((WIDTH, TOKENS), BF16),
            pltpu.VMEM((TOKENS, 3 * WIDTH), BF16),
            pltpu.SemaphoreType.DMA((5,)),
        ],
    )


KEY_SPANS = ((0, 256), (0, 384), (128, 512), (256, 512))


def fill_bias(lengths, pad, bias):
    ends, end = [], 0
    for index in range(lengths.shape[1]):
        end = end + lengths[0, index]
        ends.append(end)

    def windows(places):
        return sum([(places >= end).astype(jnp.int32) for end in ends])

    for block, (low, high) in enumerate(KEY_SPANS):
        count = high - low
        queries = lax.broadcasted_iota(jnp.int32, (1, 128), 1) + 128 * block
        keys = lax.broadcasted_iota(jnp.int32, (count, 1), 0) + low
        same = windows(queries) == windows(keys)
        usable = (pad[low:high, :] > 0) | (queries == keys)
        bias[block, :count, :] = jnp.where(same & usable, 0.0, -1e30)


def two_heads(block):
    first = lax.broadcasted_iota(jnp.int32, block.shape, 1) < block.shape[1] // 2
    zero = jnp.zeros_like(block)
    return jnp.concatenate([jnp.where(first, block, zero), jnp.where(first, zero, block)], axis=0)


def head_rows_of(stacked):
    return jnp.concatenate([stacked[:64, :128], stacked[64:, 128:]], axis=0)


def probabilities(scores, allowed):
    masked = scores * score_scale + allowed
    raised = jnp.exp(masked - jnp.max(masked, axis=0, keepdims=True))
    return raised * (1.0 / jnp.sum(raised, axis=0, keepdims=True))


def attention_kernel(where, lengths, pad, qkv, attended_out, turned_out, bias, turned, rows, sems):
    fill_bias(lengths, pad, bias)

    def pair(index, carry):
        first = index * 128
        columns = pl.ds(pl.multiple_of(first, 128), 128)
        keys_at = pl.ds(pl.multiple_of(first + WIDTH, 128), 128)
        values = qkv[:, pl.ds(pl.multiple_of(first + 2 * WIDTH, 128), 128)].T
        for block, (low, high) in enumerate(KEY_SPANS):
            span = slice(128 * block, 128 * block + 128)
            scores = across(qkv[low:high, keys_at], two_heads(qkv[span, columns]))
            allowed = bias[block, : high - low, :]
            probs = [
                probabilities(scores[:, 128 * head : 128 * head + 128], allowed).astype(BF16)
                for head in range(2)
            ]
            mixed = times(values[:, low:high], jnp.concatenate(probs, axis=1))
            turned[columns, span] = head_rows_of(mixed).astype(BF16)
        return carry

    lax.fori_loop(0, WIDTH // 128, pair, 0)
    stores = [pltpu.make_async_copy(turned, turned_out, sems.at[0])]
    stores[0].start()
    rows[...] = turned[...].T
    stores.append(pltpu.make_async_copy(rows, attended_out, sems.at[1]))
    stores[1].start()
    wait_all(stores)


def attention_forward(where, lengths, pad, qkv):
    rows, columns = (TOKENS, WIDTH), (WIDTH, TOKENS)
    return call(
        attention_kernel,
        (where, lengths, pad, qkv),
        [SMEM, SMEM, VMEM, VMEM],
        [(rows, BF16, True), (columns, BF16, True)],
        [
            pltpu.VMEM((4, 384, 128), F32),
            pltpu.VMEM(columns, BF16),
            pltpu.VMEM(rows, BF16),
            pltpu.SemaphoreType.DMA((2,)),
        ],
    )


def gate_shares(logits, cotangent, shares, gate_grad):
    gate_grad[:, 256:] = cotangent[:, 256:GATE]
    first, rest = logits[:, :128], logits[:, 128:256]
    left = lax.broadcasted_iota(jnp.int32, first.shape, 1) < PIX
    third = jnp.where(left, rest, pltpu.roll(rest, PIX, 1))
    largest = jnp.maximum(jnp.maximum(first, pltpu.roll(first, PIX, 1)), third)
    raised, raised_third = jnp.exp(first - largest), jnp.exp(third - largest)
    scale = 1.0 / (raised + pltpu.roll(raised, PIX, 1) + raised_third)
    share, share_third = raised * scale, raised_third * scale
    shares[:, :128] = share
    shares[:, 128:256] = jnp.where(left, share_third, rest)
    pull, other = cotangent[:, :128].astype(F32), cotangent[:, 128:256].astype(F32)
    pull_third = jnp.where(left, other, pltpu.roll(other, PIX, 1))
    weighed = share * pull
    inner = weighed + pltpu.roll(weighed, PIX, 1) + share_third * pull_third
    gate_grad[:, :128] = (share * (pull - inner)).astype(BF16)
    gate_grad[:, 128:256] = jnp.where(left, share_third * (pull_third - inner), other).astype(BF16)


def send_lane(where, group, lane, out, sems, side):
    rows = out.shape[1]
    copies = []
    for place in range(16):
        row = pl.multiple_of(where[table_start(group, side) + place] * rows, rows)
        copies.append(
            pltpu.make_async_copy(lane.at[pl.ds(row, rows), :], out.at[place], sems.at[place])
        )
    start_all(copies)
    return copies


def middle_kernel(
    where, small, up_bias, head_bias, attended, patches, cotangent, act_cotangent, attended_turned,
    *refs,
):
    up_sources, down_sources, head_sources, outs, scratch = taken(refs, 4, 4, 4, 15)
    outputs, shares, gate_bias, down_bias, up_bias_sum, terms, mid_grad, out_grad, mixed, *grads = outs
    down_mine, down_theirs, up_mine, up_theirs, head_mine, head_theirs = grads
    out_weight, out_sems, up, up_sems, down, down_sems, scratch = *scratch[:6], scratch[6:]
    head, head_sems, gate_sems, rows, branch, mid, mlp_turned, scratch = *scratch[:7], scratch[7:]
    act, act_turned, slope, turned, pulls, act_pulls, gate_grad, scratch = *scratch[:7], scratch[7:]
    lane, lane_sems, down_lane, down_lane_sems, mixes, more_sems, io_sems = scratch

    def loads(group, sources, part, target, sems, first=0):
        copies = []
        for side in range(2):
            copies += block_copies(where, group, sources, part, target, sems, side, first)
        return copies

    state_loads = [
        pltpu.make_async_copy(attended, rows, io_sems.at[0]),
        pltpu.make_async_copy(patches, branch, io_sems.at[1]),
    ]
    out_loads = loads("u", up_sources, OUT_PART, out_weight, out_sems)
    up_loads = loads("u", up_sources, UP_PART, up, up_sems)
    down_loads = loads("d", down_sources, DOWN_PART, down, down_sems)
    gate_loads = loads("u", up_sources, GATE_PART, head, gate_sems)
    head_loads = loads("h", head_sources, HEAD_PART, head, head_sems, GATE)
    pull_load = pltpu.make_async_copy(cotangent, pulls, io_sems.at[2])
    act_load = pltpu.make_async_copy(act_cotangent, act_pulls, io_sems.at[3])
    mix_load = pltpu.make_async_copy(attended_turned, mixes, io_sems.at[4])
    start_all(state_loads + out_loads + up_loads + down_loads + gate_loads)
    pull_load.start()
    start_all(head_loads)
    act_load.start()
    mix_load.start()

    wait_all(state_loads + out_loads)
    mid[...] = (
        branch[...].astype(F32)
        + small[16:17, :]
        + times(rows[...], out_weight[...])
        + small[2:3, :]
    )
    centered, scale = mean_and_scale(mid[...])
    rows[...] = (centered * scale * small[3:4, :] + small[4:5, :]).astype(BF16)
    mlp_turned[...] = rows[...].T
    wait_all(up_loads)
    for tile in range(6):
        span = slice(tile * 512, tile * 512 + 512)
        values = times(rows[...], up[:, span]) + up_bias[:, span]
        share = 0.5 * (1.0 + lax.erf(values * 0.7071067811865476))
        density = jnp.exp(-0.5 * values * values) * 0.3989422804014327
        activated = (values * share).astype(BF16)
        act[:, span] = activated
        act_turned[span, :] = activated.T
        slope[:, span] = (share + values * density).astype(BF16)
    wait_all(down_loads)
    outputs[...] = (mid[...] + times(act[...], down[...]) + small[5:6, :]).astype(BF16)
    turned[...] = outputs[...].T
    wait_all(gate_loads)
    shares[...] = times(outputs[...], head[:, :GATE]) + head_bias[:, :GATE]
    pull_load.wait()
    gate_shares(shares, pulls, shares, gate_grad)
    gate_bias[...] = jnp.sum(gate_grad[...].astype(F32), axis=0, keepdims=True)
    pulls[:, :GATE] = gate_grad[...]

    def head_lane(side, target, sems, out):
        target[:, :256] = times(turned[...], pulls[:, lane_columns(where, side, 256)]).astype(BF16)
        for tile in range(4):
            span = lane_columns(where, side, 2048, GATE + tile * 512, 512)
            target[:, 256 + tile * 512 : 768 + tile * 512] = times(turned[...], pulls[:, span]).astype(
                BF16
            )
        return send_lane(where, "head", target, out, sems, side)

    def down_lane_of(side, out):
        columns = branch[:, lane_columns(where, side, 384)]
        for part in range(4):
            span = slice(part * WIDTH, part * WIDTH + WIDTH)
            down_lane[span, :] = times(act_turned[span, :], columns).astype(BF16)
        return send_lane(where, "down", down_lane, out, down_lane_sems, side)

    def up_lane(side, target, sems, out):
        for tile in range(3):
            span = lane_columns(where, side, 1536, tile * 512, 512)
            target[:, tile * 512 : tile * 512 + 512] = times(mlp_turned[...], slope[:, span]).astype(
                BF16
            )
        target[:, 1536:1920] = times(
            mixes[...], out_grad[:, lane_columns(where, side, 384)]
        ).astype(BF16)
        return send_lane(where, "up", target, out, sems, side)

    first_stores = head_lane(1, lane, lane_sems, head_theirs)
    act_load.wait()
    wait_all(head_loads)
    mid_grad[...] = act_pulls[...].astype(F32) + across(pulls[...], head[...])
    branch[...] = mid_grad[...].astype(BF16)
    down_bias[...] = jnp.sum(branch[...].astype(F32), axis=0, keepdims=True)
    stores = head_lane(0, head.at[:, :2304], more_sems.at[0], head_mine)
    down_stores = down_lane_of(1, down_theirs)
    for tile in range(6):
        span = slice(tile * 512, tile * 512 + 512)
        grad = across(branch[...], down[span, :])
        rounded = (slope[:, span].astype(F32) * grad).astype(BF16)
        slope[:, span] = rounded
        up_bias_sum[:, span] = jnp.sum(rounded.astype(F32), axis=0, keepdims=True)
    wait_all(down_stores)
    stores += down_lane_of(0, down_mine)
    grad = across(slope[...], up[...])
    pulled, gain_grad, shift_grad = norm_backward(mid[...], small[3:4, :], grad)
    pulled = pulled + mid_grad[...]
    rounded = pulled.astype(BF16)
    mid_grad[...] = pulled
    out_grad[...] = rounded
    terms[...] = jnp.zeros_like(terms)
    terms[0:1, :] = jnp.sum(rounded.astype(F32), axis=0, keepdims=True)
    terms[1:2, :] = gain_grad
    terms[2:3, :] = shift_grad
    mix_load.wait()
    stores += up_lane(1, head.at[:, 2304:4224], more_sems.at[1], up_theirs)
    wait_all(first_stores)
    stores += up_lane(0, lane.at[:, :1920], lane_sems, up_mine)
    mixed[...] = across(out_grad[...], out_weight[...]).astype(BF16)
    wait_all(stores)


def middle(
    where, small, up_bias, head_bias, attended, patches, cotangent, act_cotangent, attended_turned,
    up, down, head,
):
    rows, columns = (TOKENS, WIDTH), (WIDTH, TOKENS)
    wide, tall = (TOKENS, HIDDEN), (HIDDEN, TOKENS)
    return call(
        middle_kernel,
        (
            where, small, up_bias, head_bias, attended, patches, cotangent, act_cotangent,
            attended_turned, *up, *down, *head,
        ),
        [SMEM, VMEM, VMEM, VMEM] + [HBM] * 17,
        [
            (rows, BF16, False),
            ((TOKENS, GATE), F32, False),
            ((1, GATE), F32, False),
            ((1, WIDTH), F32, False),
            ((1, HIDDEN), F32, False),
            ((8, WIDTH), F32, False),
            (rows, F32, False),
            (rows, BF16, False),
            (rows, BF16, False),
            ((16, 192, 384), BF16, True),
            ((16, 192, 384), BF16, True),
            ((16, 48, 1920), BF16, True),
            ((16, 48, 1920), BF16, True),
            ((16, 48, 2304), BF16, True),
            ((16, 48, 2304), BF16, True),
        ],
        weight_scratch(WIDTH, WIDTH)
        + weight_scratch(WIDTH, HIDDEN)
        + weight_scratch(HIDDEN, WIDTH)
        + weight_scratch(WIDTH, HEAD)
        + [
            pltpu.SemaphoreType.DMA((2, 16)),
            pltpu.VMEM(rows, BF16),
            pltpu.VMEM(rows, BF16),
            pltpu.VMEM(rows, F32),
            pltpu.VMEM(columns, BF16),
            pltpu.VMEM(wide, BF16),
            pltpu.VMEM(tall, BF16),
            pltpu.VMEM(wide, BF16),
            pltpu.VMEM(columns, BF16),
            pltpu.VMEM((TOKENS, HEAD), BF16),
            pltpu.VMEM(rows, BF16),
            pltpu.VMEM((TOKENS, GATE), BF16),
            pltpu.VMEM((WIDTH, 2304), BF16),
            pltpu.SemaphoreType.DMA((16,)),
            pltpu.VMEM((HIDDEN, 384), BF16),
            pltpu.SemaphoreType.DMA((16,)),
            pltpu.VMEM(columns, BF16),
            pltpu.SemaphoreType.DMA((2, 16)),
            pltpu.SemaphoreType.DMA((5,)),
        ],
    )


def attend_back(count, qkv, mixed, bias, turned, key_sum, value_sum, qkv_grad):
    width = 128 * count

    def columns_at(first):
        return pl.ds(pl.multiple_of(first, 128), 128)

    def pair(index, carry):
        own = index * 128
        columns, keys_at = columns_at(own), columns_at(own + width)
        values_at = columns_at(own + 2 * width)
        keys_turned = qkv[:, keys_at].T
        key_sum[...] = jnp.zeros_like(key_sum)
        value_sum[...] = jnp.zeros_like(value_sum)
        for block, (low, high) in enumerate(KEY_SPANS):
            span = slice(128 * block, 128 * block + 128)
            queries, grads = two_heads(qkv[span, columns]), two_heads(mixed[span, columns])
            scores = across(qkv[low:high, keys_at], queries)
            prob_grads = across(qkv[low:high, values_at], grads)
            allowed = bias[block, : high - low, :]
            probs, score_grads = [], []
            for head in range(2):
                part = slice(128 * head, 128 * head + 128)
                prob = probabilities(scores[:, part], allowed)
                pulled = prob * prob_grads[:, part]
                inner = jnp.sum(pulled, axis=0, keepdims=True)
                probs.append(prob.astype(BF16))
                score_grads.append((pulled - prob * inner).astype(BF16))
            score_grad = jnp.concatenate(score_grads, axis=1)
            key_sum[low:high, :] += times(score_grad, queries)
            value_sum[low:high, :] += times(jnp.concatenate(probs, axis=1), grads)
            turned[:, span] = head_rows_of(times(keys_turned[:, low:high], score_grad)) * score_scale
        qkv_grad[:, columns] = turned[...].T.astype(BF16)
        qkv_grad[:, keys_at] = (key_sum[...] * score_scale).astype(BF16)
        qkv_grad[:, values_at] = value_sum[...].astype(BF16)
        return carry

    lax.fori_loop(0, count, pair, 0)


def attention_scratch(count):
    return [
        pltpu.VMEM((4, 384, 128), F32),
        pltpu.VMEM((TOKENS, 384 * count), BF16),
        pltpu.VMEM((TOKENS, 128 * count), BF16),
        pltpu.VMEM((128, TOKENS), F32),
        pltpu.VMEM((TOKENS, 128), F32),
        pltpu.VMEM((TOKENS, 128), F32),
        pltpu.SemaphoreType.DMA((4,)),
    ]


def attention_loads(start, count, qkv, mixed, own_qkv, own_mixed, sems):
    width = 128 * count
    copies = [
        pltpu.make_async_copy(
            mixed.at[:, pl.ds(128 * start, width)], own_mixed.at[:, pl.ds(0, width)], sems.at[3]
        )
    ]
    for part in range(3):
        copies.append(
            pltpu.make_async_copy(
                qkv.at[:, pl.ds(WIDTH * part + 128 * start, width)],
                own_qkv.at[:, pl.ds(width * part, width)],
                sems.at[part],
            )
        )
    return copies


def early_back_kernel(where, lengths, pad, mixed, qkv, input_turned, *refs):
    (qkv_grad, mine_out, theirs_out), scratch = taken(refs, 3)
    bias, own_qkv, own_mixed, turned, key_sum, value_sum, sems, scratch = *scratch[:7], scratch[7:]
    lane, lane_sems, inputs, io_sems = scratch
    loads = attention_loads(0, 4, qkv, mixed, own_qkv, own_mixed, sems)
    in_load = pltpu.make_async_copy(input_turned, inputs, io_sems.at[0])
    start_all(loads + [in_load])
    fill_bias(lengths, pad, bias)
    wait_all(loads)
    attend_back(4, own_qkv, own_mixed, bias, turned, key_sum, value_sum, qkv_grad)
    in_load.wait()
    stores = []
    for side, out in ((1, theirs_out), (0, mine_out)):
        lane[side] = times(inputs[...], qkv_grad[:, lane_columns(where, side, 768)]).astype(BF16)
        stores += send_lane(where, "mix", lane.at[side], out, lane_sems.at[side], side)
    wait_all(stores)


def early_backward(where, lengths, pad, mixed, qkv, input_turned):
    return call(
        early_back_kernel,
        (where, lengths, pad, mixed, qkv, input_turned),
        [SMEM, SMEM, VMEM] + [HBM] * 3,
        [
            ((TOKENS, 1536), BF16, False),
            ((16, 48, 768), BF16, True),
            ((16, 48, 768), BF16, True),
        ],
        attention_scratch(4)
        + lane_scratch(WIDTH, 768)
        + [pltpu.VMEM((WIDTH, TOKENS), BF16), pltpu.SemaphoreType.DMA((1,))],
    )


def late_back_kernel(
    where, lead, lengths, pad, small, terms, down_row, up_rows, head_rows, head_bias,
    outputs, shares, mixed, qkv, first_grad, patches, mid_grad, input_turned, *refs
):
    sources, head_sources, outs, scratch = taken(refs, 4, 4, 4)
    patch_out, head_out, mine_out, theirs_out = outs
    head, head_sems, rows, result, head_io, scratch = *scratch[:5], scratch[5:]
    bias, own_qkv, own_mixed, turned, key_sum, value_sum, sems, scratch = *scratch[:7], scratch[7:]
    weight, weight_sems, lane, lane_sems, pulls, late_pulls, scratch = *scratch[:6], scratch[6:]
    state, mids, inputs, patch_grad, small_grad, io_sems = scratch
    own_loads = attention_loads(4, 2, qkv, mixed, own_qkv, own_mixed, sems)
    loads = [
        block_copies(where, "q", sources, QKV_PART, weight, weight_sems, side) for side in range(2)
    ]
    pairs = [(patches, state), (mid_grad, mids), (input_turned, inputs)]
    for part in range(3):
        target = pulls.at[:, pl.ds(WIDTH * part, 512)]
        pairs.append((first_grad.at[:, pl.ds(512 * part, 512)], target))
    in_loads = [pltpu.make_async_copy(*pair, io_sems.at[at]) for at, pair in enumerate(pairs)]
    head_loads = [
        block_copies(where, "h", head_sources, HEAD_PART, head, head_sems, side) for side in range(2)
    ]
    row_load = pltpu.make_async_copy(outputs, rows, head_io.at[0])
    share_load = pltpu.make_async_copy(shares, result.at[:, :GATE], head_io.at[1])
    start_all(own_loads + [row_load] + head_loads[0] + head_loads[1] + [share_load])
    start_all(in_loads + loads[0] + loads[1])
    fill_bias(lengths, pad, bias)
    wait_all(own_loads)
    attend_back(2, own_qkv, own_mixed, bias, turned, key_sum, value_sum, late_pulls)
    wait_all([row_load, share_load] + head_loads[0] + head_loads[1])
    stores = [pltpu.make_async_copy(result.at[:, :GATE], head_out.at[:, :GATE], head_io.at[2])]
    stores[0].start()
    for tile in range(8):
        span = slice(GATE + tile * 512, GATE + tile * 512 + 512)
        result[:, span] = (
            times(rows[...], head[:, tile * 512 : tile * 512 + 512]) + head_bias[:, span]
        )
        stores.append(
            pltpu.make_async_copy(result.at[:, span], head_out.at[:, span], head_io.at[3 + tile])
        )
        stores[-1].start()
    wait_all(loads[0] + loads[1] + in_loads)
    for part in range(3):
        pulls[:, WIDTH * part + 512 : WIDTH * part + 768] = late_pulls[
            :, 256 * part : 256 * part + 256
        ]
    grad = across(pulls[...], weight[...])
    pulled, gain_grad, shift_grad = norm_backward(
        state[...].astype(F32) + small[16:17, :], small[0:1, :], grad
    )
    pulled = pulled + mids[...]
    patch_grad[...] = pulled
    stores.append(pltpu.make_async_copy(patch_grad, patch_out, io_sems.at[6]))
    stores[-1].start()
    small_grad[0:1, :] = gain_grad
    small_grad[1:2, :] = shift_grad
    small_grad[2:5, :] = terms[0:3, :]
    small_grad[5:6, :] = down_row[...]
    small_grad[6:10, :] = up_rows[...]
    small_grad[10:16, :] = head_rows[...]
    places = lax.broadcasted_iota(jnp.int32, (LEADS, WIDTH), 0)
    lead_grad = jnp.sum(pulled, axis=0, keepdims=True)
    small_grad[16:32, :] = jnp.where(places == lead[0], lead_grad, 0.0)
    for side, out in ((1, theirs_out), (0, mine_out)):
        lane[side, :, :384] = times(
            inputs[...], late_pulls[:, lane_columns(where, side, 384)]
        ).astype(BF16)
        rows = small_grad[pl.ds(pl.multiple_of((where[0] ^ side) * 16, 16), 16), :]
        rows = jnp.concatenate([rows, jnp.zeros((112, WIDTH), F32)], axis=0)
        lane[side, :, 384:] = rows.T.astype(BF16)
        stores += send_lane(where, "front", lane.at[side], out, lane_sems.at[side], side)
    wait_all(stores)


def late_backward(
    where, lead, lengths, pad, small, terms, down_row, up_rows, head_rows, head_bias,
    outputs, shares, mixed, qkv, first_grad, patches, mid_grad, input_turned, arrays, head_arrays,
):
    rows, columns = (TOKENS, WIDTH), (WIDTH, TOKENS)
    return call(
        late_back_kernel,
        (
            where, lead, lengths, pad, small, terms, down_row, up_rows, head_rows, head_bias,
            outputs, shares, mixed, qkv, first_grad, patches, mid_grad, input_turned,
            *arrays, *head_arrays,
        ),
        [SMEM, SMEM, SMEM] + [VMEM] * 7 + [HBM] * 16,
        [
            (rows, F32, True),
            ((TOKENS, HEAD), F32, True),
            ((16, 48, 512), BF16, True),
            ((16, 48, 512), BF16, True),
        ],
        weight_scratch(WIDTH, HEAD - GATE)
        + [
            pltpu.VMEM(rows, BF16),
            pltpu.VMEM((TOKENS, HEAD), F32),
            pltpu.SemaphoreType.DMA((11,)),
        ]
        + attention_scratch(2)
        + weight_scratch(WIDTH, 3 * WIDTH)
        + lane_scratch(WIDTH, 512)
        + [
            pltpu.VMEM((TOKENS, 3 * WIDTH), BF16),
            pltpu.VMEM((TOKENS, WIDTH), BF16),
            pltpu.VMEM(rows, BF16),
            pltpu.VMEM(rows, F32),
            pltpu.VMEM(columns, BF16),
            pltpu.VMEM(rows, F32),
            pltpu.VMEM((32, WIDTH), F32),
            pltpu.SemaphoreType.DMA((7,)),
        ],
    )


def rows_of(vector, count):
    return vector.reshape(32, count, 24).transpose(1, 0, 2).reshape(count, WIDTH)


def vector_of(rows):
    count = rows.shape[0]
    return rows.reshape(count, 32, 24).transpose(1, 0, 2).reshape(1, count * WIDTH)


def shards(
    patches,
    lead_index,
    window_lengths,
    pad_mask,
    lead_table,
    attn_gain,
    attn_shift,
    qkv_weight,
    out_weight,
    out_bias,
    mlp_gain,
    mlp_shift,
    up_weight,
    up_bias,
    down_weight,
    down_bias,
    head_weight,
    head_bias,
    act_cotangent,
    head_cotangent,
):
    core, where = whereabouts()
    weights = (qkv_weight, out_weight, up_weight, down_weight, head_weight)
    vectors = (
        attn_gain, attn_shift, out_bias, mlp_gain, mlp_shift, down_bias, up_bias, head_bias
    )
    parts = packed(core, weights, lead_table, vectors)
    pad = pad_mask[:, None]
    cotangent_sum = jnp.sum(head_cotangent[:, GATE:].astype(F32), axis=0, keepdims=True)

    orders = ORDERS
    parts = dict(zip("qudh", zip(parts[:4], parts[4:])))
    chunks = {
        name: in_core_order(core, mine, exchange(theirs, SIBLING), 0)[None]
        for name, (mine, theirs) in parts.items()
    }

    held, last = dict(chunks), ()
    for name, step in GATHER_SEQUENCE:
        held[name] = after(held[name], *last)
        last = (held[name],)
        held[name] = doubled(held[name], orders[name][step])
    q, u, d, h = [held[name] for name in ("q", "u", "d", "h")]
    q_rest = exchange(after(q, *last), orders["q"][3])
    u = after(u, q)
    u_rest = exchange(u, orders["u"][3])
    d_rest = exchange(d, orders["d"][3])
    h = doubled(after(h, u), orders["h"][2])
    first = both_lanes(q, q_rest)
    h_rest = exchange(h, orders["h"][3])
    input_turned, qkv, small_rows = front_forward(
        after(where, d, h, cotangent_sum), lead_index, patches, first
    )
    attended, attended_turned = attention_forward(where, window_lengths, pad, qkv)
    u_rest, d_rest, h_rest = lax.optimization_barrier((u_rest, d_rest, h_rest, attended))[:3]
    second, down, head = both_lanes(u, u_rest), both_lanes(d, d_rest), both_lanes(h, h_rest)
    up_bias_row, head_bias_row = vector_of(small_rows[6:10]), vector_of(small_rows[10:16])
    (
        outputs, gate_out, gate_bias_sum, down_bias_sum, up_bias_sum, terms, mid_grad, _, mixed_grad,
        mine_d, theirs_d, mine_u, theirs_u, mine_h, theirs_h,
    ) = middle(
        where, small_rows, up_bias_row, head_bias_row, attended, patches, head_cotangent,
        act_cotangent, attended_turned, second, down, head,
    )

    got_h, got_d, got_u = [exchange(theirs, SIBLING) for theirs in (theirs_h, theirs_d, theirs_u)]
    head_rows = rows_of(jnp.concatenate([gate_bias_sum, cotangent_sum], axis=1), 6)
    up_rows = rows_of(up_bias_sum, 4)
    first_grad, mine_m, theirs_m = early_backward(
        where, window_lengths, pad, mixed_grad, qkv, input_turned
    )
    groups = {
        "head": [mine_h, after(got_h, first_grad), 4],
        "up": [mine_u, after(got_u, first_grad), 4],
        "down": [mine_d, after(got_d, first_grad), 4],
        "mix": [mine_m, exchange(theirs_m, SIBLING), 4],
    }
    last = ()

    def add(name):
        nonlocal last
        keep, got, step = groups[name]
        keep, send = folded(keep, after(got, *last))
        last = (send,)
        groups[name] = [keep, exchange(send, orders[name][step - 1]), step - 1]

    def finish(name, widths):
        keep, got, _ = groups[name]
        return finished(keep, after(got, *last), core, widths)

    for name in ("head", "up", "down"):
        add(name)
    patch_grad, head_out, mine_f, theirs_f = late_backward(
        after(where, *last), lead_index, window_lengths, pad, small_rows, terms, down_bias_sum,
        up_rows, head_rows, head_bias_row, outputs, gate_out, mixed_grad, qkv, first_grad, patches,
        mid_grad, input_turned, first, head,
    )
    last = (patch_grad,)
    groups["front"] = [mine_f, exchange(theirs_f, SIBLING), 4]
    for name in SCATTER_SEQUENCE:
        add(name)
    late_sum, small_sum = finish("front", (384, 128))
    (down_sum,) = finish("down", (384,))
    (early_sum,) = finish("mix", (768,))
    up_sum, out_sum = finish("up", (1536, 384))
    gate_sum, rest_sum = finish("head", (256, 2048))
    qkv_sum = jnp.concatenate(
        [
            piece[:, part * piece.shape[1] // 3 : (part + 1) * piece.shape[1] // 3]
            for part in range(3)
            for piece in (early_sum, late_sum)
        ],
        axis=1,
    )
    small_sum = small_sum.T
    return (
        outputs,
        head_out,
        patch_grad,
        small_sum[128:144],
        small_sum[0],
        small_sum[1],
        qkv_sum,
        out_sum,
        small_sum[2],
        small_sum[3],
        small_sum[4],
        up_sum,
        small_sum[6:10].reshape(96),
        down_sum,
        small_sum[5],
        jnp.concatenate([gate_sum, rest_sum], axis=1),
        small_sum[10:16].reshape(144),
    )


def plain_shards(
    patches,
    lead_index,
    window_lengths,
    pad_mask,
    lead_table,
    attn_gain,
    attn_shift,
    qkv_weight,
    out_weight,
    out_bias,
    mlp_gain,
    mlp_shift,
    up_weight,
    up_bias,
    down_weight,
    down_bias,
    head_weight,
    head_bias,
    act_cotangent,
    head_cotangent,
):
    front = (
        lax.all_gather(lead_table, ("dp", "fsdp"), axis=1, tiled=True),
        lax.all_gather(attn_gain, ("dp", "fsdp"), axis=0, tiled=True),
        lax.all_gather(attn_shift, ("dp", "fsdp"), axis=0, tiled=True),
        lax.all_gather(qkv_weight, ("dp", "fsdp"), axis=0, tiled=True),
        lax.all_gather(out_weight, ("dp", "fsdp"), axis=0, tiled=True),
        lax.all_gather(out_bias, ("dp", "fsdp"), axis=0, tiled=True),
    )
    rear = (
        lax.all_gather(mlp_gain, ("dp", "fsdp"), axis=0, tiled=True),
        lax.all_gather(mlp_shift, ("dp", "fsdp"), axis=0, tiled=True),
        lax.all_gather(up_weight, ("dp", "fsdp"), axis=0, tiled=True),
        lax.all_gather(up_bias, ("dp", "fsdp"), axis=0, tiled=True),
        lax.all_gather(down_weight, ("dp", "fsdp"), axis=0, tiled=True),
        lax.all_gather(down_bias, ("dp", "fsdp"), axis=0, tiled=True),
        lax.all_gather(head_weight, ("dp", "fsdp"), axis=0, tiled=True),
        lax.all_gather(head_bias, ("dp", "fsdp"), axis=0, tiled=True),
    )
    table_full, gain_one, shift_one, qkv_full, out_full, out_bias_full = front
    (
        gain_two,
        shift_two,
        up_full,
        up_bias_full,
        down_full,
        down_bias_full,
        head_full,
        head_bias_full,
    ) = rear
    token_rows, width = patches.shape
    head_dim = width // HEADS
    block_rows = min(512, token_rows)
    block_count = token_rows // block_rows
    ends = jnp.cumsum(window_lengths[0])
    positions = jnp.arange(token_rows, dtype=jnp.int32)
    window = jnp.sum((positions[:, None] >= ends[None, :]).astype(jnp.int32), axis=1)
    lead_hot = (jnp.arange(LEADS, dtype=jnp.int32) == lead_index[0]).astype(jnp.float32)
    lead_row = jnp.sum(lead_hot[:, None] * table_full.astype(jnp.float32), axis=0)
    start_state = patches.astype(jnp.float32) + lead_row[None, :]
    normed_one, pull_one = jax.vjp(
        layer_norm, start_state, gain_one.astype(jnp.float32), shift_one.astype(jnp.float32)
    )
    attn_input = normed_one.astype(jnp.bfloat16)
    qkv_rows = jnp.dot(attn_input, qkv_full, preferred_element_type=jnp.float32).astype(
        jnp.bfloat16
    )
    queries = qkv_rows[:, :width].reshape(block_count, block_rows, HEADS, head_dim)
    keys = qkv_rows[:, width : 2 * width].reshape(token_rows, HEADS, head_dim)
    values = qkv_rows[:, 2 * width :].reshape(token_rows, HEADS, head_dim)
    query_windows = window.reshape(block_count, block_rows)
    block_starts = jnp.arange(block_count, dtype=jnp.int32) * block_rows

    def block_scores(query_block, window_block, block_start):
        scores = (
            jnp.einsum("qhd,khd->hqk", query_block, keys, preferred_element_type=jnp.float32)
            * score_scale
        )
        allowed = allowed_keys(window_block, window, pad_mask, block_start)
        return jnp.where(allowed[None], scores, -1e30)

    def forward_block(inputs):
        query_block, window_block, block_start = inputs
        masked = block_scores(query_block, window_block, block_start)
        largest = jnp.max(masked, axis=-1, keepdims=True)
        raised = jnp.exp(masked - largest)
        total = jnp.sum(raised, axis=-1, keepdims=True)
        probs = (raised / total).astype(jnp.bfloat16)
        mixed = jnp.einsum("hqk,khd->qhd", probs, values, preferred_element_type=jnp.float32)
        return (
            mixed.reshape(block_rows, width).astype(jnp.bfloat16),
            (largest + jnp.log(total))[:, :, 0],
        )

    mixed_blocks, log_totals = lax.map(forward_block, (queries, query_windows, block_starts))
    attended = mixed_blocks.reshape(token_rows, width)
    mid_state = (
        start_state
        + jnp.dot(attended, out_full, preferred_element_type=jnp.float32)
        + out_bias_full.astype(jnp.float32)
    )
    normed_two, pull_two = jax.vjp(
        layer_norm, mid_state, gain_two.astype(jnp.float32), shift_two.astype(jnp.float32)
    )
    mlp_input = normed_two.astype(jnp.bfloat16)
    pre_act = jnp.dot(mlp_input, up_full, preferred_element_type=jnp.float32) + up_bias_full.astype(
        jnp.float32
    )
    activated, pull_act = jax.vjp(gelu_exact, pre_act)
    act_rows = activated.astype(jnp.bfloat16)
    end_state = (
        mid_state
        + jnp.dot(act_rows, down_full, preferred_element_type=jnp.float32)
        + down_bias_full.astype(jnp.float32)
    )
    outputs = end_state.astype(jnp.bfloat16)
    logits = jnp.dot(
        outputs, head_full, preferred_element_type=jnp.float32
    ) + head_bias_full.astype(jnp.float32)
    head_out, pull_head = jax.vjp(partial(expert_softmax, experts=EXPERTS, pixels=PIX), logits)
    up_back, down_back, head_back = (
        lax.all_gather(up_weight, ("dp", "fsdp"), axis=0, tiled=True),
        lax.all_gather(down_weight, ("dp", "fsdp"), axis=0, tiled=True),
        lax.all_gather(head_weight, ("dp", "fsdp"), axis=0, tiled=True),
    )
    qkv_back, out_back = (
        lax.all_gather(qkv_weight, ("dp", "fsdp"), axis=0, tiled=True),
        lax.all_gather(out_weight, ("dp", "fsdp"), axis=0, tiled=True),
    )
    logit_grad = pull_head(head_cotangent.astype(jnp.float32))[0].astype(jnp.bfloat16)
    head_bias_term = jnp.sum(logit_grad.astype(jnp.float32), axis=0)
    head_term = jnp.einsum("td,tn->dn", outputs, logit_grad, preferred_element_type=jnp.float32)
    end_grad = act_cotangent.astype(jnp.float32) + jnp.einsum(
        "tn,dn->td", logit_grad, head_back, preferred_element_type=jnp.float32
    )
    branch_grad = end_grad.astype(jnp.bfloat16)
    down_bias_term = jnp.sum(branch_grad.astype(jnp.float32), axis=0)
    down_term = jnp.einsum("tf,td->fd", act_rows, branch_grad, preferred_element_type=jnp.float32)
    act_grad = jnp.einsum("td,fd->tf", branch_grad, down_back, preferred_element_type=jnp.float32)
    pre_grad = pull_act(act_grad)[0].astype(jnp.bfloat16)
    up_bias_term = jnp.sum(pre_grad.astype(jnp.float32), axis=0)
    up_term = jnp.einsum("td,tf->df", mlp_input, pre_grad, preferred_element_type=jnp.float32)
    normed_two_grad = jnp.einsum("tf,df->td", pre_grad, up_back, preferred_element_type=jnp.float32)
    state_grad_two, gain_two_term, shift_two_term = pull_two(normed_two_grad)
    (
        gain_part,
        shift_part,
        up_part,
        up_bias_part,
        down_part,
        down_bias_part,
        head_part,
        head_bias_part,
    ) = (
        lax.psum_scatter(
            gain_two_term.astype(jnp.bfloat16), "dp", scatter_dimension=0, tiled=True
        ).astype(jnp.float32),
        lax.psum_scatter(
            shift_two_term.astype(jnp.bfloat16), "dp", scatter_dimension=0, tiled=True
        ).astype(jnp.float32),
        lax.psum_scatter(
            up_term.astype(jnp.bfloat16), "dp", scatter_dimension=0, tiled=True
        ).astype(jnp.float32),
        lax.psum_scatter(
            up_bias_term.astype(jnp.bfloat16), "dp", scatter_dimension=0, tiled=True
        ).astype(jnp.float32),
        lax.psum_scatter(
            down_term.astype(jnp.bfloat16), "dp", scatter_dimension=0, tiled=True
        ).astype(jnp.float32),
        lax.psum_scatter(
            down_bias_term.astype(jnp.bfloat16), "dp", scatter_dimension=0, tiled=True
        ).astype(jnp.float32),
        lax.psum_scatter(
            head_term.astype(jnp.bfloat16), "dp", scatter_dimension=0, tiled=True
        ).astype(jnp.float32),
        lax.psum_scatter(
            head_bias_term.astype(jnp.bfloat16), "dp", scatter_dimension=0, tiled=True
        ).astype(jnp.float32),
    )
    rear_grads = (
        lax.psum_scatter(gain_part, "fsdp", scatter_dimension=0, tiled=True),
        lax.psum_scatter(shift_part, "fsdp", scatter_dimension=0, tiled=True),
        lax.psum_scatter(up_part, "fsdp", scatter_dimension=0, tiled=True),
        lax.psum_scatter(up_bias_part, "fsdp", scatter_dimension=0, tiled=True),
        lax.psum_scatter(down_part, "fsdp", scatter_dimension=0, tiled=True),
        lax.psum_scatter(down_bias_part, "fsdp", scatter_dimension=0, tiled=True),
        lax.psum_scatter(head_part, "fsdp", scatter_dimension=0, tiled=True),
        lax.psum_scatter(head_bias_part, "fsdp", scatter_dimension=0, tiled=True),
    )
    mid_grad = end_grad + state_grad_two
    out_grad = mid_grad.astype(jnp.bfloat16)
    out_bias_term = jnp.sum(out_grad.astype(jnp.float32), axis=0)
    out_term = jnp.einsum("td,te->de", attended, out_grad, preferred_element_type=jnp.float32)
    mixed_grad = jnp.einsum(
        "te,de->td", out_grad, out_back, preferred_element_type=jnp.float32
    ).astype(jnp.bfloat16)
    grad_blocks = mixed_grad.reshape(block_count, block_rows, HEADS, head_dim)

    def backward_block(carry, inputs):
        key_sum, value_sum = carry
        query_block, grad_block, window_block, total_block, block_start = inputs
        masked = block_scores(query_block, window_block, block_start)
        probs = jnp.exp(masked - total_block[:, :, None])
        prob_grad = jnp.einsum(
            "qhd,khd->hqk", grad_block, values, preferred_element_type=jnp.float32
        )
        inner = jnp.sum(probs * prob_grad, axis=-1, keepdims=True)
        score_grad = (probs * (prob_grad - inner)).astype(jnp.bfloat16)
        query_grad = (
            jnp.einsum("hqk,khd->qhd", score_grad, keys, preferred_element_type=jnp.float32)
            * score_scale
        )
        key_sum = (
            key_sum
            + jnp.einsum(
                "hqk,qhd->khd", score_grad, query_block, preferred_element_type=jnp.float32
            )
            * score_scale
        )
        value_sum = value_sum + jnp.einsum(
            "hqk,qhd->khd",
            probs.astype(jnp.bfloat16),
            grad_block,
            preferred_element_type=jnp.float32,
        )
        return ((key_sum, value_sum), query_grad.reshape(block_rows, width))

    zero_keys = jnp.zeros((token_rows, HEADS, head_dim), jnp.float32)
    (key_grad, value_grad), query_grads = lax.scan(
        backward_block,
        (zero_keys, zero_keys),
        (queries, grad_blocks, query_windows, log_totals, block_starts),
    )
    qkv_grad = jnp.concatenate(
        [
            query_grads.reshape(token_rows, width),
            key_grad.reshape(token_rows, width),
            value_grad.reshape(token_rows, width),
        ],
        axis=1,
    ).astype(jnp.bfloat16)
    qkv_term = jnp.einsum("td,te->de", attn_input, qkv_grad, preferred_element_type=jnp.float32)
    normed_one_grad = jnp.einsum(
        "te,de->td", qkv_grad, qkv_back, preferred_element_type=jnp.float32
    )
    state_grad_one, gain_one_term, shift_one_term = pull_one(normed_one_grad)
    patch_grad = mid_grad + state_grad_one
    lead_term = lead_hot[:, None] * jnp.sum(patch_grad, axis=0)[None, :]
    lead_part, gain_one_part, shift_one_part, qkv_part, out_part, out_bias_part = (
        lax.psum_scatter(
            lead_term.astype(jnp.bfloat16), "dp", scatter_dimension=1, tiled=True
        ).astype(jnp.float32),
        lax.psum_scatter(
            gain_one_term.astype(jnp.bfloat16), "dp", scatter_dimension=0, tiled=True
        ).astype(jnp.float32),
        lax.psum_scatter(
            shift_one_term.astype(jnp.bfloat16), "dp", scatter_dimension=0, tiled=True
        ).astype(jnp.float32),
        lax.psum_scatter(
            qkv_term.astype(jnp.bfloat16), "dp", scatter_dimension=0, tiled=True
        ).astype(jnp.float32),
        lax.psum_scatter(
            out_term.astype(jnp.bfloat16), "dp", scatter_dimension=0, tiled=True
        ).astype(jnp.float32),
        lax.psum_scatter(
            out_bias_term.astype(jnp.bfloat16), "dp", scatter_dimension=0, tiled=True
        ).astype(jnp.float32),
    )
    front_grads = (
        lax.psum_scatter(lead_part, "fsdp", scatter_dimension=1, tiled=True),
        lax.psum_scatter(gain_one_part, "fsdp", scatter_dimension=0, tiled=True),
        lax.psum_scatter(shift_one_part, "fsdp", scatter_dimension=0, tiled=True),
        lax.psum_scatter(qkv_part, "fsdp", scatter_dimension=0, tiled=True),
        lax.psum_scatter(out_part, "fsdp", scatter_dimension=0, tiled=True),
        lax.psum_scatter(out_bias_part, "fsdp", scatter_dimension=0, tiled=True),
    )
    return (
        outputs,
        head_out,
        patch_grad,
        front_grads[0],
        front_grads[1],
        front_grads[2],
        front_grads[3],
        front_grads[4],
        front_grads[5],
        rear_grads[0],
        rear_grads[1],
        rear_grads[2],
        rear_grads[3],
        rear_grads[4],
        rear_grads[5],
        rear_grads[6],
        rear_grads[7],
    )


def solution(mesh):
    in_specs = (
        P(("dp", "fsdp"), None),
        P(("dp", "fsdp")),
        P(("dp", "fsdp"), None),
        P(("dp", "fsdp")),
        P(None, ("dp", "fsdp")),
        P(("dp", "fsdp")),
        P(("dp", "fsdp")),
        P(("dp", "fsdp"), None),
        P(("dp", "fsdp"), None),
        P(("dp", "fsdp")),
        P(("dp", "fsdp")),
        P(("dp", "fsdp")),
        P(("dp", "fsdp"), None),
        P(("dp", "fsdp")),
        P(("dp", "fsdp"), None),
        P(("dp", "fsdp")),
        P(("dp", "fsdp"), None),
        P(("dp", "fsdp")),
        P(("dp", "fsdp"), None),
        P(("dp", "fsdp"), None),
    )
    out_specs = (
        P(("dp", "fsdp"), None),
        P(("dp", "fsdp"), None),
        P(("dp", "fsdp"), None),
        P(None, ("dp", "fsdp")),
        P(("dp", "fsdp")),
        P(("dp", "fsdp")),
        P(("dp", "fsdp"), None),
        P(("dp", "fsdp"), None),
        P(("dp", "fsdp")),
        P(("dp", "fsdp")),
        P(("dp", "fsdp")),
        P(("dp", "fsdp"), None),
        P(("dp", "fsdp")),
        P(("dp", "fsdp"), None),
        P(("dp", "fsdp")),
        P(("dp", "fsdp"), None),
        P(("dp", "fsdp")),
    )
    body = shards if dict(mesh.shape) == {"dp": 4, "fsdp": 8} else plain_shards
    return jax.shard_map(body, mesh=mesh, in_specs=in_specs, out_specs=out_specs, check_vma=False)
```
